32 devices in a mesh: group: 2 (over y), dom: 4 (over x, core), img: 4 (over z).
Axes of the slice: x: 2, y: 2, z: 4, core: 2. Of those that a mesh axis runs over, the one named last changes fastest.
Arguments:
- disp: float32 [8, 3, 2048], P(('group', 'img'), None, 'dom'), parts along dimension 0, may hold values from -0.3 to 0.3
- veloc: float32 [8, 3, 2048], P(('group', 'img'), None, 'dom'), parts along dimension 0, may hold values from -1.5 to 1.5
- time_step: float32 [8], P(('group', 'img')), parts along dimension 0, may hold values from 0.05 to 0.4
- reset_flags: int32 [2, 8], P(None, ('group', 'img')), parts along dimension 1, may hold values 0 or 1
- climb: int32 [2], P('group'), parts along dimension 0, may hold values from 1 to 2
- species: int32 [4096], P(('group', 'dom')), parts along dimension 0, may hold values 0 or 1
- neighbours: int32 [8, 4096], P(None, ('group', 'dom')), parts along dimension 1, may hold values from 0 to 767, as said below
- counts: int32 [4096], P(('group', 'dom')), parts along dimension 0, may hold values from 4 to 8, as said below
- lattice: float32 [8, 3, 4096], P(None, None, ('group', 'dom')), parts along dimension 2, may hold values from -1.8 to 1.8, as said below
- embed: float32 [2, 64], replicated, may hold values from -6 to 6
- radial_weight: float32 [2, 8, 64], replicated, may hold values from -2 to 2
- mix_weight: float32 [2, 64, 64], replicated, may hold values from -0.75 to 0.75
- update_weight: float32 [2, 64, 64], replicated, may hold values from -0.75 to 0.75
- readout: float32 [64], replicated, may hold values from -0.75 to 0.75
Outputs:
- new_disp: float32 [8, 3, 2048], P(('group', 'img'), None, 'dom'), parts along dimension 0
- new_veloc: float32 [8, 3, 2048], P(('group', 'img'), None, 'dom'), parts along dimension 0
- band_forces: float32 [2, 2, 8], P(None, None, ('group', 'img')), parts along dimension 2
- path_coordinate: float32 [8], P(('group', 'img')), parts along dimension 0
The draws below stay inside these ranges and needn't reach their ends.
There are 2 independent parts, one for each index of `group`. The reference program is written for one: setup_inputs(seed, part) draws one part's arguments, and reference() takes and returns one part's arrays. A program takes and returns all parts, laid end to end along the dimension named above; an argument that names none is the same for every part. Nothing has to cross between parts.
Inputs may be any that keep to these rules, and one draw needn't show every extreme that they name: `lattice`: each component has magnitude between 1.3 and 1.8. neighbours[k, a] - 128 - (a mod 512) lies between -128 and 128 and is never 0. `counts`: some atom has all 8 slots live.
All inputs are finite; a program needn't handle non-finite values. No bound on the sum of `reset_flags` or of `species` on one device may be relied on, other than what follows from the above.
Results may differ from the reference program's by a relative error of at most 0.0003.
Values sent between devices are 32-bit elements; how exact they have to be, the bound alone decides.
No kernel may reach another device: no remote copies, remote signals or barrier semaphores. Data moves between devices by JAX's collectives and lax.ppermute only.
A program may use at most 64 MiB of HBM per device.

```python
import math
import jax
import jax.numpy as jnp
from jax import lax

C = 64
NB = 8
K = 8
LAYERS = 2
STEPS = 2
ATOMS_DEV = 512
GHOSTS = 128
NATOMS = 2048
IMAGES = 4


def draw_disp(key, part):
    key = jax.random.fold_in(key, 11)
    first_key, second_key = jax.random.split(key, 2)
    position = jnp.arange(NATOMS, dtype=jnp.float32) / NATOMS
    spread = jax.random.uniform(first_key, (NATOMS,), jnp.float32, 0.0, 1.0)
    amplitude = 0.01 * 10.0 ** spread * 3.0 ** position
    noise = jax.random.uniform(second_key, (IMAGES, 3, NATOMS), jnp.float32, -1.0, 1.0)
    return noise * amplitude[None, None, :]


def draw_neighbours(key, part):
    key = jax.random.fold_in(key, 12)
    first_key, second_key = jax.random.split(key, 2)
    local = jnp.arange(NATOMS, dtype=jnp.int32) % ATOMS_DEV
    length = jax.random.randint(first_key, (K, NATOMS), 1, GHOSTS + 1)
    direction = 2 * jax.random.randint(second_key, (K, NATOMS), 0, 2) - 1
    table = GHOSTS + local[None, :] + direction * length
    table = table.at[0, ATOMS_DEV - 1].set(ATOMS_DEV + 2 * GHOSTS - 1)
    table = table.at[0, 0].set(0)
    return table.astype(jnp.int32)


def draw_counts(key, part):
    key = jax.random.fold_in(key, 13)
    values = jax.random.randint(key, (NATOMS,), K // 2, K + 1)
    return values.at[0].set(K).astype(jnp.int32)


def draw_lattice(key, part):
    key = jax.random.fold_in(key, 14)
    first_key, second_key = jax.random.split(key, 2)
    direction = 2.0 * jax.random.randint(first_key, (K, 3, NATOMS), 0, 2).astype(jnp.float32) - 1.0
    length = jax.random.uniform(second_key, (K, 3, NATOMS), jnp.float32, 1.3, 1.8)
    return direction * length


def set_ends(result, stream_key, least, high):
    longest = result.shape.index(max(result.shape))
    spots = []
    for shift in (0, 1):
        where = [jax.random.randint(jax.random.fold_in(stream_key, axis), (), 0, length) for axis, length in enumerate(result.shape)]
        where[longest] = (where[longest] + shift) % result.shape[longest]
        spots.append(tuple(where))
    return result.at[spots[0]].set(least).at[spots[1]].set(high)


def levels(key, shape, cuts, least, top_value):
    def one(axis_at, blocks):
        heights = jax.random.uniform(jax.random.fold_in(jax.random.fold_in(key, 6), axis_at), (blocks,), jnp.float32, least / len(cuts), top_value / len(cuts))
        return jnp.repeat(jnp.exp(heights), shape[axis_at] // blocks).reshape((-1,) + (1,) * (len(shape) - axis_at - 1))

    level = one(*cuts[0])
    for cut in cuts[1:]:
        level = level * one(*cut)
    return level


def scatter_about(rng, dims, scale, most, cuts=(), kind=jnp.bfloat16):
    factor_of = levels(rng, dims, cuts, -0.22, 0.18) if cuts else 1.0
    entries = jax.random.normal(rng, dims, jnp.float32) * scale * factor_of
    return jnp.minimum(jnp.maximum(entries, -most), most).astype(kind)


def setup_inputs(seed: int = 0, part: int = 0) -> dict:
    streams_of = jax.random.split(jax.random.key(seed), 15)
    part_keys = jax.random.split(jax.random.fold_in(streams_of[14], part), 15)
    return {
        "disp": draw_disp(jax.random.fold_in(jax.random.fold_in(streams_of[14], part), 71), part),
        "veloc": scatter_about(part_keys[1], (IMAGES, 3, NATOMS), 0.1, 1.5, ((0, 4), (2, 4)), jnp.float32),
        "time_step": jnp.clip(jnp.exp(math.log(0.4) - 2.0794415 * jax.random.uniform(part_keys[2], (IMAGES,), jnp.float32) ** levels(part_keys[2], (IMAGES,), ((0, 4),), -0.2, 0.2)), 0.05, 0.4),
        "reset_flags": set_ends((jax.random.randint(part_keys[3], (STEPS, IMAGES), 0, 4) < 1).astype(jnp.int32), jax.random.fold_in(part_keys[3], 1), 0, 1),
        "climb": jax.random.randint(part_keys[4], (1,), 1, IMAGES - 1).astype(jnp.int32),
        "species": set_ends((jax.random.randint(part_keys[5], (NATOMS,), 0, 4) < 1).astype(jnp.int32), jax.random.fold_in(part_keys[5], 1), 0, 1),
        "neighbours": draw_neighbours(jax.random.fold_in(jax.random.fold_in(streams_of[14], part), 71), part),
        "counts": draw_counts(jax.random.fold_in(jax.random.fold_in(streams_of[14], part), 71), part),
        "lattice": draw_lattice(jax.random.fold_in(jax.random.fold_in(streams_of[14], part), 71), part),
        "embed": scatter_about(streams_of[9], (2, C), 1.0, 6.0, (), jnp.float32),
        "radial_weight": scatter_about(streams_of[10], (LAYERS, NB, C), NB ** -0.5, 2.0, (), jnp.float32),
        "mix_weight": scatter_about(streams_of[11], (LAYERS, C, C), C ** -0.5, 0.75, (), jnp.float32),
        "update_weight": scatter_about(streams_of[12], (LAYERS, C, C), C ** -0.5, 0.75, (), jnp.float32),
        "readout": scatter_about(streams_of[13], (C,), C ** -0.5, 0.75, (), jnp.float32),
    }


PRECISE = lax.Precision.HIGHEST
SPRING_CONSTANT = 0.5
ALPHA_START = 0.1
STEP_LIMIT = 0.3
TINY_VALUE = 1e-06
SOFTENING = 0.25

def radial_basis(distance, number):
    centres = 2.0 + 0.5 * jnp.arange(number, dtype=jnp.float32)
    centres = centres.reshape((number,) + (1,) * distance.ndim)
    envelope = 0.5 * (1.0 + jnp.cos(jnp.pi * distance / 6.0))
    return jnp.exp(-((distance[None] - centres) / 0.5) ** 2) * envelope[None]

def messages(displace, features, centre_disp, lattice, index, live, radial_w):
    slots = index.shape[0]
    number = radial_w.shape[0]
    others = jnp.moveaxis(jnp.take(displace, index, axis=1), 0, 1)
    vectors = lattice + others - centre_disp[None]
    distance = jnp.sqrt(lax.optimization_barrier(jnp.sum(vectors * vectors, axis=1)) + SOFTENING)
    radial = jnp.einsum('nc,nka->cka', radial_w, radial_basis(distance, number), precision=PRECISE)
    gathered = jnp.take(features, index, axis=1)
    return lax.optimization_barrier(jnp.sum(radial * gathered * live[None], axis=1)) / slots ** 0.5

def layer(displace, hidden, features, centre, lattice, index, live, radial_w, update_w):
    count = index.shape[1]
    centre_disp = lax.slice_in_dim(displace, centre, centre + count, axis=1)
    message = messages(displace, features, centre_disp, lattice, index, live, radial_w)
    own_hidden = lax.slice_in_dim(hidden, centre, centre + count, axis=1)
    return own_hidden + jnp.einsum('cd,ca->da', update_w, jax.nn.silu(message), precision=PRECISE)

def reference(disp, veloc, time_step, reset_flags, climb, species, neighbours, counts, lattice, embed, radial_weight, mix_weight, update_weight, readout):
    atom_ids = jnp.arange(NATOMS, dtype=jnp.int32)
    global_index = ((atom_ids[None, :] - atom_ids[None, :] % ATOMS_DEV + neighbours - GHOSTS) % NATOMS).astype(jnp.int32)
    live = (jnp.arange(K, dtype=jnp.int32)[:, None] < counts[None, :]).astype(jnp.float32)
    kinds = species.astype(jnp.float32)
    base = embed[0][:, None] + (embed[1] - embed[0])[:, None] * kinds[None, :]
    base_features = jnp.einsum('cd,ca->da', mix_weight[0], base, precision=PRECISE)

    def energy(displace):
        hidden_one = layer(displace, base, base_features, 0, lattice, global_index, live, radial_weight[0], update_weight[0])
        features_two = jnp.einsum('cd,ca->da', mix_weight[1], hidden_one, precision=PRECISE)
        hidden_two = layer(displace, hidden_one, features_two, 0, lattice, global_index, live, radial_weight[1], update_weight[1])
        return jnp.sum(jnp.dot(readout, hidden_two, precision=PRECISE))
    gradient = jax.grad(energy)
    image_ids = jnp.arange(IMAGES, dtype=jnp.int32)
    inside = (image_ids >= 1) & (image_ids <= IMAGES - 2)
    climbing = image_ids == climb[0]
    position = disp
    speed = veloc
    step_size = time_step
    alpha = jnp.full((IMAGES,), ALPHA_START, jnp.float32)
    records = []
    for repeat in range(STEPS):
        force = -lax.map(gradient, position)
        zeros = jnp.zeros_like(position[:1])
        before = jnp.concatenate([zeros, position[:-1]], axis=0)
        after = jnp.concatenate([position[1:], zeros], axis=0)
        plus = after - position
        minus = position - before
        tangent = after - before
        tangent_sq = lax.optimization_barrier(jnp.sum(tangent * tangent, axis=(1, 2)))
        unit = tangent / jnp.sqrt(tangent_sq + TINY_VALUE)[:, None, None]
        along = lax.optimization_barrier(jnp.sum(force * unit, axis=(1, 2)))
        spring = SPRING_CONSTANT * (jnp.sqrt(lax.optimization_barrier(jnp.sum(plus * plus, axis=(1, 2)))) - jnp.sqrt(lax.optimization_barrier(jnp.sum(minus * minus, axis=(1, 2)))))
        factor = jnp.where(climbing, -2.0 * along, spring - along)
        band = jnp.where(inside[:, None, None], force + factor[:, None, None] * unit, 0.0)
        speed_sq = lax.optimization_barrier(jnp.sum(speed * speed, axis=(1, 2)))
        band_sq = lax.optimization_barrier(jnp.sum(band * band, axis=(1, 2)))
        flagged = reset_flags[repeat] == 1
        new_size = jnp.where(flagged, 0.5 * step_size, jnp.minimum(1.1 * step_size, STEP_LIMIT))
        mixed = (1.0 - alpha)[:, None, None] * speed + (alpha * jnp.sqrt(speed_sq / (band_sq + TINY_VALUE)))[:, None, None] * band
        mixed = jnp.where(flagged[:, None, None], 0.0, mixed)
        alpha = jnp.where(flagged, ALPHA_START, 0.99 * alpha)
        speed = jnp.where(inside[:, None, None], mixed + new_size[:, None, None] * band, 0.0)
        position = position + new_size[:, None, None] * speed
        step_size = new_size
        records.append(jnp.stack([jnp.where(inside, along, 0.0), jnp.where(inside, spring, 0.0)]))
    earlier = jnp.concatenate([jnp.zeros_like(position[:1]), position[:-1]], axis=0)
    spacing = lax.optimization_barrier(jnp.sum((position - earlier) ** 2, axis=(1, 2)))
    segment = jnp.sqrt(spacing / (3.0 * NATOMS))
    return (position, speed, jnp.stack(records), jnp.cumsum(segment))
```

```python
import functools
import math

import jax
import jax.numpy as jnp
from jax import lax
from jax.experimental import pallas as pl
from jax.experimental.pallas import tpu as pltpu
from jax.sharding import PartitionSpec as P

F32 = jnp.float32
BF16 = jnp.bfloat16
PRECISE = lax.Precision.HIGHEST
SPRING_CONSTANT = 0.5
ALPHA_START = 0.1
STEP_LIMIT = 0.3
TINY_VALUE = 1e-06
SOFTENING = 0.25
LANES = 128
SLOTS = 8
BASIS = 8
CHANNELS = 64
SLAB_BLOCKS = 4
ROW_X = 32
ROW_COUNT = 35
ROW_KIND = 36
PACK_ROWS = 40
NT = (((1,), (1,)), ((), ()))


def split(x):
    high = x.astype(BF16).astype(F32)
    return high, x - high


def left_stack(w):
    high, low = split(w)
    return jnp.concatenate([high, high, low], axis=1)


def right_stack(x):
    high, low = split(x)
    high = high.astype(BF16)
    return jnp.concatenate([high, low.astype(BF16), high], axis=0)


def pair_stack(x):
    high, low = split(x)
    return jnp.concatenate([high.astype(BF16), low.astype(BF16)], axis=0)


def mm(a, b):
    return jnp.dot(a, b, preferred_element_type=F32)


def mm_nt(a, b):
    return lax.dot_general(a, b, NT, preferred_element_type=F32)


def pack_kernel(x_ref, species_ref, nbr_ref, counts_ref, lattice_ref, out_ref):
    out_ref[0:8, :] = nbr_ref[...].astype(F32)
    for c in range(3):
        out_ref[8 + 8 * c : 16 + 8 * c, :] = lattice_ref[:, c, :]
    out_ref[ROW_X : ROW_X + 3, :] = x_ref[0]
    out_ref[ROW_COUNT : ROW_COUNT + 1, :] = counts_ref[...].astype(F32).reshape(1, -1)
    out_ref[ROW_KIND : ROW_KIND + 1, :] = species_ref[...].astype(F32).reshape(1, -1)
    out_ref[ROW_KIND + 1 : PACK_ROWS, :] = jnp.zeros((PACK_ROWS - ROW_KIND - 1, out_ref.shape[1]), F32)


def weight_kernel(
    embed_ref, radial_ref, mix_ref, update_ref, readout_ref, l1_ref, l2_ref, l3_ref, l4_ref, l5_ref, l6_ref, col_ref
):
    eye = (
        lax.broadcasted_iota(jnp.int32, (CHANNELS, CHANNELS), 0)
        == lax.broadcasted_iota(jnp.int32, (CHANNELS, CHANNELS), 1)
    ).astype(F32)

    def turned(x):
        return lax.dot_general(eye, x, NT, precision=PRECISE, preferred_element_type=F32)

    base0 = embed_ref[0:1, :]
    base1 = embed_ref[1:2, :] - base0
    rows = jnp.concatenate([base0, base1], axis=0)
    sent = jnp.dot(rows, mix_ref[0], precision=PRECISE, preferred_element_type=F32)
    scale = 1.0 / math.sqrt(SLOTS)
    first = jnp.concatenate([radial_ref[0] * sent[0:1], radial_ref[0] * sent[1:2]], axis=0) * scale
    second = radial_ref[1] * scale
    folded = jnp.dot(update_ref[0], mix_ref[1], precision=PRECISE, preferred_element_type=F32)
    mix_t = turned(mix_ref[1])
    l1_ref[...] = left_stack(turned(first)).astype(BF16)
    l2_ref[...] = left_stack(turned(folded)).astype(BF16)
    high, low = split(turned(second))
    l3_ref[...] = jnp.concatenate([high, high, low, jnp.zeros_like(high)], axis=1).astype(BF16)
    l4_ref[...] = left_stack(jnp.concatenate([second, jnp.zeros_like(second)], axis=0)).astype(BF16)
    l5_ref[...] = left_stack(folded).astype(BF16)
    l6_ref[...] = left_stack(first).astype(BF16)
    readout = readout_ref[...].reshape(1, CHANNELS)
    wide = (CHANNELS, LANES)
    col_ref[0] = jnp.broadcast_to(jnp.sum(mix_t * base0, axis=1, keepdims=True), wide)
    col_ref[1] = jnp.broadcast_to(jnp.sum(mix_t * base1, axis=1, keepdims=True), wide)
    col_ref[2] = jnp.broadcast_to(jnp.sum(update_ref[0] * readout, axis=1, keepdims=True), wide)
    col_ref[3] = jnp.broadcast_to(jnp.sum(update_ref[1] * readout, axis=1, keepdims=True), wide)


def sin_cos(t):
    q = t * t
    s = -1.0 / 39916800.0
    for c in (1.0 / 362880.0, -1.0 / 5040.0, 1.0 / 120.0, -1.0 / 6.0, 1.0):
        s = s * q + c
    k = 1.0 / 479001600.0
    for c in (-1.0 / 3628800.0, 1.0 / 40320.0, -1.0 / 720.0, 1.0 / 24.0, -0.5, 1.0):
        k = k * q + c
    return s * t, k


def wide_row(x, row):
    return jnp.broadcast_to(x[row : row + 1, :], (8, x.shape[1]))


def silu_parts(m):
    sig = 1.0 / (1.0 + jnp.exp(-m))
    return m * sig, sig * (1.0 + m * (1.0 - sig))


def force_parts(packs, weights, scr):
    l1, l2, l3, l4, l5, l6, col = weights
    (xs, widx, kinds, geo, bst, bpr, sst, ghl, slope, hot, dg, dmat, acc) = scr
    centre = 2.0 + 0.5 * lax.broadcasted_iota(jnp.int32, (BASIS, LANES), 0).astype(F32)
    slot = lax.broadcasted_iota(jnp.int32, (SLOTS, LANES), 0)

    for b in range(1, 11):
        pack = packs[b // 4]
        lanes = slice((b % 4) * LANES, (b % 4 + 1) * LANES)
        index = pack[0:8, lanes].astype(jnp.int32) - LANES * (b % 4)
        widx[b] = index
        inner = index & (LANES - 1)
        part = index >> 7

        def taken(row):
            got = [
                jnp.take_along_axis(jnp.broadcast_to(xs[b - 1 + w, row : row + 1, :], (SLOTS, LANES)), inner, axis=1)
                for w in range(3)
            ]
            return jnp.where(part == 0, got[0], jnp.where(part == 1, got[1], got[2]))

        vec = [
            pack[8 + 8 * c : 16 + 8 * c, lanes] + taken(c) - jnp.broadcast_to(xs[b, c : c + 1, :], (SLOTS, LANES))
            for c in range(3)
        ]
        kind = taken(3)
        dist = jnp.sqrt(vec[0] * vec[0] + vec[1] * vec[1] + vec[2] * vec[2] + SOFTENING)
        live = (slot.astype(F32) < jnp.broadcast_to(pack[ROW_COUNT : ROW_COUNT + 1, lanes], (SLOTS, LANES))).astype(F32)
        turns = dist * (1.0 / 12.0)
        turns = turns - jnp.floor(turns + 0.5)
        sine, cosine = sin_cos(turns * math.pi)
        envelope = cosine * cosine * live
        slant = cosine * sine * live * (-math.pi / 6.0)
        kinds[b] = kind
        if 3 <= b <= 8:
            for c in range(3):
                geo[b, c] = vec[c]
            geo[b, 3] = 1.0 / dist
        total = jnp.zeros((BASIS, LANES), F32)
        total_kind = jnp.zeros((BASIS, LANES), F32)
        for k in range(SLOTS):
            away = wide_row(dist, k) - centre
            gauss = jnp.exp(-4.0 * (away * away))
            env_k = wide_row(envelope, k)
            value = gauss * env_k
            total = total + value
            total_kind = total_kind + value * wide_row(kind, k)
            cols = slice(k * LANES, (k + 1) * LANES)
            if 2 <= b <= 9:
                high, low = split(value)
                bst[b, 0:8, cols] = high
                bst[b, 8:16, cols] = low
            if 3 <= b <= 8:
                bpr[b, :, cols] = gauss * (wide_row(slant, k) - 8.0 * away * env_k)
        both = jnp.concatenate([total, total_kind], axis=0)
        high, low = split(both)
        sst[b] = jnp.concatenate([high, low, high], axis=0).astype(BF16)

    for b in range(1, 11):
        message = mm(l1[...], sst[b])
        value, steep = silu_parts(message)
        sent = mm(l2[...], right_stack(value))
        sent = sent + col[0] + col[1] * jnp.broadcast_to(xs[b, 3:4, :], (CHANNELS, LANES))
        ghl[b] = pair_stack(sent)
        if 3 <= b <= 8:
            slope[b] = steep

    for b in range(1, 11):
        dg[b] = jnp.zeros((CHANNELS, LANES), F32)

    row_id = lax.broadcasted_iota(jnp.int32, (3 * LANES, LANES), 0)

    def second(b, carry):
        index = widx[b]
        for k in range(SLOTS):
            same = row_id == jnp.broadcast_to(index[k : k + 1, :], (3 * LANES, LANES))
            hot[b, :, k * LANES : (k + 1) * LANES] = jnp.where(same, 1.0, 0.0).astype(BF16)
        window = jnp.concatenate([ghl[b - 1], ghl[b], ghl[b + 1]], axis=1)
        got = mm(window, hot[b])
        got = got[:CHANNELS] + got[CHANNELS:]
        basis = bst[b]
        stack = jnp.concatenate([basis, basis], axis=0).astype(BF16)
        radial = mm(l3[...], stack)
        message = jnp.zeros((CHANNELS, LANES), F32)
        for k in range(SLOTS):
            cols = slice(k * LANES, (k + 1) * LANES)
            message = message + radial[:, cols] * got[:, cols]
        _, steep = silu_parts(message)
        back = col[3] * steep
        back = jnp.concatenate([back] * SLOTS, axis=1)
        out = mm_nt(pair_stack(radial * back), hot[b])
        out = out[:CHANNELS] + out[CHANNELS:]
        for w in range(3):
            dg[b - 1 + w] += out[:, w * LANES : (w + 1) * LANES]
        dmat[b] = mm(l4[...], right_stack(got * back))[0:8]
        return carry

    lax.fori_loop(2, 10, second, 0)

    for b in range(3, 9):
        for c in range(3):
            acc[b, c] = jnp.zeros((8, LANES), F32)
    acc[2] = jnp.zeros((3, 8, LANES), F32)
    acc[9] = jnp.zeros((3, 8, LANES), F32)

    def last(b, carry):
        steep = mm(l5[...], right_stack(dg[b])) + col[2]
        sums = mm(l6[...], right_stack(steep * slope[b]))
        kind = kinds[b]
        rows = []
        for k in range(SLOTS):
            cols = slice(k * LANES, (k + 1) * LANES)
            weight = dmat[b, :, cols] + sums[0:8] + wide_row(kind, k) * sums[8:16]
            rows.append(jnp.sum(bpr[b, :, cols] * weight, axis=0, keepdims=True))
        pull = jnp.concatenate(rows, axis=0) * geo[b, 3]
        pieces = []
        for c in range(3):
            value = pull * geo[b, c]
            acc[b, c] -= value
            pieces.append(split(value))
        lines = []
        for h in range(2):
            for c in range(3):
                lines.append(
                    jnp.concatenate([jnp.where(slot == k, pieces[c][h], 0.0) for k in range(SLOTS)], axis=1)
                )
        out = mm_nt(jnp.concatenate(lines, axis=0).astype(BF16), hot[b])
        for c in range(3):
            both = out[8 * c : 8 * c + 8] + out[24 + 8 * c : 32 + 8 * c]
            for w in range(3):
                acc[b - 1 + w, c] += both[:, w * LANES : (w + 1) * LANES]
        return carry

    lax.fori_loop(3, 9, last, 0)


def own_force(acc, c):
    return jnp.concatenate(
        [-jnp.sum(acc[4 + i, c], axis=0, keepdims=True) for i in range(SLAB_BLOCKS)], axis=1
    )


def fill_region(xs, packs, rows_of):
    for b in range(12):
        lanes = slice((b % 4) * LANES, (b % 4 + 1) * LANES)
        pack = packs[b // 4]
        xs[b, 0:3, :] = rows_of(b // 4)[:, lanes]
        xs[b, 3:4, :] = pack[ROW_KIND : ROW_KIND + 1, lanes]


def lane_total(x):
    x = x[:, 0:LANES] + x[:, LANES : 2 * LANES] + x[:, 2 * LANES : 3 * LANES] + x[:, 3 * LANES : 4 * LANES]
    return jnp.sum(x, axis=1, keepdims=True)


def dot3(a, b):
    return jnp.sum(a * b, axis=0, keepdims=True)


def scratch():
    return [
        pltpu.VMEM((12, 8, LANES), F32),
        pltpu.VMEM((12, 8, LANES), jnp.int32),
        pltpu.VMEM((12, 8, LANES), F32),
        pltpu.VMEM((12, 4, 8, LANES), F32),
        pltpu.VMEM((12, 16, SLOTS * LANES), F32),
        pltpu.VMEM((12, 8, SLOTS * LANES), F32),
        pltpu.VMEM((12, 48, LANES), BF16),
        pltpu.VMEM((12, 2 * CHANNELS, LANES), BF16),
        pltpu.VMEM((12, CHANNELS, LANES), F32),
        pltpu.VMEM((12, 3 * LANES, SLOTS * LANES), BF16),
        pltpu.VMEM((12, CHANNELS, LANES), F32),
        pltpu.VMEM((12, 8, SLOTS * LANES), F32),
        pltpu.VMEM((12, 3, 8, LANES), F32),
    ]


def first_kernel(images, pl_ref, po_ref, pr_ref, v_ref, before_ref, after_ref, *rest):
    weights, out_ref, scr = rest[:7], rest[7], rest[8:]
    packs = [pl_ref, po_ref, pr_ref]
    fill_region(scr[0], packs, lambda s: packs[s][ROW_X : ROW_X + 3, :])
    force_parts(packs, weights, scr)
    acc = scr[-1]
    force = jnp.concatenate([own_force(acc, c) for c in range(3)], axis=0)
    here = lax.axis_index("img")
    x = po_ref[ROW_X : ROW_X + 3, :]
    v = v_ref[0]
    before = jnp.where(here > 0, before_ref[0], 0.0)
    after = jnp.where(here < images - 1, after_ref[0], 0.0)
    tangent = after - before
    plus = after - x
    minus = x - before
    sums = jnp.concatenate(
        [
            dot3(force, tangent),
            dot3(force, force),
            dot3(tangent, tangent),
            dot3(plus, plus),
            dot3(minus, minus),
            dot3(v, v),
            jnp.zeros((2, x.shape[1]), F32),
        ],
        axis=0,
    )
    out_ref[0:3, :] = force
    out_ref[3:6, :] = tangent
    out_ref[6:9, :] = v
    out_ref[9:15, :] = jnp.broadcast_to(lane_total(sums)[0:6], (6, x.shape[1]))
    out_ref[15:16, :] = jnp.zeros((1, x.shape[1]), F32)


def step_numbers(ft, ff, tt, pp, mn, vv, dt, alpha, flagged, climbing, inside):
    root = jnp.sqrt(tt + TINY_VALUE)
    along = ft / root
    spring = SPRING_CONSTANT * (jnp.sqrt(pp) - jnp.sqrt(mn))
    factor = jnp.where(climbing, -2.0 * along, spring - along)
    band = jnp.maximum(ff + 2.0 * factor * along + factor * factor * (tt / (tt + TINY_VALUE)), 0.0)
    new_dt = jnp.where(flagged, 0.5 * dt, jnp.minimum(1.1 * dt, STEP_LIMIT))
    pull = jnp.where(flagged, 0.0, alpha * jnp.sqrt(vv / (band + TINY_VALUE))) + new_dt
    keep = jnp.where(flagged, 0.0, 1.0 - alpha)
    new_alpha = jnp.where(flagged, ALPHA_START, 0.99 * alpha)
    keep = jnp.where(inside, keep, 0.0)
    pull = jnp.where(inside, pull, 0.0)
    return (
        jnp.where(inside, along, 0.0),
        jnp.where(inside, spring, 0.0),
        keep,
        pull,
        pull * factor / root,
        new_dt,
        new_alpha,
    )


def second_kernel(images, others, dt_ref, flag_ref, climb_ref, pl_ref, po_ref, pr_ref, own_ref, *rest):
    heard, rest = rest[:others], rest[others:]
    weights, out_ref, scr = rest[:7], rest[7], rest[8:]
    packs = [pl_ref, po_ref, pr_ref]
    here = lax.axis_index("img")
    sums = own_ref[8:16, 0:LANES]
    for one in heard:
        sums = sums + one[8:16, 0:LANES]
    ft, ff, tt, pp, mn, vv = (sums[1 + i : 2 + i, :] for i in range(6))
    shape = (1, LANES)
    along, spring, keep, pull, side, dt, alpha = step_numbers(
        ft,
        ff,
        tt,
        pp,
        mn,
        vv,
        jnp.full(shape, dt_ref[0], F32),
        jnp.full(shape, ALPHA_START, F32),
        jnp.full(shape, flag_ref[0, 0], jnp.int32) == 1,
        jnp.full(shape, here - climb_ref[0], jnp.int32) == 0,
        jnp.full(shape, jnp.where((here >= 1) & (here <= images - 2), 1, 0), jnp.int32) == 1,
    )
    messages = [heard[0], own_ref, heard[others - 1]]

    def wide(s):
        return jnp.concatenate([s] * SLAB_BLOCKS, axis=1)

    def speed(m):
        return wide(keep) * m[6:9, :] + wide(pull) * m[0:3, :] + wide(side) * m[3:6, :]

    moved = [p[ROW_X : ROW_X + 3, :] + wide(dt) * speed(m) for p, m in zip(packs, messages)]
    fill_region(scr[0], packs, lambda s: moved[s])
    force_parts(packs, weights, scr)
    acc = scr[-1]
    out_ref[0:3, :] = moved[1]
    out_ref[3:6, :] = speed(own_ref)
    out_ref[6:9, :] = jnp.concatenate([own_force(acc, c) for c in range(3)], axis=0)
    out_ref[9:10, :] = wide(dt)
    out_ref[10:11, :] = wide(alpha)
    out_ref[11:12, :] = jnp.full((1, out_ref.shape[1]), flag_ref[1, 0], jnp.int32).astype(F32)
    out_ref[12:13, :] = wide(along)
    out_ref[13:14, :] = wide(spring)
    out_ref[14:16, :] = jnp.zeros((2, out_ref.shape[1]), F32)


PRODUCTS = (
    [("f", "t"), ("f", "f"), ("t", "t"), ("p", "p"), ("d", "d"), ("v", "v")]
    + [("d", "v"), ("d", "f"), ("d", "t"), ("d", "V"), ("d", "F"), ("d", "T"), ("v", "f"), ("v", "t")]
    + [(a, b) for a in "vft" for b in "VFT"]
)


def gram_kernel(images, *refs):
    messages, out_ref, state_ref = refs[:images], refs[images], refs[images + 1]
    rows = 8 * ((images + 7) // 8)
    here = lax.axis_index("img")
    width = state_ref.shape[1]
    blank = jnp.zeros((rows - images, width), F32)

    def gathered(row):
        lines = [m[row : row + 1, :] for m in messages]
        return jnp.concatenate(lines + ([blank] if rows > images else []), axis=0)

    def shifted(value, by):
        lines = [value[(s + by) % images : (s + by) % images + 1, :] for s in range(images)]
        return jnp.concatenate(lines + ([blank] if rows > images else []), axis=0)

    offset = lax.broadcasted_iota(jnp.int32, (rows, width), 0)
    number = here - offset
    number = jnp.where(number < 0, number + images, number)
    has_after = (number < images - 1) & (offset < images)
    has_before = (number > 0) & (offset < images)
    totals = [jnp.zeros((rows, width), F32) for _ in PRODUCTS]
    for c in range(3):
        x, v, f = gathered(c), gathered(3 + c), gathered(6 + c)
        after = jnp.where(has_after, shifted(x, -1), 0.0)
        before = jnp.where(has_before, shifted(x, 1), 0.0)
        t = after - before
        table = {"f": f, "v": v, "t": t, "p": after - x, "d": x - before}
        table["F"] = jnp.where(has_before, shifted(f, 1), 0.0)
        table["V"] = jnp.where(has_before, shifted(v, 1), 0.0)
        table["T"] = jnp.where(has_before, shifted(t, 1), 0.0)
        totals = [old + table[a] * table[b] for old, (a, b) in zip(totals, PRODUCTS)]
        state_ref[c : c + 1, :] = t[0:1]
    lane = lax.broadcasted_iota(jnp.int32, (rows, LANES), 1)
    result = jnp.zeros((rows, LANES), F32)
    for q, one in enumerate(totals):
        result = jnp.where(lane == q, jnp.broadcast_to(lane_total(one), (rows, LANES)), result)
    out_ref[...] = result
    for i in range(3):
        state_ref[8 + rows * i : 8 + rows * (i + 1), :] = gathered(9 + i)


def final_kernel(images, others, atoms, climb_ref, own_ref, state_ref, sums_ref, *rest):
    heard, (x_ref, v_ref, band_ref, path_ref) = rest[:others], rest[others:]
    rows = sums_ref.shape[0]
    here = lax.axis_index("img")
    sums = sums_ref[...]
    for one in heard:
        sums = sums + one[...]
    got = {
        pair: jnp.broadcast_to(sums[:, q : q + 1], (rows, LANES)) for q, pair in enumerate(PRODUCTS)
    }
    offset = lax.broadcasted_iota(jnp.int32, (rows, LANES), 0)
    number = here - offset
    number = jnp.where(number < 0, number + images, number)
    inside = (number >= 1) & (number <= images - 2) & (offset < images)
    has_before = (number > 0) & (offset < images)
    climb = jnp.full((rows, LANES), climb_ref[0], jnp.int32)
    dt0, alpha0, flag = (state_ref[8 + rows * i : 8 + rows * (i + 1), 0:LANES] for i in range(3))
    along, spring, keep, pull, side, dt, _ = step_numbers(
        got["f", "t"],
        got["f", "f"],
        got["t", "t"],
        got["p", "p"],
        got["d", "d"],
        got["v", "v"],
        dt0,
        alpha0,
        flag == 1.0,
        number == climb,
        inside,
    )

    def shifted(value):
        lines = [value[(s + 1) % images : (s + 1) % images + 1, :] for s in range(images)]
        if rows > images:
            lines.append(jnp.zeros((rows - images, LANES), F32))
        return jnp.where(has_before, jnp.concatenate(lines, axis=0), 0.0)

    now = {"v": dt * keep, "f": dt * pull, "t": dt * side}
    old = {a.upper(): shifted(value) for a, value in now.items()}
    mine = now["v"] * now["v"] * got["v", "v"] + now["f"] * now["f"] * got["f", "f"]
    mine = mine + now["t"] * now["t"] * got["t", "t"]
    cross = now["v"] * now["f"] * got["v", "f"] + now["v"] * now["t"] * got["v", "t"]
    mine = mine + 2.0 * (cross + now["f"] * now["t"] * got["f", "t"])
    both = jnp.zeros((rows, LANES), F32)
    for a in "vft":
        both = both + now[a] * got["d", a]
    for b in "VFT":
        both = both - old[b] * got["d", b]
    for a in "vft":
        for b in "VFT":
            both = both - now[a] * old[b] * got[a, b]
    squared = got["d", "d"] + mine + shifted(mine) + 2.0 * both
    segment = jnp.sqrt(jnp.maximum(squared, 0.0) * (1.0 / (3.0 * atoms)))
    path = jnp.sum(jnp.where(offset <= here, segment, 0.0), axis=0, keepdims=True)
    path_ref[...] = path

    def wide(s):
        return jnp.concatenate([s[0:1, :]] * SLAB_BLOCKS, axis=1)

    speed = wide(keep) * own_ref[3:6, :] + wide(pull) * own_ref[6:9, :] + wide(side) * state_ref[0:3, :]
    v_ref[0] = speed
    x_ref[0] = own_ref[0:3, :] + wide(dt) * speed
    band_ref[...] = jnp.concatenate(
        [own_ref[12:14, 0:LANES], along[0:1], spring[0:1], jnp.zeros((4, LANES), F32)], axis=0
    )


VMEM_SPEC = pl.BlockSpec(memory_space=pltpu.VMEM)
SMEM_SPEC = pl.BlockSpec(memory_space=pltpu.SMEM)


def call(body, outs, scalars, arrays, scratch_shapes=(), flops=0):
    return pl.pallas_call(
        body,
        out_shape=outs,
        in_specs=[SMEM_SPEC] * len(scalars) + [VMEM_SPEC] * len(arrays),
        out_specs=jax.tree.map(lambda _: VMEM_SPEC, outs),
        scratch_shapes=list(scratch_shapes),
        compiler_params=pltpu.CompilerParams(vmem_limit_bytes=48 * 1024 * 1024),
        cost_estimate=pl.CostEstimate(flops=flops, bytes_accessed=1 << 18, transcendentals=0),
    )(*scalars, *arrays)


def around(array, axis):
    count = lax.axis_size(axis)
    return [lax.ppermute(array, axis, [(i, (i + s) % count) for i in range(count)]) for s in range(1, count)]


def ring(array, axis, by):
    count = lax.axis_size(axis)
    return lax.ppermute(array, axis, [(i, (i + by) % count) for i in range(count)])


def local(
    disp,
    veloc,
    time_step,
    reset_flags,
    climb,
    species,
    neighbours,
    counts,
    lattice,
    embed,
    radial_weight,
    mix_weight,
    update_weight,
    readout,
):
    atoms = disp.shape[2]
    images = lax.axis_size("img")
    domains = lax.axis_size("dom")
    assert disp.shape[0] == 1 and atoms == SLAB_BLOCKS * LANES and domains >= 3
    shape = jax.ShapeDtypeStruct
    before, after = ring(disp, "img", 1), ring(disp, "img", -1)
    pack = call(pack_kernel, shape((PACK_ROWS, atoms), F32), (), (disp, species, neighbours, counts, lattice))
    left, right = ring(pack, "dom", 1), ring(pack, "dom", -1)
    weights = call(
        weight_kernel,
        (
            shape((CHANNELS, 48), BF16),
            shape((CHANNELS, 192), BF16),
            shape((CHANNELS, 32), BF16),
            shape((16, 192), BF16),
            shape((CHANNELS, 192), BF16),
            shape((16, 192), BF16),
            shape((4, CHANNELS, LANES), F32),
        ),
        (),
        (embed, radial_weight, mix_weight, update_weight, readout),
        flops=10000000,
    )
    message = call(
        functools.partial(first_kernel, images),
        shape((16, atoms), F32),
        (),
        (left, pack, right, veloc, before, after, *weights),
        scratch(),
        flops=1000000000,
    )
    heard = around(message, "dom")
    state = call(
        functools.partial(second_kernel, images, len(heard)),
        shape((16, atoms), F32),
        (time_step, reset_flags, climb),
        (left, pack, right, message, *heard, *weights),
        scratch(),
        flops=1000000000,
    )
    band = around(state, "img")
    rows = 8 * ((images + 7) // 8)
    sums, extra = call(
        functools.partial(gram_kernel, images),
        (shape((rows, LANES), F32), shape((8 + 3 * rows, atoms), F32)),
        (),
        (state, *band),
    )
    others = around(sums, "dom")
    new_disp, new_veloc, records, path = call(
        functools.partial(final_kernel, images, len(others), atoms * domains),
        (shape(disp.shape, F32), shape(disp.shape, F32), shape((8, LANES), F32), shape((1, LANES), F32)),
        (climb,),
        (state, extra, sums, *others),
    )
    return new_disp, new_veloc, records[0:4, 0].reshape(2, 2, 1), path[0, 0:1]


def solution(mesh):
    in_specs = (
        P(("group", "img"), None, "dom"),
        P(("group", "img"), None, "dom"),
        P(("group", "img")),
        P(None, ("group", "img")),
        P("group"),
        P(("group", "dom")),
        P(None, ("group", "dom")),
        P(("group", "dom")),
        P(None, None, ("group", "dom")),
        P(),
        P(),
        P(),
        P(),
        P(),
    )
    out_specs = (
        P(("group", "img"), None, "dom"),
        P(("group", "img"), None, "dom"),
        P(None, None, ("group", "img")),
        P(("group", "img")),
    )
    return jax.shard_map(local, mesh=mesh, in_specs=in_specs, out_specs=out_specs, check_vma=False)
```

```python
import functools
import math

import jax
import jax.numpy as jnp
from jax import lax
from jax.experimental import pallas as pl
from jax.experimental.pallas import tpu as pltpu
from jax.sharding import PartitionSpec as P

F32 = jnp.float32
BF16 = jnp.bfloat16
PRECISE = lax.Precision.HIGHEST
SPRING_CONSTANT = 0.5
ALPHA_START = 0.1
STEP_LIMIT = 0.3
TINY_VALUE = 1e-06
SOFTENING = 0.25
LANES = 128
SLOTS = 8
BASIS = 8
CHANNELS = 64
SLAB_BLOCKS = 4
ROW_X = 32
ROW_COUNT = 35
ROW_KIND = 36
ROW_V = 37
PACK_ROWS = 40
NT = (((1,), (1,)), ((), ()))


def split(x):
    high = x.astype(BF16).astype(F32)
    return high, x - high


def left_stack(w):
    high, low = split(w)
    return jnp.concatenate([high, high, low], axis=1)


def right_stack(x):
    high, low = split(x)
    high = high.astype(BF16)
    return jnp.concatenate([high, low.astype(BF16), high], axis=0)


def pair_stack(x):
    high, low = split(x)
    return jnp.concatenate([high.astype(BF16), low.astype(BF16)], axis=0)


def mm(a, b):
    return jnp.dot(a, b, preferred_element_type=F32)


def mm_nt(a, b):
    return lax.dot_general(a, b, NT, preferred_element_type=F32)


def pack_kernel(x_ref, v_ref, species_ref, nbr_ref, counts_ref, lattice_ref, out_ref):
    out_ref[0:8, :] = nbr_ref[...].astype(F32)
    for c in range(3):
        out_ref[8 + 8 * c : 16 + 8 * c, :] = lattice_ref[c]
        out_ref[ROW_X + c : ROW_X + c + 1, :] = x_ref[c]
        out_ref[ROW_V + c : ROW_V + c + 1, :] = v_ref[c]
    out_ref[ROW_COUNT : ROW_COUNT + 1, :] = counts_ref[...].astype(F32).reshape(1, -1)
    out_ref[ROW_KIND : ROW_KIND + 1, :] = species_ref[...].astype(F32).reshape(1, -1)


def weight_kernel(
    embed_ref, radial_ref, mix_ref, update_ref, readout_ref, l1_ref, l2_ref, l3_ref, l5_ref, l6_ref, col_ref
):
    eye = (
        lax.broadcasted_iota(jnp.int32, (CHANNELS, CHANNELS), 0)
        == lax.broadcasted_iota(jnp.int32, (CHANNELS, CHANNELS), 1)
    ).astype(F32)

    def turned(x):
        return lax.dot_general(eye, x, NT, precision=PRECISE, preferred_element_type=F32)

    base0 = embed_ref[0:1, :]
    base1 = embed_ref[1:2, :] - base0
    rows = jnp.concatenate([base0, base1], axis=0)
    sent = jnp.dot(rows, mix_ref[0], precision=PRECISE, preferred_element_type=F32)
    scale = 1.0 / math.sqrt(SLOTS)
    first = jnp.concatenate([radial_ref[0] * sent[0:1], radial_ref[0] * sent[1:2]], axis=0) * scale
    second = radial_ref[1] * scale
    folded = jnp.dot(update_ref[0], mix_ref[1], precision=PRECISE, preferred_element_type=F32)
    mix_t = turned(mix_ref[1])
    l1_ref[...] = left_stack(turned(first)).astype(BF16)
    l2_ref[...] = left_stack(turned(folded)).astype(BF16)
    high, low = split(turned(second))
    l3_ref[...] = jnp.concatenate([high, high, low, jnp.zeros_like(high)], axis=1).astype(BF16)
    l5_ref[...] = left_stack(folded).astype(BF16)
    l6_ref[...] = left_stack(first).astype(BF16)
    readout = readout_ref[...].reshape(1, CHANNELS)
    wide = (CHANNELS, LANES)
    col_ref[0] = jnp.broadcast_to(jnp.sum(mix_t * base0, axis=1, keepdims=True), wide)
    col_ref[1] = jnp.broadcast_to(jnp.sum(mix_t * base1, axis=1, keepdims=True), wide)
    col_ref[2] = jnp.broadcast_to(jnp.sum(update_ref[0] * readout, axis=1, keepdims=True), wide)
    col_ref[3] = jnp.broadcast_to(jnp.sum(update_ref[1] * readout, axis=1, keepdims=True), wide)


def sin_cos(t):
    q = t * t
    s = -1.0 / 39916800.0
    for c in (1.0 / 362880.0, -1.0 / 5040.0, 1.0 / 120.0, -1.0 / 6.0, 1.0):
        s = s * q + c
    k = 1.0 / 479001600.0
    for c in (-1.0 / 3628800.0, 1.0 / 40320.0, -1.0 / 720.0, 1.0 / 24.0, -0.5, 1.0):
        k = k * q + c
    return s * t, k


def wide_row(x, row):
    return jnp.broadcast_to(x[row : row + 1, :], (8, x.shape[1]))


def silu_parts(m):
    sig = 1.0 / (1.0 + jnp.exp(-m))
    return m * sig, sig * (1.0 + m * (1.0 - sig))


def force_parts(packs, weights, scr):
    l1, l2, l3, l5, l6, col = weights
    (xs, widx, kinds, geo, bst, bps, bpr, sst, ghl, slope, hot, dg, pulls, acc) = scr
    centre = 2.0 + 0.5 * lax.broadcasted_iota(jnp.int32, (BASIS, LANES), 0).astype(F32)
    slot = lax.broadcasted_iota(jnp.int32, (SLOTS, LANES), 0)
    row_id = lax.broadcasted_iota(jnp.int32, (3 * LANES, LANES), 0)

    def part_rows(value):
        high, low = split(value)
        return jnp.concatenate([high, low], axis=0).astype(BF16)

    def pairs(b):
        pack = packs[b // 4]
        lanes = slice((b % 4) * LANES, (b % 4 + 1) * LANES)
        index = pack[0:8, lanes].astype(jnp.int32) - LANES * (b % 4)
        widx[b] = index
        inner = index & (LANES - 1)
        part = index >> 7

        def taken(row):
            got = [
                jnp.take_along_axis(jnp.broadcast_to(xs[b - 1 + w, row : row + 1, :], (SLOTS, LANES)), inner, axis=1)
                for w in range(3)
            ]
            return jnp.where(part == 0, got[0], jnp.where(part == 1, got[1], got[2]))

        vec = [
            pack[8 + 8 * c : 16 + 8 * c, lanes] + taken(c) - jnp.broadcast_to(xs[b, c : c + 1, :], (SLOTS, LANES))
            for c in range(3)
        ]
        kind = taken(3)
        dist = jnp.sqrt(vec[0] * vec[0] + vec[1] * vec[1] + vec[2] * vec[2] + SOFTENING)
        live = (slot.astype(F32) < jnp.broadcast_to(pack[ROW_COUNT : ROW_COUNT + 1, lanes], (SLOTS, LANES))).astype(F32)
        turns = dist * (1.0 / 12.0)
        turns = turns - jnp.floor(turns + 0.5)
        sine, cosine = sin_cos(turns * math.pi)
        envelope = cosine * cosine * live
        slant = cosine * sine * live * (-math.pi / 6.0)
        if 3 <= b <= 8:
            kinds[b] = kind
            for c in range(3):
                geo[b, c] = vec[c]
            geo[b, 3] = 1.0 / dist
        total = jnp.zeros((BASIS, LANES), F32)
        total_kind = jnp.zeros((BASIS, LANES), F32)
        for k in range(SLOTS):
            away = wide_row(dist, k) - centre
            gauss = jnp.exp(-4.0 * (away * away))
            env_k = wide_row(envelope, k)
            value = gauss * env_k
            total = total + value
            total_kind = total_kind + value * wide_row(kind, k)
            cols = slice(k * LANES, (k + 1) * LANES)
            if 2 <= b <= 9:
                bst[b, :, cols] = part_rows(value)
            if 3 <= b <= 8:
                value = gauss * (wide_row(slant, k) - 8.0 * away * env_k)
                bpr[b, :, cols] = value
                bps[b, :, cols] = part_rows(value)
        high, low = split(jnp.concatenate([total, total_kind], axis=0))
        sst[:, b * LANES : (b + 1) * LANES] = jnp.concatenate([high, low, high], axis=0).astype(BF16)

    for b in range(1, 11):
        pairs(b)

    for b in range(1, 11, 2):
        cols = slice(b * LANES, (b + 2) * LANES)
        value, steep = silu_parts(mm(l1[...], sst[:, cols]))
        sent = mm(l2[...], right_stack(value))
        for i in range(2):
            one = sent[:, i * LANES : (i + 1) * LANES]
            one = one + col[0] + col[1] * jnp.broadcast_to(xs[b + i, 3:4, :], (CHANNELS, LANES))
            ghl[:, (b + i) * LANES : (b + i + 1) * LANES] = pair_stack(one)
        slope[:, cols] = steep

    def mark(b):
        index = widx[b]
        for k in range(SLOTS):
            same = row_id == jnp.broadcast_to(index[k : k + 1, :], (3 * LANES, LANES))
            hot[b, :, k * LANES : (k + 1) * LANES] = jnp.where(same, 1.0, 0.0).astype(BF16)

    def reach(b, first, last):
        return [w for w in range(3) if first <= b - 1 + w <= last]

    def spread(left, b, first, last):
        ws = reach(b, first, last)
        return ws, mm_nt(left, hot[b, ws[0] * LANES : (ws[-1] + 1) * LANES, :])

    started = set()

    def gather_and_return(b):
        got = mm(ghl[:, (b - 1) * LANES : (b + 2) * LANES], hot[b])
        if b < 9:
            mark(b + 1)
        got = got[:CHANNELS] + got[CHANNELS:]
        basis = bst[b]
        radial = mm(l3[...], jnp.concatenate([basis, basis], axis=0))
        message = jnp.zeros((CHANNELS, LANES), F32)
        for k in range(SLOTS):
            cols = slice(k * LANES, (k + 1) * LANES)
            message = message + radial[:, cols] * got[:, cols]
        _, steep = silu_parts(message)
        back = jnp.concatenate([col[3] * steep] * SLOTS, axis=1)
        ws, out = spread(pair_stack(radial * back), b, 3, 8)
        out = out[:CHANNELS] + out[CHANNELS:]
        for i, w in enumerate(ws):
            target = b - 1 + w
            piece = out[:, i * LANES : (i + 1) * LANES]
            where = slice(target * LANES, (target + 1) * LANES)
            if target in started:
                dg[:, where] += piece
            else:
                dg[:, where] = piece
                started.add(target)
        if 3 <= b <= 8:
            basis = bps[b]
            steepness = mm(l3[...], jnp.concatenate([basis, basis], axis=0))
            pull = got * back * steepness
            total = pull[0:8]
            for i in range(1, CHANNELS // 8):
                total = total + pull[8 * i : 8 * i + 8]
            pulls[b] = total

    mark(2)
    for b in range(2, 10):
        gather_and_return(b)

    begun = set()

    def put(b, c, value):
        if (b, c) in begun:
            acc[b, c] += value
        else:
            acc[b, c] = value
            begun.add((b, c))

    def finish(b, sums):
        kind = kinds[b]
        rows = []
        for k in range(SLOTS):
            cols = slice(k * LANES, (k + 1) * LANES)
            weight = sums[0:8] + wide_row(kind, k) * sums[8:16]
            rows.append(jnp.sum(bpr[b, :, cols] * weight + pulls[b, :, cols], axis=0, keepdims=True))
        pull = jnp.concatenate(rows, axis=0) * geo[b, 3]
        pieces = []
        for c in range(3):
            value = pull * geo[b, c]
            if 4 <= b <= 7:
                put(b, c, -value)
            pieces.append(split(value))
        lines = []
        for h in range(2):
            for c in range(3):
                lines.append(jnp.concatenate([jnp.where(slot == k, pieces[c][h], 0.0) for k in range(SLOTS)], axis=1))
        ws, out = spread(jnp.concatenate(lines, axis=0).astype(BF16), b, 4, 7)
        for c in range(3):
            both = out[8 * c : 8 * c + 8] + out[24 + 8 * c : 32 + 8 * c]
            for i, w in enumerate(ws):
                put(b - 1 + w, c, both[:, i * LANES : (i + 1) * LANES])

    for b in range(3, 9, 2):
        cols = slice(b * LANES, (b + 2) * LANES)
        steep = mm(l5[...], right_stack(dg[:, cols]))
        steep = steep + jnp.concatenate([col[2], col[2]], axis=1)
        sums = mm(l6[...], right_stack(steep * slope[:, cols]))
        for i in range(2):
            finish(b + i, sums[:, i * LANES : (i + 1) * LANES])


def own_force(acc, c):
    return jnp.concatenate(
        [-jnp.sum(acc[4 + i, c], axis=0, keepdims=True) for i in range(SLAB_BLOCKS)], axis=1
    )


def fill_region(xs, packs, rows_of):
    for b in range(12):
        lanes = slice((b % 4) * LANES, (b % 4 + 1) * LANES)
        pack = packs[b // 4]
        xs[b, 0:3, :] = rows_of(b // 4)[:, lanes]
        xs[b, 3:4, :] = pack[ROW_KIND : ROW_KIND + 1, lanes]


def lane_total(x):
    x = x[:, 0:LANES] + x[:, LANES : 2 * LANES] + x[:, 2 * LANES : 3 * LANES] + x[:, 3 * LANES : 4 * LANES]
    return jnp.sum(x, axis=1, keepdims=True)


def dot3(a, b):
    return jnp.sum(a * b, axis=0, keepdims=True)


def scratch():
    wide = 12 * LANES
    return [
        pltpu.VMEM((12, 8, LANES), F32),
        pltpu.VMEM((12, 8, LANES), jnp.int32),
        pltpu.VMEM((12, 8, LANES), F32),
        pltpu.VMEM((12, 4, 8, LANES), F32),
        pltpu.VMEM((12, 16, SLOTS * LANES), BF16),
        pltpu.VMEM((12, 16, SLOTS * LANES), BF16),
        pltpu.VMEM((12, 8, SLOTS * LANES), F32),
        pltpu.VMEM((48, wide), BF16),
        pltpu.VMEM((2 * CHANNELS, wide), BF16),
        pltpu.VMEM((CHANNELS, wide), F32),
        pltpu.VMEM((12, 3 * LANES, SLOTS * LANES), BF16),
        pltpu.VMEM((CHANNELS, wide), F32),
        pltpu.VMEM((12, 8, SLOTS * LANES), F32),
        pltpu.VMEM((12, 3, 8, LANES), F32),
    ]


def first_kernel(pl_ref, po_ref, pr_ref, *rest):
    weights, out_ref, scr = rest[:6], rest[6], rest[7:]
    packs = [pl_ref, po_ref, pr_ref]
    fill_region(scr[0], packs, lambda s: packs[s][ROW_X : ROW_X + 3, :])
    force_parts(packs, weights, scr)
    for c in range(3):
        out_ref[c : c + 1, :] = own_force(scr[-1], c)


def rows_of(ref):
    return jnp.concatenate([ref[c] for c in range(3)], axis=0)


def block_row(*values):
    values = list(values) + [jnp.zeros((1, LANES), F32)] * (SLAB_BLOCKS - len(values))
    return jnp.concatenate(values, axis=1)


def blend_kernel(images, force_ref, po_ref, *rest):
    before_ref, after_ref, out_ref = rest[0], rest[images - 2], rest[-1]
    here = lax.axis_index("img")
    x = po_ref[ROW_X : ROW_X + 3, :]
    v = po_ref[ROW_V : ROW_V + 3, :]
    force = force_ref[...]
    before = jnp.where(here > 0, rows_of(before_ref), 0.0)
    after = jnp.where(here < images - 1, rows_of(after_ref), 0.0)
    tangent = after - before
    plus = after - x
    minus = x - before
    sums = jnp.concatenate(
        [
            dot3(force, tangent),
            dot3(force, force),
            dot3(tangent, tangent),
            dot3(plus, plus),
            dot3(minus, minus),
            dot3(v, v),
            jnp.zeros((2, x.shape[1]), F32),
        ],
        axis=0,
    )
    sums = jnp.broadcast_to(lane_total(sums), (8, LANES))
    out_ref[0:3, :] = force
    out_ref[3:6, :] = tangent
    out_ref[6:7, :] = block_row(*[sums[i : i + 1] for i in range(4)])
    out_ref[7:8, :] = block_row(sums[4:5], sums[5:6])


def step_numbers(ft, ff, tt, pp, mn, vv, dt, alpha, flagged, climbing, inside):
    root = jnp.sqrt(tt + TINY_VALUE)
    along = ft / root
    spring = SPRING_CONSTANT * (jnp.sqrt(pp) - jnp.sqrt(mn))
    factor = jnp.where(climbing, -2.0 * along, spring - along)
    band = jnp.maximum(ff + 2.0 * factor * along + factor * factor * (tt / (tt + TINY_VALUE)), 0.0)
    new_dt = jnp.where(flagged, 0.5 * dt, jnp.minimum(1.1 * dt, STEP_LIMIT))
    pull = jnp.where(flagged, 0.0, alpha * jnp.sqrt(vv / (band + TINY_VALUE))) + new_dt
    keep = jnp.where(flagged, 0.0, 1.0 - alpha)
    new_alpha = jnp.where(flagged, ALPHA_START, 0.99 * alpha)
    keep = jnp.where(inside, keep, 0.0)
    pull = jnp.where(inside, pull, 0.0)
    return (
        jnp.where(inside, along, 0.0),
        jnp.where(inside, spring, 0.0),
        keep,
        pull,
        pull * factor / root,
        new_dt,
        new_alpha,
    )


def second_kernel(images, others, dt_ref, flag_ref, climb_ref, pl_ref, po_ref, pr_ref, own_ref, *rest):
    heard, rest = rest[:others], rest[others:]
    weights, out_ref, scr = rest[:6], rest[6], rest[7:]
    packs = [pl_ref, po_ref, pr_ref]
    here = lax.axis_index("img")
    sums = own_ref[6:8, :]
    for one in heard:
        sums = sums + one[6:8, :]
    ft, ff, tt, pp = (sums[0:1, i * LANES : (i + 1) * LANES] for i in range(4))
    mn, vv = (sums[1:2, i * LANES : (i + 1) * LANES] for i in range(2))
    shape = (1, LANES)
    along, spring, keep, pull, side, dt, alpha = step_numbers(
        ft,
        ff,
        tt,
        pp,
        mn,
        vv,
        jnp.full(shape, dt_ref[0], F32),
        jnp.full(shape, ALPHA_START, F32),
        jnp.full(shape, flag_ref[0, 0], jnp.int32) == 1,
        jnp.full(shape, here - climb_ref[0], jnp.int32) == 0,
        jnp.full(shape, jnp.where((here >= 1) & (here <= images - 2), 1, 0), jnp.int32) == 1,
    )
    messages = [heard[0], own_ref, heard[others - 1]]

    def wide(s):
        return jnp.concatenate([s] * SLAB_BLOCKS, axis=1)

    speeds = [
        wide(keep) * p[ROW_V : ROW_V + 3, :] + wide(pull) * m[0:3, :] + wide(side) * m[3:6, :]
        for p, m in zip(packs, messages)
    ]
    moved = [p[ROW_X : ROW_X + 3, :] + wide(dt) * s for p, s in zip(packs, speeds)]
    fill_region(scr[0], packs, lambda s: moved[s])
    force_parts(packs, weights, scr)
    out_ref[0:3, :] = speeds[1]
    for c in range(3):
        out_ref[3 + c : 4 + c, :] = own_force(scr[-1], c)
    out_ref[6:7, :] = block_row(dt, alpha, jnp.full(shape, flag_ref[0, 1], jnp.int32).astype(F32))
    out_ref[7:8, :] = block_row(along, spring)


PRODUCTS = (
    [("f", "t"), ("f", "f"), ("t", "t"), ("p", "p"), ("d", "d"), ("v", "v")]
    + [("d", "v"), ("d", "f"), ("d", "t"), ("d", "V"), ("d", "F"), ("d", "T"), ("v", "f"), ("v", "t")]
    + [(a, b) for a in "vft" for b in "VFT"]
)


def gram_kernel(images, *refs):
    messages, starts, (out_ref, state_ref) = refs[:images], refs[images : 2 * images], refs[2 * images :]
    rows = 8 * ((images + 7) // 8)
    here = lax.axis_index("img")
    width = state_ref.shape[1]
    blank = jnp.zeros((rows - images, width), F32)

    def padded(lines):
        return jnp.concatenate(lines + ([blank[:, : lines[0].shape[1]]] if rows > images else []), axis=0)

    def gathered(row):
        return padded([m[row : row + 1, :] for m in messages])

    def number_of(i):
        return padded([m[6:7, i * LANES : (i + 1) * LANES] for m in messages])

    steps = jnp.concatenate([number_of(0)] * SLAB_BLOCKS, axis=1)

    def shifted(value, by):
        lines = [value[(s + by) % images : (s + by) % images + 1, :] for s in range(images)]
        return jnp.concatenate(lines + ([blank] if rows > images else []), axis=0)

    offset = lax.broadcasted_iota(jnp.int32, (rows, width), 0)
    number = here - offset
    number = jnp.where(number < 0, number + images, number)
    has_after = (number < images - 1) & (offset < images)
    has_before = (number > 0) & (offset < images)
    totals = [jnp.zeros((rows, width), F32) for _ in PRODUCTS]
    for c in range(3):
        v, f = gathered(c), gathered(3 + c)
        x = padded([s[c] for s in starts]) + steps * v
        after = jnp.where(has_after, shifted(x, -1), 0.0)
        before = jnp.where(has_before, shifted(x, 1), 0.0)
        t = after - before
        table = {"f": f, "v": v, "t": t, "p": after - x, "d": x - before}
        table["F"] = jnp.where(has_before, shifted(f, 1), 0.0)
        table["V"] = jnp.where(has_before, shifted(v, 1), 0.0)
        table["T"] = jnp.where(has_before, shifted(t, 1), 0.0)
        totals = [old + table[a] * table[b] for old, (a, b) in zip(totals, PRODUCTS)]
        state_ref[c : c + 1, :] = t[0:1]
        state_ref[3 + c : 4 + c, :] = x[0:1]
    lane = lax.broadcasted_iota(jnp.int32, (rows, LANES), 1)
    result = jnp.zeros((rows, LANES), F32)
    for q, one in enumerate(totals):
        result = jnp.where(lane == q, jnp.broadcast_to(lane_total(one), (rows, LANES)), result)
    out_ref[...] = result
    for i in range(3):
        state_ref[8 : 8 + rows, i * LANES : (i + 1) * LANES] = number_of(i)


def final_kernel(images, others, atoms, climb_ref, own_ref, state_ref, sums_ref, *rest):
    heard, (x_ref, v_ref, band_ref, path_ref) = rest[:others], rest[others:]
    rows = sums_ref.shape[0]
    here = lax.axis_index("img")
    sums = sums_ref[...]
    for one in heard:
        sums = sums + one[...]
    got = {
        pair: jnp.broadcast_to(sums[:, q : q + 1], (rows, LANES)) for q, pair in enumerate(PRODUCTS)
    }
    offset = lax.broadcasted_iota(jnp.int32, (rows, LANES), 0)
    number = here - offset
    number = jnp.where(number < 0, number + images, number)
    inside = (number >= 1) & (number <= images - 2) & (offset < images)
    has_before = (number > 0) & (offset < images)
    climb = jnp.full((rows, LANES), climb_ref[0], jnp.int32)
    dt0, alpha0, flag = (state_ref[8 : 8 + rows, i * LANES : (i + 1) * LANES] for i in range(3))
    along, spring, keep, pull, side, dt, _ = step_numbers(
        got["f", "t"],
        got["f", "f"],
        got["t", "t"],
        got["p", "p"],
        got["d", "d"],
        got["v", "v"],
        dt0,
        alpha0,
        flag == 1.0,
        number == climb,
        inside,
    )

    def shifted(value):
        lines = [value[(s + 1) % images : (s + 1) % images + 1, :] for s in range(images)]
        if rows > images:
            lines.append(jnp.zeros((rows - images, LANES), F32))
        return jnp.where(has_before, jnp.concatenate(lines, axis=0), 0.0)

    now = {"v": dt * keep, "f": dt * pull, "t": dt * side}
    old = {a.upper(): shifted(value) for a, value in now.items()}
    mine = now["v"] * now["v"] * got["v", "v"] + now["f"] * now["f"] * got["f", "f"]
    mine = mine + now["t"] * now["t"] * got["t", "t"]
    cross = now["v"] * now["f"] * got["v", "f"] + now["v"] * now["t"] * got["v", "t"]
    mine = mine + 2.0 * (cross + now["f"] * now["t"] * got["f", "t"])
    both = jnp.zeros((rows, LANES), F32)
    for a in "vft":
        both = both + now[a] * got["d", a]
    for b in "VFT":
        both = both - old[b] * got["d", b]
    for a in "vft":
        for b in "VFT":
            both = both - now[a] * old[b] * got[a, b]
    squared = got["d", "d"] + mine + shifted(mine) + 2.0 * both
    segment = jnp.sqrt(jnp.maximum(squared, 0.0) * (1.0 / (3.0 * atoms)))
    path = jnp.sum(jnp.where(offset <= here, segment, 0.0), axis=0, keepdims=True)
    path_ref[...] = path[:, 0:1]

    def wide(s):
        return jnp.concatenate([s[0:1, :]] * SLAB_BLOCKS, axis=1)

    speed = wide(keep) * own_ref[0:3, :] + wide(pull) * own_ref[3:6, :] + wide(side) * state_ref[0:3, :]
    moved = state_ref[3:6, :] + wide(dt) * speed
    for c in range(3):
        v_ref[c] = speed[c : c + 1]
        x_ref[c] = moved[c : c + 1]
    band_ref[0] = jnp.concatenate([own_ref[7:8, 0:1], own_ref[7:8, LANES : LANES + 1]], axis=1)
    band_ref[1] = jnp.concatenate([along[0:1, 0:1], spring[0:1, 0:1]], axis=1)


VMEM_SPEC = pl.BlockSpec(memory_space=pltpu.VMEM)
SMEM_SPEC = pl.BlockSpec(memory_space=pltpu.SMEM)


def call(body, outs, scalars, arrays, scratch_shapes=(), flops=0):
    return pl.pallas_call(
        body,
        out_shape=outs,
        in_specs=[SMEM_SPEC] * len(scalars) + [VMEM_SPEC] * len(arrays),
        out_specs=jax.tree.map(lambda _: VMEM_SPEC, outs),
        scratch_shapes=list(scratch_shapes),
        compiler_params=pltpu.CompilerParams(vmem_limit_bytes=48 * 1024 * 1024),
        cost_estimate=pl.CostEstimate(flops=flops, bytes_accessed=1 << 18, transcendentals=0),
    )(*scalars, *arrays)


def around(array, axis):
    count = lax.axis_size(axis)
    return [lax.ppermute(array, axis, [(i, (i + s) % count) for i in range(count)]) for s in range(1, count)]


def ring(array, axis, by):
    count = lax.axis_size(axis)
    return lax.ppermute(array, axis, [(i, (i + by) % count) for i in range(count)])


def local(
    disp,
    veloc,
    time_step,
    reset_flags,
    climb,
    species,
    neighbours,
    counts,
    lattice,
    embed,
    radial_weight,
    mix_weight,
    update_weight,
    readout,
):
    atoms = disp.shape[2]
    images = lax.axis_size("img")
    domains = lax.axis_size("dom")
    assert disp.shape[0] == 1 and atoms == SLAB_BLOCKS * LANES and domains >= 3
    shape = jax.ShapeDtypeStruct
    x = jnp.transpose(disp, (1, 0, 2))
    v = jnp.transpose(veloc, (1, 0, 2))
    pack = call(
        pack_kernel,
        shape((PACK_ROWS, atoms), F32),
        (),
        (x, v, species, neighbours, counts, jnp.transpose(lattice, (1, 0, 2))),
    )
    left, right = ring(pack, "dom", 1), ring(pack, "dom", -1)
    starts = around(x, "img")
    weights = call(
        weight_kernel,
        (
            shape((CHANNELS, 48), BF16),
            shape((CHANNELS, 192), BF16),
            shape((CHANNELS, 32), BF16),
            shape((CHANNELS, 192), BF16),
            shape((16, 192), BF16),
            shape((4, CHANNELS, LANES), F32),
        ),
        (),
        (embed, radial_weight, mix_weight, update_weight, readout),
        flops=10000000,
    )
    force = call(
        first_kernel, shape((3, atoms), F32), (), (left, pack, right, *weights), scratch(), flops=1000000000
    )
    message = call(
        functools.partial(blend_kernel, images), shape((8, atoms), F32), (), (force, pack, *starts)
    )
    heard = around(message, "dom")
    state = call(
        functools.partial(second_kernel, images, len(heard)),
        shape((8, atoms), F32),
        (time_step, jnp.transpose(reset_flags), climb),
        (left, pack, right, message, *heard, *weights),
        scratch(),
        flops=1000000000,
    )
    band = around(state, "img")
    rows = 8 * ((images + 7) // 8)
    sums, extra = call(
        functools.partial(gram_kernel, images),
        (shape((rows, LANES), F32), shape((8 + rows, atoms), F32)),
        (),
        (state, *band, x, *starts),
    )
    others = around(sums, "dom")
    new_x, new_v, records, path = call(
        functools.partial(final_kernel, images, len(others), atoms * domains),
        (shape(x.shape, F32), shape(x.shape, F32), shape((2, 1, 2), F32), shape((1, 1), F32)),
        (climb,),
        (state, extra, sums, *others),
    )
    return (
        jnp.transpose(new_x, (1, 0, 2)),
        jnp.transpose(new_v, (1, 0, 2)),
        jnp.transpose(records, (0, 2, 1)),
        path.reshape(1),
    )


def solution(mesh):
    in_specs = (
        P(("group", "img"), None, "dom"),
        P(("group", "img"), None, "dom"),
        P(("group", "img")),
        P(None, ("group", "img")),
        P("group"),
        P(("group", "dom")),
        P(None, ("group", "dom")),
        P(("group", "dom")),
        P(None, None, ("group", "dom")),
        P(),
        P(),
        P(),
        P(),
        P(),
    )
    out_specs = (
        P(("group", "img"), None, "dom"),
        P(("group", "img"), None, "dom"),
        P(None, None, ("group", "img")),
        P(("group", "img")),
    )
    return jax.shard_map(local, mesh=mesh, in_specs=in_specs, out_specs=out_specs, check_vma=False)
```

```python
import functools
import math

import jax
import jax.numpy as jnp
from jax import lax
from jax.experimental import pallas as pl
from jax.experimental.pallas import tpu as pltpu
from jax.sharding import PartitionSpec as P

F32 = jnp.float32
BF16 = jnp.bfloat16
PRECISE = lax.Precision.HIGHEST
SPRING_CONSTANT = 0.5
ALPHA_START = 0.1
STEP_LIMIT = 0.3
TINY_VALUE = 1e-06
SOFTENING = 0.25
LANES = 128
SLOTS = 8
BASIS = 8
CHANNELS = 64
SLAB_BLOCKS = 4
ROW_X = 32
ROW_COUNT = 35
ROW_KIND = 36
ROW_V = 37
PACK_ROWS = 40
NT = (((1,), (1,)), ((), ()))


def split(x):
    high = x.astype(BF16).astype(F32)
    return high, x - high


def left_stack(w):
    high, low = split(w)
    return jnp.concatenate([high, high, low], axis=1)


def right_stack(x):
    high, low = split(x)
    high = high.astype(BF16)
    return jnp.concatenate([high, low.astype(BF16), high], axis=0)


def pair_stack(x):
    high, low = split(x)
    return jnp.concatenate([high.astype(BF16), low.astype(BF16)], axis=0)


def mm(a, b):
    return jnp.dot(a, b, preferred_element_type=F32)


def mm_nt(a, b):
    return lax.dot_general(a, b, NT, preferred_element_type=F32)


def pack_kernel(x_ref, v_ref, species_ref, nbr_ref, counts_ref, lattice_ref, out_ref, x, v, species, nbr, counts, sems):
    copies = [
        pltpu.make_async_copy(source, target, sems.at[i])
        for i, (source, target) in enumerate(
            [(x_ref, x), (v_ref, v), (species_ref, species), (nbr_ref, nbr), (counts_ref, counts)]
            + [(lattice_ref.at[c], out_ref.at[pl.ds(8 + 8 * c, 8)]) for c in range(3)]
        )
    ]
    for one in copies:
        one.start()
    for one in copies:
        one.wait()
    out_ref[0:8, :] = nbr[...].astype(F32)
    for c in range(3):
        out_ref[ROW_X + c : ROW_X + c + 1, :] = x[c]
        out_ref[ROW_V + c : ROW_V + c + 1, :] = v[c]
    out_ref[ROW_COUNT : ROW_COUNT + 1, :] = counts[...].astype(F32).reshape(1, -1)
    out_ref[ROW_KIND : ROW_KIND + 1, :] = species[...].astype(F32).reshape(1, -1)


def weight_kernel(
    embed_ref, radial_ref, mix_ref, update_ref, readout_ref, l1_ref, l2_ref, l3_ref, l5_ref, l6_ref, col_ref
):
    eye = (
        lax.broadcasted_iota(jnp.int32, (CHANNELS, CHANNELS), 0)
        == lax.broadcasted_iota(jnp.int32, (CHANNELS, CHANNELS), 1)
    ).astype(F32)

    def turned(x):
        return lax.dot_general(eye, x, NT, precision=PRECISE, preferred_element_type=F32)

    base0 = embed_ref[0:1, :]
    base1 = embed_ref[1:2, :] - base0
    rows = jnp.concatenate([base0, base1], axis=0)
    sent = jnp.dot(rows, mix_ref[0], precision=PRECISE, preferred_element_type=F32)
    scale = 1.0 / math.sqrt(SLOTS)
    first = jnp.concatenate([radial_ref[0] * sent[0:1], radial_ref[0] * sent[1:2]], axis=0) * scale
    second = radial_ref[1] * scale
    folded = jnp.dot(update_ref[0], mix_ref[1], precision=PRECISE, preferred_element_type=F32)
    mix_t = turned(mix_ref[1])
    l1_ref[...] = left_stack(turned(first)).astype(BF16)
    l2_ref[...] = left_stack(turned(folded)).astype(BF16)
    high, low = split(turned(second))
    l3_ref[...] = jnp.concatenate([high, high, low, jnp.zeros_like(high)], axis=1).astype(BF16)
    l5_ref[...] = left_stack(folded).astype(BF16)
    l6_ref[...] = left_stack(first).astype(BF16)
    readout = readout_ref[...].reshape(1, CHANNELS)
    wide = (CHANNELS, LANES)
    col_ref[0] = jnp.broadcast_to(jnp.sum(mix_t * base0, axis=1, keepdims=True), wide)
    col_ref[1] = jnp.broadcast_to(jnp.sum(mix_t * base1, axis=1, keepdims=True), wide)
    col_ref[2] = jnp.broadcast_to(jnp.sum(update_ref[0] * readout, axis=1, keepdims=True), wide)
    col_ref[3] = jnp.broadcast_to(jnp.sum(update_ref[1] * readout, axis=1, keepdims=True), wide)


def sin_cos(t):
    q = t * t
    s = -1.0 / 39916800.0
    for c in (1.0 / 362880.0, -1.0 / 5040.0, 1.0 / 120.0, -1.0 / 6.0, 1.0):
        s = s * q + c
    k = 1.0 / 479001600.0
    for c in (-1.0 / 3628800.0, 1.0 / 40320.0, -1.0 / 720.0, 1.0 / 24.0, -0.5, 1.0):
        k = k * q + c
    return s * t, k


def wide_row(x, row):
    return jnp.broadcast_to(x[row : row + 1, :], (8, x.shape[1]))


def silu_parts(m):
    sig = 1.0 / (1.0 + jnp.exp(-m))
    return m * sig, sig * (1.0 + m * (1.0 - sig))


def force_parts(packs, weights, scr):
    l1, l2, l3, l5, l6, col = weights
    (xs, widx, kinds, geo, bst, bps, bpr, sst, ghl, slope, hot, dg, pulls, acc) = scr
    centre = 2.0 + 0.5 * lax.broadcasted_iota(jnp.int32, (BASIS, LANES), 0).astype(F32)
    slot = lax.broadcasted_iota(jnp.int32, (SLOTS, LANES), 0)
    row_id = lax.broadcasted_iota(jnp.int32, (3 * LANES, LANES), 0)

    def part_rows(value):
        high, low = split(value)
        return jnp.concatenate([high, low], axis=0).astype(BF16)

    def pairs(b):
        pack = packs[b // 4]
        lanes = slice((b % 4) * LANES, (b % 4 + 1) * LANES)
        index = pack[0:8, lanes].astype(jnp.int32) - LANES * (b % 4)
        widx[b] = index
        inner = index & (LANES - 1)
        part = index >> 7

        def taken(row):
            got = [
                jnp.take_along_axis(jnp.broadcast_to(xs[b - 1 + w, row : row + 1, :], (SLOTS, LANES)), inner, axis=1)
                for w in range(3)
            ]
            return jnp.where(part == 0, got[0], jnp.where(part == 1, got[1], got[2]))

        vec = [
            pack[8 + 8 * c : 16 + 8 * c, lanes] + taken(c) - jnp.broadcast_to(xs[b, c : c + 1, :], (SLOTS, LANES))
            for c in range(3)
        ]
        kind = taken(3)
        dist = jnp.sqrt(vec[0] * vec[0] + vec[1] * vec[1] + vec[2] * vec[2] + SOFTENING)
        live = (slot.astype(F32) < jnp.broadcast_to(pack[ROW_COUNT : ROW_COUNT + 1, lanes], (SLOTS, LANES))).astype(F32)
        turns = dist * (1.0 / 12.0)
        turns = turns - jnp.floor(turns + 0.5)
        sine, cosine = sin_cos(turns * math.pi)
        envelope = cosine * cosine * live
        slant = cosine * sine * live * (-math.pi / 6.0)
        if 3 <= b <= 8:
            kinds[b] = kind
            for c in range(3):
                geo[b, c] = vec[c]
            geo[b, 3] = 1.0 / dist
        total = jnp.zeros((BASIS, LANES), F32)
        total_kind = jnp.zeros((BASIS, LANES), F32)
        for k in range(SLOTS):
            away = wide_row(dist, k) - centre
            gauss = jnp.exp(-4.0 * (away * away))
            env_k = wide_row(envelope, k)
            value = gauss * env_k
            total = total + value
            total_kind = total_kind + value * wide_row(kind, k)
            cols = slice(k * LANES, (k + 1) * LANES)
            if 2 <= b <= 9:
                bst[b, :, cols] = part_rows(value)
            if 3 <= b <= 8:
                value = gauss * (wide_row(slant, k) - 8.0 * away * env_k)
                bpr[b, :, cols] = value
                bps[b, :, cols] = part_rows(value)
        high, low = split(jnp.concatenate([total, total_kind], axis=0))
        sst[:, b * LANES : (b + 1) * LANES] = jnp.concatenate([high, low, high], axis=0).astype(BF16)

    for b in range(1, 11):
        pairs(b)

    for b in range(1, 11, 2):
        cols = slice(b * LANES, (b + 2) * LANES)
        value, steep = silu_parts(mm(l1[...], sst[:, cols]))
        sent = mm(l2[...], right_stack(value))
        for i in range(2):
            one = sent[:, i * LANES : (i + 1) * LANES]
            one = one + col[0] + col[1] * jnp.broadcast_to(xs[b + i, 3:4, :], (CHANNELS, LANES))
            ghl[:, (b + i) * LANES : (b + i + 1) * LANES] = pair_stack(one)
        slope[:, cols] = steep

    def mark(b):
        index = widx[b]
        for k in range(SLOTS):
            same = row_id == jnp.broadcast_to(index[k : k + 1, :], (3 * LANES, LANES))
            hot[b, :, k * LANES : (k + 1) * LANES] = jnp.where(same, 1.0, 0.0).astype(BF16)

    def reach(b, first, last):
        return [w for w in range(3) if first <= b - 1 + w <= last]

    def spread(left, b, first, last):
        ws = reach(b, first, last)
        return ws, mm_nt(left, hot[b, ws[0] * LANES : (ws[-1] + 1) * LANES, :])

    started = set()

    def gather_and_return(b):
        got = mm(ghl[:, (b - 1) * LANES : (b + 2) * LANES], hot[b])
        if b < 9:
            mark(b + 1)
        got = got[:CHANNELS] + got[CHANNELS:]
        basis = bst[b]
        radial = mm(l3[...], jnp.concatenate([basis, basis], axis=0))
        message = jnp.zeros((CHANNELS, LANES), F32)
        for k in range(SLOTS):
            cols = slice(k * LANES, (k + 1) * LANES)
            message = message + radial[:, cols] * got[:, cols]
        _, steep = silu_parts(message)
        back = jnp.concatenate([col[3] * steep] * SLOTS, axis=1)
        ws, out = spread(pair_stack(radial * back), b, 3, 8)
        out = out[:CHANNELS] + out[CHANNELS:]
        for i, w in enumerate(ws):
            target = b - 1 + w
            piece = out[:, i * LANES : (i + 1) * LANES]
            where = slice(target * LANES, (target + 1) * LANES)
            if target in started:
                dg[:, where] += piece
            else:
                dg[:, where] = piece
                started.add(target)
        if 3 <= b <= 8:
            basis = bps[b]
            steepness = mm(l3[...], jnp.concatenate([basis, basis], axis=0))
            pull = got * back * steepness
            total = pull[0:8]
            for i in range(1, CHANNELS // 8):
                total = total + pull[8 * i : 8 * i + 8]
            pulls[b] = total

    mark(2)
    for b in range(2, 10):
        gather_and_return(b)

    begun = set()

    def put(b, c, value):
        if (b, c) in begun:
            acc[b, c] += value
        else:
            acc[b, c] = value
            begun.add((b, c))

    def finish(b, sums):
        kind = kinds[b]
        rows = []
        for k in range(SLOTS):
            cols = slice(k * LANES, (k + 1) * LANES)
            weight = sums[0:8] + wide_row(kind, k) * sums[8:16]
            rows.append(jnp.sum(bpr[b, :, cols] * weight + pulls[b, :, cols], axis=0, keepdims=True))
        pull = jnp.concatenate(rows, axis=0) * geo[b, 3]
        pieces = []
        for c in range(3):
            value = pull * geo[b, c]
            if 4 <= b <= 7:
                put(b, c, -value)
            pieces.append(split(value))
        lines = []
        for h in range(2):
            for c in range(3):
                lines.append(jnp.concatenate([jnp.where(slot == k, pieces[c][h], 0.0) for k in range(SLOTS)], axis=1))
        ws, out = spread(jnp.concatenate(lines, axis=0).astype(BF16), b, 4, 7)
        for c in range(3):
            both = out[8 * c : 8 * c + 8] + out[24 + 8 * c : 32 + 8 * c]
            for i, w in enumerate(ws):
                put(b - 1 + w, c, both[:, i * LANES : (i + 1) * LANES])

    for b in range(3, 9, 2):
        cols = slice(b * LANES, (b + 2) * LANES)
        steep = mm(l5[...], right_stack(dg[:, cols]))
        steep = steep + jnp.concatenate([col[2], col[2]], axis=1)
        sums = mm(l6[...], right_stack(steep * slope[:, cols]))
        for i in range(2):
            finish(b + i, sums[:, i * LANES : (i + 1) * LANES])


def own_force(acc, c):
    return jnp.concatenate(
        [-jnp.sum(acc[4 + i, c], axis=0, keepdims=True) for i in range(SLAB_BLOCKS)], axis=1
    )


def fill_region(xs, packs, rows_of):
    for b in range(12):
        lanes = slice((b % 4) * LANES, (b % 4 + 1) * LANES)
        pack = packs[b // 4]
        xs[b, 0:3, :] = rows_of(b // 4)[:, lanes]
        xs[b, 3:4, :] = pack[ROW_KIND : ROW_KIND + 1, lanes]


def lane_total(x):
    x = x[:, 0:LANES] + x[:, LANES : 2 * LANES] + x[:, 2 * LANES : 3 * LANES] + x[:, 3 * LANES : 4 * LANES]
    return jnp.sum(x, axis=1, keepdims=True)


def dot3(a, b):
    return jnp.sum(a * b, axis=0, keepdims=True)


def scratch():
    wide = 12 * LANES
    return [
        pltpu.VMEM((12, 8, LANES), F32),
        pltpu.VMEM((12, 8, LANES), jnp.int32),
        pltpu.VMEM((12, 8, LANES), F32),
        pltpu.VMEM((12, 4, 8, LANES), F32),
        pltpu.VMEM((12, 16, SLOTS * LANES), BF16),
        pltpu.VMEM((12, 16, SLOTS * LANES), BF16),
        pltpu.VMEM((12, 8, SLOTS * LANES), F32),
        pltpu.VMEM((48, wide), BF16),
        pltpu.VMEM((2 * CHANNELS, wide), BF16),
        pltpu.VMEM((CHANNELS, wide), F32),
        pltpu.VMEM((12, 3 * LANES, SLOTS * LANES), BF16),
        pltpu.VMEM((CHANNELS, wide), F32),
        pltpu.VMEM((12, 8, SLOTS * LANES), F32),
        pltpu.VMEM((12, 3, 8, LANES), F32),
    ]


def first_kernel(pl_ref, po_ref, pr_ref, *rest):
    weights, out_ref, scr = rest[:6], rest[6], rest[7:]
    packs = [pl_ref, po_ref, pr_ref]
    fill_region(scr[0], packs, lambda s: packs[s][ROW_X : ROW_X + 3, :])
    force_parts(packs, weights, scr)
    for c in range(3):
        out_ref[c : c + 1, :] = own_force(scr[-1], c)


def rows_of(ref):
    return jnp.concatenate([ref[c] for c in range(3)], axis=0)


def block_row(*values):
    values = list(values) + [jnp.zeros((1, LANES), F32)] * (SLAB_BLOCKS - len(values))
    return jnp.concatenate(values, axis=1)


def blend_kernel(images, force_ref, po_ref, before_ref, after_ref, out_ref):
    here = lax.axis_index("img")
    x = po_ref[ROW_X : ROW_X + 3, :]
    v = po_ref[ROW_V : ROW_V + 3, :]
    force = force_ref[...]
    before = jnp.where(here > 0, rows_of(before_ref), 0.0)
    after = jnp.where(here < images - 1, rows_of(after_ref), 0.0)
    tangent = after - before
    plus = after - x
    minus = x - before
    sums = jnp.concatenate(
        [
            dot3(force, tangent),
            dot3(force, force),
            dot3(tangent, tangent),
            dot3(plus, plus),
            dot3(minus, minus),
            dot3(v, v),
            jnp.zeros((2, x.shape[1]), F32),
        ],
        axis=0,
    )
    sums = jnp.broadcast_to(lane_total(sums), (8, LANES))
    out_ref[0:3, :] = force
    out_ref[3:6, :] = tangent
    out_ref[6:7, :] = block_row(*[sums[i : i + 1] for i in range(4)])
    out_ref[7:8, :] = block_row(sums[4:5], sums[5:6])


def step_numbers(ft, ff, tt, pp, mn, vv, dt, alpha, flagged, climbing, inside):
    root = jnp.sqrt(tt + TINY_VALUE)
    along = ft / root
    spring = SPRING_CONSTANT * (jnp.sqrt(pp) - jnp.sqrt(mn))
    factor = jnp.where(climbing, -2.0 * along, spring - along)
    band = jnp.maximum(ff + 2.0 * factor * along + factor * factor * (tt / (tt + TINY_VALUE)), 0.0)
    new_dt = jnp.where(flagged, 0.5 * dt, jnp.minimum(1.1 * dt, STEP_LIMIT))
    pull = jnp.where(flagged, 0.0, alpha * jnp.sqrt(vv / (band + TINY_VALUE))) + new_dt
    keep = jnp.where(flagged, 0.0, 1.0 - alpha)
    new_alpha = jnp.where(flagged, ALPHA_START, 0.99 * alpha)
    keep = jnp.where(inside, keep, 0.0)
    pull = jnp.where(inside, pull, 0.0)
    return (
        jnp.where(inside, along, 0.0),
        jnp.where(inside, spring, 0.0),
        keep,
        pull,
        pull * factor / root,
        new_dt,
        new_alpha,
    )


def second_kernel(images, others, dt_ref, flag_ref, climb_ref, pl_ref, po_ref, pr_ref, own_ref, *rest):
    heard, rest = rest[:others], rest[others:]
    weights, out_ref, record_ref, scr = rest[:6], rest[6], rest[7], rest[8:]
    packs = [pl_ref, po_ref, pr_ref]
    here = lax.axis_index("img")
    sums = own_ref[6:8, :]
    for one in heard:
        sums = sums + one[6:8, :]
    ft, ff, tt, pp = (sums[0:1, i * LANES : (i + 1) * LANES] for i in range(4))
    mn, vv = (sums[1:2, i * LANES : (i + 1) * LANES] for i in range(2))
    shape = (1, LANES)
    along, spring, keep, pull, side, dt, alpha = step_numbers(
        ft,
        ff,
        tt,
        pp,
        mn,
        vv,
        jnp.full(shape, dt_ref[0], F32),
        jnp.full(shape, ALPHA_START, F32),
        jnp.full(shape, flag_ref[0, 0], jnp.int32) == 1,
        jnp.full(shape, here - climb_ref[0], jnp.int32) == 0,
        jnp.full(shape, jnp.where((here >= 1) & (here <= images - 2), 1, 0), jnp.int32) == 1,
    )
    messages = [heard[0], own_ref, heard[others - 1]]

    def wide(s):
        return jnp.concatenate([s] * SLAB_BLOCKS, axis=1)

    speeds = [
        wide(keep) * p[ROW_V : ROW_V + 3, :] + wide(pull) * m[0:3, :] + wide(side) * m[3:6, :]
        for p, m in zip(packs, messages)
    ]
    moved = [p[ROW_X : ROW_X + 3, :] + wide(dt) * s for p, s in zip(packs, speeds)]
    fill_region(scr[0], packs, lambda s: moved[s])
    force_parts(packs, weights, scr)
    for c in range(3):
        force = own_force(scr[-1], c)
        for i in range(SLAB_BLOCKS):
            lanes = slice(i * LANES, (i + 1) * LANES)
            row = 4 * c + i
            out_ref[row : row + 1, :] = speeds[1][c : c + 1, lanes]
            out_ref[12 + row : 13 + row, :] = force[:, lanes]
            out_ref[24 + row : 25 + row, :] = moved[1][c : c + 1, lanes]
    out_ref[36:37, :] = dt
    out_ref[37:38, :] = alpha
    out_ref[38:40, :] = jnp.full((2, LANES), flag_ref[0, 1], jnp.int32).astype(F32)
    record_ref[0:1, :] = along
    record_ref[1:2, :] = spring


PRODUCTS = (
    [("f", "t"), ("f", "f"), ("t", "t"), ("p", "p"), ("d", "d"), ("v", "v")]
    + [("d", "v"), ("d", "f"), ("d", "t"), ("d", "V"), ("d", "F"), ("d", "T"), ("v", "f"), ("v", "t")]
    + [(a, b) for a in "vft" for b in "VFT"]
)


def gram_kernel(images, *refs):
    messages, out_ref, state_ref = refs[:images], refs[images], refs[images + 1]
    rows = out_ref.shape[1]
    here = lax.axis_index("img")
    blank = [jnp.zeros((rows - images, LANES), F32)] if rows > images else []

    def gathered(row):
        return jnp.concatenate([m[row : row + 1, :] for m in messages] + blank, axis=0)

    def shifted(value, by):
        lines = [value[(s + by) % images : (s + by) % images + 1, :] for s in range(images)]
        return jnp.concatenate(lines + blank, axis=0)

    offset = lax.broadcasted_iota(jnp.int32, (rows, LANES), 0)
    number = here - offset
    number = jnp.where(number < 0, number + images, number)
    has_after = (number < images - 1) & (offset < images)
    has_before = (number > 0) & (offset < images)
    totals = [jnp.zeros((rows, LANES), F32) for _ in PRODUCTS]
    for row in range(3 * SLAB_BLOCKS):
        v, f, x = gathered(row), gathered(12 + row), gathered(24 + row)
        after = jnp.where(has_after, shifted(x, -1), 0.0)
        before = jnp.where(has_before, shifted(x, 1), 0.0)
        t = after - before
        table = {"f": f, "v": v, "t": t, "p": after - x, "d": x - before}
        table["F"] = jnp.where(has_before, shifted(f, 1), 0.0)
        table["V"] = jnp.where(has_before, shifted(v, 1), 0.0)
        table["T"] = jnp.where(has_before, shifted(t, 1), 0.0)
        totals = [old + table[a] * table[b] for old, (a, b) in zip(totals, PRODUCTS)]
        state_ref[row : row + 1, :] = t[0:1]
    lane = lax.broadcasted_iota(jnp.int32, (rows, LANES), 1)
    result = jnp.zeros((rows, LANES), F32)
    for q, one in enumerate(totals):
        one = jnp.broadcast_to(jnp.sum(one, axis=1, keepdims=True), (rows, LANES))
        result = jnp.where(lane == q, one, result)
    for d in range(out_ref.shape[0]):
        out_ref[d] = result
    for i in range(3):
        state_ref[16 + rows * i : 16 + rows * (i + 1), :] = gathered(36 + i)


def final_kernel(images, atoms, climb_ref, own_ref, record_ref, state_ref, sums_ref, x_ref, v_ref, band_ref, path_ref):
    rows = sums_ref.shape[1]
    here = lax.axis_index("img")
    sums = sums_ref[0]
    for d in range(1, sums_ref.shape[0]):
        sums = sums + sums_ref[d]
    got = {
        pair: jnp.broadcast_to(sums[:, q : q + 1], (rows, LANES)) for q, pair in enumerate(PRODUCTS)
    }
    offset = lax.broadcasted_iota(jnp.int32, (rows, LANES), 0)
    number = here - offset
    number = jnp.where(number < 0, number + images, number)
    inside = (number >= 1) & (number <= images - 2) & (offset < images)
    has_before = (number > 0) & (offset < images)
    climb = jnp.full((rows, LANES), climb_ref[0], jnp.int32)
    dt0, alpha0, flag = (state_ref[16 + rows * i : 16 + rows * (i + 1), :] for i in range(3))
    along, spring, keep, pull, side, dt, _ = step_numbers(
        got["f", "t"],
        got["f", "f"],
        got["t", "t"],
        got["p", "p"],
        got["d", "d"],
        got["v", "v"],
        dt0,
        alpha0,
        flag == 1.0,
        number == climb,
        inside,
    )

    def shifted(value):
        lines = [value[(s + 1) % images : (s + 1) % images + 1, :] for s in range(images)]
        if rows > images:
            lines.append(jnp.zeros((rows - images, LANES), F32))
        return jnp.where(has_before, jnp.concatenate(lines, axis=0), 0.0)

    now = {"v": dt * keep, "f": dt * pull, "t": dt * side}
    old = {a.upper(): shifted(value) for a, value in now.items()}
    mine = now["v"] * now["v"] * got["v", "v"] + now["f"] * now["f"] * got["f", "f"]
    mine = mine + now["t"] * now["t"] * got["t", "t"]
    cross = now["v"] * now["f"] * got["v", "f"] + now["v"] * now["t"] * got["v", "t"]
    mine = mine + 2.0 * (cross + now["f"] * now["t"] * got["f", "t"])
    both = jnp.zeros((rows, LANES), F32)
    for a in "vft":
        both = both + now[a] * got["d", a]
    for b in "VFT":
        both = both - old[b] * got["d", b]
    for a in "vft":
        for b in "VFT":
            both = both - now[a] * old[b] * got[a, b]
    squared = got["d", "d"] + mine + shifted(mine) + 2.0 * both
    segment = jnp.sqrt(jnp.maximum(squared, 0.0) * (1.0 / (3.0 * atoms)))
    path = jnp.sum(jnp.where(offset <= here, segment, 0.0), axis=0, keepdims=True)
    path_ref[...] = path[:, 0:1]

    for c in range(3):
        speeds, places = [], []
        for i in range(SLAB_BLOCKS):
            row = 4 * c + i
            speed = keep[0:1] * own_ref[row : row + 1, :] + pull[0:1] * own_ref[12 + row : 13 + row, :]
            speed = speed + side[0:1] * state_ref[row : row + 1, :]
            speeds.append(speed)
            places.append(own_ref[24 + row : 25 + row, :] + dt[0:1] * speed)
        v_ref[c] = jnp.concatenate(speeds, axis=1)
        x_ref[c] = jnp.concatenate(places, axis=1)
    band_ref[0] = jnp.concatenate([record_ref[0:1, 0:1], record_ref[1:2, 0:1]], axis=1)
    band_ref[1] = jnp.concatenate([along[0:1, 0:1], spring[0:1, 0:1]], axis=1)


VMEM_SPEC = pl.BlockSpec(memory_space=pltpu.VMEM)
SMEM_SPEC = pl.BlockSpec(memory_space=pltpu.SMEM)
HBM_SPEC = pl.BlockSpec(memory_space=pltpu.HBM)


def call(body, outs, scalars, arrays, scratch_shapes=(), flops=0, spec=VMEM_SPEC, vmem=24):
    return pl.pallas_call(
        body,
        out_shape=outs,
        in_specs=[SMEM_SPEC] * len(scalars) + [spec] * len(arrays),
        out_specs=jax.tree.map(lambda _: VMEM_SPEC, outs),
        scratch_shapes=list(scratch_shapes),
        compiler_params=pltpu.CompilerParams(vmem_limit_bytes=vmem * 1024 * 1024),
        cost_estimate=pl.CostEstimate(flops=flops, bytes_accessed=1 << 18, transcendentals=0),
    )(*scalars, *arrays)


def around(array, axis):
    count = lax.axis_size(axis)
    return [lax.ppermute(array, axis, [(i, (i + s) % count) for i in range(count)]) for s in range(1, count)]


def ring(array, axis, by):
    count = lax.axis_size(axis)
    return lax.ppermute(array, axis, [(i, (i + by) % count) for i in range(count)])


def local(
    disp,
    veloc,
    time_step,
    reset_flags,
    climb,
    species,
    neighbours,
    counts,
    lattice,
    embed,
    radial_weight,
    mix_weight,
    update_weight,
    readout,
):
    atoms = disp.shape[2]
    images = lax.axis_size("img")
    domains = lax.axis_size("dom")
    assert disp.shape[0] == 1 and atoms == SLAB_BLOCKS * LANES and domains >= 3
    shape = jax.ShapeDtypeStruct
    x = jnp.transpose(disp, (1, 0, 2))
    v = jnp.transpose(veloc, (1, 0, 2))
    pack = call(
        pack_kernel,
        shape((PACK_ROWS, atoms), F32),
        (),
        (x, v, species, neighbours, counts, jnp.transpose(lattice, (1, 0, 2))),
        [pltpu.VMEM(a.shape, a.dtype) for a in (x, v, species, neighbours, counts)] + [pltpu.SemaphoreType.DMA((8,))],
        spec=HBM_SPEC,
        vmem=63,
    )
    left, right = ring(pack, "dom", 1), ring(pack, "dom", -1)
    before, after = ring(x, "img", 1), ring(x, "img", -1)
    weights = call(
        weight_kernel,
        (
            shape((CHANNELS, 48), BF16),
            shape((CHANNELS, 192), BF16),
            shape((CHANNELS, 32), BF16),
            shape((CHANNELS, 192), BF16),
            shape((16, 192), BF16),
            shape((4, CHANNELS, LANES), F32),
        ),
        (),
        (embed, radial_weight, mix_weight, update_weight, readout),
        flops=10000000,
    )
    force = call(
        first_kernel, shape((3, atoms), F32), (), (left, pack, right, *weights), scratch(), flops=1000000000
    )
    message = call(
        functools.partial(blend_kernel, images), shape((8, atoms), F32), (), (force, pack, before, after)
    )
    heard = around(message, "dom")
    state, record = call(
        functools.partial(second_kernel, images, len(heard)),
        (shape((40, LANES), F32), shape((2, LANES), F32)),
        (time_step, jnp.transpose(reset_flags), climb),
        (left, pack, right, message, *heard, *weights),
        scratch(),
        flops=1000000000,
    )
    band = around(state, "img")
    rows = 8 * ((images + 7) // 8)
    sums, extra = call(
        functools.partial(gram_kernel, images),
        (shape((domains, rows, LANES), F32), shape((16 + 3 * rows, LANES), F32)),
        (),
        (state, *band),
    )
    sums = lax.all_to_all(sums, "dom", 0, 0)
    new_x, new_v, records, path = call(
        functools.partial(final_kernel, images, atoms * domains),
        (shape(x.shape, F32), shape(x.shape, F32), shape((2, 1, 2), F32), shape((1, 1), F32)),
        (climb,),
        (state, record, extra, sums),
    )
    return (
        jnp.transpose(new_x, (1, 0, 2)),
        jnp.transpose(new_v, (1, 0, 2)),
        jnp.transpose(records, (0, 2, 1)),
        path.reshape(1),
    )


def solution(mesh):
    in_specs = (
        P(("group", "img"), None, "dom"),
        P(("group", "img"), None, "dom"),
        P(("group", "img")),
        P(None, ("group", "img")),
        P("group"),
        P(("group", "dom")),
        P(None, ("group", "dom")),
        P(("group", "dom")),
        P(None, None, ("group", "dom")),
        P(),
        P(),
        P(),
        P(),
        P(),
    )
    out_specs = (
        P(("group", "img"), None, "dom"),
        P(("group", "img"), None, "dom"),
        P(None, None, ("group", "img")),
        P(("group", "img")),
    )
    return jax.shard_map(local, mesh=mesh, in_specs=in_specs, out_specs=out_specs, check_vma=False)
```

```python
import functools
import math

import jax
import jax.numpy as jnp
from jax import lax
from jax.experimental import pallas as pl
from jax.experimental.pallas import tpu as pltpu
from jax.sharding import PartitionSpec as P

F32 = jnp.float32
BF16 = jnp.bfloat16
PRECISE = lax.Precision.HIGHEST
SPRING_CONSTANT = 0.5
ALPHA_START = 0.1
STEP_LIMIT = 0.3
TINY_VALUE = 1e-06
SOFTENING = 0.25
LANES = 128
SLOTS = 8
BASIS = 8
CHANNELS = 64
SLAB_BLOCKS = 4
ROW_X = 32
ROW_COUNT = 35
ROW_KIND = 36
ROW_V = 37
PACK_ROWS = 40
NT = (((1,), (1,)), ((), ()))


def split(x):
    high = x.astype(BF16).astype(F32)
    return high, x - high


def left_stack(w):
    high, low = split(w)
    return jnp.concatenate([high, high, low], axis=1)


def right_stack(x):
    high, low = split(x)
    high = high.astype(BF16)
    return jnp.concatenate([high, low.astype(BF16), high], axis=0)


def pair_stack(x):
    high, low = split(x)
    return jnp.concatenate([high.astype(BF16), low.astype(BF16)], axis=0)


def mm(a, b):
    return jnp.dot(a, b, preferred_element_type=F32)


def mm_nt(a, b):
    return lax.dot_general(a, b, NT, preferred_element_type=F32)


def pack_kernel(x_ref, v_ref, species_ref, nbr_ref, counts_ref, lattice_ref, out_ref, x, v, species, nbr, counts, sems):
    copies = [
        pltpu.make_async_copy(source, target, sems.at[i])
        for i, (source, target) in enumerate(
            [(x_ref, x), (v_ref, v), (species_ref, species), (nbr_ref, nbr), (counts_ref, counts)]
            + [(lattice_ref.at[c], out_ref.at[pl.ds(8 + 8 * c, 8)]) for c in range(3)]
        )
    ]
    for one in copies:
        one.start()
    for one in copies:
        one.wait()
    out_ref[0:8, :] = nbr[...].astype(F32)
    for c in range(3):
        out_ref[ROW_X + c : ROW_X + c + 1, :] = x[c]
        out_ref[ROW_V + c : ROW_V + c + 1, :] = v[c]
    out_ref[ROW_COUNT : ROW_COUNT + 1, :] = counts[...].astype(F32).reshape(1, -1)
    out_ref[ROW_KIND : ROW_KIND + 1, :] = species[...].astype(F32).reshape(1, -1)


def weight_kernel(
    embed_ref, radial_ref, mix_ref, update_ref, readout_ref, l1_ref, l2_ref, l3_ref, l5_ref, l6_ref, col_ref
):
    eye = (
        lax.broadcasted_iota(jnp.int32, (CHANNELS, CHANNELS), 0)
        == lax.broadcasted_iota(jnp.int32, (CHANNELS, CHANNELS), 1)
    ).astype(F32)

    def turned(x):
        return lax.dot_general(eye, x, NT, precision=PRECISE, preferred_element_type=F32)

    base0 = embed_ref[0:1, :]
    base1 = embed_ref[1:2, :] - base0
    rows = jnp.concatenate([base0, base1], axis=0)
    sent = jnp.dot(rows, mix_ref[0], precision=PRECISE, preferred_element_type=F32)
    scale = 1.0 / math.sqrt(SLOTS)
    first = jnp.concatenate([radial_ref[0] * sent[0:1], radial_ref[0] * sent[1:2]], axis=0) * scale
    second = radial_ref[1] * scale
    folded = jnp.dot(update_ref[0], mix_ref[1], precision=PRECISE, preferred_element_type=F32)
    mix_t = turned(mix_ref[1])
    l1_ref[...] = left_stack(turned(first)).astype(BF16)
    l2_ref[...] = left_stack(turned(folded)).astype(BF16)
    high, low = split(turned(second))
    l3_ref[...] = jnp.concatenate([high, high, low, jnp.zeros_like(high)], axis=1).astype(BF16)
    l5_ref[...] = left_stack(folded).astype(BF16)
    l6_ref[...] = left_stack(first).astype(BF16)
    readout = readout_ref[...].reshape(1, CHANNELS)
    wide = (CHANNELS, LANES)
    col_ref[0] = jnp.broadcast_to(jnp.sum(mix_t * base0, axis=1, keepdims=True), wide)
    col_ref[1] = jnp.broadcast_to(jnp.sum(mix_t * base1, axis=1, keepdims=True), wide)
    col_ref[2] = jnp.broadcast_to(jnp.sum(update_ref[0] * readout, axis=1, keepdims=True), wide)
    col_ref[3] = jnp.broadcast_to(jnp.sum(update_ref[1] * readout, axis=1, keepdims=True), wide)


def sin_cos(t):
    q = t * t
    s = -1.0 / 39916800.0
    for c in (1.0 / 362880.0, -1.0 / 5040.0, 1.0 / 120.0, -1.0 / 6.0, 1.0):
        s = s * q + c
    k = 1.0 / 479001600.0
    for c in (-1.0 / 3628800.0, 1.0 / 40320.0, -1.0 / 720.0, 1.0 / 24.0, -0.5, 1.0):
        k = k * q + c
    return s * t, k


def wide_row(x, row):
    return jnp.broadcast_to(x[row : row + 1, :], (8, x.shape[1]))


def silu_parts(m):
    sig = 1.0 / (1.0 + jnp.exp(-m))
    return m * sig, sig * (1.0 + m * (1.0 - sig))


def force_parts(packs, weights, scr):
    l1, l2, l3, l5, l6, col = weights
    (xs, widx, kinds, geo, bst, bps, bpr, sst, sent_all, slope, hot, dg, pulls, acc) = scr
    centre = 2.0 + 0.5 * lax.broadcasted_iota(jnp.int32, (BASIS, LANES), 0).astype(F32)
    slot = lax.broadcasted_iota(jnp.int32, (SLOTS, LANES), 0)
    row_id = lax.broadcasted_iota(jnp.int32, (3 * LANES, LANES), 0)

    def part_rows(value):
        high, low = split(value)
        return jnp.concatenate([high, low], axis=0).astype(BF16)

    def pairs(b):
        pack = packs[b // 4]
        lanes = slice((b % 4) * LANES, (b % 4 + 1) * LANES)
        index = pack[0:8, lanes].astype(jnp.int32) - LANES * (b % 4)
        widx[b] = index
        inner = index & (LANES - 1)
        part = index >> 7

        def taken(row):
            got = [
                jnp.take_along_axis(jnp.broadcast_to(xs[b - 1 + w, row : row + 1, :], (SLOTS, LANES)), inner, axis=1)
                for w in range(3)
            ]
            return jnp.where(part == 0, got[0], jnp.where(part == 1, got[1], got[2]))

        vec = [
            pack[8 + 8 * c : 16 + 8 * c, lanes] + taken(c) - jnp.broadcast_to(xs[b, c : c + 1, :], (SLOTS, LANES))
            for c in range(3)
        ]
        kind = taken(3)
        dist = jnp.sqrt(vec[0] * vec[0] + vec[1] * vec[1] + vec[2] * vec[2] + SOFTENING)
        live = (slot.astype(F32) < jnp.broadcast_to(pack[ROW_COUNT : ROW_COUNT + 1, lanes], (SLOTS, LANES))).astype(F32)
        turns = dist * (1.0 / 12.0)
        turns = turns - jnp.floor(turns + 0.5)
        sine, cosine = sin_cos(turns * math.pi)
        envelope = cosine * cosine * live
        slant = cosine * sine * live * (-math.pi / 6.0)
        if 3 <= b <= 8:
            kinds[b] = kind
            for c in range(3):
                geo[b, c] = vec[c]
            geo[b, 3] = 1.0 / dist
        total = jnp.zeros((BASIS, LANES), F32)
        total_kind = jnp.zeros((BASIS, LANES), F32)
        for k in range(SLOTS):
            away = wide_row(dist, k) - centre
            gauss = jnp.exp(-4.0 * (away * away))
            env_k = wide_row(envelope, k)
            value = gauss * env_k
            total = total + value
            total_kind = total_kind + value * wide_row(kind, k)
            cols = slice(k * LANES, (k + 1) * LANES)
            if 2 <= b <= 9:
                bst[b, :, cols] = part_rows(value)
            if 3 <= b <= 8:
                value = gauss * (wide_row(slant, k) - 8.0 * away * env_k)
                bpr[b, :, cols] = value
                bps[b, :, cols] = part_rows(value)
        high, low = split(jnp.concatenate([total, total_kind], axis=0))
        sst[:, b * LANES : (b + 1) * LANES] = jnp.concatenate([high, low, high], axis=0).astype(BF16)

    for b in range(1, 11):
        pairs(b)

    for b in range(1, 11, 2):
        cols = slice(b * LANES, (b + 2) * LANES)
        value, steep = silu_parts(mm(l1[...], sst[:, cols]))
        sent = mm(l2[...], right_stack(value))
        for i in range(2):
            one = sent[:, i * LANES : (i + 1) * LANES]
            one = one + col[0] + col[1] * jnp.broadcast_to(xs[b + i, 3:4, :], (CHANNELS, LANES))
            sent_all[:, (b + i) * LANES : (b + i + 1) * LANES] = one
        slope[:, cols] = steep

    def mark(b):
        index = widx[b]
        for k in range(SLOTS):
            same = row_id == jnp.broadcast_to(index[k : k + 1, :], (3 * LANES, LANES))
            hot[b, :, k * LANES : (k + 1) * LANES] = jnp.where(same, 1.0, 0.0).astype(BF16)

    def reach(b, first, last):
        return [w for w in range(3) if first <= b - 1 + w <= last]

    def spread(left, b, first, last):
        ws = reach(b, first, last)
        return ws, mm_nt(left, hot[b, ws[0] * LANES : (ws[-1] + 1) * LANES, :])

    started = set()

    def gather_and_return(b):
        index = widx[b]
        inner, part = index & (LANES - 1), index >> 7
        windows = [sent_all[:, (b - 1 + w) * LANES : (b + w) * LANES] for w in range(3)]
        got = []
        for k in range(SLOTS):
            lane = jnp.broadcast_to(inner[k : k + 1, :], (CHANNELS, LANES))
            which = jnp.broadcast_to(part[k : k + 1, :], (CHANNELS, LANES))
            pick = [jnp.take_along_axis(window, lane, axis=1) for window in windows]
            got.append(jnp.where(which == 0, pick[0], jnp.where(which == 1, pick[1], pick[2])))
        got = jnp.concatenate(got, axis=1)
        mark(b)
        basis = bst[b]
        radial = mm(l3[...], jnp.concatenate([basis, basis], axis=0))
        message = jnp.zeros((CHANNELS, LANES), F32)
        for k in range(SLOTS):
            cols = slice(k * LANES, (k + 1) * LANES)
            message = message + radial[:, cols] * got[:, cols]
        _, steep = silu_parts(message)
        back = jnp.concatenate([col[3] * steep] * SLOTS, axis=1)
        ws, out = spread(pair_stack(radial * back), b, 3, 8)
        out = out[:CHANNELS] + out[CHANNELS:]
        for i, w in enumerate(ws):
            target = b - 1 + w
            piece = out[:, i * LANES : (i + 1) * LANES]
            where = slice(target * LANES, (target + 1) * LANES)
            if target in started:
                dg[:, where] += piece
            else:
                dg[:, where] = piece
                started.add(target)
        if 3 <= b <= 8:
            basis = bps[b]
            steepness = mm(l3[...], jnp.concatenate([basis, basis], axis=0))
            pull = got * back * steepness
            total = pull[0:8]
            for i in range(1, CHANNELS // 8):
                total = total + pull[8 * i : 8 * i + 8]
            pulls[b] = total

    for b in range(2, 10):
        gather_and_return(b)

    begun = set()

    def put(b, c, value):
        if (b, c) in begun:
            acc[b, c] += value
        else:
            acc[b, c] = value
            begun.add((b, c))

    def finish(b, sums):
        kind = kinds[b]
        rows = []
        for k in range(SLOTS):
            cols = slice(k * LANES, (k + 1) * LANES)
            weight = sums[0:8] + wide_row(kind, k) * sums[8:16]
            rows.append(jnp.sum(bpr[b, :, cols] * weight + pulls[b, :, cols], axis=0, keepdims=True))
        pull = jnp.concatenate(rows, axis=0) * geo[b, 3]
        pieces = []
        for c in range(3):
            value = pull * geo[b, c]
            if 4 <= b <= 7:
                put(b, c, -value)
            pieces.append(split(value))
        lines = []
        for h in range(2):
            for c in range(3):
                lines.append(jnp.concatenate([jnp.where(slot == k, pieces[c][h], 0.0) for k in range(SLOTS)], axis=1))
        ws, out = spread(jnp.concatenate(lines, axis=0).astype(BF16), b, 4, 7)
        for c in range(3):
            both = out[8 * c : 8 * c + 8] + out[24 + 8 * c : 32 + 8 * c]
            for i, w in enumerate(ws):
                put(b - 1 + w, c, both[:, i * LANES : (i + 1) * LANES])

    for b in range(3, 9, 2):
        cols = slice(b * LANES, (b + 2) * LANES)
        steep = mm(l5[...], right_stack(dg[:, cols]))
        steep = steep + jnp.concatenate([col[2], col[2]], axis=1)
        sums = mm(l6[...], right_stack(steep * slope[:, cols]))
        for i in range(2):
            finish(b + i, sums[:, i * LANES : (i + 1) * LANES])


def own_force(acc, c):
    return jnp.concatenate(
        [-jnp.sum(acc[4 + i, c], axis=0, keepdims=True) for i in range(SLAB_BLOCKS)], axis=1
    )


def fill_region(xs, packs, rows_of):
    for b in range(12):
        lanes = slice((b % 4) * LANES, (b % 4 + 1) * LANES)
        pack = packs[b // 4]
        xs[b, 0:3, :] = rows_of(b // 4)[:, lanes]
        xs[b, 3:4, :] = pack[ROW_KIND : ROW_KIND + 1, lanes]


def lane_total(x):
    x = x[:, 0:LANES] + x[:, LANES : 2 * LANES] + x[:, 2 * LANES : 3 * LANES] + x[:, 3 * LANES : 4 * LANES]
    return jnp.sum(x, axis=1, keepdims=True)


def dot3(a, b):
    return jnp.sum(a * b, axis=0, keepdims=True)


def scratch():
    wide = 12 * LANES
    return [
        pltpu.VMEM((12, 8, LANES), F32),
        pltpu.VMEM((12, 8, LANES), jnp.int32),
        pltpu.VMEM((12, 8, LANES), F32),
        pltpu.VMEM((12, 4, 8, LANES), F32),
        pltpu.VMEM((12, 16, SLOTS * LANES), BF16),
        pltpu.VMEM((12, 16, SLOTS * LANES), BF16),
        pltpu.VMEM((12, 8, SLOTS * LANES), F32),
        pltpu.VMEM((48, wide), BF16),
        pltpu.VMEM((CHANNELS, wide), F32),
        pltpu.VMEM((CHANNELS, wide), F32),
        pltpu.VMEM((12, 3 * LANES, SLOTS * LANES), BF16),
        pltpu.VMEM((CHANNELS, wide), F32),
        pltpu.VMEM((12, 8, SLOTS * LANES), F32),
        pltpu.VMEM((12, 3, 8, LANES), F32),
    ]


def first_kernel(pl_ref, po_ref, pr_ref, *rest):
    weights, out_ref, scr = rest[:6], rest[6], rest[7:]
    packs = [pl_ref, po_ref, pr_ref]
    fill_region(scr[0], packs, lambda s: packs[s][ROW_X : ROW_X + 3, :])
    force_parts(packs, weights, scr)
    for c in range(3):
        out_ref[c : c + 1, :] = own_force(scr[-1], c)


def rows_of(ref):
    return jnp.concatenate([ref[c] for c in range(3)], axis=0)


def block_row(*values):
    values = list(values) + [jnp.zeros((1, LANES), F32)] * (SLAB_BLOCKS - len(values))
    return jnp.concatenate(values, axis=1)


def blend_kernel(force_ref, po_ref, before_ref, after_ref, out_ref):
    x = po_ref[ROW_X : ROW_X + 3, :]
    v = po_ref[ROW_V : ROW_V + 3, :]
    force = force_ref[...]
    before = rows_of(before_ref)
    after = rows_of(after_ref)
    tangent = after - before
    plus = after - x
    minus = x - before
    sums = jnp.concatenate(
        [
            dot3(force, tangent),
            dot3(force, force),
            dot3(tangent, tangent),
            dot3(plus, plus),
            dot3(minus, minus),
            dot3(v, v),
            jnp.zeros((2, x.shape[1]), F32),
        ],
        axis=0,
    )
    sums = jnp.broadcast_to(lane_total(sums), (8, LANES))
    out_ref[0:3, :] = force
    out_ref[3:6, :] = tangent
    out_ref[6:7, :] = block_row(*[sums[i : i + 1] for i in range(4)])
    out_ref[7:8, :] = block_row(sums[4:5], sums[5:6])


def step_numbers(ft, ff, tt, pp, mn, vv, dt, alpha, flagged, climbing, inside):
    root = jnp.sqrt(tt + TINY_VALUE)
    along = ft / root
    spring = SPRING_CONSTANT * (jnp.sqrt(pp) - jnp.sqrt(mn))
    factor = jnp.where(climbing, -2.0 * along, spring - along)
    band = jnp.maximum(ff + 2.0 * factor * along + factor * factor * (tt / (tt + TINY_VALUE)), 0.0)
    new_dt = jnp.where(flagged, 0.5 * dt, jnp.minimum(1.1 * dt, STEP_LIMIT))
    pull = jnp.where(flagged, 0.0, alpha * jnp.sqrt(vv / (band + TINY_VALUE))) + new_dt
    keep = jnp.where(flagged, 0.0, 1.0 - alpha)
    new_alpha = jnp.where(flagged, ALPHA_START, 0.99 * alpha)
    keep = jnp.where(inside, keep, 0.0)
    pull = jnp.where(inside, pull, 0.0)
    return (
        jnp.where(inside, along, 0.0),
        jnp.where(inside, spring, 0.0),
        keep,
        pull,
        pull * factor / root,
        new_dt,
        new_alpha,
    )


def second_kernel(images, others, dt_ref, flag_ref, climb_ref, pl_ref, po_ref, pr_ref, own_ref, *rest):
    heard, rest = rest[:others], rest[others:]
    weights, out_ref, record_ref, scr = rest[:6], rest[6], rest[7], rest[8:]
    packs = [pl_ref, po_ref, pr_ref]
    here = lax.axis_index("img")
    sums = own_ref[6:8, :]
    for one in heard:
        sums = sums + one[6:8, :]
    ft, ff, tt, pp = (sums[0:1, i * LANES : (i + 1) * LANES] for i in range(4))
    mn, vv = (sums[1:2, i * LANES : (i + 1) * LANES] for i in range(2))
    shape = (1, LANES)
    along, spring, keep, pull, side, dt, alpha = step_numbers(
        ft,
        ff,
        tt,
        pp,
        mn,
        vv,
        jnp.full(shape, dt_ref[0], F32),
        jnp.full(shape, ALPHA_START, F32),
        jnp.full(shape, flag_ref[0, 0], jnp.int32) == 1,
        jnp.full(shape, here - climb_ref[0], jnp.int32) == 0,
        jnp.full(shape, jnp.where((here >= 1) & (here <= images - 2), 1, 0), jnp.int32) == 1,
    )
    messages = [heard[0], own_ref, heard[others - 1]]

    def wide(s):
        return jnp.concatenate([s] * SLAB_BLOCKS, axis=1)

    speeds = [
        wide(keep) * p[ROW_V : ROW_V + 3, :] + wide(pull) * m[0:3, :] + wide(side) * m[3:6, :]
        for p, m in zip(packs, messages)
    ]
    moved = [p[ROW_X : ROW_X + 3, :] + wide(dt) * s for p, s in zip(packs, speeds)]
    fill_region(scr[0], packs, lambda s: moved[s])
    force_parts(packs, weights, scr)
    for c in range(3):
        force = own_force(scr[-1], c)
        for i in range(SLAB_BLOCKS):
            lanes = slice(i * LANES, (i + 1) * LANES)
            row = 4 * c + i
            out_ref[row : row + 1, :] = speeds[1][c : c + 1, lanes]
            out_ref[12 + row : 13 + row, :] = force[:, lanes]
            out_ref[24 + row : 25 + row, :] = moved[1][c : c + 1, lanes]
    out_ref[36:37, :] = dt
    out_ref[37:38, :] = alpha
    out_ref[38:40, :] = jnp.full((2, LANES), flag_ref[0, 1], jnp.int32).astype(F32)
    record_ref[0:1, :] = along
    record_ref[1:2, :] = spring


PRODUCTS = (
    [("f", "t"), ("f", "f"), ("t", "t"), ("p", "p"), ("d", "d"), ("v", "v")]
    + [("d", "v"), ("d", "f"), ("d", "t"), ("d", "V"), ("d", "F"), ("d", "T"), ("v", "f"), ("v", "t")]
    + [(a, b) for a in "vft" for b in "VFT"]
)


def gram_kernel(images, *refs):
    messages, out_ref, state_ref = refs[:images], refs[images], refs[images + 1]
    rows = out_ref.shape[0]
    here = lax.axis_index("img")
    blank = [jnp.zeros((rows - images, LANES), F32)] if rows > images else []

    def gathered(row):
        return jnp.concatenate([m[row : row + 1, :] for m in messages] + blank, axis=0)

    def shifted(value, by):
        lines = [value[(s + by) % images : (s + by) % images + 1, :] for s in range(images)]
        return jnp.concatenate(lines + blank, axis=0)

    offset = lax.broadcasted_iota(jnp.int32, (rows, LANES), 0)
    number = here - offset
    number = jnp.where(number < 0, number + images, number)
    has_after = (number < images - 1) & (offset < images)
    has_before = (number > 0) & (offset < images)
    totals = [jnp.zeros((rows, LANES), F32) for _ in PRODUCTS]
    for row in range(3 * SLAB_BLOCKS):
        v, f, x = gathered(row), gathered(12 + row), gathered(24 + row)
        after = jnp.where(has_after, shifted(x, -1), 0.0)
        before = jnp.where(has_before, shifted(x, 1), 0.0)
        t = after - before
        table = {"f": f, "v": v, "t": t, "p": after - x, "d": x - before}
        table["F"] = jnp.where(has_before, shifted(f, 1), 0.0)
        table["V"] = jnp.where(has_before, shifted(v, 1), 0.0)
        table["T"] = jnp.where(has_before, shifted(t, 1), 0.0)
        totals = [old + table[a] * table[b] for old, (a, b) in zip(totals, PRODUCTS)]
        state_ref[row : row + 1, :] = t[0:1]
    lane = lax.broadcasted_iota(jnp.int32, (rows, LANES), 1)
    result = jnp.zeros((rows, LANES), F32)
    for q, one in enumerate(totals):
        one = jnp.broadcast_to(jnp.sum(one, axis=1, keepdims=True), (rows, LANES))
        result = jnp.where(lane == q, one, result)
    out_ref[...] = result
    for i in range(3):
        state_ref[16 + rows * i : 16 + rows * (i + 1), :] = gathered(36 + i)


def final_kernel(images, others, atoms, climb_ref, own_ref, record_ref, state_ref, sums_ref, *rest):
    heard, (x_ref, v_ref, band_ref, path_ref) = rest[:others], rest[others:]
    rows = sums_ref.shape[0]
    here = lax.axis_index("img")
    sums = sums_ref[...]
    for one in heard:
        sums = sums + one[...]
    got = {
        pair: jnp.broadcast_to(sums[:, q : q + 1], (rows, LANES)) for q, pair in enumerate(PRODUCTS)
    }
    offset = lax.broadcasted_iota(jnp.int32, (rows, LANES), 0)
    number = here - offset
    number = jnp.where(number < 0, number + images, number)
    inside = (number >= 1) & (number <= images - 2) & (offset < images)
    has_before = (number > 0) & (offset < images)
    climb = jnp.full((rows, LANES), climb_ref[0], jnp.int32)
    dt0, alpha0, flag = (state_ref[16 + rows * i : 16 + rows * (i + 1), :] for i in range(3))
    along, spring, keep, pull, side, dt, _ = step_numbers(
        got["f", "t"],
        got["f", "f"],
        got["t", "t"],
        got["p", "p"],
        got["d", "d"],
        got["v", "v"],
        dt0,
        alpha0,
        flag == 1.0,
        number == climb,
        inside,
    )

    def shifted(value):
        lines = [value[(s + 1) % images : (s + 1) % images + 1, :] for s in range(images)]
        if rows > images:
            lines.append(jnp.zeros((rows - images, LANES), F32))
        return jnp.where(has_before, jnp.concatenate(lines, axis=0), 0.0)

    now = {"v": dt * keep, "f": dt * pull, "t": dt * side}
    old = {a.upper(): shifted(value) for a, value in now.items()}
    mine = now["v"] * now["v"] * got["v", "v"] + now["f"] * now["f"] * got["f", "f"]
    mine = mine + now["t"] * now["t"] * got["t", "t"]
    cross = now["v"] * now["f"] * got["v", "f"] + now["v"] * now["t"] * got["v", "t"]
    mine = mine + 2.0 * (cross + now["f"] * now["t"] * got["f", "t"])
    both = jnp.zeros((rows, LANES), F32)
    for a in "vft":
        both = both + now[a] * got["d", a]
    for b in "VFT":
        both = both - old[b] * got["d", b]
    for a in "vft":
        for b in "VFT":
            both = both - now[a] * old[b] * got[a, b]
    squared = got["d", "d"] + mine + shifted(mine) + 2.0 * both
    segment = jnp.sqrt(jnp.maximum(squared, 0.0) * (1.0 / (3.0 * atoms)))
    path = jnp.sum(jnp.where(offset <= here, segment, 0.0), axis=0, keepdims=True)
    path_ref[...] = path[:, 0:1]

    for c in range(3):
        speeds, places = [], []
        for i in range(SLAB_BLOCKS):
            row = 4 * c + i
            speed = keep[0:1] * own_ref[row : row + 1, :] + pull[0:1] * own_ref[12 + row : 13 + row, :]
            speed = speed + side[0:1] * state_ref[row : row + 1, :]
            speeds.append(speed)
            places.append(own_ref[24 + row : 25 + row, :] + dt[0:1] * speed)
        v_ref[c] = jnp.concatenate(speeds, axis=1)
        x_ref[c] = jnp.concatenate(places, axis=1)
    band_ref[0] = jnp.concatenate([record_ref[0:1, 0:1], record_ref[1:2, 0:1]], axis=1)
    band_ref[1] = jnp.concatenate([along[0:1, 0:1], spring[0:1, 0:1]], axis=1)


VMEM_SPEC = pl.BlockSpec(memory_space=pltpu.VMEM)
SMEM_SPEC = pl.BlockSpec(memory_space=pltpu.SMEM)
HBM_SPEC = pl.BlockSpec(memory_space=pltpu.HBM)


def call(body, outs, scalars, arrays, scratch_shapes=(), flops=0, spec=VMEM_SPEC, vmem=24):
    return pl.pallas_call(
        body,
        out_shape=outs,
        in_specs=[SMEM_SPEC] * len(scalars) + [spec] * len(arrays),
        out_specs=jax.tree.map(lambda _: VMEM_SPEC, outs),
        scratch_shapes=list(scratch_shapes),
        compiler_params=pltpu.CompilerParams(vmem_limit_bytes=vmem * 1024 * 1024),
        cost_estimate=pl.CostEstimate(flops=flops, bytes_accessed=1 << 18, transcendentals=0),
    )(*scalars, *arrays)


def around(array, axis):
    count = lax.axis_size(axis)
    return [lax.ppermute(array, axis, [(i, (i + s) % count) for i in range(count)]) for s in range(1, count)]


def ring(array, axis, by):
    count = lax.axis_size(axis)
    return lax.ppermute(array, axis, [(i, (i + by) % count) for i in range(count)])


def beside(array, axis, by):
    count = lax.axis_size(axis)
    return lax.ppermute(array, axis, [(i, i + by) for i in range(count) if 0 <= i + by < count])


def local(
    disp,
    veloc,
    time_step,
    reset_flags,
    climb,
    species,
    neighbours,
    counts,
    lattice,
    embed,
    radial_weight,
    mix_weight,
    update_weight,
    readout,
):
    atoms = disp.shape[2]
    images = lax.axis_size("img")
    domains = lax.axis_size("dom")
    assert disp.shape[0] == 1 and atoms == SLAB_BLOCKS * LANES and domains >= 3
    shape = jax.ShapeDtypeStruct
    x = jnp.transpose(disp, (1, 0, 2))
    v = jnp.transpose(veloc, (1, 0, 2))
    pack = call(
        pack_kernel,
        shape((PACK_ROWS, atoms), F32),
        (),
        (x, v, species, neighbours, counts, jnp.transpose(lattice, (1, 0, 2))),
        [pltpu.VMEM(a.shape, a.dtype) for a in (x, v, species, neighbours, counts)] + [pltpu.SemaphoreType.DMA((8,))],
        spec=HBM_SPEC,
        vmem=63,
    )
    left, right = ring(pack, "dom", 1), ring(pack, "dom", -1)
    before, after = beside(x, "img", 1), beside(x, "img", -1)
    weights = call(
        weight_kernel,
        (
            shape((CHANNELS, 48), BF16),
            shape((CHANNELS, 192), BF16),
            shape((CHANNELS, 32), BF16),
            shape((CHANNELS, 192), BF16),
            shape((16, 192), BF16),
            shape((4, CHANNELS, LANES), F32),
        ),
        (),
        (embed, radial_weight, mix_weight, update_weight, readout),
        flops=10000000,
    )
    force = call(
        first_kernel, shape((3, atoms), F32), (), (left, pack, right, *weights), scratch(), flops=1000000000
    )
    message = call(
        blend_kernel, shape((8, atoms), F32), (), (force, pack, before, after)
    )
    heard = around(message, "dom")
    state, record = call(
        functools.partial(second_kernel, images, len(heard)),
        (shape((40, LANES), F32), shape((2, LANES), F32)),
        (time_step, jnp.transpose(reset_flags), climb),
        (left, pack, right, message, *heard, *weights),
        scratch(),
        flops=1000000000,
    )
    band = around(state, "img")
    rows = 8 * ((images + 7) // 8)
    sums, extra = call(
        functools.partial(gram_kernel, images),
        (shape((rows, LANES), F32), shape((16 + 3 * rows, LANES), F32)),
        (),
        (state, *band),
    )
    others = around(sums, "dom")
    new_x, new_v, records, path = call(
        functools.partial(final_kernel, images, len(others), atoms * domains),
        (shape(x.shape, F32), shape(x.shape, F32), shape((2, 1, 2), F32), shape((1, 1), F32)),
        (climb,),
        (state, record, extra, sums, *others),
    )
    return (
        jnp.transpose(new_x, (1, 0, 2)),
        jnp.transpose(new_v, (1, 0, 2)),
        jnp.transpose(records, (0, 2, 1)),
        path.reshape(1),
    )


def solution(mesh):
    in_specs = (
        P(("group", "img"), None, "dom"),
        P(("group", "img"), None, "dom"),
        P(("group", "img")),
        P(None, ("group", "img")),
        P("group"),
        P(("group", "dom")),
        P(None, ("group", "dom")),
        P(("group", "dom")),
        P(None, None, ("group", "dom")),
        P(),
        P(),
        P(),
        P(),
        P(),
    )
    out_specs = (
        P(("group", "img"), None, "dom"),
        P(("group", "img"), None, "dom"),
        P(None, None, ("group", "img")),
        P(("group", "img")),
    )
    return jax.shard_map(local, mesh=mesh, in_specs=in_specs, out_specs=out_specs, check_vma=False)
```

```python
import functools
import math

import jax
import jax.numpy as jnp
from jax import lax
from jax.experimental import pallas as pl
from jax.experimental.pallas import tpu as pltpu
from jax.sharding import PartitionSpec as P

F32 = jnp.float32
BF16 = jnp.bfloat16
PRECISE = lax.Precision.HIGHEST
SPRING_CONSTANT = 0.5
ALPHA_START = 0.1
STEP_LIMIT = 0.3
TINY_VALUE = 1e-06
SOFTENING = 0.25
LANES = 128
SLOTS = 8
BASIS = 8
CHANNELS = 64
SLAB_BLOCKS = 4
ROW_X = 32
ROW_COUNT = 35
ROW_KIND = 36
ROW_V = 37
PACK_ROWS = 40
NT = (((1,), (1,)), ((), ()))


def split(x):
    high = x.astype(BF16).astype(F32)
    return high, x - high


def left_stack(w):
    high, low = split(w)
    return jnp.concatenate([high, high, low], axis=1)


def right_stack(x):
    high, low = split(x)
    high = high.astype(BF16)
    return jnp.concatenate([high, low.astype(BF16), high], axis=0)


def pair_stack(x):
    high, low = split(x)
    return jnp.concatenate([high.astype(BF16), low.astype(BF16)], axis=0)


def mm(a, b):
    return jnp.dot(a, b, preferred_element_type=F32)


def mm_nt(a, b):
    return lax.dot_general(a, b, NT, preferred_element_type=F32)


def pack_kernel(x_ref, v_ref, species_ref, nbr_ref, counts_ref, lattice_ref, out_ref, x, v, species, nbr, counts, sems):
    copies = [
        pltpu.make_async_copy(source, target, sems.at[i])
        for i, (source, target) in enumerate(
            [(x_ref, x), (v_ref, v), (species_ref, species), (nbr_ref, nbr), (counts_ref, counts)]
            + [(lattice_ref.at[c], out_ref.at[pl.ds(8 + 8 * c, 8)]) for c in range(3)]
        )
    ]
    for one in copies:
        one.start()
    for one in copies:
        one.wait()
    out_ref[0:8, :] = nbr[...].astype(F32)
    for c in range(3):
        out_ref[ROW_X + c : ROW_X + c + 1, :] = x[c]
        out_ref[ROW_V + c : ROW_V + c + 1, :] = v[c]
    out_ref[ROW_COUNT : ROW_COUNT + 1, :] = counts[...].astype(F32).reshape(1, -1)
    out_ref[ROW_KIND : ROW_KIND + 1, :] = species[...].astype(F32).reshape(1, -1)


def weight_kernel(
    dt_ref, flag_ref, climb_ref, x_ref, embed_ref, radial_ref, mix_ref, update_ref, readout_ref, l1_ref, l2_ref, l3_ref, l5_ref, l6_ref, col_ref, copy_ref, number_ref
):
    copy_ref[...] = x_ref[...]
    flags = [flag_ref[0, s].astype(F32) for s in range(flag_ref.shape[1])]
    for i, value in enumerate([dt_ref[0], climb_ref[0].astype(F32)] + flags):
        number_ref[i : i + 1, :] = jnp.full((1, LANES), value, F32)
    eye = (
        lax.broadcasted_iota(jnp.int32, (CHANNELS, CHANNELS), 0)
        == lax.broadcasted_iota(jnp.int32, (CHANNELS, CHANNELS), 1)
    ).astype(F32)

    def turned(x):
        return lax.dot_general(eye, x, NT, precision=PRECISE, preferred_element_type=F32)

    base0 = embed_ref[0:1, :]
    base1 = embed_ref[1:2, :] - base0
    rows = jnp.concatenate([base0, base1], axis=0)
    sent = jnp.dot(rows, mix_ref[0], precision=PRECISE, preferred_element_type=F32)
    scale = 1.0 / math.sqrt(SLOTS)
    first = jnp.concatenate([radial_ref[0] * sent[0:1], radial_ref[0] * sent[1:2]], axis=0) * scale
    second = radial_ref[1] * scale
    folded = jnp.dot(update_ref[0], mix_ref[1], precision=PRECISE, preferred_element_type=F32)
    mix_t = turned(mix_ref[1])
    l1_ref[...] = left_stack(turned(first)).astype(BF16)
    l2_ref[...] = left_stack(turned(folded)).astype(BF16)
    high, low = split(turned(second))
    l3_ref[...] = jnp.concatenate([high, high, low, jnp.zeros_like(high)], axis=1).astype(BF16)
    l5_ref[...] = left_stack(folded).astype(BF16)
    l6_ref[...] = left_stack(first).astype(BF16)
    readout = readout_ref[...].reshape(1, CHANNELS)
    wide = (CHANNELS, LANES)
    col_ref[0] = jnp.broadcast_to(jnp.sum(mix_t * base0, axis=1, keepdims=True), wide)
    col_ref[1] = jnp.broadcast_to(jnp.sum(mix_t * base1, axis=1, keepdims=True), wide)
    col_ref[2] = jnp.broadcast_to(jnp.sum(update_ref[0] * readout, axis=1, keepdims=True), wide)
    col_ref[3] = jnp.broadcast_to(jnp.sum(update_ref[1] * readout, axis=1, keepdims=True), wide)


def sin_cos(t):
    q = t * t
    s = -1.0 / 39916800.0
    for c in (1.0 / 362880.0, -1.0 / 5040.0, 1.0 / 120.0, -1.0 / 6.0, 1.0):
        s = s * q + c
    k = 1.0 / 479001600.0
    for c in (-1.0 / 3628800.0, 1.0 / 40320.0, -1.0 / 720.0, 1.0 / 24.0, -0.5, 1.0):
        k = k * q + c
    return s * t, k


def wide_row(x, row):
    return jnp.broadcast_to(x[row : row + 1, :], (8, x.shape[1]))


def silu_parts(m):
    sig = 1.0 / (1.0 + jnp.exp(-m))
    return m * sig, sig * (1.0 + m * (1.0 - sig))


def force_parts(packs, weights, scr):
    l1, l2, l3, l5, l6, col = weights
    (xs, widx, kinds, geo, bst, bps, bpr, sst, sent_all, slope, hot, dg, pulls, acc) = scr
    centre = 2.0 + 0.5 * lax.broadcasted_iota(jnp.int32, (BASIS, LANES), 0).astype(F32)
    slot = lax.broadcasted_iota(jnp.int32, (SLOTS, LANES), 0)
    row_id = lax.broadcasted_iota(jnp.int32, (3 * LANES, LANES), 0)

    def part_rows(value):
        high, low = split(value)
        return jnp.concatenate([high, low], axis=0).astype(BF16)

    def pairs(b):
        pack = packs[b // 4]
        lanes = slice((b % 4) * LANES, (b % 4 + 1) * LANES)
        index = pack[0:8, lanes].astype(jnp.int32) - LANES * (b % 4)
        widx[b] = index
        inner = index & (LANES - 1)
        part = index >> 7

        def taken(row):
            got = [
                jnp.take_along_axis(jnp.broadcast_to(xs[b - 1 + w, row : row + 1, :], (SLOTS, LANES)), inner, axis=1)
                for w in range(3)
            ]
            return jnp.where(part == 0, got[0], jnp.where(part == 1, got[1], got[2]))

        vec = [
            pack[8 + 8 * c : 16 + 8 * c, lanes] + taken(c) - jnp.broadcast_to(xs[b, c : c + 1, :], (SLOTS, LANES))
            for c in range(3)
        ]
        kind = taken(3)
        dist = jnp.sqrt(vec[0] * vec[0] + vec[1] * vec[1] + vec[2] * vec[2] + SOFTENING)
        live = (slot.astype(F32) < jnp.broadcast_to(pack[ROW_COUNT : ROW_COUNT + 1, lanes], (SLOTS, LANES))).astype(F32)
        turns = dist * (1.0 / 12.0)
        turns = turns - jnp.floor(turns + 0.5)
        sine, cosine = sin_cos(turns * math.pi)
        envelope = cosine * cosine * live
        slant = cosine * sine * live * (-math.pi / 6.0)
        if 3 <= b <= 8:
            kinds[b] = kind
            for c in range(3):
                geo[b, c] = vec[c]
            geo[b, 3] = 1.0 / dist
        total = jnp.zeros((BASIS, LANES), F32)
        total_kind = jnp.zeros((BASIS, LANES), F32)
        for k in range(SLOTS):
            away = wide_row(dist, k) - centre
            gauss = jnp.exp(-4.0 * (away * away))
            env_k = wide_row(envelope, k)
            value = gauss * env_k
            total = total + value
            total_kind = total_kind + value * wide_row(kind, k)
            cols = slice(k * LANES, (k + 1) * LANES)
            if 2 <= b <= 9:
                bst[b, :, cols] = part_rows(value)
            if 3 <= b <= 8:
                value = gauss * (wide_row(slant, k) - 8.0 * away * env_k)
                bpr[b, :, cols] = value
                bps[b, :, cols] = part_rows(value)
        high, low = split(jnp.concatenate([total, total_kind], axis=0))
        sst[:, b * LANES : (b + 1) * LANES] = jnp.concatenate([high, low, high], axis=0).astype(BF16)

    for b in range(1, 11):
        pairs(b)

    for b in range(1, 11, 2):
        cols = slice(b * LANES, (b + 2) * LANES)
        value, steep = silu_parts(mm(l1[...], sst[:, cols]))
        sent = mm(l2[...], right_stack(value))
        for i in range(2):
            one = sent[:, i * LANES : (i + 1) * LANES]
            one = one + col[0] + col[1] * jnp.broadcast_to(xs[b + i, 3:4, :], (CHANNELS, LANES))
            sent_all[:, (b + i) * LANES : (b + i + 1) * LANES] = one
        slope[:, cols] = steep

    def reach(b, first, last):
        return [w for w in range(3) if first <= b - 1 + w <= last]

    def mark(b):
        index = widx[b]
        ws = reach(b, 3, 8)
        rows = slice(ws[0] * LANES, (ws[-1] + 1) * LANES)
        for k in range(SLOTS):
            same = row_id[rows] == jnp.broadcast_to(index[k : k + 1, :], (rows.stop - rows.start, LANES))
            hot[b, rows, k * LANES : (k + 1) * LANES] = jnp.where(same, 1.0, 0.0).astype(BF16)

    def spread(left, b, first, last):
        ws = reach(b, first, last)
        return ws, mm_nt(left, hot[b, ws[0] * LANES : (ws[-1] + 1) * LANES, :])

    started = set()

    def gather_and_return(b):
        index = widx[b]
        inner, part = index & (LANES - 1), index >> 7
        windows = [sent_all[:, (b - 1 + w) * LANES : (b + w) * LANES] for w in range(3)]
        got = []
        for k in range(SLOTS):
            lane = jnp.broadcast_to(inner[k : k + 1, :], (CHANNELS, LANES))
            which = jnp.broadcast_to(part[k : k + 1, :], (CHANNELS, LANES))
            pick = [jnp.take_along_axis(window, lane, axis=1) for window in windows]
            got.append(jnp.where(which == 0, pick[0], jnp.where(which == 1, pick[1], pick[2])))
        got = jnp.concatenate(got, axis=1)
        mark(b)
        basis = bst[b]
        radial = mm(l3[...], jnp.concatenate([basis, basis], axis=0))
        message = jnp.zeros((CHANNELS, LANES), F32)
        for k in range(SLOTS):
            cols = slice(k * LANES, (k + 1) * LANES)
            message = message + radial[:, cols] * got[:, cols]
        _, steep = silu_parts(message)
        back = jnp.concatenate([col[3] * steep] * SLOTS, axis=1)
        ws, out = spread(pair_stack(radial * back), b, 3, 8)
        out = out[:CHANNELS] + out[CHANNELS:]
        for i, w in enumerate(ws):
            target = b - 1 + w
            piece = out[:, i * LANES : (i + 1) * LANES]
            where = slice(target * LANES, (target + 1) * LANES)
            if target in started:
                dg[:, where] += piece
            else:
                dg[:, where] = piece
                started.add(target)
        if 3 <= b <= 8:
            basis = bps[b]
            steepness = mm(l3[...], jnp.concatenate([basis, basis], axis=0))
            pull = got * back * steepness
            total = pull[0:8]
            for i in range(1, CHANNELS // 8):
                total = total + pull[8 * i : 8 * i + 8]
            pulls[b] = total

    for b in range(2, 10):
        gather_and_return(b)

    begun = set()

    def put(b, c, value):
        if (b, c) in begun:
            acc[b, c] += value
        else:
            acc[b, c] = value
            begun.add((b, c))

    def finish(b, sums):
        kind = kinds[b]
        rows = []
        for k in range(SLOTS):
            cols = slice(k * LANES, (k + 1) * LANES)
            weight = sums[0:8] + wide_row(kind, k) * sums[8:16]
            rows.append(jnp.sum(bpr[b, :, cols] * weight + pulls[b, :, cols], axis=0, keepdims=True))
        pull = jnp.concatenate(rows, axis=0) * geo[b, 3]
        pieces = []
        for c in range(3):
            value = pull * geo[b, c]
            if 4 <= b <= 7:
                put(b, c, -value)
            pieces.append(split(value))
        lines = []
        for h in range(2):
            for c in range(3):
                lines.append(jnp.concatenate([jnp.where(slot == k, pieces[c][h], 0.0) for k in range(SLOTS)], axis=1))
        ws, out = spread(jnp.concatenate(lines, axis=0).astype(BF16), b, 4, 7)
        for c in range(3):
            both = out[8 * c : 8 * c + 8] + out[24 + 8 * c : 32 + 8 * c]
            for i, w in enumerate(ws):
                put(b - 1 + w, c, both[:, i * LANES : (i + 1) * LANES])

    for b in range(3, 9, 2):
        cols = slice(b * LANES, (b + 2) * LANES)
        steep = mm(l5[...], right_stack(dg[:, cols]))
        steep = steep + jnp.concatenate([col[2], col[2]], axis=1)
        sums = mm(l6[...], right_stack(steep * slope[:, cols]))
        for i in range(2):
            finish(b + i, sums[:, i * LANES : (i + 1) * LANES])


def own_force(acc, c):
    return jnp.concatenate(
        [-jnp.sum(acc[4 + i, c], axis=0, keepdims=True) for i in range(SLAB_BLOCKS)], axis=1
    )


def fill_region(xs, packs, rows_of):
    for b in range(12):
        lanes = slice((b % 4) * LANES, (b % 4 + 1) * LANES)
        pack = packs[b // 4]
        xs[b, 0:3, :] = rows_of(b // 4)[:, lanes]
        xs[b, 3:4, :] = pack[ROW_KIND : ROW_KIND + 1, lanes]


def lane_total(x):
    x = x[:, 0:LANES] + x[:, LANES : 2 * LANES] + x[:, 2 * LANES : 3 * LANES] + x[:, 3 * LANES : 4 * LANES]
    return jnp.sum(x, axis=1, keepdims=True)


def dot3(a, b):
    return jnp.sum(a * b, axis=0, keepdims=True)


def scratch():
    wide = 12 * LANES
    return [
        pltpu.VMEM((12, 8, LANES), F32),
        pltpu.VMEM((12, 8, LANES), jnp.int32),
        pltpu.VMEM((12, 8, LANES), F32),
        pltpu.VMEM((12, 4, 8, LANES), F32),
        pltpu.VMEM((12, 16, SLOTS * LANES), BF16),
        pltpu.VMEM((12, 16, SLOTS * LANES), BF16),
        pltpu.VMEM((12, 8, SLOTS * LANES), F32),
        pltpu.VMEM((48, wide), BF16),
        pltpu.VMEM((CHANNELS, wide), F32),
        pltpu.VMEM((CHANNELS, wide), F32),
        pltpu.VMEM((12, 3 * LANES, SLOTS * LANES), BF16),
        pltpu.VMEM((CHANNELS, wide), F32),
        pltpu.VMEM((12, 8, SLOTS * LANES), F32),
        pltpu.VMEM((12, 3, 8, LANES), F32),
    ]


def by_parity(sibling, across):
    even = jnp.full(sibling.shape, lax.axis_index("dom") % 2, jnp.int32) == 0
    return jnp.where(even, across, sibling), jnp.where(even, sibling, across)


def first_kernel(sibling_ref, po_ref, across_ref, *rest):
    weights, (out_ref, pl_ref, pr_ref), scr = rest[:6], rest[6:9], rest[9:]
    pl_ref[...], pr_ref[...] = by_parity(sibling_ref[...], across_ref[...])
    packs = [pl_ref, po_ref, pr_ref]
    fill_region(scr[0], packs, lambda s: packs[s][ROW_X : ROW_X + 3, :])
    force_parts(packs, weights, scr)
    for c in range(3):
        out_ref[c : c + 1, :] = own_force(scr[-1], c)


def rows_of(ref):
    return jnp.concatenate([ref[c] for c in range(3)], axis=0)


def block_row(*values):
    values = list(values) + [jnp.zeros((1, LANES), F32)] * (SLAB_BLOCKS - len(values))
    return jnp.concatenate(values, axis=1)


def blend_kernel(images, force_ref, po_ref, before_ref, after_ref, out_ref):
    x = po_ref[ROW_X : ROW_X + 3, :]
    v = po_ref[ROW_V : ROW_V + 3, :]
    force = force_ref[...]
    here = lax.axis_index("img")
    before = jnp.where(here > 0, rows_of(before_ref), 0.0)
    after = jnp.where(here < images - 1, rows_of(after_ref), 0.0)
    tangent = after - before
    plus = after - x
    minus = x - before
    sums = jnp.concatenate(
        [
            dot3(force, tangent),
            dot3(force, force),
            dot3(tangent, tangent),
            dot3(plus, plus),
            dot3(minus, minus),
            dot3(v, v),
            jnp.zeros((2, x.shape[1]), F32),
        ],
        axis=0,
    )
    sums = jnp.broadcast_to(lane_total(sums), (8, LANES))
    out_ref[0:3, :] = force
    out_ref[3:6, :] = tangent
    out_ref[6:7, :] = block_row(*[sums[i : i + 1] for i in range(4)])
    out_ref[7:8, :] = block_row(sums[4:5], sums[5:6])


def step_numbers(ft, ff, tt, pp, mn, vv, dt, alpha, flagged, climbing, inside):
    root = jnp.sqrt(tt + TINY_VALUE)
    along = ft / root
    spring = SPRING_CONSTANT * (jnp.sqrt(pp) - jnp.sqrt(mn))
    factor = jnp.where(climbing, -2.0 * along, spring - along)
    band = jnp.maximum(ff + 2.0 * factor * along + factor * factor * (tt / (tt + TINY_VALUE)), 0.0)
    new_dt = jnp.where(flagged, 0.5 * dt, jnp.minimum(1.1 * dt, STEP_LIMIT))
    pull = jnp.where(flagged, 0.0, alpha * jnp.sqrt(vv / (band + TINY_VALUE))) + new_dt
    keep = jnp.where(flagged, 0.0, 1.0 - alpha)
    new_alpha = jnp.where(flagged, ALPHA_START, 0.99 * alpha)
    keep = jnp.where(inside, keep, 0.0)
    pull = jnp.where(inside, pull, 0.0)
    return (
        jnp.where(inside, along, 0.0),
        jnp.where(inside, spring, 0.0),
        keep,
        pull,
        pull * factor / root,
        new_dt,
        new_alpha,
    )


def forward_kernel(own_ref, sibling_ref, out_ref):
    out_ref[0:6, :] = sibling_ref[0:6, :]
    out_ref[6:8, :] = own_ref[6:8, :] + sibling_ref[6:8, :]


def add_kernel(a_ref, b_ref, out_ref):
    out_ref[...] = a_ref[...] + b_ref[...]


def join_kernel(a_ref, b_ref, out_ref):
    count = a_ref.shape[0]
    out_ref[0:count] = a_ref[...]
    out_ref[count : 2 * count] = b_ref[...]


def second_kernel(images, others, paired, number_ref, pl_ref, po_ref, pr_ref, own_ref, *rest):
    heard, rest = rest[:others], rest[others:]
    weights, out_ref, record_ref, scr = rest[:6], rest[6], rest[7], rest[8:]
    packs = [pl_ref, po_ref, pr_ref]
    here = lax.axis_index("img")
    if others == 3 and paired:
        sibling, both, far = heard
        sums = both[6:8, :] + far[6:8, :]
        beside = by_parity(sibling[0:6, :], far[0:6, :])
    else:
        sums = own_ref[6:8, :]
        for one in heard:
            sums = sums + one[6:8, :]
        beside = heard[0][0:6, :], heard[others - 1][0:6, :]
    ft, ff, tt, pp = (sums[0:1, i * LANES : (i + 1) * LANES] for i in range(4))
    mn, vv = (sums[1:2, i * LANES : (i + 1) * LANES] for i in range(2))
    shape = (1, LANES)
    along, spring, keep, pull, side, dt, alpha = step_numbers(
        ft,
        ff,
        tt,
        pp,
        mn,
        vv,
        number_ref[0:1, :],
        jnp.full(shape, ALPHA_START, F32),
        number_ref[2:3, :] == 1.0,
        number_ref[1:2, :] == jnp.full(shape, here, jnp.int32).astype(F32),
        jnp.full(shape, jnp.where((here >= 1) & (here <= images - 2), 1, 0), jnp.int32) == 1,
    )
    messages = [beside[0], own_ref[0:6, :], beside[1]]

    def wide(s):
        return jnp.concatenate([s] * SLAB_BLOCKS, axis=1)

    speeds = [
        wide(keep) * p[ROW_V : ROW_V + 3, :] + wide(pull) * m[0:3, :] + wide(side) * m[3:6, :]
        for p, m in zip(packs, messages)
    ]
    moved = [p[ROW_X : ROW_X + 3, :] + wide(dt) * s for p, s in zip(packs, speeds)]
    fill_region(scr[0], packs, lambda s: moved[s])
    force_parts(packs, weights, scr)
    for c in range(3):
        force = own_force(scr[-1], c)
        for i in range(SLAB_BLOCKS):
            lanes = slice(i * LANES, (i + 1) * LANES)
            row = 4 * c + i
            out_ref[0, row : row + 1, :] = speeds[1][c : c + 1, lanes]
            out_ref[0, 12 + row : 13 + row, :] = force[:, lanes]
            out_ref[0, 24 + row : 25 + row, :] = moved[1][c : c + 1, lanes]
    out_ref[0, 36:37, :] = dt
    out_ref[0, 37:38, :] = alpha
    out_ref[0, 38:40, :] = jnp.broadcast_to(number_ref[3:4, :], (2, LANES))
    record_ref[0:1, :] = along
    record_ref[1:2, :] = spring


PRODUCTS = (
    [("f", "t"), ("f", "f"), ("t", "t"), ("p", "p"), ("d", "d"), ("v", "v")]
    + [("d", "v"), ("d", "f"), ("d", "t"), ("d", "V"), ("d", "F"), ("d", "T"), ("v", "f"), ("v", "t")]
    + [(a, b) for a in "vft" for b in "VFT"]
)


def gram_kernel(images, messages_ref, out_ref, state_ref):
    rows = out_ref.shape[0]
    here = lax.axis_index("img")
    blank = [jnp.zeros((rows - images, LANES), F32)] if rows > images else []
    zero = jnp.zeros((1, LANES), F32)

    def gathered(row):
        return jnp.concatenate([messages_ref[here ^ i, row : row + 1, :] for i in range(images)] + blank, axis=0)

    def earlier(value):
        return jnp.concatenate([zero, value[0 : rows - 1]], axis=0)

    def later(value):
        return jnp.concatenate([value[1:images], zero] + blank, axis=0)

    number = lax.broadcasted_iota(jnp.int32, (rows, LANES), 0)
    held = number < images
    totals = [jnp.zeros((rows, LANES), F32) for _ in PRODUCTS]
    for row in range(3 * SLAB_BLOCKS):
        v, f, x = gathered(row), gathered(12 + row), gathered(24 + row)
        before = jnp.where(held, earlier(x), 0.0)
        after = later(x)
        t = after - before
        table = {"f": f, "v": v, "t": t, "p": after - x, "d": x - before}
        table["F"], table["V"], table["T"] = earlier(f), earlier(v), earlier(t)
        totals = [old + table[a] * table[b] for old, (a, b) in zip(totals, PRODUCTS)]
        state_ref[row : row + 1, :] = jnp.sum(jnp.where(number == here, t, 0.0), axis=0, keepdims=True)
    lane = lax.broadcasted_iota(jnp.int32, (rows, LANES), 1)
    result = jnp.zeros((rows, LANES), F32)
    for q, one in enumerate(totals):
        one = jnp.broadcast_to(jnp.sum(one, axis=1, keepdims=True), (rows, LANES))
        result = jnp.where(lane == q, one, result)
    out_ref[...] = result
    for i in range(3):
        state_ref[16 + rows * i : 16 + rows * (i + 1), :] = gathered(36 + i)


def final_kernel(images, atoms, number_ref, own_ref, record_ref, state_ref, sums_ref, more_ref, *rest):
    x_ref, v_ref, band_ref, path_ref = rest
    rows = sums_ref.shape[0]
    here = lax.axis_index("img")
    sums = sums_ref[...] + more_ref[...]
    got = {
        pair: jnp.broadcast_to(sums[:, q : q + 1], (rows, LANES)) for q, pair in enumerate(PRODUCTS)
    }
    number = lax.broadcasted_iota(jnp.int32, (rows, LANES), 0)
    inside = (number >= 1) & (number <= images - 2)
    climb = jnp.broadcast_to(number_ref[1:2, :], (rows, LANES))
    dt0, alpha0, flag = (state_ref[16 + rows * i : 16 + rows * (i + 1), :] for i in range(3))
    along, spring, keep, pull, side, dt, _ = step_numbers(
        got["f", "t"],
        got["f", "f"],
        got["t", "t"],
        got["p", "p"],
        got["d", "d"],
        got["v", "v"],
        dt0,
        alpha0,
        flag == 1.0,
        number.astype(F32) == climb,
        inside,
    )

    def shifted(value):
        return jnp.concatenate([jnp.zeros((1, LANES), F32), value[0 : rows - 1]], axis=0)

    now = {"v": dt * keep, "f": dt * pull, "t": dt * side}
    old = {a.upper(): shifted(value) for a, value in now.items()}
    mine = now["v"] * now["v"] * got["v", "v"] + now["f"] * now["f"] * got["f", "f"]
    mine = mine + now["t"] * now["t"] * got["t", "t"]
    cross = now["v"] * now["f"] * got["v", "f"] + now["v"] * now["t"] * got["v", "t"]
    mine = mine + 2.0 * (cross + now["f"] * now["t"] * got["f", "t"])
    both = jnp.zeros((rows, LANES), F32)
    for a in "vft":
        both = both + now[a] * got["d", a]
    for b in "VFT":
        both = both - old[b] * got["d", b]
    for a in "vft":
        for b in "VFT":
            both = both - now[a] * old[b] * got[a, b]
    squared = got["d", "d"] + mine + shifted(mine) + 2.0 * both
    segment = jnp.sqrt(jnp.maximum(squared, 0.0) * (1.0 / (3.0 * atoms)))
    path = jnp.sum(jnp.where(number <= here, segment, 0.0), axis=0, keepdims=True)
    path_ref[...] = path[:, 0:1]
    keep, pull, side, dt, along, spring = (
        jnp.sum(jnp.where(number == here, value, 0.0), axis=0, keepdims=True)
        for value in (keep, pull, side, dt, along, spring)
    )

    for c in range(3):
        speeds, places = [], []
        for i in range(SLAB_BLOCKS):
            row = 4 * c + i
            speed = keep * own_ref[0, row : row + 1, :] + pull * own_ref[0, 12 + row : 13 + row, :]
            speed = speed + side * state_ref[row : row + 1, :]
            speeds.append(speed)
            places.append(own_ref[0, 24 + row : 25 + row, :] + dt * speed)
        v_ref[c] = jnp.concatenate(speeds, axis=1)
        x_ref[c] = jnp.concatenate(places, axis=1)
    band_ref[0] = jnp.concatenate([record_ref[0:1, 0:1], record_ref[1:2, 0:1]], axis=1)
    band_ref[1] = jnp.concatenate([along[:, 0:1], spring[:, 0:1]], axis=1)


VMEM_SPEC = pl.BlockSpec(memory_space=pltpu.VMEM)
SMEM_SPEC = pl.BlockSpec(memory_space=pltpu.SMEM)
HBM_SPEC = pl.BlockSpec(memory_space=pltpu.HBM)


def call(body, outs, scalars, arrays, scratch_shapes=(), flops=0, spec=VMEM_SPEC, vmem=24):
    return pl.pallas_call(
        body,
        out_shape=outs,
        in_specs=[SMEM_SPEC] * len(scalars) + [spec] * len(arrays),
        out_specs=jax.tree.map(lambda _: VMEM_SPEC, outs),
        scratch_shapes=list(scratch_shapes),
        compiler_params=pltpu.CompilerParams(vmem_limit_bytes=vmem * 1024 * 1024),
        cost_estimate=pl.CostEstimate(flops=flops, bytes_accessed=1 << 18, transcendentals=0),
    )(*scalars, *arrays)


def around(array, axis):
    count = lax.axis_size(axis)
    return [lax.ppermute(array, axis, [(i, (i + s) % count) for i in range(count)]) for s in range(1, count)]


def ring(array, axis, by):
    count = lax.axis_size(axis)
    return lax.ppermute(array, axis, [(i, (i + by) % count) for i in range(count)])


def swap(array, axis, partner):
    return lax.ppermute(array, axis, [(i, partner(i)) for i in range(lax.axis_size(axis))])


def local(
    disp,
    veloc,
    time_step,
    reset_flags,
    climb,
    species,
    neighbours,
    counts,
    lattice,
    embed,
    radial_weight,
    mix_weight,
    update_weight,
    readout,
):
    atoms = disp.shape[2]
    images = lax.axis_size("img")
    domains = lax.axis_size("dom")
    assert disp.shape[0] == 1 and atoms == SLAB_BLOCKS * LANES and domains >= 4
    assert domains & (domains - 1) == 0 and images & (images - 1) == 0
    shape = jax.ShapeDtypeStruct
    x = jnp.transpose(disp, (1, 0, 2))
    v = jnp.transpose(veloc, (1, 0, 2))
    pack = call(
        pack_kernel,
        shape((PACK_ROWS, atoms), F32),
        (),
        (x, v, species, neighbours, counts, jnp.transpose(lattice, (1, 0, 2))),
        [pltpu.VMEM(a.shape, a.dtype) for a in (x, v, species, neighbours, counts)] + [pltpu.SemaphoreType.DMA((8,))],
        spec=HBM_SPEC,
        vmem=63,
    )
    sibling = swap(pack, "dom", lambda i: i ^ 1)
    across = swap(pack, "dom", lambda i: (i + 2 * (i % 2) - 1) % domains)
    *weights, x_copy, numbers = call(
        weight_kernel,
        (
            shape((CHANNELS, 48), BF16),
            shape((CHANNELS, 192), BF16),
            shape((CHANNELS, 32), BF16),
            shape((CHANNELS, 192), BF16),
            shape((16, 192), BF16),
            shape((4, CHANNELS, LANES), F32),
            shape(x.shape, F32),
            shape((8, LANES), F32),
        ),
        (time_step, jnp.transpose(reset_flags), climb),
        (x, embed, radial_weight, mix_weight, update_weight, readout),
        flops=10000000,
    )
    before, after = ring(x_copy, "img", 1), ring(x_copy, "img", -1)
    force, left, right = call(
        first_kernel,
        (shape((3, atoms), F32), shape(pack.shape, F32), shape(pack.shape, F32)),
        (),
        (sibling, pack, across, *weights),
        scratch(),
        flops=1000000000,
    )
    message = call(
        functools.partial(blend_kernel, images), shape((8, atoms), F32), (), (force, pack, before, after)
    )
    paired = domains == 4
    if paired:
        near = swap(message, "dom", lambda i: i ^ 1)
        both = call(forward_kernel, shape((8, atoms), F32), (), (message, near))
        heard = [near, both, swap(both, "dom", lambda i: i ^ 2)]
    else:
        heard = around(message, "dom")
    state, record = call(
        functools.partial(second_kernel, images, len(heard), paired),
        (shape((1, 40, LANES), F32), shape((2, LANES), F32)),
        (),
        (numbers, left, pack, right, message, *heard, *weights),
        scratch(),
        flops=1000000000,
    )
    gathered, distance = state, 1
    while distance < images:
        more = swap(gathered, "img", lambda i, distance=distance: i ^ distance)
        gathered = call(join_kernel, shape((2 * distance, 40, LANES), F32), (), (gathered, more))
        distance *= 2
    rows = 8 * ((images + 7) // 8)
    sums, extra = call(
        functools.partial(gram_kernel, images),
        (shape((rows, LANES), F32), shape((16 + 3 * rows, LANES), F32)),
        (),
        (gathered,),
    )
    distance = 1
    while True:
        more = swap(sums, "dom", lambda i, distance=distance: i ^ distance)
        distance *= 2
        if distance == domains:
            break
        sums = call(add_kernel, shape((rows, LANES), F32), (), (sums, more))
    new_x, new_v, records, path = call(
        functools.partial(final_kernel, images, atoms * domains),
        (shape(x.shape, F32), shape(x.shape, F32), shape((2, 1, 2), F32), shape((1, 1), F32)),
        (),
        (numbers, state, record, extra, sums, more),
    )
    return (
        jnp.transpose(new_x, (1, 0, 2)),
        jnp.transpose(new_v, (1, 0, 2)),
        jnp.transpose(records, (0, 2, 1)),
        path.reshape(1),
    )


def solution(mesh):
    in_specs = (
        P(("group", "img"), None, "dom"),
        P(("group", "img"), None, "dom"),
        P(("group", "img")),
        P(None, ("group", "img")),
        P("group"),
        P(("group", "dom")),
        P(None, ("group", "dom")),
        P(("group", "dom")),
        P(None, None, ("group", "dom")),
        P(),
        P(),
        P(),
        P(),
        P(),
    )
    out_specs = (
        P(("group", "img"), None, "dom"),
        P(("group", "img"), None, "dom"),
        P(None, None, ("group", "img")),
        P(("group", "img")),
    )
    return jax.shard_map(local, mesh=mesh, in_specs=in_specs, out_specs=out_specs, check_vma=False)
```

```python
import functools
import math

import jax
import jax.numpy as jnp
from jax import lax
from jax.experimental import pallas as pl
from jax.experimental.pallas import tpu as pltpu
from jax.sharding import PartitionSpec as P

F32 = jnp.float32
BF16 = jnp.bfloat16
PRECISE = lax.Precision.HIGHEST
SPRING_CONSTANT = 0.5
ALPHA_START = 0.1
STEP_LIMIT = 0.3
TINY_VALUE = 1e-06
SOFTENING = 0.25
LANES = 128
SLOTS = 8
BASIS = 8
CHANNELS = 64
SLAB_BLOCKS = 4
ROW_X = 32
ROW_COUNT = 35
ROW_KIND = 36
ROW_V = 37
PACK_ROWS = 40
RAW_MIX = 16
RAW_UPDATE = 144
RAW_EMBED = 272
RAW_READOUT = 280
RAW_NUMBER = 288
RAW_ROWS = 296
NT = (((1,), (1,)), ((), ()))


def split(x):
    high = x.astype(BF16).astype(F32)
    return high, x - high


def left_stack(w):
    high, low = split(w)
    return jnp.concatenate([high, high, low], axis=1)


def right_stack(x):
    high, low = split(x)
    high = high.astype(BF16)
    return jnp.concatenate([high, low.astype(BF16), high], axis=0)


def pair_stack(x):
    high, low = split(x)
    return jnp.concatenate([high.astype(BF16), low.astype(BF16)], axis=0)


def mm(a, b):
    return jnp.dot(a, b, preferred_element_type=F32)


def mm_nt(a, b):
    return lax.dot_general(a, b, NT, preferred_element_type=F32)


def pack_kernel(*refs):
    sources, (out_ref, raw_ref), held, sems = refs[:14], refs[14:16], refs[16:26], refs[26]
    lattice, radial, mix, update = sources[10:]
    pairs = list(zip(sources, held))
    pairs += [(lattice.at[c], out_ref.at[pl.ds(8 + 8 * c, 8)]) for c in range(3)]
    pairs += [(radial.at[l], raw_ref.at[pl.ds(BASIS * l, BASIS)]) for l in range(2)]
    pairs += [(mix.at[l], raw_ref.at[pl.ds(RAW_MIX + CHANNELS * l, CHANNELS)]) for l in range(2)]
    pairs += [(update.at[l], raw_ref.at[pl.ds(RAW_UPDATE + CHANNELS * l, CHANNELS)]) for l in range(2)]
    copies = [pltpu.make_async_copy(a, b, sems.at[i]) for i, (a, b) in enumerate(pairs)]
    for one in copies:
        one.start()
    for one in copies:
        one.wait()
    x, v, species, nbr, counts, embed, readout, dt, flags, climb = held
    out_ref[0:8, :] = nbr[...].astype(F32)
    for c in range(3):
        out_ref[ROW_X + c : ROW_X + c + 1, :] = x[c]
        out_ref[ROW_V + c : ROW_V + c + 1, :] = v[c]
    out_ref[ROW_COUNT : ROW_COUNT + 1, :] = counts[...].astype(F32).reshape(1, -1)
    out_ref[ROW_KIND : ROW_KIND + 1, :] = species[...].astype(F32).reshape(1, -1)
    raw_ref[RAW_EMBED : RAW_EMBED + 2, :] = embed[...]
    raw_ref[RAW_READOUT : RAW_READOUT + 1, :] = readout[...].reshape(1, CHANNELS)
    numbers = [dt[0, 0], climb[0, 0].astype(F32)] + [flags[0, s].astype(F32) for s in range(flags.shape[1])]
    for i, value in enumerate(numbers):
        raw_ref[RAW_NUMBER + i : RAW_NUMBER + i + 1, :] = jnp.full((1, CHANNELS), value, F32)


def prepare_kernel(po_ref, raw_ref, *rest):
    own_hot, l1_ref, l2_ref, l3_ref, l5_ref, l6_ref, col_ref, copy_ref, number_ref = rest
    for b in range(SLAB_BLOCKS):
        mark(window_index(po_ref, b), [0, 1, 2], own_hot.at[b])
    for c in range(3):
        copy_ref[c] = po_ref[ROW_X + c : ROW_X + c + 1, :]
    number_ref[...] = jnp.broadcast_to(raw_ref[RAW_NUMBER : RAW_NUMBER + 8, 0:1], (8, LANES))
    radial_ref = [raw_ref[BASIS * l : BASIS * (l + 1), :] for l in range(2)]
    mix_ref = [raw_ref[RAW_MIX + CHANNELS * l : RAW_MIX + CHANNELS * (l + 1), :] for l in range(2)]
    update_ref = [raw_ref[RAW_UPDATE + CHANNELS * l : RAW_UPDATE + CHANNELS * (l + 1), :] for l in range(2)]
    embed_ref = raw_ref[RAW_EMBED : RAW_EMBED + 2, :]
    readout = raw_ref[RAW_READOUT : RAW_READOUT + 1, :]
    eye = (
        lax.broadcasted_iota(jnp.int32, (CHANNELS, CHANNELS), 0)
        == lax.broadcasted_iota(jnp.int32, (CHANNELS, CHANNELS), 1)
    ).astype(F32)

    def turned(x):
        return lax.dot_general(eye, x, NT, precision=PRECISE, preferred_element_type=F32)

    base0 = embed_ref[0:1, :]
    base1 = embed_ref[1:2, :] - base0
    rows = jnp.concatenate([base0, base1], axis=0)
    sent = jnp.dot(rows, mix_ref[0], precision=PRECISE, preferred_element_type=F32)
    scale = 1.0 / math.sqrt(SLOTS)
    first = jnp.concatenate([radial_ref[0] * sent[0:1], radial_ref[0] * sent[1:2]], axis=0) * scale
    second = radial_ref[1] * scale
    folded = jnp.dot(update_ref[0], mix_ref[1], precision=PRECISE, preferred_element_type=F32)
    mix_t = turned(mix_ref[1])
    l1_ref[...] = left_stack(turned(first)).astype(BF16)
    l2_ref[...] = left_stack(turned(folded)).astype(BF16)
    high, low = split(turned(second))
    l3_ref[...] = jnp.concatenate([high, high, low, jnp.zeros_like(high)], axis=1).astype(BF16)
    l5_ref[...] = left_stack(folded).astype(BF16)
    l6_ref[...] = left_stack(first).astype(BF16)
    wide = (CHANNELS, LANES)
    col_ref[0] = jnp.broadcast_to(jnp.sum(mix_t * base0, axis=1, keepdims=True), wide)
    col_ref[1] = jnp.broadcast_to(jnp.sum(mix_t * base1, axis=1, keepdims=True), wide)
    col_ref[2] = jnp.broadcast_to(jnp.sum(update_ref[0] * readout, axis=1, keepdims=True), wide)
    col_ref[3] = jnp.broadcast_to(jnp.sum(update_ref[1] * readout, axis=1, keepdims=True), wide)


def sin_cos(t):
    q = t * t
    s = -1.0 / 39916800.0
    for c in (1.0 / 362880.0, -1.0 / 5040.0, 1.0 / 120.0, -1.0 / 6.0, 1.0):
        s = s * q + c
    k = 1.0 / 479001600.0
    for c in (-1.0 / 3628800.0, 1.0 / 40320.0, -1.0 / 720.0, 1.0 / 24.0, -0.5, 1.0):
        k = k * q + c
    return s * t, k


def wide_row(x, row):
    return jnp.broadcast_to(x[row : row + 1, :], (8, x.shape[1]))


def silu_parts(m):
    sig = 1.0 / (1.0 + jnp.exp(-m))
    return m * sig, sig * (1.0 + m * (1.0 - sig))


def reach(b, first, last):
    return [w for w in range(3) if first <= b - 1 + w <= last]


SIDE_START = {2: 0, 3: LANES, 8: 3 * LANES, 9: 5 * LANES}
SIDE_ROWS = 6 * LANES


def mark(index, ws, target):
    count = len(ws) * LANES
    row_id = lax.broadcasted_iota(jnp.int32, (count, LANES), 0) + ws[0] * LANES
    for k in range(SLOTS):
        same = row_id == jnp.broadcast_to(index[k : k + 1, :], (count, LANES))
        target[:, k * LANES : (k + 1) * LANES] = jnp.where(same, 1.0, 0.0).astype(BF16)


def window_index(pack, b):
    lanes = slice((b % 4) * LANES, (b % 4 + 1) * LANES)
    return pack[0:8, lanes].astype(jnp.int32) - LANES * (b % 4)


def mark_sides(packs, side):
    for b, start in SIDE_START.items():
        ws = reach(b, 3, 8)
        mark(window_index(packs[b // 4], b), ws, side.at[start : start + len(ws) * LANES])


def force_parts(packs, weights, own_hot, side_hot, scr):
    l1, l2, l3, l5, l6, col = weights
    (xs, widx, kinds, geo, bst, bps, bpr, sst, sent_all, slope, dg, pulls, acc) = scr
    centre = 2.0 + 0.5 * lax.broadcasted_iota(jnp.int32, (BASIS, LANES), 0).astype(F32)
    slot = lax.broadcasted_iota(jnp.int32, (SLOTS, LANES), 0)

    def part_rows(value):
        high, low = split(value)
        return jnp.concatenate([high, low], axis=0).astype(BF16)

    def pairs(b):
        pack = packs[b // 4]
        lanes = slice((b % 4) * LANES, (b % 4 + 1) * LANES)
        index = window_index(pack, b)
        widx[b] = index
        inner = index & (LANES - 1)
        part = index >> 7

        def taken(row):
            got = [
                jnp.take_along_axis(jnp.broadcast_to(xs[b - 1 + w, row : row + 1, :], (SLOTS, LANES)), inner, axis=1)
                for w in range(3)
            ]
            return jnp.where(part == 0, got[0], jnp.where(part == 1, got[1], got[2]))

        vec = [
            pack[8 + 8 * c : 16 + 8 * c, lanes] + taken(c) - jnp.broadcast_to(xs[b, c : c + 1, :], (SLOTS, LANES))
            for c in range(3)
        ]
        kind = taken(3)
        dist = jnp.sqrt(vec[0] * vec[0] + vec[1] * vec[1] + vec[2] * vec[2] + SOFTENING)
        live = (slot.astype(F32) < jnp.broadcast_to(pack[ROW_COUNT : ROW_COUNT + 1, lanes], (SLOTS, LANES))).astype(F32)
        turns = dist * (1.0 / 12.0)
        turns = turns - jnp.floor(turns + 0.5)
        sine, cosine = sin_cos(turns * math.pi)
        envelope = cosine * cosine * live
        slant = cosine * sine * live * (-math.pi / 6.0)
        if 3 <= b <= 8:
            kinds[b] = kind
            for c in range(3):
                geo[b, c] = vec[c]
            geo[b, 3] = 1.0 / dist
        total = jnp.zeros((BASIS, LANES), F32)
        total_kind = jnp.zeros((BASIS, LANES), F32)
        for k in range(SLOTS):
            away = wide_row(dist, k) - centre
            gauss = jnp.exp(-4.0 * (away * away))
            env_k = wide_row(envelope, k)
            value = gauss * env_k
            total = total + value
            total_kind = total_kind + value * wide_row(kind, k)
            cols = slice(k * LANES, (k + 1) * LANES)
            if 2 <= b <= 9:
                bst[b, :, cols] = part_rows(value)
            if 3 <= b <= 8:
                value = gauss * (wide_row(slant, k) - 8.0 * away * env_k)
                bpr[b, :, cols] = value
                bps[b, :, cols] = part_rows(value)
        high, low = split(jnp.concatenate([total, total_kind], axis=0))
        sst[:, b * LANES : (b + 1) * LANES] = jnp.concatenate([high, low, high], axis=0).astype(BF16)

    for b in range(1, 11):
        pairs(b)

    for b in range(1, 11, 2):
        cols = slice(b * LANES, (b + 2) * LANES)
        value, steep = silu_parts(mm(l1[...], sst[:, cols]))
        sent = mm(l2[...], right_stack(value))
        for i in range(2):
            one = sent[:, i * LANES : (i + 1) * LANES]
            one = one + col[0] + col[1] * jnp.broadcast_to(xs[b + i, 3:4, :], (CHANNELS, LANES))
            sent_all[:, (b + i) * LANES : (b + i + 1) * LANES] = one
        slope[:, cols] = steep

    def spread(left, b, first, last):
        ws = reach(b, first, last)
        if b in SIDE_START:
            start = SIDE_START[b] + (ws[0] - reach(b, 3, 8)[0]) * LANES
            return ws, mm_nt(left, side_hot[start : start + len(ws) * LANES, :])
        return ws, mm_nt(left, own_hot[b - 4, ws[0] * LANES : (ws[-1] + 1) * LANES, :])

    started = set()

    def gather_and_return(b):
        index = widx[b]
        inner, part = index & (LANES - 1), index >> 7
        windows = [sent_all[:, (b - 1 + w) * LANES : (b + w) * LANES] for w in range(3)]
        got = []
        for k in range(SLOTS):
            lane = jnp.broadcast_to(inner[k : k + 1, :], (CHANNELS, LANES))
            which = jnp.broadcast_to(part[k : k + 1, :], (CHANNELS, LANES))
            pick = [jnp.take_along_axis(window, lane, axis=1) for window in windows]
            got.append(jnp.where(which == 0, pick[0], jnp.where(which == 1, pick[1], pick[2])))
        got = jnp.concatenate(got, axis=1)
        basis = bst[b]
        radial = mm(l3[...], jnp.concatenate([basis, basis], axis=0))
        message = jnp.zeros((CHANNELS, LANES), F32)
        for k in range(SLOTS):
            cols = slice(k * LANES, (k + 1) * LANES)
            message = message + radial[:, cols] * got[:, cols]
        _, steep = silu_parts(message)
        back = jnp.concatenate([col[3] * steep] * SLOTS, axis=1)
        ws, out = spread(pair_stack(radial * back), b, 3, 8)
        out = out[:CHANNELS] + out[CHANNELS:]
        for i, w in enumerate(ws):
            target = b - 1 + w
            piece = out[:, i * LANES : (i + 1) * LANES]
            where = slice(target * LANES, (target + 1) * LANES)
            if target in started:
                dg[:, where] += piece
            else:
                dg[:, where] = piece
                started.add(target)
        if 3 <= b <= 8:
            basis = bps[b]
            steepness = mm(l3[...], jnp.concatenate([basis, basis], axis=0))
            pull = got * back * steepness
            total = pull[0:8]
            for i in range(1, CHANNELS // 8):
                total = total + pull[8 * i : 8 * i + 8]
            pulls[b] = total

    for b in range(2, 10):
        gather_and_return(b)

    begun = set()

    def put(b, c, value):
        if (b, c) in begun:
            acc[b, c] += value
        else:
            acc[b, c] = value
            begun.add((b, c))

    def finish(b, sums):
        kind = kinds[b]
        rows = []
        for k in range(SLOTS):
            cols = slice(k * LANES, (k + 1) * LANES)
            weight = sums[0:8] + wide_row(kind, k) * sums[8:16]
            rows.append(jnp.sum(bpr[b, :, cols] * weight + pulls[b, :, cols], axis=0, keepdims=True))
        pull = jnp.concatenate(rows, axis=0) * geo[b, 3]
        pieces = []
        for c in range(3):
            value = pull * geo[b, c]
            if 4 <= b <= 7:
                put(b, c, -value)
            pieces.append(split(value))
        lines = []
        for h in range(2):
            for c in range(3):
                lines.append(jnp.concatenate([jnp.where(slot == k, pieces[c][h], 0.0) for k in range(SLOTS)], axis=1))
        ws, out = spread(jnp.concatenate(lines, axis=0).astype(BF16), b, 4, 7)
        for c in range(3):
            both = out[8 * c : 8 * c + 8] + out[24 + 8 * c : 32 + 8 * c]
            for i, w in enumerate(ws):
                put(b - 1 + w, c, both[:, i * LANES : (i + 1) * LANES])

    for b in range(3, 9, 2):
        cols = slice(b * LANES, (b + 2) * LANES)
        steep = mm(l5[...], right_stack(dg[:, cols]))
        steep = steep + jnp.concatenate([col[2], col[2]], axis=1)
        sums = mm(l6[...], right_stack(steep * slope[:, cols]))
        for i in range(2):
            finish(b + i, sums[:, i * LANES : (i + 1) * LANES])


def own_force(acc, c):
    return jnp.concatenate(
        [-jnp.sum(acc[4 + i, c], axis=0, keepdims=True) for i in range(SLAB_BLOCKS)], axis=1
    )


def fill_region(xs, packs, rows_of):
    for b in range(12):
        lanes = slice((b % 4) * LANES, (b % 4 + 1) * LANES)
        pack = packs[b // 4]
        xs[b, 0:3, :] = rows_of(b // 4)[:, lanes]
        xs[b, 3:4, :] = pack[ROW_KIND : ROW_KIND + 1, lanes]


def lane_total(x):
    x = x[:, 0:LANES] + x[:, LANES : 2 * LANES] + x[:, 2 * LANES : 3 * LANES] + x[:, 3 * LANES : 4 * LANES]
    return jnp.sum(x, axis=1, keepdims=True)


def dot3(a, b):
    return jnp.sum(a * b, axis=0, keepdims=True)


def scratch():
    wide = 12 * LANES
    return [
        pltpu.VMEM((12, 8, LANES), F32),
        pltpu.VMEM((12, 8, LANES), jnp.int32),
        pltpu.VMEM((12, 8, LANES), F32),
        pltpu.VMEM((12, 4, 8, LANES), F32),
        pltpu.VMEM((12, 16, SLOTS * LANES), BF16),
        pltpu.VMEM((12, 16, SLOTS * LANES), BF16),
        pltpu.VMEM((12, 8, SLOTS * LANES), F32),
        pltpu.VMEM((48, wide), BF16),
        pltpu.VMEM((CHANNELS, wide), F32),
        pltpu.VMEM((CHANNELS, wide), F32),
        pltpu.VMEM((CHANNELS, wide), F32),
        pltpu.VMEM((12, 8, SLOTS * LANES), F32),
        pltpu.VMEM((12, 3, 8, LANES), F32),
    ]


def by_parity(sibling, across):
    even = jnp.full(sibling.shape, lax.axis_index("dom") % 2, jnp.int32) == 0
    return jnp.where(even, across, sibling), jnp.where(even, sibling, across)


def first_kernel(sibling_ref, po_ref, across_ref, own_hot, *rest):
    weights, (out_ref, pl_ref, pr_ref, side_hot), scr = rest[:6], rest[6:10], rest[10:]
    pl_ref[...], pr_ref[...] = by_parity(sibling_ref[...], across_ref[...])
    packs = [pl_ref, po_ref, pr_ref]
    mark_sides(packs, side_hot)
    fill_region(scr[0], packs, lambda s: packs[s][ROW_X : ROW_X + 3, :])
    force_parts(packs, weights, own_hot, side_hot, scr)
    for c in range(3):
        out_ref[c : c + 1, :] = own_force(scr[-1], c)


def rows_of(ref):
    return jnp.concatenate([ref[c] for c in range(3)], axis=0)


def block_row(*values):
    values = list(values) + [jnp.zeros((1, LANES), F32)] * (SLAB_BLOCKS - len(values))
    return jnp.concatenate(values, axis=1)


def blend_kernel(images, force_ref, po_ref, pair_ref, other_ref, out_ref, sums_ref):
    x = po_ref[ROW_X : ROW_X + 3, :]
    v = po_ref[ROW_V : ROW_V + 3, :]
    force = force_ref[...]
    here = lax.axis_index("img")
    pair, other = rows_of(pair_ref), rows_of(other_ref)
    even = here % 2 == 0
    before = jnp.where(here > 0, jnp.where(even, other, pair), 0.0)
    after = jnp.where(here < images - 1, jnp.where(even, pair, other), 0.0)
    tangent = after - before
    plus = after - x
    minus = x - before
    sums = jnp.concatenate(
        [
            dot3(force, tangent),
            dot3(force, force),
            dot3(tangent, tangent),
            dot3(plus, plus),
            dot3(minus, minus),
            dot3(v, v),
            jnp.zeros((2, x.shape[1]), F32),
        ],
        axis=0,
    )
    sums = jnp.broadcast_to(lane_total(sums), (8, LANES))
    sums_ref[...] = sums
    out_ref[0:3, :] = force
    out_ref[3:6, :] = tangent
    out_ref[6:7, :] = block_row(*[sums[i : i + 1] for i in range(4)])
    out_ref[7:8, :] = block_row(sums[4:5], sums[5:6])


def step_numbers(ft, ff, tt, pp, mn, vv, dt, alpha, flagged, climbing, inside):
    root = jnp.sqrt(tt + TINY_VALUE)
    along = ft / root
    spring = SPRING_CONSTANT * (jnp.sqrt(pp) - jnp.sqrt(mn))
    factor = jnp.where(climbing, -2.0 * along, spring - along)
    band = jnp.maximum(ff + 2.0 * factor * along + factor * factor * (tt / (tt + TINY_VALUE)), 0.0)
    new_dt = jnp.where(flagged, 0.5 * dt, jnp.minimum(1.1 * dt, STEP_LIMIT))
    pull = jnp.where(flagged, 0.0, alpha * jnp.sqrt(vv / (band + TINY_VALUE))) + new_dt
    keep = jnp.where(flagged, 0.0, 1.0 - alpha)
    new_alpha = jnp.where(flagged, ALPHA_START, 0.99 * alpha)
    keep = jnp.where(inside, keep, 0.0)
    pull = jnp.where(inside, pull, 0.0)
    return (
        jnp.where(inside, along, 0.0),
        jnp.where(inside, spring, 0.0),
        keep,
        pull,
        pull * factor / root,
        new_dt,
        new_alpha,
    )


def add_kernel(a_ref, b_ref, out_ref):
    out_ref[...] = a_ref[...] + b_ref[...]


def join_kernel(a_ref, b_ref, out_ref):
    count = a_ref.shape[0]
    out_ref[0:count] = a_ref[...]
    out_ref[count : 2 * count] = b_ref[...]


def second_kernel(images, domains, number_ref, pl_ref, po_ref, pr_ref, own_ref, near_ref, far_ref, *rest):
    count = 2 if domains == 4 else 1
    parts, rest = rest[:count], rest[count:]
    (own_hot, side_hot), weights, (out_ref, record_ref), scr = rest[:2], rest[2:8], rest[8:10], rest[10:]
    packs = [pl_ref, po_ref, pr_ref]
    here = lax.axis_index("img")
    sums = parts[0][...]
    if domains == 4:
        sums = sums + parts[1][...]
    got = [sums[i : i + 1, :] for i in range(6)]
    if domains == 4:
        for one in (near_ref, far_ref):
            for i in range(6):
                got[i] = got[i] + one[6 + i // 4 : 7 + i // 4, (i % 4) * LANES : (i % 4 + 1) * LANES]
    ft, ff, tt, pp, mn, vv = got
    beside = by_parity(near_ref[0:6, :], far_ref[0:6, :])
    shape = (1, LANES)
    along, spring, keep, pull, side, dt, alpha = step_numbers(
        ft,
        ff,
        tt,
        pp,
        mn,
        vv,
        number_ref[0:1, :],
        jnp.full(shape, ALPHA_START, F32),
        number_ref[2:3, :] == 1.0,
        number_ref[1:2, :] == jnp.full(shape, here, jnp.int32).astype(F32),
        jnp.full(shape, jnp.where((here >= 1) & (here <= images - 2), 1, 0), jnp.int32) == 1,
    )
    messages = [beside[0], own_ref[0:6, :], beside[1]]

    def wide(s):
        return jnp.concatenate([s] * SLAB_BLOCKS, axis=1)

    speeds = [
        wide(keep) * p[ROW_V : ROW_V + 3, :] + wide(pull) * m[0:3, :] + wide(side) * m[3:6, :]
        for p, m in zip(packs, messages)
    ]
    moved = [p[ROW_X : ROW_X + 3, :] + wide(dt) * s for p, s in zip(packs, speeds)]
    fill_region(scr[0], packs, lambda s: moved[s])
    force_parts(packs, weights, own_hot, side_hot, scr)
    for c in range(3):
        force = own_force(scr[-1], c)
        for i in range(SLAB_BLOCKS):
            lanes = slice(i * LANES, (i + 1) * LANES)
            row = 4 * c + i
            out_ref[0, row : row + 1, :] = speeds[1][c : c + 1, lanes]
            out_ref[0, 12 + row : 13 + row, :] = force[:, lanes]
            out_ref[0, 24 + row : 25 + row, :] = moved[1][c : c + 1, lanes]
    out_ref[0, 36:37, :] = dt
    out_ref[0, 37:38, :] = alpha
    out_ref[0, 38:40, :] = jnp.broadcast_to(number_ref[3:4, :], (2, LANES))
    record_ref[0:1, :] = along
    record_ref[1:2, :] = spring


PRODUCTS = (
    [("f", "t"), ("f", "f"), ("t", "t"), ("p", "p"), ("d", "d"), ("v", "v")]
    + [("d", "v"), ("d", "f"), ("d", "t"), ("d", "V"), ("d", "F"), ("d", "T"), ("v", "f"), ("v", "t")]
    + [(a, b) for a in "vft" for b in "VFT"]
)


def gram_kernel(images, *refs):
    parts, (out_ref, state_ref, messages_ref) = refs[:-3], refs[-3:]
    rows = out_ref.shape[0]
    place = 0
    for part in parts:
        messages_ref[place : place + part.shape[0]] = part[...]
        place += part.shape[0]
    here = lax.axis_index("img")
    blank = [jnp.zeros((rows - images, LANES), F32)] if rows > images else []
    zero = jnp.zeros((1, LANES), F32)

    def gathered(row):
        return jnp.concatenate([messages_ref[here ^ i, row : row + 1, :] for i in range(images)] + blank, axis=0)

    def earlier(value):
        return jnp.concatenate([zero, value[0 : rows - 1]], axis=0)

    def later(value):
        return jnp.concatenate([value[1:images], zero] + blank, axis=0)

    number = lax.broadcasted_iota(jnp.int32, (rows, LANES), 0)
    held = number < images
    totals = [jnp.zeros((rows, LANES), F32) for _ in PRODUCTS]
    for row in range(3 * SLAB_BLOCKS):
        v, f, x = gathered(row), gathered(12 + row), gathered(24 + row)
        before = jnp.where(held, earlier(x), 0.0)
        after = later(x)
        t = after - before
        table = {"f": f, "v": v, "t": t, "p": after - x, "d": x - before}
        table["F"], table["V"], table["T"] = earlier(f), earlier(v), earlier(t)
        totals = [old + table[a] * table[b] for old, (a, b) in zip(totals, PRODUCTS)]
        state_ref[row : row + 1, :] = jnp.sum(jnp.where(number == here, t, 0.0), axis=0, keepdims=True)
    lane = lax.broadcasted_iota(jnp.int32, (rows, LANES), 1)
    result = jnp.zeros((rows, LANES), F32)
    for q, one in enumerate(totals):
        one = jnp.broadcast_to(jnp.sum(one, axis=1, keepdims=True), (rows, LANES))
        result = jnp.where(lane == q, one, result)
    out_ref[...] = result
    for i in range(3):
        state_ref[16 + rows * i : 16 + rows * (i + 1), :] = gathered(36 + i)


def final_kernel(images, atoms, number_ref, own_ref, record_ref, state_ref, *rest):
    parts, (x_ref, v_ref, band_ref, path_ref) = rest[:-4], rest[-4:]
    rows = parts[0].shape[0]
    here = lax.axis_index("img")
    sums = parts[0][...]
    for one in parts[1:]:
        sums = sums + one[...]
    got = {
        pair: jnp.broadcast_to(sums[:, q : q + 1], (rows, LANES)) for q, pair in enumerate(PRODUCTS)
    }
    number = lax.broadcasted_iota(jnp.int32, (rows, LANES), 0)
    inside = (number >= 1) & (number <= images - 2)
    climb = jnp.broadcast_to(number_ref[1:2, :], (rows, LANES))
    dt0, alpha0, flag = (state_ref[16 + rows * i : 16 + rows * (i + 1), :] for i in range(3))
    along, spring, keep, pull, side, dt, _ = step_numbers(
        got["f", "t"],
        got["f", "f"],
        got["t", "t"],
        got["p", "p"],
        got["d", "d"],
        got["v", "v"],
        dt0,
        alpha0,
        flag == 1.0,
        number.astype(F32) == climb,
        inside,
    )

    def shifted(value):
        return jnp.concatenate([jnp.zeros((1, LANES), F32), value[0 : rows - 1]], axis=0)

    now = {"v": dt * keep, "f": dt * pull, "t": dt * side}
    old = {a.upper(): shifted(value) for a, value in now.items()}
    mine = now["v"] * now["v"] * got["v", "v"] + now["f"] * now["f"] * got["f", "f"]
    mine = mine + now["t"] * now["t"] * got["t", "t"]
    cross = now["v"] * now["f"] * got["v", "f"] + now["v"] * now["t"] * got["v", "t"]
    mine = mine + 2.0 * (cross + now["f"] * now["t"] * got["f", "t"])
    both = jnp.zeros((rows, LANES), F32)
    for a in "vft":
        both = both + now[a] * got["d", a]
    for b in "VFT":
        both = both - old[b] * got["d", b]
    for a in "vft":
        for b in "VFT":
            both = both - now[a] * old[b] * got[a, b]
    squared = got["d", "d"] + mine + shifted(mine) + 2.0 * both
    segment = jnp.sqrt(jnp.maximum(squared, 0.0) * (1.0 / (3.0 * atoms)))
    path = jnp.sum(jnp.where(number <= here, segment, 0.0), axis=0, keepdims=True)
    path_ref[...] = path[:, 0:1]
    keep, pull, side, dt, along, spring = (
        jnp.sum(jnp.where(number == here, value, 0.0), axis=0, keepdims=True)
        for value in (keep, pull, side, dt, along, spring)
    )

    for c in range(3):
        speeds, places = [], []
        for i in range(SLAB_BLOCKS):
            row = 4 * c + i
            speed = keep * own_ref[0, row : row + 1, :] + pull * own_ref[0, 12 + row : 13 + row, :]
            speed = speed + side * state_ref[row : row + 1, :]
            speeds.append(speed)
            places.append(own_ref[0, 24 + row : 25 + row, :] + dt * speed)
        v_ref[c] = jnp.concatenate(speeds, axis=1)
        x_ref[c] = jnp.concatenate(places, axis=1)
    band_ref[0] = jnp.concatenate([record_ref[0:1, 0:1], record_ref[1:2, 0:1]], axis=1)
    band_ref[1] = jnp.concatenate([along[:, 0:1], spring[:, 0:1]], axis=1)


VMEM_SPEC = pl.BlockSpec(memory_space=pltpu.VMEM)
SMEM_SPEC = pl.BlockSpec(memory_space=pltpu.SMEM)
HBM_SPEC = pl.BlockSpec(memory_space=pltpu.HBM)


def call(body, outs, scalars, arrays, scratch_shapes=(), flops=0, spec=VMEM_SPEC, vmem=24):
    return pl.pallas_call(
        body,
        out_shape=outs,
        in_specs=[SMEM_SPEC] * len(scalars) + [spec] * len(arrays),
        out_specs=jax.tree.map(lambda _: VMEM_SPEC, outs),
        scratch_shapes=list(scratch_shapes),
        compiler_params=pltpu.CompilerParams(vmem_limit_bytes=vmem * 1024 * 1024),
        cost_estimate=pl.CostEstimate(flops=flops, bytes_accessed=1 << 18, transcendentals=0),
    )(*scalars, *arrays)


def swap(array, axis, partner):
    return lax.ppermute(array, axis, [(i, partner(i)) for i in range(lax.axis_size(axis))])


def exchanged(sums, axis):
    count = lax.axis_size(axis)
    if count == 4:
        return [sums] + [swap(sums, axis, lambda i, by=by: i ^ by) for by in (2, 3, 1)]
    distance = 1
    while distance < count:
        more = swap(sums, axis, lambda i, by=distance: i ^ by)
        sums = call(add_kernel, jax.ShapeDtypeStruct(sums.shape, F32), (), (sums, more))
        distance *= 2
    return [sums]


def collected(array, axis):
    count = lax.axis_size(axis)
    if count == 4:
        far = [swap(array, axis, lambda i, by=by: i ^ by) for by in (3, 2, 1)]
        return [array] + far[::-1]
    distance = 1
    while distance < count:
        more = swap(array, axis, lambda i, by=distance: i ^ by)
        shape = jax.ShapeDtypeStruct((2 * distance,) + array.shape[1:], F32)
        array = call(join_kernel, shape, (), (array, more))
        distance *= 2
    return [array]


def local(
    disp,
    veloc,
    time_step,
    reset_flags,
    climb,
    species,
    neighbours,
    counts,
    lattice,
    embed,
    radial_weight,
    mix_weight,
    update_weight,
    readout,
):
    atoms = disp.shape[2]
    images = lax.axis_size("img")
    domains = lax.axis_size("dom")
    assert disp.shape[0] == 1 and atoms == SLAB_BLOCKS * LANES and domains >= 4
    assert domains & (domains - 1) == 0 and images & (images - 1) == 0
    shape = jax.ShapeDtypeStruct
    x = jnp.transpose(disp, (1, 0, 2))
    v = jnp.transpose(veloc, (1, 0, 2))
    small = (x, v, species, neighbours, counts, embed, readout)
    numbers = (time_step.reshape(1, 1), jnp.transpose(reset_flags), climb.reshape(1, 1))
    pack, raw = call(
        pack_kernel,
        (shape((PACK_ROWS, atoms), F32), shape((RAW_ROWS, CHANNELS), F32)),
        (),
        (*small, *numbers, jnp.transpose(lattice, (1, 0, 2)), radial_weight, mix_weight, update_weight),
        [pltpu.VMEM(a.shape, a.dtype) for a in small]
        + [pltpu.SMEM(a.shape, a.dtype) for a in numbers]
        + [pltpu.SemaphoreType.DMA((19,))],
        spec=HBM_SPEC,
        vmem=63,
    )
    sibling = swap(pack, "dom", lambda i: i ^ 1)
    across = swap(pack, "dom", lambda i: (i + 2 * (i % 2) - 1) % domains)
    own_hot, *weights, x_copy, numbers = call(
        prepare_kernel,
        (
            shape((SLAB_BLOCKS, 3 * LANES, SLOTS * LANES), BF16),
            shape((CHANNELS, 48), BF16),
            shape((CHANNELS, 192), BF16),
            shape((CHANNELS, 32), BF16),
            shape((CHANNELS, 192), BF16),
            shape((16, 192), BF16),
            shape((4, CHANNELS, LANES), F32),
            shape(x.shape, F32),
            shape((8, LANES), F32),
        ),
        (),
        (pack, raw),
        flops=100000000,
    )
    pair = swap(x_copy, "img", lambda i: i ^ 1)
    other = swap(x_copy, "img", lambda i: i if i in (0, images - 1) else i + 2 * (i % 2) - 1)
    force, left, right, side_hot = call(
        first_kernel,
        (
            shape((3, atoms), F32),
            shape(pack.shape, F32),
            shape(pack.shape, F32),
            shape((SIDE_ROWS, SLOTS * LANES), BF16),
        ),
        (),
        (sibling, pack, across, own_hot, *weights),
        scratch(),
        flops=1000000000,
    )
    message, sums = call(
        functools.partial(blend_kernel, images),
        (shape((8, atoms), F32), shape((8, LANES), F32)),
        (),
        (force, pack, pair, other),
    )
    far = swap(message, "dom", lambda i: (i + 2 * (i % 2) - 1) % domains)
    if domains == 4:
        parts = [sums, swap(sums, "dom", lambda i: i ^ 2)]
    else:
        parts = exchanged(sums, "dom")
    near = swap(message, "dom", lambda i: i ^ 1)
    state, record = call(
        functools.partial(second_kernel, images, domains),
        (shape((1, 40, LANES), F32), shape((2, LANES), F32)),
        (),
        (numbers, left, pack, right, message, near, far, *parts, own_hot, side_hot, *weights),
        scratch(),
        flops=1000000000,
    )
    rows = 8 * ((images + 7) // 8)
    sums, extra = call(
        functools.partial(gram_kernel, images),
        (shape((rows, LANES), F32), shape((16 + 3 * rows, LANES), F32)),
        (),
        collected(state, "img"),
        [pltpu.VMEM((images, 40, LANES), F32)],
    )
    new_x, new_v, records, path = call(
        functools.partial(final_kernel, images, atoms * domains),
        (shape(x.shape, F32), shape(x.shape, F32), shape((2, 1, 2), F32), shape((1, 1), F32)),
        (),
        (numbers, state, record, extra, *exchanged(sums, "dom")),
    )
    return (
        jnp.transpose(new_x, (1, 0, 2)),
        jnp.transpose(new_v, (1, 0, 2)),
        jnp.transpose(records, (0, 2, 1)),
        path.reshape(1),
    )


def solution(mesh):
    in_specs = (
        P(("group", "img"), None, "dom"),
        P(("group", "img"), None, "dom"),
        P(("group", "img")),
        P(None, ("group", "img")),
        P("group"),
        P(("group", "dom")),
        P(None, ("group", "dom")),
        P(("group", "dom")),
        P(None, None, ("group", "dom")),
        P(),
        P(),
        P(),
        P(),
        P(),
    )
    out_specs = (
        P(("group", "img"), None, "dom"),
        P(("group", "img"), None, "dom"),
        P(None, None, ("group", "img")),
        P(("group", "img")),
    )
    return jax.shard_map(local, mesh=mesh, in_specs=in_specs, out_specs=out_specs, check_vma=False)
```

```python
import functools
import math

import jax
import jax.numpy as jnp
from jax import lax
from jax.experimental import pallas as pl
from jax.experimental.pallas import tpu as pltpu
from jax.sharding import PartitionSpec as P

F32 = jnp.float32
BF16 = jnp.bfloat16
PRECISE = lax.Precision.HIGHEST
SPRING_CONSTANT = 0.5
ALPHA_START = 0.1
STEP_LIMIT = 0.3
TINY_VALUE = 1e-06
SOFTENING = 0.25
LANES = 128
SLOTS = 8
BASIS = 8
CHANNELS = 64
SLAB_BLOCKS = 4
ROW_X = 32
ROW_COUNT = 35
ROW_KIND = 36
ROW_V = 37
PACK_ROWS = 40
OWN_ROWS = PACK_ROWS + CHANNELS + BASIS
NT = (((1,), (1,)), ((), ()))


def split(x):
    high = x.astype(BF16).astype(F32)
    return high, x - high


def left_stack(w):
    high, low = split(w)
    return jnp.concatenate([high, high, low], axis=1)


def right_stack(x):
    high, low = split(x)
    high = high.astype(BF16)
    return jnp.concatenate([high, low.astype(BF16), high], axis=0)


def pair_stack(x):
    high, low = split(x)
    return jnp.concatenate([high.astype(BF16), low.astype(BF16)], axis=0)


def mm(a, b):
    return jnp.dot(a, b, preferred_element_type=F32)


def mm_nt(a, b):
    return lax.dot_general(a, b, NT, preferred_element_type=F32)


def pack_kernel(*refs):
    sources, (out_ref, own_ref), held, sems = refs[:11], refs[11:13], refs[13:23], refs[23]
    lattice = sources[10]
    pairs = list(zip(sources, held))
    for c in range(3):
        rows = pl.ds(8 + 8 * c, 8)
        pairs += [(lattice.at[c], out_ref.at[rows]), (lattice.at[c], own_ref.at[rows])]
    copies = [pltpu.make_async_copy(a, b, sems.at[i]) for i, (a, b) in enumerate(pairs)]
    for one in copies:
        one.start()
    for one in copies:
        one.wait()
    x, v, species, nbr, counts, embed, readout, radial, mix, update = held
    for ref in (out_ref, own_ref):
        ref[0:8, :] = nbr[...].astype(F32)
        for c in range(3):
            ref[ROW_X + c : ROW_X + c + 1, :] = x[c]
            ref[ROW_V + c : ROW_V + c + 1, :] = v[c]
        ref[ROW_COUNT : ROW_COUNT + 1, :] = counts[...].astype(F32).reshape(1, -1)
        ref[ROW_KIND : ROW_KIND + 1, :] = species[...].astype(F32).reshape(1, -1)
    top, low = PACK_ROWS, PACK_ROWS + CHANNELS
    for i, value in enumerate([mix[0], mix[1], update[0], update[1]]):
        own_ref[top:low, i * LANES : i * LANES + CHANNELS] = value
    for i, value in enumerate([radial[0], radial[1], embed[...], readout[...].reshape(1, CHANNELS)]):
        own_ref[low : low + value.shape[0], i * LANES : i * LANES + CHANNELS] = value


def prepare_kernel(po_ref, *rest):
    own_hot, l1_ref, l2_ref, l3_ref, l5_ref, l6_ref, col_ref, copy_ref = rest
    for b in range(SLAB_BLOCKS):
        mark(window_index(po_ref, b), [0, 1, 2], own_hot.at[b])
    for c in range(3):
        copy_ref[c] = po_ref[ROW_X + c : ROW_X + c + 1, :]

    def raw(first, count, i):
        return po_ref[first : first + count, i * LANES : i * LANES + CHANNELS]

    low = PACK_ROWS + CHANNELS
    mix_ref = [raw(PACK_ROWS, CHANNELS, i) for i in range(2)]
    update_ref = [raw(PACK_ROWS, CHANNELS, 2 + i) for i in range(2)]
    radial_ref = [raw(low, BASIS, i) for i in range(2)]
    embed_ref, readout = raw(low, 2, 2), raw(low, 1, 3)
    eye = (
        lax.broadcasted_iota(jnp.int32, (CHANNELS, CHANNELS), 0)
        == lax.broadcasted_iota(jnp.int32, (CHANNELS, CHANNELS), 1)
    ).astype(F32)

    def turned(x):
        return lax.dot_general(eye, x, NT, precision=PRECISE, preferred_element_type=F32)

    base0 = embed_ref[0:1, :]
    base1 = embed_ref[1:2, :] - base0
    rows = jnp.concatenate([base0, base1], axis=0)
    sent = jnp.dot(rows, mix_ref[0], precision=PRECISE, preferred_element_type=F32)
    scale = 1.0 / math.sqrt(SLOTS)
    first = jnp.concatenate([radial_ref[0] * sent[0:1], radial_ref[0] * sent[1:2]], axis=0) * scale
    second = radial_ref[1] * scale
    folded = jnp.dot(update_ref[0], mix_ref[1], precision=PRECISE, preferred_element_type=F32)
    mix_t = turned(mix_ref[1])
    l1_ref[...] = left_stack(turned(first)).astype(BF16)
    l2_ref[...] = left_stack(turned(folded)).astype(BF16)
    high, low = split(turned(second))
    l3_ref[...] = jnp.concatenate([high, high, low, jnp.zeros_like(high)], axis=1).astype(BF16)
    l5_ref[...] = left_stack(folded).astype(BF16)
    l6_ref[...] = left_stack(first).astype(BF16)
    wide = (CHANNELS, LANES)
    col_ref[0] = jnp.broadcast_to(jnp.sum(mix_t * base0, axis=1, keepdims=True), wide)
    col_ref[1] = jnp.broadcast_to(jnp.sum(mix_t * base1, axis=1, keepdims=True), wide)
    col_ref[2] = jnp.broadcast_to(jnp.sum(update_ref[0] * readout, axis=1, keepdims=True), wide)
    col_ref[3] = jnp.broadcast_to(jnp.sum(update_ref[1] * readout, axis=1, keepdims=True), wide)


def sin_cos(t):
    q = t * t
    s = -1.0 / 39916800.0
    for c in (1.0 / 362880.0, -1.0 / 5040.0, 1.0 / 120.0, -1.0 / 6.0, 1.0):
        s = s * q + c
    k = 1.0 / 479001600.0
    for c in (-1.0 / 3628800.0, 1.0 / 40320.0, -1.0 / 720.0, 1.0 / 24.0, -0.5, 1.0):
        k = k * q + c
    return s * t, k


def wide_row(x, row):
    return jnp.broadcast_to(x[row : row + 1, :], (8, x.shape[1]))


def silu_parts(m):
    sig = 1.0 / (1.0 + jnp.exp(-m))
    return m * sig, sig * (1.0 + m * (1.0 - sig))


def reach(b, first, last):
    return [w for w in range(3) if first <= b - 1 + w <= last]


SIDE_START = {2: 0, 3: LANES, 8: 3 * LANES, 9: 5 * LANES}
SIDE_ROWS = 6 * LANES


def mark(index, ws, target):
    count = len(ws) * LANES
    row_id = lax.broadcasted_iota(jnp.int32, (count, LANES), 0) + ws[0] * LANES
    for k in range(SLOTS):
        same = row_id == jnp.broadcast_to(index[k : k + 1, :], (count, LANES))
        target[:, k * LANES : (k + 1) * LANES] = jnp.where(same, 1.0, 0.0).astype(BF16)


def window_index(pack, b):
    lanes = slice((b % 4) * LANES, (b % 4 + 1) * LANES)
    return pack[0:8, lanes].astype(jnp.int32) - LANES * (b % 4)


def mark_sides(packs, side):
    for b, start in SIDE_START.items():
        ws = reach(b, 3, 8)
        mark(window_index(packs[b // 4], b), ws, side.at[start : start + len(ws) * LANES])


def forward_parts(packs, weights, xs, sst, kept):
    l1, l2, l3, l5, l6, col = weights
    (widx, kinds, geo, bst, bps, bpr, sent_all, slope) = kept
    centre = 2.0 + 0.5 * lax.broadcasted_iota(jnp.int32, (BASIS, LANES), 0).astype(F32)
    slot = lax.broadcasted_iota(jnp.int32, (SLOTS, LANES), 0)

    def part_rows(value):
        high, low = split(value)
        return jnp.concatenate([high, low], axis=0).astype(BF16)

    def pairs(b):
        pack = packs[b // 4]
        lanes = slice((b % 4) * LANES, (b % 4 + 1) * LANES)
        index = window_index(pack, b)
        widx[b] = index
        inner = index & (LANES - 1)
        part = index >> 7

        def taken(row):
            got = [
                jnp.take_along_axis(jnp.broadcast_to(xs[b - 1 + w, row : row + 1, :], (SLOTS, LANES)), inner, axis=1)
                for w in range(3)
            ]
            return jnp.where(part == 0, got[0], jnp.where(part == 1, got[1], got[2]))

        vec = [
            pack[8 + 8 * c : 16 + 8 * c, lanes] + taken(c) - jnp.broadcast_to(xs[b, c : c + 1, :], (SLOTS, LANES))
            for c in range(3)
        ]
        kind = taken(3)
        dist = jnp.sqrt(vec[0] * vec[0] + vec[1] * vec[1] + vec[2] * vec[2] + SOFTENING)
        live = (slot.astype(F32) < jnp.broadcast_to(pack[ROW_COUNT : ROW_COUNT + 1, lanes], (SLOTS, LANES))).astype(F32)
        turns = dist * (1.0 / 12.0)
        turns = turns - jnp.floor(turns + 0.5)
        sine, cosine = sin_cos(turns * math.pi)
        envelope = cosine * cosine * live
        slant = cosine * sine * live * (-math.pi / 6.0)
        if 3 <= b <= 8:
            kinds[b] = kind
            for c in range(3):
                geo[b, c] = vec[c]
            geo[b, 3] = 1.0 / dist
        total = jnp.zeros((BASIS, LANES), F32)
        total_kind = jnp.zeros((BASIS, LANES), F32)
        for k in range(SLOTS):
            away = wide_row(dist, k) - centre
            gauss = jnp.exp(-4.0 * (away * away))
            env_k = wide_row(envelope, k)
            value = gauss * env_k
            total = total + value
            total_kind = total_kind + value * wide_row(kind, k)
            cols = slice(k * LANES, (k + 1) * LANES)
            if 2 <= b <= 9:
                bst[b, :, cols] = part_rows(value)
            if 3 <= b <= 8:
                value = gauss * (wide_row(slant, k) - 8.0 * away * env_k)
                bpr[b, :, cols] = value
                bps[b, :, cols] = part_rows(value)
        high, low = split(jnp.concatenate([total, total_kind], axis=0))
        sst[:, b * LANES : (b + 1) * LANES] = jnp.concatenate([high, low, high], axis=0).astype(BF16)

    for b in range(1, 11):
        pairs(b)

    for b in range(1, 11, 2):
        cols = slice(b * LANES, (b + 2) * LANES)
        value, steep = silu_parts(mm(l1[...], sst[:, cols]))
        sent = mm(l2[...], right_stack(value))
        for i in range(2):
            one = sent[:, i * LANES : (i + 1) * LANES]
            one = one + col[0] + col[1] * jnp.broadcast_to(xs[b + i, 3:4, :], (CHANNELS, LANES))
            sent_all[:, (b + i) * LANES : (b + i + 1) * LANES] = one
        slope[:, cols] = steep


def force_parts(weights, own_hot, side_hot, kept, dg, pulls, acc):
    l1, l2, l3, l5, l6, col = weights
    (widx, kinds, geo, bst, bps, bpr, sent_all, slope) = kept
    slot = lax.broadcasted_iota(jnp.int32, (SLOTS, LANES), 0)

    def spread(left, b, first, last):
        ws = reach(b, first, last)
        if b in SIDE_START:
            start = SIDE_START[b] + (ws[0] - reach(b, 3, 8)[0]) * LANES
            return ws, mm_nt(left, side_hot[start : start + len(ws) * LANES, :])
        return ws, mm_nt(left, own_hot[b - 4, ws[0] * LANES : (ws[-1] + 1) * LANES, :])

    started = set()

    def gather_and_return(b):
        index = widx[b]
        inner, part = index & (LANES - 1), index >> 7
        windows = [sent_all[:, (b - 1 + w) * LANES : (b + w) * LANES] for w in range(3)]
        got = []
        for k in range(SLOTS):
            lane = jnp.broadcast_to(inner[k : k + 1, :], (CHANNELS, LANES))
            which = jnp.broadcast_to(part[k : k + 1, :], (CHANNELS, LANES))
            pick = [jnp.take_along_axis(window, lane, axis=1) for window in windows]
            got.append(jnp.where(which == 0, pick[0], jnp.where(which == 1, pick[1], pick[2])))
        got = jnp.concatenate(got, axis=1)
        basis = bst[b]
        radial = mm(l3[...], jnp.concatenate([basis, basis], axis=0))
        message = jnp.zeros((CHANNELS, LANES), F32)
        for k in range(SLOTS):
            cols = slice(k * LANES, (k + 1) * LANES)
            message = message + radial[:, cols] * got[:, cols]
        _, steep = silu_parts(message)
        back = jnp.concatenate([col[3] * steep] * SLOTS, axis=1)
        ws, out = spread(pair_stack(radial * back), b, 3, 8)
        out = out[:CHANNELS] + out[CHANNELS:]
        for i, w in enumerate(ws):
            target = b - 1 + w
            piece = out[:, i * LANES : (i + 1) * LANES]
            where = slice(target * LANES, (target + 1) * LANES)
            if target in started:
                dg[:, where] += piece
            else:
                dg[:, where] = piece
                started.add(target)
        if 3 <= b <= 8:
            basis = bps[b]
            steepness = mm(l3[...], jnp.concatenate([basis, basis], axis=0))
            pull = got * back * steepness
            total = pull[0:8]
            for i in range(1, CHANNELS // 8):
                total = total + pull[8 * i : 8 * i + 8]
            pulls[b] = total

    for b in range(2, 10):
        gather_and_return(b)

    begun = set()

    def put(b, c, value):
        if (b, c) in begun:
            acc[b, c] += value
        else:
            acc[b, c] = value
            begun.add((b, c))

    def finish(b, sums):
        kind = kinds[b]
        rows = []
        for k in range(SLOTS):
            cols = slice(k * LANES, (k + 1) * LANES)
            weight = sums[0:8] + wide_row(kind, k) * sums[8:16]
            rows.append(jnp.sum(bpr[b, :, cols] * weight + pulls[b, :, cols], axis=0, keepdims=True))
        pull = jnp.concatenate(rows, axis=0) * geo[b, 3]
        pieces = []
        for c in range(3):
            value = pull * geo[b, c]
            if 4 <= b <= 7:
                put(b, c, -value)
            pieces.append(split(value))
        lines = []
        for h in range(2):
            for c in range(3):
                lines.append(jnp.concatenate([jnp.where(slot == k, pieces[c][h], 0.0) for k in range(SLOTS)], axis=1))
        ws, out = spread(jnp.concatenate(lines, axis=0).astype(BF16), b, 4, 7)
        for c in range(3):
            both = out[8 * c : 8 * c + 8] + out[24 + 8 * c : 32 + 8 * c]
            for i, w in enumerate(ws):
                put(b - 1 + w, c, both[:, i * LANES : (i + 1) * LANES])

    for b in range(3, 9, 2):
        cols = slice(b * LANES, (b + 2) * LANES)
        steep = mm(l5[...], right_stack(dg[:, cols]))
        steep = steep + jnp.concatenate([col[2], col[2]], axis=1)
        sums = mm(l6[...], right_stack(steep * slope[:, cols]))
        for i in range(2):
            finish(b + i, sums[:, i * LANES : (i + 1) * LANES])


def own_force(acc, c):
    return jnp.concatenate(
        [-jnp.sum(acc[4 + i, c], axis=0, keepdims=True) for i in range(SLAB_BLOCKS)], axis=1
    )


def fill_region(xs, packs, rows_of):
    for b in range(12):
        lanes = slice((b % 4) * LANES, (b % 4 + 1) * LANES)
        pack = packs[b // 4]
        xs[b, 0:3, :] = rows_of(b // 4)[:, lanes]
        xs[b, 3:4, :] = pack[ROW_KIND : ROW_KIND + 1, lanes]


def lane_total(x):
    x = x[:, 0:LANES] + x[:, LANES : 2 * LANES] + x[:, 2 * LANES : 3 * LANES] + x[:, 3 * LANES : 4 * LANES]
    return jnp.sum(x, axis=1, keepdims=True)


def dot3(a, b):
    return jnp.sum(a * b, axis=0, keepdims=True)


def kept_shapes():
    wide = 12 * LANES
    return [
        ((12, 8, LANES), jnp.int32),
        ((12, 8, LANES), F32),
        ((12, 4, 8, LANES), F32),
        ((12, 16, SLOTS * LANES), BF16),
        ((12, 16, SLOTS * LANES), BF16),
        ((12, 8, SLOTS * LANES), F32),
        ((CHANNELS, wide), F32),
        ((CHANNELS, wide), F32),
    ]


def forward_scratch():
    return [pltpu.VMEM((12, 8, LANES), F32), pltpu.VMEM((48, 12 * LANES), BF16)]


def back_scratch():
    return [
        pltpu.VMEM((CHANNELS, 12 * LANES), F32),
        pltpu.VMEM((12, 8, SLOTS * LANES), F32),
        pltpu.VMEM((12, 3, 8, LANES), F32),
    ]


def by_parity(sibling, across):
    even = jnp.full(sibling.shape, lax.axis_index("dom") % 2, jnp.int32) == 0
    return jnp.where(even, across, sibling), jnp.where(even, sibling, across)


def first_kernel(x_ref, sibling_ref, po_ref, across_ref, *rest):
    weights, (pl_ref, pr_ref, side_hot, copy_ref), kept, (xs, sst) = rest[:6], rest[6:10], rest[10:18], rest[18:]
    copy_ref[...] = x_ref[...]
    pl_ref[...], pr_ref[...] = by_parity(sibling_ref[...], across_ref[...])
    packs = [pl_ref, po_ref, pr_ref]
    mark_sides(packs, side_hot)
    fill_region(xs, packs, lambda s: packs[s][ROW_X : ROW_X + 3, :])
    forward_parts(packs, weights, xs, sst, kept)


def first_back_kernel(own_hot, side_hot, *rest):
    weights, kept, out_ref, scr = rest[:6], rest[6:14], rest[14], rest[15:]
    force_parts(weights, own_hot, side_hot, kept, *scr)
    for c in range(3):
        out_ref[c : c + 1, :] = own_force(scr[-1], c)


def rows_of(ref):
    return jnp.concatenate([ref[c] for c in range(3)], axis=0)


def block_row(*values):
    values = list(values) + [jnp.zeros((1, LANES), F32)] * (SLAB_BLOCKS - len(values))
    return jnp.concatenate(values, axis=1)


def blend_kernel(images, force_ref, po_ref, pair_ref, other_ref, out_ref, sums_ref):
    x = po_ref[ROW_X : ROW_X + 3, :]
    v = po_ref[ROW_V : ROW_V + 3, :]
    force = force_ref[...]
    here = lax.axis_index("img")
    pair, other = rows_of(pair_ref), rows_of(other_ref)
    even = here % 2 == 0
    before = jnp.where(here > 0, jnp.where(even, other, pair), 0.0)
    after = jnp.where(here < images - 1, jnp.where(even, pair, other), 0.0)
    tangent = after - before
    plus = after - x
    minus = x - before
    sums = jnp.concatenate(
        [
            dot3(force, tangent),
            dot3(force, force),
            dot3(tangent, tangent),
            dot3(plus, plus),
            dot3(minus, minus),
            dot3(v, v),
            jnp.zeros((2, x.shape[1]), F32),
        ],
        axis=0,
    )
    sums = jnp.broadcast_to(lane_total(sums), (8, LANES))
    sums_ref[...] = sums
    out_ref[0:3, :] = force
    out_ref[3:6, :] = tangent
    out_ref[6:7, :] = block_row(*[sums[i : i + 1] for i in range(4)])
    out_ref[7:8, :] = block_row(sums[4:5], sums[5:6])


def step_numbers(ft, ff, tt, pp, mn, vv, dt, alpha, flagged, climbing, inside):
    root = jnp.sqrt(tt + TINY_VALUE)
    along = ft / root
    spring = SPRING_CONSTANT * (jnp.sqrt(pp) - jnp.sqrt(mn))
    factor = jnp.where(climbing, -2.0 * along, spring - along)
    band = jnp.maximum(ff + 2.0 * factor * along + factor * factor * (tt / (tt + TINY_VALUE)), 0.0)
    new_dt = jnp.where(flagged, 0.5 * dt, jnp.minimum(1.1 * dt, STEP_LIMIT))
    pull = jnp.where(flagged, 0.0, alpha * jnp.sqrt(vv / (band + TINY_VALUE))) + new_dt
    keep = jnp.where(flagged, 0.0, 1.0 - alpha)
    new_alpha = jnp.where(flagged, ALPHA_START, 0.99 * alpha)
    keep = jnp.where(inside, keep, 0.0)
    pull = jnp.where(inside, pull, 0.0)
    return (
        jnp.where(inside, along, 0.0),
        jnp.where(inside, spring, 0.0),
        keep,
        pull,
        pull * factor / root,
        new_dt,
        new_alpha,
    )


def add_kernel(a_ref, b_ref, out_ref):
    out_ref[...] = a_ref[...] + b_ref[...]


def join_kernel(a_ref, b_ref, out_ref):
    count = a_ref.shape[0]
    out_ref[0:count] = a_ref[...]
    out_ref[count : 2 * count] = b_ref[...]


def second_kernel(images, domains, dt_ref, flag_ref, climb_ref, pl_ref, po_ref, pr_ref, own_ref, near_ref, far_ref, *rest):
    count = 2 if domains == 4 else 1
    parts, rest = rest[:count], rest[count:]
    (own_hot, side_hot), weights, (out_ref, record_ref), scr = rest[:2], rest[2:8], rest[8:10], rest[10:]
    packs = [pl_ref, po_ref, pr_ref]
    here = lax.axis_index("img")
    sums = parts[0][...]
    if domains == 4:
        sums = sums + parts[1][...]
    got = [sums[i : i + 1, :] for i in range(6)]
    if domains == 4:
        for one in (near_ref, far_ref):
            for i in range(6):
                got[i] = got[i] + one[6 + i // 4 : 7 + i // 4, (i % 4) * LANES : (i % 4 + 1) * LANES]
    ft, ff, tt, pp, mn, vv = got
    beside = by_parity(near_ref[0:6, :], far_ref[0:6, :])
    shape = (1, LANES)
    along, spring, keep, pull, side, dt, alpha = step_numbers(
        ft,
        ff,
        tt,
        pp,
        mn,
        vv,
        jnp.full(shape, dt_ref[0], F32),
        jnp.full(shape, ALPHA_START, F32),
        jnp.full(shape, flag_ref[0, 0], jnp.int32) == 1,
        jnp.full(shape, here - climb_ref[0], jnp.int32) == 0,
        jnp.full(shape, jnp.where((here >= 1) & (here <= images - 2), 1, 0), jnp.int32) == 1,
    )
    messages = [beside[0], own_ref[0:6, :], beside[1]]

    def wide(s):
        return jnp.concatenate([s] * SLAB_BLOCKS, axis=1)

    speeds = [
        wide(keep) * p[ROW_V : ROW_V + 3, :] + wide(pull) * m[0:3, :] + wide(side) * m[3:6, :]
        for p, m in zip(packs, messages)
    ]
    moved = [p[ROW_X : ROW_X + 3, :] + wide(dt) * s for p, s in zip(packs, speeds)]
    xs, sst, kept = scr[0], scr[1], scr[2:10]
    fill_region(xs, packs, lambda s: moved[s])
    forward_parts(packs, weights, xs, sst, kept)
    force_parts(weights, own_hot, side_hot, kept, *scr[10:])
    for c in range(3):
        force = own_force(scr[-1], c)
        for i in range(SLAB_BLOCKS):
            lanes = slice(i * LANES, (i + 1) * LANES)
            row = 4 * c + i
            out_ref[0, row : row + 1, :] = speeds[1][c : c + 1, lanes]
            out_ref[0, 12 + row : 13 + row, :] = force[:, lanes]
            out_ref[0, 24 + row : 25 + row, :] = moved[1][c : c + 1, lanes]
    out_ref[0, 36:37, :] = dt
    out_ref[0, 37:38, :] = alpha
    out_ref[0, 38:40, :] = jnp.full((2, LANES), flag_ref[0, 1], jnp.int32).astype(F32)
    record_ref[0:1, :] = along
    record_ref[1:2, :] = spring
    record_ref[2:3, :] = jnp.full(shape, climb_ref[0], jnp.int32).astype(F32)


PRODUCTS = (
    [("f", "t"), ("f", "f"), ("t", "t"), ("p", "p"), ("d", "d"), ("v", "v")]
    + [("d", "v"), ("d", "f"), ("d", "t"), ("d", "V"), ("d", "F"), ("d", "T"), ("v", "f"), ("v", "t")]
    + [(a, b) for a in "vft" for b in "VFT"]
)


def gram_kernel(images, *refs):
    parts, (out_ref, state_ref, messages_ref) = refs[:-3], refs[-3:]
    rows = out_ref.shape[0]
    place = 0
    for part in parts:
        messages_ref[place : place + part.shape[0]] = part[...]
        place += part.shape[0]
    here = lax.axis_index("img")
    blank = [jnp.zeros((rows - images, LANES), F32)] if rows > images else []
    zero = jnp.zeros((1, LANES), F32)

    def gathered(row):
        return jnp.concatenate([messages_ref[here ^ i, row : row + 1, :] for i in range(images)] + blank, axis=0)

    def earlier(value):
        return jnp.concatenate([zero, value[0 : rows - 1]], axis=0)

    def later(value):
        return jnp.concatenate([value[1:images], zero] + blank, axis=0)

    number = lax.broadcasted_iota(jnp.int32, (rows, LANES), 0)
    held = number < images
    totals = [jnp.zeros((rows, LANES), F32) for _ in PRODUCTS]
    for row in range(3 * SLAB_BLOCKS):
        v, f, x = gathered(row), gathered(12 + row), gathered(24 + row)
        before = jnp.where(held, earlier(x), 0.0)
        after = later(x)
        t = after - before
        table = {"f": f, "v": v, "t": t, "p": after - x, "d": x - before}
        table["F"], table["V"], table["T"] = earlier(f), earlier(v), earlier(t)
        totals = [old + table[a] * table[b] for old, (a, b) in zip(totals, PRODUCTS)]
        state_ref[row : row + 1, :] = jnp.sum(jnp.where(number == here, t, 0.0), axis=0, keepdims=True)
    lane = lax.broadcasted_iota(jnp.int32, (rows, LANES), 1)
    result = jnp.zeros((rows, LANES), F32)
    for q, one in enumerate(totals):
        one = jnp.broadcast_to(jnp.sum(one, axis=1, keepdims=True), (rows, LANES))
        result = jnp.where(lane == q, one, result)
    out_ref[...] = result
    for i in range(3):
        state_ref[16 + rows * i : 16 + rows * (i + 1), :] = gathered(36 + i)


def final_kernel(images, atoms, own_ref, record_ref, state_ref, *rest):
    parts, (x_ref, v_ref, band_ref, path_ref) = rest[:-4], rest[-4:]
    rows = parts[0].shape[0]
    here = lax.axis_index("img")
    sums = parts[0][...]
    for one in parts[1:]:
        sums = sums + one[...]
    got = {
        pair: jnp.broadcast_to(sums[:, q : q + 1], (rows, LANES)) for q, pair in enumerate(PRODUCTS)
    }
    number = lax.broadcasted_iota(jnp.int32, (rows, LANES), 0)
    inside = (number >= 1) & (number <= images - 2)
    climb = jnp.broadcast_to(record_ref[2:3, :], (rows, LANES))
    dt0, alpha0, flag = (state_ref[16 + rows * i : 16 + rows * (i + 1), :] for i in range(3))
    along, spring, keep, pull, side, dt, _ = step_numbers(
        got["f", "t"],
        got["f", "f"],
        got["t", "t"],
        got["p", "p"],
        got["d", "d"],
        got["v", "v"],
        dt0,
        alpha0,
        flag == 1.0,
        number.astype(F32) == climb,
        inside,
    )

    def shifted(value):
        return jnp.concatenate([jnp.zeros((1, LANES), F32), value[0 : rows - 1]], axis=0)

    now = {"v": dt * keep, "f": dt * pull, "t": dt * side}
    old = {a.upper(): shifted(value) for a, value in now.items()}
    mine = now["v"] * now["v"] * got["v", "v"] + now["f"] * now["f"] * got["f", "f"]
    mine = mine + now["t"] * now["t"] * got["t", "t"]
    cross = now["v"] * now["f"] * got["v", "f"] + now["v"] * now["t"] * got["v", "t"]
    mine = mine + 2.0 * (cross + now["f"] * now["t"] * got["f", "t"])
    both = jnp.zeros((rows, LANES), F32)
    for a in "vft":
        both = both + now[a] * got["d", a]
    for b in "VFT":
        both = both - old[b] * got["d", b]
    for a in "vft":
        for b in "VFT":
            both = both - now[a] * old[b] * got[a, b]
    squared = got["d", "d"] + mine + shifted(mine) + 2.0 * both
    segment = jnp.sqrt(jnp.maximum(squared, 0.0) * (1.0 / (3.0 * atoms)))
    path = jnp.sum(jnp.where(number <= here, segment, 0.0), axis=0, keepdims=True)
    path_ref[...] = path[:, 0:1]
    keep, pull, side, dt, along, spring = (
        jnp.sum(jnp.where(number == here, value, 0.0), axis=0, keepdims=True)
        for value in (keep, pull, side, dt, along, spring)
    )

    for c in range(3):
        speeds, places = [], []
        for i in range(SLAB_BLOCKS):
            row = 4 * c + i
            speed = keep * own_ref[0, row : row + 1, :] + pull * own_ref[0, 12 + row : 13 + row, :]
            speed = speed + side * state_ref[row : row + 1, :]
            speeds.append(speed)
            places.append(own_ref[0, 24 + row : 25 + row, :] + dt * speed)
        v_ref[c] = jnp.concatenate(speeds, axis=1)
        x_ref[c] = jnp.concatenate(places, axis=1)
    band_ref[0] = jnp.concatenate([record_ref[0:1, 0:1], record_ref[1:2, 0:1]], axis=1)
    band_ref[1] = jnp.concatenate([along[:, 0:1], spring[:, 0:1]], axis=1)


VMEM_SPEC = pl.BlockSpec(memory_space=pltpu.VMEM)
SMEM_SPEC = pl.BlockSpec(memory_space=pltpu.SMEM)
HBM_SPEC = pl.BlockSpec(memory_space=pltpu.HBM)


def call(body, outs, scalars, arrays, scratch_shapes=(), flops=0, spec=VMEM_SPEC, vmem=24):
    return pl.pallas_call(
        body,
        out_shape=outs,
        in_specs=[SMEM_SPEC] * len(scalars) + [spec] * len(arrays),
        out_specs=jax.tree.map(lambda _: VMEM_SPEC, outs),
        scratch_shapes=list(scratch_shapes),
        compiler_params=pltpu.CompilerParams(vmem_limit_bytes=vmem * 1024 * 1024),
        cost_estimate=pl.CostEstimate(flops=flops, bytes_accessed=1 << 18, transcendentals=0),
    )(*scalars, *arrays)


def swap(array, axis, partner):
    return lax.ppermute(array, axis, [(i, partner(i)) for i in range(lax.axis_size(axis))])


def exchanged(sums, axis):
    count = lax.axis_size(axis)
    if count == 4:
        return [sums] + [swap(sums, axis, lambda i, by=by: i ^ by) for by in (2, 3, 1)]
    distance = 1
    while distance < count:
        more = swap(sums, axis, lambda i, by=distance: i ^ by)
        sums = call(add_kernel, jax.ShapeDtypeStruct(sums.shape, F32), (), (sums, more))
        distance *= 2
    return [sums]


def collected(array, axis):
    count = lax.axis_size(axis)
    if count == 4:
        far = [swap(array, axis, lambda i, by=by: i ^ by) for by in (3, 2, 1)]
        return [array] + far[::-1]
    distance = 1
    while distance < count:
        more = swap(array, axis, lambda i, by=distance: i ^ by)
        shape = jax.ShapeDtypeStruct((2 * distance,) + array.shape[1:], F32)
        array = call(join_kernel, shape, (), (array, more))
        distance *= 2
    return [array]


def local(
    disp,
    veloc,
    time_step,
    reset_flags,
    climb,
    species,
    neighbours,
    counts,
    lattice,
    embed,
    radial_weight,
    mix_weight,
    update_weight,
    readout,
):
    atoms = disp.shape[2]
    images = lax.axis_size("img")
    domains = lax.axis_size("dom")
    assert disp.shape[0] == 1 and atoms == SLAB_BLOCKS * LANES and domains >= 4
    assert domains & (domains - 1) == 0 and images & (images - 1) == 0
    shape = jax.ShapeDtypeStruct
    x = jnp.transpose(disp, (1, 0, 2))
    v = jnp.transpose(veloc, (1, 0, 2))
    small = (x, v, species, neighbours, counts, embed, readout, radial_weight, mix_weight, update_weight)
    sent, pack = call(
        pack_kernel,
        (shape((PACK_ROWS, atoms), F32), shape((OWN_ROWS, atoms), F32)),
        (),
        (*small, jnp.transpose(lattice, (1, 0, 2))),
        [pltpu.VMEM(a.shape, a.dtype) for a in small] + [pltpu.SemaphoreType.DMA((16,))],
        spec=HBM_SPEC,
        vmem=63,
    )
    sibling = swap(sent, "dom", lambda i: i ^ 1)
    across = swap(sent, "dom", lambda i: (i + 2 * (i % 2) - 1) % domains)
    own_hot, *weights, x_copy = call(
        prepare_kernel,
        (
            shape((SLAB_BLOCKS, 3 * LANES, SLOTS * LANES), BF16),
            shape((CHANNELS, 48), BF16),
            shape((CHANNELS, 192), BF16),
            shape((CHANNELS, 32), BF16),
            shape((CHANNELS, 192), BF16),
            shape((16, 192), BF16),
            shape((4, CHANNELS, LANES), F32),
            shape(x.shape, F32),
        ),
        (),
        (pack,),
        flops=100000000,
    )
    pair = swap(x_copy, "img", lambda i: i ^ 1)
    left, right, side_hot, x_copy, *kept = call(
        first_kernel,
        (
            shape(sent.shape, F32),
            shape(sent.shape, F32),
            shape((SIDE_ROWS, SLOTS * LANES), BF16),
            shape(x.shape, F32),
            *[shape(*one) for one in kept_shapes()],
        ),
        (),
        (x_copy, sibling, pack, across, *weights),
        forward_scratch(),
        flops=1000000000,
    )
    other = swap(x_copy, "img", lambda i: i if i in (0, images - 1) else i + 2 * (i % 2) - 1)
    force = call(
        first_back_kernel,
        shape((3, atoms), F32),
        (),
        (own_hot, side_hot, *weights, *kept),
        back_scratch(),
        flops=1000000000,
    )
    message, sums = call(
        functools.partial(blend_kernel, images),
        (shape((8, atoms), F32), shape((8, LANES), F32)),
        (),
        (force, pack, pair, other),
    )
    far = swap(message, "dom", lambda i: (i + 2 * (i % 2) - 1) % domains)
    if domains == 4:
        parts = [sums, swap(sums, "dom", lambda i: i ^ 2)]
    else:
        parts = exchanged(sums, "dom")
    near = swap(message, "dom", lambda i: i ^ 1)
    state, record = call(
        functools.partial(second_kernel, images, domains),
        (shape((1, 40, LANES), F32), shape((3, LANES), F32)),
        (time_step, jnp.transpose(reset_flags), climb),
        (left, pack, right, message, near, far, *parts, own_hot, side_hot, *weights),
        forward_scratch() + [pltpu.VMEM(*one) for one in kept_shapes()] + back_scratch(),
        flops=1000000000,
    )
    rows = 8 * ((images + 7) // 8)
    sums, extra = call(
        functools.partial(gram_kernel, images),
        (shape((rows, LANES), F32), shape((16 + 3 * rows, LANES), F32)),
        (),
        collected(state, "img"),
        [pltpu.VMEM((images, 40, LANES), F32)],
    )
    new_x, new_v, records, path = call(
        functools.partial(final_kernel, images, atoms * domains),
        (shape(x.shape, F32), shape(x.shape, F32), shape((2, 1, 2), F32), shape((1, 1), F32)),
        (),
        (state, record, extra, *exchanged(sums, "dom")),
    )
    return (
        jnp.transpose(new_x, (1, 0, 2)),
        jnp.transpose(new_v, (1, 0, 2)),
        jnp.transpose(records, (0, 2, 1)),
        path.reshape(1),
    )


def solution(mesh):
    in_specs = (
        P(("group", "img"), None, "dom"),
        P(("group", "img"), None, "dom"),
        P(("group", "img")),
        P(None, ("group", "img")),
        P("group"),
        P(("group", "dom")),
        P(None, ("group", "dom")),
        P(("group", "dom")),
        P(None, None, ("group", "dom")),
        P(),
        P(),
        P(),
        P(),
        P(),
    )
    out_specs = (
        P(("group", "img"), None, "dom"),
        P(("group", "img"), None, "dom"),
        P(None, None, ("group", "img")),
        P(("group", "img")),
    )
    return jax.shard_map(local, mesh=mesh, in_specs=in_specs, out_specs=out_specs, check_vma=False)
```

```python
import functools
import math

import jax
import jax.numpy as jnp
from jax import lax
from jax.experimental import pallas as pl
from jax.experimental.pallas import tpu as pltpu
from jax.sharding import PartitionSpec as P

F32 = jnp.float32
BF16 = jnp.bfloat16
PRECISE = lax.Precision.HIGHEST
SPRING_CONSTANT = 0.5
ALPHA_START = 0.1
STEP_LIMIT = 0.3
TINY_VALUE = 1e-06
SOFTENING = 0.25
LANES = 128
SLOTS = 8
BASIS = 8
CHANNELS = 64
SLAB_BLOCKS = 4
ROW_X = 32
ROW_COUNT = 35
ROW_KIND = 36
ROW_V = 37
PACK_ROWS = 40
OWN_ROWS = PACK_ROWS + CHANNELS + BASIS
NT = (((1,), (1,)), ((), ()))


def split(x):
    high = x.astype(BF16).astype(F32)
    return high, x - high


def left_stack(w):
    high, low = split(w)
    return jnp.concatenate([high, high, low], axis=1)


def right_stack(x):
    high, low = split(x)
    high = high.astype(BF16)
    return jnp.concatenate([high, low.astype(BF16), high], axis=0)


def pair_stack(x):
    high, low = split(x)
    return jnp.concatenate([high.astype(BF16), low.astype(BF16)], axis=0)


def mm(a, b):
    return jnp.dot(a, b, preferred_element_type=F32)


def mm_nt(a, b):
    return lax.dot_general(a, b, NT, preferred_element_type=F32)


def pack_kernel(*refs):
    sources, (out_ref, own_ref), held, sems = refs[:11], refs[11:13], refs[13:23], refs[23]
    lattice = sources[10]
    pairs = list(zip(sources, held))
    for c in range(3):
        rows = pl.ds(8 + 8 * c, 8)
        pairs += [(lattice.at[c], out_ref.at[rows]), (lattice.at[c], own_ref.at[rows])]
    copies = [pltpu.make_async_copy(a, b, sems.at[i]) for i, (a, b) in enumerate(pairs)]
    for one in copies:
        one.start()
    for one in copies:
        one.wait()
    x, v, species, nbr, counts, embed, readout, radial, mix, update = held
    for ref in (out_ref, own_ref):
        ref[0:8, :] = nbr[...].astype(F32)
        for c in range(3):
            ref[ROW_X + c : ROW_X + c + 1, :] = x[c]
            ref[ROW_V + c : ROW_V + c + 1, :] = v[c]
        ref[ROW_COUNT : ROW_COUNT + 1, :] = counts[...].astype(F32).reshape(1, -1)
        ref[ROW_KIND : ROW_KIND + 1, :] = species[...].astype(F32).reshape(1, -1)
    top, low = PACK_ROWS, PACK_ROWS + CHANNELS
    for i, value in enumerate([mix[0], mix[1], update[0], update[1]]):
        own_ref[top:low, i * LANES : i * LANES + CHANNELS] = value
    for i, value in enumerate([radial[0], radial[1], embed[...], readout[...].reshape(1, CHANNELS)]):
        own_ref[low : low + value.shape[0], i * LANES : i * LANES + CHANNELS] = value


def prepare_kernel(po_ref, *rest):
    own_hot, l1_ref, l2_ref, l3_ref, l5_ref, l6_ref, col_ref, copy_ref = rest
    for b in range(SLAB_BLOCKS):
        mark(window_index(po_ref, b), [0, 1, 2], own_hot.at[b])
    for c in range(3):
        copy_ref[c] = po_ref[ROW_X + c : ROW_X + c + 1, :]

    def raw(first, count, i):
        return po_ref[first : first + count, i * LANES : i * LANES + CHANNELS]

    low = PACK_ROWS + CHANNELS
    mix_ref = [raw(PACK_ROWS, CHANNELS, i) for i in range(2)]
    update_ref = [raw(PACK_ROWS, CHANNELS, 2 + i) for i in range(2)]
    radial_ref = [raw(low, BASIS, i) for i in range(2)]
    embed_ref, readout = raw(low, 2, 2), raw(low, 1, 3)
    eye = (
        lax.broadcasted_iota(jnp.int32, (CHANNELS, CHANNELS), 0)
        == lax.broadcasted_iota(jnp.int32, (CHANNELS, CHANNELS), 1)
    ).astype(F32)

    def turned(x):
        return lax.dot_general(eye, x, NT, precision=PRECISE, preferred_element_type=F32)

    base0 = embed_ref[0:1, :]
    base1 = embed_ref[1:2, :] - base0
    rows = jnp.concatenate([base0, base1], axis=0)
    sent = jnp.dot(rows, mix_ref[0], precision=PRECISE, preferred_element_type=F32)
    scale = 1.0 / math.sqrt(SLOTS)
    first = jnp.concatenate([radial_ref[0] * sent[0:1], radial_ref[0] * sent[1:2]], axis=0) * scale
    second = radial_ref[1] * scale
    folded = jnp.dot(update_ref[0], mix_ref[1], precision=PRECISE, preferred_element_type=F32)
    mix_t = turned(mix_ref[1])
    l1_ref[...] = left_stack(turned(first)).astype(BF16)
    l2_ref[...] = left_stack(turned(folded)).astype(BF16)
    high, low = split(turned(second))
    l3_ref[...] = jnp.concatenate([high, high, low, jnp.zeros_like(high)], axis=1).astype(BF16)
    high, low = split(folded)
    l5_ref[...] = jnp.concatenate([high, high, high, high, low, low], axis=1).astype(BF16)
    l6_ref[...] = left_stack(first).astype(BF16)
    wide = (CHANNELS, LANES)
    col_ref[0] = jnp.broadcast_to(jnp.sum(mix_t * base0, axis=1, keepdims=True), wide)
    col_ref[1] = jnp.broadcast_to(jnp.sum(mix_t * base1, axis=1, keepdims=True), wide)
    col_ref[2] = jnp.broadcast_to(jnp.sum(update_ref[0] * readout, axis=1, keepdims=True), wide)
    col_ref[3] = jnp.broadcast_to(jnp.sum(update_ref[1] * readout, axis=1, keepdims=True), wide)


def sin_cos(t):
    q = t * t
    s = -1.0 / 39916800.0
    for c in (1.0 / 362880.0, -1.0 / 5040.0, 1.0 / 120.0, -1.0 / 6.0, 1.0):
        s = s * q + c
    k = 1.0 / 479001600.0
    for c in (-1.0 / 3628800.0, 1.0 / 40320.0, -1.0 / 720.0, 1.0 / 24.0, -0.5, 1.0):
        k = k * q + c
    return s * t, k


def wide_row(x, row):
    return jnp.broadcast_to(x[row : row + 1, :], (8, x.shape[1]))


def silu_parts(m):
    sig = 1.0 / (1.0 + jnp.exp(-m))
    return m * sig, sig * (1.0 + m * (1.0 - sig))


def reach(b, first, last):
    return [w for w in range(3) if first <= b - 1 + w <= last]


SIDE_START = {2: 0, 3: LANES, 8: 3 * LANES, 9: 5 * LANES}
SIDE_ROWS = 6 * LANES


def mark(index, ws, target):
    count = len(ws) * LANES
    row_id = lax.broadcasted_iota(jnp.int32, (count, LANES), 0) + ws[0] * LANES
    for k in range(SLOTS):
        same = row_id == jnp.broadcast_to(index[k : k + 1, :], (count, LANES))
        target[:, k * LANES : (k + 1) * LANES] = jnp.where(same, 1.0, 0.0).astype(BF16)


def window_index(pack, b):
    lanes = slice((b % 4) * LANES, (b % 4 + 1) * LANES)
    return pack[0:8, lanes].astype(jnp.int32) - LANES * (b % 4)


def mark_sides(packs, side):
    for b, start in SIDE_START.items():
        ws = reach(b, 3, 8)
        mark(window_index(packs[b // 4], b), ws, side.at[start : start + len(ws) * LANES])


def forward_parts(packs, weights, xs, sst, kept):
    l1, l2, l3, l5, l6, col = weights
    (widx, kinds, geo, bst, bps, bpr, sent_all, slope) = kept
    centre = 2.0 + 0.5 * lax.broadcasted_iota(jnp.int32, (BASIS, LANES), 0).astype(F32)
    slot = lax.broadcasted_iota(jnp.int32, (SLOTS, LANES), 0)

    def part_rows(value):
        high, low = split(value)
        return jnp.concatenate([high, low], axis=0).astype(BF16)

    def pairs(b):
        pack = packs[b // 4]
        lanes = slice((b % 4) * LANES, (b % 4 + 1) * LANES)
        index = window_index(pack, b)
        widx[b] = index
        inner = index & (LANES - 1)
        part = index >> 7

        def taken(row):
            got = [
                jnp.take_along_axis(jnp.broadcast_to(xs[b - 1 + w, row : row + 1, :], (SLOTS, LANES)), inner, axis=1)
                for w in range(3)
            ]
            return jnp.where(part == 0, got[0], jnp.where(part == 1, got[1], got[2]))

        vec = [
            pack[8 + 8 * c : 16 + 8 * c, lanes] + taken(c) - jnp.broadcast_to(xs[b, c : c + 1, :], (SLOTS, LANES))
            for c in range(3)
        ]
        kind = taken(3)
        dist = jnp.sqrt(vec[0] * vec[0] + vec[1] * vec[1] + vec[2] * vec[2] + SOFTENING)
        live = (slot.astype(F32) < jnp.broadcast_to(pack[ROW_COUNT : ROW_COUNT + 1, lanes], (SLOTS, LANES))).astype(F32)
        turns = dist * (1.0 / 12.0)
        turns = turns - jnp.floor(turns + 0.5)
        sine, cosine = sin_cos(turns * math.pi)
        envelope = cosine * cosine * live
        slant = cosine * sine * live * (-math.pi / 6.0)
        if 3 <= b <= 8:
            kinds[b] = kind
            for c in range(3):
                geo[b, c] = vec[c]
            geo[b, 3] = 1.0 / dist
        total = jnp.zeros((BASIS, LANES), F32)
        total_kind = jnp.zeros((BASIS, LANES), F32)
        for k in range(SLOTS):
            away = wide_row(dist, k) - centre
            gauss = jnp.exp(-4.0 * (away * away))
            env_k = wide_row(envelope, k)
            value = gauss * env_k
            total = total + value
            total_kind = total_kind + value * wide_row(kind, k)
            cols = slice(k * LANES, (k + 1) * LANES)
            if 2 <= b <= 9:
                bst[b, :, cols] = part_rows(value)
            if 3 <= b <= 8:
                value = gauss * (wide_row(slant, k) - 8.0 * away * env_k)
                bpr[b, :, cols] = value
                bps[b, :, cols] = part_rows(value)
        high, low = split(jnp.concatenate([total, total_kind], axis=0))
        sst[:, b * LANES : (b + 1) * LANES] = jnp.concatenate([high, low, high], axis=0).astype(BF16)

    for b in range(1, 11):
        pairs(b)

    for b in range(1, 11, 2):
        cols = slice(b * LANES, (b + 2) * LANES)
        value, steep = silu_parts(mm(l1[...], sst[:, cols]))
        sent = mm(l2[...], right_stack(value))
        for i in range(2):
            one = sent[:, i * LANES : (i + 1) * LANES]
            one = one + col[0] + col[1] * jnp.broadcast_to(xs[b + i, 3:4, :], (CHANNELS, LANES))
            sent_all[:, (b + i) * LANES : (b + i + 1) * LANES] = one
        slope[:, cols] = steep


def force_parts(weights, own_hot, side_hot, kept, dg, pulls, met, acc):
    l1, l2, l3, l5, l6, col = weights
    (widx, kinds, geo, bst, bps, bpr, sent_all, slope) = kept
    slot = lax.broadcasted_iota(jnp.int32, (SLOTS, LANES), 0)

    def spread(left, b, first, last, held):
        ws = reach(b, first, last)
        if b in SIDE_START:
            start = SIDE_START[b] + (ws[0] - reach(b, 3, 8)[0]) * LANES
            picked = side_hot[start : start + len(ws) * LANES, :]
        else:
            picked = own_hot[b - 4, ws[0] * LANES : (ws[-1] + 1) * LANES, :]
        out = mm_nt(picked, left)
        for i, w in enumerate(ws):
            target = b - 1 + w
            piece = out[i * LANES : (i + 1) * LANES]
            rows = slice((target - first) * LANES, (target - first + 1) * LANES)
            if (id(held), target) in started:
                held[rows, :] += piece
            else:
                held[rows, :] = piece
                started.add((id(held), target))

    started = set()

    def gather_and_return(b):
        index = widx[b]
        inner, part = index & (LANES - 1), index >> 7
        windows = [sent_all[:, (b - 1 + w) * LANES : (b + w) * LANES] for w in range(3)]
        got = []
        for k in range(SLOTS):
            lane = jnp.broadcast_to(inner[k : k + 1, :], (CHANNELS, LANES))
            which = jnp.broadcast_to(part[k : k + 1, :], (CHANNELS, LANES))
            pick = [jnp.take_along_axis(window, lane, axis=1) for window in windows]
            got.append(jnp.where(which == 0, pick[0], jnp.where(which == 1, pick[1], pick[2])))
        got = jnp.concatenate(got, axis=1)
        basis = bst[b]
        radial = mm(l3[...], jnp.concatenate([basis, basis], axis=0))
        message = jnp.zeros((CHANNELS, LANES), F32)
        for k in range(SLOTS):
            cols = slice(k * LANES, (k + 1) * LANES)
            message = message + radial[:, cols] * got[:, cols]
        _, steep = silu_parts(message)
        back = jnp.concatenate([col[3] * steep] * SLOTS, axis=1)
        spread(pair_stack(radial * back), b, 3, 8, dg)
        if 3 <= b <= 8:
            basis = bps[b]
            steepness = mm(l3[...], jnp.concatenate([basis, basis], axis=0))
            pull = got * back * steepness
            total = pull[0:8]
            for i in range(1, CHANNELS // 8):
                total = total + pull[8 * i : 8 * i + 8]
            pulls[b] = total

    for b in range(2, 10):
        gather_and_return(b)

    def finish(b, sums):
        kind = kinds[b]
        rows = []
        for k in range(SLOTS):
            cols = slice(k * LANES, (k + 1) * LANES)
            weight = sums[0:8] + wide_row(kind, k) * sums[8:16]
            rows.append(jnp.sum(bpr[b, :, cols] * weight + pulls[b, :, cols], axis=0, keepdims=True))
        pull = jnp.concatenate(rows, axis=0) * geo[b, 3]
        pieces = []
        for c in range(3):
            value = pull * geo[b, c]
            if 4 <= b <= 7:
                acc[b - 4, c] = jnp.sum(value, axis=0, keepdims=True)
            pieces.append(split(value))
        lines = []
        for h in range(2):
            for c in range(3):
                lines.append(jnp.concatenate([jnp.where(slot == k, pieces[c][h], 0.0) for k in range(SLOTS)], axis=1))
        spread(jnp.concatenate(lines, axis=0).astype(BF16), b, 4, 7, met)

    for b in range(3, 9, 2):
        cols = slice(b * LANES, (b + 2) * LANES)
        high, low = split(dg[(b - 3) * LANES : (b - 1) * LANES, :])
        steep = mm_nt(l5[...], jnp.concatenate([high, low, high], axis=1).astype(BF16))
        steep = steep + jnp.concatenate([col[2], col[2]], axis=1)
        sums = mm(l6[...], right_stack(steep * slope[:, cols]))
        for i in range(2):
            finish(b + i, sums[:, i * LANES : (i + 1) * LANES])

    high, low = split(met[...])
    column = lax.broadcasted_iota(jnp.int32, (16, 6 * SLOTS), 1)
    column = jnp.where(column < 3 * SLOTS, column, column - 3 * SLOTS)
    first = SLOTS * lax.broadcasted_iota(jnp.int32, (16, 6 * SLOTS), 0)
    choose = jnp.where((column >= first) & (column < first + SLOTS), 1.0, 0.0).astype(BF16)
    back = mm_nt(choose, high.astype(BF16)) + mm_nt(choose, low.astype(BF16))
    away = [jnp.concatenate([acc[i, c] for i in range(SLAB_BLOCKS)], axis=1) for c in range(3)]
    return jnp.concatenate(away, axis=0) - back[0:3]


def fill_region(xs, packs, rows_of):
    for b in range(12):
        lanes = slice((b % 4) * LANES, (b % 4 + 1) * LANES)
        pack = packs[b // 4]
        xs[b, 0:3, :] = rows_of(b // 4)[:, lanes]
        xs[b, 3:4, :] = pack[ROW_KIND : ROW_KIND + 1, lanes]


def lane_total(x):
    x = x[:, 0:LANES] + x[:, LANES : 2 * LANES] + x[:, 2 * LANES : 3 * LANES] + x[:, 3 * LANES : 4 * LANES]
    return jnp.sum(x, axis=1, keepdims=True)


def dot3(a, b):
    return jnp.sum(a * b, axis=0, keepdims=True)


def kept_shapes():
    wide = 12 * LANES
    return [
        ((12, 8, LANES), jnp.int32),
        ((12, 8, LANES), F32),
        ((12, 4, 8, LANES), F32),
        ((12, 16, SLOTS * LANES), BF16),
        ((12, 16, SLOTS * LANES), BF16),
        ((12, 8, SLOTS * LANES), F32),
        ((CHANNELS, wide), F32),
        ((CHANNELS, wide), F32),
    ]


def forward_scratch():
    return [pltpu.VMEM((12, 8, LANES), F32), pltpu.VMEM((48, 12 * LANES), BF16)]


def back_scratch():
    return [
        pltpu.VMEM((6 * LANES, 2 * CHANNELS), F32),
        pltpu.VMEM((12, 8, SLOTS * LANES), F32),
        pltpu.VMEM((SLAB_BLOCKS * LANES, 6 * SLOTS), F32),
        pltpu.VMEM((SLAB_BLOCKS, 3, 1, LANES), F32),
    ]


def by_parity(sibling, across):
    even = jnp.full(sibling.shape, lax.axis_index("dom") % 2, jnp.int32) == 0
    return jnp.where(even, across, sibling), jnp.where(even, sibling, across)


def first_kernel(x_ref, sibling_ref, po_ref, across_ref, *rest):
    weights, (pl_ref, pr_ref, side_hot, copy_ref), kept, (xs, sst) = rest[:6], rest[6:10], rest[10:18], rest[18:]
    copy_ref[...] = x_ref[...]
    pl_ref[...], pr_ref[...] = by_parity(sibling_ref[...], across_ref[...])
    packs = [pl_ref, po_ref, pr_ref]
    mark_sides(packs, side_hot)
    fill_region(xs, packs, lambda s: packs[s][ROW_X : ROW_X + 3, :])
    forward_parts(packs, weights, xs, sst, kept)


def first_back_kernel(own_hot, side_hot, *rest):
    weights, kept, out_ref, scr = rest[:6], rest[6:14], rest[14], rest[15:]
    out_ref[...] = force_parts(weights, own_hot, side_hot, kept, *scr)


def rows_of(ref):
    return jnp.concatenate([ref[c] for c in range(3)], axis=0)


def block_row(*values):
    values = list(values) + [jnp.zeros((1, LANES), F32)] * (SLAB_BLOCKS - len(values))
    return jnp.concatenate(values, axis=1)


def blend_kernel(images, force_ref, po_ref, before_ref, after_ref, out_ref, sums_ref):
    x = po_ref[ROW_X : ROW_X + 3, :]
    v = po_ref[ROW_V : ROW_V + 3, :]
    force = force_ref[...]
    here = lax.axis_index("img")
    before = jnp.where(here > 0, rows_of(before_ref), 0.0)
    after = jnp.where(here < images - 1, rows_of(after_ref), 0.0)
    tangent = after - before
    plus = after - x
    minus = x - before
    sums = jnp.concatenate(
        [
            dot3(force, tangent),
            dot3(force, force),
            dot3(tangent, tangent),
            dot3(plus, plus),
            dot3(minus, minus),
            dot3(v, v),
            jnp.zeros((2, x.shape[1]), F32),
        ],
        axis=0,
    )
    sums = jnp.broadcast_to(lane_total(sums), (8, LANES))
    sums_ref[...] = sums
    out_ref[0:3, :] = force
    out_ref[3:6, :] = tangent
    out_ref[6:7, :] = block_row(*[sums[i : i + 1] for i in range(4)])
    out_ref[7:8, :] = block_row(sums[4:5], sums[5:6])


def step_numbers(ft, ff, tt, pp, mn, vv, dt, alpha, flagged, climbing, inside):
    root = jnp.sqrt(tt + TINY_VALUE)
    along = ft / root
    spring = SPRING_CONSTANT * (jnp.sqrt(pp) - jnp.sqrt(mn))
    factor = jnp.where(climbing, -2.0 * along, spring - along)
    band = jnp.maximum(ff + 2.0 * factor * along + factor * factor * (tt / (tt + TINY_VALUE)), 0.0)
    new_dt = jnp.where(flagged, 0.5 * dt, jnp.minimum(1.1 * dt, STEP_LIMIT))
    pull = jnp.where(flagged, 0.0, alpha * jnp.sqrt(vv / (band + TINY_VALUE))) + new_dt
    keep = jnp.where(flagged, 0.0, 1.0 - alpha)
    new_alpha = jnp.where(flagged, ALPHA_START, 0.99 * alpha)
    keep = jnp.where(inside, keep, 0.0)
    pull = jnp.where(inside, pull, 0.0)
    return (
        jnp.where(inside, along, 0.0),
        jnp.where(inside, spring, 0.0),
        keep,
        pull,
        pull * factor / root,
        new_dt,
        new_alpha,
    )


def add_kernel(a_ref, b_ref, out_ref):
    out_ref[...] = a_ref[...] + b_ref[...]


def join_kernel(a_ref, b_ref, out_ref):
    count = a_ref.shape[0]
    out_ref[0:count] = a_ref[...]
    out_ref[count : 2 * count] = b_ref[...]


def number_kernel(dt_ref, flag_ref, climb_ref, out_ref):
    flags = [flag_ref[0, s].astype(F32) for s in range(flag_ref.shape[1])]
    for i, value in enumerate([dt_ref[0], climb_ref[0].astype(F32)] + flags):
        out_ref[i : i + 1, :] = jnp.full((1, LANES), value, F32)


def second_kernel(images, domains, number_ref, pl_ref, po_ref, pr_ref, own_ref, near_ref, far_ref, *rest):
    count = 2 if domains == 4 else 1
    parts, rest = rest[:count], rest[count:]
    (own_hot, side_hot), weights, (out_ref, record_ref), scr = rest[:2], rest[2:8], rest[8:10], rest[10:]
    packs = [pl_ref, po_ref, pr_ref]
    here = lax.axis_index("img")
    sums = parts[0][...]
    if domains == 4:
        sums = sums + parts[1][...]
    got = [sums[i : i + 1, :] for i in range(6)]
    if domains == 4:
        for one in (near_ref, far_ref):
            for i in range(6):
                got[i] = got[i] + one[6 + i // 4 : 7 + i // 4, (i % 4) * LANES : (i % 4 + 1) * LANES]
    ft, ff, tt, pp, mn, vv = got
    beside = by_parity(near_ref[0:6, :], far_ref[0:6, :])
    shape = (1, LANES)
    along, spring, keep, pull, side, dt, alpha = step_numbers(
        ft,
        ff,
        tt,
        pp,
        mn,
        vv,
        number_ref[0:1, :],
        jnp.full(shape, ALPHA_START, F32),
        number_ref[2:3, :] == 1.0,
        number_ref[1:2, :] == jnp.full(shape, here, jnp.int32).astype(F32),
        jnp.full(shape, jnp.where((here >= 1) & (here <= images - 2), 1, 0), jnp.int32) == 1,
    )
    messages = [beside[0], own_ref[0:6, :], beside[1]]

    def wide(s):
        return jnp.concatenate([s] * SLAB_BLOCKS, axis=1)

    speeds = [
        wide(keep) * p[ROW_V : ROW_V + 3, :] + wide(pull) * m[0:3, :] + wide(side) * m[3:6, :]
        for p, m in zip(packs, messages)
    ]
    moved = [p[ROW_X : ROW_X + 3, :] + wide(dt) * s for p, s in zip(packs, speeds)]
    xs, sst, kept = scr[0], scr[1], scr[2:10]
    fill_region(xs, packs, lambda s: moved[s])
    forward_parts(packs, weights, xs, sst, kept)
    force = force_parts(weights, own_hot, side_hot, kept, *scr[10:])
    for c in range(3):
        for i in range(SLAB_BLOCKS):
            lanes = slice(i * LANES, (i + 1) * LANES)
            row = 4 * c + i
            out_ref[0, row : row + 1, :] = speeds[1][c : c + 1, lanes]
            out_ref[0, 12 + row : 13 + row, :] = force[c : c + 1, lanes]
            out_ref[0, 24 + row : 25 + row, :] = moved[1][c : c + 1, lanes]
    out_ref[0, 36:37, :] = dt
    out_ref[0, 37:38, :] = alpha
    out_ref[0, 38:40, :] = jnp.broadcast_to(number_ref[3:4, :], (2, LANES))
    record_ref[0:1, :] = along
    record_ref[1:2, :] = spring
    record_ref[2:3, :] = number_ref[1:2, :]


PRODUCTS = (
    [("f", "t"), ("f", "f"), ("t", "t"), ("p", "p"), ("d", "d"), ("v", "v")]
    + [("d", "v"), ("d", "f"), ("d", "t"), ("d", "V"), ("d", "F"), ("d", "T"), ("v", "f"), ("v", "t")]
    + [(a, b) for a in "vft" for b in "VFT"]
)


def gram_kernel(images, *refs):
    parts, (out_ref, state_ref, messages_ref) = refs[:-3], refs[-3:]
    rows = out_ref.shape[0]
    place = 0
    for part in parts:
        messages_ref[place : place + part.shape[0]] = part[...]
        place += part.shape[0]
    here = lax.axis_index("img")
    blank = [jnp.zeros((rows - images, LANES), F32)] if rows > images else []
    zero = jnp.zeros((1, LANES), F32)

    def gathered(row):
        return jnp.concatenate([messages_ref[here ^ i, row : row + 1, :] for i in range(images)] + blank, axis=0)

    def earlier(value):
        return jnp.concatenate([zero, value[0 : rows - 1]], axis=0)

    def later(value):
        return jnp.concatenate([value[1:images], zero] + blank, axis=0)

    number = lax.broadcasted_iota(jnp.int32, (rows, LANES), 0)
    held = number < images
    totals = [jnp.zeros((rows, LANES), F32) for _ in PRODUCTS]
    for row in range(3 * SLAB_BLOCKS):
        v, f, x = gathered(row), gathered(12 + row), gathered(24 + row)
        before = jnp.where(held, earlier(x), 0.0)
        after = later(x)
        t = after - before
        table = {"f": f, "v": v, "t": t, "p": after - x, "d": x - before}
        table["F"], table["V"], table["T"] = earlier(f), earlier(v), earlier(t)
        totals = [old + table[a] * table[b] for old, (a, b) in zip(totals, PRODUCTS)]
        state_ref[row : row + 1, :] = jnp.sum(jnp.where(number == here, t, 0.0), axis=0, keepdims=True)
    lane = lax.broadcasted_iota(jnp.int32, (rows, LANES), 1)
    result = jnp.zeros((rows, LANES), F32)
    for q, one in enumerate(totals):
        one = jnp.broadcast_to(jnp.sum(one, axis=1, keepdims=True), (rows, LANES))
        result = jnp.where(lane == q, one, result)
    out_ref[...] = result
    for i in range(3):
        state_ref[16 + rows * i : 16 + rows * (i + 1), :] = gathered(36 + i)


def final_kernel(images, atoms, own_ref, record_ref, state_ref, *rest):
    parts, (x_ref, v_ref, band_ref, path_ref) = rest[:-4], rest[-4:]
    rows = parts[0].shape[0]
    here = lax.axis_index("img")
    sums = parts[0][...]
    for one in parts[1:]:
        sums = sums + one[...]
    got = {
        pair: jnp.broadcast_to(sums[:, q : q + 1], (rows, LANES)) for q, pair in enumerate(PRODUCTS)
    }
    number = lax.broadcasted_iota(jnp.int32, (rows, LANES), 0)
    inside = (number >= 1) & (number <= images - 2)
    climb = jnp.broadcast_to(record_ref[2:3, :], (rows, LANES))
    dt0, alpha0, flag = (state_ref[16 + rows * i : 16 + rows * (i + 1), :] for i in range(3))
    along, spring, keep, pull, side, dt, _ = step_numbers(
        got["f", "t"],
        got["f", "f"],
        got["t", "t"],
        got["p", "p"],
        got["d", "d"],
        got["v", "v"],
        dt0,
        alpha0,
        flag == 1.0,
        number.astype(F32) == climb,
        inside,
    )

    def shifted(value):
        return jnp.concatenate([jnp.zeros((1, LANES), F32), value[0 : rows - 1]], axis=0)

    now = {"v": dt * keep, "f": dt * pull, "t": dt * side}
    old = {a.upper(): shifted(value) for a, value in now.items()}
    mine = now["v"] * now["v"] * got["v", "v"] + now["f"] * now["f"] * got["f", "f"]
    mine = mine + now["t"] * now["t"] * got["t", "t"]
    cross = now["v"] * now["f"] * got["v", "f"] + now["v"] * now["t"] * got["v", "t"]
    mine = mine + 2.0 * (cross + now["f"] * now["t"] * got["f", "t"])
    both = jnp.zeros((rows, LANES), F32)
    for a in "vft":
        both = both + now[a] * got["d", a]
    for b in "VFT":
        both = both - old[b] * got["d", b]
    for a in "vft":
        for b in "VFT":
            both = both - now[a] * old[b] * got[a, b]
    squared = got["d", "d"] + mine + shifted(mine) + 2.0 * both
    segment = jnp.sqrt(jnp.maximum(squared, 0.0) * (1.0 / (3.0 * atoms)))
    path = jnp.sum(jnp.where(number <= here, segment, 0.0), axis=0, keepdims=True)
    path_ref[...] = path[:, 0:1]
    keep, pull, side, dt, along, spring = (
        jnp.sum(jnp.where(number == here, value, 0.0), axis=0, keepdims=True)
        for value in (keep, pull, side, dt, along, spring)
    )

    for c in range(3):
        speeds, places = [], []
        for i in range(SLAB_BLOCKS):
            row = 4 * c + i
            speed = keep * own_ref[0, row : row + 1, :] + pull * own_ref[0, 12 + row : 13 + row, :]
            speed = speed + side * state_ref[row : row + 1, :]
            speeds.append(speed)
            places.append(own_ref[0, 24 + row : 25 + row, :] + dt * speed)
        v_ref[c] = jnp.concatenate(speeds, axis=1)
        x_ref[c] = jnp.concatenate(places, axis=1)
    band_ref[0] = jnp.concatenate([record_ref[0:1, 0:1], record_ref[1:2, 0:1]], axis=1)
    band_ref[1] = jnp.concatenate([along[:, 0:1], spring[:, 0:1]], axis=1)


VMEM_SPEC = pl.BlockSpec(memory_space=pltpu.VMEM)
SMEM_SPEC = pl.BlockSpec(memory_space=pltpu.SMEM)
HBM_SPEC = pl.BlockSpec(memory_space=pltpu.HBM)


def call(body, outs, scalars, arrays, scratch_shapes=(), flops=0, spec=VMEM_SPEC, vmem=24):
    return pl.pallas_call(
        body,
        out_shape=outs,
        in_specs=[SMEM_SPEC] * len(scalars) + [spec] * len(arrays),
        out_specs=jax.tree.map(lambda _: VMEM_SPEC, outs),
        scratch_shapes=list(scratch_shapes),
        compiler_params=pltpu.CompilerParams(vmem_limit_bytes=vmem * 1024 * 1024),
        cost_estimate=pl.CostEstimate(flops=flops, bytes_accessed=1 << 18, transcendentals=0),
    )(*scalars, *arrays)


def swap(array, axis, partner):
    return lax.ppermute(array, axis, [(i, partner(i)) for i in range(lax.axis_size(axis))])


def exchanged(sums, axis):
    count = lax.axis_size(axis)
    if count == 4:
        return [sums] + [swap(sums, axis, lambda i, by=by: i ^ by) for by in (2, 3, 1)]
    distance = 1
    while distance < count:
        more = swap(sums, axis, lambda i, by=distance: i ^ by)
        sums = call(add_kernel, jax.ShapeDtypeStruct(sums.shape, F32), (), (sums, more))
        distance *= 2
    return [sums]


def collected(array, axis):
    count = lax.axis_size(axis)
    if count == 4:
        far = [swap(array, axis, lambda i, by=by: i ^ by) for by in (3, 2, 1)]
        return [array] + far[::-1]
    distance = 1
    while distance < count:
        more = swap(array, axis, lambda i, by=distance: i ^ by)
        shape = jax.ShapeDtypeStruct((2 * distance,) + array.shape[1:], F32)
        array = call(join_kernel, shape, (), (array, more))
        distance *= 2
    return [array]


def local(
    disp,
    veloc,
    time_step,
    reset_flags,
    climb,
    species,
    neighbours,
    counts,
    lattice,
    embed,
    radial_weight,
    mix_weight,
    update_weight,
    readout,
):
    atoms = disp.shape[2]
    images = lax.axis_size("img")
    domains = lax.axis_size("dom")
    assert disp.shape[0] == 1 and atoms == SLAB_BLOCKS * LANES and domains >= 4
    assert domains & (domains - 1) == 0 and images & (images - 1) == 0
    shape = jax.ShapeDtypeStruct
    x = jnp.transpose(disp, (1, 0, 2))
    v = jnp.transpose(veloc, (1, 0, 2))
    small = (x, v, species, neighbours, counts, embed, readout, radial_weight, mix_weight, update_weight)
    sent, pack = call(
        pack_kernel,
        (shape((PACK_ROWS, atoms), F32), shape((OWN_ROWS, atoms), F32)),
        (),
        (*small, jnp.transpose(lattice, (1, 0, 2))),
        [pltpu.VMEM(a.shape, a.dtype) for a in small] + [pltpu.SemaphoreType.DMA((16,))],
        spec=HBM_SPEC,
        vmem=63,
    )
    sibling = swap(sent, "dom", lambda i: i ^ 1)
    across = swap(sent, "dom", lambda i: (i + 2 * (i % 2) - 1) % domains)
    own_hot, *weights, x_copy = call(
        prepare_kernel,
        (
            shape((SLAB_BLOCKS, 3 * LANES, SLOTS * LANES), BF16),
            shape((CHANNELS, 48), BF16),
            shape((CHANNELS, 192), BF16),
            shape((CHANNELS, 32), BF16),
            shape((CHANNELS, 3 * LANES), BF16),
            shape((16, 192), BF16),
            shape((4, CHANNELS, LANES), F32),
            shape(x.shape, F32),
        ),
        (),
        (pack,),
        flops=100000000,
    )
    before = swap(x_copy, "img", lambda i: (i + 1) % images)
    left, right, side_hot, x_copy, *kept = call(
        first_kernel,
        (
            shape(sent.shape, F32),
            shape(sent.shape, F32),
            shape((SIDE_ROWS, SLOTS * LANES), BF16),
            shape(x.shape, F32),
            *[shape(*one) for one in kept_shapes()],
        ),
        (),
        (x_copy, sibling, pack, across, *weights),
        forward_scratch(),
        flops=1000000000,
    )
    after = swap(x_copy, "img", lambda i: (i - 1) % images)
    force = call(
        first_back_kernel,
        shape((3, atoms), F32),
        (),
        (own_hot, side_hot, *weights, *kept),
        back_scratch(),
        flops=1000000000,
    )
    message, sums = call(
        functools.partial(blend_kernel, images),
        (shape((8, atoms), F32), shape((8, LANES), F32)),
        (),
        (force, pack, before, after),
    )
    far = swap(message, "dom", lambda i: (i + 2 * (i % 2) - 1) % domains)
    if domains == 4:
        parts = [sums, swap(sums, "dom", lambda i: i ^ 2)]
    else:
        parts = exchanged(sums, "dom")
    near = swap(message, "dom", lambda i: i ^ 1)
    numbers = call(number_kernel, shape((8, LANES), F32), (time_step, jnp.transpose(reset_flags), climb), ())
    state, record = call(
        functools.partial(second_kernel, images, domains),
        (shape((1, 40, LANES), F32), shape((3, LANES), F32)),
        (),
        (numbers, left, pack, right, message, near, far, *parts, own_hot, side_hot, *weights),
        forward_scratch() + [pltpu.VMEM(*one) for one in kept_shapes()] + back_scratch(),
        flops=1000000000,
    )
    rows = 8 * ((images + 7) // 8)
    sums, extra = call(
        functools.partial(gram_kernel, images),
        (shape((rows, LANES), F32), shape((16 + 3 * rows, LANES), F32)),
        (),
        collected(state, "img"),
        [pltpu.VMEM((images, 40, LANES), F32)],
    )
    new_x, new_v, records, path = call(
        functools.partial(final_kernel, images, atoms * domains),
        (shape(x.shape, F32), shape(x.shape, F32), shape((2, 1, 2), F32), shape((1, 1), F32)),
        (),
        (state, record, extra, *exchanged(sums, "dom")),
    )
    return (
        jnp.transpose(new_x, (1, 0, 2)),
        jnp.transpose(new_v, (1, 0, 2)),
        jnp.transpose(records, (0, 2, 1)),
        path.reshape(1),
    )


def solution(mesh):
    in_specs = (
        P(("group", "img"), None, "dom"),
        P(("group", "img"), None, "dom"),
        P(("group", "img")),
        P(None, ("group", "img")),
        P("group"),
        P(("group", "dom")),
        P(None, ("group", "dom")),
        P(("group", "dom")),
        P(None, None, ("group", "dom")),
        P(),
        P(),
        P(),
        P(),
        P(),
    )
    out_specs = (
        P(("group", "img"), None, "dom"),
        P(("group", "img"), None, "dom"),
        P(None, None, ("group", "img")),
        P(("group", "img")),
    )
    return jax.shard_map(local, mesh=mesh, in_specs=in_specs, out_specs=out_specs, check_vma=False)
```

```python
import functools
import math

import jax
import jax.numpy as jnp
from jax import lax
from jax.experimental import pallas as pl
from jax.experimental.pallas import tpu as pltpu
from jax.sharding import PartitionSpec as P

F32 = jnp.float32
BF16 = jnp.bfloat16
PRECISE = lax.Precision.HIGHEST
SPRING_CONSTANT = 0.5
ALPHA_START = 0.1
STEP_LIMIT = 0.3
TINY_VALUE = 1e-06
SOFTENING = 0.25
LANES = 128
SLOTS = 8
BASIS = 8
CHANNELS = 64
SLAB_BLOCKS = 4
ROW_X = 32
ROW_COUNT = 35
ROW_KIND = 36
ROW_V = 37
PACK_ROWS = 40
OWN_ROWS = PACK_ROWS + CHANNELS + BASIS
NT = (((1,), (1,)), ((), ()))


def split(x):
    high = x.astype(BF16).astype(F32)
    return high, x - high


def left_stack(w):
    high, low = split(w)
    return jnp.concatenate([high, high, low], axis=1)


def right_stack(x):
    high, low = split(x)
    high = high.astype(BF16)
    return jnp.concatenate([high, low.astype(BF16), high], axis=0)


def pair_stack(x):
    high, low = split(x)
    return jnp.concatenate([high.astype(BF16), low.astype(BF16)], axis=0)


def mm(a, b):
    return jnp.dot(a, b, preferred_element_type=F32)


def mm_nt(a, b):
    return lax.dot_general(a, b, NT, preferred_element_type=F32)


def pack_kernel(*refs):
    sources, (out_ref, own_ref), held, sems = refs[:11], refs[11:13], refs[13:23], refs[23]
    lattice = sources[10]
    pairs = list(zip(sources, held))
    for c in range(3):
        rows = pl.ds(8 + 8 * c, 8)
        pairs += [(lattice.at[c], out_ref.at[rows]), (lattice.at[c], own_ref.at[rows])]
    copies = [pltpu.make_async_copy(a, b, sems.at[i]) for i, (a, b) in enumerate(pairs)]
    for one in copies:
        one.start()
    for one in copies:
        one.wait()
    x, v, species, nbr, counts, embed, readout, radial, mix, update = held
    for ref in (out_ref, own_ref):
        ref[0:8, :] = nbr[...].astype(F32)
        for c in range(3):
            ref[ROW_X + c : ROW_X + c + 1, :] = x[c]
            ref[ROW_V + c : ROW_V + c + 1, :] = v[c]
        ref[ROW_COUNT : ROW_COUNT + 1, :] = counts[...].astype(F32).reshape(1, -1)
        ref[ROW_KIND : ROW_KIND + 1, :] = species[...].astype(F32).reshape(1, -1)
    top, low = PACK_ROWS, PACK_ROWS + CHANNELS
    for i, value in enumerate([mix[0], mix[1], update[0], update[1]]):
        own_ref[top:low, i * LANES : i * LANES + CHANNELS] = value
    for i, value in enumerate([radial[0], radial[1], embed[...], readout[...].reshape(1, CHANNELS)]):
        own_ref[low : low + value.shape[0], i * LANES : i * LANES + CHANNELS] = value


def prepare_kernel(po_ref, *rest):
    own_hot, l1_ref, l2_ref, l3_ref, l5_ref, l6_ref, col_ref, copy_ref = rest
    for b in range(SLAB_BLOCKS):
        mark(window_index(po_ref, b), [0, 1, 2], own_hot.at[b])
    for c in range(3):
        copy_ref[c] = po_ref[ROW_X + c : ROW_X + c + 1, :]

    def raw(first, count, i):
        return po_ref[first : first + count, i * LANES : i * LANES + CHANNELS]

    low = PACK_ROWS + CHANNELS
    mix_ref = [raw(PACK_ROWS, CHANNELS, i) for i in range(2)]
    update_ref = [raw(PACK_ROWS, CHANNELS, 2 + i) for i in range(2)]
    radial_ref = [raw(low, BASIS, i) for i in range(2)]
    embed_ref, readout = raw(low, 2, 2), raw(low, 1, 3)
    eye = (
        lax.broadcasted_iota(jnp.int32, (CHANNELS, CHANNELS), 0)
        == lax.broadcasted_iota(jnp.int32, (CHANNELS, CHANNELS), 1)
    ).astype(F32)

    def turned(x):
        return lax.dot_general(eye, x, NT, precision=PRECISE, preferred_element_type=F32)

    base0 = embed_ref[0:1, :]
    base1 = embed_ref[1:2, :] - base0
    rows = jnp.concatenate([base0, base1], axis=0)
    sent = jnp.dot(rows, mix_ref[0], precision=PRECISE, preferred_element_type=F32)
    scale = 1.0 / math.sqrt(SLOTS)
    first = jnp.concatenate([radial_ref[0] * sent[0:1], radial_ref[0] * sent[1:2]], axis=0) * scale
    second = radial_ref[1] * scale
    folded = jnp.dot(update_ref[0], mix_ref[1], precision=PRECISE, preferred_element_type=F32)
    mix_t = turned(mix_ref[1])
    l1_ref[...] = left_stack(turned(first)).astype(BF16)
    l2_ref[...] = left_stack(turned(folded)).astype(BF16)
    high, low = split(turned(second))
    l3_ref[...] = jnp.concatenate([high, high, low, jnp.zeros_like(high)], axis=1).astype(BF16)
    high, low = split(folded)
    l5_ref[...] = jnp.concatenate([high, high, high, high, low, low], axis=1).astype(BF16)
    l6_ref[...] = left_stack(first).astype(BF16)
    wide = (CHANNELS, LANES)
    col_ref[0] = jnp.broadcast_to(jnp.sum(mix_t * base0, axis=1, keepdims=True), wide)
    col_ref[1] = jnp.broadcast_to(jnp.sum(mix_t * base1, axis=1, keepdims=True), wide)
    col_ref[2] = jnp.broadcast_to(jnp.sum(update_ref[0] * readout, axis=1, keepdims=True), wide)
    col_ref[3] = jnp.broadcast_to(jnp.sum(update_ref[1] * readout, axis=1, keepdims=True), wide)


def sin_cos(t):
    q = t * t
    s = -1.0 / 39916800.0
    for c in (1.0 / 362880.0, -1.0 / 5040.0, 1.0 / 120.0, -1.0 / 6.0, 1.0):
        s = s * q + c
    k = 1.0 / 479001600.0
    for c in (-1.0 / 3628800.0, 1.0 / 40320.0, -1.0 / 720.0, 1.0 / 24.0, -0.5, 1.0):
        k = k * q + c
    return s * t, k


def wide_row(x, row):
    return jnp.broadcast_to(x[row : row + 1, :], (8, x.shape[1]))


def silu_parts(m):
    sig = 1.0 / (1.0 + jnp.exp(-m))
    return m * sig, sig * (1.0 + m * (1.0 - sig))


def pick(values, lanes):
    return jnp.take_along_axis(values, lanes, axis=1, mode="promise_in_bounds")


def reach(b, first, last):
    return [w for w in range(3) if first <= b - 1 + w <= last]


SIDE_START = {2: 0, 3: LANES, 8: 3 * LANES, 9: 5 * LANES}
SIDE_ROWS = 6 * LANES


def mark(index, ws, target):
    count = len(ws) * LANES
    row_id = (lax.broadcasted_iota(jnp.int32, (count, LANES), 0) + ws[0] * LANES).astype(jnp.int16)
    one, zero = jnp.ones((count, LANES), BF16), jnp.zeros((count, LANES), BF16)
    for k in range(SLOTS):
        wanted = jnp.broadcast_to(index[k : k + 1, :], (16, LANES)).astype(jnp.int16)
        wanted = jnp.concatenate([wanted] * (count // 16), axis=0)
        target[:, k * LANES : (k + 1) * LANES] = jnp.where(row_id == wanted, one, zero)


def window_index(pack, b):
    lanes = slice((b % 4) * LANES, (b % 4 + 1) * LANES)
    return pack[0:8, lanes].astype(jnp.int32) - LANES * (b % 4)


def mark_sides(packs, side):
    for b, start in SIDE_START.items():
        ws = reach(b, 3, 8)
        mark(window_index(packs[b // 4], b), ws, side.at[start : start + len(ws) * LANES])


def forward_parts(packs, weights, xs, sst, kept):
    l1, l2, l3, l5, l6, col = weights
    (widx, kinds, geo, bst, bps, bpr, sent_all, slope) = kept
    centre = 2.0 + 0.5 * lax.broadcasted_iota(jnp.int32, (BASIS, LANES), 0).astype(F32)
    slot = lax.broadcasted_iota(jnp.int32, (SLOTS, LANES), 0)

    def part_rows(value):
        high, low = split(value)
        return jnp.concatenate([high, low], axis=0).astype(BF16)

    def pairs(b):
        pack = packs[b // 4]
        lanes = slice((b % 4) * LANES, (b % 4 + 1) * LANES)
        index = window_index(pack, b)
        widx[b] = index
        inner = index & (LANES - 1)
        part = index >> 7

        def taken(row):
            got = [
                pick(jnp.broadcast_to(xs[b - 1 + w, row : row + 1, :], (SLOTS, LANES)), inner)
                for w in range(3)
            ]
            return jnp.where(part == 0, got[0], jnp.where(part == 1, got[1], got[2]))

        vec = [
            pack[8 + 8 * c : 16 + 8 * c, lanes] + taken(c) - jnp.broadcast_to(xs[b, c : c + 1, :], (SLOTS, LANES))
            for c in range(3)
        ]
        kind = taken(3)
        dist = jnp.sqrt(vec[0] * vec[0] + vec[1] * vec[1] + vec[2] * vec[2] + SOFTENING)
        live = (slot.astype(F32) < jnp.broadcast_to(pack[ROW_COUNT : ROW_COUNT + 1, lanes], (SLOTS, LANES))).astype(F32)
        turns = dist * (1.0 / 12.0)
        turns = turns - jnp.floor(turns + 0.5)
        sine, cosine = sin_cos(turns * math.pi)
        envelope = cosine * cosine * live
        slant = cosine * sine * live * (-math.pi / 6.0)
        if 3 <= b <= 8:
            kinds[b] = kind
            for c in range(3):
                geo[b, c] = vec[c]
            geo[b, 3] = 1.0 / dist
        total = jnp.zeros((BASIS, LANES), F32)
        total_kind = jnp.zeros((BASIS, LANES), F32)
        for k in range(SLOTS):
            away = wide_row(dist, k) - centre
            gauss = jnp.exp(-4.0 * (away * away))
            env_k = wide_row(envelope, k)
            value = gauss * env_k
            total = total + value
            total_kind = total_kind + value * wide_row(kind, k)
            cols = slice(k * LANES, (k + 1) * LANES)
            if 2 <= b <= 9:
                bst[b, :, cols] = part_rows(value)
            if 3 <= b <= 8:
                value = gauss * (wide_row(slant, k) - 8.0 * away * env_k)
                bpr[b, :, cols] = value
                bps[b, :, cols] = part_rows(value)
        high, low = split(jnp.concatenate([total, total_kind], axis=0))
        sst[:, b * LANES : (b + 1) * LANES] = jnp.concatenate([high, low, high], axis=0).astype(BF16)

    for b in range(1, 11):
        pairs(b)

    for b in range(1, 11, 2):
        cols = slice(b * LANES, (b + 2) * LANES)
        value, steep = silu_parts(mm(l1[...], sst[:, cols]))
        sent = mm(l2[...], right_stack(value))
        for i in range(2):
            one = sent[:, i * LANES : (i + 1) * LANES]
            one = one + col[0] + col[1] * jnp.broadcast_to(xs[b + i, 3:4, :], (CHANNELS, LANES))
            sent_all[:, (b + i) * LANES : (b + i + 1) * LANES] = one
        slope[:, cols] = steep


def force_parts(weights, own_hot, side_hot, kept, dg, pulls, met, acc, held):
    l1, l2, l3, l5, l6, col = weights
    (widx, kinds, geo, bst, bps, bpr, sent_all, slope) = kept
    slot = lax.broadcasted_iota(jnp.int32, (SLOTS, LANES), 0)

    def spread(left, b, first, last, sums):
        ws = reach(b, first, last)
        if b in SIDE_START:
            start = SIDE_START[b] + (ws[0] - reach(b, 3, 8)[0]) * LANES
            picked = side_hot[start : start + len(ws) * LANES, :]
        else:
            picked = own_hot[b - 4, ws[0] * LANES : (ws[-1] + 1) * LANES, :]
        out = mm_nt(picked, left)
        for i, w in enumerate(ws):
            target = b - 1 + w
            piece = out[i * LANES : (i + 1) * LANES]
            rows = slice((target - first) * LANES, (target - first + 1) * LANES)
            if (first, target) in started:
                sums[rows, :] += piece
            else:
                sums[rows, :] = piece
                started.add((first, target))

    started = set()

    def gather_and_return(b):
        index = widx[b]
        inner, part = index & (LANES - 1), index >> 7
        basis = bst[b]
        radial = mm(l3[...], jnp.concatenate([basis, basis], axis=0))
        if 3 <= b <= 8:
            basis = bps[b]
            steepness = mm(l3[...], jnp.concatenate([basis, basis], axis=0))
        lanes = [jnp.broadcast_to(inner[k : k + 1, :], (16, LANES)) for k in range(SLOTS)]
        parts = [jnp.broadcast_to(part[k : k + 1, :], (16, LANES)) for k in range(SLOTS)]
        value = held.at[b % 2]
        total = [jnp.zeros((8, LANES), F32)] * SLOTS
        for u in range(CHANNELS // 16):
            rows = slice(16 * u, 16 * u + 16)
            low_rows = slice(CHANNELS + 16 * u, CHANNELS + 16 * u + 16)
            windows = [sent_all[rows, (b - 1 + w) * LANES : (b + w) * LANES] for w in range(3)]
            got = []
            message = jnp.zeros((16, LANES), F32)
            for k in range(SLOTS):
                cols = slice(k * LANES, (k + 1) * LANES)
                found = [pick(window, lanes[k]) for window in windows]
                got.append(jnp.where(parts[k] == 0, found[0], jnp.where(parts[k] == 1, found[1], found[2])))
                message = message + radial[rows, cols] * got[k]
            _, steep = silu_parts(message)
            back = col[3, rows] * steep
            for k in range(SLOTS):
                cols = slice(k * LANES, (k + 1) * LANES)
                high, low = split(radial[rows, cols] * back)
                value[rows, cols] = high.astype(BF16)
                value[low_rows, cols] = low.astype(BF16)
                if 3 <= b <= 8:
                    pull = got[k] * back * steepness[rows, cols]
                    total[k] = total[k] + pull[0:8] + pull[8:16]
        spread(value[...], b, 3, 8, dg)
        if 3 <= b <= 8:
            for k in range(SLOTS):
                pulls[b, :, k * LANES : (k + 1) * LANES] = total[k]

    for b in range(2, 10):
        gather_and_return(b)

    def finish(b, sums):
        kind = kinds[b]
        rows = []
        for k in range(SLOTS):
            cols = slice(k * LANES, (k + 1) * LANES)
            weight = sums[0:8] + wide_row(kind, k) * sums[8:16]
            rows.append(jnp.sum(bpr[b, :, cols] * weight + pulls[b, :, cols], axis=0, keepdims=True))
        pull = jnp.concatenate(rows, axis=0) * geo[b, 3]
        pieces = []
        for c in range(3):
            value = pull * geo[b, c]
            if 4 <= b <= 7:
                acc[b - 4, c] = jnp.sum(value, axis=0, keepdims=True)
            pieces.append(split(value))
        lines = []
        for h in range(2):
            for c in range(3):
                lines.append(jnp.concatenate([jnp.where(slot == k, pieces[c][h], 0.0) for k in range(SLOTS)], axis=1))
        spread(jnp.concatenate(lines, axis=0).astype(BF16), b, 4, 7, met)

    for b in range(3, 9, 2):
        cols = slice(b * LANES, (b + 2) * LANES)
        high, low = split(dg[(b - 3) * LANES : (b - 1) * LANES, :])
        steep = mm_nt(l5[...], jnp.concatenate([high, low, high], axis=1).astype(BF16))
        steep = steep + jnp.concatenate([col[2], col[2]], axis=1)
        sums = mm(l6[...], right_stack(steep * slope[:, cols]))
        for i in range(2):
            finish(b + i, sums[:, i * LANES : (i + 1) * LANES])

    high, low = split(met[...])
    column = lax.broadcasted_iota(jnp.int32, (16, 6 * SLOTS), 1)
    column = jnp.where(column < 3 * SLOTS, column, column - 3 * SLOTS)
    first = SLOTS * lax.broadcasted_iota(jnp.int32, (16, 6 * SLOTS), 0)
    choose = jnp.where((column >= first) & (column < first + SLOTS), 1.0, 0.0).astype(BF16)
    back = mm_nt(choose, high.astype(BF16)) + mm_nt(choose, low.astype(BF16))
    away = [jnp.concatenate([acc[i, c] for i in range(SLAB_BLOCKS)], axis=1) for c in range(3)]
    return jnp.concatenate(away, axis=0) - back[0:3]


def fill_region(xs, packs, rows_of):
    for b in range(12):
        lanes = slice((b % 4) * LANES, (b % 4 + 1) * LANES)
        pack = packs[b // 4]
        xs[b, 0:3, :] = rows_of(b // 4)[:, lanes]
        xs[b, 3:4, :] = pack[ROW_KIND : ROW_KIND + 1, lanes]


def lane_total(x):
    x = x[:, 0:LANES] + x[:, LANES : 2 * LANES] + x[:, 2 * LANES : 3 * LANES] + x[:, 3 * LANES : 4 * LANES]
    return jnp.sum(x, axis=1, keepdims=True)


def dot3(a, b):
    return jnp.sum(a * b, axis=0, keepdims=True)


def kept_shapes():
    wide = 12 * LANES
    return [
        ((12, 8, LANES), jnp.int32),
        ((12, 8, LANES), F32),
        ((12, 4, 8, LANES), F32),
        ((12, 16, SLOTS * LANES), BF16),
        ((12, 16, SLOTS * LANES), BF16),
        ((12, 8, SLOTS * LANES), F32),
        ((CHANNELS, wide), F32),
        ((CHANNELS, wide), F32),
    ]


def forward_scratch():
    return [pltpu.VMEM((12, 8, LANES), F32), pltpu.VMEM((48, 12 * LANES), BF16)]


def back_scratch():
    return [
        pltpu.VMEM((6 * LANES, 2 * CHANNELS), F32),
        pltpu.VMEM((12, 8, SLOTS * LANES), F32),
        pltpu.VMEM((SLAB_BLOCKS * LANES, 6 * SLOTS), F32),
        pltpu.VMEM((SLAB_BLOCKS, 3, 1, LANES), F32),
        pltpu.VMEM((2, 2 * CHANNELS, SLOTS * LANES), BF16),
    ]


def by_parity(sibling, across):
    even = jnp.full(sibling.shape, lax.axis_index("dom") % 2, jnp.int32) == 0
    return jnp.where(even, across, sibling), jnp.where(even, sibling, across)


def first_kernel(x_ref, sibling_ref, po_ref, across_ref, *rest):
    weights, (pl_ref, pr_ref, side_hot, copy_ref), kept, (xs, sst) = rest[:6], rest[6:10], rest[10:18], rest[18:]
    copy_ref[...] = x_ref[...]
    pl_ref[...], pr_ref[...] = by_parity(sibling_ref[...], across_ref[...])
    packs = [pl_ref, po_ref, pr_ref]
    mark_sides(packs, side_hot)
    fill_region(xs, packs, lambda s: packs[s][ROW_X : ROW_X + 3, :])
    forward_parts(packs, weights, xs, sst, kept)


def first_back_kernel(own_hot, side_hot, *rest):
    weights, kept, out_ref, scr = rest[:6], rest[6:14], rest[14], rest[15:]
    out_ref[...] = force_parts(weights, own_hot, side_hot, kept, *scr)


def rows_of(ref):
    return jnp.concatenate([ref[c] for c in range(3)], axis=0)


def block_row(*values):
    values = list(values) + [jnp.zeros((1, LANES), F32)] * (SLAB_BLOCKS - len(values))
    return jnp.concatenate(values, axis=1)


def blend_kernel(images, force_ref, po_ref, before_ref, after_ref, out_ref, sums_ref):
    x = po_ref[ROW_X : ROW_X + 3, :]
    v = po_ref[ROW_V : ROW_V + 3, :]
    force = force_ref[...]
    here = lax.axis_index("img")
    before = jnp.where(here > 0, rows_of(before_ref), 0.0)
    after = jnp.where(here < images - 1, rows_of(after_ref), 0.0)
    tangent = after - before
    plus = after - x
    minus = x - before
    sums = jnp.concatenate(
        [
            dot3(force, tangent),
            dot3(force, force),
            dot3(tangent, tangent),
            dot3(plus, plus),
            dot3(minus, minus),
            dot3(v, v),
            jnp.zeros((2, x.shape[1]), F32),
        ],
        axis=0,
    )
    sums = jnp.broadcast_to(lane_total(sums), (8, LANES))
    sums_ref[...] = sums
    out_ref[0:3, :] = force
    out_ref[3:6, :] = tangent
    out_ref[6:7, :] = block_row(*[sums[i : i + 1] for i in range(4)])
    out_ref[7:8, :] = block_row(sums[4:5], sums[5:6])


def step_numbers(ft, ff, tt, pp, mn, vv, dt, alpha, flagged, climbing, inside):
    root = jnp.sqrt(tt + TINY_VALUE)
    along = ft / root
    spring = SPRING_CONSTANT * (jnp.sqrt(pp) - jnp.sqrt(mn))
    factor = jnp.where(climbing, -2.0 * along, spring - along)
    band = jnp.maximum(ff + 2.0 * factor * along + factor * factor * (tt / (tt + TINY_VALUE)), 0.0)
    new_dt = jnp.where(flagged, 0.5 * dt, jnp.minimum(1.1 * dt, STEP_LIMIT))
    pull = jnp.where(flagged, 0.0, alpha * jnp.sqrt(vv / (band + TINY_VALUE))) + new_dt
    keep = jnp.where(flagged, 0.0, 1.0 - alpha)
    new_alpha = jnp.where(flagged, ALPHA_START, 0.99 * alpha)
    keep = jnp.where(inside, keep, 0.0)
    pull = jnp.where(inside, pull, 0.0)
    return (
        jnp.where(inside, along, 0.0),
        jnp.where(inside, spring, 0.0),
        keep,
        pull,
        pull * factor / root,
        new_dt,
        new_alpha,
    )


def add_kernel(a_ref, b_ref, out_ref):
    out_ref[...] = a_ref[...] + b_ref[...]


def join_kernel(a_ref, b_ref, out_ref):
    count = a_ref.shape[0]
    out_ref[0:count] = a_ref[...]
    out_ref[count : 2 * count] = b_ref[...]


def number_kernel(dt_ref, flag_ref, climb_ref, out_ref):
    flags = [flag_ref[0, s].astype(F32) for s in range(flag_ref.shape[1])]
    for i, value in enumerate([dt_ref[0], climb_ref[0].astype(F32)] + flags):
        out_ref[i : i + 1, :] = jnp.full((1, LANES), value, F32)


def second_kernel(images, domains, number_ref, pl_ref, po_ref, pr_ref, own_ref, near_ref, far_ref, *rest):
    count = 2 if domains == 4 else 1
    parts, rest = rest[:count], rest[count:]
    (own_hot, side_hot), weights, (out_ref, record_ref), scr = rest[:2], rest[2:8], rest[8:10], rest[10:]
    packs = [pl_ref, po_ref, pr_ref]
    here = lax.axis_index("img")
    sums = parts[0][...]
    if domains == 4:
        sums = sums + parts[1][...]
    got = [sums[i : i + 1, :] for i in range(6)]
    if domains == 4:
        for one in (near_ref, far_ref):
            for i in range(6):
                got[i] = got[i] + one[6 + i // 4 : 7 + i // 4, (i % 4) * LANES : (i % 4 + 1) * LANES]
    ft, ff, tt, pp, mn, vv = got
    beside = by_parity(near_ref[0:6, :], far_ref[0:6, :])
    shape = (1, LANES)
    along, spring, keep, pull, side, dt, alpha = step_numbers(
        ft,
        ff,
        tt,
        pp,
        mn,
        vv,
        number_ref[0:1, :],
        jnp.full(shape, ALPHA_START, F32),
        number_ref[2:3, :] == 1.0,
        number_ref[1:2, :] == jnp.full(shape, here, jnp.int32).astype(F32),
        jnp.full(shape, jnp.where((here >= 1) & (here <= images - 2), 1, 0), jnp.int32) == 1,
    )
    messages = [beside[0], own_ref[0:6, :], beside[1]]

    def wide(s):
        return jnp.concatenate([s] * SLAB_BLOCKS, axis=1)

    speeds = [
        wide(keep) * p[ROW_V : ROW_V + 3, :] + wide(pull) * m[0:3, :] + wide(side) * m[3:6, :]
        for p, m in zip(packs, messages)
    ]
    moved = [p[ROW_X : ROW_X + 3, :] + wide(dt) * s for p, s in zip(packs, speeds)]
    xs, sst, kept = scr[0], scr[1], scr[2:10]
    fill_region(xs, packs, lambda s: moved[s])
    forward_parts(packs, weights, xs, sst, kept)
    force = force_parts(weights, own_hot, side_hot, kept, *scr[10:])
    for c in range(3):
        for i in range(SLAB_BLOCKS):
            lanes = slice(i * LANES, (i + 1) * LANES)
            row = 4 * c + i
            out_ref[0, row : row + 1, :] = speeds[1][c : c + 1, lanes]
            out_ref[0, 12 + row : 13 + row, :] = force[c : c + 1, lanes]
            out_ref[0, 24 + row : 25 + row, :] = moved[1][c : c + 1, lanes]
    out_ref[0, 36:37, :] = dt
    out_ref[0, 37:38, :] = alpha
    out_ref[0, 38:40, :] = jnp.broadcast_to(number_ref[3:4, :], (2, LANES))
    record_ref[0:1, :] = along
    record_ref[1:2, :] = spring
    record_ref[2:3, :] = number_ref[1:2, :]


PRODUCTS = (
    [("f", "t"), ("f", "f"), ("t", "t"), ("p", "p"), ("d", "d"), ("v", "v")]
    + [("d", "v"), ("d", "f"), ("d", "t"), ("d", "V"), ("d", "F"), ("d", "T"), ("v", "f"), ("v", "t")]
    + [(a, b) for a in "vft" for b in "VFT"]
)


def gram_kernel(images, *refs):
    parts, (out_ref, state_ref, messages_ref) = refs[:-3], refs[-3:]
    rows = out_ref.shape[0]
    place = 0
    for part in parts:
        messages_ref[place : place + part.shape[0]] = part[...]
        place += part.shape[0]
    here = lax.axis_index("img")
    blank = [jnp.zeros((rows - images, LANES), F32)] if rows > images else []
    zero = jnp.zeros((1, LANES), F32)

    def gathered(row):
        return jnp.concatenate([messages_ref[here ^ i, row : row + 1, :] for i in range(images)] + blank, axis=0)

    def earlier(value):
        return jnp.concatenate([zero, value[0 : rows - 1]], axis=0)

    def later(value):
        return jnp.concatenate([value[1:images], zero] + blank, axis=0)

    number = lax.broadcasted_iota(jnp.int32, (rows, LANES), 0)
    held = number < images
    totals = [jnp.zeros((rows, LANES), F32) for _ in PRODUCTS]
    for row in range(3 * SLAB_BLOCKS):
        v, f, x = gathered(row), gathered(12 + row), gathered(24 + row)
        before = jnp.where(held, earlier(x), 0.0)
        after = later(x)
        t = after - before
        table = {"f": f, "v": v, "t": t, "p": after - x, "d": x - before}
        table["F"], table["V"], table["T"] = earlier(f), earlier(v), earlier(t)
        totals = [old + table[a] * table[b] for old, (a, b) in zip(totals, PRODUCTS)]
        state_ref[row : row + 1, :] = jnp.sum(jnp.where(number == here, t, 0.0), axis=0, keepdims=True)
    lane = lax.broadcasted_iota(jnp.int32, (rows, LANES), 1)
    result = jnp.zeros((rows, LANES), F32)
    for q, one in enumerate(totals):
        one = jnp.broadcast_to(jnp.sum(one, axis=1, keepdims=True), (rows, LANES))
        result = jnp.where(lane == q, one, result)
    out_ref[...] = result
    for i in range(3):
        state_ref[16 + rows * i : 16 + rows * (i + 1), :] = gathered(36 + i)


def final_kernel(images, atoms, own_ref, record_ref, state_ref, *rest):
    parts, (x_ref, v_ref, band_ref, path_ref) = rest[:-4], rest[-4:]
    rows = parts[0].shape[0]
    here = lax.axis_index("img")
    sums = parts[0][...]
    for one in parts[1:]:
        sums = sums + one[...]
    got = {
        pair: jnp.broadcast_to(sums[:, q : q + 1], (rows, LANES)) for q, pair in enumerate(PRODUCTS)
    }
    number = lax.broadcasted_iota(jnp.int32, (rows, LANES), 0)
    inside = (number >= 1) & (number <= images - 2)
    climb = jnp.broadcast_to(record_ref[2:3, :], (rows, LANES))
    dt0, alpha0, flag = (state_ref[16 + rows * i : 16 + rows * (i + 1), :] for i in range(3))
    along, spring, keep, pull, side, dt, _ = step_numbers(
        got["f", "t"],
        got["f", "f"],
        got["t", "t"],
        got["p", "p"],
        got["d", "d"],
        got["v", "v"],
        dt0,
        alpha0,
        flag == 1.0,
        number.astype(F32) == climb,
        inside,
    )

    def shifted(value):
        return jnp.concatenate([jnp.zeros((1, LANES), F32), value[0 : rows - 1]], axis=0)

    now = {"v": dt * keep, "f": dt * pull, "t": dt * side}
    old = {a.upper(): shifted(value) for a, value in now.items()}
    mine = now["v"] * now["v"] * got["v", "v"] + now["f"] * now["f"] * got["f", "f"]
    mine = mine + now["t"] * now["t"] * got["t", "t"]
    cross = now["v"] * now["f"] * got["v", "f"] + now["v"] * now["t"] * got["v", "t"]
    mine = mine + 2.0 * (cross + now["f"] * now["t"] * got["f", "t"])
    both = jnp.zeros((rows, LANES), F32)
    for a in "vft":
        both = both + now[a] * got["d", a]
    for b in "VFT":
        both = both - old[b] * got["d", b]
    for a in "vft":
        for b in "VFT":
            both = both - now[a] * old[b] * got[a, b]
    squared = got["d", "d"] + mine + shifted(mine) + 2.0 * both
    segment = jnp.sqrt(jnp.maximum(squared, 0.0) * (1.0 / (3.0 * atoms)))
    path = jnp.sum(jnp.where(number <= here, segment, 0.0), axis=0, keepdims=True)
    path_ref[...] = path[:, 0:1]
    keep, pull, side, dt, along, spring = (
        jnp.sum(jnp.where(number == here, value, 0.0), axis=0, keepdims=True)
        for value in (keep, pull, side, dt, along, spring)
    )

    for c in range(3):
        speeds, places = [], []
        for i in range(SLAB_BLOCKS):
            row = 4 * c + i
            speed = keep * own_ref[0, row : row + 1, :] + pull * own_ref[0, 12 + row : 13 + row, :]
            speed = speed + side * state_ref[row : row + 1, :]
            speeds.append(speed)
            places.append(own_ref[0, 24 + row : 25 + row, :] + dt * speed)
        v_ref[c] = jnp.concatenate(speeds, axis=1)
        x_ref[c] = jnp.concatenate(places, axis=1)
    band_ref[0] = jnp.concatenate([record_ref[0:1, 0:1], record_ref[1:2, 0:1]], axis=1)
    band_ref[1] = jnp.concatenate([along[:, 0:1], spring[:, 0:1]], axis=1)


VMEM_SPEC = pl.BlockSpec(memory_space=pltpu.VMEM)
SMEM_SPEC = pl.BlockSpec(memory_space=pltpu.SMEM)
HBM_SPEC = pl.BlockSpec(memory_space=pltpu.HBM)


def call(body, outs, scalars, arrays, scratch_shapes=(), flops=0, spec=VMEM_SPEC, vmem=24):
    return pl.pallas_call(
        body,
        out_shape=outs,
        in_specs=[SMEM_SPEC] * len(scalars) + [spec] * len(arrays),
        out_specs=jax.tree.map(lambda _: VMEM_SPEC, outs),
        scratch_shapes=list(scratch_shapes),
        compiler_params=pltpu.CompilerParams(vmem_limit_bytes=vmem * 1024 * 1024),
        cost_estimate=pl.CostEstimate(flops=flops, bytes_accessed=1 << 18, transcendentals=0),
    )(*scalars, *arrays)


def swap(array, axis, partner):
    return lax.ppermute(array, axis, [(i, partner(i)) for i in range(lax.axis_size(axis))])


def exchanged(sums, axis):
    count = lax.axis_size(axis)
    if count == 4:
        return [sums] + [swap(sums, axis, lambda i, by=by: i ^ by) for by in (2, 3, 1)]
    distance = 1
    while distance < count:
        more = swap(sums, axis, lambda i, by=distance: i ^ by)
        sums = call(add_kernel, jax.ShapeDtypeStruct(sums.shape, F32), (), (sums, more))
        distance *= 2
    return [sums]


def collected(array, axis):
    count = lax.axis_size(axis)
    if count == 4:
        far = [swap(array, axis, lambda i, by=by: i ^ by) for by in (3, 2, 1)]
        return [array] + far[::-1]
    distance = 1
    while distance < count:
        more = swap(array, axis, lambda i, by=distance: i ^ by)
        shape = jax.ShapeDtypeStruct((2 * distance,) + array.shape[1:], F32)
        array = call(join_kernel, shape, (), (array, more))
        distance *= 2
    return [array]


def local(
    disp,
    veloc,
    time_step,
    reset_flags,
    climb,
    species,
    neighbours,
    counts,
    lattice,
    embed,
    radial_weight,
    mix_weight,
    update_weight,
    readout,
):
    atoms = disp.shape[2]
    images = lax.axis_size("img")
    domains = lax.axis_size("dom")
    assert disp.shape[0] == 1 and atoms == SLAB_BLOCKS * LANES and domains >= 4
    assert domains & (domains - 1) == 0 and images & (images - 1) == 0
    shape = jax.ShapeDtypeStruct
    x = jnp.transpose(disp, (1, 0, 2))
    v = jnp.transpose(veloc, (1, 0, 2))
    small = (x, v, species, neighbours, counts, embed, readout, radial_weight, mix_weight, update_weight)
    sent, pack = call(
        pack_kernel,
        (shape((PACK_ROWS, atoms), F32), shape((OWN_ROWS, atoms), F32)),
        (),
        (*small, jnp.transpose(lattice, (1, 0, 2))),
        [pltpu.VMEM(a.shape, a.dtype) for a in small] + [pltpu.SemaphoreType.DMA((16,))],
        spec=HBM_SPEC,
        vmem=63,
    )
    sibling = swap(sent, "dom", lambda i: i ^ 1)
    across = swap(sent, "dom", lambda i: (i + 2 * (i % 2) - 1) % domains)
    own_hot, *weights, x_copy = call(
        prepare_kernel,
        (
            shape((SLAB_BLOCKS, 3 * LANES, SLOTS * LANES), BF16),
            shape((CHANNELS, 48), BF16),
            shape((CHANNELS, 192), BF16),
            shape((CHANNELS, 32), BF16),
            shape((CHANNELS, 3 * LANES), BF16),
            shape((16, 192), BF16),
            shape((4, CHANNELS, LANES), F32),
            shape(x.shape, F32),
        ),
        (),
        (pack,),
        flops=100000000,
    )
    before = swap(x_copy, "img", lambda i: (i + 1) % images)
    left, right, side_hot, x_copy, *kept = call(
        first_kernel,
        (
            shape(sent.shape, F32),
            shape(sent.shape, F32),
            shape((SIDE_ROWS, SLOTS * LANES), BF16),
            shape(x.shape, F32),
            *[shape(*one) for one in kept_shapes()],
        ),
        (),
        (x_copy, sibling, pack, across, *weights),
        forward_scratch(),
        flops=1000000000,
    )
    after = swap(x_copy, "img", lambda i: (i - 1) % images)
    force = call(
        first_back_kernel,
        shape((3, atoms), F32),
        (),
        (own_hot, side_hot, *weights, *kept),
        back_scratch(),
        flops=1000000000,
    )
    message, sums = call(
        functools.partial(blend_kernel, images),
        (shape((8, atoms), F32), shape((8, LANES), F32)),
        (),
        (force, pack, before, after),
    )
    far = swap(message, "dom", lambda i: (i + 2 * (i % 2) - 1) % domains)
    if domains == 4:
        parts = [sums, swap(sums, "dom", lambda i: i ^ 2)]
    else:
        parts = exchanged(sums, "dom")
    near = swap(message, "dom", lambda i: i ^ 1)
    numbers = call(number_kernel, shape((8, LANES), F32), (time_step, jnp.transpose(reset_flags), climb), ())
    state, record = call(
        functools.partial(second_kernel, images, domains),
        (shape((1, 40, LANES), F32), shape((3, LANES), F32)),
        (),
        (numbers, left, pack, right, message, near, far, *parts, own_hot, side_hot, *weights),
        forward_scratch() + [pltpu.VMEM(*one) for one in kept_shapes()] + back_scratch(),
        flops=1000000000,
    )
    rows = 8 * ((images + 7) // 8)
    sums, extra = call(
        functools.partial(gram_kernel, images),
        (shape((rows, LANES), F32), shape((16 + 3 * rows, LANES), F32)),
        (),
        collected(state, "img"),
        [pltpu.VMEM((images, 40, LANES), F32)],
    )
    new_x, new_v, records, path = call(
        functools.partial(final_kernel, images, atoms * domains),
        (shape(x.shape, F32), shape(x.shape, F32), shape((2, 1, 2), F32), shape((1, 1), F32)),
        (),
        (state, record, extra, *exchanged(sums, "dom")),
    )
    return (
        jnp.transpose(new_x, (1, 0, 2)),
        jnp.transpose(new_v, (1, 0, 2)),
        jnp.transpose(records, (0, 2, 1)),
        path.reshape(1),
    )


def solution(mesh):
    in_specs = (
        P(("group", "img"), None, "dom"),
        P(("group", "img"), None, "dom"),
        P(("group", "img")),
        P(None, ("group", "img")),
        P("group"),
        P(("group", "dom")),
        P(None, ("group", "dom")),
        P(("group", "dom")),
        P(None, None, ("group", "dom")),
        P(),
        P(),
        P(),
        P(),
        P(),
    )
    out_specs = (
        P(("group", "img"), None, "dom"),
        P(("group", "img"), None, "dom"),
        P(None, None, ("group", "img")),
        P(("group", "img")),
    )
    return jax.shard_map(local, mesh=mesh, in_specs=in_specs, out_specs=out_specs, check_vma=False)
```

```python
import functools
import math

import jax
import jax.numpy as jnp
from jax import lax
from jax.experimental import pallas as pl
from jax.experimental.pallas import tpu as pltpu
from jax.sharding import PartitionSpec as P

F32 = jnp.float32
BF16 = jnp.bfloat16
PRECISE = lax.Precision.HIGHEST
SPRING_CONSTANT = 0.5
ALPHA_START = 0.1
STEP_LIMIT = 0.3
TINY_VALUE = 1e-06
SOFTENING = 0.25
LANES = 128
SLOTS = 8
BASIS = 8
CHANNELS = 64
SLAB_BLOCKS = 4
ROW_X = 32
ROW_COUNT = 35
ROW_KIND = 36
ROW_V = 37
PACK_ROWS = 40
OWN_ROWS = PACK_ROWS + CHANNELS + BASIS
NT = (((1,), (1,)), ((), ()))


def split(x):
    high = x.astype(BF16).astype(F32)
    return high, x - high


def left_stack(w):
    high, low = split(w)
    return jnp.concatenate([high, high, low], axis=1)


def right_stack(x):
    high, low = split(x)
    high = high.astype(BF16)
    return jnp.concatenate([high, low.astype(BF16), high], axis=0)


def pair_stack(x):
    high, low = split(x)
    return jnp.concatenate([high.astype(BF16), low.astype(BF16)], axis=0)


def mm(a, b):
    return jnp.dot(a, b, preferred_element_type=F32)


def mm_nt(a, b):
    return lax.dot_general(a, b, NT, preferred_element_type=F32)


def pack_kernel(*refs):
    sources, (out_ref, own_ref), held, sems = refs[:11], refs[11:13], refs[13:23], refs[23]
    lattice = sources[10]
    pairs = list(zip(sources, held))
    for c in range(3):
        rows = pl.ds(8 + 8 * c, 8)
        pairs += [(lattice.at[c], out_ref.at[rows]), (lattice.at[c], own_ref.at[rows])]
    copies = [pltpu.make_async_copy(a, b, sems.at[i]) for i, (a, b) in enumerate(pairs)]
    for one in copies:
        one.start()
    for one in copies:
        one.wait()
    x, v, species, nbr, counts, embed, readout, radial, mix, update = held
    for ref in (out_ref, own_ref):
        ref[0:8, :] = nbr[...].astype(F32)
        for c in range(3):
            ref[ROW_X + c : ROW_X + c + 1, :] = x[c]
            ref[ROW_V + c : ROW_V + c + 1, :] = v[c]
        ref[ROW_COUNT : ROW_COUNT + 1, :] = counts[...].astype(F32).reshape(1, -1)
        ref[ROW_KIND : ROW_KIND + 1, :] = species[...].astype(F32).reshape(1, -1)
    top, low = PACK_ROWS, PACK_ROWS + CHANNELS
    for i, value in enumerate([mix[0], mix[1], update[0], update[1]]):
        own_ref[top:low, i * LANES : i * LANES + CHANNELS] = value
    for i, value in enumerate([radial[0], radial[1], embed[...], readout[...].reshape(1, CHANNELS)]):
        own_ref[low : low + value.shape[0], i * LANES : i * LANES + CHANNELS] = value


def prepare_kernel(po_ref, *rest):
    own_hot, l1_ref, l2_ref, l3_ref, l5_ref, l6_ref, col_ref, copy_ref = rest
    for b in range(SLAB_BLOCKS):
        mark(window_index(po_ref, b), [0, 1, 2], own_hot.at[b])
    for c in range(3):
        copy_ref[c] = po_ref[ROW_X + c : ROW_X + c + 1, :]

    def raw(first, count, i):
        return po_ref[first : first + count, i * LANES : i * LANES + CHANNELS]

    low = PACK_ROWS + CHANNELS
    mix_ref = [raw(PACK_ROWS, CHANNELS, i) for i in range(2)]
    update_ref = [raw(PACK_ROWS, CHANNELS, 2 + i) for i in range(2)]
    radial_ref = [raw(low, BASIS, i) for i in range(2)]
    embed_ref, readout = raw(low, 2, 2), raw(low, 1, 3)
    eye = (
        lax.broadcasted_iota(jnp.int32, (CHANNELS, CHANNELS), 0)
        == lax.broadcasted_iota(jnp.int32, (CHANNELS, CHANNELS), 1)
    ).astype(F32)

    def turned(x):
        return lax.dot_general(eye, x, NT, precision=PRECISE, preferred_element_type=F32)

    base0 = embed_ref[0:1, :]
    base1 = embed_ref[1:2, :] - base0
    rows = jnp.concatenate([base0, base1], axis=0)
    sent = jnp.dot(rows, mix_ref[0], precision=PRECISE, preferred_element_type=F32)
    scale = 1.0 / math.sqrt(SLOTS)
    first = jnp.concatenate([radial_ref[0] * sent[0:1], radial_ref[0] * sent[1:2]], axis=0) * scale
    second = radial_ref[1] * scale
    folded = jnp.dot(update_ref[0], mix_ref[1], precision=PRECISE, preferred_element_type=F32)
    mix_t = turned(mix_ref[1])
    l1_ref[...] = left_stack(turned(first)).astype(BF16)
    l2_ref[...] = left_stack(turned(folded)).astype(BF16)
    high, low = split(turned(second))
    l3_ref[...] = jnp.concatenate([high, high, low, jnp.zeros_like(high)], axis=1).astype(BF16)
    high, low = split(folded)
    l5_ref[...] = jnp.concatenate([high, high, high, high, low, low], axis=1).astype(BF16)
    l6_ref[...] = left_stack(first).astype(BF16)
    wide = (CHANNELS, LANES)
    col_ref[0] = jnp.broadcast_to(jnp.sum(mix_t * base0, axis=1, keepdims=True), wide)
    col_ref[1] = jnp.broadcast_to(jnp.sum(mix_t * base1, axis=1, keepdims=True), wide)
    col_ref[2] = jnp.broadcast_to(jnp.sum(update_ref[0] * readout, axis=1, keepdims=True), wide)
    col_ref[3] = jnp.broadcast_to(jnp.sum(update_ref[1] * readout, axis=1, keepdims=True), wide)


def sin_cos(t):
    q = t * t
    s = -1.0 / 39916800.0
    for c in (1.0 / 362880.0, -1.0 / 5040.0, 1.0 / 120.0, -1.0 / 6.0, 1.0):
        s = s * q + c
    k = 1.0 / 479001600.0
    for c in (-1.0 / 3628800.0, 1.0 / 40320.0, -1.0 / 720.0, 1.0 / 24.0, -0.5, 1.0):
        k = k * q + c
    return s * t, k


def wide_row(x, row):
    return jnp.broadcast_to(x[row : row + 1, :], (8, x.shape[1]))


def silu_parts(m):
    sig = 1.0 / (1.0 + jnp.exp(-m))
    return m * sig, sig * (1.0 + m * (1.0 - sig))


def pick(values, lanes):
    return jnp.take_along_axis(values, lanes, axis=1, mode="promise_in_bounds")


def reach(b, first, last):
    return [w for w in range(3) if first <= b - 1 + w <= last]


SIDE_START = {2: 0, 3: LANES, 8: 3 * LANES, 9: 5 * LANES}
SIDE_ROWS = 6 * LANES


def mark(index, ws, target):
    count = len(ws) * LANES
    row_id = (lax.broadcasted_iota(jnp.int32, (count, LANES), 0) + ws[0] * LANES).astype(jnp.int16)
    one, zero = jnp.ones((count, LANES), BF16), jnp.zeros((count, LANES), BF16)
    for k in range(SLOTS):
        wanted = jnp.broadcast_to(index[k : k + 1, :], (16, LANES)).astype(jnp.int16)
        wanted = jnp.concatenate([wanted] * (count // 16), axis=0)
        target[:, k * LANES : (k + 1) * LANES] = jnp.where(row_id == wanted, one, zero)


def window_index(pack, b):
    lanes = slice((b % 4) * LANES, (b % 4 + 1) * LANES)
    return pack[0:8, lanes].astype(jnp.int32) - LANES * (b % 4)


def mark_sides(packs, side):
    for b, start in SIDE_START.items():
        ws = reach(b, 3, 8)
        mark(window_index(packs[b // 4], b), ws, side.at[start : start + len(ws) * LANES])


def forward_parts(packs, weights, xs, sst, kept):
    l1, l2, l3, l5, l6, col = weights
    (widx, kinds, geo, bst, bps, bpr, sent_all, slope) = kept
    centre = 2.0 + 0.5 * lax.broadcasted_iota(jnp.int32, (BASIS, LANES), 0).astype(F32)
    slot = lax.broadcasted_iota(jnp.int32, (SLOTS, LANES), 0)

    def part_rows(value):
        high, low = split(value)
        return jnp.concatenate([high, low], axis=0).astype(BF16)

    def pairs(b):
        pack = packs[b // 4]
        lanes = slice((b % 4) * LANES, (b % 4 + 1) * LANES)
        index = window_index(pack, b)
        widx[b] = index
        inner = index & (LANES - 1)
        part = index >> 7

        def taken(row):
            got = [
                pick(jnp.broadcast_to(xs[b - 1 + w, row : row + 1, :], (SLOTS, LANES)), inner)
                for w in range(3)
            ]
            return jnp.where(part == 0, got[0], jnp.where(part == 1, got[1], got[2]))

        vec = [
            pack[8 + 8 * c : 16 + 8 * c, lanes] + taken(c) - jnp.broadcast_to(xs[b, c : c + 1, :], (SLOTS, LANES))
            for c in range(3)
        ]
        kind = taken(3)
        dist = jnp.sqrt(vec[0] * vec[0] + vec[1] * vec[1] + vec[2] * vec[2] + SOFTENING)
        live = (slot.astype(F32) < jnp.broadcast_to(pack[ROW_COUNT : ROW_COUNT + 1, lanes], (SLOTS, LANES))).astype(F32)
        turns = dist * (1.0 / 12.0)
        turns = turns - jnp.floor(turns + 0.5)
        sine, cosine = sin_cos(turns * math.pi)
        envelope = cosine * cosine * live
        slant = cosine * sine * live * (-math.pi / 6.0)
        if 3 <= b <= 8:
            kinds[b] = kind
            for c in range(3):
                geo[b, c] = vec[c]
            geo[b, 3] = 1.0 / dist
        total = jnp.zeros((BASIS, LANES), F32)
        total_kind = jnp.zeros((BASIS, LANES), F32)
        for k in range(SLOTS):
            away = wide_row(dist, k) - centre
            gauss = jnp.exp(-4.0 * (away * away))
            env_k = wide_row(envelope, k)
            value = gauss * env_k
            total = total + value
            total_kind = total_kind + value * wide_row(kind, k)
            cols = slice(k * LANES, (k + 1) * LANES)
            if 2 <= b <= 9:
                bst[b, :, cols] = part_rows(value)
            if 3 <= b <= 8:
                value = gauss * (wide_row(slant, k) - 8.0 * away * env_k)
                bpr[b, :, cols] = value
                bps[b, :, cols] = part_rows(value)
        high, low = split(jnp.concatenate([total, total_kind], axis=0))
        sst[:, b * LANES : (b + 1) * LANES] = jnp.concatenate([high, low, high], axis=0).astype(BF16)

    for b in range(1, 11):
        pairs(b)

    for b in range(1, 11, 2):
        cols = slice(b * LANES, (b + 2) * LANES)
        value, steep = silu_parts(mm(l1[...], sst[:, cols]))
        sent = mm(l2[...], right_stack(value))
        for i in range(2):
            one = sent[:, i * LANES : (i + 1) * LANES]
            one = one + col[0] + col[1] * jnp.broadcast_to(xs[b + i, 3:4, :], (CHANNELS, LANES))
            sent_all[:, (b + i) * LANES : (b + i + 1) * LANES] = one
        slope[:, cols] = steep


def force_parts(weights, own_hot, side_hot, kept, dg, pulls, met, acc, held, radial, steepness, got, backs):
    l1, l2, l3, l5, l6, col = weights
    (widx, kinds, geo, bst, bps, bpr, sent_all, slope) = kept
    slot = lax.broadcasted_iota(jnp.int32, (SLOTS, LANES), 0)

    def spread(left, b, first, last, sums):
        ws = reach(b, first, last)
        if b in SIDE_START:
            start = SIDE_START[b] + (ws[0] - reach(b, 3, 8)[0]) * LANES
            picked = side_hot[start : start + len(ws) * LANES, :]
        else:
            picked = own_hot[b - 4, ws[0] * LANES : (ws[-1] + 1) * LANES, :]
        out = mm_nt(picked, left)
        for i, w in enumerate(ws):
            target = b - 1 + w
            piece = out[i * LANES : (i + 1) * LANES]
            rows = slice((target - first) * LANES, (target - first + 1) * LANES)
            if (first, target) in started:
                sums[rows, :] += piece
            else:
                sums[rows, :] = piece
                started.add((first, target))

    started = set()

    blocks, inner_blocks = range(2, 10), range(3, 9)
    for b in blocks:
        basis = bst[b]
        radial[b - 2] = mm(l3[...], jnp.concatenate([basis, basis], axis=0))
    for b in inner_blocks:
        basis = bps[b]
        steepness[b - 3] = mm(l3[...], jnp.concatenate([basis, basis], axis=0))

    for b in blocks:
        index = widx[b]
        inner, part = index & (LANES - 1), index >> 7
        lanes = [jnp.broadcast_to(inner[k : k + 1, :], (16, LANES)) for k in range(SLOTS)]
        parts = [jnp.broadcast_to(part[k : k + 1, :], (16, LANES)) for k in range(SLOTS)]
        for u in range(CHANNELS // 16):
            rows = slice(16 * u, 16 * u + 16)
            windows = [sent_all[rows, (b - 1 + w) * LANES : (b + w) * LANES] for w in range(3)]
            message = jnp.zeros((16, LANES), F32)
            for k in range(SLOTS):
                cols = slice(k * LANES, (k + 1) * LANES)
                found = [pick(window, lanes[k]) for window in windows]
                one = jnp.where(parts[k] == 0, found[0], jnp.where(parts[k] == 1, found[1], found[2]))
                if b in inner_blocks:
                    got[b - 3, rows, cols] = one
                message = message + radial[b - 2, rows, cols] * one
            backs[b - 2, rows] = message

    for b in blocks:
        _, steep = silu_parts(backs[b - 2])
        backs[b - 2] = col[3] * steep

    for b in blocks:
        total = [jnp.zeros((8, LANES), F32)] * SLOTS
        for u in range(CHANNELS // 16):
            rows = slice(16 * u, 16 * u + 16)
            low_rows = slice(CHANNELS + 16 * u, CHANNELS + 16 * u + 16)
            back = backs[b - 2, rows]
            for k in range(SLOTS):
                cols = slice(k * LANES, (k + 1) * LANES)
                high, low = split(radial[b - 2, rows, cols] * back)
                held[b - 2, rows, cols] = high.astype(BF16)
                held[b - 2, low_rows, cols] = low.astype(BF16)
                if b in inner_blocks:
                    pull = got[b - 3, rows, cols] * back * steepness[b - 3, rows, cols]
                    total[k] = total[k] + pull[0:8] + pull[8:16]
        if b in inner_blocks:
            for k in range(SLOTS):
                pulls[b, :, k * LANES : (k + 1) * LANES] = total[k]

    for b in blocks:
        spread(held[b - 2], b, 3, 8, dg)

    steeps = []
    for b in range(3, 9, 2):
        high, low = split(dg[(b - 3) * LANES : (b - 1) * LANES, :])
        steeps.append(mm_nt(l5[...], jnp.concatenate([high, low, high], axis=1).astype(BF16)))
    steeps = [
        (steep + jnp.concatenate([col[2], col[2]], axis=1)) * slope[:, b * LANES : (b + 2) * LANES]
        for b, steep in zip(range(3, 9, 2), steeps)
    ]
    sums = [mm(l6[...], right_stack(steep)) for steep in steeps]

    lines = []
    for b in inner_blocks:
        mine = sums[(b - 3) // 2][:, (b - 3) % 2 * LANES : ((b - 3) % 2 + 1) * LANES]
        kind = kinds[b]
        rows = []
        for k in range(SLOTS):
            cols = slice(k * LANES, (k + 1) * LANES)
            weight = mine[0:8] + wide_row(kind, k) * mine[8:16]
            rows.append(jnp.sum(bpr[b, :, cols] * weight + pulls[b, :, cols], axis=0, keepdims=True))
        pull = jnp.concatenate(rows, axis=0) * geo[b, 3]
        pieces = []
        for c in range(3):
            value = pull * geo[b, c]
            if 4 <= b <= 7:
                acc[b - 4, c] = jnp.sum(value, axis=0, keepdims=True)
            pieces.append(split(value))
        parts = []
        for h in range(2):
            for c in range(3):
                parts.append(jnp.concatenate([jnp.where(slot == k, pieces[c][h], 0.0) for k in range(SLOTS)], axis=1))
        lines.append(jnp.concatenate(parts, axis=0).astype(BF16))
    for b in inner_blocks:
        spread(lines[b - 3], b, 4, 7, met)

    high, low = split(met[...])
    column = lax.broadcasted_iota(jnp.int32, (16, 6 * SLOTS), 1)
    column = jnp.where(column < 3 * SLOTS, column, column - 3 * SLOTS)
    first = SLOTS * lax.broadcasted_iota(jnp.int32, (16, 6 * SLOTS), 0)
    choose = jnp.where((column >= first) & (column < first + SLOTS), 1.0, 0.0).astype(BF16)
    back = mm_nt(choose, high.astype(BF16)) + mm_nt(choose, low.astype(BF16))
    away = [jnp.concatenate([acc[i, c] for i in range(SLAB_BLOCKS)], axis=1) for c in range(3)]
    return jnp.concatenate(away, axis=0) - back[0:3]


def fill_region(xs, packs, rows_of):
    for b in range(12):
        lanes = slice((b % 4) * LANES, (b % 4 + 1) * LANES)
        pack = packs[b // 4]
        xs[b, 0:3, :] = rows_of(b // 4)[:, lanes]
        xs[b, 3:4, :] = pack[ROW_KIND : ROW_KIND + 1, lanes]


def lane_total(x):
    x = x[:, 0:LANES] + x[:, LANES : 2 * LANES] + x[:, 2 * LANES : 3 * LANES] + x[:, 3 * LANES : 4 * LANES]
    return jnp.sum(x, axis=1, keepdims=True)


def dot3(a, b):
    return jnp.sum(a * b, axis=0, keepdims=True)


def kept_shapes():
    wide = 12 * LANES
    return [
        ((12, 8, LANES), jnp.int32),
        ((12, 8, LANES), F32),
        ((12, 4, 8, LANES), F32),
        ((12, 16, SLOTS * LANES), BF16),
        ((12, 16, SLOTS * LANES), BF16),
        ((12, 8, SLOTS * LANES), F32),
        ((CHANNELS, wide), F32),
        ((CHANNELS, wide), F32),
    ]


def forward_scratch():
    return [pltpu.VMEM((12, 8, LANES), F32), pltpu.VMEM((48, 12 * LANES), BF16)]


def back_scratch():
    return [
        pltpu.VMEM((6 * LANES, 2 * CHANNELS), F32),
        pltpu.VMEM((12, 8, SLOTS * LANES), F32),
        pltpu.VMEM((SLAB_BLOCKS * LANES, 6 * SLOTS), F32),
        pltpu.VMEM((SLAB_BLOCKS, 3, 1, LANES), F32),
        pltpu.VMEM((8, 2 * CHANNELS, SLOTS * LANES), BF16),
        pltpu.VMEM((8, CHANNELS, SLOTS * LANES), F32),
        pltpu.VMEM((6, CHANNELS, SLOTS * LANES), F32),
        pltpu.VMEM((6, CHANNELS, SLOTS * LANES), F32),
        pltpu.VMEM((8, CHANNELS, LANES), F32),
    ]


def by_parity(sibling, across):
    even = jnp.full(sibling.shape, lax.axis_index("dom") % 2, jnp.int32) == 0
    return jnp.where(even, across, sibling), jnp.where(even, sibling, across)


def first_kernel(x_ref, sibling_ref, po_ref, across_ref, *rest):
    weights, (pl_ref, pr_ref, side_hot, copy_ref), kept, (xs, sst) = rest[:6], rest[6:10], rest[10:18], rest[18:]
    copy_ref[...] = x_ref[...]
    pl_ref[...], pr_ref[...] = by_parity(sibling_ref[...], across_ref[...])
    packs = [pl_ref, po_ref, pr_ref]
    mark_sides(packs, side_hot)
    fill_region(xs, packs, lambda s: packs[s][ROW_X : ROW_X + 3, :])
    forward_parts(packs, weights, xs, sst, kept)


def first_back_kernel(own_hot, side_hot, *rest):
    weights, kept, out_ref, scr = rest[:6], rest[6:14], rest[14], rest[15:]
    out_ref[...] = force_parts(weights, own_hot, side_hot, kept, *scr)


def rows_of(ref):
    return jnp.concatenate([ref[c] for c in range(3)], axis=0)


def block_row(*values):
    values = list(values) + [jnp.zeros((1, LANES), F32)] * (SLAB_BLOCKS - len(values))
    return jnp.concatenate(values, axis=1)


def blend_kernel(images, force_ref, po_ref, before_ref, after_ref, out_ref, sums_ref):
    x = po_ref[ROW_X : ROW_X + 3, :]
    v = po_ref[ROW_V : ROW_V + 3, :]
    force = force_ref[...]
    here = lax.axis_index("img")
    before = jnp.where(here > 0, rows_of(before_ref), 0.0)
    after = jnp.where(here < images - 1, rows_of(after_ref), 0.0)
    tangent = after - before
    plus = after - x
    minus = x - before
    sums = jnp.concatenate(
        [
            dot3(force, tangent),
            dot3(force, force),
            dot3(tangent, tangent),
            dot3(plus, plus),
            dot3(minus, minus),
            dot3(v, v),
            jnp.zeros((2, x.shape[1]), F32),
        ],
        axis=0,
    )
    sums = jnp.broadcast_to(lane_total(sums), (8, LANES))
    sums_ref[...] = sums
    out_ref[0:3, :] = force
    out_ref[3:6, :] = tangent
    out_ref[6:7, :] = block_row(*[sums[i : i + 1] for i in range(4)])
    out_ref[7:8, :] = block_row(sums[4:5], sums[5:6])


def step_numbers(ft, ff, tt, pp, mn, vv, dt, alpha, flagged, climbing, inside):
    root = jnp.sqrt(tt + TINY_VALUE)
    along = ft / root
    spring = SPRING_CONSTANT * (jnp.sqrt(pp) - jnp.sqrt(mn))
    factor = jnp.where(climbing, -2.0 * along, spring - along)
    band = jnp.maximum(ff + 2.0 * factor * along + factor * factor * (tt / (tt + TINY_VALUE)), 0.0)
    new_dt = jnp.where(flagged, 0.5 * dt, jnp.minimum(1.1 * dt, STEP_LIMIT))
    pull = jnp.where(flagged, 0.0, alpha * jnp.sqrt(vv / (band + TINY_VALUE))) + new_dt
    keep = jnp.where(flagged, 0.0, 1.0 - alpha)
    new_alpha = jnp.where(flagged, ALPHA_START, 0.99 * alpha)
    keep = jnp.where(inside, keep, 0.0)
    pull = jnp.where(inside, pull, 0.0)
    return (
        jnp.where(inside, along, 0.0),
        jnp.where(inside, spring, 0.0),
        keep,
        pull,
        pull * factor / root,
        new_dt,
        new_alpha,
    )


def add_kernel(a_ref, b_ref, out_ref):
    out_ref[...] = a_ref[...] + b_ref[...]


def join_kernel(a_ref, b_ref, out_ref):
    count = a_ref.shape[0]
    out_ref[0:count] = a_ref[...]
    out_ref[count : 2 * count] = b_ref[...]


def number_kernel(dt_ref, flag_ref, climb_ref, out_ref):
    flags = [flag_ref[0, s].astype(F32) for s in range(flag_ref.shape[1])]
    for i, value in enumerate([dt_ref[0], climb_ref[0].astype(F32)] + flags):
        out_ref[i : i + 1, :] = jnp.full((1, LANES), value, F32)


def second_kernel(images, domains, number_ref, pl_ref, po_ref, pr_ref, own_ref, near_ref, far_ref, *rest):
    count = 2 if domains == 4 else 1
    parts, rest = rest[:count], rest[count:]
    (own_hot, side_hot), weights, (out_ref, record_ref), scr = rest[:2], rest[2:8], rest[8:10], rest[10:]
    packs = [pl_ref, po_ref, pr_ref]
    here = lax.axis_index("img")
    sums = parts[0][...]
    if domains == 4:
        sums = sums + parts[1][...]
    got = [sums[i : i + 1, :] for i in range(6)]
    if domains == 4:
        for one in (near_ref, far_ref):
            for i in range(6):
                got[i] = got[i] + one[6 + i // 4 : 7 + i // 4, (i % 4) * LANES : (i % 4 + 1) * LANES]
    ft, ff, tt, pp, mn, vv = got
    beside = by_parity(near_ref[0:6, :], far_ref[0:6, :])
    shape = (1, LANES)
    along, spring, keep, pull, side, dt, alpha = step_numbers(
        ft,
        ff,
        tt,
        pp,
        mn,
        vv,
        number_ref[0:1, :],
        jnp.full(shape, ALPHA_START, F32),
        number_ref[2:3, :] == 1.0,
        number_ref[1:2, :] == jnp.full(shape, here, jnp.int32).astype(F32),
        jnp.full(shape, jnp.where((here >= 1) & (here <= images - 2), 1, 0), jnp.int32) == 1,
    )
    messages = [beside[0], own_ref[0:6, :], beside[1]]

    def wide(s):
        return jnp.concatenate([s] * SLAB_BLOCKS, axis=1)

    speeds = [
        wide(keep) * p[ROW_V : ROW_V + 3, :] + wide(pull) * m[0:3, :] + wide(side) * m[3:6, :]
        for p, m in zip(packs, messages)
    ]
    moved = [p[ROW_X : ROW_X + 3, :] + wide(dt) * s for p, s in zip(packs, speeds)]
    xs, sst, kept = scr[0], scr[1], scr[2:10]
    fill_region(xs, packs, lambda s: moved[s])
    forward_parts(packs, weights, xs, sst, kept)
    force = force_parts(weights, own_hot, side_hot, kept, *scr[10:])
    for c in range(3):
        for i in range(SLAB_BLOCKS):
            lanes = slice(i * LANES, (i + 1) * LANES)
            row = 4 * c + i
            out_ref[0, row : row + 1, :] = speeds[1][c : c + 1, lanes]
            out_ref[0, 12 + row : 13 + row, :] = force[c : c + 1, lanes]
            out_ref[0, 24 + row : 25 + row, :] = moved[1][c : c + 1, lanes]
    out_ref[0, 36:37, :] = dt
    out_ref[0, 37:38, :] = alpha
    out_ref[0, 38:40, :] = jnp.broadcast_to(number_ref[3:4, :], (2, LANES))
    record_ref[0:1, :] = along
    record_ref[1:2, :] = spring
    record_ref[2:3, :] = number_ref[1:2, :]


PRODUCTS = (
    [("f", "t"), ("f", "f"), ("t", "t"), ("p", "p"), ("d", "d"), ("v", "v")]
    + [("d", "v"), ("d", "f"), ("d", "t"), ("d", "V"), ("d", "F"), ("d", "T"), ("v", "f"), ("v", "t")]
    + [(a, b) for a in "vft" for b in "VFT"]
)


def gram_kernel(images, *refs):
    parts, (out_ref, state_ref, messages_ref) = refs[:-3], refs[-3:]
    rows = out_ref.shape[0]
    place = 0
    for part in parts:
        messages_ref[place : place + part.shape[0]] = part[...]
        place += part.shape[0]
    here = lax.axis_index("img")
    blank = [jnp.zeros((rows - images, LANES), F32)] if rows > images else []
    zero = jnp.zeros((1, LANES), F32)

    def gathered(row):
        return jnp.concatenate([messages_ref[here ^ i, row : row + 1, :] for i in range(images)] + blank, axis=0)

    def earlier(value):
        return jnp.concatenate([zero, value[0 : rows - 1]], axis=0)

    def later(value):
        return jnp.concatenate([value[1:images], zero] + blank, axis=0)

    number = lax.broadcasted_iota(jnp.int32, (rows, LANES), 0)
    held = number < images
    totals = [jnp.zeros((rows, LANES), F32) for _ in PRODUCTS]
    for row in range(3 * SLAB_BLOCKS):
        v, f, x = gathered(row), gathered(12 + row), gathered(24 + row)
        before = jnp.where(held, earlier(x), 0.0)
        after = later(x)
        t = after - before
        table = {"f": f, "v": v, "t": t, "p": after - x, "d": x - before}
        table["F"], table["V"], table["T"] = earlier(f), earlier(v), earlier(t)
        totals = [old + table[a] * table[b] for old, (a, b) in zip(totals, PRODUCTS)]
        state_ref[row : row + 1, :] = jnp.sum(jnp.where(number == here, t, 0.0), axis=0, keepdims=True)
    lane = lax.broadcasted_iota(jnp.int32, (rows, LANES), 1)
    result = jnp.zeros((rows, LANES), F32)
    for q, one in enumerate(totals):
        one = jnp.broadcast_to(jnp.sum(one, axis=1, keepdims=True), (rows, LANES))
        result = jnp.where(lane == q, one, result)
    out_ref[...] = result
    for i in range(3):
        state_ref[16 + rows * i : 16 + rows * (i + 1), :] = gathered(36 + i)


def final_kernel(images, atoms, own_ref, record_ref, state_ref, *rest):
    parts, (x_ref, v_ref, band_ref, path_ref) = rest[:-4], rest[-4:]
    rows = parts[0].shape[0]
    here = lax.axis_index("img")
    sums = parts[0][...]
    for one in parts[1:]:
        sums = sums + one[...]
    got = {
        pair: jnp.broadcast_to(sums[:, q : q + 1], (rows, LANES)) for q, pair in enumerate(PRODUCTS)
    }
    number = lax.broadcasted_iota(jnp.int32, (rows, LANES), 0)
    inside = (number >= 1) & (number <= images - 2)
    climb = jnp.broadcast_to(record_ref[2:3, :], (rows, LANES))
    dt0, alpha0, flag = (state_ref[16 + rows * i : 16 + rows * (i + 1), :] for i in range(3))
    along, spring, keep, pull, side, dt, _ = step_numbers(
        got["f", "t"],
        got["f", "f"],
        got["t", "t"],
        got["p", "p"],
        got["d", "d"],
        got["v", "v"],
        dt0,
        alpha0,
        flag == 1.0,
        number.astype(F32) == climb,
        inside,
    )

    def shifted(value):
        return jnp.concatenate([jnp.zeros((1, LANES), F32), value[0 : rows - 1]], axis=0)

    now = {"v": dt * keep, "f": dt * pull, "t": dt * side}
    old = {a.upper(): shifted(value) for a, value in now.items()}
    mine = now["v"] * now["v"] * got["v", "v"] + now["f"] * now["f"] * got["f", "f"]
    mine = mine + now["t"] * now["t"] * got["t", "t"]
    cross = now["v"] * now["f"] * got["v", "f"] + now["v"] * now["t"] * got["v", "t"]
    mine = mine + 2.0 * (cross + now["f"] * now["t"] * got["f", "t"])
    both = jnp.zeros((rows, LANES), F32)
    for a in "vft":
        both = both + now[a] * got["d", a]
    for b in "VFT":
        both = both - old[b] * got["d", b]
    for a in "vft":
        for b in "VFT":
            both = both - now[a] * old[b] * got[a, b]
    squared = got["d", "d"] + mine + shifted(mine) + 2.0 * both
    segment = jnp.sqrt(jnp.maximum(squared, 0.0) * (1.0 / (3.0 * atoms)))
    path = jnp.sum(jnp.where(number <= here, segment, 0.0), axis=0, keepdims=True)
    path_ref[...] = path[:, 0:1]
    keep, pull, side, dt, along, spring = (
        jnp.sum(jnp.where(number == here, value, 0.0), axis=0, keepdims=True)
        for value in (keep, pull, side, dt, along, spring)
    )

    for c in range(3):
        speeds, places = [], []
        for i in range(SLAB_BLOCKS):
            row = 4 * c + i
            speed = keep * own_ref[0, row : row + 1, :] + pull * own_ref[0, 12 + row : 13 + row, :]
            speed = speed + side * state_ref[row : row + 1, :]
            speeds.append(speed)
            places.append(own_ref[0, 24 + row : 25 + row, :] + dt * speed)
        v_ref[c] = jnp.concatenate(speeds, axis=1)
        x_ref[c] = jnp.concatenate(places, axis=1)
    band_ref[0] = jnp.concatenate([record_ref[0:1, 0:1], record_ref[1:2, 0:1]], axis=1)
    band_ref[1] = jnp.concatenate([along[:, 0:1], spring[:, 0:1]], axis=1)


VMEM_SPEC = pl.BlockSpec(memory_space=pltpu.VMEM)
SMEM_SPEC = pl.BlockSpec(memory_space=pltpu.SMEM)
HBM_SPEC = pl.BlockSpec(memory_space=pltpu.HBM)


def call(body, outs, scalars, arrays, scratch_shapes=(), flops=0, spec=VMEM_SPEC, vmem=24):
    return pl.pallas_call(
        body,
        out_shape=outs,
        in_specs=[SMEM_SPEC] * len(scalars) + [spec] * len(arrays),
        out_specs=jax.tree.map(lambda _: VMEM_SPEC, outs),
        scratch_shapes=list(scratch_shapes),
        compiler_params=pltpu.CompilerParams(vmem_limit_bytes=vmem * 1024 * 1024),
        cost_estimate=pl.CostEstimate(flops=flops, bytes_accessed=1 << 18, transcendentals=0),
    )(*scalars, *arrays)


def swap(array, axis, partner):
    return lax.ppermute(array, axis, [(i, partner(i)) for i in range(lax.axis_size(axis))])


def exchanged(sums, axis):
    count = lax.axis_size(axis)
    if count == 4:
        return [sums] + [swap(sums, axis, lambda i, by=by: i ^ by) for by in (2, 3, 1)]
    distance = 1
    while distance < count:
        more = swap(sums, axis, lambda i, by=distance: i ^ by)
        sums = call(add_kernel, jax.ShapeDtypeStruct(sums.shape, F32), (), (sums, more))
        distance *= 2
    return [sums]


def collected(array, axis):
    count = lax.axis_size(axis)
    if count == 4:
        far = [swap(array, axis, lambda i, by=by: i ^ by) for by in (3, 2, 1)]
        return [array] + far[::-1]
    distance = 1
    while distance < count:
        more = swap(array, axis, lambda i, by=distance: i ^ by)
        shape = jax.ShapeDtypeStruct((2 * distance,) + array.shape[1:], F32)
        array = call(join_kernel, shape, (), (array, more))
        distance *= 2
    return [array]


def local(
    disp,
    veloc,
    time_step,
    reset_flags,
    climb,
    species,
    neighbours,
    counts,
    lattice,
    embed,
    radial_weight,
    mix_weight,
    update_weight,
    readout,
):
    atoms = disp.shape[2]
    images = lax.axis_size("img")
    domains = lax.axis_size("dom")
    assert disp.shape[0] == 1 and atoms == SLAB_BLOCKS * LANES and domains >= 4
    assert domains & (domains - 1) == 0 and images & (images - 1) == 0
    shape = jax.ShapeDtypeStruct
    x = jnp.transpose(disp, (1, 0, 2))
    v = jnp.transpose(veloc, (1, 0, 2))
    small = (x, v, species, neighbours, counts, embed, readout, radial_weight, mix_weight, update_weight)
    sent, pack = call(
        pack_kernel,
        (shape((PACK_ROWS, atoms), F32), shape((OWN_ROWS, atoms), F32)),
        (),
        (*small, jnp.transpose(lattice, (1, 0, 2))),
        [pltpu.VMEM(a.shape, a.dtype) for a in small] + [pltpu.SemaphoreType.DMA((16,))],
        spec=HBM_SPEC,
        vmem=63,
    )
    sibling = swap(sent, "dom", lambda i: i ^ 1)
    across = swap(sent, "dom", lambda i: (i + 2 * (i % 2) - 1) % domains)
    own_hot, *weights, x_copy = call(
        prepare_kernel,
        (
            shape((SLAB_BLOCKS, 3 * LANES, SLOTS * LANES), BF16),
            shape((CHANNELS, 48), BF16),
            shape((CHANNELS, 192), BF16),
            shape((CHANNELS, 32), BF16),
            shape((CHANNELS, 3 * LANES), BF16),
            shape((16, 192), BF16),
            shape((4, CHANNELS, LANES), F32),
            shape(x.shape, F32),
        ),
        (),
        (pack,),
        flops=100000000,
    )
    before = swap(x_copy, "img", lambda i: (i + 1) % images)
    left, right, side_hot, x_copy, *kept = call(
        first_kernel,
        (
            shape(sent.shape, F32),
            shape(sent.shape, F32),
            shape((SIDE_ROWS, SLOTS * LANES), BF16),
            shape(x.shape, F32),
            *[shape(*one) for one in kept_shapes()],
        ),
        (),
        (x_copy, sibling, pack, across, *weights),
        forward_scratch(),
        flops=1000000000,
    )
    after = swap(x_copy, "img", lambda i: (i - 1) % images)
    force = call(
        first_back_kernel,
        shape((3, atoms), F32),
        (),
        (own_hot, side_hot, *weights, *kept),
        back_scratch(),
        flops=1000000000,
    )
    message, sums = call(
        functools.partial(blend_kernel, images),
        (shape((8, atoms), F32), shape((8, LANES), F32)),
        (),
        (force, pack, before, after),
    )
    far = swap(message, "dom", lambda i: (i + 2 * (i % 2) - 1) % domains)
    if domains == 4:
        parts = [sums, swap(sums, "dom", lambda i: i ^ 2)]
    else:
        parts = exchanged(sums, "dom")
    near = swap(message, "dom", lambda i: i ^ 1)
    numbers = call(number_kernel, shape((8, LANES), F32), (time_step, jnp.transpose(reset_flags), climb), ())
    state, record = call(
        functools.partial(second_kernel, images, domains),
        (shape((1, 40, LANES), F32), shape((3, LANES), F32)),
        (),
        (numbers, left, pack, right, message, near, far, *parts, own_hot, side_hot, *weights),
        forward_scratch() + [pltpu.VMEM(*one) for one in kept_shapes()] + back_scratch(),
        flops=1000000000,
    )
    rows = 8 * ((images + 7) // 8)
    sums, extra = call(
        functools.partial(gram_kernel, images),
        (shape((rows, LANES), F32), shape((16 + 3 * rows, LANES), F32)),
        (),
        collected(state, "img"),
        [pltpu.VMEM((images, 40, LANES), F32)],
    )
    new_x, new_v, records, path = call(
        functools.partial(final_kernel, images, atoms * domains),
        (shape(x.shape, F32), shape(x.shape, F32), shape((2, 1, 2), F32), shape((1, 1), F32)),
        (),
        (state, record, extra, *exchanged(sums, "dom")),
    )
    return (
        jnp.transpose(new_x, (1, 0, 2)),
        jnp.transpose(new_v, (1, 0, 2)),
        jnp.transpose(records, (0, 2, 1)),
        path.reshape(1),
    )


def solution(mesh):
    in_specs = (
        P(("group", "img"), None, "dom"),
        P(("group", "img"), None, "dom"),
        P(("group", "img")),
        P(None, ("group", "img")),
        P("group"),
        P(("group", "dom")),
        P(None, ("group", "dom")),
        P(("group", "dom")),
        P(None, None, ("group", "dom")),
        P(),
        P(),
        P(),
        P(),
        P(),
    )
    out_specs = (
        P(("group", "img"), None, "dom"),
        P(("group", "img"), None, "dom"),
        P(None, None, ("group", "img")),
        P(("group", "img")),
    )
    return jax.shard_map(local, mesh=mesh, in_specs=in_specs, out_specs=out_specs, check_vma=False)
```

```python
import functools
import math

import jax
import jax.numpy as jnp
from jax import lax
from jax.experimental import pallas as pl
from jax.experimental.pallas import tpu as pltpu
from jax.sharding import PartitionSpec as P

F32 = jnp.float32
BF16 = jnp.bfloat16
PRECISE = lax.Precision.HIGHEST
SPRING_CONSTANT = 0.5
ALPHA_START = 0.1
STEP_LIMIT = 0.3
TINY_VALUE = 1e-06
SOFTENING = 0.25
LANES = 128
SLOTS = 8
BASIS = 8
CHANNELS = 64
SLAB_BLOCKS = 4
ROW_X = 32
ROW_COUNT = 35
ROW_KIND = 36
ROW_V = 37
PACK_ROWS = 40
OWN_ROWS = PACK_ROWS + CHANNELS + BASIS
NT = (((1,), (1,)), ((), ()))


def split(x):
    high = x.astype(BF16).astype(F32)
    return high, x - high


def left_stack(w):
    high, low = split(w)
    return jnp.concatenate([high, high, low], axis=1)


def right_stack(x):
    high, low = split(x)
    high = high.astype(BF16)
    return jnp.concatenate([high, low.astype(BF16), high], axis=0)


def pair_stack(x):
    high, low = split(x)
    return jnp.concatenate([high.astype(BF16), low.astype(BF16)], axis=0)


def mm(a, b):
    return jnp.dot(a, b, preferred_element_type=F32)


def mm_nt(a, b):
    return lax.dot_general(a, b, NT, preferred_element_type=F32)


def pack_kernel(*refs):
    sources, (out_ref, own_ref), held, sems = refs[:11], refs[11:13], refs[13:23], refs[23]
    lattice = sources[10]
    pairs = list(zip(sources, held))
    for c in range(3):
        rows = pl.ds(8 + 8 * c, 8)
        pairs += [(lattice.at[c], out_ref.at[rows]), (lattice.at[c], own_ref.at[rows])]
    copies = [pltpu.make_async_copy(a, b, sems.at[i]) for i, (a, b) in enumerate(pairs)]
    for one in copies:
        one.start()
    for one in copies:
        one.wait()
    x, v, species, nbr, counts, embed, readout, radial, mix, update = held
    for ref in (out_ref, own_ref):
        ref[0:8, :] = nbr[...].astype(F32)
        for c in range(3):
            ref[ROW_X + c : ROW_X + c + 1, :] = x[c]
            ref[ROW_V + c : ROW_V + c + 1, :] = v[c]
        ref[ROW_COUNT : ROW_COUNT + 1, :] = counts[...].astype(F32).reshape(1, -1)
        ref[ROW_KIND : ROW_KIND + 1, :] = species[...].astype(F32).reshape(1, -1)
    top, low = PACK_ROWS, PACK_ROWS + CHANNELS
    for i, value in enumerate([mix[0], mix[1], update[0], update[1]]):
        own_ref[top:low, i * LANES : i * LANES + CHANNELS] = value
    for i, value in enumerate([radial[0], radial[1], embed[...], readout[...].reshape(1, CHANNELS)]):
        own_ref[low : low + value.shape[0], i * LANES : i * LANES + CHANNELS] = value


def prepare_kernel(po_ref, *rest):
    own_hot, l1_ref, l2_ref, l3_ref, l5_ref, l6_ref, col_ref, copy_ref = rest
    for b in range(SLAB_BLOCKS):
        mark(window_index(po_ref, b), [0, 1, 2], own_hot.at[b])
    for c in range(3):
        copy_ref[c] = po_ref[ROW_X + c : ROW_X + c + 1, :]

    def raw(first, count, i):
        return po_ref[first : first + count, i * LANES : i * LANES + CHANNELS]

    low = PACK_ROWS + CHANNELS
    mix_ref = [raw(PACK_ROWS, CHANNELS, i) for i in range(2)]
    update_ref = [raw(PACK_ROWS, CHANNELS, 2 + i) for i in range(2)]
    radial_ref = [raw(low, BASIS, i) for i in range(2)]
    embed_ref, readout = raw(low, 2, 2), raw(low, 1, 3)
    eye = (
        lax.broadcasted_iota(jnp.int32, (CHANNELS, CHANNELS), 0)
        == lax.broadcasted_iota(jnp.int32, (CHANNELS, CHANNELS), 1)
    ).astype(F32)

    def turned(x):
        return lax.dot_general(eye, x, NT, precision=PRECISE, preferred_element_type=F32)

    base0 = embed_ref[0:1, :]
    base1 = embed_ref[1:2, :] - base0
    rows = jnp.concatenate([base0, base1], axis=0)
    sent = jnp.dot(rows, mix_ref[0], precision=PRECISE, preferred_element_type=F32)
    scale = 1.0 / math.sqrt(SLOTS)
    first = jnp.concatenate([radial_ref[0] * sent[0:1], radial_ref[0] * sent[1:2]], axis=0) * scale
    second = radial_ref[1] * scale
    folded = jnp.dot(update_ref[0], mix_ref[1], precision=PRECISE, preferred_element_type=F32)
    mix_t = turned(mix_ref[1])
    l1_ref[...] = left_stack(turned(first)).astype(BF16)
    l2_ref[...] = left_stack(turned(folded)).astype(BF16)
    high, low = split(turned(second))
    l3_ref[...] = jnp.concatenate([high, high, low, jnp.zeros_like(high)], axis=1).astype(BF16)
    high, low = split(folded)
    l5_ref[...] = jnp.concatenate([high, high, high, high, low, low], axis=1).astype(BF16)
    l6_ref[...] = left_stack(first).astype(BF16)
    wide = (CHANNELS, LANES)
    col_ref[0] = jnp.broadcast_to(jnp.sum(mix_t * base0, axis=1, keepdims=True), wide)
    col_ref[1] = jnp.broadcast_to(jnp.sum(mix_t * base1, axis=1, keepdims=True), wide)
    col_ref[2] = jnp.broadcast_to(jnp.sum(update_ref[0] * readout, axis=1, keepdims=True), wide)
    col_ref[3] = jnp.broadcast_to(jnp.sum(update_ref[1] * readout, axis=1, keepdims=True), wide)


def sin_cos(t):
    q = t * t
    s = -1.0 / 39916800.0
    for c in (1.0 / 362880.0, -1.0 / 5040.0, 1.0 / 120.0, -1.0 / 6.0, 1.0):
        s = s * q + c
    k = 1.0 / 479001600.0
    for c in (-1.0 / 3628800.0, 1.0 / 40320.0, -1.0 / 720.0, 1.0 / 24.0, -0.5, 1.0):
        k = k * q + c
    return s * t, k


def wide_row(x, row):
    return jnp.broadcast_to(x[row : row + 1, :], (8, x.shape[1]))


def silu_parts(m):
    sig = 1.0 / (1.0 + jnp.exp(-m))
    return m * sig, sig * (1.0 + m * (1.0 - sig))


def pick(values, lanes):
    return jnp.take_along_axis(values, lanes, axis=1, mode="promise_in_bounds")


def reach(b, first, last):
    return [w for w in range(3) if first <= b - 1 + w <= last]


SIDE_START = {2: 0, 3: LANES, 8: 3 * LANES, 9: 5 * LANES}
SIDE_ROWS = 6 * LANES


def mark(index, ws, target):
    count = len(ws) * LANES
    row_id = (lax.broadcasted_iota(jnp.int32, (count, LANES), 0) + ws[0] * LANES).astype(jnp.int16)
    one, zero = jnp.ones((count, LANES), BF16), jnp.zeros((count, LANES), BF16)
    for k in range(SLOTS):
        wanted = jnp.broadcast_to(index[k : k + 1, :], (16, LANES)).astype(jnp.int16)
        wanted = jnp.concatenate([wanted] * (count // 16), axis=0)
        target[:, k * LANES : (k + 1) * LANES] = jnp.where(row_id == wanted, one, zero)


def window_index(pack, b):
    lanes = slice((b % 4) * LANES, (b % 4 + 1) * LANES)
    return pack[0:8, lanes].astype(jnp.int32) - LANES * (b % 4)


def mark_sides(packs, side):
    for b, start in SIDE_START.items():
        ws = reach(b, 3, 8)
        mark(window_index(packs[b // 4], b), ws, side.at[start : start + len(ws) * LANES])


def forward_parts(packs, weights, xs, sst, kept):
    l1, l2, l3, l5, l6, col = weights
    (widx, kinds, geo, bst, bps, bpr, sent_all, slope) = kept
    centre = 2.0 + 0.5 * lax.broadcasted_iota(jnp.int32, (BASIS, LANES), 0).astype(F32)
    slot = lax.broadcasted_iota(jnp.int32, (SLOTS, LANES), 0)

    def part_rows(value):
        high, low = split(value)
        return jnp.concatenate([high, low], axis=0).astype(BF16)

    def pairs(b):
        pack = packs[b // 4]
        lanes = slice((b % 4) * LANES, (b % 4 + 1) * LANES)
        index = window_index(pack, b)
        widx[b] = index
        inner = index & (LANES - 1)
        part = index >> 7

        def taken(row):
            got = [
                pick(jnp.broadcast_to(xs[b - 1 + w, row : row + 1, :], (SLOTS, LANES)), inner)
                for w in range(3)
            ]
            return jnp.where(part == 0, got[0], jnp.where(part == 1, got[1], got[2]))

        vec = [
            pack[8 + 8 * c : 16 + 8 * c, lanes] + taken(c) - jnp.broadcast_to(xs[b, c : c + 1, :], (SLOTS, LANES))
            for c in range(3)
        ]
        kind = taken(3)
        dist = jnp.sqrt(vec[0] * vec[0] + vec[1] * vec[1] + vec[2] * vec[2] + SOFTENING)
        live = (slot.astype(F32) < jnp.broadcast_to(pack[ROW_COUNT : ROW_COUNT + 1, lanes], (SLOTS, LANES))).astype(F32)
        turns = dist * (1.0 / 12.0)
        turns = turns - jnp.floor(turns + 0.5)
        sine, cosine = sin_cos(turns * math.pi)
        envelope = cosine * cosine * live
        slant = cosine * sine * live * (-math.pi / 6.0)
        if 3 <= b <= 8:
            kinds[b] = kind
            for c in range(3):
                geo[b, c] = vec[c]
            geo[b, 3] = 1.0 / dist
        total = jnp.zeros((BASIS, LANES), F32)
        total_kind = jnp.zeros((BASIS, LANES), F32)
        for k in range(SLOTS):
            away = wide_row(dist, k) - centre
            gauss = jnp.exp(-4.0 * (away * away))
            env_k = wide_row(envelope, k)
            value = gauss * env_k
            total = total + value
            total_kind = total_kind + value * wide_row(kind, k)
            cols = slice(k * LANES, (k + 1) * LANES)
            if 2 <= b <= 9:
                bst[b, :, cols] = part_rows(value)
            if 3 <= b <= 8:
                value = gauss * (wide_row(slant, k) - 8.0 * away * env_k)
                bpr[b, :, cols] = value
                bps[b, :, cols] = part_rows(value)
        high, low = split(jnp.concatenate([total, total_kind], axis=0))
        sst[:, b * LANES : (b + 1) * LANES] = jnp.concatenate([high, low, high], axis=0).astype(BF16)

    for b in range(1, 11):
        pairs(b)

    for b in range(1, 11, 2):
        cols = slice(b * LANES, (b + 2) * LANES)
        value, steep = silu_parts(mm(l1[...], sst[:, cols]))
        sent = mm(l2[...], right_stack(value))
        for i in range(2):
            one = sent[:, i * LANES : (i + 1) * LANES]
            one = one + col[0] + col[1] * jnp.broadcast_to(xs[b + i, 3:4, :], (CHANNELS, LANES))
            sent_all[:, (b + i) * LANES : (b + i + 1) * LANES] = one
        slope[:, cols] = steep


def force_parts(weights, own_hot, side_hot, kept, dg, pulls, met, acc, held):
    l1, l2, l3, l5, l6, col = weights
    (widx, kinds, geo, bst, bps, bpr, sent_all, slope) = kept
    slot = lax.broadcasted_iota(jnp.int32, (SLOTS, LANES), 0)

    def marks(b, ws):
        if b in SIDE_START:
            start = SIDE_START[b] + (ws[0] - reach(b, 3, 8)[0]) * LANES
            return side_hot.at[start : start + len(ws) * LANES]
        return own_hot.at[b - 4, ws[0] * LANES : (ws[-1] + 1) * LANES]

    def add_rows(sums, first, b, ws, out):
        for i, w in enumerate(ws):
            target = b - 1 + w
            piece = out[i * LANES : (i + 1) * LANES]
            rows = slice((target - first) * LANES, (target - first + 1) * LANES)
            if (first, target) in started:
                sums[rows, :] += piece
            else:
                sums[rows, :] = piece
                started.add((first, target))

    started = set()

    def block_work(b):
        index = widx[b]
        inner, part = index & (LANES - 1), index >> 7
        basis = bst[b]
        radial = mm(l3[...], jnp.concatenate([basis, basis], axis=0))
        if 3 <= b <= 8:
            basis = bps[b]
            steepness = mm(l3[...], jnp.concatenate([basis, basis], axis=0))
        lanes = [jnp.broadcast_to(inner[k : k + 1, :], (16, LANES)) for k in range(SLOTS)]
        parts = [jnp.broadcast_to(part[k : k + 1, :], (16, LANES)) for k in range(SLOTS)]
        value = held.at[b % 2]
        total = [jnp.zeros((8, LANES), F32)] * SLOTS
        for u in range(CHANNELS // 16):
            rows = slice(16 * u, 16 * u + 16)
            low_rows = slice(CHANNELS + 16 * u, CHANNELS + 16 * u + 16)
            windows = [sent_all[rows, (b - 1 + w) * LANES : (b + w) * LANES] for w in range(3)]
            got = []
            message = jnp.zeros((16, LANES), F32)
            for k in range(SLOTS):
                cols = slice(k * LANES, (k + 1) * LANES)
                found = [pick(window, lanes[k]) for window in windows]
                got.append(jnp.where(parts[k] == 0, found[0], jnp.where(parts[k] == 1, found[1], found[2])))
                message = message + radial[rows, cols] * got[k]
            _, steep = silu_parts(message)
            back = col[3, rows] * steep
            for k in range(SLOTS):
                cols = slice(k * LANES, (k + 1) * LANES)
                high, low = split(radial[rows, cols] * back)
                value[rows, cols] = high.astype(BF16)
                value[low_rows, cols] = low.astype(BF16)
                if 3 <= b <= 8:
                    pull = got[k] * back * steepness[rows, cols]
                    total[k] = total[k] + pull[0:8] + pull[8:16]
            yield
        if 3 <= b <= 8:
            for k in range(SLOTS):
                pulls[b, :, k * LANES : (k + 1) * LANES] = total[k]

    def scatter_work(b):
        ws = reach(b, 3, 8)
        chosen, value = marks(b, ws), held.at[b % 2]
        out = None
        for u in range(4):
            cols = slice(u * 2 * LANES, (u + 1) * 2 * LANES)
            one = mm_nt(chosen[:, cols], value[:, cols])
            out = one if out is None else out + one
            yield
        add_rows(dg, 3, b, ws, out)

    def together(*works):
        works = list(works)
        while works:
            works = [work for work in works if next(work, "end") != "end"]

    together(block_work(2))
    for b in range(3, 10):
        together(scatter_work(b - 1), block_work(b))
    together(scatter_work(9))

    def finish(b, sums):
        kind = kinds[b]
        rows = []
        for k in range(SLOTS):
            cols = slice(k * LANES, (k + 1) * LANES)
            weight = sums[0:8] + wide_row(kind, k) * sums[8:16]
            rows.append(jnp.sum(bpr[b, :, cols] * weight + pulls[b, :, cols], axis=0, keepdims=True))
        pull = jnp.concatenate(rows, axis=0) * geo[b, 3]
        pieces = []
        for c in range(3):
            value = pull * geo[b, c]
            if 4 <= b <= 7:
                acc[b - 4, c] = jnp.sum(value, axis=0, keepdims=True)
            pieces.append(split(value))
        lines = []
        for h in range(2):
            for c in range(3):
                lines.append(jnp.concatenate([jnp.where(slot == k, pieces[c][h], 0.0) for k in range(SLOTS)], axis=1))
        ws = reach(b, 4, 7)
        out = mm_nt(jnp.concatenate(lines, axis=0).astype(BF16), marks(b, ws)[...])
        for c in range(3):
            both = out[8 * c : 8 * c + 8] + out[24 + 8 * c : 32 + 8 * c]
            for i, w in enumerate(ws):
                target = b - 5 + w
                piece = both[:, i * LANES : (i + 1) * LANES]
                if (c, target) in met_blocks:
                    met[target, c] += piece
                else:
                    met[target, c] = piece
                    met_blocks.add((c, target))

    met_blocks = set()

    for b in range(3, 9, 2):
        cols = slice(b * LANES, (b + 2) * LANES)
        high, low = split(dg[(b - 3) * LANES : (b - 1) * LANES, :])
        steep = mm_nt(l5[...], jnp.concatenate([high, low, high], axis=1).astype(BF16))
        steep = steep + jnp.concatenate([col[2], col[2]], axis=1)
        sums = mm(l6[...], right_stack(steep * slope[:, cols]))
        for i in range(2):
            finish(b + i, sums[:, i * LANES : (i + 1) * LANES])

    away = []
    for c in range(3):
        back = [acc[i, c] - jnp.sum(met[i, c], axis=0, keepdims=True) for i in range(SLAB_BLOCKS)]
        away.append(jnp.concatenate(back, axis=1))
    return jnp.concatenate(away, axis=0)


def fill_region(xs, packs, rows_of):
    for b in range(12):
        lanes = slice((b % 4) * LANES, (b % 4 + 1) * LANES)
        pack = packs[b // 4]
        xs[b, 0:3, :] = rows_of(b // 4)[:, lanes]
        xs[b, 3:4, :] = pack[ROW_KIND : ROW_KIND + 1, lanes]


def lane_total(x):
    x = x[:, 0:LANES] + x[:, LANES : 2 * LANES] + x[:, 2 * LANES : 3 * LANES] + x[:, 3 * LANES : 4 * LANES]
    return jnp.sum(x, axis=1, keepdims=True)


def dot3(a, b):
    return jnp.sum(a * b, axis=0, keepdims=True)


def kept_shapes():
    wide = 12 * LANES
    return [
        ((12, 8, LANES), jnp.int32),
        ((12, 8, LANES), F32),
        ((12, 4, 8, LANES), F32),
        ((12, 16, SLOTS * LANES), BF16),
        ((12, 16, SLOTS * LANES), BF16),
        ((12, 8, SLOTS * LANES), F32),
        ((CHANNELS, wide), F32),
        ((CHANNELS, wide), F32),
    ]


def forward_scratch():
    return [pltpu.VMEM((12, 8, LANES), F32), pltpu.VMEM((48, 12 * LANES), BF16)]


def back_scratch():
    return [
        pltpu.VMEM((6 * LANES, 2 * CHANNELS), F32),
        pltpu.VMEM((12, 8, SLOTS * LANES), F32),
        pltpu.VMEM((SLAB_BLOCKS, 3, SLOTS, LANES), F32),
        pltpu.VMEM((SLAB_BLOCKS, 3, 1, LANES), F32),
        pltpu.VMEM((2, 2 * CHANNELS, SLOTS * LANES), BF16),
    ]


def by_parity(sibling, across):
    even = jnp.full(sibling.shape, lax.axis_index("dom") % 2, jnp.int32) == 0
    return jnp.where(even, across, sibling), jnp.where(even, sibling, across)


def first_kernel(x_ref, sibling_ref, po_ref, across_ref, *rest):
    weights, (pl_ref, pr_ref, side_hot, copy_ref), kept, (xs, sst) = rest[:6], rest[6:10], rest[10:18], rest[18:]
    copy_ref[...] = x_ref[...]
    pl_ref[...], pr_ref[...] = by_parity(sibling_ref[...], across_ref[...])
    packs = [pl_ref, po_ref, pr_ref]
    mark_sides(packs, side_hot)
    fill_region(xs, packs, lambda s: packs[s][ROW_X : ROW_X + 3, :])
    forward_parts(packs, weights, xs, sst, kept)


def first_back_kernel(own_hot, side_hot, *rest):
    weights, kept, out_ref, scr = rest[:6], rest[6:14], rest[14], rest[15:]
    out_ref[...] = force_parts(weights, own_hot, side_hot, kept, *scr)


def rows_of(ref):
    return jnp.concatenate([ref[c] for c in range(3)], axis=0)


def block_row(*values):
    values = list(values) + [jnp.zeros((1, LANES), F32)] * (SLAB_BLOCKS - len(values))
    return jnp.concatenate(values, axis=1)


def blend_kernel(images, force_ref, po_ref, before_ref, after_ref, out_ref, sums_ref):
    x = po_ref[ROW_X : ROW_X + 3, :]
    v = po_ref[ROW_V : ROW_V + 3, :]
    force = force_ref[...]
    here = lax.axis_index("img")
    before = jnp.where(here > 0, rows_of(before_ref), 0.0)
    after = jnp.where(here < images - 1, rows_of(after_ref), 0.0)
    tangent = after - before
    plus = after - x
    minus = x - before
    sums = jnp.concatenate(
        [
            dot3(force, tangent),
            dot3(force, force),
            dot3(tangent, tangent),
            dot3(plus, plus),
            dot3(minus, minus),
            dot3(v, v),
            jnp.zeros((2, x.shape[1]), F32),
        ],
        axis=0,
    )
    sums = jnp.broadcast_to(lane_total(sums), (8, LANES))
    sums_ref[...] = sums
    out_ref[0:3, :] = force
    out_ref[3:6, :] = tangent
    out_ref[6:7, :] = block_row(*[sums[i : i + 1] for i in range(4)])
    out_ref[7:8, :] = block_row(sums[4:5], sums[5:6])


def step_numbers(ft, ff, tt, pp, mn, vv, dt, alpha, flagged, climbing, inside):
    root = jnp.sqrt(tt + TINY_VALUE)
    along = ft / root
    spring = SPRING_CONSTANT * (jnp.sqrt(pp) - jnp.sqrt(mn))
    factor = jnp.where(climbing, -2.0 * along, spring - along)
    band = jnp.maximum(ff + 2.0 * factor * along + factor * factor * (tt / (tt + TINY_VALUE)), 0.0)
    new_dt = jnp.where(flagged, 0.5 * dt, jnp.minimum(1.1 * dt, STEP_LIMIT))
    pull = jnp.where(flagged, 0.0, alpha * jnp.sqrt(vv / (band + TINY_VALUE))) + new_dt
    keep = jnp.where(flagged, 0.0, 1.0 - alpha)
    new_alpha = jnp.where(flagged, ALPHA_START, 0.99 * alpha)
    keep = jnp.where(inside, keep, 0.0)
    pull = jnp.where(inside, pull, 0.0)
    return (
        jnp.where(inside, along, 0.0),
        jnp.where(inside, spring, 0.0),
        keep,
        pull,
        pull * factor / root,
        new_dt,
        new_alpha,
    )


def add_kernel(a_ref, b_ref, out_ref):
    out_ref[...] = a_ref[...] + b_ref[...]


def join_kernel(a_ref, b_ref, out_ref):
    count = a_ref.shape[0]
    out_ref[0:count] = a_ref[...]
    out_ref[count : 2 * count] = b_ref[...]


def number_kernel(dt_ref, flag_ref, climb_ref, out_ref):
    flags = [flag_ref[0, s].astype(F32) for s in range(flag_ref.shape[1])]
    for i, value in enumerate([dt_ref[0], climb_ref[0].astype(F32)] + flags):
        out_ref[i : i + 1, :] = jnp.full((1, LANES), value, F32)


def second_kernel(images, domains, number_ref, pl_ref, po_ref, pr_ref, own_ref, near_ref, far_ref, *rest):
    count = 2 if domains == 4 else 1
    parts, rest = rest[:count], rest[count:]
    (own_hot, side_hot), weights, (out_ref, record_ref), scr = rest[:2], rest[2:8], rest[8:10], rest[10:]
    packs = [pl_ref, po_ref, pr_ref]
    here = lax.axis_index("img")
    sums = parts[0][...]
    if domains == 4:
        sums = sums + parts[1][...]
    got = [sums[i : i + 1, :] for i in range(6)]
    if domains == 4:
        for one in (near_ref, far_ref):
            for i in range(6):
                got[i] = got[i] + one[6 + i // 4 : 7 + i // 4, (i % 4) * LANES : (i % 4 + 1) * LANES]
    ft, ff, tt, pp, mn, vv = got
    beside = by_parity(near_ref[0:6, :], far_ref[0:6, :])
    shape = (1, LANES)
    along, spring, keep, pull, side, dt, alpha = step_numbers(
        ft,
        ff,
        tt,
        pp,
        mn,
        vv,
        number_ref[0:1, :],
        jnp.full(shape, ALPHA_START, F32),
        number_ref[2:3, :] == 1.0,
        number_ref[1:2, :] == jnp.full(shape, here, jnp.int32).astype(F32),
        jnp.full(shape, jnp.where((here >= 1) & (here <= images - 2), 1, 0), jnp.int32) == 1,
    )
    messages = [beside[0], own_ref[0:6, :], beside[1]]

    def wide(s):
        return jnp.concatenate([s] * SLAB_BLOCKS, axis=1)

    speeds = [
        wide(keep) * p[ROW_V : ROW_V + 3, :] + wide(pull) * m[0:3, :] + wide(side) * m[3:6, :]
        for p, m in zip(packs, messages)
    ]
    moved = [p[ROW_X : ROW_X + 3, :] + wide(dt) * s for p, s in zip(packs, speeds)]
    xs, sst, kept = scr[0], scr[1], scr[2:10]
    fill_region(xs, packs, lambda s: moved[s])
    forward_parts(packs, weights, xs, sst, kept)
    force = force_parts(weights, own_hot, side_hot, kept, *scr[10:])
    for c in range(3):
        for i in range(SLAB_BLOCKS):
            lanes = slice(i * LANES, (i + 1) * LANES)
            row = 4 * c + i
            out_ref[0, row : row + 1, :] = speeds[1][c : c + 1, lanes]
            out_ref[0, 12 + row : 13 + row, :] = force[c : c + 1, lanes]
            out_ref[0, 24 + row : 25 + row, :] = moved[1][c : c + 1, lanes]
    out_ref[0, 36:37, :] = dt
    out_ref[0, 37:38, :] = alpha
    out_ref[0, 38:40, :] = jnp.broadcast_to(number_ref[3:4, :], (2, LANES))
    record_ref[0:1, :] = along
    record_ref[1:2, :] = spring
    record_ref[2:3, :] = number_ref[1:2, :]


PRODUCTS = (
    [("f", "t"), ("f", "f"), ("t", "t"), ("p", "p"), ("d", "d"), ("v", "v")]
    + [("d", "v"), ("d", "f"), ("d", "t"), ("d", "V"), ("d", "F"), ("d", "T"), ("v", "f"), ("v", "t")]
    + [(a, b) for a in "vft" for b in "VFT"]
)


def gram_kernel(images, *refs):
    parts, (out_ref, state_ref, messages_ref) = refs[:-3], refs[-3:]
    rows = out_ref.shape[0]
    place = 0
    for part in parts:
        messages_ref[place : place + part.shape[0]] = part[...]
        place += part.shape[0]
    here = lax.axis_index("img")
    blank = [jnp.zeros((rows - images, LANES), F32)] if rows > images else []
    zero = jnp.zeros((1, LANES), F32)

    def gathered(row):
        return jnp.concatenate([messages_ref[here ^ i, row : row + 1, :] for i in range(images)] + blank, axis=0)

    def earlier(value):
        return jnp.concatenate([zero, value[0 : rows - 1]], axis=0)

    def later(value):
        return jnp.concatenate([value[1:images], zero] + blank, axis=0)

    number = lax.broadcasted_iota(jnp.int32, (rows, LANES), 0)
    held = number < images
    totals = [jnp.zeros((rows, LANES), F32) for _ in PRODUCTS]
    for row in range(3 * SLAB_BLOCKS):
        v, f, x = gathered(row), gathered(12 + row), gathered(24 + row)
        before = jnp.where(held, earlier(x), 0.0)
        after = later(x)
        t = after - before
        table = {"f": f, "v": v, "t": t, "p": after - x, "d": x - before}
        table["F"], table["V"], table["T"] = earlier(f), earlier(v), earlier(t)
        totals = [old + table[a] * table[b] for old, (a, b) in zip(totals, PRODUCTS)]
        state_ref[row : row + 1, :] = jnp.sum(jnp.where(number == here, t, 0.0), axis=0, keepdims=True)
    lane = lax.broadcasted_iota(jnp.int32, (rows, LANES), 1)
    result = jnp.zeros((rows, LANES), F32)
    for q, one in enumerate(totals):
        one = jnp.broadcast_to(jnp.sum(one, axis=1, keepdims=True), (rows, LANES))
        result = jnp.where(lane == q, one, result)
    out_ref[...] = result
    for i in range(3):
        state_ref[16 + rows * i : 16 + rows * (i + 1), :] = gathered(36 + i)


def final_kernel(images, atoms, own_ref, record_ref, state_ref, *rest):
    parts, (x_ref, v_ref, band_ref, path_ref) = rest[:-4], rest[-4:]
    rows = parts[0].shape[0]
    here = lax.axis_index("img")
    sums = parts[0][...]
    for one in parts[1:]:
        sums = sums + one[...]
    got = {
        pair: jnp.broadcast_to(sums[:, q : q + 1], (rows, LANES)) for q, pair in enumerate(PRODUCTS)
    }
    number = lax.broadcasted_iota(jnp.int32, (rows, LANES), 0)
    inside = (number >= 1) & (number <= images - 2)
    climb = jnp.broadcast_to(record_ref[2:3, :], (rows, LANES))
    dt0, alpha0, flag = (state_ref[16 + rows * i : 16 + rows * (i + 1), :] for i in range(3))
    along, spring, keep, pull, side, dt, _ = step_numbers(
        got["f", "t"],
        got["f", "f"],
        got["t", "t"],
        got["p", "p"],
        got["d", "d"],
        got["v", "v"],
        dt0,
        alpha0,
        flag == 1.0,
        number.astype(F32) == climb,
        inside,
    )

    def shifted(value):
        return jnp.concatenate([jnp.zeros((1, LANES), F32), value[0 : rows - 1]], axis=0)

    now = {"v": dt * keep, "f": dt * pull, "t": dt * side}
    old = {a.upper(): shifted(value) for a, value in now.items()}
    mine = now["v"] * now["v"] * got["v", "v"] + now["f"] * now["f"] * got["f", "f"]
    mine = mine + now["t"] * now["t"] * got["t", "t"]
    cross = now["v"] * now["f"] * got["v", "f"] + now["v"] * now["t"] * got["v", "t"]
    mine = mine + 2.0 * (cross + now["f"] * now["t"] * got["f", "t"])
    both = jnp.zeros((rows, LANES), F32)
    for a in "vft":
        both = both + now[a] * got["d", a]
    for b in "VFT":
        both = both - old[b] * got["d", b]
    for a in "vft":
        for b in "VFT":
            both = both - now[a] * old[b] * got[a, b]
    squared = got["d", "d"] + mine + shifted(mine) + 2.0 * both
    segment = jnp.sqrt(jnp.maximum(squared, 0.0) * (1.0 / (3.0 * atoms)))
    path = jnp.sum(jnp.where(number <= here, segment, 0.0), axis=0, keepdims=True)
    path_ref[...] = path[:, 0:1]
    keep, pull, side, dt, along, spring = (
        jnp.sum(jnp.where(number == here, value, 0.0), axis=0, keepdims=True)
        for value in (keep, pull, side, dt, along, spring)
    )

    for c in range(3):
        speeds, places = [], []
        for i in range(SLAB_BLOCKS):
            row = 4 * c + i
            speed = keep * own_ref[0, row : row + 1, :] + pull * own_ref[0, 12 + row : 13 + row, :]
            speed = speed + side * state_ref[row : row + 1, :]
            speeds.append(speed)
            places.append(own_ref[0, 24 + row : 25 + row, :] + dt * speed)
        v_ref[c] = jnp.concatenate(speeds, axis=1)
        x_ref[c] = jnp.concatenate(places, axis=1)
    band_ref[0] = jnp.concatenate([record_ref[0:1, 0:1], record_ref[1:2, 0:1]], axis=1)
    band_ref[1] = jnp.concatenate([along[:, 0:1], spring[:, 0:1]], axis=1)


VMEM_SPEC = pl.BlockSpec(memory_space=pltpu.VMEM)
SMEM_SPEC = pl.BlockSpec(memory_space=pltpu.SMEM)
HBM_SPEC = pl.BlockSpec(memory_space=pltpu.HBM)


def call(body, outs, scalars, arrays, scratch_shapes=(), flops=0, spec=VMEM_SPEC, vmem=24):
    return pl.pallas_call(
        body,
        out_shape=outs,
        in_specs=[SMEM_SPEC] * len(scalars) + [spec] * len(arrays),
        out_specs=jax.tree.map(lambda _: VMEM_SPEC, outs),
        scratch_shapes=list(scratch_shapes),
        compiler_params=pltpu.CompilerParams(vmem_limit_bytes=vmem * 1024 * 1024),
        cost_estimate=pl.CostEstimate(flops=flops, bytes_accessed=1 << 18, transcendentals=0),
    )(*scalars, *arrays)


def swap(array, axis, partner):
    return lax.ppermute(array, axis, [(i, partner(i)) for i in range(lax.axis_size(axis))])


def exchanged(sums, axis):
    count = lax.axis_size(axis)
    if count == 4:
        return [sums] + [swap(sums, axis, lambda i, by=by: i ^ by) for by in (2, 3, 1)]
    distance = 1
    while distance < count:
        more = swap(sums, axis, lambda i, by=distance: i ^ by)
        sums = call(add_kernel, jax.ShapeDtypeStruct(sums.shape, F32), (), (sums, more))
        distance *= 2
    return [sums]


def collected(array, axis):
    count = lax.axis_size(axis)
    if count == 4:
        far = [swap(array, axis, lambda i, by=by: i ^ by) for by in (3, 2, 1)]
        return [array] + far[::-1]
    distance = 1
    while distance < count:
        more = swap(array, axis, lambda i, by=distance: i ^ by)
        shape = jax.ShapeDtypeStruct((2 * distance,) + array.shape[1:], F32)
        array = call(join_kernel, shape, (), (array, more))
        distance *= 2
    return [array]


def local(
    disp,
    veloc,
    time_step,
    reset_flags,
    climb,
    species,
    neighbours,
    counts,
    lattice,
    embed,
    radial_weight,
    mix_weight,
    update_weight,
    readout,
):
    atoms = disp.shape[2]
    images = lax.axis_size("img")
    domains = lax.axis_size("dom")
    assert disp.shape[0] == 1 and atoms == SLAB_BLOCKS * LANES and domains >= 4
    assert domains & (domains - 1) == 0 and images & (images - 1) == 0
    shape = jax.ShapeDtypeStruct
    x = jnp.transpose(disp, (1, 0, 2))
    v = jnp.transpose(veloc, (1, 0, 2))
    small = (x, v, species, neighbours, counts, embed, readout, radial_weight, mix_weight, update_weight)
    sent, pack = call(
        pack_kernel,
        (shape((PACK_ROWS, atoms), F32), shape((OWN_ROWS, atoms), F32)),
        (),
        (*small, jnp.transpose(lattice, (1, 0, 2))),
        [pltpu.VMEM(a.shape, a.dtype) for a in small] + [pltpu.SemaphoreType.DMA((16,))],
        spec=HBM_SPEC,
        vmem=63,
    )
    sibling = swap(sent, "dom", lambda i: i ^ 1)
    across = swap(sent, "dom", lambda i: (i + 2 * (i % 2) - 1) % domains)
    own_hot, *weights, x_copy = call(
        prepare_kernel,
        (
            shape((SLAB_BLOCKS, 3 * LANES, SLOTS * LANES), BF16),
            shape((CHANNELS, 48), BF16),
            shape((CHANNELS, 192), BF16),
            shape((CHANNELS, 32), BF16),
            shape((CHANNELS, 3 * LANES), BF16),
            shape((16, 192), BF16),
            shape((4, CHANNELS, LANES), F32),
            shape(x.shape, F32),
        ),
        (),
        (pack,),
        flops=100000000,
    )
    before = swap(x_copy, "img", lambda i: (i + 1) % images)
    left, right, side_hot, x_copy, *kept = call(
        first_kernel,
        (
            shape(sent.shape, F32),
            shape(sent.shape, F32),
            shape((SIDE_ROWS, SLOTS * LANES), BF16),
            shape(x.shape, F32),
            *[shape(*one) for one in kept_shapes()],
        ),
        (),
        (x_copy, sibling, pack, across, *weights),
        forward_scratch(),
        flops=1000000000,
    )
    after = swap(x_copy, "img", lambda i: (i - 1) % images)
    force = call(
        first_back_kernel,
        shape((3, atoms), F32),
        (),
        (own_hot, side_hot, *weights, *kept),
        back_scratch(),
        flops=1000000000,
    )
    message, sums = call(
        functools.partial(blend_kernel, images),
        (shape((8, atoms), F32), shape((8, LANES), F32)),
        (),
        (force, pack, before, after),
    )
    far = swap(message, "dom", lambda i: (i + 2 * (i % 2) - 1) % domains)
    if domains == 4:
        parts = [sums, swap(sums, "dom", lambda i: i ^ 2)]
    else:
        parts = exchanged(sums, "dom")
    near = swap(message, "dom", lambda i: i ^ 1)
    numbers = call(number_kernel, shape((8, LANES), F32), (time_step, jnp.transpose(reset_flags), climb), ())
    state, record = call(
        functools.partial(second_kernel, images, domains),
        (shape((1, 40, LANES), F32), shape((3, LANES), F32)),
        (),
        (numbers, left, pack, right, message, near, far, *parts, own_hot, side_hot, *weights),
        forward_scratch() + [pltpu.VMEM(*one) for one in kept_shapes()] + back_scratch(),
        flops=1000000000,
    )
    rows = 8 * ((images + 7) // 8)
    sums, extra = call(
        functools.partial(gram_kernel, images),
        (shape((rows, LANES), F32), shape((16 + 3 * rows, LANES), F32)),
        (),
        collected(state, "img"),
        [pltpu.VMEM((images, 40, LANES), F32)],
    )
    new_x, new_v, records, path = call(
        functools.partial(final_kernel, images, atoms * domains),
        (shape(x.shape, F32), shape(x.shape, F32), shape((2, 1, 2), F32), shape((1, 1), F32)),
        (),
        (state, record, extra, *exchanged(sums, "dom")),
    )
    return (
        jnp.transpose(new_x, (1, 0, 2)),
        jnp.transpose(new_v, (1, 0, 2)),
        jnp.transpose(records, (0, 2, 1)),
        path.reshape(1),
    )


def solution(mesh):
    in_specs = (
        P(("group", "img"), None, "dom"),
        P(("group", "img"), None, "dom"),
        P(("group", "img")),
        P(None, ("group", "img")),
        P("group"),
        P(("group", "dom")),
        P(None, ("group", "dom")),
        P(("group", "dom")),
        P(None, None, ("group", "dom")),
        P(),
        P(),
        P(),
        P(),
        P(),
    )
    out_specs = (
        P(("group", "img"), None, "dom"),
        P(("group", "img"), None, "dom"),
        P(None, None, ("group", "img")),
        P(("group", "img")),
    )
    return jax.shard_map(local, mesh=mesh, in_specs=in_specs, out_specs=out_specs, check_vma=False)
```

```python
import functools
import math

import jax
import jax.numpy as jnp
from jax import lax
from jax.experimental import pallas as pl
from jax.experimental.pallas import tpu as pltpu
from jax.sharding import PartitionSpec as P

F32 = jnp.float32
BF16 = jnp.bfloat16
PRECISE = lax.Precision.HIGHEST
SPRING_CONSTANT = 0.5
ALPHA_START = 0.1
STEP_LIMIT = 0.3
TINY_VALUE = 1e-06
SOFTENING = 0.25
LANES = 128
SLOTS = 8
BASIS = 8
CHANNELS = 64
SLAB_BLOCKS = 4
ROW_X = 32
ROW_COUNT = 35
ROW_KIND = 36
ROW_V = 37
PACK_ROWS = 40
OWN_ROWS = PACK_ROWS + CHANNELS + BASIS
NT = (((1,), (1,)), ((), ()))


def split(x):
    high = x.astype(BF16).astype(F32)
    return high, x - high


def left_stack(w):
    high, low = split(w)
    return jnp.concatenate([high, high, low], axis=1)


def right_stack(x):
    high, low = split(x)
    high = high.astype(BF16)
    return jnp.concatenate([high, low.astype(BF16), high], axis=0)


def pair_stack(x):
    high, low = split(x)
    return jnp.concatenate([high.astype(BF16), low.astype(BF16)], axis=0)


def mm(a, b):
    return jnp.dot(a, b, preferred_element_type=F32)


def mm_nt(a, b):
    return lax.dot_general(a, b, NT, preferred_element_type=F32)


def pack_kernel(*refs):
    sources, (out_ref, own_ref), held, sems = refs[:11], refs[11:13], refs[13:23], refs[23]
    lattice = sources[10]
    pairs = list(zip(sources, held))
    for c in range(3):
        rows = pl.ds(8 + 8 * c, 8)
        pairs += [(lattice.at[c], out_ref.at[rows]), (lattice.at[c], own_ref.at[rows])]
    copies = [pltpu.make_async_copy(a, b, sems.at[i]) for i, (a, b) in enumerate(pairs)]
    for one in copies:
        one.start()
    for one in copies:
        one.wait()
    x, v, species, nbr, counts, embed, readout, radial, mix, update = held
    for ref in (out_ref, own_ref):
        ref[0:8, :] = nbr[...].astype(F32)
        for c in range(3):
            ref[ROW_X + c : ROW_X + c + 1, :] = x[c]
            ref[ROW_V + c : ROW_V + c + 1, :] = v[c]
        ref[ROW_COUNT : ROW_COUNT + 1, :] = counts[...].astype(F32).reshape(1, -1)
        ref[ROW_KIND : ROW_KIND + 1, :] = species[...].astype(F32).reshape(1, -1)
    top, low = PACK_ROWS, PACK_ROWS + CHANNELS
    for i, value in enumerate([mix[0], mix[1], update[0], update[1]]):
        own_ref[top:low, i * LANES : i * LANES + CHANNELS] = value
    for i, value in enumerate([radial[0], radial[1], embed[...], readout[...].reshape(1, CHANNELS)]):
        own_ref[low : low + value.shape[0], i * LANES : i * LANES + CHANNELS] = value


def prepare_kernel(po_ref, *rest):
    own_hot, l1_ref, l2_ref, l3_ref, l5_ref, l6_ref, col_ref, copy_ref = rest
    for b in range(SLAB_BLOCKS):
        mark(window_index(po_ref, b), [0, 1, 2], own_hot.at[b])
    for c in range(3):
        copy_ref[c] = po_ref[ROW_X + c : ROW_X + c + 1, :]

    def raw(first, count, i):
        return po_ref[first : first + count, i * LANES : i * LANES + CHANNELS]

    low = PACK_ROWS + CHANNELS
    mix_ref = [raw(PACK_ROWS, CHANNELS, i) for i in range(2)]
    update_ref = [raw(PACK_ROWS, CHANNELS, 2 + i) for i in range(2)]
    radial_ref = [raw(low, BASIS, i) for i in range(2)]
    embed_ref, readout = raw(low, 2, 2), raw(low, 1, 3)
    eye = (
        lax.broadcasted_iota(jnp.int32, (CHANNELS, CHANNELS), 0)
        == lax.broadcasted_iota(jnp.int32, (CHANNELS, CHANNELS), 1)
    ).astype(F32)

    def turned(x):
        return lax.dot_general(eye, x, NT, precision=PRECISE, preferred_element_type=F32)

    base0 = embed_ref[0:1, :]
    base1 = embed_ref[1:2, :] - base0
    rows = jnp.concatenate([base0, base1], axis=0)
    sent = jnp.dot(rows, mix_ref[0], precision=PRECISE, preferred_element_type=F32)
    scale = 1.0 / math.sqrt(SLOTS)
    first = jnp.concatenate([radial_ref[0] * sent[0:1], radial_ref[0] * sent[1:2]], axis=0) * scale
    second = radial_ref[1] * scale
    folded = jnp.dot(update_ref[0], mix_ref[1], precision=PRECISE, preferred_element_type=F32)
    mix_t = turned(mix_ref[1])
    l1_ref[...] = left_stack(turned(first)).astype(BF16)
    l2_ref[...] = left_stack(turned(folded)).astype(BF16)
    high, low = split(turned(second))
    l3_ref[...] = jnp.concatenate([high, high, low, jnp.zeros_like(high)], axis=1).astype(BF16)
    high, low = split(folded)
    l5_ref[...] = jnp.concatenate([high, high, high, high, low, low], axis=1).astype(BF16)
    l6_ref[...] = left_stack(first).astype(BF16)
    wide = (CHANNELS, LANES)
    col_ref[0] = jnp.broadcast_to(jnp.sum(mix_t * base0, axis=1, keepdims=True), wide)
    col_ref[1] = jnp.broadcast_to(jnp.sum(mix_t * base1, axis=1, keepdims=True), wide)
    col_ref[2] = jnp.broadcast_to(jnp.sum(update_ref[0] * readout, axis=1, keepdims=True), wide)
    col_ref[3] = jnp.broadcast_to(jnp.sum(update_ref[1] * readout, axis=1, keepdims=True), wide)


def sin_cos(t):
    q = t * t
    s = -1.0 / 39916800.0
    for c in (1.0 / 362880.0, -1.0 / 5040.0, 1.0 / 120.0, -1.0 / 6.0, 1.0):
        s = s * q + c
    k = 1.0 / 479001600.0
    for c in (-1.0 / 3628800.0, 1.0 / 40320.0, -1.0 / 720.0, 1.0 / 24.0, -0.5, 1.0):
        k = k * q + c
    return s * t, k


def wide_row(x, row):
    return jnp.broadcast_to(x[row : row + 1, :], (8, x.shape[1]))


def silu_parts(m):
    sig = 1.0 / (1.0 + jnp.exp(-m))
    return m * sig, sig * (1.0 + m * (1.0 - sig))


def pick(values, lanes):
    return jnp.take_along_axis(values, lanes, axis=1, mode="promise_in_bounds")


def reach(b, first, last):
    return [w for w in range(3) if first <= b - 1 + w <= last]


SIDE_START = {2: 0, 3: LANES, 8: 3 * LANES, 9: 5 * LANES}
SIDE_ROWS = 6 * LANES


def mark(index, ws, target):
    count = len(ws) * LANES
    row_id = (lax.broadcasted_iota(jnp.int32, (count, LANES), 0) + ws[0] * LANES).astype(jnp.int16)
    one, zero = jnp.ones((count, LANES), BF16), jnp.zeros((count, LANES), BF16)
    for k in range(SLOTS):
        wanted = jnp.broadcast_to(index[k : k + 1, :], (16, LANES)).astype(jnp.int16)
        wanted = jnp.concatenate([wanted] * (count // 16), axis=0)
        target[:, k * LANES : (k + 1) * LANES] = jnp.where(row_id == wanted, one, zero)


def window_index(pack, b):
    lanes = slice((b % 4) * LANES, (b % 4 + 1) * LANES)
    return pack[0:8, lanes].astype(jnp.int32) - LANES * (b % 4)


def mark_sides(packs, side):
    for b, start in SIDE_START.items():
        ws = reach(b, 3, 8)
        mark(window_index(packs[b // 4], b), ws, side.at[start : start + len(ws) * LANES])


def forward_parts(packs, weights, xs, sst, kept):
    l1, l2, l3, l5, l6, col = weights
    (widx, kinds, geo, bst, bps, bpr, sent_all, sent_pair, slope) = kept
    centre = 2.0 + 0.5 * lax.broadcasted_iota(jnp.int32, (BASIS, LANES), 0).astype(F32)
    slot = lax.broadcasted_iota(jnp.int32, (SLOTS, LANES), 0)

    def part_rows(value):
        high, low = split(value)
        return jnp.concatenate([high, low], axis=0).astype(BF16)

    def pairs(b):
        pack = packs[b // 4]
        lanes = slice((b % 4) * LANES, (b % 4 + 1) * LANES)
        index = window_index(pack, b)
        widx[b] = index
        inner = index & (LANES - 1)
        part = index >> 7

        def taken(row):
            got = [
                pick(jnp.broadcast_to(xs[b - 1 + w, row : row + 1, :], (SLOTS, LANES)), inner)
                for w in range(3)
            ]
            return jnp.where(part == 0, got[0], jnp.where(part == 1, got[1], got[2]))

        vec = [
            pack[8 + 8 * c : 16 + 8 * c, lanes] + taken(c) - jnp.broadcast_to(xs[b, c : c + 1, :], (SLOTS, LANES))
            for c in range(3)
        ]
        kind = taken(3)
        dist = jnp.sqrt(vec[0] * vec[0] + vec[1] * vec[1] + vec[2] * vec[2] + SOFTENING)
        live = (slot.astype(F32) < jnp.broadcast_to(pack[ROW_COUNT : ROW_COUNT + 1, lanes], (SLOTS, LANES))).astype(F32)
        turns = dist * (1.0 / 12.0)
        turns = turns - jnp.floor(turns + 0.5)
        sine, cosine = sin_cos(turns * math.pi)
        envelope = cosine * cosine * live
        slant = cosine * sine * live * (-math.pi / 6.0)
        if 3 <= b <= 8:
            kinds[b] = kind
            for c in range(3):
                geo[b, c] = vec[c]
            geo[b, 3] = 1.0 / dist
        total = jnp.zeros((BASIS, LANES), F32)
        total_kind = jnp.zeros((BASIS, LANES), F32)
        for k in range(SLOTS):
            away = wide_row(dist, k) - centre
            gauss = jnp.exp(-4.0 * (away * away))
            env_k = wide_row(envelope, k)
            value = gauss * env_k
            total = total + value
            total_kind = total_kind + value * wide_row(kind, k)
            cols = slice(k * LANES, (k + 1) * LANES)
            if 2 <= b <= 9:
                bst[b, :, cols] = part_rows(value)
            if 3 <= b <= 8:
                value = gauss * (wide_row(slant, k) - 8.0 * away * env_k)
                bpr[b, :, cols] = value
                bps[b, :, cols] = part_rows(value)
        high, low = split(jnp.concatenate([total, total_kind], axis=0))
        sst[:, b * LANES : (b + 1) * LANES] = jnp.concatenate([high, low, high], axis=0).astype(BF16)

    for b in range(1, 11):
        pairs(b)

    for b in range(1, 11, 2):
        cols = slice(b * LANES, (b + 2) * LANES)
        value, steep = silu_parts(mm(l1[...], sst[:, cols]))
        sent = mm(l2[...], right_stack(value))
        for i in range(2):
            one = sent[:, i * LANES : (i + 1) * LANES]
            one = one + col[0] + col[1] * jnp.broadcast_to(xs[b + i, 3:4, :], (CHANNELS, LANES))
            sent_all[:, (b + i) * LANES : (b + i + 1) * LANES] = one
            if 3 <= b + i <= 8:
                sent_pair[:, (b + i) * LANES : (b + i + 1) * LANES] = pair_stack(one)
        slope[:, cols] = steep


def force_parts(weights, own_hot, side_hot, kept, dg, pulls, met, acc, held):
    l1, l2, l3, l5, l6, col = weights
    (widx, kinds, geo, bst, bps, bpr, sent_all, sent_pair, slope) = kept
    slot = lax.broadcasted_iota(jnp.int32, (SLOTS, LANES), 0)

    def marks(b, ws):
        if b in SIDE_START:
            start = SIDE_START[b] + (ws[0] - reach(b, 3, 8)[0]) * LANES
            return side_hot.at[start : start + len(ws) * LANES]
        return own_hot.at[b - 4, ws[0] * LANES : (ws[-1] + 1) * LANES]

    def add_rows(sums, first, b, ws, out):
        for i, w in enumerate(ws):
            target = b - 1 + w
            piece = out[i * LANES : (i + 1) * LANES]
            rows = slice((target - first) * LANES, (target - first + 1) * LANES)
            if (first, target) in started:
                sums[rows, :] += piece
            else:
                sums[rows, :] = piece
                started.add((first, target))

    started = set()

    def block_work(b):
        index = widx[b]
        inner, part = index & (LANES - 1), index >> 7
        basis = bst[b]
        radial = mm(l3[...], jnp.concatenate([basis, basis], axis=0))
        if 3 <= b <= 8:
            basis = bps[b]
            steepness = mm(l3[...], jnp.concatenate([basis, basis], axis=0))
        lanes = [jnp.broadcast_to(inner[k : k + 1, :], (16, LANES)) for k in range(SLOTS)]
        parts = [jnp.broadcast_to(part[k : k + 1, :], (16, LANES)) for k in range(SLOTS)]
        own = 4 <= b <= 7
        if own:
            found_all = mm(sent_pair[:, (b - 1) * LANES : (b + 2) * LANES], own_hot[b - 4])
        value = held.at[b % 2]
        total = [jnp.zeros((8, LANES), F32)] * SLOTS
        for u in range(CHANNELS // 16):
            rows = slice(16 * u, 16 * u + 16)
            low_rows = slice(CHANNELS + 16 * u, CHANNELS + 16 * u + 16)
            windows = [sent_all[rows, (b - 1 + w) * LANES : (b + w) * LANES] for w in range(3)]
            got = []
            message = jnp.zeros((16, LANES), F32)
            for k in range(SLOTS):
                cols = slice(k * LANES, (k + 1) * LANES)
                if own:
                    got.append(found_all[rows, cols] + found_all[low_rows, cols])
                else:
                    found = [pick(window, lanes[k]) for window in windows]
                    got.append(jnp.where(parts[k] == 0, found[0], jnp.where(parts[k] == 1, found[1], found[2])))
                message = message + radial[rows, cols] * got[k]
            _, steep = silu_parts(message)
            back = col[3, rows] * steep
            for k in range(SLOTS):
                cols = slice(k * LANES, (k + 1) * LANES)
                high, low = split(radial[rows, cols] * back)
                value[rows, cols] = high.astype(BF16)
                value[low_rows, cols] = low.astype(BF16)
                if 3 <= b <= 8:
                    pull = got[k] * back * steepness[rows, cols]
                    total[k] = total[k] + pull[0:8] + pull[8:16]
            yield
        if 3 <= b <= 8:
            for k in range(SLOTS):
                pulls[b, :, k * LANES : (k + 1) * LANES] = total[k]

    def scatter_work(b):
        ws = reach(b, 3, 8)
        chosen, value = marks(b, ws), held.at[b % 2]
        out = None
        for u in range(4):
            cols = slice(u * 2 * LANES, (u + 1) * 2 * LANES)
            one = mm_nt(chosen[:, cols], value[:, cols])
            out = one if out is None else out + one
            yield
        add_rows(dg, 3, b, ws, out)

    def together(*works):
        works = list(works)
        while works:
            works = [work for work in works if next(work, "end") != "end"]

    together(block_work(2))
    for b in range(3, 10):
        together(scatter_work(b - 1), block_work(b))
    together(scatter_work(9))

    def finish(b, sums):
        kind = kinds[b]
        rows = []
        for k in range(SLOTS):
            cols = slice(k * LANES, (k + 1) * LANES)
            weight = sums[0:8] + wide_row(kind, k) * sums[8:16]
            rows.append(jnp.sum(bpr[b, :, cols] * weight + pulls[b, :, cols], axis=0, keepdims=True))
        pull = jnp.concatenate(rows, axis=0) * geo[b, 3]
        pieces = []
        for c in range(3):
            value = pull * geo[b, c]
            if 4 <= b <= 7:
                acc[b - 4, c] = jnp.sum(value, axis=0, keepdims=True)
            pieces.append(split(value))
        lines = []
        for h in range(2):
            for c in range(3):
                lines.append(jnp.concatenate([jnp.where(slot == k, pieces[c][h], 0.0) for k in range(SLOTS)], axis=1))
        ws = reach(b, 4, 7)
        out = mm_nt(jnp.concatenate(lines, axis=0).astype(BF16), marks(b, ws)[...])
        for c in range(3):
            both = out[8 * c : 8 * c + 8] + out[24 + 8 * c : 32 + 8 * c]
            for i, w in enumerate(ws):
                target = b - 5 + w
                piece = both[:, i * LANES : (i + 1) * LANES]
                if (c, target) in met_blocks:
                    met[target, c] += piece
                else:
                    met[target, c] = piece
                    met_blocks.add((c, target))

    met_blocks = set()

    for b in range(3, 9, 2):
        cols = slice(b * LANES, (b + 2) * LANES)
        high, low = split(dg[(b - 3) * LANES : (b - 1) * LANES, :])
        steep = mm_nt(l5[...], jnp.concatenate([high, low, high], axis=1).astype(BF16))
        steep = steep + jnp.concatenate([col[2], col[2]], axis=1)
        sums = mm(l6[...], right_stack(steep * slope[:, cols]))
        for i in range(2):
            finish(b + i, sums[:, i * LANES : (i + 1) * LANES])

    away = []
    for c in range(3):
        back = [acc[i, c] - jnp.sum(met[i, c], axis=0, keepdims=True) for i in range(SLAB_BLOCKS)]
        away.append(jnp.concatenate(back, axis=1))
    return jnp.concatenate(away, axis=0)


def fill_region(xs, packs, rows_of):
    for b in range(12):
        lanes = slice((b % 4) * LANES, (b % 4 + 1) * LANES)
        pack = packs[b // 4]
        xs[b, 0:3, :] = rows_of(b // 4)[:, lanes]
        xs[b, 3:4, :] = pack[ROW_KIND : ROW_KIND + 1, lanes]


def lane_total(x):
    x = x[:, 0:LANES] + x[:, LANES : 2 * LANES] + x[:, 2 * LANES : 3 * LANES] + x[:, 3 * LANES : 4 * LANES]
    return jnp.sum(x, axis=1, keepdims=True)


def dot3(a, b):
    return jnp.sum(a * b, axis=0, keepdims=True)


def kept_shapes():
    wide = 12 * LANES
    return [
        ((12, 8, LANES), jnp.int32),
        ((12, 8, LANES), F32),
        ((12, 4, 8, LANES), F32),
        ((12, 16, SLOTS * LANES), BF16),
        ((12, 16, SLOTS * LANES), BF16),
        ((12, 8, SLOTS * LANES), F32),
        ((CHANNELS, wide), F32),
        ((2 * CHANNELS, wide), BF16),
        ((CHANNELS, wide), F32),
    ]


def forward_scratch():
    return [pltpu.VMEM((12, 8, LANES), F32), pltpu.VMEM((48, 12 * LANES), BF16)]


def back_scratch():
    return [
        pltpu.VMEM((6 * LANES, 2 * CHANNELS), F32),
        pltpu.VMEM((12, 8, SLOTS * LANES), F32),
        pltpu.VMEM((SLAB_BLOCKS, 3, SLOTS, LANES), F32),
        pltpu.VMEM((SLAB_BLOCKS, 3, 1, LANES), F32),
        pltpu.VMEM((2, 2 * CHANNELS, SLOTS * LANES), BF16),
    ]


def by_parity(sibling, across):
    even = jnp.full(sibling.shape, lax.axis_index("dom") % 2, jnp.int32) == 0
    return jnp.where(even, across, sibling), jnp.where(even, sibling, across)


def first_kernel(x_ref, sibling_ref, po_ref, across_ref, *rest):
    weights, (pl_ref, pr_ref, side_hot, copy_ref), kept, (xs, sst) = rest[:6], rest[6:10], rest[10:19], rest[19:]
    copy_ref[...] = x_ref[...]
    pl_ref[...], pr_ref[...] = by_parity(sibling_ref[...], across_ref[...])
    packs = [pl_ref, po_ref, pr_ref]
    mark_sides(packs, side_hot)
    fill_region(xs, packs, lambda s: packs[s][ROW_X : ROW_X + 3, :])
    forward_parts(packs, weights, xs, sst, kept)


def first_back_kernel(own_hot, side_hot, *rest):
    weights, kept, out_ref, scr = rest[:6], rest[6:15], rest[15], rest[16:]
    out_ref[...] = force_parts(weights, own_hot, side_hot, kept, *scr)


def rows_of(ref):
    return jnp.concatenate([ref[c] for c in range(3)], axis=0)


def block_row(*values):
    values = list(values) + [jnp.zeros((1, LANES), F32)] * (SLAB_BLOCKS - len(values))
    return jnp.concatenate(values, axis=1)


def blend_kernel(images, force_ref, po_ref, before_ref, after_ref, out_ref, sums_ref):
    x = po_ref[ROW_X : ROW_X + 3, :]
    v = po_ref[ROW_V : ROW_V + 3, :]
    force = force_ref[...]
    here = lax.axis_index("img")
    before = jnp.where(here > 0, rows_of(before_ref), 0.0)
    after = jnp.where(here < images - 1, rows_of(after_ref), 0.0)
    tangent = after - before
    plus = after - x
    minus = x - before
    sums = jnp.concatenate(
        [
            dot3(force, tangent),
            dot3(force, force),
            dot3(tangent, tangent),
            dot3(plus, plus),
            dot3(minus, minus),
            dot3(v, v),
            jnp.zeros((2, x.shape[1]), F32),
        ],
        axis=0,
    )
    sums = jnp.broadcast_to(lane_total(sums), (8, LANES))
    sums_ref[...] = sums
    out_ref[0:3, :] = force
    out_ref[3:6, :] = tangent
    out_ref[6:7, :] = block_row(*[sums[i : i + 1] for i in range(4)])
    out_ref[7:8, :] = block_row(sums[4:5], sums[5:6])


def step_numbers(ft, ff, tt, pp, mn, vv, dt, alpha, flagged, climbing, inside):
    root = jnp.sqrt(tt + TINY_VALUE)
    along = ft / root
    spring = SPRING_CONSTANT * (jnp.sqrt(pp) - jnp.sqrt(mn))
    factor = jnp.where(climbing, -2.0 * along, spring - along)
    band = jnp.maximum(ff + 2.0 * factor * along + factor * factor * (tt / (tt + TINY_VALUE)), 0.0)
    new_dt = jnp.where(flagged, 0.5 * dt, jnp.minimum(1.1 * dt, STEP_LIMIT))
    pull = jnp.where(flagged, 0.0, alpha * jnp.sqrt(vv / (band + TINY_VALUE))) + new_dt
    keep = jnp.where(flagged, 0.0, 1.0 - alpha)
    new_alpha = jnp.where(flagged, ALPHA_START, 0.99 * alpha)
    keep = jnp.where(inside, keep, 0.0)
    pull = jnp.where(inside, pull, 0.0)
    return (
        jnp.where(inside, along, 0.0),
        jnp.where(inside, spring, 0.0),
        keep,
        pull,
        pull * factor / root,
        new_dt,
        new_alpha,
    )


def add_kernel(a_ref, b_ref, out_ref):
    out_ref[...] = a_ref[...] + b_ref[...]


def join_kernel(a_ref, b_ref, out_ref):
    count = a_ref.shape[0]
    out_ref[0:count] = a_ref[...]
    out_ref[count : 2 * count] = b_ref[...]


def number_kernel(dt_ref, flag_ref, climb_ref, out_ref):
    flags = [flag_ref[0, s].astype(F32) for s in range(flag_ref.shape[1])]
    for i, value in enumerate([dt_ref[0], climb_ref[0].astype(F32)] + flags):
        out_ref[i : i + 1, :] = jnp.full((1, LANES), value, F32)


def second_kernel(images, domains, number_ref, pl_ref, po_ref, pr_ref, own_ref, near_ref, far_ref, *rest):
    count = 2 if domains == 4 else 1
    parts, rest = rest[:count], rest[count:]
    (own_hot, side_hot), weights, (out_ref, record_ref), scr = rest[:2], rest[2:8], rest[8:10], rest[10:]
    packs = [pl_ref, po_ref, pr_ref]
    here = lax.axis_index("img")
    sums = parts[0][...]
    if domains == 4:
        sums = sums + parts[1][...]
    got = [sums[i : i + 1, :] for i in range(6)]
    if domains == 4:
        for one in (near_ref, far_ref):
            for i in range(6):
                got[i] = got[i] + one[6 + i // 4 : 7 + i // 4, (i % 4) * LANES : (i % 4 + 1) * LANES]
    ft, ff, tt, pp, mn, vv = got
    beside = by_parity(near_ref[0:6, :], far_ref[0:6, :])
    shape = (1, LANES)
    along, spring, keep, pull, side, dt, alpha = step_numbers(
        ft,
        ff,
        tt,
        pp,
        mn,
        vv,
        number_ref[0:1, :],
        jnp.full(shape, ALPHA_START, F32),
        number_ref[2:3, :] == 1.0,
        number_ref[1:2, :] == jnp.full(shape, here, jnp.int32).astype(F32),
        jnp.full(shape, jnp.where((here >= 1) & (here <= images - 2), 1, 0), jnp.int32) == 1,
    )
    messages = [beside[0], own_ref[0:6, :], beside[1]]

    def wide(s):
        return jnp.concatenate([s] * SLAB_BLOCKS, axis=1)

    speeds = [
        wide(keep) * p[ROW_V : ROW_V + 3, :] + wide(pull) * m[0:3, :] + wide(side) * m[3:6, :]
        for p, m in zip(packs, messages)
    ]
    moved = [p[ROW_X : ROW_X + 3, :] + wide(dt) * s for p, s in zip(packs, speeds)]
    xs, sst, kept = scr[0], scr[1], scr[2:11]
    fill_region(xs, packs, lambda s: moved[s])
    forward_parts(packs, weights, xs, sst, kept)
    force = force_parts(weights, own_hot, side_hot, kept, *scr[11:])
    for c in range(3):
        for i in range(SLAB_BLOCKS):
            lanes = slice(i * LANES, (i + 1) * LANES)
            row = 4 * c + i
            out_ref[0, row : row + 1, :] = speeds[1][c : c + 1, lanes]
            out_ref[0, 12 + row : 13 + row, :] = force[c : c + 1, lanes]
            out_ref[0, 24 + row : 25 + row, :] = moved[1][c : c + 1, lanes]
    out_ref[0, 36:37, :] = dt
    out_ref[0, 37:38, :] = alpha
    out_ref[0, 38:40, :] = jnp.broadcast_to(number_ref[3:4, :], (2, LANES))
    record_ref[0:1, :] = along
    record_ref[1:2, :] = spring
    record_ref[2:3, :] = number_ref[1:2, :]


PRODUCTS = (
    [("f", "t"), ("f", "f"), ("t", "t"), ("p", "p"), ("d", "d"), ("v", "v")]
    + [("d", "v"), ("d", "f"), ("d", "t"), ("d", "V"), ("d", "F"), ("d", "T"), ("v", "f"), ("v", "t")]
    + [(a, b) for a in "vft" for b in "VFT"]
)


def gram_kernel(images, *refs):
    parts, (out_ref, state_ref, messages_ref) = refs[:-3], refs[-3:]
    rows = out_ref.shape[0]
    place = 0
    for part in parts:
        messages_ref[place : place + part.shape[0]] = part[...]
        place += part.shape[0]
    here = lax.axis_index("img")
    blank = [jnp.zeros((rows - images, LANES), F32)] if rows > images else []
    zero = jnp.zeros((1, LANES), F32)

    def gathered(row):
        return jnp.concatenate([messages_ref[here ^ i, row : row + 1, :] for i in range(images)] + blank, axis=0)

    def earlier(value):
        return jnp.concatenate([zero, value[0 : rows - 1]], axis=0)

    def later(value):
        return jnp.concatenate([value[1:images], zero] + blank, axis=0)

    number = lax.broadcasted_iota(jnp.int32, (rows, LANES), 0)
    held = number < images
    totals = [jnp.zeros((rows, LANES), F32) for _ in PRODUCTS]
    for row in range(3 * SLAB_BLOCKS):
        v, f, x = gathered(row), gathered(12 + row), gathered(24 + row)
        before = jnp.where(held, earlier(x), 0.0)
        after = later(x)
        t = after - before
        table = {"f": f, "v": v, "t": t, "p": after - x, "d": x - before}
        table["F"], table["V"], table["T"] = earlier(f), earlier(v), earlier(t)
        totals = [old + table[a] * table[b] for old, (a, b) in zip(totals, PRODUCTS)]
        state_ref[row : row + 1, :] = jnp.sum(jnp.where(number == here, t, 0.0), axis=0, keepdims=True)
    lane = lax.broadcasted_iota(jnp.int32, (rows, LANES), 1)
    result = jnp.zeros((rows, LANES), F32)
    for q, one in enumerate(totals):
        one = jnp.broadcast_to(jnp.sum(one, axis=1, keepdims=True), (rows, LANES))
        result = jnp.where(lane == q, one, result)
    out_ref[...] = result
    for i in range(3):
        state_ref[16 + rows * i : 16 + rows * (i + 1), :] = gathered(36 + i)


def final_kernel(images, atoms, own_ref, record_ref, state_ref, *rest):
    parts, (x_ref, v_ref, band_ref, path_ref) = rest[:-4], rest[-4:]
    rows = parts[0].shape[0]
    here = lax.axis_index("img")
    sums = parts[0][...]
    for one in parts[1:]:
        sums = sums + one[...]
    got = {
        pair: jnp.broadcast_to(sums[:, q : q + 1], (rows, LANES)) for q, pair in enumerate(PRODUCTS)
    }
    number = lax.broadcasted_iota(jnp.int32, (rows, LANES), 0)
    inside = (number >= 1) & (number <= images - 2)
    climb = jnp.broadcast_to(record_ref[2:3, :], (rows, LANES))
    dt0, alpha0, flag = (state_ref[16 + rows * i : 16 + rows * (i + 1), :] for i in range(3))
    along, spring, keep, pull, side, dt, _ = step_numbers(
        got["f", "t"],
        got["f", "f"],
        got["t", "t"],
        got["p", "p"],
        got["d", "d"],
        got["v", "v"],
        dt0,
        alpha0,
        flag == 1.0,
        number.astype(F32) == climb,
        inside,
    )

    def shifted(value):
        return jnp.concatenate([jnp.zeros((1, LANES), F32), value[0 : rows - 1]], axis=0)

    now = {"v": dt * keep, "f": dt * pull, "t": dt * side}
    old = {a.upper(): shifted(value) for a, value in now.items()}
    mine = now["v"] * now["v"] * got["v", "v"] + now["f"] * now["f"] * got["f", "f"]
    mine = mine + now["t"] * now["t"] * got["t", "t"]
    cross = now["v"] * now["f"] * got["v", "f"] + now["v"] * now["t"] * got["v", "t"]
    mine = mine + 2.0 * (cross + now["f"] * now["t"] * got["f", "t"])
    both = jnp.zeros((rows, LANES), F32)
    for a in "vft":
        both = both + now[a] * got["d", a]
    for b in "VFT":
        both = both - old[b] * got["d", b]
    for a in "vft":
        for b in "VFT":
            both = both - now[a] * old[b] * got[a, b]
    squared = got["d", "d"] + mine + shifted(mine) + 2.0 * both
    segment = jnp.sqrt(jnp.maximum(squared, 0.0) * (1.0 / (3.0 * atoms)))
    path = jnp.sum(jnp.where(number <= here, segment, 0.0), axis=0, keepdims=True)
    path_ref[...] = path[:, 0:1]
    keep, pull, side, dt, along, spring = (
        jnp.sum(jnp.where(number == here, value, 0.0), axis=0, keepdims=True)
        for value in (keep, pull, side, dt, along, spring)
    )

    for c in range(3):
        speeds, places = [], []
        for i in range(SLAB_BLOCKS):
            row = 4 * c + i
            speed = keep * own_ref[0, row : row + 1, :] + pull * own_ref[0, 12 + row : 13 + row, :]
            speed = speed + side * state_ref[row : row + 1, :]
            speeds.append(speed)
            places.append(own_ref[0, 24 + row : 25 + row, :] + dt * speed)
        v_ref[c] = jnp.concatenate(speeds, axis=1)
        x_ref[c] = jnp.concatenate(places, axis=1)
    band_ref[0] = jnp.concatenate([record_ref[0:1, 0:1], record_ref[1:2, 0:1]], axis=1)
    band_ref[1] = jnp.concatenate([along[:, 0:1], spring[:, 0:1]], axis=1)


VMEM_SPEC = pl.BlockSpec(memory_space=pltpu.VMEM)
SMEM_SPEC = pl.BlockSpec(memory_space=pltpu.SMEM)
HBM_SPEC = pl.BlockSpec(memory_space=pltpu.HBM)


def call(body, outs, scalars, arrays, scratch_shapes=(), flops=0, spec=VMEM_SPEC, vmem=24):
    return pl.pallas_call(
        body,
        out_shape=outs,
        in_specs=[SMEM_SPEC] * len(scalars) + [spec] * len(arrays),
        out_specs=jax.tree.map(lambda _: VMEM_SPEC, outs),
        scratch_shapes=list(scratch_shapes),
        compiler_params=pltpu.CompilerParams(vmem_limit_bytes=vmem * 1024 * 1024),
        cost_estimate=pl.CostEstimate(flops=flops, bytes_accessed=1 << 18, transcendentals=0),
    )(*scalars, *arrays)


def swap(array, axis, partner):
    return lax.ppermute(array, axis, [(i, partner(i)) for i in range(lax.axis_size(axis))])


def exchanged(sums, axis):
    count = lax.axis_size(axis)
    if count == 4:
        return [sums] + [swap(sums, axis, lambda i, by=by: i ^ by) for by in (2, 3, 1)]
    distance = 1
    while distance < count:
        more = swap(sums, axis, lambda i, by=distance: i ^ by)
        sums = call(add_kernel, jax.ShapeDtypeStruct(sums.shape, F32), (), (sums, more))
        distance *= 2
    return [sums]


def collected(array, axis):
    count = lax.axis_size(axis)
    if count == 4:
        far = [swap(array, axis, lambda i, by=by: i ^ by) for by in (3, 2, 1)]
        return [array] + far[::-1]
    distance = 1
    while distance < count:
        more = swap(array, axis, lambda i, by=distance: i ^ by)
        shape = jax.ShapeDtypeStruct((2 * distance,) + array.shape[1:], F32)
        array = call(join_kernel, shape, (), (array, more))
        distance *= 2
    return [array]


def local(
    disp,
    veloc,
    time_step,
    reset_flags,
    climb,
    species,
    neighbours,
    counts,
    lattice,
    embed,
    radial_weight,
    mix_weight,
    update_weight,
    readout,
):
    atoms = disp.shape[2]
    images = lax.axis_size("img")
    domains = lax.axis_size("dom")
    assert disp.shape[0] == 1 and atoms == SLAB_BLOCKS * LANES and domains >= 4
    assert domains & (domains - 1) == 0 and images & (images - 1) == 0
    shape = jax.ShapeDtypeStruct
    x = jnp.transpose(disp, (1, 0, 2))
    v = jnp.transpose(veloc, (1, 0, 2))
    small = (x, v, species, neighbours, counts, embed, readout, radial_weight, mix_weight, update_weight)
    sent, pack = call(
        pack_kernel,
        (shape((PACK_ROWS, atoms), F32), shape((OWN_ROWS, atoms), F32)),
        (),
        (*small, jnp.transpose(lattice, (1, 0, 2))),
        [pltpu.VMEM(a.shape, a.dtype) for a in small] + [pltpu.SemaphoreType.DMA((16,))],
        spec=HBM_SPEC,
        vmem=63,
    )
    sibling = swap(sent, "dom", lambda i: i ^ 1)
    across = swap(sent, "dom", lambda i: (i + 2 * (i % 2) - 1) % domains)
    own_hot, *weights, x_copy = call(
        prepare_kernel,
        (
            shape((SLAB_BLOCKS, 3 * LANES, SLOTS * LANES), BF16),
            shape((CHANNELS, 48), BF16),
            shape((CHANNELS, 192), BF16),
            shape((CHANNELS, 32), BF16),
            shape((CHANNELS, 3 * LANES), BF16),
            shape((16, 192), BF16),
            shape((4, CHANNELS, LANES), F32),
            shape(x.shape, F32),
        ),
        (),
        (pack,),
        flops=100000000,
    )
    before = swap(x_copy, "img", lambda i: (i + 1) % images)
    left, right, side_hot, x_copy, *kept = call(
        first_kernel,
        (
            shape(sent.shape, F32),
            shape(sent.shape, F32),
            shape((SIDE_ROWS, SLOTS * LANES), BF16),
            shape(x.shape, F32),
            *[shape(*one) for one in kept_shapes()],
        ),
        (),
        (x_copy, sibling, pack, across, *weights),
        forward_scratch(),
        flops=1000000000,
    )
    after = swap(x_copy, "img", lambda i: (i - 1) % images)
    force = call(
        first_back_kernel,
        shape((3, atoms), F32),
        (),
        (own_hot, side_hot, *weights, *kept),
        back_scratch(),
        flops=1000000000,
    )
    message, sums = call(
        functools.partial(blend_kernel, images),
        (shape((8, atoms), F32), shape((8, LANES), F32)),
        (),
        (force, pack, before, after),
    )
    far = swap(message, "dom", lambda i: (i + 2 * (i % 2) - 1) % domains)
    if domains == 4:
        parts = [sums, swap(sums, "dom", lambda i: i ^ 2)]
    else:
        parts = exchanged(sums, "dom")
    near = swap(message, "dom", lambda i: i ^ 1)
    numbers = call(number_kernel, shape((8, LANES), F32), (time_step, jnp.transpose(reset_flags), climb), ())
    state, record = call(
        functools.partial(second_kernel, images, domains),
        (shape((1, 40, LANES), F32), shape((3, LANES), F32)),
        (),
        (numbers, left, pack, right, message, near, far, *parts, own_hot, side_hot, *weights),
        forward_scratch() + [pltpu.VMEM(*one) for one in kept_shapes()] + back_scratch(),
        flops=1000000000,
    )
    rows = 8 * ((images + 7) // 8)
    sums, extra = call(
        functools.partial(gram_kernel, images),
        (shape((rows, LANES), F32), shape((16 + 3 * rows, LANES), F32)),
        (),
        collected(state, "img"),
        [pltpu.VMEM((images, 40, LANES), F32)],
    )
    new_x, new_v, records, path = call(
        functools.partial(final_kernel, images, atoms * domains),
        (shape(x.shape, F32), shape(x.shape, F32), shape((2, 1, 2), F32), shape((1, 1), F32)),
        (),
        (state, record, extra, *exchanged(sums, "dom")),
    )
    return (
        jnp.transpose(new_x, (1, 0, 2)),
        jnp.transpose(new_v, (1, 0, 2)),
        jnp.transpose(records, (0, 2, 1)),
        path.reshape(1),
    )


def solution(mesh):
    in_specs = (
        P(("group", "img"), None, "dom"),
        P(("group", "img"), None, "dom"),
        P(("group", "img")),
        P(None, ("group", "img")),
        P("group"),
        P(("group", "dom")),
        P(None, ("group", "dom")),
        P(("group", "dom")),
        P(None, None, ("group", "dom")),
        P(),
        P(),
        P(),
        P(),
        P(),
    )
    out_specs = (
        P(("group", "img"), None, "dom"),
        P(("group", "img"), None, "dom"),
        P(None, None, ("group", "img")),
        P(("group", "img")),
    )
    return jax.shard_map(local, mesh=mesh, in_specs=in_specs, out_specs=out_specs, check_vma=False)
```

```python
import functools
import math

import jax
import jax.numpy as jnp
from jax import lax
from jax.experimental import pallas as pl
from jax.experimental.pallas import tpu as pltpu
from jax.sharding import PartitionSpec as P

F32 = jnp.float32
BF16 = jnp.bfloat16
PRECISE = lax.Precision.HIGHEST
SPRING_CONSTANT = 0.5
ALPHA_START = 0.1
STEP_LIMIT = 0.3
TINY_VALUE = 1e-06
SOFTENING = 0.25
LANES = 128
SLOTS = 8
BASIS = 8
CHANNELS = 64
SLAB_BLOCKS = 4
ROW_X = 32
ROW_COUNT = 35
ROW_KIND = 36
ROW_V = 37
PACK_ROWS = 40
OWN_ROWS = PACK_ROWS + CHANNELS + BASIS
NT = (((1,), (1,)), ((), ()))


def split(x):
    high = x.astype(BF16).astype(F32)
    return high, x - high


def left_stack(w):
    high, low = split(w)
    return jnp.concatenate([high, high, low], axis=1)


def right_stack(x):
    high, low = split(x)
    high = high.astype(BF16)
    return jnp.concatenate([high, low.astype(BF16), high], axis=0)


def pair_stack(x):
    high, low = split(x)
    return jnp.concatenate([high.astype(BF16), low.astype(BF16)], axis=0)


def mm(a, b):
    return jnp.dot(a, b, preferred_element_type=F32)


def mm_nt(a, b):
    return lax.dot_general(a, b, NT, preferred_element_type=F32)


def pack_kernel(*refs):
    sources, (out_ref, own_ref), held, sems = refs[:11], refs[11:13], refs[13:23], refs[23]
    lattice = sources[10]
    pairs = list(zip(sources, held))
    for c in range(3):
        rows = pl.ds(8 + 8 * c, 8)
        pairs += [(lattice.at[c], out_ref.at[rows]), (lattice.at[c], own_ref.at[rows])]
    copies = [pltpu.make_async_copy(a, b, sems.at[i]) for i, (a, b) in enumerate(pairs)]
    for one in copies:
        one.start()
    for one in copies:
        one.wait()
    x, v, species, nbr, counts, embed, readout, radial, mix, update = held
    for ref in (out_ref, own_ref):
        ref[0:8, :] = nbr[...].astype(F32)
        for c in range(3):
            ref[ROW_X + c : ROW_X + c + 1, :] = x[c]
            ref[ROW_V + c : ROW_V + c + 1, :] = v[c]
        ref[ROW_COUNT : ROW_COUNT + 1, :] = counts[...].astype(F32).reshape(1, -1)
        ref[ROW_KIND : ROW_KIND + 1, :] = species[...].astype(F32).reshape(1, -1)
    top, low = PACK_ROWS, PACK_ROWS + CHANNELS
    for i, value in enumerate([mix[0], mix[1], update[0], update[1]]):
        own_ref[top:low, i * LANES : i * LANES + CHANNELS] = value
    for i, value in enumerate([radial[0], radial[1], embed[...], readout[...].reshape(1, CHANNELS)]):
        own_ref[low : low + value.shape[0], i * LANES : i * LANES + CHANNELS] = value


def prepare_kernel(po_ref, *rest):
    own_hot, l1_ref, l2_ref, l3_ref, l5_ref, l6_ref, col_ref, copy_ref = rest
    for b in range(SLAB_BLOCKS):
        mark(window_index(po_ref, b), [0, 1, 2], own_hot.at[b])
    copy_ref[...] = po_ref[ROW_X : ROW_X + 8, :]

    def raw(first, count, i):
        return po_ref[first : first + count, i * LANES : i * LANES + CHANNELS]

    low = PACK_ROWS + CHANNELS
    mix_ref = [raw(PACK_ROWS, CHANNELS, i) for i in range(2)]
    update_ref = [raw(PACK_ROWS, CHANNELS, 2 + i) for i in range(2)]
    radial_ref = [raw(low, BASIS, i) for i in range(2)]
    embed_ref, readout = raw(low, 2, 2), raw(low, 1, 3)
    eye = (
        lax.broadcasted_iota(jnp.int32, (CHANNELS, CHANNELS), 0)
        == lax.broadcasted_iota(jnp.int32, (CHANNELS, CHANNELS), 1)
    ).astype(F32)

    def turned(x):
        return lax.dot_general(eye, x, NT, precision=PRECISE, preferred_element_type=F32)

    base0 = embed_ref[0:1, :]
    base1 = embed_ref[1:2, :] - base0
    rows = jnp.concatenate([base0, base1], axis=0)
    sent = jnp.dot(rows, mix_ref[0], precision=PRECISE, preferred_element_type=F32)
    scale = 1.0 / math.sqrt(SLOTS)
    first = jnp.concatenate([radial_ref[0] * sent[0:1], radial_ref[0] * sent[1:2]], axis=0) * scale
    second = radial_ref[1] * scale
    folded = jnp.dot(update_ref[0], mix_ref[1], precision=PRECISE, preferred_element_type=F32)
    mix_t = turned(mix_ref[1])
    l1_ref[...] = left_stack(turned(first)).astype(BF16)
    l2_ref[...] = left_stack(turned(folded)).astype(BF16)
    high, low = split(turned(second))
    l3_ref[...] = jnp.concatenate([high, high, low, jnp.zeros_like(high)], axis=1).astype(BF16)
    high, low = split(folded)
    l5_ref[...] = jnp.concatenate([high, high, high, high, low, low], axis=1).astype(BF16)
    l6_ref[...] = left_stack(first).astype(BF16)
    wide = (CHANNELS, LANES)
    col_ref[0] = jnp.broadcast_to(jnp.sum(mix_t * base0, axis=1, keepdims=True), wide)
    col_ref[1] = jnp.broadcast_to(jnp.sum(mix_t * base1, axis=1, keepdims=True), wide)
    col_ref[2] = jnp.broadcast_to(jnp.sum(update_ref[0] * readout, axis=1, keepdims=True), wide)
    col_ref[3] = jnp.broadcast_to(jnp.sum(update_ref[1] * readout, axis=1, keepdims=True), wide)


def sin_cos(t):
    q = t * t
    s = -1.0 / 39916800.0
    for c in (1.0 / 362880.0, -1.0 / 5040.0, 1.0 / 120.0, -1.0 / 6.0, 1.0):
        s = s * q + c
    k = 1.0 / 479001600.0
    for c in (-1.0 / 3628800.0, 1.0 / 40320.0, -1.0 / 720.0, 1.0 / 24.0, -0.5, 1.0):
        k = k * q + c
    return s * t, k


def wide_row(x, row):
    return jnp.broadcast_to(x[row : row + 1, :], (8, x.shape[1]))


def silu_parts(m):
    sig = 1.0 / (1.0 + jnp.exp(-m))
    return m * sig, sig * (1.0 + m * (1.0 - sig))


def pick(values, lanes):
    return jnp.take_along_axis(values, lanes, axis=1, mode="promise_in_bounds")


def reach(b, first, last):
    return [w for w in range(3) if first <= b - 1 + w <= last]


SIDE_START = {2: 0, 3: LANES, 8: 3 * LANES, 9: 5 * LANES}
SIDE_ROWS = 6 * LANES


def mark(index, ws, target):
    count = len(ws) * LANES
    row_id = (lax.broadcasted_iota(jnp.int32, (count, LANES), 0) + ws[0] * LANES).astype(jnp.int16)
    one, zero = jnp.ones((count, LANES), BF16), jnp.zeros((count, LANES), BF16)
    for k in range(SLOTS):
        wanted = jnp.broadcast_to(index[k : k + 1, :], (16, LANES)).astype(jnp.int16)
        wanted = jnp.concatenate([wanted] * (count // 16), axis=0)
        target[:, k * LANES : (k + 1) * LANES] = jnp.where(row_id == wanted, one, zero)


def window_index(pack, b):
    lanes = slice((b % 4) * LANES, (b % 4 + 1) * LANES)
    return pack[0:8, lanes].astype(jnp.int32) - LANES * (b % 4)


def mark_sides(packs, side):
    for b, start in SIDE_START.items():
        ws = reach(b, 3, 8)
        mark(window_index(packs[b // 4], b), ws, side.at[start : start + len(ws) * LANES])


def forward_parts(packs, weights, xs, sst, kept):
    l1, l2, l3, l5, l6, col = weights
    (widx, kinds, geo, bst, bps, bpr, sent_all, sent_pair, slope) = kept
    centre = 2.0 + 0.5 * lax.broadcasted_iota(jnp.int32, (BASIS, LANES), 0).astype(F32)
    slot = lax.broadcasted_iota(jnp.int32, (SLOTS, LANES), 0)

    def part_rows(value):
        high, low = split(value)
        return jnp.concatenate([high, low], axis=0).astype(BF16)

    def pairs(b):
        pack = packs[b // 4]
        lanes = slice((b % 4) * LANES, (b % 4 + 1) * LANES)
        index = window_index(pack, b)
        widx[b] = index
        inner = index & (LANES - 1)
        part = index >> 7

        def taken(row):
            got = [
                pick(jnp.broadcast_to(xs[b - 1 + w, row : row + 1, :], (SLOTS, LANES)), inner)
                for w in range(3)
            ]
            return jnp.where(part == 0, got[0], jnp.where(part == 1, got[1], got[2]))

        vec = [
            pack[8 + 8 * c : 16 + 8 * c, lanes] + taken(c) - jnp.broadcast_to(xs[b, c : c + 1, :], (SLOTS, LANES))
            for c in range(3)
        ]
        kind = taken(3)
        dist = jnp.sqrt(vec[0] * vec[0] + vec[1] * vec[1] + vec[2] * vec[2] + SOFTENING)
        live = (slot.astype(F32) < jnp.broadcast_to(pack[ROW_COUNT : ROW_COUNT + 1, lanes], (SLOTS, LANES))).astype(F32)
        turns = dist * (1.0 / 12.0)
        turns = turns - jnp.floor(turns + 0.5)
        sine, cosine = sin_cos(turns * math.pi)
        envelope = cosine * cosine * live
        slant = cosine * sine * live * (-math.pi / 6.0)
        if 3 <= b <= 8:
            kinds[b] = kind
            for c in range(3):
                geo[b, c] = vec[c]
            geo[b, 3] = 1.0 / dist
        total = jnp.zeros((BASIS, LANES), F32)
        total_kind = jnp.zeros((BASIS, LANES), F32)
        for k in range(SLOTS):
            away = wide_row(dist, k) - centre
            gauss = jnp.exp(-4.0 * (away * away))
            env_k = wide_row(envelope, k)
            value = gauss * env_k
            total = total + value
            total_kind = total_kind + value * wide_row(kind, k)
            cols = slice(k * LANES, (k + 1) * LANES)
            if 2 <= b <= 9:
                bst[b, :, cols] = part_rows(value)
            if 3 <= b <= 8:
                value = gauss * (wide_row(slant, k) - 8.0 * away * env_k)
                bpr[b, :, cols] = value
                bps[b, :, cols] = part_rows(value)
        high, low = split(jnp.concatenate([total, total_kind], axis=0))
        sst[:, b * LANES : (b + 1) * LANES] = jnp.concatenate([high, low, high], axis=0).astype(BF16)

    for b in range(1, 11):
        pairs(b)

    for b in range(1, 11, 2):
        cols = slice(b * LANES, (b + 2) * LANES)
        value, steep = silu_parts(mm(l1[...], sst[:, cols]))
        sent = mm(l2[...], right_stack(value))
        for i in range(2):
            one = sent[:, i * LANES : (i + 1) * LANES]
            one = one + col[0] + col[1] * jnp.broadcast_to(xs[b + i, 3:4, :], (CHANNELS, LANES))
            sent_all[:, (b + i) * LANES : (b + i + 1) * LANES] = one
            if 3 <= b + i <= 8:
                sent_pair[:, (b + i) * LANES : (b + i + 1) * LANES] = pair_stack(one)
        slope[:, cols] = steep


def force_parts(weights, own_hot, side_hot, kept, dg, pulls, met, acc, held):
    l1, l2, l3, l5, l6, col = weights
    (widx, kinds, geo, bst, bps, bpr, sent_all, sent_pair, slope) = kept
    slot = lax.broadcasted_iota(jnp.int32, (SLOTS, LANES), 0)

    def marks(b, ws):
        if b in SIDE_START:
            start = SIDE_START[b] + (ws[0] - reach(b, 3, 8)[0]) * LANES
            return side_hot.at[start : start + len(ws) * LANES]
        return own_hot.at[b - 4, ws[0] * LANES : (ws[-1] + 1) * LANES]

    def add_rows(sums, first, b, ws, out):
        for i, w in enumerate(ws):
            target = b - 1 + w
            piece = out[i * LANES : (i + 1) * LANES]
            rows = slice((target - first) * LANES, (target - first + 1) * LANES)
            if (first, target) in started:
                sums[rows, :] += piece
            else:
                sums[rows, :] = piece
                started.add((first, target))

    started = set()

    def block_work(b):
        index = widx[b]
        inner, part = index & (LANES - 1), index >> 7
        basis = bst[b]
        radial = mm(l3[...], jnp.concatenate([basis, basis], axis=0))
        if 3 <= b <= 8:
            basis = bps[b]
            steepness = mm(l3[...], jnp.concatenate([basis, basis], axis=0))
        lanes = [jnp.broadcast_to(inner[k : k + 1, :], (16, LANES)) for k in range(SLOTS)]
        parts = [jnp.broadcast_to(part[k : k + 1, :], (16, LANES)) for k in range(SLOTS)]
        own = 4 <= b <= 7
        if own:
            found_all = mm(sent_pair[:, (b - 1) * LANES : (b + 2) * LANES], own_hot[b - 4])
        value = held.at[b % 2]
        total = [jnp.zeros((8, LANES), F32)] * SLOTS
        for u in range(CHANNELS // 16):
            rows = slice(16 * u, 16 * u + 16)
            low_rows = slice(CHANNELS + 16 * u, CHANNELS + 16 * u + 16)
            windows = [sent_all[rows, (b - 1 + w) * LANES : (b + w) * LANES] for w in range(3)]
            got = []
            message = jnp.zeros((16, LANES), F32)
            for k in range(SLOTS):
                cols = slice(k * LANES, (k + 1) * LANES)
                if own:
                    got.append(found_all[rows, cols] + found_all[low_rows, cols])
                else:
                    found = [pick(window, lanes[k]) for window in windows]
                    got.append(jnp.where(parts[k] == 0, found[0], jnp.where(parts[k] == 1, found[1], found[2])))
                message = message + radial[rows, cols] * got[k]
            _, steep = silu_parts(message)
            back = col[3, rows] * steep
            for k in range(SLOTS):
                cols = slice(k * LANES, (k + 1) * LANES)
                high, low = split(radial[rows, cols] * back)
                value[rows, cols] = high.astype(BF16)
                value[low_rows, cols] = low.astype(BF16)
                if 3 <= b <= 8:
                    pull = got[k] * back * steepness[rows, cols]
                    total[k] = total[k] + pull[0:8] + pull[8:16]
            yield
        if 3 <= b <= 8:
            for k in range(SLOTS):
                pulls[b, :, k * LANES : (k + 1) * LANES] = total[k]

    def scatter_work(b):
        ws = reach(b, 3, 8)
        chosen, value = marks(b, ws), held.at[b % 2]
        out = None
        for u in range(4):
            cols = slice(u * 2 * LANES, (u + 1) * 2 * LANES)
            one = mm_nt(chosen[:, cols], value[:, cols])
            out = one if out is None else out + one
            yield
        add_rows(dg, 3, b, ws, out)

    def together(*works):
        works = list(works)
        while works:
            works = [work for work in works if next(work, "end") != "end"]

    together(block_work(2))
    for b in range(3, 10):
        together(scatter_work(b - 1), block_work(b))
    together(scatter_work(9))

    def finish(b, sums):
        kind = kinds[b]
        rows = []
        for k in range(SLOTS):
            cols = slice(k * LANES, (k + 1) * LANES)
            weight = sums[0:8] + wide_row(kind, k) * sums[8:16]
            rows.append(jnp.sum(bpr[b, :, cols] * weight + pulls[b, :, cols], axis=0, keepdims=True))
        pull = jnp.concatenate(rows, axis=0) * geo[b, 3]
        pieces = []
        for c in range(3):
            value = pull * geo[b, c]
            if 4 <= b <= 7:
                acc[b - 4, c] = jnp.sum(value, axis=0, keepdims=True)
            pieces.append(split(value))
        lines = []
        for h in range(2):
            for c in range(3):
                lines.append(jnp.concatenate([jnp.where(slot == k, pieces[c][h], 0.0) for k in range(SLOTS)], axis=1))
        ws = reach(b, 4, 7)
        out = mm_nt(jnp.concatenate(lines, axis=0).astype(BF16), marks(b, ws)[...])
        for c in range(3):
            both = out[8 * c : 8 * c + 8] + out[24 + 8 * c : 32 + 8 * c]
            for i, w in enumerate(ws):
                target = b - 5 + w
                piece = both[:, i * LANES : (i + 1) * LANES]
                if (c, target) in met_blocks:
                    met[target, c] += piece
                else:
                    met[target, c] = piece
                    met_blocks.add((c, target))

    met_blocks = set()

    for b in range(3, 9, 2):
        cols = slice(b * LANES, (b + 2) * LANES)
        high, low = split(dg[(b - 3) * LANES : (b - 1) * LANES, :])
        steep = mm_nt(l5[...], jnp.concatenate([high, low, high], axis=1).astype(BF16))
        steep = steep + jnp.concatenate([col[2], col[2]], axis=1)
        sums = mm(l6[...], right_stack(steep * slope[:, cols]))
        for i in range(2):
            finish(b + i, sums[:, i * LANES : (i + 1) * LANES])

    away = []
    for c in range(3):
        back = [acc[i, c] - jnp.sum(met[i, c], axis=0, keepdims=True) for i in range(SLAB_BLOCKS)]
        away.append(jnp.concatenate(back, axis=1))
    return jnp.concatenate(away, axis=0)


def fill_region(xs, packs, rows_of):
    for b in range(12):
        lanes = slice((b % 4) * LANES, (b % 4 + 1) * LANES)
        pack = packs[b // 4]
        xs[b, 0:3, :] = rows_of(b // 4)[:, lanes]
        xs[b, 3:4, :] = pack[ROW_KIND : ROW_KIND + 1, lanes]


def lane_total(x):
    x = x[:, 0:LANES] + x[:, LANES : 2 * LANES] + x[:, 2 * LANES : 3 * LANES] + x[:, 3 * LANES : 4 * LANES]
    return jnp.sum(x, axis=1, keepdims=True)


def dot3(a, b):
    return jnp.sum(a * b, axis=0, keepdims=True)


def kept_shapes():
    wide = 12 * LANES
    return [
        ((12, 8, LANES), jnp.int32),
        ((12, 8, LANES), F32),
        ((12, 4, 8, LANES), F32),
        ((12, 16, SLOTS * LANES), BF16),
        ((12, 16, SLOTS * LANES), BF16),
        ((12, 8, SLOTS * LANES), F32),
        ((CHANNELS, wide), F32),
        ((2 * CHANNELS, wide), BF16),
        ((CHANNELS, wide), F32),
    ]


def forward_scratch():
    return [pltpu.VMEM((12, 8, LANES), F32), pltpu.VMEM((48, 12 * LANES), BF16)]


def back_scratch():
    return [
        pltpu.VMEM((6 * LANES, 2 * CHANNELS), F32),
        pltpu.VMEM((12, 8, SLOTS * LANES), F32),
        pltpu.VMEM((SLAB_BLOCKS, 3, SLOTS, LANES), F32),
        pltpu.VMEM((SLAB_BLOCKS, 3, 1, LANES), F32),
        pltpu.VMEM((2, 2 * CHANNELS, SLOTS * LANES), BF16),
    ]


def by_parity(sibling, across):
    even = jnp.full(sibling.shape, lax.axis_index("dom") % 2, jnp.int32) == 0
    return jnp.where(even, across, sibling), jnp.where(even, sibling, across)


def first_kernel(sibling_ref, po_ref, across_ref, own_hot, *rest):
    weights, (out_ref, pl_ref, pr_ref, side_hot), scr = rest[:6], rest[6:10], rest[10:]
    xs, sst, kept = scr[0], scr[1], scr[2:11]
    pl_ref[...], pr_ref[...] = by_parity(sibling_ref[...], across_ref[...])
    packs = [pl_ref, po_ref, pr_ref]
    mark_sides(packs, side_hot)
    fill_region(xs, packs, lambda s: packs[s][ROW_X : ROW_X + 3, :])
    forward_parts(packs, weights, xs, sst, kept)
    out_ref[...] = force_parts(weights, own_hot, side_hot, kept, *scr[11:])


def block_row(*values):
    values = list(values) + [jnp.zeros((1, LANES), F32)] * (SLAB_BLOCKS - len(values))
    return jnp.concatenate(values, axis=1)


def blend_kernel(images, force_ref, po_ref, all_ref, out_ref, sums_ref):
    x = po_ref[ROW_X : ROW_X + 3, :]
    v = po_ref[ROW_V : ROW_V + 3, :]
    force = force_ref[...]
    here = lax.axis_index("img")
    before = all_ref[pl.ds(pl.multiple_of(8 * jnp.maximum(here - 1, 0), 8), 8), :][0:3]
    after = all_ref[pl.ds(pl.multiple_of(8 * jnp.minimum(here + 1, images - 1), 8), 8), :][0:3]
    before = jnp.where(here > 0, before, 0.0)
    after = jnp.where(here < images - 1, after, 0.0)
    tangent = after - before
    plus = after - x
    minus = x - before
    sums = jnp.concatenate(
        [
            dot3(force, tangent),
            dot3(force, force),
            dot3(tangent, tangent),
            dot3(plus, plus),
            dot3(minus, minus),
            dot3(v, v),
            jnp.zeros((2, x.shape[1]), F32),
        ],
        axis=0,
    )
    sums = jnp.broadcast_to(lane_total(sums), (8, LANES))
    sums_ref[...] = sums
    out_ref[0:3, :] = force
    out_ref[3:6, :] = tangent
    out_ref[6:7, :] = block_row(*[sums[i : i + 1] for i in range(4)])
    out_ref[7:8, :] = block_row(sums[4:5], sums[5:6])


def step_numbers(ft, ff, tt, pp, mn, vv, dt, alpha, flagged, climbing, inside):
    root = jnp.sqrt(tt + TINY_VALUE)
    along = ft / root
    spring = SPRING_CONSTANT * (jnp.sqrt(pp) - jnp.sqrt(mn))
    factor = jnp.where(climbing, -2.0 * along, spring - along)
    band = jnp.maximum(ff + 2.0 * factor * along + factor * factor * (tt / (tt + TINY_VALUE)), 0.0)
    new_dt = jnp.where(flagged, 0.5 * dt, jnp.minimum(1.1 * dt, STEP_LIMIT))
    pull = jnp.where(flagged, 0.0, alpha * jnp.sqrt(vv / (band + TINY_VALUE))) + new_dt
    keep = jnp.where(flagged, 0.0, 1.0 - alpha)
    new_alpha = jnp.where(flagged, ALPHA_START, 0.99 * alpha)
    keep = jnp.where(inside, keep, 0.0)
    pull = jnp.where(inside, pull, 0.0)
    return (
        jnp.where(inside, along, 0.0),
        jnp.where(inside, spring, 0.0),
        keep,
        pull,
        pull * factor / root,
        new_dt,
        new_alpha,
    )


def add_kernel(a_ref, b_ref, out_ref):
    out_ref[...] = a_ref[...] + b_ref[...]


def join_kernel(a_ref, b_ref, out_ref):
    count = a_ref.shape[0]
    out_ref[0:count] = a_ref[...]
    out_ref[count : 2 * count] = b_ref[...]


def number_kernel(dt_ref, flag_ref, climb_ref, out_ref):
    flags = [flag_ref[0, s].astype(F32) for s in range(flag_ref.shape[1])]
    for i, value in enumerate([dt_ref[0], climb_ref[0].astype(F32)] + flags):
        out_ref[i : i + 1, :] = jnp.full((1, LANES), value, F32)


def second_kernel(images, domains, number_ref, pl_ref, po_ref, pr_ref, own_ref, near_ref, far_ref, *rest):
    count = 2 if domains == 4 else 1
    parts, rest = rest[:count], rest[count:]
    (own_hot, side_hot), weights, (out_ref, record_ref), scr = rest[:2], rest[2:8], rest[8:10], rest[10:]
    packs = [pl_ref, po_ref, pr_ref]
    here = lax.axis_index("img")
    sums = parts[0][...]
    if domains == 4:
        sums = sums + parts[1][...]
    got = [sums[i : i + 1, :] for i in range(6)]
    if domains == 4:
        for one in (near_ref, far_ref):
            for i in range(6):
                got[i] = got[i] + one[6 + i // 4 : 7 + i // 4, (i % 4) * LANES : (i % 4 + 1) * LANES]
    ft, ff, tt, pp, mn, vv = got
    beside = by_parity(near_ref[0:6, :], far_ref[0:6, :])
    shape = (1, LANES)
    along, spring, keep, pull, side, dt, alpha = step_numbers(
        ft,
        ff,
        tt,
        pp,
        mn,
        vv,
        number_ref[0:1, :],
        jnp.full(shape, ALPHA_START, F32),
        number_ref[2:3, :] == 1.0,
        number_ref[1:2, :] == jnp.full(shape, here, jnp.int32).astype(F32),
        jnp.full(shape, jnp.where((here >= 1) & (here <= images - 2), 1, 0), jnp.int32) == 1,
    )
    messages = [beside[0], own_ref[0:6, :], beside[1]]

    def wide(s):
        return jnp.concatenate([s] * SLAB_BLOCKS, axis=1)

    speeds = [
        wide(keep) * p[ROW_V : ROW_V + 3, :] + wide(pull) * m[0:3, :] + wide(side) * m[3:6, :]
        for p, m in zip(packs, messages)
    ]
    moved = [p[ROW_X : ROW_X + 3, :] + wide(dt) * s for p, s in zip(packs, speeds)]
    xs, sst, kept = scr[0], scr[1], scr[2:11]
    fill_region(xs, packs, lambda s: moved[s])
    forward_parts(packs, weights, xs, sst, kept)
    force = force_parts(weights, own_hot, side_hot, kept, *scr[11:])
    for c in range(3):
        for i in range(SLAB_BLOCKS):
            lanes = slice(i * LANES, (i + 1) * LANES)
            row = 4 * c + i
            out_ref[0, row : row + 1, :] = speeds[1][c : c + 1, lanes]
            out_ref[0, 12 + row : 13 + row, :] = force[c : c + 1, lanes]
            out_ref[0, 24 + row : 25 + row, :] = moved[1][c : c + 1, lanes]
    out_ref[0, 36:37, :] = dt
    out_ref[0, 37:38, :] = alpha
    out_ref[0, 38:40, :] = jnp.broadcast_to(number_ref[3:4, :], (2, LANES))
    record_ref[0:1, :] = along
    record_ref[1:2, :] = spring
    record_ref[2:3, :] = number_ref[1:2, :]


PRODUCTS = (
    [("f", "t"), ("f", "f"), ("t", "t"), ("p", "p"), ("d", "d"), ("v", "v")]
    + [("d", "v"), ("d", "f"), ("d", "t"), ("d", "V"), ("d", "F"), ("d", "T"), ("v", "f"), ("v", "t")]
    + [(a, b) for a in "vft" for b in "VFT"]
)


def gram_kernel(images, *refs):
    parts, (out_ref, state_ref, messages_ref) = refs[:-3], refs[-3:]
    rows = out_ref.shape[0]
    place = 0
    for part in parts:
        messages_ref[place : place + part.shape[0]] = part[...]
        place += part.shape[0]
    here = lax.axis_index("img")
    blank = [jnp.zeros((rows - images, LANES), F32)] if rows > images else []
    zero = jnp.zeros((1, LANES), F32)

    def gathered(row):
        return jnp.concatenate([messages_ref[here ^ i, row : row + 1, :] for i in range(images)] + blank, axis=0)

    def earlier(value):
        return jnp.concatenate([zero, value[0 : rows - 1]], axis=0)

    def later(value):
        return jnp.concatenate([value[1:images], zero] + blank, axis=0)

    number = lax.broadcasted_iota(jnp.int32, (rows, LANES), 0)
    held = number < images
    totals = [jnp.zeros((rows, LANES), F32) for _ in PRODUCTS]
    for row in range(3 * SLAB_BLOCKS):
        v, f, x = gathered(row), gathered(12 + row), gathered(24 + row)
        before = jnp.where(held, earlier(x), 0.0)
        after = later(x)
        t = after - before
        table = {"f": f, "v": v, "t": t, "p": after - x, "d": x - before}
        table["F"], table["V"], table["T"] = earlier(f), earlier(v), earlier(t)
        totals = [old + table[a] * table[b] for old, (a, b) in zip(totals, PRODUCTS)]
        state_ref[row : row + 1, :] = jnp.sum(jnp.where(number == here, t, 0.0), axis=0, keepdims=True)
    lane = lax.broadcasted_iota(jnp.int32, (rows, LANES), 1)
    result = jnp.zeros((rows, LANES), F32)
    for q, one in enumerate(totals):
        one = jnp.broadcast_to(jnp.sum(one, axis=1, keepdims=True), (rows, LANES))
        result = jnp.where(lane == q, one, result)
    out_ref[...] = result
    for i in range(3):
        state_ref[16 + rows * i : 16 + rows * (i + 1), :] = gathered(36 + i)


def final_kernel(images, atoms, own_ref, record_ref, state_ref, *rest):
    parts, (x_ref, v_ref, band_ref, path_ref) = rest[:-4], rest[-4:]
    rows = parts[0].shape[0]
    here = lax.axis_index("img")
    sums = parts[0][...]
    for one in parts[1:]:
        sums = sums + one[...]
    got = {
        pair: jnp.broadcast_to(sums[:, q : q + 1], (rows, LANES)) for q, pair in enumerate(PRODUCTS)
    }
    number = lax.broadcasted_iota(jnp.int32, (rows, LANES), 0)
    inside = (number >= 1) & (number <= images - 2)
    climb = jnp.broadcast_to(record_ref[2:3, :], (rows, LANES))
    dt0, alpha0, flag = (state_ref[16 + rows * i : 16 + rows * (i + 1), :] for i in range(3))
    along, spring, keep, pull, side, dt, _ = step_numbers(
        got["f", "t"],
        got["f", "f"],
        got["t", "t"],
        got["p", "p"],
        got["d", "d"],
        got["v", "v"],
        dt0,
        alpha0,
        flag == 1.0,
        number.astype(F32) == climb,
        inside,
    )

    def shifted(value):
        return jnp.concatenate([jnp.zeros((1, LANES), F32), value[0 : rows - 1]], axis=0)

    now = {"v": dt * keep, "f": dt * pull, "t": dt * side}
    old = {a.upper(): shifted(value) for a, value in now.items()}
    mine = now["v"] * now["v"] * got["v", "v"] + now["f"] * now["f"] * got["f", "f"]
    mine = mine + now["t"] * now["t"] * got["t", "t"]
    cross = now["v"] * now["f"] * got["v", "f"] + now["v"] * now["t"] * got["v", "t"]
    mine = mine + 2.0 * (cross + now["f"] * now["t"] * got["f", "t"])
    both = jnp.zeros((rows, LANES), F32)
    for a in "vft":
        both = both + now[a] * got["d", a]
    for b in "VFT":
        both = both - old[b] * got["d", b]
    for a in "vft":
        for b in "VFT":
            both = both - now[a] * old[b] * got[a, b]
    squared = got["d", "d"] + mine + shifted(mine) + 2.0 * both
    segment = jnp.sqrt(jnp.maximum(squared, 0.0) * (1.0 / (3.0 * atoms)))
    path = jnp.sum(jnp.where(number <= here, segment, 0.0), axis=0, keepdims=True)
    path_ref[...] = path[:, 0:1]
    keep, pull, side, dt, along, spring = (
        jnp.sum(jnp.where(number == here, value, 0.0), axis=0, keepdims=True)
        for value in (keep, pull, side, dt, along, spring)
    )

    for c in range(3):
        speeds, places = [], []
        for i in range(SLAB_BLOCKS):
            row = 4 * c + i
            speed = keep * own_ref[0, row : row + 1, :] + pull * own_ref[0, 12 + row : 13 + row, :]
            speed = speed + side * state_ref[row : row + 1, :]
            speeds.append(speed)
            places.append(own_ref[0, 24 + row : 25 + row, :] + dt * speed)
        v_ref[c] = jnp.concatenate(speeds, axis=1)
        x_ref[c] = jnp.concatenate(places, axis=1)
    band_ref[0] = jnp.concatenate([record_ref[0:1, 0:1], record_ref[1:2, 0:1]], axis=1)
    band_ref[1] = jnp.concatenate([along[:, 0:1], spring[:, 0:1]], axis=1)


VMEM_SPEC = pl.BlockSpec(memory_space=pltpu.VMEM)
SMEM_SPEC = pl.BlockSpec(memory_space=pltpu.SMEM)
HBM_SPEC = pl.BlockSpec(memory_space=pltpu.HBM)


def call(body, outs, scalars, arrays, scratch_shapes=(), flops=0, spec=VMEM_SPEC, vmem=24):
    return pl.pallas_call(
        body,
        out_shape=outs,
        in_specs=[SMEM_SPEC] * len(scalars) + [spec] * len(arrays),
        out_specs=jax.tree.map(lambda _: VMEM_SPEC, outs),
        scratch_shapes=list(scratch_shapes),
        compiler_params=pltpu.CompilerParams(vmem_limit_bytes=vmem * 1024 * 1024),
        cost_estimate=pl.CostEstimate(flops=flops, bytes_accessed=1 << 18, transcendentals=0),
    )(*scalars, *arrays)


def swap(array, axis, partner):
    return lax.ppermute(array, axis, [(i, partner(i)) for i in range(lax.axis_size(axis))])


def exchanged(sums, axis):
    count = lax.axis_size(axis)
    if count == 4:
        return [sums] + [swap(sums, axis, lambda i, by=by: i ^ by) for by in (2, 3, 1)]
    distance = 1
    while distance < count:
        more = swap(sums, axis, lambda i, by=distance: i ^ by)
        sums = call(add_kernel, jax.ShapeDtypeStruct(sums.shape, F32), (), (sums, more))
        distance *= 2
    return [sums]


def collected(array, axis):
    count = lax.axis_size(axis)
    if count == 4:
        far = [swap(array, axis, lambda i, by=by: i ^ by) for by in (3, 2, 1)]
        return [array] + far[::-1]
    distance = 1
    while distance < count:
        more = swap(array, axis, lambda i, by=distance: i ^ by)
        shape = jax.ShapeDtypeStruct((2 * distance,) + array.shape[1:], F32)
        array = call(join_kernel, shape, (), (array, more))
        distance *= 2
    return [array]


def local(
    disp,
    veloc,
    time_step,
    reset_flags,
    climb,
    species,
    neighbours,
    counts,
    lattice,
    embed,
    radial_weight,
    mix_weight,
    update_weight,
    readout,
):
    atoms = disp.shape[2]
    images = lax.axis_size("img")
    domains = lax.axis_size("dom")
    assert disp.shape[0] == 1 and atoms == SLAB_BLOCKS * LANES and domains >= 4
    assert domains & (domains - 1) == 0 and images & (images - 1) == 0
    shape = jax.ShapeDtypeStruct
    x = jnp.transpose(disp, (1, 0, 2))
    v = jnp.transpose(veloc, (1, 0, 2))
    small = (x, v, species, neighbours, counts, embed, readout, radial_weight, mix_weight, update_weight)
    sent, pack = call(
        pack_kernel,
        (shape((PACK_ROWS, atoms), F32), shape((OWN_ROWS, atoms), F32)),
        (),
        (*small, jnp.transpose(lattice, (1, 0, 2))),
        [pltpu.VMEM(a.shape, a.dtype) for a in small] + [pltpu.SemaphoreType.DMA((16,))],
        spec=HBM_SPEC,
        vmem=63,
    )
    sibling = swap(sent, "dom", lambda i: i ^ 1)
    across = swap(sent, "dom", lambda i: (i + 2 * (i % 2) - 1) % domains)
    own_hot, *weights, x_copy = call(
        prepare_kernel,
        (
            shape((SLAB_BLOCKS, 3 * LANES, SLOTS * LANES), BF16),
            shape((CHANNELS, 48), BF16),
            shape((CHANNELS, 192), BF16),
            shape((CHANNELS, 32), BF16),
            shape((CHANNELS, 3 * LANES), BF16),
            shape((16, 192), BF16),
            shape((4, CHANNELS, LANES), F32),
            shape((8, atoms), F32),
        ),
        (),
        (pack,),
        flops=100000000,
    )
    everyone = lax.all_gather(x_copy, "img", tiled=True)
    force_scratch = forward_scratch() + [pltpu.VMEM(*one) for one in kept_shapes()] + back_scratch()
    force, left, right, side_hot = call(
        first_kernel,
        (
            shape((3, atoms), F32),
            shape(sent.shape, F32),
            shape(sent.shape, F32),
            shape((SIDE_ROWS, SLOTS * LANES), BF16),
        ),
        (),
        (sibling, pack, across, own_hot, *weights),
        force_scratch,
        flops=1000000000,
    )
    message, sums = call(
        functools.partial(blend_kernel, images),
        (shape((8, atoms), F32), shape((8, LANES), F32)),
        (),
        (force, pack, everyone),
    )
    far = swap(message, "dom", lambda i: (i + 2 * (i % 2) - 1) % domains)
    if domains == 4:
        parts = [sums, swap(sums, "dom", lambda i: i ^ 2)]
    else:
        parts = exchanged(sums, "dom")
    near = swap(message, "dom", lambda i: i ^ 1)
    numbers = call(number_kernel, shape((8, LANES), F32), (time_step, jnp.transpose(reset_flags), climb), ())
    state, record = call(
        functools.partial(second_kernel, images, domains),
        (shape((1, 40, LANES), F32), shape((3, LANES), F32)),
        (),
        (numbers, left, pack, right, message, near, far, *parts, own_hot, side_hot, *weights),
        force_scratch,
        flops=1000000000,
    )
    rows = 8 * ((images + 7) // 8)
    sums, extra = call(
        functools.partial(gram_kernel, images),
        (shape((rows, LANES), F32), shape((16 + 3 * rows, LANES), F32)),
        (),
        collected(state, "img"),
        [pltpu.VMEM((images, 40, LANES), F32)],
    )
    new_x, new_v, records, path = call(
        functools.partial(final_kernel, images, atoms * domains),
        (shape(x.shape, F32), shape(x.shape, F32), shape((2, 1, 2), F32), shape((1, 1), F32)),
        (),
        (state, record, extra, *exchanged(sums, "dom")),
    )
    return (
        jnp.transpose(new_x, (1, 0, 2)),
        jnp.transpose(new_v, (1, 0, 2)),
        jnp.transpose(records, (0, 2, 1)),
        path.reshape(1),
    )


def solution(mesh):
    in_specs = (
        P(("group", "img"), None, "dom"),
        P(("group", "img"), None, "dom"),
        P(("group", "img")),
        P(None, ("group", "img")),
        P("group"),
        P(("group", "dom")),
        P(None, ("group", "dom")),
        P(("group", "dom")),
        P(None, None, ("group", "dom")),
        P(),
        P(),
        P(),
        P(),
        P(),
    )
    out_specs = (
        P(("group", "img"), None, "dom"),
        P(("group", "img"), None, "dom"),
        P(None, None, ("group", "img")),
        P(("group", "img")),
    )
    return jax.shard_map(local, mesh=mesh, in_specs=in_specs, out_specs=out_specs, check_vma=False)
```

```python
import functools
import math

import jax
import jax.numpy as jnp
from jax import lax
from jax.experimental import pallas as pl
from jax.experimental.pallas import tpu as pltpu
from jax.sharding import PartitionSpec as P

F32 = jnp.float32
BF16 = jnp.bfloat16
PRECISE = lax.Precision.HIGHEST
SPRING_CONSTANT = 0.5
ALPHA_START = 0.1
STEP_LIMIT = 0.3
TINY_VALUE = 1e-06
SOFTENING = 0.25
LANES = 128
SLOTS = 8
BASIS = 8
CHANNELS = 64
SLAB_BLOCKS = 4
ROW_X = 32
ROW_COUNT = 35
ROW_KIND = 36
ROW_V = 37
PACK_ROWS = 40
OWN_ROWS = PACK_ROWS + CHANNELS + BASIS
NT = (((1,), (1,)), ((), ()))


def split(x):
    high = x.astype(BF16).astype(F32)
    return high, x - high


def left_stack(w):
    high, low = split(w)
    return jnp.concatenate([high, high, low], axis=1)


def right_stack(x):
    high, low = split(x)
    high = high.astype(BF16)
    return jnp.concatenate([high, low.astype(BF16), high], axis=0)


def pair_stack(x):
    high, low = split(x)
    return jnp.concatenate([high.astype(BF16), low.astype(BF16)], axis=0)


def mm(a, b):
    return jnp.dot(a, b, preferred_element_type=F32)


def mm_nt(a, b):
    return lax.dot_general(a, b, NT, preferred_element_type=F32)


def pack_kernel(*refs):
    sources, (out_ref, own_ref), held, sems = refs[:11], refs[11:13], refs[13:23], refs[23]
    lattice = sources[10]
    pairs = list(zip(sources, held))
    for c in range(3):
        rows = pl.ds(8 + 8 * c, 8)
        pairs += [(lattice.at[c], out_ref.at[rows]), (lattice.at[c], own_ref.at[rows])]
    copies = [pltpu.make_async_copy(a, b, sems.at[i]) for i, (a, b) in enumerate(pairs)]
    for one in copies:
        one.start()
    for one in copies:
        one.wait()
    x, v, species, nbr, counts, embed, readout, radial, mix, update = held
    for ref in (out_ref, own_ref):
        ref[0:8, :] = nbr[...].astype(F32)
        for c in range(3):
            ref[ROW_X + c : ROW_X + c + 1, :] = x[c]
            ref[ROW_V + c : ROW_V + c + 1, :] = v[c]
        ref[ROW_COUNT : ROW_COUNT + 1, :] = counts[...].astype(F32).reshape(1, -1)
        ref[ROW_KIND : ROW_KIND + 1, :] = species[...].astype(F32).reshape(1, -1)
    top, low = PACK_ROWS, PACK_ROWS + CHANNELS
    for i, value in enumerate([mix[0], mix[1], update[0], update[1]]):
        own_ref[top:low, i * LANES : i * LANES + CHANNELS] = value
    for i, value in enumerate([radial[0], radial[1], embed[...], readout[...].reshape(1, CHANNELS)]):
        own_ref[low : low + value.shape[0], i * LANES : i * LANES + CHANNELS] = value


def prepare_kernel(po_ref, *rest):
    own_hot, l1_ref, l2_ref, l3_ref, l5_ref, l6_ref, col_ref, copy_ref = rest
    for b in range(SLAB_BLOCKS):
        mark(window_index(po_ref, b), [0, 1, 2], own_hot.at[b])
    for c in range(3):
        copy_ref[c] = po_ref[ROW_X + c : ROW_X + c + 1, :]

    def raw(first, count, i):
        return po_ref[first : first + count, i * LANES : i * LANES + CHANNELS]

    low = PACK_ROWS + CHANNELS
    mix_ref = [raw(PACK_ROWS, CHANNELS, i) for i in range(2)]
    update_ref = [raw(PACK_ROWS, CHANNELS, 2 + i) for i in range(2)]
    radial_ref = [raw(low, BASIS, i) for i in range(2)]
    embed_ref, readout = raw(low, 2, 2), raw(low, 1, 3)
    eye = (
        lax.broadcasted_iota(jnp.int32, (CHANNELS, CHANNELS), 0)
        == lax.broadcasted_iota(jnp.int32, (CHANNELS, CHANNELS), 1)
    ).astype(F32)

    def turned(x):
        return lax.dot_general(eye, x, NT, precision=PRECISE, preferred_element_type=F32)

    base0 = embed_ref[0:1, :]
    base1 = embed_ref[1:2, :] - base0
    rows = jnp.concatenate([base0, base1], axis=0)
    sent = jnp.dot(rows, mix_ref[0], precision=PRECISE, preferred_element_type=F32)
    scale = 1.0 / math.sqrt(SLOTS)
    first = jnp.concatenate([radial_ref[0] * sent[0:1], radial_ref[0] * sent[1:2]], axis=0) * scale
    second = radial_ref[1] * scale
    folded = jnp.dot(update_ref[0], mix_ref[1], precision=PRECISE, preferred_element_type=F32)
    mix_t = turned(mix_ref[1])
    l1_ref[...] = left_stack(turned(first)).astype(BF16)
    l2_ref[...] = left_stack(turned(folded)).astype(BF16)
    high, low = split(turned(second))
    l3_ref[...] = jnp.concatenate([high, high, low, jnp.zeros_like(high)], axis=1).astype(BF16)
    high, low = split(folded)
    l5_ref[...] = jnp.concatenate([high, high, high, high, low, low], axis=1).astype(BF16)
    l6_ref[...] = left_stack(first).astype(BF16)
    wide = (CHANNELS, LANES)
    col_ref[0] = jnp.broadcast_to(jnp.sum(mix_t * base0, axis=1, keepdims=True), wide)
    col_ref[1] = jnp.broadcast_to(jnp.sum(mix_t * base1, axis=1, keepdims=True), wide)
    col_ref[2] = jnp.broadcast_to(jnp.sum(update_ref[0] * readout, axis=1, keepdims=True), wide)
    col_ref[3] = jnp.broadcast_to(jnp.sum(update_ref[1] * readout, axis=1, keepdims=True), wide)


def sin_cos(t):
    q = t * t
    s = -1.0 / 39916800.0
    for c in (1.0 / 362880.0, -1.0 / 5040.0, 1.0 / 120.0, -1.0 / 6.0, 1.0):
        s = s * q + c
    k = 1.0 / 479001600.0
    for c in (-1.0 / 3628800.0, 1.0 / 40320.0, -1.0 / 720.0, 1.0 / 24.0, -0.5, 1.0):
        k = k * q + c
    return s * t, k


def wide_row(x, row):
    return jnp.broadcast_to(x[row : row + 1, :], (8, x.shape[1]))


def silu_parts(m):
    sig = 1.0 / (1.0 + jnp.exp(-m))
    return m * sig, sig * (1.0 + m * (1.0 - sig))


def pick(values, lanes):
    return jnp.take_along_axis(values, lanes, axis=1, mode="promise_in_bounds")


def reach(b, first, last):
    return [w for w in range(3) if first <= b - 1 + w <= last]


SIDES = {2: 0, 3: 1, 8: 2, 9: 3}


def mark(index, ws, target):
    count = len(ws) * LANES
    row_id = (lax.broadcasted_iota(jnp.int32, (count, LANES), 0) + ws[0] * LANES).astype(jnp.int16)
    one, zero = jnp.ones((count, LANES), BF16), jnp.zeros((count, LANES), BF16)
    for k in range(SLOTS):
        wanted = jnp.broadcast_to(index[k : k + 1, :], (16, LANES)).astype(jnp.int16)
        wanted = jnp.concatenate([wanted] * (count // 16), axis=0)
        target[:, k * LANES : (k + 1) * LANES] = jnp.where(row_id == wanted, one, zero)


def window_index(pack, b):
    lanes = slice((b % 4) * LANES, (b % 4 + 1) * LANES)
    return pack[0:8, lanes].astype(jnp.int32) - LANES * (b % 4)


def mark_sides(packs, side):
    for b, place in SIDES.items():
        mark(window_index(packs[b // 4], b), [0, 1, 2], side.at[place])


def forward_parts(packs, weights, xs, sst, kept):
    l1, l2, l3, l5, l6, col = weights
    (kinds, geo, bst, bps, bpr, sent_pair, slope) = kept
    centre = 2.0 + 0.5 * lax.broadcasted_iota(jnp.int32, (BASIS, LANES), 0).astype(F32)
    slot = lax.broadcasted_iota(jnp.int32, (SLOTS, LANES), 0)

    def part_rows(value):
        high, low = split(value)
        return jnp.concatenate([high, low], axis=0).astype(BF16)

    def pairs(b):
        pack = packs[b // 4]
        lanes = slice((b % 4) * LANES, (b % 4 + 1) * LANES)
        index = window_index(pack, b)
        inner = index & (LANES - 1)
        part = index >> 7

        def taken(row):
            got = [
                pick(jnp.broadcast_to(xs[b - 1 + w, row : row + 1, :], (SLOTS, LANES)), inner)
                for w in range(3)
            ]
            return jnp.where(part == 0, got[0], jnp.where(part == 1, got[1], got[2]))

        vec = [
            pack[8 + 8 * c : 16 + 8 * c, lanes] + taken(c) - jnp.broadcast_to(xs[b, c : c + 1, :], (SLOTS, LANES))
            for c in range(3)
        ]
        kind = taken(3)
        dist = jnp.sqrt(vec[0] * vec[0] + vec[1] * vec[1] + vec[2] * vec[2] + SOFTENING)
        live = (slot.astype(F32) < jnp.broadcast_to(pack[ROW_COUNT : ROW_COUNT + 1, lanes], (SLOTS, LANES))).astype(F32)
        turns = dist * (1.0 / 12.0)
        turns = turns - jnp.floor(turns + 0.5)
        sine, cosine = sin_cos(turns * math.pi)
        envelope = cosine * cosine * live
        slant = cosine * sine * live * (-math.pi / 6.0)
        if 3 <= b <= 8:
            kinds[b] = kind
            for c in range(3):
                geo[b, c] = vec[c]
            geo[b, 3] = 1.0 / dist
        total = jnp.zeros((BASIS, LANES), F32)
        total_kind = jnp.zeros((BASIS, LANES), F32)
        for k in range(SLOTS):
            away = wide_row(dist, k) - centre
            gauss = jnp.exp(-4.0 * (away * away))
            env_k = wide_row(envelope, k)
            value = gauss * env_k
            total = total + value
            total_kind = total_kind + value * wide_row(kind, k)
            cols = slice(k * LANES, (k + 1) * LANES)
            if 2 <= b <= 9:
                bst[b, :, cols] = part_rows(value)
            if 3 <= b <= 8:
                value = gauss * (wide_row(slant, k) - 8.0 * away * env_k)
                bpr[b, :, cols] = value
                bps[b, :, cols] = part_rows(value)
        high, low = split(jnp.concatenate([total, total_kind], axis=0))
        sst[:, b * LANES : (b + 1) * LANES] = jnp.concatenate([high, low, high], axis=0).astype(BF16)

    for b in range(1, 11):
        pairs(b)

    for b in range(1, 11, 2):
        cols = slice(b * LANES, (b + 2) * LANES)
        value, steep = silu_parts(mm(l1[...], sst[:, cols]))
        sent = mm(l2[...], right_stack(value))
        for i in range(2):
            one = sent[:, i * LANES : (i + 1) * LANES]
            one = one + col[0] + col[1] * jnp.broadcast_to(xs[b + i, 3:4, :], (CHANNELS, LANES))
            sent_pair[:, (b + i) * LANES : (b + i + 1) * LANES] = pair_stack(one)
        slope[:, cols] = steep


def force_parts(weights, own_hot, side_hot, kept, dg, pulls, met, acc, held):
    l1, l2, l3, l5, l6, col = weights
    (kinds, geo, bst, bps, bpr, sent_pair, slope) = kept
    slot = lax.broadcasted_iota(jnp.int32, (SLOTS, LANES), 0)

    def marks(b, ws):
        rows = slice(ws[0] * LANES, (ws[-1] + 1) * LANES)
        return side_hot.at[SIDES[b], rows] if b in SIDES else own_hot.at[b - 4, rows]

    def add_rows(sums, first, b, ws, out):
        for i, w in enumerate(ws):
            target = b - 1 + w
            piece = out[i * LANES : (i + 1) * LANES]
            rows = slice((target - first) * LANES, (target - first + 1) * LANES)
            if (first, target) in started:
                sums[rows, :] += piece
            else:
                sums[rows, :] = piece
                started.add((first, target))

    started = set()

    def block_work(b):
        found = mm(sent_pair[:, (b - 1) * LANES : (b + 2) * LANES], marks(b, [0, 1, 2])[...])
        basis = bst[b]
        radial = mm(l3[...], jnp.concatenate([basis, basis], axis=0))
        if 3 <= b <= 8:
            basis = bps[b]
            steepness = mm(l3[...], jnp.concatenate([basis, basis], axis=0))
        value = held.at[b % 2]
        total = [jnp.zeros((8, LANES), F32)] * SLOTS
        for u in range(CHANNELS // 16):
            rows = slice(16 * u, 16 * u + 16)
            low_rows = slice(CHANNELS + 16 * u, CHANNELS + 16 * u + 16)
            got = []
            message = jnp.zeros((16, LANES), F32)
            for k in range(SLOTS):
                cols = slice(k * LANES, (k + 1) * LANES)
                got.append(found[rows, cols] + found[low_rows, cols])
                message = message + radial[rows, cols] * got[k]
            _, steep = silu_parts(message)
            back = col[3, rows] * steep
            for k in range(SLOTS):
                cols = slice(k * LANES, (k + 1) * LANES)
                high, low = split(radial[rows, cols] * back)
                value[rows, cols] = high.astype(BF16)
                value[low_rows, cols] = low.astype(BF16)
                if 3 <= b <= 8:
                    pull = got[k] * back * steepness[rows, cols]
                    total[k] = total[k] + pull[0:8] + pull[8:16]
            yield
        if 3 <= b <= 8:
            for k in range(SLOTS):
                pulls[b, :, k * LANES : (k + 1) * LANES] = total[k]

    def scatter_work(b):
        ws = reach(b, 3, 8)
        chosen, value = marks(b, ws), held.at[b % 2]
        out = None
        for u in range(4):
            cols = slice(u * 2 * LANES, (u + 1) * 2 * LANES)
            one = mm_nt(chosen[:, cols], value[:, cols])
            out = one if out is None else out + one
            yield
        add_rows(dg, 3, b, ws, out)

    def together(*works):
        works = list(works)
        while works:
            works = [work for work in works if next(work, "end") != "end"]

    together(block_work(2))
    for b in range(3, 10):
        together(scatter_work(b - 1), block_work(b))
    together(scatter_work(9))

    def finish(b, sums):
        kind = kinds[b]
        rows = []
        for k in range(SLOTS):
            cols = slice(k * LANES, (k + 1) * LANES)
            weight = sums[0:8] + wide_row(kind, k) * sums[8:16]
            rows.append(jnp.sum(bpr[b, :, cols] * weight + pulls[b, :, cols], axis=0, keepdims=True))
        pull = jnp.concatenate(rows, axis=0) * geo[b, 3]
        pieces = []
        for c in range(3):
            value = pull * geo[b, c]
            if 4 <= b <= 7:
                acc[b - 4, c] = jnp.sum(value, axis=0, keepdims=True)
            pieces.append(split(value))
        lines = []
        for h in range(2):
            for c in range(3):
                lines.append(jnp.concatenate([jnp.where(slot == k, pieces[c][h], 0.0) for k in range(SLOTS)], axis=1))
        ws = reach(b, 4, 7)
        out = mm_nt(jnp.concatenate(lines, axis=0).astype(BF16), marks(b, ws)[...])
        for c in range(3):
            both = out[8 * c : 8 * c + 8] + out[24 + 8 * c : 32 + 8 * c]
            for i, w in enumerate(ws):
                target = b - 5 + w
                piece = both[:, i * LANES : (i + 1) * LANES]
                if (c, target) in met_blocks:
                    met[target, c] += piece
                else:
                    met[target, c] = piece
                    met_blocks.add((c, target))

    met_blocks = set()

    for b in range(3, 9, 2):
        cols = slice(b * LANES, (b + 2) * LANES)
        high, low = split(dg[(b - 3) * LANES : (b - 1) * LANES, :])
        steep = mm_nt(l5[...], jnp.concatenate([high, low, high], axis=1).astype(BF16))
        steep = steep + jnp.concatenate([col[2], col[2]], axis=1)
        sums = mm(l6[...], right_stack(steep * slope[:, cols]))
        for i in range(2):
            finish(b + i, sums[:, i * LANES : (i + 1) * LANES])

    away = []
    for c in range(3):
        back = [acc[i, c] - jnp.sum(met[i, c], axis=0, keepdims=True) for i in range(SLAB_BLOCKS)]
        away.append(jnp.concatenate(back, axis=1))
    return jnp.concatenate(away, axis=0)


def fill_region(xs, packs, rows_of):
    for b in range(12):
        lanes = slice((b % 4) * LANES, (b % 4 + 1) * LANES)
        pack = packs[b // 4]
        xs[b, 0:3, :] = rows_of(b // 4)[:, lanes]
        xs[b, 3:4, :] = pack[ROW_KIND : ROW_KIND + 1, lanes]


def lane_total(x):
    x = x[:, 0:LANES] + x[:, LANES : 2 * LANES] + x[:, 2 * LANES : 3 * LANES] + x[:, 3 * LANES : 4 * LANES]
    return jnp.sum(x, axis=1, keepdims=True)


def dot3(a, b):
    return jnp.sum(a * b, axis=0, keepdims=True)


def kept_shapes():
    wide = 12 * LANES
    return [
        ((12, 8, LANES), F32),
        ((12, 4, 8, LANES), F32),
        ((12, 16, SLOTS * LANES), BF16),
        ((12, 16, SLOTS * LANES), BF16),
        ((12, 8, SLOTS * LANES), F32),
        ((2 * CHANNELS, wide), BF16),
        ((CHANNELS, wide), F32),
    ]


def forward_scratch():
    return [pltpu.VMEM((12, 8, LANES), F32), pltpu.VMEM((48, 12 * LANES), BF16)]


def back_scratch():
    return [
        pltpu.VMEM((6 * LANES, 2 * CHANNELS), F32),
        pltpu.VMEM((12, 8, SLOTS * LANES), F32),
        pltpu.VMEM((SLAB_BLOCKS, 3, SLOTS, LANES), F32),
        pltpu.VMEM((SLAB_BLOCKS, 3, 1, LANES), F32),
        pltpu.VMEM((2, 2 * CHANNELS, SLOTS * LANES), BF16),
    ]


def by_parity(sibling, across):
    even = jnp.full(sibling.shape, lax.axis_index("dom") % 2, jnp.int32) == 0
    return jnp.where(even, across, sibling), jnp.where(even, sibling, across)


def first_kernel(x_ref, sibling_ref, po_ref, across_ref, *rest):
    weights, (pl_ref, pr_ref, side_hot, copy_ref), kept, (xs, sst) = rest[:6], rest[6:10], rest[10:17], rest[17:]
    copy_ref[...] = x_ref[...]
    pl_ref[...], pr_ref[...] = by_parity(sibling_ref[...], across_ref[...])
    packs = [pl_ref, po_ref, pr_ref]
    mark_sides(packs, side_hot)
    fill_region(xs, packs, lambda s: packs[s][ROW_X : ROW_X + 3, :])
    forward_parts(packs, weights, xs, sst, kept)


def first_back_kernel(own_hot, side_hot, *rest):
    weights, kept, out_ref, scr = rest[:6], rest[6:13], rest[13], rest[14:]
    out_ref[...] = force_parts(weights, own_hot, side_hot, kept, *scr)


def rows_of(ref):
    return jnp.concatenate([ref[c] for c in range(3)], axis=0)


def block_row(*values):
    values = list(values) + [jnp.zeros((1, LANES), F32)] * (SLAB_BLOCKS - len(values))
    return jnp.concatenate(values, axis=1)


def blend_kernel(images, force_ref, po_ref, before_ref, after_ref, out_ref, sums_ref):
    x = po_ref[ROW_X : ROW_X + 3, :]
    v = po_ref[ROW_V : ROW_V + 3, :]
    force = force_ref[...]
    here = lax.axis_index("img")
    before = jnp.where(here > 0, rows_of(before_ref), 0.0)
    after = jnp.where(here < images - 1, rows_of(after_ref), 0.0)
    tangent = after - before
    plus = after - x
    minus = x - before
    sums = jnp.concatenate(
        [
            dot3(force, tangent),
            dot3(force, force),
            dot3(tangent, tangent),
            dot3(plus, plus),
            dot3(minus, minus),
            dot3(v, v),
            jnp.zeros((2, x.shape[1]), F32),
        ],
        axis=0,
    )
    sums = jnp.broadcast_to(lane_total(sums), (8, LANES))
    sums_ref[...] = sums
    out_ref[0:3, :] = force
    out_ref[3:6, :] = tangent
    out_ref[6:7, :] = block_row(*[sums[i : i + 1] for i in range(4)])
    out_ref[7:8, :] = block_row(sums[4:5], sums[5:6])


def step_numbers(ft, ff, tt, pp, mn, vv, dt, alpha, flagged, climbing, inside):
    root = jnp.sqrt(tt + TINY_VALUE)
    along = ft / root
    spring = SPRING_CONSTANT * (jnp.sqrt(pp) - jnp.sqrt(mn))
    factor = jnp.where(climbing, -2.0 * along, spring - along)
    band = jnp.maximum(ff + 2.0 * factor * along + factor * factor * (tt / (tt + TINY_VALUE)), 0.0)
    new_dt = jnp.where(flagged, 0.5 * dt, jnp.minimum(1.1 * dt, STEP_LIMIT))
    pull = jnp.where(flagged, 0.0, alpha * jnp.sqrt(vv / (band + TINY_VALUE))) + new_dt
    keep = jnp.where(flagged, 0.0, 1.0 - alpha)
    new_alpha = jnp.where(flagged, ALPHA_START, 0.99 * alpha)
    keep = jnp.where(inside, keep, 0.0)
    pull = jnp.where(inside, pull, 0.0)
    return (
        jnp.where(inside, along, 0.0),
        jnp.where(inside, spring, 0.0),
        keep,
        pull,
        pull * factor / root,
        new_dt,
        new_alpha,
    )


def add_kernel(a_ref, b_ref, out_ref):
    out_ref[...] = a_ref[...] + b_ref[...]


def join_kernel(a_ref, b_ref, out_ref):
    count = a_ref.shape[0]
    out_ref[0:count] = a_ref[...]
    out_ref[count : 2 * count] = b_ref[...]


def number_kernel(dt_ref, flag_ref, climb_ref, out_ref):
    flags = [flag_ref[0, s].astype(F32) for s in range(flag_ref.shape[1])]
    for i, value in enumerate([dt_ref[0], climb_ref[0].astype(F32)] + flags):
        out_ref[i : i + 1, :] = jnp.full((1, LANES), value, F32)


def second_kernel(images, domains, number_ref, pl_ref, po_ref, pr_ref, own_ref, near_ref, far_ref, *rest):
    count = 2 if domains == 4 else 1
    parts, rest = rest[:count], rest[count:]
    (own_hot, side_hot), weights, (out_ref, record_ref), scr = rest[:2], rest[2:8], rest[8:10], rest[10:]
    packs = [pl_ref, po_ref, pr_ref]
    here = lax.axis_index("img")
    sums = parts[0][...]
    if domains == 4:
        sums = sums + parts[1][...]
    got = [sums[i : i + 1, :] for i in range(6)]
    if domains == 4:
        for one in (near_ref, far_ref):
            for i in range(6):
                got[i] = got[i] + one[6 + i // 4 : 7 + i // 4, (i % 4) * LANES : (i % 4 + 1) * LANES]
    ft, ff, tt, pp, mn, vv = got
    beside = by_parity(near_ref[0:6, :], far_ref[0:6, :])
    shape = (1, LANES)
    along, spring, keep, pull, side, dt, alpha = step_numbers(
        ft,
        ff,
        tt,
        pp,
        mn,
        vv,
        number_ref[0:1, :],
        jnp.full(shape, ALPHA_START, F32),
        number_ref[2:3, :] == 1.0,
        number_ref[1:2, :] == jnp.full(shape, here, jnp.int32).astype(F32),
        jnp.full(shape, jnp.where((here >= 1) & (here <= images - 2), 1, 0), jnp.int32) == 1,
    )
    messages = [beside[0], own_ref[0:6, :], beside[1]]

    def wide(s):
        return jnp.concatenate([s] * SLAB_BLOCKS, axis=1)

    speeds = [
        wide(keep) * p[ROW_V : ROW_V + 3, :] + wide(pull) * m[0:3, :] + wide(side) * m[3:6, :]
        for p, m in zip(packs, messages)
    ]
    moved = [p[ROW_X : ROW_X + 3, :] + wide(dt) * s for p, s in zip(packs, speeds)]
    xs, sst, kept = scr[0], scr[1], scr[2:9]
    fill_region(xs, packs, lambda s: moved[s])
    forward_parts(packs, weights, xs, sst, kept)
    force = force_parts(weights, own_hot, side_hot, kept, *scr[9:])
    for c in range(3):
        for i in range(SLAB_BLOCKS):
            lanes = slice(i * LANES, (i + 1) * LANES)
            row = 4 * c + i
            out_ref[0, row : row + 1, :] = speeds[1][c : c + 1, lanes]
            out_ref[0, 12 + row : 13 + row, :] = force[c : c + 1, lanes]
            out_ref[0, 24 + row : 25 + row, :] = moved[1][c : c + 1, lanes]
    out_ref[0, 36:37, :] = dt
    out_ref[0, 37:38, :] = alpha
    out_ref[0, 38:40, :] = jnp.broadcast_to(number_ref[3:4, :], (2, LANES))
    record_ref[0:1, :] = along
    record_ref[1:2, :] = spring
    record_ref[2:3, :] = number_ref[1:2, :]


PRODUCTS = (
    [("f", "t"), ("f", "f"), ("t", "t"), ("p", "p"), ("d", "d"), ("v", "v")]
    + [("d", "v"), ("d", "f"), ("d", "t"), ("d", "V"), ("d", "F"), ("d", "T"), ("v", "f"), ("v", "t")]
    + [(a, b) for a in "vft" for b in "VFT"]
)


def gram_kernel(images, *refs):
    parts, (out_ref, state_ref, messages_ref) = refs[:-3], refs[-3:]
    rows = out_ref.shape[0]
    place = 0
    for part in parts:
        messages_ref[place : place + part.shape[0]] = part[...]
        place += part.shape[0]
    here = lax.axis_index("img")
    blank = [jnp.zeros((rows - images, LANES), F32)] if rows > images else []
    zero = jnp.zeros((1, LANES), F32)

    def gathered(row):
        return jnp.concatenate([messages_ref[here ^ i, row : row + 1, :] for i in range(images)] + blank, axis=0)

    def earlier(value):
        return jnp.concatenate([zero, value[0 : rows - 1]], axis=0)

    def later(value):
        return jnp.concatenate([value[1:images], zero] + blank, axis=0)

    number = lax.broadcasted_iota(jnp.int32, (rows, LANES), 0)
    held = number < images
    totals = [jnp.zeros((rows, LANES), F32) for _ in PRODUCTS]
    for row in range(3 * SLAB_BLOCKS):
        v, f, x = gathered(row), gathered(12 + row), gathered(24 + row)
        before = jnp.where(held, earlier(x), 0.0)
        after = later(x)
        t = after - before
        table = {"f": f, "v": v, "t": t, "p": after - x, "d": x - before}
        table["F"], table["V"], table["T"] = earlier(f), earlier(v), earlier(t)
        totals = [old + table[a] * table[b] for old, (a, b) in zip(totals, PRODUCTS)]
        state_ref[row : row + 1, :] = jnp.sum(jnp.where(number == here, t, 0.0), axis=0, keepdims=True)
    lane = lax.broadcasted_iota(jnp.int32, (rows, LANES), 1)
    result = jnp.zeros((rows, LANES), F32)
    for q, one in enumerate(totals):
        one = jnp.broadcast_to(jnp.sum(one, axis=1, keepdims=True), (rows, LANES))
        result = jnp.where(lane == q, one, result)
    out_ref[...] = result
    for i in range(3):
        state_ref[16 + rows * i : 16 + rows * (i + 1), :] = gathered(36 + i)


def final_kernel(images, atoms, own_ref, record_ref, state_ref, *rest):
    parts, (x_ref, v_ref, band_ref, path_ref) = rest[:-4], rest[-4:]
    rows = parts[0].shape[0]
    here = lax.axis_index("img")
    sums = parts[0][...]
    for one in parts[1:]:
        sums = sums + one[...]
    got = {
        pair: jnp.broadcast_to(sums[:, q : q + 1], (rows, LANES)) for q, pair in enumerate(PRODUCTS)
    }
    number = lax.broadcasted_iota(jnp.int32, (rows, LANES), 0)
    inside = (number >= 1) & (number <= images - 2)
    climb = jnp.broadcast_to(record_ref[2:3, :], (rows, LANES))
    dt0, alpha0, flag = (state_ref[16 + rows * i : 16 + rows * (i + 1), :] for i in range(3))
    along, spring, keep, pull, side, dt, _ = step_numbers(
        got["f", "t"],
        got["f", "f"],
        got["t", "t"],
        got["p", "p"],
        got["d", "d"],
        got["v", "v"],
        dt0,
        alpha0,
        flag == 1.0,
        number.astype(F32) == climb,
        inside,
    )

    def shifted(value):
        return jnp.concatenate([jnp.zeros((1, LANES), F32), value[0 : rows - 1]], axis=0)

    now = {"v": dt * keep, "f": dt * pull, "t": dt * side}
    old = {a.upper(): shifted(value) for a, value in now.items()}
    mine = now["v"] * now["v"] * got["v", "v"] + now["f"] * now["f"] * got["f", "f"]
    mine = mine + now["t"] * now["t"] * got["t", "t"]
    cross = now["v"] * now["f"] * got["v", "f"] + now["v"] * now["t"] * got["v", "t"]
    mine = mine + 2.0 * (cross + now["f"] * now["t"] * got["f", "t"])
    both = jnp.zeros((rows, LANES), F32)
    for a in "vft":
        both = both + now[a] * got["d", a]
    for b in "VFT":
        both = both - old[b] * got["d", b]
    for a in "vft":
        for b in "VFT":
            both = both - now[a] * old[b] * got[a, b]
    squared = got["d", "d"] + mine + shifted(mine) + 2.0 * both
    segment = jnp.sqrt(jnp.maximum(squared, 0.0) * (1.0 / (3.0 * atoms)))
    path = jnp.sum(jnp.where(number <= here, segment, 0.0), axis=0, keepdims=True)
    path_ref[...] = path[:, 0:1]
    keep, pull, side, dt, along, spring = (
        jnp.sum(jnp.where(number == here, value, 0.0), axis=0, keepdims=True)
        for value in (keep, pull, side, dt, along, spring)
    )

    for c in range(3):
        speeds, places = [], []
        for i in range(SLAB_BLOCKS):
            row = 4 * c + i
            speed = keep * own_ref[0, row : row + 1, :] + pull * own_ref[0, 12 + row : 13 + row, :]
            speed = speed + side * state_ref[row : row + 1, :]
            speeds.append(speed)
            places.append(own_ref[0, 24 + row : 25 + row, :] + dt * speed)
        v_ref[c] = jnp.concatenate(speeds, axis=1)
        x_ref[c] = jnp.concatenate(places, axis=1)
    band_ref[0] = jnp.concatenate([record_ref[0:1, 0:1], record_ref[1:2, 0:1]], axis=1)
    band_ref[1] = jnp.concatenate([along[:, 0:1], spring[:, 0:1]], axis=1)


VMEM_SPEC = pl.BlockSpec(memory_space=pltpu.VMEM)
SMEM_SPEC = pl.BlockSpec(memory_space=pltpu.SMEM)
HBM_SPEC = pl.BlockSpec(memory_space=pltpu.HBM)


def call(body, outs, scalars, arrays, scratch_shapes=(), flops=0, spec=VMEM_SPEC, vmem=24):
    return pl.pallas_call(
        body,
        out_shape=outs,
        in_specs=[SMEM_SPEC] * len(scalars) + [spec] * len(arrays),
        out_specs=jax.tree.map(lambda _: VMEM_SPEC, outs),
        scratch_shapes=list(scratch_shapes),
        compiler_params=pltpu.CompilerParams(vmem_limit_bytes=vmem * 1024 * 1024),
        cost_estimate=pl.CostEstimate(flops=flops, bytes_accessed=1 << 18, transcendentals=0),
    )(*scalars, *arrays)


def swap(array, axis, partner):
    return lax.ppermute(array, axis, [(i, partner(i)) for i in range(lax.axis_size(axis))])


def exchanged(sums, axis):
    count = lax.axis_size(axis)
    if count == 4:
        return [sums] + [swap(sums, axis, lambda i, by=by: i ^ by) for by in (2, 3, 1)]
    distance = 1
    while distance < count:
        more = swap(sums, axis, lambda i, by=distance: i ^ by)
        sums = call(add_kernel, jax.ShapeDtypeStruct(sums.shape, F32), (), (sums, more))
        distance *= 2
    return [sums]


def collected(array, axis):
    count = lax.axis_size(axis)
    if count == 4:
        far = [swap(array, axis, lambda i, by=by: i ^ by) for by in (3, 2, 1)]
        return [array] + far[::-1]
    distance = 1
    while distance < count:
        more = swap(array, axis, lambda i, by=distance: i ^ by)
        shape = jax.ShapeDtypeStruct((2 * distance,) + array.shape[1:], F32)
        array = call(join_kernel, shape, (), (array, more))
        distance *= 2
    return [array]


def local(
    disp,
    veloc,
    time_step,
    reset_flags,
    climb,
    species,
    neighbours,
    counts,
    lattice,
    embed,
    radial_weight,
    mix_weight,
    update_weight,
    readout,
):
    atoms = disp.shape[2]
    images = lax.axis_size("img")
    domains = lax.axis_size("dom")
    assert disp.shape[0] == 1 and atoms == SLAB_BLOCKS * LANES and domains >= 4
    assert domains & (domains - 1) == 0 and images & (images - 1) == 0
    shape = jax.ShapeDtypeStruct
    x = jnp.transpose(disp, (1, 0, 2))
    v = jnp.transpose(veloc, (1, 0, 2))
    small = (x, v, species, neighbours, counts, embed, readout, radial_weight, mix_weight, update_weight)
    sent, pack = call(
        pack_kernel,
        (shape((PACK_ROWS, atoms), F32), shape((OWN_ROWS, atoms), F32)),
        (),
        (*small, jnp.transpose(lattice, (1, 0, 2))),
        [pltpu.VMEM(a.shape, a.dtype) for a in small] + [pltpu.SemaphoreType.DMA((16,))],
        spec=HBM_SPEC,
        vmem=63,
    )
    sibling = swap(sent, "dom", lambda i: i ^ 1)
    across = swap(sent, "dom", lambda i: (i + 2 * (i % 2) - 1) % domains)
    own_hot, *weights, x_copy = call(
        prepare_kernel,
        (
            shape((SLAB_BLOCKS, 3 * LANES, SLOTS * LANES), BF16),
            shape((CHANNELS, 48), BF16),
            shape((CHANNELS, 192), BF16),
            shape((CHANNELS, 32), BF16),
            shape((CHANNELS, 3 * LANES), BF16),
            shape((16, 192), BF16),
            shape((4, CHANNELS, LANES), F32),
            shape(x.shape, F32),
        ),
        (),
        (pack,),
        flops=100000000,
    )
    before = swap(x_copy, "img", lambda i: (i + 1) % images)
    left, right, side_hot, x_copy, *kept = call(
        first_kernel,
        (
            shape(sent.shape, F32),
            shape(sent.shape, F32),
            shape((len(SIDES), 3 * LANES, SLOTS * LANES), BF16),
            shape(x.shape, F32),
            *[shape(*one) for one in kept_shapes()],
        ),
        (),
        (x_copy, sibling, pack, across, *weights),
        forward_scratch(),
        flops=1000000000,
    )
    after = swap(x_copy, "img", lambda i: (i - 1) % images)
    force = call(
        first_back_kernel,
        shape((3, atoms), F32),
        (),
        (own_hot, side_hot, *weights, *kept),
        back_scratch(),
        flops=1000000000,
    )
    message, sums = call(
        functools.partial(blend_kernel, images),
        (shape((8, atoms), F32), shape((8, LANES), F32)),
        (),
        (force, pack, before, after),
    )
    far = swap(message, "dom", lambda i: (i + 2 * (i % 2) - 1) % domains)
    if domains == 4:
        parts = [sums, swap(sums, "dom", lambda i: i ^ 2)]
    else:
        parts = exchanged(sums, "dom")
    near = swap(message, "dom", lambda i: i ^ 1)
    numbers = call(number_kernel, shape((8, LANES), F32), (time_step, jnp.transpose(reset_flags), climb), ())
    state, record = call(
        functools.partial(second_kernel, images, domains),
        (shape((1, 40, LANES), F32), shape((3, LANES), F32)),
        (),
        (numbers, left, pack, right, message, near, far, *parts, own_hot, side_hot, *weights),
        forward_scratch() + [pltpu.VMEM(*one) for one in kept_shapes()] + back_scratch(),
        flops=1000000000,
    )
    rows = 8 * ((images + 7) // 8)
    sums, extra = call(
        functools.partial(gram_kernel, images),
        (shape((rows, LANES), F32), shape((16 + 3 * rows, LANES), F32)),
        (),
        collected(state, "img"),
        [pltpu.VMEM((images, 40, LANES), F32)],
    )
    new_x, new_v, records, path = call(
        functools.partial(final_kernel, images, atoms * domains),
        (shape(x.shape, F32), shape(x.shape, F32), shape((2, 1, 2), F32), shape((1, 1), F32)),
        (),
        (state, record, extra, *exchanged(sums, "dom")),
    )
    return (
        jnp.transpose(new_x, (1, 0, 2)),
        jnp.transpose(new_v, (1, 0, 2)),
        jnp.transpose(records, (0, 2, 1)),
        path.reshape(1),
    )


def solution(mesh):
    in_specs = (
        P(("group", "img"), None, "dom"),
        P(("group", "img"), None, "dom"),
        P(("group", "img")),
        P(None, ("group", "img")),
        P("group"),
        P(("group", "dom")),
        P(None, ("group", "dom")),
        P(("group", "dom")),
        P(None, None, ("group", "dom")),
        P(),
        P(),
        P(),
        P(),
        P(),
    )
    out_specs = (
        P(("group", "img"), None, "dom"),
        P(("group", "img"), None, "dom"),
        P(None, None, ("group", "img")),
        P(("group", "img")),
    )
    return jax.shard_map(local, mesh=mesh, in_specs=in_specs, out_specs=out_specs, check_vma=False)
```

```python
import functools
import math

import jax
import jax.numpy as jnp
from jax import lax
from jax.experimental import pallas as pl
from jax.experimental.pallas import tpu as pltpu
from jax.sharding import PartitionSpec as P

F32 = jnp.float32
BF16 = jnp.bfloat16
PRECISE = lax.Precision.HIGHEST
SPRING_CONSTANT = 0.5
ALPHA_START = 0.1
STEP_LIMIT = 0.3
TINY_VALUE = 1e-06
SOFTENING = 0.25
LANES = 128
SLOTS = 8
BASIS = 8
CHANNELS = 64
SLAB_BLOCKS = 4
ROW_X = 32
ROW_COUNT = 35
ROW_KIND = 36
ROW_V = 37
PACK_ROWS = 40
OWN_ROWS = PACK_ROWS + CHANNELS + BASIS
NT = (((1,), (1,)), ((), ()))


def split(x):
    high = x.astype(BF16).astype(F32)
    return high, x - high


def left_stack(w):
    high, low = split(w)
    return jnp.concatenate([high, high, low], axis=1)


def right_stack(x):
    high, low = split(x)
    high = high.astype(BF16)
    return jnp.concatenate([high, low.astype(BF16), high], axis=0)


def pair_stack(x):
    high, low = split(x)
    return jnp.concatenate([high.astype(BF16), low.astype(BF16)], axis=0)


def mm(a, b):
    return jnp.dot(a, b, preferred_element_type=F32)


def mm_nt(a, b):
    return lax.dot_general(a, b, NT, preferred_element_type=F32)


def pack_kernel(*refs):
    sources, (out_ref, own_ref), held, sems = refs[:11], refs[11:13], refs[13:23], refs[23]
    lattice = sources[10]
    pairs = list(zip(sources, held))
    for c in range(3):
        rows = pl.ds(8 + 8 * c, 8)
        pairs += [(lattice.at[c], out_ref.at[rows]), (lattice.at[c], own_ref.at[rows])]
    copies = [pltpu.make_async_copy(a, b, sems.at[i]) for i, (a, b) in enumerate(pairs)]
    for one in copies:
        one.start()
    for one in copies:
        one.wait()
    x, v, species, nbr, counts, embed, readout, radial, mix, update = held
    for ref in (out_ref, own_ref):
        ref[0:8, :] = nbr[...].astype(F32)
        for c in range(3):
            ref[ROW_X + c : ROW_X + c + 1, :] = x[c]
            ref[ROW_V + c : ROW_V + c + 1, :] = v[c]
        ref[ROW_COUNT : ROW_COUNT + 1, :] = counts[...].astype(F32).reshape(1, -1)
        ref[ROW_KIND : ROW_KIND + 1, :] = species[...].astype(F32).reshape(1, -1)
    top, low = PACK_ROWS, PACK_ROWS + CHANNELS
    for i, value in enumerate([mix[0], mix[1], update[0], update[1]]):
        own_ref[top:low, i * LANES : i * LANES + CHANNELS] = value
    for i, value in enumerate([radial[0], radial[1], embed[...], readout[...].reshape(1, CHANNELS)]):
        own_ref[low : low + value.shape[0], i * LANES : i * LANES + CHANNELS] = value


def prepare_kernel(po_ref, *rest):
    own_hot, l1_ref, l2_ref, l3_ref, l5_ref, l6_ref, col_ref, copy_ref = rest
    for b in range(SLAB_BLOCKS):
        mark(window_index(po_ref, b), [0, 1, 2], own_hot.at[b])
    for c in range(3):
        copy_ref[c] = po_ref[ROW_X + c : ROW_X + c + 1, :]

    def raw(first, count, i):
        return po_ref[first : first + count, i * LANES : i * LANES + CHANNELS]

    low = PACK_ROWS + CHANNELS
    mix_ref = [raw(PACK_ROWS, CHANNELS, i) for i in range(2)]
    update_ref = [raw(PACK_ROWS, CHANNELS, 2 + i) for i in range(2)]
    radial_ref = [raw(low, BASIS, i) for i in range(2)]
    embed_ref, readout = raw(low, 2, 2), raw(low, 1, 3)
    eye = (
        lax.broadcasted_iota(jnp.int32, (CHANNELS, CHANNELS), 0)
        == lax.broadcasted_iota(jnp.int32, (CHANNELS, CHANNELS), 1)
    ).astype(F32)

    def turned(x):
        return lax.dot_general(eye, x, NT, precision=PRECISE, preferred_element_type=F32)

    base0 = embed_ref[0:1, :]
    base1 = embed_ref[1:2, :] - base0
    rows = jnp.concatenate([base0, base1], axis=0)
    sent = jnp.dot(rows, mix_ref[0], precision=PRECISE, preferred_element_type=F32)
    scale = 1.0 / math.sqrt(SLOTS)
    first = jnp.concatenate([radial_ref[0] * sent[0:1], radial_ref[0] * sent[1:2]], axis=0) * scale
    second = radial_ref[1] * scale
    folded = jnp.dot(update_ref[0], mix_ref[1], precision=PRECISE, preferred_element_type=F32)
    mix_t = turned(mix_ref[1])
    l1_ref[...] = left_stack(turned(first)).astype(BF16)
    l2_ref[...] = left_stack(turned(folded)).astype(BF16)
    high, low = split(turned(second))
    l3_ref[...] = jnp.concatenate([high, high, low, jnp.zeros_like(high)], axis=1).astype(BF16)
    high, low = split(folded)
    l5_ref[...] = jnp.concatenate([high, high, high, high, low, low], axis=1).astype(BF16)
    l6_ref[...] = left_stack(first).astype(BF16)
    wide = (CHANNELS, LANES)
    col_ref[0] = jnp.broadcast_to(jnp.sum(mix_t * base0, axis=1, keepdims=True), wide)
    col_ref[1] = jnp.broadcast_to(jnp.sum(mix_t * base1, axis=1, keepdims=True), wide)
    col_ref[2] = jnp.broadcast_to(jnp.sum(update_ref[0] * readout, axis=1, keepdims=True), wide)
    col_ref[3] = jnp.broadcast_to(jnp.sum(update_ref[1] * readout, axis=1, keepdims=True), wide)


def sin_cos(t):
    q = t * t
    s = -1.0 / 39916800.0
    for c in (1.0 / 362880.0, -1.0 / 5040.0, 1.0 / 120.0, -1.0 / 6.0, 1.0):
        s = s * q + c
    k = 1.0 / 479001600.0
    for c in (-1.0 / 3628800.0, 1.0 / 40320.0, -1.0 / 720.0, 1.0 / 24.0, -0.5, 1.0):
        k = k * q + c
    return s * t, k


def wide_row(x, row):
    return jnp.broadcast_to(x[row : row + 1, :], (8, x.shape[1]))


def silu_parts(m):
    sig = 1.0 / (1.0 + jnp.exp(-m))
    return m * sig, sig * (1.0 + m * (1.0 - sig))


def pick(values, lanes):
    return jnp.take_along_axis(values, lanes, axis=1, mode="promise_in_bounds")


def reach(b, first, last):
    return [w for w in range(3) if first <= b - 1 + w <= last]


SIDE_START = {2: 0, 3: LANES, 8: 3 * LANES, 9: 5 * LANES}
SIDE_ROWS = 6 * LANES


def mark(index, ws, target):
    count = len(ws) * LANES
    row_id = (lax.broadcasted_iota(jnp.int32, (count, LANES), 0) + ws[0] * LANES).astype(jnp.int16)
    one, zero = jnp.ones((count, LANES), BF16), jnp.zeros((count, LANES), BF16)
    for k in range(SLOTS):
        wanted = jnp.broadcast_to(index[k : k + 1, :], (16, LANES)).astype(jnp.int16)
        wanted = jnp.concatenate([wanted] * (count // 16), axis=0)
        target[:, k * LANES : (k + 1) * LANES] = jnp.where(row_id == wanted, one, zero)


def window_index(pack, b):
    lanes = slice((b % 4) * LANES, (b % 4 + 1) * LANES)
    return pack[0:8, lanes].astype(jnp.int32) - LANES * (b % 4)


def mark_sides(packs, side):
    for b, start in SIDE_START.items():
        ws = reach(b, 3, 8)
        mark(window_index(packs[b // 4], b), ws, side.at[start : start + len(ws) * LANES])


def forward_parts(packs, weights, xs, sst, kept):
    l1, l2, l3, l5, l6, col = weights
    (widx, kinds, geo, bst, bps, bpr, sent_all, sent_pair, slope) = kept
    centre = 2.0 + 0.5 * lax.broadcasted_iota(jnp.int32, (BASIS, LANES), 0).astype(F32)
    slot = lax.broadcasted_iota(jnp.int32, (SLOTS, LANES), 0)

    def part_rows(value):
        high, low = split(value)
        return jnp.concatenate([high, low], axis=0).astype(BF16)

    def pairs(b):
        pack = packs[b // 4]
        lanes = slice((b % 4) * LANES, (b % 4 + 1) * LANES)
        index = window_index(pack, b)
        widx[b] = index
        inner = index & (LANES - 1)
        part = index >> 7

        def taken(row):
            got = [
                pick(jnp.broadcast_to(xs[b - 1 + w, row : row + 1, :], (SLOTS, LANES)), inner)
                for w in range(3)
            ]
            return jnp.where(part == 0, got[0], jnp.where(part == 1, got[1], got[2]))

        vec = [
            pack[8 + 8 * c : 16 + 8 * c, lanes] + taken(c) - jnp.broadcast_to(xs[b, c : c + 1, :], (SLOTS, LANES))
            for c in range(3)
        ]
        kind = taken(3)
        dist = jnp.sqrt(vec[0] * vec[0] + vec[1] * vec[1] + vec[2] * vec[2] + SOFTENING)
        live = (slot.astype(F32) < jnp.broadcast_to(pack[ROW_COUNT : ROW_COUNT + 1, lanes], (SLOTS, LANES))).astype(F32)
        turns = dist * (1.0 / 12.0)
        turns = turns - jnp.floor(turns + 0.5)
        sine, cosine = sin_cos(turns * math.pi)
        envelope = cosine * cosine * live
        slant = cosine * sine * live * (-math.pi / 6.0)
        if 3 <= b <= 8:
            kinds[b] = kind
            for c in range(3):
                geo[b, c] = vec[c]
            geo[b, 3] = 1.0 / dist
        total = jnp.zeros((BASIS, LANES), F32)
        total_kind = jnp.zeros((BASIS, LANES), F32)
        for k in range(SLOTS):
            away = wide_row(dist, k) - centre
            gauss = jnp.exp(-4.0 * (away * away))
            env_k = wide_row(envelope, k)
            value = gauss * env_k
            total = total + value
            total_kind = total_kind + value * wide_row(kind, k)
            cols = slice(k * LANES, (k + 1) * LANES)
            if 2 <= b <= 9:
                bst[b, :, cols] = part_rows(value)
            if 3 <= b <= 8:
                value = gauss * (wide_row(slant, k) - 8.0 * away * env_k)
                bpr[b, :, cols] = value
                bps[b, :, cols] = part_rows(value)
        high, low = split(jnp.concatenate([total, total_kind], axis=0))
        sst[:, b * LANES : (b + 1) * LANES] = jnp.concatenate([high, low, high], axis=0).astype(BF16)

    for b in range(1, 11):
        pairs(b)

    for b in range(1, 11, 2):
        cols = slice(b * LANES, (b + 2) * LANES)
        value, steep = silu_parts(mm(l1[...], sst[:, cols]))
        sent = mm(l2[...], right_stack(value))
        for i in range(2):
            one = sent[:, i * LANES : (i + 1) * LANES]
            one = one + col[0] + col[1] * jnp.broadcast_to(xs[b + i, 3:4, :], (CHANNELS, LANES))
            sent_all[:, (b + i) * LANES : (b + i + 1) * LANES] = one
            if 3 <= b + i <= 8:
                sent_pair[:, (b + i) * LANES : (b + i + 1) * LANES] = pair_stack(one)
        slope[:, cols] = steep


def force_parts(weights, own_hot, side_hot, kept, dg, pulls, met, acc, held):
    l1, l2, l3, l5, l6, col = weights
    (widx, kinds, geo, bst, bps, bpr, sent_all, sent_pair, slope) = kept
    slot = lax.broadcasted_iota(jnp.int32, (SLOTS, LANES), 0)

    def marks(b, ws):
        if b in SIDE_START:
            start = SIDE_START[b] + (ws[0] - reach(b, 3, 8)[0]) * LANES
            return side_hot.at[start : start + len(ws) * LANES]
        return own_hot.at[b - 4, ws[0] * LANES : (ws[-1] + 1) * LANES]

    def add_rows(sums, first, b, ws, out):
        for i, w in enumerate(ws):
            target = b - 1 + w
            piece = out[i * LANES : (i + 1) * LANES]
            rows = slice((target - first) * LANES, (target - first + 1) * LANES)
            if (first, target) in started:
                sums[rows, :] += piece
            else:
                sums[rows, :] = piece
                started.add((first, target))

    started = set()

    def block_work(b):
        index = widx[b]
        inner, part = index & (LANES - 1), index >> 7
        basis = bst[b]
        radial = mm(l3[...], jnp.concatenate([basis, basis], axis=0))
        if 3 <= b <= 8:
            basis = bps[b]
            steepness = mm(l3[...], jnp.concatenate([basis, basis], axis=0))
        lanes = [jnp.broadcast_to(inner[k : k + 1, :], (16, LANES)) for k in range(SLOTS)]
        parts = [jnp.broadcast_to(part[k : k + 1, :], (16, LANES)) for k in range(SLOTS)]
        own = 4 <= b <= 7
        if own:
            found_all = mm(sent_pair[:, (b - 1) * LANES : (b + 2) * LANES], own_hot[b - 4])
        value = held.at[b % 2]
        total = [jnp.zeros((8, LANES), F32)] * SLOTS
        for u in range(CHANNELS // 16):
            rows = slice(16 * u, 16 * u + 16)
            low_rows = slice(CHANNELS + 16 * u, CHANNELS + 16 * u + 16)
            windows = [sent_all[rows, (b - 1 + w) * LANES : (b + w) * LANES] for w in range(3)]
            got = []
            message = jnp.zeros((16, LANES), F32)
            for k in range(SLOTS):
                cols = slice(k * LANES, (k + 1) * LANES)
                if own:
                    got.append(found_all[rows, cols] + found_all[low_rows, cols])
                else:
                    found = [pick(window, lanes[k]) for window in windows]
                    got.append(jnp.where(parts[k] == 0, found[0], jnp.where(parts[k] == 1, found[1], found[2])))
                message = message + radial[rows, cols] * got[k]
            _, steep = silu_parts(message)
            back = col[3, rows] * steep
            for k in range(SLOTS):
                cols = slice(k * LANES, (k + 1) * LANES)
                high, low = split(radial[rows, cols] * back)
                value[rows, cols] = high.astype(BF16)
                value[low_rows, cols] = low.astype(BF16)
                if 3 <= b <= 8:
                    pull = got[k] * back * steepness[rows, cols]
                    total[k] = total[k] + pull[0:8] + pull[8:16]
            yield
        if 3 <= b <= 8:
            for k in range(SLOTS):
                pulls[b, :, k * LANES : (k + 1) * LANES] = total[k]

    def scatter_work(b):
        ws = reach(b, 3, 8)
        chosen, value = marks(b, ws), held.at[b % 2]
        out = None
        for u in range(4):
            cols = slice(u * 2 * LANES, (u + 1) * 2 * LANES)
            one = mm_nt(chosen[:, cols], value[:, cols])
            out = one if out is None else out + one
            yield
        add_rows(dg, 3, b, ws, out)

    def together(*works):
        works = list(works)
        while works:
            works = [work for work in works if next(work, "end") != "end"]

    together(block_work(2))
    for b in range(3, 10):
        together(scatter_work(b - 1), block_work(b))
    together(scatter_work(9))

    def finish(b, sums):
        kind = kinds[b]
        rows = []
        for k in range(SLOTS):
            cols = slice(k * LANES, (k + 1) * LANES)
            weight = sums[0:8] + wide_row(kind, k) * sums[8:16]
            rows.append(jnp.sum(bpr[b, :, cols] * weight + pulls[b, :, cols], axis=0, keepdims=True))
        pull = jnp.concatenate(rows, axis=0) * geo[b, 3]
        pieces = []
        for c in range(3):
            value = pull * geo[b, c]
            if 4 <= b <= 7:
                acc[b - 4, c] = jnp.sum(value, axis=0, keepdims=True)
            pieces.append(split(value))
        lines = []
        for h in range(2):
            for c in range(3):
                lines.append(jnp.concatenate([jnp.where(slot == k, pieces[c][h], 0.0) for k in range(SLOTS)], axis=1))
        ws = reach(b, 4, 7)
        out = mm_nt(jnp.concatenate(lines, axis=0).astype(BF16), marks(b, ws)[...])
        for c in range(3):
            both = out[8 * c : 8 * c + 8] + out[24 + 8 * c : 32 + 8 * c]
            for i, w in enumerate(ws):
                target = b - 5 + w
                piece = both[:, i * LANES : (i + 1) * LANES]
                if (c, target) in met_blocks:
                    met[target, c] += piece
                else:
                    met[target, c] = piece
                    met_blocks.add((c, target))

    met_blocks = set()

    for b in range(3, 9, 2):
        cols = slice(b * LANES, (b + 2) * LANES)
        high, low = split(dg[(b - 3) * LANES : (b - 1) * LANES, :])
        steep = mm_nt(l5[...], jnp.concatenate([high, low, high], axis=1).astype(BF16))
        steep = steep + jnp.concatenate([col[2], col[2]], axis=1)
        sums = mm(l6[...], right_stack(steep * slope[:, cols]))
        for i in range(2):
            finish(b + i, sums[:, i * LANES : (i + 1) * LANES])

    away = []
    for c in range(3):
        back = [acc[i, c] - jnp.sum(met[i, c], axis=0, keepdims=True) for i in range(SLAB_BLOCKS)]
        away.append(jnp.concatenate(back, axis=1))
    return jnp.concatenate(away, axis=0)


def fill_region(xs, packs, rows_of):
    for b in range(12):
        lanes = slice((b % 4) * LANES, (b % 4 + 1) * LANES)
        pack = packs[b // 4]
        xs[b, 0:3, :] = rows_of(b // 4)[:, lanes]
        xs[b, 3:4, :] = pack[ROW_KIND : ROW_KIND + 1, lanes]


def lane_total(x):
    x = x[:, 0:LANES] + x[:, LANES : 2 * LANES] + x[:, 2 * LANES : 3 * LANES] + x[:, 3 * LANES : 4 * LANES]
    return jnp.sum(x, axis=1, keepdims=True)


def dot3(a, b):
    return jnp.sum(a * b, axis=0, keepdims=True)


def kept_shapes():
    wide = 12 * LANES
    return [
        ((12, 8, LANES), jnp.int32),
        ((12, 8, LANES), F32),
        ((12, 4, 8, LANES), F32),
        ((12, 16, SLOTS * LANES), BF16),
        ((12, 16, SLOTS * LANES), BF16),
        ((12, 8, SLOTS * LANES), F32),
        ((CHANNELS, wide), F32),
        ((2 * CHANNELS, wide), BF16),
        ((CHANNELS, wide), F32),
    ]


def forward_scratch():
    return [pltpu.VMEM((12, 8, LANES), F32), pltpu.VMEM((48, 12 * LANES), BF16)]


def back_scratch():
    return [
        pltpu.VMEM((6 * LANES, 2 * CHANNELS), F32),
        pltpu.VMEM((12, 8, SLOTS * LANES), F32),
        pltpu.VMEM((SLAB_BLOCKS, 3, SLOTS, LANES), F32),
        pltpu.VMEM((SLAB_BLOCKS, 3, 1, LANES), F32),
        pltpu.VMEM((2, 2 * CHANNELS, SLOTS * LANES), BF16),
    ]


def by_parity(sibling, across):
    even = jnp.full(sibling.shape, lax.axis_index("dom") % 2, jnp.int32) == 0
    return jnp.where(even, across, sibling), jnp.where(even, sibling, across)


def first_kernel(x_ref, sibling_ref, po_ref, across_ref, *rest):
    weights, (pl_ref, pr_ref, side_hot, copy_ref), kept, (xs, sst) = rest[:6], rest[6:10], rest[10:19], rest[19:]
    copy_ref[...] = x_ref[...]
    pl_ref[...], pr_ref[...] = by_parity(sibling_ref[...], across_ref[...])
    packs = [pl_ref, po_ref, pr_ref]
    mark_sides(packs, side_hot)
    fill_region(xs, packs, lambda s: packs[s][ROW_X : ROW_X + 3, :])
    forward_parts(packs, weights, xs, sst, kept)


def first_back_kernel(own_hot, side_hot, *rest):
    weights, kept, out_ref, scr = rest[:6], rest[6:15], rest[15], rest[16:]
    out_ref[...] = force_parts(weights, own_hot, side_hot, kept, *scr)


def rows_of(ref):
    return jnp.concatenate([ref[c] for c in range(3)], axis=0)


def block_row(*values):
    values = list(values) + [jnp.zeros((1, LANES), F32)] * (SLAB_BLOCKS - len(values))
    return jnp.concatenate(values, axis=1)


def blend_kernel(images, force_ref, po_ref, before_ref, after_ref, out_ref, sums_ref):
    x = po_ref[ROW_X : ROW_X + 3, :]
    v = po_ref[ROW_V : ROW_V + 3, :]
    force = force_ref[...]
    here = lax.axis_index("img")
    before = jnp.where(here > 0, rows_of(before_ref), 0.0)
    after = jnp.where(here < images - 1, rows_of(after_ref), 0.0)
    tangent = after - before
    plus = after - x
    minus = x - before
    sums = jnp.concatenate(
        [
            dot3(force, tangent),
            dot3(force, force),
            dot3(tangent, tangent),
            dot3(plus, plus),
            dot3(minus, minus),
            dot3(v, v),
            jnp.zeros((2, x.shape[1]), F32),
        ],
        axis=0,
    )
    sums = jnp.broadcast_to(lane_total(sums), (8, LANES))
    sums_ref[...] = sums
    out_ref[0:3, :] = force
    out_ref[3:6, :] = tangent
    out_ref[6:7, :] = block_row(*[sums[i : i + 1] for i in range(4)])
    out_ref[7:8, :] = block_row(sums[4:5], sums[5:6])


def step_numbers(ft, ff, tt, pp, mn, vv, dt, alpha, flagged, climbing, inside):
    root = jnp.sqrt(tt + TINY_VALUE)
    along = ft / root
    spring = SPRING_CONSTANT * (jnp.sqrt(pp) - jnp.sqrt(mn))
    factor = jnp.where(climbing, -2.0 * along, spring - along)
    band = jnp.maximum(ff + 2.0 * factor * along + factor * factor * (tt / (tt + TINY_VALUE)), 0.0)
    new_dt = jnp.where(flagged, 0.5 * dt, jnp.minimum(1.1 * dt, STEP_LIMIT))
    pull = jnp.where(flagged, 0.0, alpha * jnp.sqrt(vv / (band + TINY_VALUE))) + new_dt
    keep = jnp.where(flagged, 0.0, 1.0 - alpha)
    new_alpha = jnp.where(flagged, ALPHA_START, 0.99 * alpha)
    keep = jnp.where(inside, keep, 0.0)
    pull = jnp.where(inside, pull, 0.0)
    return (
        jnp.where(inside, along, 0.0),
        jnp.where(inside, spring, 0.0),
        keep,
        pull,
        pull * factor / root,
        new_dt,
        new_alpha,
    )


def add_kernel(a_ref, b_ref, out_ref):
    out_ref[...] = a_ref[...] + b_ref[...]


def number_kernel(dt_ref, flag_ref, climb_ref, out_ref):
    flags = [flag_ref[0, s].astype(F32) for s in range(flag_ref.shape[1])]
    for i, value in enumerate([dt_ref[0], climb_ref[0].astype(F32)] + flags):
        out_ref[i : i + 1, :] = jnp.full((1, LANES), value, F32)


def second_kernel(images, domains, number_ref, pl_ref, po_ref, pr_ref, own_ref, near_ref, far_ref, *rest):
    count = 2 if domains == 4 else 1
    parts, rest = rest[:count], rest[count:]
    (own_hot, side_hot), weights, (out_ref, record_ref), scr = rest[:2], rest[2:8], rest[8:10], rest[10:]
    packs = [pl_ref, po_ref, pr_ref]
    here = lax.axis_index("img")
    sums = parts[0][...]
    if domains == 4:
        sums = sums + parts[1][...]
    got = [sums[i : i + 1, :] for i in range(6)]
    if domains == 4:
        for one in (near_ref, far_ref):
            for i in range(6):
                got[i] = got[i] + one[6 + i // 4 : 7 + i // 4, (i % 4) * LANES : (i % 4 + 1) * LANES]
    ft, ff, tt, pp, mn, vv = got
    beside = by_parity(near_ref[0:6, :], far_ref[0:6, :])
    shape = (1, LANES)
    along, spring, keep, pull, side, dt, alpha = step_numbers(
        ft,
        ff,
        tt,
        pp,
        mn,
        vv,
        number_ref[0:1, :],
        jnp.full(shape, ALPHA_START, F32),
        number_ref[2:3, :] == 1.0,
        number_ref[1:2, :] == jnp.full(shape, here, jnp.int32).astype(F32),
        jnp.full(shape, jnp.where((here >= 1) & (here <= images - 2), 1, 0), jnp.int32) == 1,
    )
    messages = [beside[0], own_ref[0:6, :], beside[1]]

    def wide(s):
        return jnp.concatenate([s] * SLAB_BLOCKS, axis=1)

    speeds = [
        wide(keep) * p[ROW_V : ROW_V + 3, :] + wide(pull) * m[0:3, :] + wide(side) * m[3:6, :]
        for p, m in zip(packs, messages)
    ]
    moved = [p[ROW_X : ROW_X + 3, :] + wide(dt) * s for p, s in zip(packs, speeds)]
    xs, sst, kept = scr[0], scr[1], scr[2:11]
    fill_region(xs, packs, lambda s: moved[s])
    forward_parts(packs, weights, xs, sst, kept)
    force = force_parts(weights, own_hot, side_hot, kept, *scr[11:])
    for c in range(3):
        for i in range(SLAB_BLOCKS):
            lanes = slice(i * LANES, (i + 1) * LANES)
            row = 4 * c + i
            out_ref[0, row : row + 1, :] = speeds[1][c : c + 1, lanes]
            out_ref[0, 12 + row : 13 + row, :] = force[c : c + 1, lanes]
            out_ref[0, 24 + row : 25 + row, :] = moved[1][c : c + 1, lanes]
    out_ref[0, 36:37, :] = dt
    out_ref[0, 37:38, :] = alpha
    out_ref[0, 38:40, :] = jnp.broadcast_to(number_ref[3:4, :], (2, LANES))
    record_ref[0:1, :] = along
    record_ref[1:2, :] = spring
    record_ref[2:3, :] = number_ref[1:2, :]


PRODUCTS = (
    [("f", "t"), ("f", "f"), ("t", "t"), ("p", "p"), ("d", "d"), ("v", "v")]
    + [("d", "v"), ("d", "f"), ("d", "t"), ("d", "V"), ("d", "F"), ("d", "T"), ("v", "f"), ("v", "t")]
    + [(a, b) for a in "vft" for b in "VFT"]
)


def gram_kernel(images, *refs):
    parts, (out_ref, state_ref, messages_ref) = refs[:-3], refs[-3:]
    rows = out_ref.shape[0]
    place = 0
    for part in parts:
        messages_ref[place : place + part.shape[0]] = part[...]
        place += part.shape[0]
    here = lax.axis_index("img")
    blank = [jnp.zeros((rows - images, LANES), F32)] if rows > images else []
    zero = jnp.zeros((1, LANES), F32)

    def gathered(row):
        return jnp.concatenate([messages_ref[lax.rem(here + images - i, images), row : row + 1, :] for i in range(images)] + blank, axis=0)

    def earlier(value):
        return jnp.concatenate([zero, value[0 : rows - 1]], axis=0)

    def later(value):
        return jnp.concatenate([value[1:images], zero] + blank, axis=0)

    number = lax.broadcasted_iota(jnp.int32, (rows, LANES), 0)
    held = number < images
    totals = [jnp.zeros((rows, LANES), F32) for _ in PRODUCTS]
    for row in range(3 * SLAB_BLOCKS):
        v, f, x = gathered(row), gathered(12 + row), gathered(24 + row)
        before = jnp.where(held, earlier(x), 0.0)
        after = later(x)
        t = after - before
        table = {"f": f, "v": v, "t": t, "p": after - x, "d": x - before}
        table["F"], table["V"], table["T"] = earlier(f), earlier(v), earlier(t)
        totals = [old + table[a] * table[b] for old, (a, b) in zip(totals, PRODUCTS)]
        state_ref[row : row + 1, :] = jnp.sum(jnp.where(number == here, t, 0.0), axis=0, keepdims=True)
    lane = lax.broadcasted_iota(jnp.int32, (rows, LANES), 1)
    result = jnp.zeros((rows, LANES), F32)
    for q, one in enumerate(totals):
        one = jnp.broadcast_to(jnp.sum(one, axis=1, keepdims=True), (rows, LANES))
        result = jnp.where(lane == q, one, result)
    out_ref[...] = result
    for i in range(3):
        state_ref[16 + rows * i : 16 + rows * (i + 1), :] = gathered(36 + i)


def final_kernel(images, atoms, own_ref, record_ref, state_ref, *rest):
    parts, (x_ref, v_ref, band_ref, path_ref) = rest[:-4], rest[-4:]
    rows = parts[0].shape[0]
    here = lax.axis_index("img")
    sums = parts[0][...]
    for one in parts[1:]:
        sums = sums + one[...]
    got = {
        pair: jnp.broadcast_to(sums[:, q : q + 1], (rows, LANES)) for q, pair in enumerate(PRODUCTS)
    }
    number = lax.broadcasted_iota(jnp.int32, (rows, LANES), 0)
    inside = (number >= 1) & (number <= images - 2)
    climb = jnp.broadcast_to(record_ref[2:3, :], (rows, LANES))
    dt0, alpha0, flag = (state_ref[16 + rows * i : 16 + rows * (i + 1), :] for i in range(3))
    along, spring, keep, pull, side, dt, _ = step_numbers(
        got["f", "t"],
        got["f", "f"],
        got["t", "t"],
        got["p", "p"],
        got["d", "d"],
        got["v", "v"],
        dt0,
        alpha0,
        flag == 1.0,
        number.astype(F32) == climb,
        inside,
    )

    def shifted(value):
        return jnp.concatenate([jnp.zeros((1, LANES), F32), value[0 : rows - 1]], axis=0)

    now = {"v": dt * keep, "f": dt * pull, "t": dt * side}
    old = {a.upper(): shifted(value) for a, value in now.items()}
    mine = now["v"] * now["v"] * got["v", "v"] + now["f"] * now["f"] * got["f", "f"]
    mine = mine + now["t"] * now["t"] * got["t", "t"]
    cross = now["v"] * now["f"] * got["v", "f"] + now["v"] * now["t"] * got["v", "t"]
    mine = mine + 2.0 * (cross + now["f"] * now["t"] * got["f", "t"])
    both = jnp.zeros((rows, LANES), F32)
    for a in "vft":
        both = both + now[a] * got["d", a]
    for b in "VFT":
        both = both - old[b] * got["d", b]
    for a in "vft":
        for b in "VFT":
            both = both - now[a] * old[b] * got[a, b]
    squared = got["d", "d"] + mine + shifted(mine) + 2.0 * both
    segment = jnp.sqrt(jnp.maximum(squared, 0.0) * (1.0 / (3.0 * atoms)))
    path = jnp.sum(jnp.where(number <= here, segment, 0.0), axis=0, keepdims=True)
    path_ref[...] = path[:, 0:1]
    keep, pull, side, dt, along, spring = (
        jnp.sum(jnp.where(number == here, value, 0.0), axis=0, keepdims=True)
        for value in (keep, pull, side, dt, along, spring)
    )

    for c in range(3):
        speeds, places = [], []
        for i in range(SLAB_BLOCKS):
            row = 4 * c + i
            speed = keep * own_ref[0, row : row + 1, :] + pull * own_ref[0, 12 + row : 13 + row, :]
            speed = speed + side * state_ref[row : row + 1, :]
            speeds.append(speed)
            places.append(own_ref[0, 24 + row : 25 + row, :] + dt * speed)
        v_ref[c] = jnp.concatenate(speeds, axis=1)
        x_ref[c] = jnp.concatenate(places, axis=1)
    band_ref[0] = jnp.concatenate([record_ref[0:1, 0:1], record_ref[1:2, 0:1]], axis=1)
    band_ref[1] = jnp.concatenate([along[:, 0:1], spring[:, 0:1]], axis=1)


VMEM_SPEC = pl.BlockSpec(memory_space=pltpu.VMEM)
SMEM_SPEC = pl.BlockSpec(memory_space=pltpu.SMEM)
HBM_SPEC = pl.BlockSpec(memory_space=pltpu.HBM)


def call(body, outs, scalars, arrays, scratch_shapes=(), flops=0, spec=VMEM_SPEC, vmem=24):
    return pl.pallas_call(
        body,
        out_shape=outs,
        in_specs=[SMEM_SPEC] * len(scalars) + [spec] * len(arrays),
        out_specs=jax.tree.map(lambda _: VMEM_SPEC, outs),
        scratch_shapes=list(scratch_shapes),
        compiler_params=pltpu.CompilerParams(vmem_limit_bytes=vmem * 1024 * 1024),
        cost_estimate=pl.CostEstimate(flops=flops, bytes_accessed=1 << 18, transcendentals=0),
    )(*scalars, *arrays)


def swap(array, axis, partner):
    return lax.ppermute(array, axis, [(i, partner(i)) for i in range(lax.axis_size(axis))])


def exchanged(sums, axis):
    count = lax.axis_size(axis)
    if count == 4:
        return [sums] + [swap(sums, axis, lambda i, by=by: i ^ by) for by in (2, 3, 1)]
    distance = 1
    while distance < count:
        more = swap(sums, axis, lambda i, by=distance: i ^ by)
        sums = call(add_kernel, jax.ShapeDtypeStruct(sums.shape, F32), (), (sums, more))
        distance *= 2
    return [sums]


def collected(array, axis):
    count = lax.axis_size(axis)
    return [array] + [swap(array, axis, lambda i, by=by: (i + by) % count) for by in range(1, count)]


def local(
    disp,
    veloc,
    time_step,
    reset_flags,
    climb,
    species,
    neighbours,
    counts,
    lattice,
    embed,
    radial_weight,
    mix_weight,
    update_weight,
    readout,
):
    atoms = disp.shape[2]
    images = lax.axis_size("img")
    domains = lax.axis_size("dom")
    assert disp.shape[0] == 1 and atoms == SLAB_BLOCKS * LANES and domains >= 4
    assert domains & (domains - 1) == 0 and images & (images - 1) == 0
    shape = jax.ShapeDtypeStruct
    x = jnp.transpose(disp, (1, 0, 2))
    v = jnp.transpose(veloc, (1, 0, 2))
    small = (x, v, species, neighbours, counts, embed, readout, radial_weight, mix_weight, update_weight)
    sent, pack = call(
        pack_kernel,
        (shape((PACK_ROWS, atoms), F32), shape((OWN_ROWS, atoms), F32)),
        (),
        (*small, jnp.transpose(lattice, (1, 0, 2))),
        [pltpu.VMEM(a.shape, a.dtype) for a in small] + [pltpu.SemaphoreType.DMA((16,))],
        spec=HBM_SPEC,
        vmem=63,
    )
    sibling = swap(sent, "dom", lambda i: i ^ 1)
    across = swap(sent, "dom", lambda i: (i + 2 * (i % 2) - 1) % domains)
    own_hot, *weights, x_copy = call(
        prepare_kernel,
        (
            shape((SLAB_BLOCKS, 3 * LANES, SLOTS * LANES), BF16),
            shape((CHANNELS, 48), BF16),
            shape((CHANNELS, 192), BF16),
            shape((CHANNELS, 32), BF16),
            shape((CHANNELS, 3 * LANES), BF16),
            shape((16, 192), BF16),
            shape((4, CHANNELS, LANES), F32),
            shape(x.shape, F32),
        ),
        (),
        (pack,),
        flops=100000000,
    )
    before = swap(x_copy, "img", lambda i: (i + 1) % images)
    left, right, side_hot, x_copy, *kept = call(
        first_kernel,
        (
            shape(sent.shape, F32),
            shape(sent.shape, F32),
            shape((SIDE_ROWS, SLOTS * LANES), BF16),
            shape(x.shape, F32),
            *[shape(*one) for one in kept_shapes()],
        ),
        (),
        (x_copy, sibling, pack, across, *weights),
        forward_scratch(),
        flops=1000000000,
    )
    after = swap(x_copy, "img", lambda i: (i - 1) % images)
    force = call(
        first_back_kernel,
        shape((3, atoms), F32),
        (),
        (own_hot, side_hot, *weights, *kept),
        back_scratch(),
        flops=1000000000,
    )
    message, sums = call(
        functools.partial(blend_kernel, images),
        (shape((8, atoms), F32), shape((8, LANES), F32)),
        (),
        (force, pack, before, after),
    )
    far = swap(message, "dom", lambda i: (i + 2 * (i % 2) - 1) % domains)
    if domains == 4:
        parts = [sums, swap(sums, "dom", lambda i: i ^ 2)]
    else:
        parts = exchanged(sums, "dom")
    near = swap(message, "dom", lambda i: i ^ 1)
    numbers = call(number_kernel, shape((8, LANES), F32), (time_step, jnp.transpose(reset_flags), climb), ())
    state, record = call(
        functools.partial(second_kernel, images, domains),
        (shape((1, 40, LANES), F32), shape((3, LANES), F32)),
        (),
        (numbers, left, pack, right, message, near, far, *parts, own_hot, side_hot, *weights),
        forward_scratch() + [pltpu.VMEM(*one) for one in kept_shapes()] + back_scratch(),
        flops=1000000000,
    )
    rows = 8 * ((images + 7) // 8)
    sums, extra = call(
        functools.partial(gram_kernel, images),
        (shape((rows, LANES), F32), shape((16 + 3 * rows, LANES), F32)),
        (),
        collected(state, "img"),
        [pltpu.VMEM((images, 40, LANES), F32)],
    )
    new_x, new_v, records, path = call(
        functools.partial(final_kernel, images, atoms * domains),
        (shape(x.shape, F32), shape(x.shape, F32), shape((2, 1, 2), F32), shape((1, 1), F32)),
        (),
        (state, record, extra, *exchanged(sums, "dom")),
    )
    return (
        jnp.transpose(new_x, (1, 0, 2)),
        jnp.transpose(new_v, (1, 0, 2)),
        jnp.transpose(records, (0, 2, 1)),
        path.reshape(1),
    )


def solution(mesh):
    in_specs = (
        P(("group", "img"), None, "dom"),
        P(("group", "img"), None, "dom"),
        P(("group", "img")),
        P(None, ("group", "img")),
        P("group"),
        P(("group", "dom")),
        P(None, ("group", "dom")),
        P(("group", "dom")),
        P(None, None, ("group", "dom")),
        P(),
        P(),
        P(),
        P(),
        P(),
    )
    out_specs = (
        P(("group", "img"), None, "dom"),
        P(("group", "img"), None, "dom"),
        P(None, None, ("group", "img")),
        P(("group", "img")),
    )
    return jax.shard_map(local, mesh=mesh, in_specs=in_specs, out_specs=out_specs, check_vma=False)
```

```python
import functools
import math

import jax
import jax.numpy as jnp
from jax import lax
from jax.experimental import pallas as pl
from jax.experimental.pallas import tpu as pltpu
from jax.sharding import PartitionSpec as P

F32 = jnp.float32
BF16 = jnp.bfloat16
PRECISE = lax.Precision.HIGHEST
SPRING_CONSTANT = 0.5
ALPHA_START = 0.1
STEP_LIMIT = 0.3
TINY_VALUE = 1e-06
SOFTENING = 0.25
LANES = 128
SLOTS = 8
BASIS = 8
CHANNELS = 64
SLAB_BLOCKS = 4
ROW_X = 32
ROW_COUNT = 35
ROW_KIND = 36
ROW_V = 37
PACK_ROWS = 40
OWN_ROWS = PACK_ROWS + CHANNELS + BASIS
NT = (((1,), (1,)), ((), ()))


def split(x):
    high = x.astype(BF16).astype(F32)
    return high, x - high


def left_stack(w):
    high, low = split(w)
    return jnp.concatenate([high, high, low], axis=1)


def right_stack(x):
    high, low = split(x)
    high = high.astype(BF16)
    return jnp.concatenate([high, low.astype(BF16), high], axis=0)


def pair_stack(x):
    high, low = split(x)
    return jnp.concatenate([high.astype(BF16), low.astype(BF16)], axis=0)


def mm(a, b):
    return jnp.dot(a, b, preferred_element_type=F32)


def mm_nt(a, b):
    return lax.dot_general(a, b, NT, preferred_element_type=F32)


def pack_kernel(*refs):
    sources, (out_ref, own_ref), held, sems = refs[:11], refs[11:13], refs[13:23], refs[23]
    lattice = sources[10]
    pairs = list(zip(sources, held))
    for c in range(3):
        rows = pl.ds(8 + 8 * c, 8)
        pairs += [(lattice.at[c], out_ref.at[rows]), (lattice.at[c], own_ref.at[rows])]
    copies = [pltpu.make_async_copy(a, b, sems.at[i]) for i, (a, b) in enumerate(pairs)]
    for one in copies:
        one.start()
    for one in copies:
        one.wait()
    x, v, species, nbr, counts, embed, readout, radial, mix, update = held
    for ref in (out_ref, own_ref):
        ref[0:8, :] = nbr[...].astype(F32)
        for c in range(3):
            ref[ROW_X + c : ROW_X + c + 1, :] = x[c]
            ref[ROW_V + c : ROW_V + c + 1, :] = v[c]
        ref[ROW_COUNT : ROW_COUNT + 1, :] = counts[...].astype(F32).reshape(1, -1)
        ref[ROW_KIND : ROW_KIND + 1, :] = species[...].astype(F32).reshape(1, -1)
    top, low = PACK_ROWS, PACK_ROWS + CHANNELS
    for i, value in enumerate([mix[0], mix[1], update[0], update[1]]):
        own_ref[top:low, i * LANES : i * LANES + CHANNELS] = value
    for i, value in enumerate([radial[0], radial[1], embed[...], readout[...].reshape(1, CHANNELS)]):
        own_ref[low : low + value.shape[0], i * LANES : i * LANES + CHANNELS] = value


def prepare_kernel(po_ref, *rest):
    own_hot, l1_ref, l2_ref, l3_ref, l5_ref, l6_ref, col_ref, copy_ref = rest
    for b in range(SLAB_BLOCKS):
        mark(window_index(po_ref, b), [0, 1, 2], own_hot.at[b])
    for c in range(3):
        copy_ref[c] = po_ref[ROW_X + c : ROW_X + c + 1, :]

    def raw(first, count, i):
        return po_ref[first : first + count, i * LANES : i * LANES + CHANNELS]

    low = PACK_ROWS + CHANNELS
    mix_ref = [raw(PACK_ROWS, CHANNELS, i) for i in range(2)]
    update_ref = [raw(PACK_ROWS, CHANNELS, 2 + i) for i in range(2)]
    radial_ref = [raw(low, BASIS, i) for i in range(2)]
    embed_ref, readout = raw(low, 2, 2), raw(low, 1, 3)
    eye = (
        lax.broadcasted_iota(jnp.int32, (CHANNELS, CHANNELS), 0)
        == lax.broadcasted_iota(jnp.int32, (CHANNELS, CHANNELS), 1)
    ).astype(F32)

    def turned(x):
        return lax.dot_general(eye, x, NT, precision=PRECISE, preferred_element_type=F32)

    base0 = embed_ref[0:1, :]
    base1 = embed_ref[1:2, :] - base0
    rows = jnp.concatenate([base0, base1], axis=0)
    sent = jnp.dot(rows, mix_ref[0], precision=PRECISE, preferred_element_type=F32)
    scale = 1.0 / math.sqrt(SLOTS)
    first = jnp.concatenate([radial_ref[0] * sent[0:1], radial_ref[0] * sent[1:2]], axis=0) * scale
    second = radial_ref[1] * scale
    folded = jnp.dot(update_ref[0], mix_ref[1], precision=PRECISE, preferred_element_type=F32)
    mix_t = turned(mix_ref[1])
    l1_ref[...] = left_stack(turned(first)).astype(BF16)
    l2_ref[...] = left_stack(turned(folded)).astype(BF16)
    high, low = split(turned(second))
    l3_ref[...] = jnp.concatenate([high, high, low, jnp.zeros_like(high)], axis=1).astype(BF16)
    high, low = split(folded)
    l5_ref[...] = jnp.concatenate([high, high, high, high, low, low], axis=1).astype(BF16)
    l6_ref[...] = left_stack(first).astype(BF16)
    wide = (CHANNELS, LANES)
    col_ref[0] = jnp.broadcast_to(jnp.sum(mix_t * base0, axis=1, keepdims=True), wide)
    col_ref[1] = jnp.broadcast_to(jnp.sum(mix_t * base1, axis=1, keepdims=True), wide)
    col_ref[2] = jnp.broadcast_to(jnp.sum(update_ref[0] * readout, axis=1, keepdims=True), wide)
    col_ref[3] = jnp.broadcast_to(jnp.sum(update_ref[1] * readout, axis=1, keepdims=True), wide)


def sin_cos(t):
    q = t * t
    s = -1.0 / 39916800.0
    for c in (1.0 / 362880.0, -1.0 / 5040.0, 1.0 / 120.0, -1.0 / 6.0, 1.0):
        s = s * q + c
    k = 1.0 / 479001600.0
    for c in (-1.0 / 3628800.0, 1.0 / 40320.0, -1.0 / 720.0, 1.0 / 24.0, -0.5, 1.0):
        k = k * q + c
    return s * t, k


def wide_row(x, row):
    return jnp.broadcast_to(x[row : row + 1, :], (8, x.shape[1]))


def silu_parts(m):
    sig = 1.0 / (1.0 + jnp.exp(-m))
    return m * sig, sig * (1.0 + m * (1.0 - sig))


def pick(values, lanes):
    return jnp.take_along_axis(values, lanes, axis=1, mode="promise_in_bounds")


def reach(b, first, last):
    return [w for w in range(3) if first <= b - 1 + w <= last]


SIDE_START = {2: 0, 3: LANES, 8: 3 * LANES, 9: 5 * LANES}
SIDE_ROWS = 6 * LANES


def mark(index, ws, target):
    count = len(ws) * LANES
    row_id = (lax.broadcasted_iota(jnp.int32, (count, LANES), 0) + ws[0] * LANES).astype(jnp.int16)
    one, zero = jnp.ones((count, LANES), BF16), jnp.zeros((count, LANES), BF16)
    for k in range(SLOTS):
        wanted = jnp.broadcast_to(index[k : k + 1, :], (16, LANES)).astype(jnp.int16)
        wanted = jnp.concatenate([wanted] * (count // 16), axis=0)
        target[:, k * LANES : (k + 1) * LANES] = jnp.where(row_id == wanted, one, zero)


def window_index(pack, b):
    lanes = slice((b % 4) * LANES, (b % 4 + 1) * LANES)
    return pack[0:8, lanes].astype(jnp.int32) - LANES * (b % 4)


def mark_sides(packs, side):
    for b, start in SIDE_START.items():
        ws = reach(b, 3, 8)
        mark(window_index(packs[b // 4], b), ws, side.at[start : start + len(ws) * LANES])


def forward_parts(packs, weights, xs, sst, kept):
    l1, l2, l3, l5, l6, col = weights
    (widx, kinds, geo, bst, bps, bpr, sent_all, sent_pair, slope) = kept
    centre = 2.0 + 0.5 * lax.broadcasted_iota(jnp.int32, (BASIS, LANES), 0).astype(F32)
    slot = lax.broadcasted_iota(jnp.int32, (SLOTS, LANES), 0)

    def part_rows(value):
        high, low = split(value)
        return jnp.concatenate([high, low], axis=0).astype(BF16)

    def pairs(b):
        pack = packs[b // 4]
        lanes = slice((b % 4) * LANES, (b % 4 + 1) * LANES)
        index = window_index(pack, b)
        widx[b] = index
        inner = index & (LANES - 1)
        part = index >> 7

        def taken(row):
            got = [
                pick(jnp.broadcast_to(xs[b - 1 + w, row : row + 1, :], (SLOTS, LANES)), inner)
                for w in range(3)
            ]
            return jnp.where(part == 0, got[0], jnp.where(part == 1, got[1], got[2]))

        vec = [
            pack[8 + 8 * c : 16 + 8 * c, lanes] + taken(c) - jnp.broadcast_to(xs[b, c : c + 1, :], (SLOTS, LANES))
            for c in range(3)
        ]
        kind = taken(3)
        dist = jnp.sqrt(vec[0] * vec[0] + vec[1] * vec[1] + vec[2] * vec[2] + SOFTENING)
        live = (slot.astype(F32) < jnp.broadcast_to(pack[ROW_COUNT : ROW_COUNT + 1, lanes], (SLOTS, LANES))).astype(F32)
        turns = dist * (1.0 / 12.0)
        turns = turns - jnp.floor(turns + 0.5)
        sine, cosine = sin_cos(turns * math.pi)
        envelope = cosine * cosine * live
        slant = cosine * sine * live * (-math.pi / 6.0)
        if 3 <= b <= 8:
            kinds[b] = kind
            for c in range(3):
                geo[b, c] = vec[c]
            geo[b, 3] = 1.0 / dist
        total = jnp.zeros((BASIS, LANES), F32)
        total_kind = jnp.zeros((BASIS, LANES), F32)
        for k in range(SLOTS):
            away = wide_row(dist, k) - centre
            gauss = jnp.exp(-4.0 * (away * away))
            env_k = wide_row(envelope, k)
            value = gauss * env_k
            total = total + value
            total_kind = total_kind + value * wide_row(kind, k)
            cols = slice(k * LANES, (k + 1) * LANES)
            if 2 <= b <= 9:
                bst[b, :, cols] = part_rows(value)
            if 3 <= b <= 8:
                value = gauss * (wide_row(slant, k) - 8.0 * away * env_k)
                bpr[b, :, cols] = value
                bps[b, :, cols] = part_rows(value)
        high, low = split(jnp.concatenate([total, total_kind], axis=0))
        sst[:, b * LANES : (b + 1) * LANES] = jnp.concatenate([high, low, high], axis=0).astype(BF16)

    for b in range(1, 11):
        pairs(b)

    for b in range(1, 11, 2):
        cols = slice(b * LANES, (b + 2) * LANES)
        value, steep = silu_parts(mm(l1[...], sst[:, cols]))
        sent = mm(l2[...], right_stack(value))
        for i in range(2):
            one = sent[:, i * LANES : (i + 1) * LANES]
            one = one + col[0] + col[1] * jnp.broadcast_to(xs[b + i, 3:4, :], (CHANNELS, LANES))
            sent_all[:, (b + i) * LANES : (b + i + 1) * LANES] = one
            if 3 <= b + i <= 8:
                sent_pair[:, (b + i) * LANES : (b + i + 1) * LANES] = pair_stack(one)
        slope[:, cols] = steep


def force_parts(weights, own_hot, side_hot, kept, dg, pulls, met, acc, held):
    l1, l2, l3, l5, l6, col = weights
    (widx, kinds, geo, bst, bps, bpr, sent_all, sent_pair, slope) = kept
    slot = lax.broadcasted_iota(jnp.int32, (SLOTS, LANES), 0)

    def marks(b, ws):
        if b in SIDE_START:
            start = SIDE_START[b] + (ws[0] - reach(b, 3, 8)[0]) * LANES
            return side_hot.at[start : start + len(ws) * LANES]
        return own_hot.at[b - 4, ws[0] * LANES : (ws[-1] + 1) * LANES]

    def add_rows(sums, first, b, ws, out):
        for i, w in enumerate(ws):
            target = b - 1 + w
            piece = out[i * LANES : (i + 1) * LANES]
            rows = slice((target - first) * LANES, (target - first + 1) * LANES)
            if (first, target) in started:
                sums[rows, :] += piece
            else:
                sums[rows, :] = piece
                started.add((first, target))

    started = set()

    def block_work(b):
        index = widx[b]
        inner, part = index & (LANES - 1), index >> 7
        basis = bst[b]
        radial = mm(l3[...], jnp.concatenate([basis, basis], axis=0))
        if 3 <= b <= 8:
            basis = bps[b]
            steepness = mm(l3[...], jnp.concatenate([basis, basis], axis=0))
        lanes = [jnp.broadcast_to(inner[k : k + 1, :], (16, LANES)) for k in range(SLOTS)]
        parts = [jnp.broadcast_to(part[k : k + 1, :], (16, LANES)) for k in range(SLOTS)]
        own = 4 <= b <= 7
        if own:
            found_all = mm(sent_pair[:, (b - 1) * LANES : (b + 2) * LANES], own_hot[b - 4])
        value = held.at[b % 2]
        total = [jnp.zeros((8, LANES), F32)] * SLOTS
        for u in range(CHANNELS // 16):
            rows = slice(16 * u, 16 * u + 16)
            low_rows = slice(CHANNELS + 16 * u, CHANNELS + 16 * u + 16)
            windows = [sent_all[rows, (b - 1 + w) * LANES : (b + w) * LANES] for w in range(3)]
            got = []
            message = jnp.zeros((16, LANES), F32)
            for k in range(SLOTS):
                cols = slice(k * LANES, (k + 1) * LANES)
                if own:
                    got.append(found_all[rows, cols] + found_all[low_rows, cols])
                else:
                    found = [pick(window, lanes[k]) for window in windows]
                    got.append(jnp.where(parts[k] == 0, found[0], jnp.where(parts[k] == 1, found[1], found[2])))
                message = message + radial[rows, cols] * got[k]
            _, steep = silu_parts(message)
            back = col[3, rows] * steep
            for k in range(SLOTS):
                cols = slice(k * LANES, (k + 1) * LANES)
                high, low = split(radial[rows, cols] * back)
                value[rows, cols] = high.astype(BF16)
                value[low_rows, cols] = low.astype(BF16)
                if 3 <= b <= 8:
                    pull = got[k] * back * steepness[rows, cols]
                    total[k] = total[k] + pull[0:8] + pull[8:16]
            yield
        if 3 <= b <= 8:
            for k in range(SLOTS):
                pulls[b, :, k * LANES : (k + 1) * LANES] = total[k]

    def scatter_work(b):
        ws = reach(b, 3, 8)
        chosen, value = marks(b, ws), held.at[b % 2]
        out = None
        for u in range(4):
            cols = slice(u * 2 * LANES, (u + 1) * 2 * LANES)
            one = mm_nt(chosen[:, cols], value[:, cols])
            out = one if out is None else out + one
            yield
        add_rows(dg, 3, b, ws, out)

    def together(*works):
        works = list(works)
        while works:
            works = [work for work in works if next(work, "end") != "end"]

    together(block_work(2))
    for b in range(3, 10):
        together(scatter_work(b - 1), block_work(b))
    together(scatter_work(9))

    def finish(b, sums):
        kind = kinds[b]
        rows = []
        for k in range(SLOTS):
            cols = slice(k * LANES, (k + 1) * LANES)
            weight = sums[0:8] + wide_row(kind, k) * sums[8:16]
            rows.append(jnp.sum(bpr[b, :, cols] * weight + pulls[b, :, cols], axis=0, keepdims=True))
        pull = jnp.concatenate(rows, axis=0) * geo[b, 3]
        pieces = []
        for c in range(3):
            value = pull * geo[b, c]
            if 4 <= b <= 7:
                acc[b - 4, c] = jnp.sum(value, axis=0, keepdims=True)
            pieces.append(split(value))
        lines = []
        for h in range(2):
            for c in range(3):
                lines.append(jnp.concatenate([jnp.where(slot == k, pieces[c][h], 0.0) for k in range(SLOTS)], axis=1))
        ws = reach(b, 4, 7)
        out = mm_nt(jnp.concatenate(lines, axis=0).astype(BF16), marks(b, ws)[...])
        for c in range(3):
            both = out[8 * c : 8 * c + 8] + out[24 + 8 * c : 32 + 8 * c]
            for i, w in enumerate(ws):
                target = b - 5 + w
                piece = both[:, i * LANES : (i + 1) * LANES]
                if (c, target) in met_blocks:
                    met[target, c] += piece
                else:
                    met[target, c] = piece
                    met_blocks.add((c, target))

    met_blocks = set()

    for b in range(3, 9, 2):
        cols = slice(b * LANES, (b + 2) * LANES)
        high, low = split(dg[(b - 3) * LANES : (b - 1) * LANES, :])
        steep = mm_nt(l5[...], jnp.concatenate([high, low, high], axis=1).astype(BF16))
        steep = steep + jnp.concatenate([col[2], col[2]], axis=1)
        sums = mm(l6[...], right_stack(steep * slope[:, cols]))
        for i in range(2):
            finish(b + i, sums[:, i * LANES : (i + 1) * LANES])

    away = []
    for c in range(3):
        back = [acc[i, c] - jnp.sum(met[i, c], axis=0, keepdims=True) for i in range(SLAB_BLOCKS)]
        away.append(jnp.concatenate(back, axis=1))
    return jnp.concatenate(away, axis=0)


def fill_region(xs, packs, rows_of):
    for b in range(12):
        lanes = slice((b % 4) * LANES, (b % 4 + 1) * LANES)
        pack = packs[b // 4]
        xs[b, 0:3, :] = rows_of(b // 4)[:, lanes]
        xs[b, 3:4, :] = pack[ROW_KIND : ROW_KIND + 1, lanes]


def lane_total(x):
    x = x[:, 0:LANES] + x[:, LANES : 2 * LANES] + x[:, 2 * LANES : 3 * LANES] + x[:, 3 * LANES : 4 * LANES]
    return jnp.sum(x, axis=1, keepdims=True)


def dot3(a, b):
    return jnp.sum(a * b, axis=0, keepdims=True)


def kept_shapes():
    wide = 12 * LANES
    return [
        ((12, 8, LANES), jnp.int32),
        ((12, 8, LANES), F32),
        ((12, 4, 8, LANES), F32),
        ((12, 16, SLOTS * LANES), BF16),
        ((12, 16, SLOTS * LANES), BF16),
        ((12, 8, SLOTS * LANES), F32),
        ((CHANNELS, wide), F32),
        ((2 * CHANNELS, wide), BF16),
        ((CHANNELS, wide), F32),
    ]


def forward_scratch():
    return [pltpu.VMEM((12, 8, LANES), F32), pltpu.VMEM((48, 12 * LANES), BF16)]


def back_scratch():
    return [
        pltpu.VMEM((6 * LANES, 2 * CHANNELS), F32),
        pltpu.VMEM((12, 8, SLOTS * LANES), F32),
        pltpu.VMEM((SLAB_BLOCKS, 3, SLOTS, LANES), F32),
        pltpu.VMEM((SLAB_BLOCKS, 3, 1, LANES), F32),
        pltpu.VMEM((2, 2 * CHANNELS, SLOTS * LANES), BF16),
    ]


def by_parity(sibling, across):
    even = jnp.full(sibling.shape, lax.axis_index("dom") % 2, jnp.int32) == 0
    return jnp.where(even, across, sibling), jnp.where(even, sibling, across)


def first_kernel(sibling_ref, po_ref, across_ref, own_hot, *rest):
    weights, (out_ref, pl_ref, pr_ref, side_hot), scr = rest[:6], rest[6:10], rest[10:]
    xs, sst, kept = scr[0], scr[1], scr[2:11]
    pl_ref[...], pr_ref[...] = by_parity(sibling_ref[...], across_ref[...])
    packs = [pl_ref, po_ref, pr_ref]
    mark_sides(packs, side_hot)
    fill_region(xs, packs, lambda s: packs[s][ROW_X : ROW_X + 3, :])
    forward_parts(packs, weights, xs, sst, kept)
    out_ref[...] = force_parts(weights, own_hot, side_hot, kept, *scr[11:])


def rows_of(ref):
    return jnp.concatenate([ref[c] for c in range(3)], axis=0)


def block_row(*values):
    values = list(values) + [jnp.zeros((1, LANES), F32)] * (SLAB_BLOCKS - len(values))
    return jnp.concatenate(values, axis=1)


def blend_kernel(images, force_ref, po_ref, before_ref, after_ref, out_ref, sums_ref):
    x = po_ref[ROW_X : ROW_X + 3, :]
    v = po_ref[ROW_V : ROW_V + 3, :]
    force = force_ref[...]
    here = lax.axis_index("img")
    before = jnp.where(here > 0, rows_of(before_ref), 0.0)
    after = jnp.where(here < images - 1, rows_of(after_ref), 0.0)
    tangent = after - before
    plus = after - x
    minus = x - before
    sums = jnp.concatenate(
        [
            dot3(force, tangent),
            dot3(force, force),
            dot3(tangent, tangent),
            dot3(plus, plus),
            dot3(minus, minus),
            dot3(v, v),
            jnp.zeros((2, x.shape[1]), F32),
        ],
        axis=0,
    )
    sums = jnp.broadcast_to(lane_total(sums), (8, LANES))
    sums_ref[...] = sums
    out_ref[0:3, :] = force
    out_ref[3:6, :] = tangent
    out_ref[6:7, :] = block_row(*[sums[i : i + 1] for i in range(4)])
    out_ref[7:8, :] = block_row(sums[4:5], sums[5:6])


def step_numbers(ft, ff, tt, pp, mn, vv, dt, alpha, flagged, climbing, inside):
    root = jnp.sqrt(tt + TINY_VALUE)
    along = ft / root
    spring = SPRING_CONSTANT * (jnp.sqrt(pp) - jnp.sqrt(mn))
    factor = jnp.where(climbing, -2.0 * along, spring - along)
    band = jnp.maximum(ff + 2.0 * factor * along + factor * factor * (tt / (tt + TINY_VALUE)), 0.0)
    new_dt = jnp.where(flagged, 0.5 * dt, jnp.minimum(1.1 * dt, STEP_LIMIT))
    pull = jnp.where(flagged, 0.0, alpha * jnp.sqrt(vv / (band + TINY_VALUE))) + new_dt
    keep = jnp.where(flagged, 0.0, 1.0 - alpha)
    new_alpha = jnp.where(flagged, ALPHA_START, 0.99 * alpha)
    keep = jnp.where(inside, keep, 0.0)
    pull = jnp.where(inside, pull, 0.0)
    return (
        jnp.where(inside, along, 0.0),
        jnp.where(inside, spring, 0.0),
        keep,
        pull,
        pull * factor / root,
        new_dt,
        new_alpha,
    )


def add_kernel(a_ref, b_ref, out_ref):
    out_ref[...] = a_ref[...] + b_ref[...]


def number_kernel(dt_ref, flag_ref, climb_ref, out_ref):
    flags = [flag_ref[0, s].astype(F32) for s in range(flag_ref.shape[1])]
    for i, value in enumerate([dt_ref[0], climb_ref[0].astype(F32)] + flags):
        out_ref[i : i + 1, :] = jnp.full((1, LANES), value, F32)


def second_kernel(images, domains, number_ref, pl_ref, po_ref, pr_ref, own_ref, near_ref, far_ref, *rest):
    count = 2 if domains == 4 else 1
    parts, rest = rest[:count], rest[count:]
    (own_hot, side_hot), weights, (out_ref, record_ref), scr = rest[:2], rest[2:8], rest[8:10], rest[10:]
    packs = [pl_ref, po_ref, pr_ref]
    here = lax.axis_index("img")
    sums = parts[0][...]
    if domains == 4:
        sums = sums + parts[1][...]
    got = [sums[i : i + 1, :] for i in range(6)]
    if domains == 4:
        for one in (near_ref, far_ref):
            for i in range(6):
                got[i] = got[i] + one[6 + i // 4 : 7 + i // 4, (i % 4) * LANES : (i % 4 + 1) * LANES]
    ft, ff, tt, pp, mn, vv = got
    beside = by_parity(near_ref[0:6, :], far_ref[0:6, :])
    shape = (1, LANES)
    along, spring, keep, pull, side, dt, alpha = step_numbers(
        ft,
        ff,
        tt,
        pp,
        mn,
        vv,
        number_ref[0:1, :],
        jnp.full(shape, ALPHA_START, F32),
        number_ref[2:3, :] == 1.0,
        number_ref[1:2, :] == jnp.full(shape, here, jnp.int32).astype(F32),
        jnp.full(shape, jnp.where((here >= 1) & (here <= images - 2), 1, 0), jnp.int32) == 1,
    )
    messages = [beside[0], own_ref[0:6, :], beside[1]]

    def wide(s):
        return jnp.concatenate([s] * SLAB_BLOCKS, axis=1)

    speeds = [
        wide(keep) * p[ROW_V : ROW_V + 3, :] + wide(pull) * m[0:3, :] + wide(side) * m[3:6, :]
        for p, m in zip(packs, messages)
    ]
    moved = [p[ROW_X : ROW_X + 3, :] + wide(dt) * s for p, s in zip(packs, speeds)]
    xs, sst, kept = scr[0], scr[1], scr[2:11]
    fill_region(xs, packs, lambda s: moved[s])
    forward_parts(packs, weights, xs, sst, kept)
    force = force_parts(weights, own_hot, side_hot, kept, *scr[11:])
    for c in range(3):
        for i in range(SLAB_BLOCKS):
            lanes = slice(i * LANES, (i + 1) * LANES)
            row = 4 * c + i
            out_ref[0, row : row + 1, :] = speeds[1][c : c + 1, lanes]
            out_ref[0, 12 + row : 13 + row, :] = force[c : c + 1, lanes]
            out_ref[0, 24 + row : 25 + row, :] = moved[1][c : c + 1, lanes]
    out_ref[0, 36:37, :] = dt
    out_ref[0, 37:38, :] = alpha
    out_ref[0, 38:40, :] = jnp.broadcast_to(number_ref[3:4, :], (2, LANES))
    record_ref[0:1, :] = along
    record_ref[1:2, :] = spring
    record_ref[2:3, :] = number_ref[1:2, :]


PRODUCTS = (
    [("f", "t"), ("f", "f"), ("t", "t"), ("p", "p"), ("d", "d"), ("v", "v")]
    + [("d", "v"), ("d", "f"), ("d", "t"), ("d", "V"), ("d", "F"), ("d", "T"), ("v", "f"), ("v", "t")]
    + [(a, b) for a in "vft" for b in "VFT"]
)


def gram_kernel(images, *refs):
    parts, (out_ref, state_ref, messages_ref) = refs[:-3], refs[-3:]
    rows = out_ref.shape[0]
    place = 0
    for part in parts:
        messages_ref[place : place + part.shape[0]] = part[...]
        place += part.shape[0]
    here = lax.axis_index("img")
    blank = [jnp.zeros((rows - images, LANES), F32)] if rows > images else []
    zero = jnp.zeros((1, LANES), F32)

    def gathered(row):
        return jnp.concatenate([messages_ref[lax.rem(here + images - i, images), row : row + 1, :] for i in range(images)] + blank, axis=0)

    def earlier(value):
        return jnp.concatenate([zero, value[0 : rows - 1]], axis=0)

    def later(value):
        return jnp.concatenate([value[1:images], zero] + blank, axis=0)

    number = lax.broadcasted_iota(jnp.int32, (rows, LANES), 0)
    held = number < images
    totals = [jnp.zeros((rows, LANES), F32) for _ in PRODUCTS]
    for row in range(3 * SLAB_BLOCKS):
        v, f, x = gathered(row), gathered(12 + row), gathered(24 + row)
        before = jnp.where(held, earlier(x), 0.0)
        after = later(x)
        t = after - before
        table = {"f": f, "v": v, "t": t, "p": after - x, "d": x - before}
        table["F"], table["V"], table["T"] = earlier(f), earlier(v), earlier(t)
        totals = [old + table[a] * table[b] for old, (a, b) in zip(totals, PRODUCTS)]
        state_ref[row : row + 1, :] = jnp.sum(jnp.where(number == here, t, 0.0), axis=0, keepdims=True)
    lane = lax.broadcasted_iota(jnp.int32, (rows, LANES), 1)
    result = jnp.zeros((rows, LANES), F32)
    for q, one in enumerate(totals):
        one = jnp.broadcast_to(jnp.sum(one, axis=1, keepdims=True), (rows, LANES))
        result = jnp.where(lane == q, one, result)
    out_ref[...] = result
    for i in range(3):
        state_ref[16 + rows * i : 16 + rows * (i + 1), :] = gathered(36 + i)


def final_kernel(images, atoms, own_ref, record_ref, state_ref, *rest):
    parts, (x_ref, v_ref, band_ref, path_ref) = rest[:-4], rest[-4:]
    rows = parts[0].shape[0]
    here = lax.axis_index("img")
    sums = parts[0][...]
    for one in parts[1:]:
        sums = sums + one[...]
    got = {
        pair: jnp.broadcast_to(sums[:, q : q + 1], (rows, LANES)) for q, pair in enumerate(PRODUCTS)
    }
    number = lax.broadcasted_iota(jnp.int32, (rows, LANES), 0)
    inside = (number >= 1) & (number <= images - 2)
    climb = jnp.broadcast_to(record_ref[2:3, :], (rows, LANES))
    dt0, alpha0, flag = (state_ref[16 + rows * i : 16 + rows * (i + 1), :] for i in range(3))
    along, spring, keep, pull, side, dt, _ = step_numbers(
        got["f", "t"],
        got["f", "f"],
        got["t", "t"],
        got["p", "p"],
        got["d", "d"],
        got["v", "v"],
        dt0,
        alpha0,
        flag == 1.0,
        number.astype(F32) == climb,
        inside,
    )

    def shifted(value):
        return jnp.concatenate([jnp.zeros((1, LANES), F32), value[0 : rows - 1]], axis=0)

    now = {"v": dt * keep, "f": dt * pull, "t": dt * side}
    old = {a.upper(): shifted(value) for a, value in now.items()}
    mine = now["v"] * now["v"] * got["v", "v"] + now["f"] * now["f"] * got["f", "f"]
    mine = mine + now["t"] * now["t"] * got["t", "t"]
    cross = now["v"] * now["f"] * got["v", "f"] + now["v"] * now["t"] * got["v", "t"]
    mine = mine + 2.0 * (cross + now["f"] * now["t"] * got["f", "t"])
    both = jnp.zeros((rows, LANES), F32)
    for a in "vft":
        both = both + now[a] * got["d", a]
    for b in "VFT":
        both = both - old[b] * got["d", b]
    for a in "vft":
        for b in "VFT":
            both = both - now[a] * old[b] * got[a, b]
    squared = got["d", "d"] + mine + shifted(mine) + 2.0 * both
    segment = jnp.sqrt(jnp.maximum(squared, 0.0) * (1.0 / (3.0 * atoms)))
    path = jnp.sum(jnp.where(number <= here, segment, 0.0), axis=0, keepdims=True)
    path_ref[...] = path[:, 0:1]
    keep, pull, side, dt, along, spring = (
        jnp.sum(jnp.where(number == here, value, 0.0), axis=0, keepdims=True)
        for value in (keep, pull, side, dt, along, spring)
    )

    for c in range(3):
        speeds, places = [], []
        for i in range(SLAB_BLOCKS):
            row = 4 * c + i
            speed = keep * own_ref[0, row : row + 1, :] + pull * own_ref[0, 12 + row : 13 + row, :]
            speed = speed + side * state_ref[row : row + 1, :]
            speeds.append(speed)
            places.append(own_ref[0, 24 + row : 25 + row, :] + dt * speed)
        v_ref[c] = jnp.concatenate(speeds, axis=1)
        x_ref[c] = jnp.concatenate(places, axis=1)
    band_ref[0] = jnp.concatenate([record_ref[0:1, 0:1], record_ref[1:2, 0:1]], axis=1)
    band_ref[1] = jnp.concatenate([along[:, 0:1], spring[:, 0:1]], axis=1)


VMEM_SPEC = pl.BlockSpec(memory_space=pltpu.VMEM)
SMEM_SPEC = pl.BlockSpec(memory_space=pltpu.SMEM)
HBM_SPEC = pl.BlockSpec(memory_space=pltpu.HBM)


def call(body, outs, scalars, arrays, scratch_shapes=(), flops=0, spec=VMEM_SPEC, vmem=24):
    return pl.pallas_call(
        body,
        out_shape=outs,
        in_specs=[SMEM_SPEC] * len(scalars) + [spec] * len(arrays),
        out_specs=jax.tree.map(lambda _: VMEM_SPEC, outs),
        scratch_shapes=list(scratch_shapes),
        compiler_params=pltpu.CompilerParams(vmem_limit_bytes=vmem * 1024 * 1024),
        cost_estimate=pl.CostEstimate(flops=flops, bytes_accessed=1 << 18, transcendentals=0),
    )(*scalars, *arrays)


def swap(array, axis, partner):
    return lax.ppermute(array, axis, [(i, partner(i)) for i in range(lax.axis_size(axis))])


def exchanged(sums, axis):
    count = lax.axis_size(axis)
    if count == 4:
        return [sums] + [swap(sums, axis, lambda i, by=by: i ^ by) for by in (2, 3, 1)]
    distance = 1
    while distance < count:
        more = swap(sums, axis, lambda i, by=distance: i ^ by)
        sums = call(add_kernel, jax.ShapeDtypeStruct(sums.shape, F32), (), (sums, more))
        distance *= 2
    return [sums]


def collected(array, axis):
    count = lax.axis_size(axis)
    return [array] + [swap(array, axis, lambda i, by=by: (i + by) % count) for by in range(1, count)]


def local(
    disp,
    veloc,
    time_step,
    reset_flags,
    climb,
    species,
    neighbours,
    counts,
    lattice,
    embed,
    radial_weight,
    mix_weight,
    update_weight,
    readout,
):
    atoms = disp.shape[2]
    images = lax.axis_size("img")
    domains = lax.axis_size("dom")
    assert disp.shape[0] == 1 and atoms == SLAB_BLOCKS * LANES and domains >= 4
    assert domains & (domains - 1) == 0 and images & (images - 1) == 0
    shape = jax.ShapeDtypeStruct
    x = jnp.transpose(disp, (1, 0, 2))
    v = jnp.transpose(veloc, (1, 0, 2))
    small = (x, v, species, neighbours, counts, embed, readout, radial_weight, mix_weight, update_weight)
    sent, pack = call(
        pack_kernel,
        (shape((PACK_ROWS, atoms), F32), shape((OWN_ROWS, atoms), F32)),
        (),
        (*small, jnp.transpose(lattice, (1, 0, 2))),
        [pltpu.VMEM(a.shape, a.dtype) for a in small] + [pltpu.SemaphoreType.DMA((16,))],
        spec=HBM_SPEC,
        vmem=63,
    )
    sibling = swap(sent, "dom", lambda i: i ^ 1)
    across = swap(sent, "dom", lambda i: (i + 2 * (i % 2) - 1) % domains)
    own_hot, *weights, x_copy = call(
        prepare_kernel,
        (
            shape((SLAB_BLOCKS, 3 * LANES, SLOTS * LANES), BF16),
            shape((CHANNELS, 48), BF16),
            shape((CHANNELS, 192), BF16),
            shape((CHANNELS, 32), BF16),
            shape((CHANNELS, 3 * LANES), BF16),
            shape((16, 192), BF16),
            shape((4, CHANNELS, LANES), F32),
            shape(x.shape, F32),
        ),
        (),
        (pack,),
        flops=100000000,
    )
    before = swap(x_copy, "img", lambda i: (i + 1) % images)
    after = swap(x_copy, "img", lambda i: (i - 1) % images)
    force_scratch = forward_scratch() + [pltpu.VMEM(*one) for one in kept_shapes()] + back_scratch()
    force, left, right, side_hot = call(
        first_kernel,
        (
            shape((3, atoms), F32),
            shape(sent.shape, F32),
            shape(sent.shape, F32),
            shape((SIDE_ROWS, SLOTS * LANES), BF16),
        ),
        (),
        (sibling, pack, across, own_hot, *weights),
        force_scratch,
        flops=1000000000,
    )
    message, sums = call(
        functools.partial(blend_kernel, images),
        (shape((8, atoms), F32), shape((8, LANES), F32)),
        (),
        (force, pack, before, after),
    )
    far = swap(message, "dom", lambda i: (i + 2 * (i % 2) - 1) % domains)
    if domains == 4:
        parts = [sums, swap(sums, "dom", lambda i: i ^ 2)]
    else:
        parts = exchanged(sums, "dom")
    near = swap(message, "dom", lambda i: i ^ 1)
    numbers = call(number_kernel, shape((8, LANES), F32), (time_step, jnp.transpose(reset_flags), climb), ())
    state, record = call(
        functools.partial(second_kernel, images, domains),
        (shape((1, 40, LANES), F32), shape((3, LANES), F32)),
        (),
        (numbers, left, pack, right, message, near, far, *parts, own_hot, side_hot, *weights),
        force_scratch,
        flops=1000000000,
    )
    rows = 8 * ((images + 7) // 8)
    sums, extra = call(
        functools.partial(gram_kernel, images),
        (shape((rows, LANES), F32), shape((16 + 3 * rows, LANES), F32)),
        (),
        collected(state, "img"),
        [pltpu.VMEM((images, 40, LANES), F32)],
    )
    new_x, new_v, records, path = call(
        functools.partial(final_kernel, images, atoms * domains),
        (shape(x.shape, F32), shape(x.shape, F32), shape((2, 1, 2), F32), shape((1, 1), F32)),
        (),
        (state, record, extra, *exchanged(sums, "dom")),
    )
    return (
        jnp.transpose(new_x, (1, 0, 2)),
        jnp.transpose(new_v, (1, 0, 2)),
        jnp.transpose(records, (0, 2, 1)),
        path.reshape(1),
    )


def solution(mesh):
    in_specs = (
        P(("group", "img"), None, "dom"),
        P(("group", "img"), None, "dom"),
        P(("group", "img")),
        P(None, ("group", "img")),
        P("group"),
        P(("group", "dom")),
        P(None, ("group", "dom")),
        P(("group", "dom")),
        P(None, None, ("group", "dom")),
        P(),
        P(),
        P(),
        P(),
        P(),
    )
    out_specs = (
        P(("group", "img"), None, "dom"),
        P(("group", "img"), None, "dom"),
        P(None, None, ("group", "img")),
        P(("group", "img")),
    )
    return jax.shard_map(local, mesh=mesh, in_specs=in_specs, out_specs=out_specs, check_vma=False)
```

```python
import functools
import math

import jax
import jax.numpy as jnp
from jax import lax
from jax.experimental import pallas as pl
from jax.experimental.pallas import tpu as pltpu
from jax.sharding import PartitionSpec as P

F32 = jnp.float32
BF16 = jnp.bfloat16
PRECISE = lax.Precision.HIGHEST
SPRING_CONSTANT = 0.5
ALPHA_START = 0.1
STEP_LIMIT = 0.3
TINY_VALUE = 1e-06
SOFTENING = 0.25
LANES = 128
SLOTS = 8
BASIS = 8
CHANNELS = 64
SLAB_BLOCKS = 4
ROW_X = 32
ROW_COUNT = 35
ROW_KIND = 36
ROW_V = 37
PACK_ROWS = 40
OWN_ROWS = PACK_ROWS + CHANNELS + BASIS
NT = (((1,), (1,)), ((), ()))


def split(x):
    high = x.astype(BF16).astype(F32)
    return high, x - high


def left_stack(w):
    high, low = split(w)
    return jnp.concatenate([high, high, low], axis=1)


def right_stack(x):
    high, low = split(x)
    high = high.astype(BF16)
    return jnp.concatenate([high, low.astype(BF16), high], axis=0)


def pair_stack(x):
    high, low = split(x)
    return jnp.concatenate([high.astype(BF16), low.astype(BF16)], axis=0)


def mm(a, b):
    return jnp.dot(a, b, preferred_element_type=F32)


def mm_nt(a, b):
    return lax.dot_general(a, b, NT, preferred_element_type=F32)


def pack_kernel(*refs):
    sources, (out_ref, own_ref), held, sems = refs[:11], refs[11:13], refs[13:23], refs[23]
    lattice = sources[10]
    pairs = list(zip(sources, held))
    for c in range(3):
        rows = pl.ds(8 + 8 * c, 8)
        pairs += [(lattice.at[c], out_ref.at[rows]), (lattice.at[c], own_ref.at[rows])]
    copies = [pltpu.make_async_copy(a, b, sems.at[i]) for i, (a, b) in enumerate(pairs)]
    for one in copies:
        one.start()
    for one in copies:
        one.wait()
    x, v, species, nbr, counts, embed, readout, radial, mix, update = held
    for ref in (out_ref, own_ref):
        ref[0:8, :] = nbr[...].astype(F32)
        for c in range(3):
            ref[ROW_X + c : ROW_X + c + 1, :] = x[c]
            ref[ROW_V + c : ROW_V + c + 1, :] = v[c]
        ref[ROW_COUNT : ROW_COUNT + 1, :] = counts[...].astype(F32).reshape(1, -1)
        ref[ROW_KIND : ROW_KIND + 1, :] = species[...].astype(F32).reshape(1, -1)
    top, low = PACK_ROWS, PACK_ROWS + CHANNELS
    for i, value in enumerate([mix[0], mix[1], update[0], update[1]]):
        own_ref[top:low, i * LANES : i * LANES + CHANNELS] = value
    for i, value in enumerate([radial[0], radial[1], embed[...], readout[...].reshape(1, CHANNELS)]):
        own_ref[low : low + value.shape[0], i * LANES : i * LANES + CHANNELS] = value


def prepare_kernel(po_ref, *rest):
    own_hot, l1_ref, l2_ref, l3_ref, l5_ref, l6_ref, col_ref, copy_ref, pack_ref = rest
    pack_ref[...] = po_ref[0:PACK_ROWS, :]
    for b in range(SLAB_BLOCKS):
        mark(window_index(po_ref, b), [0, 1, 2], own_hot.at[b])
    for c in range(3):
        copy_ref[c] = po_ref[ROW_X + c : ROW_X + c + 1, :]

    def raw(first, count, i):
        return po_ref[first : first + count, i * LANES : i * LANES + CHANNELS]

    low = PACK_ROWS + CHANNELS
    mix_ref = [raw(PACK_ROWS, CHANNELS, i) for i in range(2)]
    update_ref = [raw(PACK_ROWS, CHANNELS, 2 + i) for i in range(2)]
    radial_ref = [raw(low, BASIS, i) for i in range(2)]
    embed_ref, readout = raw(low, 2, 2), raw(low, 1, 3)
    eye = (
        lax.broadcasted_iota(jnp.int32, (CHANNELS, CHANNELS), 0)
        == lax.broadcasted_iota(jnp.int32, (CHANNELS, CHANNELS), 1)
    ).astype(F32)

    def turned(x):
        return lax.dot_general(eye, x, NT, precision=PRECISE, preferred_element_type=F32)

    base0 = embed_ref[0:1, :]
    base1 = embed_ref[1:2, :] - base0
    rows = jnp.concatenate([base0, base1], axis=0)
    sent = jnp.dot(rows, mix_ref[0], precision=PRECISE, preferred_element_type=F32)
    scale = 1.0 / math.sqrt(SLOTS)
    first = jnp.concatenate([radial_ref[0] * sent[0:1], radial_ref[0] * sent[1:2]], axis=0) * scale
    second = radial_ref[1] * scale
    folded = jnp.dot(update_ref[0], mix_ref[1], precision=PRECISE, preferred_element_type=F32)
    mix_t = turned(mix_ref[1])
    l1_ref[...] = left_stack(turned(first)).astype(BF16)
    l2_ref[...] = left_stack(turned(folded)).astype(BF16)
    high, low = split(turned(second))
    l3_ref[...] = jnp.concatenate([high, high, low, jnp.zeros_like(high)], axis=1).astype(BF16)
    high, low = split(folded)
    l5_ref[...] = jnp.concatenate([high, high, high, high, low, low], axis=1).astype(BF16)
    l6_ref[...] = left_stack(first).astype(BF16)
    wide = (CHANNELS, LANES)
    col_ref[0] = jnp.broadcast_to(jnp.sum(mix_t * base0, axis=1, keepdims=True), wide)
    col_ref[1] = jnp.broadcast_to(jnp.sum(mix_t * base1, axis=1, keepdims=True), wide)
    col_ref[2] = jnp.broadcast_to(jnp.sum(update_ref[0] * readout, axis=1, keepdims=True), wide)
    col_ref[3] = jnp.broadcast_to(jnp.sum(update_ref[1] * readout, axis=1, keepdims=True), wide)


def sin_cos(t):
    q = t * t
    s = -1.0 / 39916800.0
    for c in (1.0 / 362880.0, -1.0 / 5040.0, 1.0 / 120.0, -1.0 / 6.0, 1.0):
        s = s * q + c
    k = 1.0 / 479001600.0
    for c in (-1.0 / 3628800.0, 1.0 / 40320.0, -1.0 / 720.0, 1.0 / 24.0, -0.5, 1.0):
        k = k * q + c
    return s * t, k


def wide_row(x, row):
    return jnp.broadcast_to(x[row : row + 1, :], (8, x.shape[1]))


def silu_parts(m):
    sig = 1.0 / (1.0 + jnp.exp(-m))
    return m * sig, sig * (1.0 + m * (1.0 - sig))


def pick(values, lanes):
    return jnp.take_along_axis(values, lanes, axis=1, mode="promise_in_bounds")


def reach(b, first, last):
    return [w for w in range(3) if first <= b - 1 + w <= last]


SIDE_START = {2: 0, 3: LANES, 8: 3 * LANES, 9: 5 * LANES}
SIDE_ROWS = 6 * LANES


def mark(index, ws, target):
    count = len(ws) * LANES
    row_id = (lax.broadcasted_iota(jnp.int32, (count, LANES), 0) + ws[0] * LANES).astype(jnp.int16)
    one, zero = jnp.ones((count, LANES), BF16), jnp.zeros((count, LANES), BF16)
    for k in range(SLOTS):
        wanted = jnp.broadcast_to(index[k : k + 1, :], (16, LANES)).astype(jnp.int16)
        wanted = jnp.concatenate([wanted] * (count // 16), axis=0)
        target[:, k * LANES : (k + 1) * LANES] = jnp.where(row_id == wanted, one, zero)


def window_index(pack, b):
    lanes = slice((b % 4) * LANES, (b % 4 + 1) * LANES)
    return pack[0:8, lanes].astype(jnp.int32) - LANES * (b % 4)


def mark_sides(packs, side):
    for b, start in SIDE_START.items():
        ws = reach(b, 3, 8)
        mark(window_index(packs[b // 4], b), ws, side.at[start : start + len(ws) * LANES])


def forward_parts(packs, weights, xs, sst, kept):
    l1, l2, l3, l5, l6, col = weights
    (widx, kinds, geo, bst, bps, bpr, sent_all, sent_pair, slope) = kept
    centre = 2.0 + 0.5 * lax.broadcasted_iota(jnp.int32, (BASIS, LANES), 0).astype(F32)
    slot = lax.broadcasted_iota(jnp.int32, (SLOTS, LANES), 0)

    def part_rows(value):
        high, low = split(value)
        return jnp.concatenate([high, low], axis=0).astype(BF16)

    def pairs(b):
        pack = packs[b // 4]
        lanes = slice((b % 4) * LANES, (b % 4 + 1) * LANES)
        index = window_index(pack, b)
        widx[b] = index
        inner = index & (LANES - 1)
        part = index >> 7

        def taken(row):
            got = [
                pick(jnp.broadcast_to(xs[b - 1 + w, row : row + 1, :], (SLOTS, LANES)), inner)
                for w in range(3)
            ]
            return jnp.where(part == 0, got[0], jnp.where(part == 1, got[1], got[2]))

        vec = [
            pack[8 + 8 * c : 16 + 8 * c, lanes] + taken(c) - jnp.broadcast_to(xs[b, c : c + 1, :], (SLOTS, LANES))
            for c in range(3)
        ]
        kind = taken(3)
        dist = jnp.sqrt(vec[0] * vec[0] + vec[1] * vec[1] + vec[2] * vec[2] + SOFTENING)
        live = (slot.astype(F32) < jnp.broadcast_to(pack[ROW_COUNT : ROW_COUNT + 1, lanes], (SLOTS, LANES))).astype(F32)
        turns = dist * (1.0 / 12.0)
        turns = turns - jnp.floor(turns + 0.5)
        sine, cosine = sin_cos(turns * math.pi)
        envelope = cosine * cosine * live
        slant = cosine * sine * live * (-math.pi / 6.0)
        if 3 <= b <= 8:
            kinds[b] = kind
            for c in range(3):
                geo[b, c] = vec[c]
            geo[b, 3] = 1.0 / dist
        total = jnp.zeros((BASIS, LANES), F32)
        total_kind = jnp.zeros((BASIS, LANES), F32)
        for k in range(SLOTS):
            away = wide_row(dist, k) - centre
            gauss = jnp.exp(-4.0 * (away * away))
            env_k = wide_row(envelope, k)
            value = gauss * env_k
            total = total + value
            total_kind = total_kind + value * wide_row(kind, k)
            cols = slice(k * LANES, (k + 1) * LANES)
            if 2 <= b <= 9:
                bst[b, :, cols] = part_rows(value)
            if 3 <= b <= 8:
                value = gauss * (wide_row(slant, k) - 8.0 * away * env_k)
                bpr[b, :, cols] = value
                bps[b, :, cols] = part_rows(value)
        high, low = split(jnp.concatenate([total, total_kind], axis=0))
        sst[:, b * LANES : (b + 1) * LANES] = jnp.concatenate([high, low, high], axis=0).astype(BF16)

    for b in range(1, 11):
        pairs(b)

    for b in range(1, 11, 2):
        cols = slice(b * LANES, (b + 2) * LANES)
        value, steep = silu_parts(mm(l1[...], sst[:, cols]))
        sent = mm(l2[...], right_stack(value))
        for i in range(2):
            one = sent[:, i * LANES : (i + 1) * LANES]
            one = one + col[0] + col[1] * jnp.broadcast_to(xs[b + i, 3:4, :], (CHANNELS, LANES))
            sent_all[:, (b + i) * LANES : (b + i + 1) * LANES] = one
            if 3 <= b + i <= 8:
                sent_pair[:, (b + i) * LANES : (b + i + 1) * LANES] = pair_stack(one)
        slope[:, cols] = steep


def force_parts(weights, own_hot, side_hot, kept, dg, pulls, met, acc, held):
    l1, l2, l3, l5, l6, col = weights
    (widx, kinds, geo, bst, bps, bpr, sent_all, sent_pair, slope) = kept
    slot = lax.broadcasted_iota(jnp.int32, (SLOTS, LANES), 0)

    def marks(b, ws):
        if b in SIDE_START:
            start = SIDE_START[b] + (ws[0] - reach(b, 3, 8)[0]) * LANES
            return side_hot.at[start : start + len(ws) * LANES]
        return own_hot.at[b - 4, ws[0] * LANES : (ws[-1] + 1) * LANES]

    def add_rows(sums, first, b, ws, out):
        for i, w in enumerate(ws):
            target = b - 1 + w
            piece = out[i * LANES : (i + 1) * LANES]
            rows = slice((target - first) * LANES, (target - first + 1) * LANES)
            if (first, target) in started:
                sums[rows, :] += piece
            else:
                sums[rows, :] = piece
                started.add((first, target))

    started = set()

    def block_work(b):
        index = widx[b]
        inner, part = index & (LANES - 1), index >> 7
        basis = bst[b]
        radial = mm(l3[...], jnp.concatenate([basis, basis], axis=0))
        if 3 <= b <= 8:
            basis = bps[b]
            steepness = mm(l3[...], jnp.concatenate([basis, basis], axis=0))
        lanes = [jnp.broadcast_to(inner[k : k + 1, :], (16, LANES)) for k in range(SLOTS)]
        parts = [jnp.broadcast_to(part[k : k + 1, :], (16, LANES)) for k in range(SLOTS)]
        own = 4 <= b <= 7
        if own:
            found_all = mm(sent_pair[:, (b - 1) * LANES : (b + 2) * LANES], own_hot[b - 4])
        value = held.at[b % 2]
        total = [jnp.zeros((8, LANES), F32)] * SLOTS
        for u in range(CHANNELS // 16):
            rows = slice(16 * u, 16 * u + 16)
            low_rows = slice(CHANNELS + 16 * u, CHANNELS + 16 * u + 16)
            windows = [sent_all[rows, (b - 1 + w) * LANES : (b + w) * LANES] for w in range(3)]
            got = []
            message = jnp.zeros((16, LANES), F32)
            for k in range(SLOTS):
                cols = slice(k * LANES, (k + 1) * LANES)
                if own:
                    got.append(found_all[rows, cols] + found_all[low_rows, cols])
                else:
                    found = [pick(window, lanes[k]) for window in windows]
                    got.append(jnp.where(parts[k] == 0, found[0], jnp.where(parts[k] == 1, found[1], found[2])))
                message = message + radial[rows, cols] * got[k]
            _, steep = silu_parts(message)
            back = col[3, rows] * steep
            for k in range(SLOTS):
                cols = slice(k * LANES, (k + 1) * LANES)
                high, low = split(radial[rows, cols] * back)
                value[rows, cols] = high.astype(BF16)
                value[low_rows, cols] = low.astype(BF16)
                if 3 <= b <= 8:
                    pull = got[k] * back * steepness[rows, cols]
                    total[k] = total[k] + pull[0:8] + pull[8:16]
            yield
        if 3 <= b <= 8:
            for k in range(SLOTS):
                pulls[b, :, k * LANES : (k + 1) * LANES] = total[k]

    def scatter_work(b):
        ws = reach(b, 3, 8)
        chosen, value = marks(b, ws), held.at[b % 2]
        out = None
        for u in range(4):
            cols = slice(u * 2 * LANES, (u + 1) * 2 * LANES)
            one = mm_nt(chosen[:, cols], value[:, cols])
            out = one if out is None else out + one
            yield
        add_rows(dg, 3, b, ws, out)

    def together(*works):
        works = list(works)
        while works:
            works = [work for work in works if next(work, "end") != "end"]

    together(block_work(2))
    for b in range(3, 10):
        together(scatter_work(b - 1), block_work(b))
    together(scatter_work(9))

    def finish(b, sums):
        kind = kinds[b]
        rows = []
        for k in range(SLOTS):
            cols = slice(k * LANES, (k + 1) * LANES)
            weight = sums[0:8] + wide_row(kind, k) * sums[8:16]
            rows.append(jnp.sum(bpr[b, :, cols] * weight + pulls[b, :, cols], axis=0, keepdims=True))
        pull = jnp.concatenate(rows, axis=0) * geo[b, 3]
        pieces = []
        for c in range(3):
            value = pull * geo[b, c]
            if 4 <= b <= 7:
                acc[b - 4, c] = jnp.sum(value, axis=0, keepdims=True)
            pieces.append(split(value))
        lines = []
        for h in range(2):
            for c in range(3):
                lines.append(jnp.concatenate([jnp.where(slot == k, pieces[c][h], 0.0) for k in range(SLOTS)], axis=1))
        ws = reach(b, 4, 7)
        out = mm_nt(jnp.concatenate(lines, axis=0).astype(BF16), marks(b, ws)[...])
        for c in range(3):
            both = out[8 * c : 8 * c + 8] + out[24 + 8 * c : 32 + 8 * c]
            for i, w in enumerate(ws):
                target = b - 5 + w
                piece = both[:, i * LANES : (i + 1) * LANES]
                if (c, target) in met_blocks:
                    met[target, c] += piece
                else:
                    met[target, c] = piece
                    met_blocks.add((c, target))

    met_blocks = set()

    for b in range(3, 9, 2):
        cols = slice(b * LANES, (b + 2) * LANES)
        high, low = split(dg[(b - 3) * LANES : (b - 1) * LANES, :])
        steep = mm_nt(l5[...], jnp.concatenate([high, low, high], axis=1).astype(BF16))
        steep = steep + jnp.concatenate([col[2], col[2]], axis=1)
        sums = mm(l6[...], right_stack(steep * slope[:, cols]))
        for i in range(2):
            finish(b + i, sums[:, i * LANES : (i + 1) * LANES])

    away = []
    for c in range(3):
        back = [acc[i, c] - jnp.sum(met[i, c], axis=0, keepdims=True) for i in range(SLAB_BLOCKS)]
        away.append(jnp.concatenate(back, axis=1))
    return jnp.concatenate(away, axis=0)


def fill_region(xs, packs, rows_of):
    for b in range(12):
        lanes = slice((b % 4) * LANES, (b % 4 + 1) * LANES)
        pack = packs[b // 4]
        xs[b, 0:3, :] = rows_of(b // 4)[:, lanes]
        xs[b, 3:4, :] = pack[ROW_KIND : ROW_KIND + 1, lanes]


def lane_total(x):
    x = x[:, 0:LANES] + x[:, LANES : 2 * LANES] + x[:, 2 * LANES : 3 * LANES] + x[:, 3 * LANES : 4 * LANES]
    return jnp.sum(x, axis=1, keepdims=True)


def dot3(a, b):
    return jnp.sum(a * b, axis=0, keepdims=True)


def kept_shapes():
    wide = 12 * LANES
    return [
        ((12, 8, LANES), jnp.int32),
        ((12, 8, LANES), F32),
        ((12, 4, 8, LANES), F32),
        ((12, 16, SLOTS * LANES), BF16),
        ((12, 16, SLOTS * LANES), BF16),
        ((12, 8, SLOTS * LANES), F32),
        ((CHANNELS, wide), F32),
        ((2 * CHANNELS, wide), BF16),
        ((CHANNELS, wide), F32),
    ]


def forward_scratch():
    return [pltpu.VMEM((12, 8, LANES), F32), pltpu.VMEM((48, 12 * LANES), BF16)]


def back_scratch():
    return [
        pltpu.VMEM((6 * LANES, 2 * CHANNELS), F32),
        pltpu.VMEM((12, 8, SLOTS * LANES), F32),
        pltpu.VMEM((SLAB_BLOCKS, 3, SLOTS, LANES), F32),
        pltpu.VMEM((SLAB_BLOCKS, 3, 1, LANES), F32),
        pltpu.VMEM((2, 2 * CHANNELS, SLOTS * LANES), BF16),
    ]


def by_parity(sibling, across):
    even = jnp.full(sibling.shape, lax.axis_index("dom") % 2, jnp.int32) == 0
    return jnp.where(even, across, sibling), jnp.where(even, sibling, across)


def first_kernel(sibling_ref, po_ref, across_ref, own_hot, *rest):
    weights, (out_ref, pl_ref, pr_ref, side_hot), scr = rest[:6], rest[6:10], rest[10:]
    xs, sst, kept = scr[0], scr[1], scr[2:11]
    pl_ref[...], pr_ref[...] = by_parity(sibling_ref[...], across_ref[...])
    packs = [pl_ref, po_ref, pr_ref]
    mark_sides(packs, side_hot)
    fill_region(xs, packs, lambda s: packs[s][ROW_X : ROW_X + 3, :])
    forward_parts(packs, weights, xs, sst, kept)
    out_ref[...] = force_parts(weights, own_hot, side_hot, kept, *scr[11:])


def rows_of(ref):
    return jnp.concatenate([ref[c] for c in range(3)], axis=0)


def block_row(*values):
    values = list(values) + [jnp.zeros((1, LANES), F32)] * (SLAB_BLOCKS - len(values))
    return jnp.concatenate(values, axis=1)


def blend_kernel(images, force_ref, po_ref, before_ref, after_ref, out_ref, sums_ref):
    x = po_ref[ROW_X : ROW_X + 3, :]
    v = po_ref[ROW_V : ROW_V + 3, :]
    force = force_ref[...]
    here = lax.axis_index("img")
    before = jnp.where(here > 0, rows_of(before_ref), 0.0)
    after = jnp.where(here < images - 1, rows_of(after_ref), 0.0)
    tangent = after - before
    plus = after - x
    minus = x - before
    sums = jnp.concatenate(
        [
            dot3(force, tangent),
            dot3(force, force),
            dot3(tangent, tangent),
            dot3(plus, plus),
            dot3(minus, minus),
            dot3(v, v),
            jnp.zeros((2, x.shape[1]), F32),
        ],
        axis=0,
    )
    sums = jnp.broadcast_to(lane_total(sums), (8, LANES))
    sums_ref[...] = sums
    out_ref[0:3, :] = force
    out_ref[3:6, :] = tangent
    out_ref[6:7, :] = block_row(*[sums[i : i + 1] for i in range(4)])
    out_ref[7:8, :] = block_row(sums[4:5], sums[5:6])


def step_numbers(ft, ff, tt, pp, mn, vv, dt, alpha, flagged, climbing, inside):
    root = jnp.sqrt(tt + TINY_VALUE)
    along = ft / root
    spring = SPRING_CONSTANT * (jnp.sqrt(pp) - jnp.sqrt(mn))
    factor = jnp.where(climbing, -2.0 * along, spring - along)
    band = jnp.maximum(ff + 2.0 * factor * along + factor * factor * (tt / (tt + TINY_VALUE)), 0.0)
    new_dt = jnp.where(flagged, 0.5 * dt, jnp.minimum(1.1 * dt, STEP_LIMIT))
    pull = jnp.where(flagged, 0.0, alpha * jnp.sqrt(vv / (band + TINY_VALUE))) + new_dt
    keep = jnp.where(flagged, 0.0, 1.0 - alpha)
    new_alpha = jnp.where(flagged, ALPHA_START, 0.99 * alpha)
    keep = jnp.where(inside, keep, 0.0)
    pull = jnp.where(inside, pull, 0.0)
    return (
        jnp.where(inside, along, 0.0),
        jnp.where(inside, spring, 0.0),
        keep,
        pull,
        pull * factor / root,
        new_dt,
        new_alpha,
    )


def add_kernel(a_ref, b_ref, out_ref):
    out_ref[...] = a_ref[...] + b_ref[...]


def number_kernel(dt_ref, flag_ref, climb_ref, out_ref):
    flags = [flag_ref[0, s].astype(F32) for s in range(flag_ref.shape[1])]
    for i, value in enumerate([dt_ref[0], climb_ref[0].astype(F32)] + flags):
        out_ref[i : i + 1, :] = jnp.full((1, LANES), value, F32)


def second_kernel(images, domains, number_ref, pl_ref, po_ref, pr_ref, own_ref, near_ref, far_ref, *rest):
    count = 2 if domains == 4 else 1
    parts, rest = rest[:count], rest[count:]
    (own_hot, side_hot), weights, (out_ref, record_ref), scr = rest[:2], rest[2:8], rest[8:10], rest[10:]
    packs = [pl_ref, po_ref, pr_ref]
    here = lax.axis_index("img")
    sums = parts[0][...]
    if domains == 4:
        sums = sums + parts[1][...]
    got = [sums[i : i + 1, :] for i in range(6)]
    if domains == 4:
        for one in (near_ref, far_ref):
            for i in range(6):
                got[i] = got[i] + one[6 + i // 4 : 7 + i // 4, (i % 4) * LANES : (i % 4 + 1) * LANES]
    ft, ff, tt, pp, mn, vv = got
    beside = by_parity(near_ref[0:6, :], far_ref[0:6, :])
    shape = (1, LANES)
    along, spring, keep, pull, side, dt, alpha = step_numbers(
        ft,
        ff,
        tt,
        pp,
        mn,
        vv,
        number_ref[0:1, :],
        jnp.full(shape, ALPHA_START, F32),
        number_ref[2:3, :] == 1.0,
        number_ref[1:2, :] == jnp.full(shape, here, jnp.int32).astype(F32),
        jnp.full(shape, jnp.where((here >= 1) & (here <= images - 2), 1, 0), jnp.int32) == 1,
    )
    messages = [beside[0], own_ref[0:6, :], beside[1]]

    def wide(s):
        return jnp.concatenate([s] * SLAB_BLOCKS, axis=1)

    speeds = [
        wide(keep) * p[ROW_V : ROW_V + 3, :] + wide(pull) * m[0:3, :] + wide(side) * m[3:6, :]
        for p, m in zip(packs, messages)
    ]
    moved = [p[ROW_X : ROW_X + 3, :] + wide(dt) * s for p, s in zip(packs, speeds)]
    xs, sst, kept = scr[0], scr[1], scr[2:11]
    fill_region(xs, packs, lambda s: moved[s])
    forward_parts(packs, weights, xs, sst, kept)
    force = force_parts(weights, own_hot, side_hot, kept, *scr[11:])
    for c in range(3):
        for i in range(SLAB_BLOCKS):
            lanes = slice(i * LANES, (i + 1) * LANES)
            row = 4 * c + i
            out_ref[0, row : row + 1, :] = speeds[1][c : c + 1, lanes]
            out_ref[0, 12 + row : 13 + row, :] = force[c : c + 1, lanes]
            out_ref[0, 24 + row : 25 + row, :] = moved[1][c : c + 1, lanes]
    out_ref[0, 36:37, :] = dt
    out_ref[0, 37:38, :] = alpha
    out_ref[0, 38:40, :] = jnp.broadcast_to(number_ref[3:4, :], (2, LANES))
    record_ref[0:1, :] = along
    record_ref[1:2, :] = spring
    record_ref[2:3, :] = number_ref[1:2, :]


PRODUCTS = (
    [("f", "t"), ("f", "f"), ("t", "t"), ("p", "p"), ("d", "d"), ("v", "v")]
    + [("d", "v"), ("d", "f"), ("d", "t"), ("d", "V"), ("d", "F"), ("d", "T"), ("v", "f"), ("v", "t")]
    + [(a, b) for a in "vft" for b in "VFT"]
)


def gram_kernel(images, *refs):
    parts, (out_ref, state_ref, messages_ref) = refs[:-3], refs[-3:]
    rows = out_ref.shape[0]
    place = 0
    for part in parts:
        messages_ref[place : place + part.shape[0]] = part[...]
        place += part.shape[0]
    here = lax.axis_index("img")
    blank = [jnp.zeros((rows - images, LANES), F32)] if rows > images else []
    zero = jnp.zeros((1, LANES), F32)

    def gathered(row):
        return jnp.concatenate([messages_ref[lax.rem(here + images - i, images), row : row + 1, :] for i in range(images)] + blank, axis=0)

    def earlier(value):
        return jnp.concatenate([zero, value[0 : rows - 1]], axis=0)

    def later(value):
        return jnp.concatenate([value[1:images], zero] + blank, axis=0)

    number = lax.broadcasted_iota(jnp.int32, (rows, LANES), 0)
    held = number < images
    totals = [jnp.zeros((rows, LANES), F32) for _ in PRODUCTS]
    for row in range(3 * SLAB_BLOCKS):
        v, f, x = gathered(row), gathered(12 + row), gathered(24 + row)
        before = jnp.where(held, earlier(x), 0.0)
        after = later(x)
        t = after - before
        table = {"f": f, "v": v, "t": t, "p": after - x, "d": x - before}
        table["F"], table["V"], table["T"] = earlier(f), earlier(v), earlier(t)
        totals = [old + table[a] * table[b] for old, (a, b) in zip(totals, PRODUCTS)]
        state_ref[row : row + 1, :] = jnp.sum(jnp.where(number == here, t, 0.0), axis=0, keepdims=True)
    lane = lax.broadcasted_iota(jnp.int32, (rows, LANES), 1)
    result = jnp.zeros((rows, LANES), F32)
    for q, one in enumerate(totals):
        one = jnp.broadcast_to(jnp.sum(one, axis=1, keepdims=True), (rows, LANES))
        result = jnp.where(lane == q, one, result)
    out_ref[...] = result
    for i in range(3):
        state_ref[16 + rows * i : 16 + rows * (i + 1), :] = gathered(36 + i)


def final_kernel(images, atoms, own_ref, record_ref, state_ref, *rest):
    parts, (x_ref, v_ref, band_ref, path_ref) = rest[:-4], rest[-4:]
    rows = parts[0].shape[0]
    here = lax.axis_index("img")
    sums = parts[0][...]
    for one in parts[1:]:
        sums = sums + one[...]
    got = {
        pair: jnp.broadcast_to(sums[:, q : q + 1], (rows, LANES)) for q, pair in enumerate(PRODUCTS)
    }
    number = lax.broadcasted_iota(jnp.int32, (rows, LANES), 0)
    inside = (number >= 1) & (number <= images - 2)
    climb = jnp.broadcast_to(record_ref[2:3, :], (rows, LANES))
    dt0, alpha0, flag = (state_ref[16 + rows * i : 16 + rows * (i + 1), :] for i in range(3))
    along, spring, keep, pull, side, dt, _ = step_numbers(
        got["f", "t"],
        got["f", "f"],
        got["t", "t"],
        got["p", "p"],
        got["d", "d"],
        got["v", "v"],
        dt0,
        alpha0,
        flag == 1.0,
        number.astype(F32) == climb,
        inside,
    )

    def shifted(value):
        return jnp.concatenate([jnp.zeros((1, LANES), F32), value[0 : rows - 1]], axis=0)

    now = {"v": dt * keep, "f": dt * pull, "t": dt * side}
    old = {a.upper(): shifted(value) for a, value in now.items()}
    mine = now["v"] * now["v"] * got["v", "v"] + now["f"] * now["f"] * got["f", "f"]
    mine = mine + now["t"] * now["t"] * got["t", "t"]
    cross = now["v"] * now["f"] * got["v", "f"] + now["v"] * now["t"] * got["v", "t"]
    mine = mine + 2.0 * (cross + now["f"] * now["t"] * got["f", "t"])
    both = jnp.zeros((rows, LANES), F32)
    for a in "vft":
        both = both + now[a] * got["d", a]
    for b in "VFT":
        both = both - old[b] * got["d", b]
    for a in "vft":
        for b in "VFT":
            both = both - now[a] * old[b] * got[a, b]
    squared = got["d", "d"] + mine + shifted(mine) + 2.0 * both
    segment = jnp.sqrt(jnp.maximum(squared, 0.0) * (1.0 / (3.0 * atoms)))
    path = jnp.sum(jnp.where(number <= here, segment, 0.0), axis=0, keepdims=True)
    path_ref[...] = path[:, 0:1]
    keep, pull, side, dt, along, spring = (
        jnp.sum(jnp.where(number == here, value, 0.0), axis=0, keepdims=True)
        for value in (keep, pull, side, dt, along, spring)
    )

    for c in range(3):
        speeds, places = [], []
        for i in range(SLAB_BLOCKS):
            row = 4 * c + i
            speed = keep * own_ref[0, row : row + 1, :] + pull * own_ref[0, 12 + row : 13 + row, :]
            speed = speed + side * state_ref[row : row + 1, :]
            speeds.append(speed)
            places.append(own_ref[0, 24 + row : 25 + row, :] + dt * speed)
        v_ref[c] = jnp.concatenate(speeds, axis=1)
        x_ref[c] = jnp.concatenate(places, axis=1)
    band_ref[0] = jnp.concatenate([record_ref[0:1, 0:1], record_ref[1:2, 0:1]], axis=1)
    band_ref[1] = jnp.concatenate([along[:, 0:1], spring[:, 0:1]], axis=1)


VMEM_SPEC = pl.BlockSpec(memory_space=pltpu.VMEM)
SMEM_SPEC = pl.BlockSpec(memory_space=pltpu.SMEM)
HBM_SPEC = pl.BlockSpec(memory_space=pltpu.HBM)


def call(body, outs, scalars, arrays, scratch_shapes=(), flops=0, spec=VMEM_SPEC, vmem=24):
    return pl.pallas_call(
        body,
        out_shape=outs,
        in_specs=[SMEM_SPEC] * len(scalars) + [spec] * len(arrays),
        out_specs=jax.tree.map(lambda _: VMEM_SPEC, outs),
        scratch_shapes=list(scratch_shapes),
        compiler_params=pltpu.CompilerParams(vmem_limit_bytes=vmem * 1024 * 1024),
        cost_estimate=pl.CostEstimate(flops=flops, bytes_accessed=1 << 18, transcendentals=0),
    )(*scalars, *arrays)


def swap(array, axis, partner):
    return lax.ppermute(array, axis, [(i, partner(i)) for i in range(lax.axis_size(axis))])


def exchanged(sums, axis):
    count = lax.axis_size(axis)
    if count == 4:
        return [sums] + [swap(sums, axis, lambda i, by=by: i ^ by) for by in (2, 3, 1)]
    distance = 1
    while distance < count:
        more = swap(sums, axis, lambda i, by=distance: i ^ by)
        sums = call(add_kernel, jax.ShapeDtypeStruct(sums.shape, F32), (), (sums, more))
        distance *= 2
    return [sums]


def collected(array, axis):
    count = lax.axis_size(axis)
    return [array] + [swap(array, axis, lambda i, by=by: (i + by) % count) for by in range(1, count)]


def local(
    disp,
    veloc,
    time_step,
    reset_flags,
    climb,
    species,
    neighbours,
    counts,
    lattice,
    embed,
    radial_weight,
    mix_weight,
    update_weight,
    readout,
):
    atoms = disp.shape[2]
    images = lax.axis_size("img")
    domains = lax.axis_size("dom")
    assert disp.shape[0] == 1 and atoms == SLAB_BLOCKS * LANES and domains >= 4
    assert domains & (domains - 1) == 0 and images & (images - 1) == 0
    shape = jax.ShapeDtypeStruct
    x = jnp.transpose(disp, (1, 0, 2))
    v = jnp.transpose(veloc, (1, 0, 2))
    small = (x, v, species, neighbours, counts, embed, readout, radial_weight, mix_weight, update_weight)
    sent, kept_pack = call(
        pack_kernel,
        (shape((PACK_ROWS, atoms), F32), shape((OWN_ROWS, atoms), F32)),
        (),
        (*small, jnp.transpose(lattice, (1, 0, 2))),
        [pltpu.VMEM(a.shape, a.dtype) for a in small] + [pltpu.SemaphoreType.DMA((16,))],
        spec=HBM_SPEC,
        vmem=63,
    )
    sibling = swap(sent, "dom", lambda i: i ^ 1)
    across = swap(sent, "dom", lambda i: (i + 2 * (i % 2) - 1) % domains)
    own_hot, *weights, x_copy, pack = call(
        prepare_kernel,
        (
            shape((SLAB_BLOCKS, 3 * LANES, SLOTS * LANES), BF16),
            shape((CHANNELS, 48), BF16),
            shape((CHANNELS, 192), BF16),
            shape((CHANNELS, 32), BF16),
            shape((CHANNELS, 3 * LANES), BF16),
            shape((16, 192), BF16),
            shape((4, CHANNELS, LANES), F32),
            shape(x.shape, F32),
            shape(sent.shape, F32),
        ),
        (),
        (kept_pack,),
        flops=100000000,
    )
    before = swap(x_copy, "img", lambda i: (i + 1) % images)
    after = swap(x_copy, "img", lambda i: (i - 1) % images)
    force_scratch = forward_scratch() + [pltpu.VMEM(*one) for one in kept_shapes()] + back_scratch()
    force, left, right, side_hot = call(
        first_kernel,
        (
            shape((3, atoms), F32),
            shape(sent.shape, F32),
            shape(sent.shape, F32),
            shape((SIDE_ROWS, SLOTS * LANES), BF16),
        ),
        (),
        (sibling, pack, across, own_hot, *weights),
        force_scratch,
        flops=1000000000,
    )
    message, sums = call(
        functools.partial(blend_kernel, images),
        (shape((8, atoms), F32), shape((8, LANES), F32)),
        (),
        (force, pack, before, after),
    )
    far = swap(message, "dom", lambda i: (i + 2 * (i % 2) - 1) % domains)
    if domains == 4:
        parts = [sums, swap(sums, "dom", lambda i: i ^ 2)]
    else:
        parts = exchanged(sums, "dom")
    near = swap(message, "dom", lambda i: i ^ 1)
    numbers = call(number_kernel, shape((8, LANES), F32), (time_step, jnp.transpose(reset_flags), climb), ())
    state, record = call(
        functools.partial(second_kernel, images, domains),
        (shape((1, 40, LANES), F32), shape((3, LANES), F32)),
        (),
        (numbers, left, pack, right, message, near, far, *parts, own_hot, side_hot, *weights),
        force_scratch,
        flops=1000000000,
    )
    rows = 8 * ((images + 7) // 8)
    sums, extra = call(
        functools.partial(gram_kernel, images),
        (shape((rows, LANES), F32), shape((16 + 3 * rows, LANES), F32)),
        (),
        collected(state, "img"),
        [pltpu.VMEM((images, 40, LANES), F32)],
    )
    new_x, new_v, records, path = call(
        functools.partial(final_kernel, images, atoms * domains),
        (shape(x.shape, F32), shape(x.shape, F32), shape((2, 1, 2), F32), shape((1, 1), F32)),
        (),
        (state, record, extra, *exchanged(sums, "dom")),
    )
    return (
        jnp.transpose(new_x, (1, 0, 2)),
        jnp.transpose(new_v, (1, 0, 2)),
        jnp.transpose(records, (0, 2, 1)),
        path.reshape(1),
    )


def solution(mesh):
    in_specs = (
        P(("group", "img"), None, "dom"),
        P(("group", "img"), None, "dom"),
        P(("group", "img")),
        P(None, ("group", "img")),
        P("group"),
        P(("group", "dom")),
        P(None, ("group", "dom")),
        P(("group", "dom")),
        P(None, None, ("group", "dom")),
        P(),
        P(),
        P(),
        P(),
        P(),
    )
    out_specs = (
        P(("group", "img"), None, "dom"),
        P(("group", "img"), None, "dom"),
        P(None, None, ("group", "img")),
        P(("group", "img")),
    )
    return jax.shard_map(local, mesh=mesh, in_specs=in_specs, out_specs=out_specs, check_vma=False)
```

```python
import functools
import math

import jax
import jax.numpy as jnp
from jax import lax
from jax.experimental import pallas as pl
from jax.experimental.pallas import tpu as pltpu
from jax.sharding import PartitionSpec as P

F32 = jnp.float32
BF16 = jnp.bfloat16
PRECISE = lax.Precision.HIGHEST
SPRING_CONSTANT = 0.5
ALPHA_START = 0.1
STEP_LIMIT = 0.3
TINY_VALUE = 1e-06
SOFTENING = 0.25
LANES = 128
SLOTS = 8
BASIS = 8
CHANNELS = 64
SLAB_BLOCKS = 4
ROW_X = 32
ROW_COUNT = 35
ROW_KIND = 36
ROW_V = 37
PACK_ROWS = 40
OWN_ROWS = PACK_ROWS + CHANNELS + BASIS
NT = (((1,), (1,)), ((), ()))


def split(x):
    high = x.astype(BF16).astype(F32)
    return high, x - high


def left_stack(w):
    high, low = split(w)
    return jnp.concatenate([high, high, low], axis=1)


def right_stack(x):
    high, low = split(x)
    high = high.astype(BF16)
    return jnp.concatenate([high, low.astype(BF16), high], axis=0)


def pair_stack(x):
    high, low = split(x)
    return jnp.concatenate([high.astype(BF16), low.astype(BF16)], axis=0)


def mm(a, b):
    return jnp.dot(a, b, preferred_element_type=F32)


def mm_nt(a, b):
    return lax.dot_general(a, b, NT, preferred_element_type=F32)


def pack_kernel(*refs):
    sources, (out_ref, own_ref), held, sems = refs[:11], refs[11:13], refs[13:23], refs[23]
    lattice = sources[10]
    pairs = list(zip(sources, held))
    for c in range(3):
        rows = pl.ds(8 + 8 * c, 8)
        pairs += [(lattice.at[c], out_ref.at[rows]), (lattice.at[c], own_ref.at[rows])]
    copies = [pltpu.make_async_copy(a, b, sems.at[i]) for i, (a, b) in enumerate(pairs)]
    for one in copies:
        one.start()
    for one in copies:
        one.wait()
    x, v, species, nbr, counts, embed, readout, radial, mix, update = held
    for ref in (out_ref, own_ref):
        ref[0:8, :] = nbr[...].astype(F32)
        for c in range(3):
            ref[ROW_X + c : ROW_X + c + 1, :] = x[c]
            ref[ROW_V + c : ROW_V + c + 1, :] = v[c]
        ref[ROW_COUNT : ROW_COUNT + 1, :] = counts[...].astype(F32).reshape(1, -1)
        ref[ROW_KIND : ROW_KIND + 1, :] = species[...].astype(F32).reshape(1, -1)
    top, low = PACK_ROWS, PACK_ROWS + CHANNELS
    for i, value in enumerate([mix[0], mix[1], update[0], update[1]]):
        own_ref[top:low, i * LANES : i * LANES + CHANNELS] = value
    for i, value in enumerate([radial[0], radial[1], embed[...], readout[...].reshape(1, CHANNELS)]):
        own_ref[low : low + value.shape[0], i * LANES : i * LANES + CHANNELS] = value


def prepare_kernel(po_ref, *rest):
    own_hot, l1_ref, l2_ref, l3_ref, l5_ref, l6_ref, col_ref, copy_ref, pack_ref = rest
    pack_ref[...] = po_ref[0:PACK_ROWS, :]
    for b in range(SLAB_BLOCKS):
        mark(window_index(po_ref, b), [0, 1, 2], own_hot.at[b])
    for c in range(3):
        copy_ref[c] = po_ref[ROW_X + c : ROW_X + c + 1, :]

    def raw(first, count, i):
        return po_ref[first : first + count, i * LANES : i * LANES + CHANNELS]

    low = PACK_ROWS + CHANNELS
    mix_ref = [raw(PACK_ROWS, CHANNELS, i) for i in range(2)]
    update_ref = [raw(PACK_ROWS, CHANNELS, 2 + i) for i in range(2)]
    radial_ref = [raw(low, BASIS, i) for i in range(2)]
    embed_ref, readout = raw(low, 2, 2), raw(low, 1, 3)
    eye = (
        lax.broadcasted_iota(jnp.int32, (CHANNELS, CHANNELS), 0)
        == lax.broadcasted_iota(jnp.int32, (CHANNELS, CHANNELS), 1)
    ).astype(F32)

    def turned(x):
        return lax.dot_general(eye, x, NT, precision=PRECISE, preferred_element_type=F32)

    base0 = embed_ref[0:1, :]
    base1 = embed_ref[1:2, :] - base0
    rows = jnp.concatenate([base0, base1], axis=0)
    sent = jnp.dot(rows, mix_ref[0], precision=PRECISE, preferred_element_type=F32)
    scale = 1.0 / math.sqrt(SLOTS)
    first = jnp.concatenate([radial_ref[0] * sent[0:1], radial_ref[0] * sent[1:2]], axis=0) * scale
    second = radial_ref[1] * scale
    folded = jnp.dot(update_ref[0], mix_ref[1], precision=PRECISE, preferred_element_type=F32)
    mix_t = turned(mix_ref[1])
    l1_ref[...] = left_stack(turned(first)).astype(BF16)
    l2_ref[...] = left_stack(turned(folded)).astype(BF16)
    high, low = split(turned(second))
    l3_ref[...] = jnp.concatenate([high, high, low, jnp.zeros_like(high)], axis=1).astype(BF16)
    high, low = split(folded)
    l5_ref[...] = jnp.concatenate([high, high, high, high, low, low], axis=1).astype(BF16)
    l6_ref[...] = left_stack(first).astype(BF16)
    wide = (CHANNELS, LANES)
    col_ref[0] = jnp.broadcast_to(jnp.sum(mix_t * base0, axis=1, keepdims=True), wide)
    col_ref[1] = jnp.broadcast_to(jnp.sum(mix_t * base1, axis=1, keepdims=True), wide)
    col_ref[2] = jnp.broadcast_to(jnp.sum(update_ref[0] * readout, axis=1, keepdims=True), wide)
    col_ref[3] = jnp.broadcast_to(jnp.sum(update_ref[1] * readout, axis=1, keepdims=True), wide)


def sin_cos(t):
    q = t * t
    s = -1.0 / 39916800.0
    for c in (1.0 / 362880.0, -1.0 / 5040.0, 1.0 / 120.0, -1.0 / 6.0, 1.0):
        s = s * q + c
    k = 1.0 / 479001600.0
    for c in (-1.0 / 3628800.0, 1.0 / 40320.0, -1.0 / 720.0, 1.0 / 24.0, -0.5, 1.0):
        k = k * q + c
    return s * t, k


def wide_row(x, row):
    return jnp.broadcast_to(x[row : row + 1, :], (8, x.shape[1]))


def silu_parts(m):
    sig = 1.0 / (1.0 + jnp.exp(-m))
    return m * sig, sig * (1.0 + m * (1.0 - sig))


def pick(values, lanes):
    return jnp.take_along_axis(values, lanes, axis=1, mode="promise_in_bounds")


def reach(b, first, last):
    return [w for w in range(3) if first <= b - 1 + w <= last]


SIDE_START = {2: 0, 3: LANES, 8: 3 * LANES, 9: 5 * LANES}
SIDE_ROWS = 6 * LANES


def mark(index, ws, target):
    count = len(ws) * LANES
    row_id = (lax.broadcasted_iota(jnp.int32, (count, LANES), 0) + ws[0] * LANES).astype(jnp.int16)
    one, zero = jnp.ones((count, LANES), BF16), jnp.zeros((count, LANES), BF16)
    for k in range(SLOTS):
        wanted = jnp.broadcast_to(index[k : k + 1, :], (16, LANES)).astype(jnp.int16)
        wanted = jnp.concatenate([wanted] * (count // 16), axis=0)
        target[:, k * LANES : (k + 1) * LANES] = jnp.where(row_id == wanted, one, zero)


def window_index(pack, b):
    lanes = slice((b % 4) * LANES, (b % 4 + 1) * LANES)
    return pack[0:8, lanes].astype(jnp.int32) - LANES * (b % 4)


def mark_sides(packs, side):
    for b, start in SIDE_START.items():
        ws = reach(b, 3, 8)
        mark(window_index(packs[b // 4], b), ws, side.at[start : start + len(ws) * LANES])


def forward_parts(packs, weights, xs, sst, kept):
    l1, l2, l3, l5, l6, col = weights
    (widx, kinds, geo, bst, bps, bpr, sent_all, sent_pair, slope) = kept
    centre = 2.0 + 0.5 * lax.broadcasted_iota(jnp.int32, (BASIS, LANES), 0).astype(F32)
    slot = lax.broadcasted_iota(jnp.int32, (SLOTS, LANES), 0)

    def part_rows(value):
        high, low = split(value)
        return jnp.concatenate([high, low], axis=0).astype(BF16)

    def pairs(b):
        pack = packs[b // 4]
        lanes = slice((b % 4) * LANES, (b % 4 + 1) * LANES)
        index = window_index(pack, b)
        widx[b] = index
        inner = index & (LANES - 1)
        part = index >> 7

        def taken(row):
            got = [
                pick(jnp.broadcast_to(xs[b - 1 + w, row : row + 1, :], (SLOTS, LANES)), inner)
                for w in range(3)
            ]
            return jnp.where(part == 0, got[0], jnp.where(part == 1, got[1], got[2]))

        vec = [
            pack[8 + 8 * c : 16 + 8 * c, lanes] + taken(c) - jnp.broadcast_to(xs[b, c : c + 1, :], (SLOTS, LANES))
            for c in range(3)
        ]
        kind = taken(3)
        dist = jnp.sqrt(vec[0] * vec[0] + vec[1] * vec[1] + vec[2] * vec[2] + SOFTENING)
        live = (slot.astype(F32) < jnp.broadcast_to(pack[ROW_COUNT : ROW_COUNT + 1, lanes], (SLOTS, LANES))).astype(F32)
        turns = dist * (1.0 / 12.0)
        turns = turns - jnp.floor(turns + 0.5)
        sine, cosine = sin_cos(turns * math.pi)
        envelope = cosine * cosine * live
        slant = cosine * sine * live * (-math.pi / 6.0)
        if 3 <= b <= 8:
            kinds[b] = kind
            for c in range(3):
                geo[b, c] = vec[c]
            geo[b, 3] = 1.0 / dist
        total = jnp.zeros((BASIS, LANES), F32)
        total_kind = jnp.zeros((BASIS, LANES), F32)
        for k in range(SLOTS):
            away = wide_row(dist, k) - centre
            gauss = jnp.exp(-4.0 * (away * away))
            env_k = wide_row(envelope, k)
            value = gauss * env_k
            total = total + value
            total_kind = total_kind + value * wide_row(kind, k)
            cols = slice(k * LANES, (k + 1) * LANES)
            if 2 <= b <= 9:
                bst[b, :, cols] = part_rows(value)
            if 3 <= b <= 8:
                value = gauss * (wide_row(slant, k) - 8.0 * away * env_k)
                bpr[b, :, cols] = value
                bps[b, :, cols] = part_rows(value)
        high, low = split(jnp.concatenate([total, total_kind], axis=0))
        sst[:, b * LANES : (b + 1) * LANES] = jnp.concatenate([high, low, high], axis=0).astype(BF16)

    for b in range(1, 11):
        pairs(b)

    for b in range(1, 11, 2):
        cols = slice(b * LANES, (b + 2) * LANES)
        value, steep = silu_parts(mm(l1[...], sst[:, cols]))
        sent = mm(l2[...], right_stack(value))
        for i in range(2):
            one = sent[:, i * LANES : (i + 1) * LANES]
            one = one + col[0] + col[1] * jnp.broadcast_to(xs[b + i, 3:4, :], (CHANNELS, LANES))
            sent_all[:, (b + i) * LANES : (b + i + 1) * LANES] = one
            if 3 <= b + i <= 8:
                sent_pair[:, (b + i) * LANES : (b + i + 1) * LANES] = pair_stack(one)
        slope[:, cols] = steep


def force_parts(weights, own_hot, side_hot, kept, dg, pulls, met, acc, held):
    l1, l2, l3, l5, l6, col = weights
    (widx, kinds, geo, bst, bps, bpr, sent_all, sent_pair, slope) = kept
    slot = lax.broadcasted_iota(jnp.int32, (SLOTS, LANES), 0)

    def marks(b, ws):
        if b in SIDE_START:
            start = SIDE_START[b] + (ws[0] - reach(b, 3, 8)[0]) * LANES
            return side_hot.at[start : start + len(ws) * LANES]
        return own_hot.at[b - 4, ws[0] * LANES : (ws[-1] + 1) * LANES]

    def add_rows(sums, first, b, ws, out):
        for i, w in enumerate(ws):
            target = b - 1 + w
            piece = out[i * LANES : (i + 1) * LANES]
            rows = slice((target - first) * LANES, (target - first + 1) * LANES)
            if (first, target) in started:
                sums[rows, :] += piece
            else:
                sums[rows, :] = piece
                started.add((first, target))

    started = set()

    def block_work(b):
        index = widx[b]
        inner, part = index & (LANES - 1), index >> 7
        basis = bst[b]
        radial = mm(l3[...], jnp.concatenate([basis, basis], axis=0))
        if 3 <= b <= 8:
            basis = bps[b]
            steepness = mm(l3[...], jnp.concatenate([basis, basis], axis=0))
        lanes = [jnp.broadcast_to(inner[k : k + 1, :], (16, LANES)) for k in range(SLOTS)]
        parts = [jnp.broadcast_to(part[k : k + 1, :], (16, LANES)) for k in range(SLOTS)]
        own = 4 <= b <= 7
        if own:
            found_all = mm(sent_pair[:, (b - 1) * LANES : (b + 2) * LANES], own_hot[b - 4])
        value = held.at[b % 2]
        total = [jnp.zeros((8, LANES), F32)] * SLOTS
        for u in range(CHANNELS // 16):
            rows = slice(16 * u, 16 * u + 16)
            low_rows = slice(CHANNELS + 16 * u, CHANNELS + 16 * u + 16)
            windows = [sent_all[rows, (b - 1 + w) * LANES : (b + w) * LANES] for w in range(3)]
            got = []
            message = jnp.zeros((16, LANES), F32)
            for k in range(SLOTS):
                cols = slice(k * LANES, (k + 1) * LANES)
                if own:
                    got.append(found_all[rows, cols] + found_all[low_rows, cols])
                else:
                    found = [pick(window, lanes[k]) for window in windows]
                    got.append(jnp.where(parts[k] == 0, found[0], jnp.where(parts[k] == 1, found[1], found[2])))
                message = message + radial[rows, cols] * got[k]
            _, steep = silu_parts(message)
            back = col[3, rows] * steep
            for k in range(SLOTS):
                cols = slice(k * LANES, (k + 1) * LANES)
                high, low = split(radial[rows, cols] * back)
                value[rows, cols] = high.astype(BF16)
                value[low_rows, cols] = low.astype(BF16)
                if 3 <= b <= 8:
                    pull = got[k] * back * steepness[rows, cols]
                    total[k] = total[k] + pull[0:8] + pull[8:16]
            yield
        if 3 <= b <= 8:
            for k in range(SLOTS):
                pulls[b, :, k * LANES : (k + 1) * LANES] = total[k]

    def scatter_work(b):
        ws = reach(b, 3, 8)
        chosen, value = marks(b, ws), held.at[b % 2]
        out = None
        for u in range(4):
            cols = slice(u * 2 * LANES, (u + 1) * 2 * LANES)
            one = mm_nt(chosen[:, cols], value[:, cols])
            out = one if out is None else out + one
            yield
        add_rows(dg, 3, b, ws, out)

    def together(*works):
        works = list(works)
        while works:
            works = [work for work in works if next(work, "end") != "end"]

    together(block_work(2))
    for b in range(3, 10):
        together(scatter_work(b - 1), block_work(b))
    together(scatter_work(9))

    def finish(b, sums):
        kind = kinds[b]
        rows = []
        for k in range(SLOTS):
            cols = slice(k * LANES, (k + 1) * LANES)
            weight = sums[0:8] + wide_row(kind, k) * sums[8:16]
            rows.append(jnp.sum(bpr[b, :, cols] * weight + pulls[b, :, cols], axis=0, keepdims=True))
        pull = jnp.concatenate(rows, axis=0) * geo[b, 3]
        pieces = []
        for c in range(3):
            value = pull * geo[b, c]
            if 4 <= b <= 7:
                acc[b - 4, c] = jnp.sum(value, axis=0, keepdims=True)
            pieces.append(split(value))
        lines = []
        for h in range(2):
            for c in range(3):
                lines.append(jnp.concatenate([jnp.where(slot == k, pieces[c][h], 0.0) for k in range(SLOTS)], axis=1))
        ws = reach(b, 4, 7)
        out = mm_nt(jnp.concatenate(lines, axis=0).astype(BF16), marks(b, ws)[...])
        for c in range(3):
            both = out[8 * c : 8 * c + 8] + out[24 + 8 * c : 32 + 8 * c]
            for i, w in enumerate(ws):
                target = b - 5 + w
                piece = both[:, i * LANES : (i + 1) * LANES]
                if (c, target) in met_blocks:
                    met[target, c] += piece
                else:
                    met[target, c] = piece
                    met_blocks.add((c, target))

    met_blocks = set()

    for b in range(3, 9, 2):
        cols = slice(b * LANES, (b + 2) * LANES)
        high, low = split(dg[(b - 3) * LANES : (b - 1) * LANES, :])
        steep = mm_nt(l5[...], jnp.concatenate([high, low, high], axis=1).astype(BF16))
        steep = steep + jnp.concatenate([col[2], col[2]], axis=1)
        sums = mm(l6[...], right_stack(steep * slope[:, cols]))
        for i in range(2):
            finish(b + i, sums[:, i * LANES : (i + 1) * LANES])

    away = []
    for c in range(3):
        back = [acc[i, c] - jnp.sum(met[i, c], axis=0, keepdims=True) for i in range(SLAB_BLOCKS)]
        away.append(jnp.concatenate(back, axis=1))
    return jnp.concatenate(away, axis=0)


def fill_region(xs, packs, rows_of):
    for b in range(12):
        lanes = slice((b % 4) * LANES, (b % 4 + 1) * LANES)
        pack = packs[b // 4]
        xs[b, 0:3, :] = rows_of(b // 4)[:, lanes]
        xs[b, 3:4, :] = pack[ROW_KIND : ROW_KIND + 1, lanes]


def lane_total(x):
    x = x[:, 0:LANES] + x[:, LANES : 2 * LANES] + x[:, 2 * LANES : 3 * LANES] + x[:, 3 * LANES : 4 * LANES]
    return jnp.sum(x, axis=1, keepdims=True)


def dot3(a, b):
    return jnp.sum(a * b, axis=0, keepdims=True)


def kept_shapes():
    wide = 12 * LANES
    return [
        ((12, 8, LANES), jnp.int32),
        ((12, 8, LANES), F32),
        ((12, 4, 8, LANES), F32),
        ((12, 16, SLOTS * LANES), BF16),
        ((12, 16, SLOTS * LANES), BF16),
        ((12, 8, SLOTS * LANES), F32),
        ((CHANNELS, wide), F32),
        ((2 * CHANNELS, wide), BF16),
        ((CHANNELS, wide), F32),
    ]


def forward_scratch():
    return [pltpu.VMEM((12, 8, LANES), F32), pltpu.VMEM((48, 12 * LANES), BF16)]


def back_scratch():
    return [
        pltpu.VMEM((6 * LANES, 2 * CHANNELS), F32),
        pltpu.VMEM((12, 8, SLOTS * LANES), F32),
        pltpu.VMEM((SLAB_BLOCKS, 3, SLOTS, LANES), F32),
        pltpu.VMEM((SLAB_BLOCKS, 3, 1, LANES), F32),
        pltpu.VMEM((2, 2 * CHANNELS, SLOTS * LANES), BF16),
    ]


def by_parity(sibling, across):
    even = jnp.full(sibling.shape, lax.axis_index("dom") % 2, jnp.int32) == 0
    return jnp.where(even, across, sibling), jnp.where(even, sibling, across)


def first_kernel(sibling_ref, po_ref, across_ref, own_hot, *rest):
    weights, (out_ref, pl_ref, pr_ref, side_hot), scr = rest[:6], rest[6:10], rest[10:]
    xs, sst, kept = scr[0], scr[1], scr[2:11]
    pl_ref[...], pr_ref[...] = by_parity(sibling_ref[...], across_ref[...])
    packs = [pl_ref, po_ref, pr_ref]
    mark_sides(packs, side_hot)
    fill_region(xs, packs, lambda s: packs[s][ROW_X : ROW_X + 3, :])
    forward_parts(packs, weights, xs, sst, kept)
    out_ref[...] = force_parts(weights, own_hot, side_hot, kept, *scr[11:])


def rows_of(ref):
    return jnp.concatenate([ref[c] for c in range(3)], axis=0)


def block_row(*values):
    values = list(values) + [jnp.zeros((1, LANES), F32)] * (SLAB_BLOCKS - len(values))
    return jnp.concatenate(values, axis=1)


def blend_kernel(images, force_ref, po_ref, before_ref, after_ref, out_ref, sums_ref):
    x = po_ref[ROW_X : ROW_X + 3, :]
    v = po_ref[ROW_V : ROW_V + 3, :]
    force = force_ref[...]
    here = lax.axis_index("img")
    before = jnp.where(here > 0, rows_of(before_ref), 0.0)
    after = jnp.where(here < images - 1, rows_of(after_ref), 0.0)
    tangent = after - before
    plus = after - x
    minus = x - before
    sums = jnp.concatenate(
        [
            dot3(force, tangent),
            dot3(force, force),
            dot3(tangent, tangent),
            dot3(plus, plus),
            dot3(minus, minus),
            dot3(v, v),
            jnp.zeros((2, x.shape[1]), F32),
        ],
        axis=0,
    )
    sums = jnp.broadcast_to(lane_total(sums), (8, LANES))
    sums_ref[...] = sums
    out_ref[0:3, :] = force
    out_ref[3:6, :] = tangent
    out_ref[6:7, :] = block_row(*[sums[i : i + 1] for i in range(4)])
    out_ref[7:8, :] = block_row(sums[4:5], sums[5:6])


def step_numbers(ft, ff, tt, pp, mn, vv, dt, alpha, flagged, climbing, inside):
    root = jnp.sqrt(tt + TINY_VALUE)
    along = ft / root
    spring = SPRING_CONSTANT * (jnp.sqrt(pp) - jnp.sqrt(mn))
    factor = jnp.where(climbing, -2.0 * along, spring - along)
    band = jnp.maximum(ff + 2.0 * factor * along + factor * factor * (tt / (tt + TINY_VALUE)), 0.0)
    new_dt = jnp.where(flagged, 0.5 * dt, jnp.minimum(1.1 * dt, STEP_LIMIT))
    pull = jnp.where(flagged, 0.0, alpha * jnp.sqrt(vv / (band + TINY_VALUE))) + new_dt
    keep = jnp.where(flagged, 0.0, 1.0 - alpha)
    new_alpha = jnp.where(flagged, ALPHA_START, 0.99 * alpha)
    keep = jnp.where(inside, keep, 0.0)
    pull = jnp.where(inside, pull, 0.0)
    return (
        jnp.where(inside, along, 0.0),
        jnp.where(inside, spring, 0.0),
        keep,
        pull,
        pull * factor / root,
        new_dt,
        new_alpha,
    )


def add_kernel(a_ref, b_ref, out_ref):
    out_ref[...] = a_ref[...] + b_ref[...]


def number_kernel(dt_ref, flag_ref, climb_ref, out_ref):
    flags = [flag_ref[0, s].astype(F32) for s in range(flag_ref.shape[1])]
    for i, value in enumerate([dt_ref[0], climb_ref[0].astype(F32)] + flags):
        out_ref[i : i + 1, :] = jnp.full((1, LANES), value, F32)


def second_kernel(images, domains, number_ref, pl_ref, po_ref, pr_ref, own_ref, near_ref, far_ref, *rest):
    count = 2 if domains == 4 else 1
    parts, rest = rest[:count], rest[count:]
    (own_hot, side_hot), weights, (out_ref, record_ref), scr = rest[:2], rest[2:8], rest[8:10], rest[10:]
    packs = [pl_ref, po_ref, pr_ref]
    here = lax.axis_index("img")
    sums = parts[0][...]
    if domains == 4:
        sums = sums + parts[1][...]
    got = [sums[i : i + 1, :] for i in range(6)]
    if domains == 4:
        for one in (near_ref, far_ref):
            for i in range(6):
                got[i] = got[i] + one[6 + i // 4 : 7 + i // 4, (i % 4) * LANES : (i % 4 + 1) * LANES]
    ft, ff, tt, pp, mn, vv = got
    beside = by_parity(near_ref[0:6, :], far_ref[0:6, :])
    shape = (1, LANES)
    along, spring, keep, pull, side, dt, alpha = step_numbers(
        ft,
        ff,
        tt,
        pp,
        mn,
        vv,
        number_ref[0:1, :],
        jnp.full(shape, ALPHA_START, F32),
        number_ref[2:3, :] == 1.0,
        number_ref[1:2, :] == jnp.full(shape, here, jnp.int32).astype(F32),
        jnp.full(shape, jnp.where((here >= 1) & (here <= images - 2), 1, 0), jnp.int32) == 1,
    )
    messages = [beside[0], own_ref[0:6, :], beside[1]]

    def wide(s):
        return jnp.concatenate([s] * SLAB_BLOCKS, axis=1)

    speeds = [
        wide(keep) * p[ROW_V : ROW_V + 3, :] + wide(pull) * m[0:3, :] + wide(side) * m[3:6, :]
        for p, m in zip(packs, messages)
    ]
    moved = [p[ROW_X : ROW_X + 3, :] + wide(dt) * s for p, s in zip(packs, speeds)]
    xs, sst, kept = scr[0], scr[1], scr[2:11]
    fill_region(xs, packs, lambda s: moved[s])
    forward_parts(packs, weights, xs, sst, kept)
    force = force_parts(weights, own_hot, side_hot, kept, *scr[11:])
    for c in range(3):
        for i in range(SLAB_BLOCKS):
            lanes = slice(i * LANES, (i + 1) * LANES)
            row = 4 * c + i
            out_ref[0, row : row + 1, :] = speeds[1][c : c + 1, lanes]
            out_ref[0, 12 + row : 13 + row, :] = force[c : c + 1, lanes]
            out_ref[0, 24 + row : 25 + row, :] = moved[1][c : c + 1, lanes]
    out_ref[0, 36:37, :] = dt
    out_ref[0, 37:38, :] = alpha
    out_ref[0, 38:40, :] = jnp.broadcast_to(number_ref[3:4, :], (2, LANES))
    record_ref[0:1, :] = along
    record_ref[1:2, :] = spring
    record_ref[2:3, :] = number_ref[1:2, :]


PRODUCTS = (
    [("f", "t"), ("f", "f"), ("t", "t"), ("p", "p"), ("d", "d"), ("v", "v")]
    + [("d", "v"), ("d", "f"), ("d", "t"), ("d", "V"), ("d", "F"), ("d", "T"), ("v", "f"), ("v", "t")]
    + [(a, b) for a in "vft" for b in "VFT"]
)


def gram_kernel(images, *refs):
    parts, after_ref, (out_ref, state_ref, messages_ref) = refs[:-4], refs[-4], refs[-3:]
    rows = out_ref.shape[0]
    here = lax.axis_index("img")
    if images == 4:
        places = [here, lax.rem(here + 3, 4), jnp.where(here < 2, 3 - here, here - 2)]
        messages_ref[...] = jnp.zeros(messages_ref.shape, F32)
        follower = lax.rem(here + 1, 4)
        for c in range(3):
            for i in range(SLAB_BLOCKS):
                row = 24 + 4 * c + i
                messages_ref[follower, row : row + 1, :] = after_ref[c][:, i * LANES : (i + 1) * LANES]
    else:
        places = [lax.rem(here + images - s, images) for s in range(images)]
    for place, part in zip(places, parts):
        messages_ref[place] = part[0]
    blank = [jnp.zeros((rows - images, LANES), F32)] if rows > images else []
    zero = jnp.zeros((1, LANES), F32)

    def gathered(row):
        return jnp.concatenate([messages_ref[i, row : row + 1, :] for i in range(images)] + blank, axis=0)

    def earlier(value):
        return jnp.concatenate([zero, value[0 : rows - 1]], axis=0)

    def later(value):
        return jnp.concatenate([value[1:images], zero] + blank, axis=0)

    number = lax.broadcasted_iota(jnp.int32, (rows, LANES), 0)
    held = number < images
    totals = [jnp.zeros((rows, LANES), F32) for _ in PRODUCTS]
    for row in range(3 * SLAB_BLOCKS):
        v, f, x = gathered(row), gathered(12 + row), gathered(24 + row)
        before = jnp.where(held, earlier(x), 0.0)
        after = later(x)
        t = after - before
        table = {"f": f, "v": v, "t": t, "p": after - x, "d": x - before}
        table["F"], table["V"], table["T"] = earlier(f), earlier(v), earlier(t)
        totals = [old + table[a] * table[b] for old, (a, b) in zip(totals, PRODUCTS)]
        state_ref[row : row + 1, :] = jnp.sum(jnp.where(number == here, t, 0.0), axis=0, keepdims=True)
    lane = lax.broadcasted_iota(jnp.int32, (rows, LANES), 1)
    result = jnp.zeros((rows, LANES), F32)
    for q, one in enumerate(totals):
        one = jnp.broadcast_to(jnp.sum(one, axis=1, keepdims=True), (rows, LANES))
        result = jnp.where(lane == q, one, result)
    out_ref[...] = result
    for i in range(3):
        state_ref[16 + rows * i : 16 + rows * (i + 1), :] = gathered(36 + i)


def final_kernel(images, atoms, own_ref, record_ref, state_ref, *rest):
    parts, (x_ref, v_ref, band_ref, path_ref) = rest[:-4], rest[-4:]
    rows = parts[0].shape[0]
    here = lax.axis_index("img")
    sums = parts[0][...]
    for one in parts[1:]:
        sums = sums + one[...]
    got = {
        pair: jnp.broadcast_to(sums[:, q : q + 1], (rows, LANES)) for q, pair in enumerate(PRODUCTS)
    }
    number = lax.broadcasted_iota(jnp.int32, (rows, LANES), 0)
    inside = (number >= 1) & (number <= images - 2)
    climb = jnp.broadcast_to(record_ref[2:3, :], (rows, LANES))
    dt0, alpha0, flag = (state_ref[16 + rows * i : 16 + rows * (i + 1), :] for i in range(3))
    along, spring, keep, pull, side, dt, _ = step_numbers(
        got["f", "t"],
        got["f", "f"],
        got["t", "t"],
        got["p", "p"],
        got["d", "d"],
        got["v", "v"],
        dt0,
        alpha0,
        flag == 1.0,
        number.astype(F32) == climb,
        inside,
    )

    def shifted(value):
        return jnp.concatenate([jnp.zeros((1, LANES), F32), value[0 : rows - 1]], axis=0)

    now = {"v": dt * keep, "f": dt * pull, "t": dt * side}
    old = {a.upper(): shifted(value) for a, value in now.items()}
    mine = now["v"] * now["v"] * got["v", "v"] + now["f"] * now["f"] * got["f", "f"]
    mine = mine + now["t"] * now["t"] * got["t", "t"]
    cross = now["v"] * now["f"] * got["v", "f"] + now["v"] * now["t"] * got["v", "t"]
    mine = mine + 2.0 * (cross + now["f"] * now["t"] * got["f", "t"])
    both = jnp.zeros((rows, LANES), F32)
    for a in "vft":
        both = both + now[a] * got["d", a]
    for b in "VFT":
        both = both - old[b] * got["d", b]
    for a in "vft":
        for b in "VFT":
            both = both - now[a] * old[b] * got[a, b]
    squared = got["d", "d"] + mine + shifted(mine) + 2.0 * both
    segment = jnp.sqrt(jnp.maximum(squared, 0.0) * (1.0 / (3.0 * atoms)))
    path = jnp.sum(jnp.where(number <= here, segment, 0.0), axis=0, keepdims=True)
    path_ref[...] = path[:, 0:1]
    keep, pull, side, dt, along, spring = (
        jnp.sum(jnp.where(number == here, value, 0.0), axis=0, keepdims=True)
        for value in (keep, pull, side, dt, along, spring)
    )

    for c in range(3):
        speeds, places = [], []
        for i in range(SLAB_BLOCKS):
            row = 4 * c + i
            speed = keep * own_ref[0, row : row + 1, :] + pull * own_ref[0, 12 + row : 13 + row, :]
            speed = speed + side * state_ref[row : row + 1, :]
            speeds.append(speed)
            places.append(own_ref[0, 24 + row : 25 + row, :] + dt * speed)
        v_ref[c] = jnp.concatenate(speeds, axis=1)
        x_ref[c] = jnp.concatenate(places, axis=1)
    band_ref[0] = jnp.concatenate([record_ref[0:1, 0:1], record_ref[1:2, 0:1]], axis=1)
    band_ref[1] = jnp.concatenate([along[:, 0:1], spring[:, 0:1]], axis=1)


VMEM_SPEC = pl.BlockSpec(memory_space=pltpu.VMEM)
SMEM_SPEC = pl.BlockSpec(memory_space=pltpu.SMEM)
HBM_SPEC = pl.BlockSpec(memory_space=pltpu.HBM)


def call(body, outs, scalars, arrays, scratch_shapes=(), flops=0, spec=VMEM_SPEC, vmem=24):
    return pl.pallas_call(
        body,
        out_shape=outs,
        in_specs=[SMEM_SPEC] * len(scalars) + [spec] * len(arrays),
        out_specs=jax.tree.map(lambda _: VMEM_SPEC, outs),
        scratch_shapes=list(scratch_shapes),
        compiler_params=pltpu.CompilerParams(vmem_limit_bytes=vmem * 1024 * 1024),
        cost_estimate=pl.CostEstimate(flops=flops, bytes_accessed=1 << 18, transcendentals=0),
    )(*scalars, *arrays)


def swap(array, axis, partner):
    return lax.ppermute(array, axis, [(i, partner(i)) for i in range(lax.axis_size(axis))])


def exchanged(sums, axis):
    count = lax.axis_size(axis)
    if count == 4:
        return [sums] + [swap(sums, axis, lambda i, by=by: i ^ by) for by in (2, 3, 1)]
    distance = 1
    while distance < count:
        more = swap(sums, axis, lambda i, by=distance: i ^ by)
        sums = call(add_kernel, jax.ShapeDtypeStruct(sums.shape, F32), (), (sums, more))
        distance *= 2
    return [sums]


def collected(state, axis, after):
    count = lax.axis_size(axis)
    if count == 4:
        return [state, swap(state, axis, lambda i: (i + 1) % 4), swap(state, axis, lambda i: (2, 3, 1, 0)[i]), after]
    return [state] + [swap(state, axis, lambda i, by=by: (i + by) % count) for by in range(1, count)] + [after]


def local(
    disp,
    veloc,
    time_step,
    reset_flags,
    climb,
    species,
    neighbours,
    counts,
    lattice,
    embed,
    radial_weight,
    mix_weight,
    update_weight,
    readout,
):
    atoms = disp.shape[2]
    images = lax.axis_size("img")
    domains = lax.axis_size("dom")
    assert disp.shape[0] == 1 and atoms == SLAB_BLOCKS * LANES and domains >= 4
    assert domains & (domains - 1) == 0 and images & (images - 1) == 0
    shape = jax.ShapeDtypeStruct
    x = jnp.transpose(disp, (1, 0, 2))
    v = jnp.transpose(veloc, (1, 0, 2))
    small = (x, v, species, neighbours, counts, embed, readout, radial_weight, mix_weight, update_weight)
    sent, kept_pack = call(
        pack_kernel,
        (shape((PACK_ROWS, atoms), F32), shape((OWN_ROWS, atoms), F32)),
        (),
        (*small, jnp.transpose(lattice, (1, 0, 2))),
        [pltpu.VMEM(a.shape, a.dtype) for a in small] + [pltpu.SemaphoreType.DMA((16,))],
        spec=HBM_SPEC,
        vmem=63,
    )
    sibling = swap(sent, "dom", lambda i: i ^ 1)
    across = swap(sent, "dom", lambda i: (i + 2 * (i % 2) - 1) % domains)
    own_hot, *weights, x_copy, pack = call(
        prepare_kernel,
        (
            shape((SLAB_BLOCKS, 3 * LANES, SLOTS * LANES), BF16),
            shape((CHANNELS, 48), BF16),
            shape((CHANNELS, 192), BF16),
            shape((CHANNELS, 32), BF16),
            shape((CHANNELS, 3 * LANES), BF16),
            shape((16, 192), BF16),
            shape((4, CHANNELS, LANES), F32),
            shape(x.shape, F32),
            shape(sent.shape, F32),
        ),
        (),
        (kept_pack,),
        flops=100000000,
    )
    before = swap(x_copy, "img", lambda i: (i + 1) % images)
    after = swap(x_copy, "img", lambda i: (i - 1) % images)
    force_scratch = forward_scratch() + [pltpu.VMEM(*one) for one in kept_shapes()] + back_scratch()
    force, left, right, side_hot = call(
        first_kernel,
        (
            shape((3, atoms), F32),
            shape(sent.shape, F32),
            shape(sent.shape, F32),
            shape((SIDE_ROWS, SLOTS * LANES), BF16),
        ),
        (),
        (sibling, pack, across, own_hot, *weights),
        force_scratch,
        flops=1000000000,
    )
    message, sums = call(
        functools.partial(blend_kernel, images),
        (shape((8, atoms), F32), shape((8, LANES), F32)),
        (),
        (force, pack, before, after),
    )
    far = swap(message, "dom", lambda i: (i + 2 * (i % 2) - 1) % domains)
    if domains == 4:
        parts = [sums, swap(sums, "dom", lambda i: i ^ 2)]
    else:
        parts = exchanged(sums, "dom")
    near = swap(message, "dom", lambda i: i ^ 1)
    numbers = call(number_kernel, shape((8, LANES), F32), (time_step, jnp.transpose(reset_flags), climb), ())
    state, record = call(
        functools.partial(second_kernel, images, domains),
        (shape((1, 40, LANES), F32), shape((3, LANES), F32)),
        (),
        (numbers, left, pack, right, message, near, far, *parts, own_hot, side_hot, *weights),
        force_scratch,
        flops=1000000000,
    )
    rows = 8 * ((images + 7) // 8)
    sums, extra = call(
        functools.partial(gram_kernel, images),
        (shape((rows, LANES), F32), shape((16 + 3 * rows, LANES), F32)),
        (),
        collected(state, "img", after),
        [pltpu.VMEM((images, 40, LANES), F32)],
    )
    new_x, new_v, records, path = call(
        functools.partial(final_kernel, images, atoms * domains),
        (shape(x.shape, F32), shape(x.shape, F32), shape((2, 1, 2), F32), shape((1, 1), F32)),
        (),
        (state, record, extra, *exchanged(sums, "dom")),
    )
    return (
        jnp.transpose(new_x, (1, 0, 2)),
        jnp.transpose(new_v, (1, 0, 2)),
        jnp.transpose(records, (0, 2, 1)),
        path.reshape(1),
    )


def solution(mesh):
    in_specs = (
        P(("group", "img"), None, "dom"),
        P(("group", "img"), None, "dom"),
        P(("group", "img")),
        P(None, ("group", "img")),
        P("group"),
        P(("group", "dom")),
        P(None, ("group", "dom")),
        P(("group", "dom")),
        P(None, None, ("group", "dom")),
        P(),
        P(),
        P(),
        P(),
        P(),
    )
    out_specs = (
        P(("group", "img"), None, "dom"),
        P(("group", "img"), None, "dom"),
        P(None, None, ("group", "img")),
        P(("group", "img")),
    )
    return jax.shard_map(local, mesh=mesh, in_specs=in_specs, out_specs=out_specs, check_vma=False)
```

```python
import functools
import math

import jax
import jax.numpy as jnp
from jax import lax
from jax.experimental import pallas as pl
from jax.experimental.pallas import tpu as pltpu
from jax.sharding import PartitionSpec as P

F32 = jnp.float32
BF16 = jnp.bfloat16
PRECISE = lax.Precision.HIGHEST
SPRING_CONSTANT = 0.5
ALPHA_START = 0.1
STEP_LIMIT = 0.3
TINY_VALUE = 1e-06
SOFTENING = 0.25
LANES = 128
SLOTS = 8
BASIS = 8
CHANNELS = 64
SLAB_BLOCKS = 4
ROW_X = 32
ROW_COUNT = 35
ROW_KIND = 36
ROW_V = 37
PACK_ROWS = 40
OWN_ROWS = PACK_ROWS + CHANNELS + BASIS
NT = (((1,), (1,)), ((), ()))


def split(x):
    high = x.astype(BF16).astype(F32)
    return high, x - high


def left_stack(w):
    high, low = split(w)
    return jnp.concatenate([high, high, low], axis=1)


def right_stack(x):
    high, low = split(x)
    high = high.astype(BF16)
    return jnp.concatenate([high, low.astype(BF16), high], axis=0)


def pair_stack(x):
    high, low = split(x)
    return jnp.concatenate([high.astype(BF16), low.astype(BF16)], axis=0)


def mm(a, b):
    return jnp.dot(a, b, preferred_element_type=F32)


def mm_nt(a, b):
    return lax.dot_general(a, b, NT, preferred_element_type=F32)


def pack_kernel(*refs):
    sources, (out_ref, own_ref), held, sems = refs[:11], refs[11:13], refs[13:23], refs[23]
    lattice = sources[10]
    pairs = list(zip(sources, held))
    for c in range(3):
        rows = pl.ds(8 + 8 * c, 8)
        pairs += [(lattice.at[c], out_ref.at[rows]), (lattice.at[c], own_ref.at[rows])]
    copies = [pltpu.make_async_copy(a, b, sems.at[i]) for i, (a, b) in enumerate(pairs)]
    for one in copies:
        one.start()
    for one in copies:
        one.wait()
    x, v, species, nbr, counts, embed, readout, radial, mix, update = held
    for ref in (out_ref, own_ref):
        ref[0:8, :] = nbr[...].astype(F32)
        for c in range(3):
            ref[ROW_X + c : ROW_X + c + 1, :] = x[c]
            ref[ROW_V + c : ROW_V + c + 1, :] = v[c]
        ref[ROW_COUNT : ROW_COUNT + 1, :] = counts[...].astype(F32).reshape(1, -1)
        ref[ROW_KIND : ROW_KIND + 1, :] = species[...].astype(F32).reshape(1, -1)
    top, low = PACK_ROWS, PACK_ROWS + CHANNELS
    for i, value in enumerate([mix[0], mix[1], update[0], update[1]]):
        own_ref[top:low, i * LANES : i * LANES + CHANNELS] = value
    for i, value in enumerate([radial[0], radial[1], embed[...], readout[...].reshape(1, CHANNELS)]):
        own_ref[low : low + value.shape[0], i * LANES : i * LANES + CHANNELS] = value


def prepare_kernel(po_ref, *rest):
    own_hot, l1_ref, l2_ref, l3_ref, l5_ref, l6_ref, col_ref, copy_ref, pack_ref = rest
    pack_ref[...] = po_ref[0:PACK_ROWS, :]
    for b in range(SLAB_BLOCKS):
        mark(window_index(po_ref, b), [0, 1, 2], own_hot.at[b])
    for c in range(3):
        copy_ref[c] = po_ref[ROW_X + c : ROW_X + c + 1, :]

    def raw(first, count, i):
        return po_ref[first : first + count, i * LANES : i * LANES + CHANNELS]

    low = PACK_ROWS + CHANNELS
    mix_ref = [raw(PACK_ROWS, CHANNELS, i) for i in range(2)]
    update_ref = [raw(PACK_ROWS, CHANNELS, 2 + i) for i in range(2)]
    radial_ref = [raw(low, BASIS, i) for i in range(2)]
    embed_ref, readout = raw(low, 2, 2), raw(low, 1, 3)
    eye = (
        lax.broadcasted_iota(jnp.int32, (CHANNELS, CHANNELS), 0)
        == lax.broadcasted_iota(jnp.int32, (CHANNELS, CHANNELS), 1)
    ).astype(F32)

    def turned(x):
        return lax.dot_general(eye, x, NT, precision=PRECISE, preferred_element_type=F32)

    base0 = embed_ref[0:1, :]
    base1 = embed_ref[1:2, :] - base0
    rows = jnp.concatenate([base0, base1], axis=0)
    sent = jnp.dot(rows, mix_ref[0], precision=PRECISE, preferred_element_type=F32)
    scale = 1.0 / math.sqrt(SLOTS)
    first = jnp.concatenate([radial_ref[0] * sent[0:1], radial_ref[0] * sent[1:2]], axis=0) * scale
    second = radial_ref[1] * scale
    folded = jnp.dot(update_ref[0], mix_ref[1], precision=PRECISE, preferred_element_type=F32)
    mix_t = turned(mix_ref[1])
    l1_ref[...] = left_stack(turned(first)).astype(BF16)
    l2_ref[...] = left_stack(turned(folded)).astype(BF16)
    high, low = split(turned(second))
    l3_ref[...] = jnp.concatenate([high, high, low, jnp.zeros_like(high)], axis=1).astype(BF16)
    high, low = split(folded)
    l5_ref[...] = jnp.concatenate([high, high, high, high, low, low], axis=1).astype(BF16)
    l6_ref[...] = left_stack(first).astype(BF16)
    wide = (CHANNELS, LANES)
    col_ref[0] = jnp.broadcast_to(jnp.sum(mix_t * base0, axis=1, keepdims=True), wide)
    col_ref[1] = jnp.broadcast_to(jnp.sum(mix_t * base1, axis=1, keepdims=True), wide)
    col_ref[2] = jnp.broadcast_to(jnp.sum(update_ref[0] * readout, axis=1, keepdims=True), wide)
    col_ref[3] = jnp.broadcast_to(jnp.sum(update_ref[1] * readout, axis=1, keepdims=True), wide)


def sin_cos(t):
    q = t * t
    s = -1.0 / 39916800.0
    for c in (1.0 / 362880.0, -1.0 / 5040.0, 1.0 / 120.0, -1.0 / 6.0, 1.0):
        s = s * q + c
    k = 1.0 / 479001600.0
    for c in (-1.0 / 3628800.0, 1.0 / 40320.0, -1.0 / 720.0, 1.0 / 24.0, -0.5, 1.0):
        k = k * q + c
    return s * t, k


def wide_row(x, row):
    return jnp.broadcast_to(x[row : row + 1, :], (8, x.shape[1]))


def silu_parts(m):
    sig = 1.0 / (1.0 + jnp.exp(-m))
    return m * sig, sig * (1.0 + m * (1.0 - sig))


def pick(values, lanes):
    return jnp.take_along_axis(values, lanes, axis=1, mode="promise_in_bounds")


def reach(b, first, last):
    return [w for w in range(3) if first <= b - 1 + w <= last]


SIDE_START = {2: 0, 3: LANES, 8: 3 * LANES, 9: 5 * LANES}
SIDE_ROWS = 6 * LANES


def mark(index, ws, target):
    count = len(ws) * LANES
    row_id = (lax.broadcasted_iota(jnp.int32, (count, LANES), 0) + ws[0] * LANES).astype(jnp.int16)
    one, zero = jnp.ones((count, LANES), BF16), jnp.zeros((count, LANES), BF16)
    for k in range(SLOTS):
        wanted = jnp.broadcast_to(index[k : k + 1, :], (16, LANES)).astype(jnp.int16)
        wanted = jnp.concatenate([wanted] * (count // 16), axis=0)
        target[:, k * LANES : (k + 1) * LANES] = jnp.where(row_id == wanted, one, zero)


def window_index(pack, b):
    lanes = slice((b % 4) * LANES, (b % 4 + 1) * LANES)
    return pack[0:8, lanes].astype(jnp.int32) - LANES * (b % 4)


def mark_sides(packs, side):
    for b, start in SIDE_START.items():
        ws = reach(b, 3, 8)
        mark(window_index(packs[b // 4], b), ws, side.at[start : start + len(ws) * LANES])


def forward_parts(packs, weights, xs, sst, kept):
    l1, l2, l3, l5, l6, col = weights
    (widx, kinds, geo, bst, bps, bpr, sent_all, sent_pair, slope) = kept
    centre = 2.0 + 0.5 * lax.broadcasted_iota(jnp.int32, (BASIS, LANES), 0).astype(F32)
    slot = lax.broadcasted_iota(jnp.int32, (SLOTS, LANES), 0)

    def part_rows(value):
        high, low = split(value)
        return jnp.concatenate([high, low], axis=0).astype(BF16)

    def pairs(b):
        pack = packs[b // 4]
        lanes = slice((b % 4) * LANES, (b % 4 + 1) * LANES)
        index = window_index(pack, b)
        widx[b] = index
        inner = index & (LANES - 1)
        part = index >> 7

        def taken(row):
            got = [
                pick(jnp.broadcast_to(xs[b - 1 + w, row : row + 1, :], (SLOTS, LANES)), inner)
                for w in range(3)
            ]
            return jnp.where(part == 0, got[0], jnp.where(part == 1, got[1], got[2]))

        vec = [
            pack[8 + 8 * c : 16 + 8 * c, lanes] + taken(c) - jnp.broadcast_to(xs[b, c : c + 1, :], (SLOTS, LANES))
            for c in range(3)
        ]
        kind = taken(3)
        dist = jnp.sqrt(vec[0] * vec[0] + vec[1] * vec[1] + vec[2] * vec[2] + SOFTENING)
        live = (slot.astype(F32) < jnp.broadcast_to(pack[ROW_COUNT : ROW_COUNT + 1, lanes], (SLOTS, LANES))).astype(F32)
        turns = dist * (1.0 / 12.0)
        turns = turns - jnp.floor(turns + 0.5)
        sine, cosine = sin_cos(turns * math.pi)
        envelope = cosine * cosine * live
        slant = cosine * sine * live * (-math.pi / 6.0)
        if 3 <= b <= 8:
            kinds[b] = kind
            for c in range(3):
                geo[b, c] = vec[c]
            geo[b, 3] = 1.0 / dist
        total = jnp.zeros((BASIS, LANES), F32)
        total_kind = jnp.zeros((BASIS, LANES), F32)
        for k in range(SLOTS):
            away = wide_row(dist, k) - centre
            gauss = jnp.exp(-4.0 * (away * away))
            env_k = wide_row(envelope, k)
            value = gauss * env_k
            total = total + value
            total_kind = total_kind + value * wide_row(kind, k)
            cols = slice(k * LANES, (k + 1) * LANES)
            if 2 <= b <= 9:
                bst[b, :, cols] = part_rows(value)
            if 3 <= b <= 8:
                value = gauss * (wide_row(slant, k) - 8.0 * away * env_k)
                bpr[b, :, cols] = value
                bps[b, :, cols] = part_rows(value)
        high, low = split(jnp.concatenate([total, total_kind], axis=0))
        sst[:, b * LANES : (b + 1) * LANES] = jnp.concatenate([high, low, high], axis=0).astype(BF16)

    for b in range(1, 11):
        pairs(b)

    for b in range(1, 11, 2):
        cols = slice(b * LANES, (b + 2) * LANES)
        value, steep = silu_parts(mm(l1[...], sst[:, cols]))
        sent = mm(l2[...], right_stack(value))
        for i in range(2):
            one = sent[:, i * LANES : (i + 1) * LANES]
            one = one + col[0] + col[1] * jnp.broadcast_to(xs[b + i, 3:4, :], (CHANNELS, LANES))
            sent_all[:, (b + i) * LANES : (b + i + 1) * LANES] = one
            if 3 <= b + i <= 8:
                sent_pair[:, (b + i) * LANES : (b + i + 1) * LANES] = pair_stack(one)
        slope[:, cols] = steep


def force_parts(weights, own_hot, side_hot, kept, dg, pulls, met, acc, held):
    l1, l2, l3, l5, l6, col = weights
    (widx, kinds, geo, bst, bps, bpr, sent_all, sent_pair, slope) = kept
    slot = lax.broadcasted_iota(jnp.int32, (SLOTS, LANES), 0)

    def marks(b, ws):
        if b in SIDE_START:
            start = SIDE_START[b] + (ws[0] - reach(b, 3, 8)[0]) * LANES
            return side_hot.at[start : start + len(ws) * LANES]
        return own_hot.at[b - 4, ws[0] * LANES : (ws[-1] + 1) * LANES]

    def add_rows(sums, first, b, ws, out):
        for i, w in enumerate(ws):
            target = b - 1 + w
            piece = out[i * LANES : (i + 1) * LANES]
            rows = slice((target - first) * LANES, (target - first + 1) * LANES)
            if (first, target) in started:
                sums[rows, :] += piece
            else:
                sums[rows, :] = piece
                started.add((first, target))

    started = set()

    def block_work(b):
        index = widx[b]
        inner, part = index & (LANES - 1), index >> 7
        basis = bst[b]
        radial = mm(l3[...], jnp.concatenate([basis, basis], axis=0))
        if 3 <= b <= 8:
            basis = bps[b]
            steepness = mm(l3[...], jnp.concatenate([basis, basis], axis=0))
        lanes = [jnp.broadcast_to(inner[k : k + 1, :], (16, LANES)) for k in range(SLOTS)]
        parts = [jnp.broadcast_to(part[k : k + 1, :], (16, LANES)) for k in range(SLOTS)]
        own = 4 <= b <= 7
        if own:
            found_all = mm(sent_pair[:, (b - 1) * LANES : (b + 2) * LANES], own_hot[b - 4])
        value = held.at[b % 2]
        total = [jnp.zeros((8, LANES), F32)] * SLOTS
        for u in range(CHANNELS // 16):
            rows = slice(16 * u, 16 * u + 16)
            low_rows = slice(CHANNELS + 16 * u, CHANNELS + 16 * u + 16)
            windows = [sent_all[rows, (b - 1 + w) * LANES : (b + w) * LANES] for w in range(3)]
            got = []
            message = jnp.zeros((16, LANES), F32)
            for k in range(SLOTS):
                cols = slice(k * LANES, (k + 1) * LANES)
                if own:
                    got.append(found_all[rows, cols] + found_all[low_rows, cols])
                else:
                    found = [pick(window, lanes[k]) for window in windows]
                    got.append(jnp.where(parts[k] == 0, found[0], jnp.where(parts[k] == 1, found[1], found[2])))
                message = message + radial[rows, cols] * got[k]
            _, steep = silu_parts(message)
            back = col[3, rows] * steep
            for k in range(SLOTS):
                cols = slice(k * LANES, (k + 1) * LANES)
                high, low = split(radial[rows, cols] * back)
                value[rows, cols] = high.astype(BF16)
                value[low_rows, cols] = low.astype(BF16)
                if 3 <= b <= 8:
                    pull = got[k] * back * steepness[rows, cols]
                    total[k] = total[k] + pull[0:8] + pull[8:16]
            yield
        if 3 <= b <= 8:
            for k in range(SLOTS):
                pulls[b, :, k * LANES : (k + 1) * LANES] = total[k]

    def scatter_work(b):
        ws = reach(b, 3, 8)
        chosen, value = marks(b, ws), held.at[b % 2]
        out = None
        for u in range(4):
            cols = slice(u * 2 * LANES, (u + 1) * 2 * LANES)
            one = mm_nt(chosen[:, cols], value[:, cols])
            out = one if out is None else out + one
            yield
        add_rows(dg, 3, b, ws, out)

    def together(*works):
        works = list(works)
        while works:
            works = [work for work in works if next(work, "end") != "end"]

    together(block_work(2))
    for b in range(3, 10):
        together(scatter_work(b - 1), block_work(b))
    together(scatter_work(9))

    def finish(b, sums):
        kind = kinds[b]
        rows = []
        for k in range(SLOTS):
            cols = slice(k * LANES, (k + 1) * LANES)
            weight = sums[0:8] + wide_row(kind, k) * sums[8:16]
            rows.append(jnp.sum(bpr[b, :, cols] * weight + pulls[b, :, cols], axis=0, keepdims=True))
        pull = jnp.concatenate(rows, axis=0) * geo[b, 3]
        pieces = []
        for c in range(3):
            value = pull * geo[b, c]
            if 4 <= b <= 7:
                acc[b - 4, c] = jnp.sum(value, axis=0, keepdims=True)
            pieces.append(split(value))
        lines = []
        for h in range(2):
            for c in range(3):
                lines.append(jnp.concatenate([jnp.where(slot == k, pieces[c][h], 0.0) for k in range(SLOTS)], axis=1))
        ws = reach(b, 4, 7)
        out = mm_nt(jnp.concatenate(lines, axis=0).astype(BF16), marks(b, ws)[...])
        for c in range(3):
            both = out[8 * c : 8 * c + 8] + out[24 + 8 * c : 32 + 8 * c]
            for i, w in enumerate(ws):
                target = b - 5 + w
                piece = both[:, i * LANES : (i + 1) * LANES]
                if (c, target) in met_blocks:
                    met[target, c] += piece
                else:
                    met[target, c] = piece
                    met_blocks.add((c, target))

    met_blocks = set()

    for b in range(3, 9, 2):
        cols = slice(b * LANES, (b + 2) * LANES)
        high, low = split(dg[(b - 3) * LANES : (b - 1) * LANES, :])
        steep = mm_nt(l5[...], jnp.concatenate([high, low, high], axis=1).astype(BF16))
        steep = steep + jnp.concatenate([col[2], col[2]], axis=1)
        sums = mm(l6[...], right_stack(steep * slope[:, cols]))
        for i in range(2):
            finish(b + i, sums[:, i * LANES : (i + 1) * LANES])

    away = []
    for c in range(3):
        back = [acc[i, c] - jnp.sum(met[i, c], axis=0, keepdims=True) for i in range(SLAB_BLOCKS)]
        away.append(jnp.concatenate(back, axis=1))
    return jnp.concatenate(away, axis=0)


def fill_region(xs, packs, rows_of):
    for b in range(12):
        lanes = slice((b % 4) * LANES, (b % 4 + 1) * LANES)
        pack = packs[b // 4]
        xs[b, 0:3, :] = rows_of(b // 4)[:, lanes]
        xs[b, 3:4, :] = pack[ROW_KIND : ROW_KIND + 1, lanes]


def lane_total(x):
    x = x[:, 0:LANES] + x[:, LANES : 2 * LANES] + x[:, 2 * LANES : 3 * LANES] + x[:, 3 * LANES : 4 * LANES]
    return jnp.sum(x, axis=1, keepdims=True)


def dot3(a, b):
    return jnp.sum(a * b, axis=0, keepdims=True)


def kept_shapes():
    wide = 12 * LANES
    return [
        ((12, 8, LANES), jnp.int32),
        ((12, 8, LANES), F32),
        ((12, 4, 8, LANES), F32),
        ((12, 16, SLOTS * LANES), BF16),
        ((12, 16, SLOTS * LANES), BF16),
        ((12, 8, SLOTS * LANES), F32),
        ((CHANNELS, wide), F32),
        ((2 * CHANNELS, wide), BF16),
        ((CHANNELS, wide), F32),
    ]


def forward_scratch():
    return [pltpu.VMEM((12, 8, LANES), F32), pltpu.VMEM((48, 12 * LANES), BF16)]


def back_scratch():
    return [
        pltpu.VMEM((6 * LANES, 2 * CHANNELS), F32),
        pltpu.VMEM((12, 8, SLOTS * LANES), F32),
        pltpu.VMEM((SLAB_BLOCKS, 3, SLOTS, LANES), F32),
        pltpu.VMEM((SLAB_BLOCKS, 3, 1, LANES), F32),
        pltpu.VMEM((2, 2 * CHANNELS, SLOTS * LANES), BF16),
    ]


def by_parity(sibling, across):
    even = jnp.full(sibling.shape, lax.axis_index("dom") % 2, jnp.int32) == 0
    return jnp.where(even, across, sibling), jnp.where(even, sibling, across)


def first_kernel(sibling_ref, po_ref, across_ref, own_hot, *rest):
    weights, (out_ref, pl_ref, pr_ref, side_hot), scr = rest[:6], rest[6:10], rest[10:]
    xs, sst, kept = scr[0], scr[1], scr[2:11]
    pl_ref[...], pr_ref[...] = by_parity(sibling_ref[...], across_ref[...])
    packs = [pl_ref, po_ref, pr_ref]
    mark_sides(packs, side_hot)
    fill_region(xs, packs, lambda s: packs[s][ROW_X : ROW_X + 3, :])
    forward_parts(packs, weights, xs, sst, kept)
    out_ref[...] = force_parts(weights, own_hot, side_hot, kept, *scr[11:])


def rows_of(ref):
    return jnp.concatenate([ref[c] for c in range(3)], axis=0)


def block_row(*values):
    values = list(values) + [jnp.zeros((1, LANES), F32)] * (SLAB_BLOCKS - len(values))
    return jnp.concatenate(values, axis=1)


def blend_kernel(images, force_ref, po_ref, before_ref, after_ref, out_ref, sums_ref):
    x = po_ref[ROW_X : ROW_X + 3, :]
    v = po_ref[ROW_V : ROW_V + 3, :]
    force = force_ref[...]
    here = lax.axis_index("img")
    before = jnp.where(here > 0, rows_of(before_ref), 0.0)
    after = jnp.where(here < images - 1, rows_of(after_ref), 0.0)
    tangent = after - before
    plus = after - x
    minus = x - before
    sums = jnp.concatenate(
        [
            dot3(force, tangent),
            dot3(force, force),
            dot3(tangent, tangent),
            dot3(plus, plus),
            dot3(minus, minus),
            dot3(v, v),
            jnp.zeros((2, x.shape[1]), F32),
        ],
        axis=0,
    )
    sums = jnp.broadcast_to(lane_total(sums), (8, LANES))
    sums_ref[...] = sums
    out_ref[0:3, :] = force
    out_ref[3:6, :] = tangent
    out_ref[6:7, :] = block_row(*[sums[i : i + 1] for i in range(4)])
    out_ref[7:8, :] = block_row(sums[4:5], sums[5:6])


def step_numbers(ft, ff, tt, pp, mn, vv, dt, alpha, flagged, climbing, inside):
    root = jnp.sqrt(tt + TINY_VALUE)
    along = ft / root
    spring = SPRING_CONSTANT * (jnp.sqrt(pp) - jnp.sqrt(mn))
    factor = jnp.where(climbing, -2.0 * along, spring - along)
    band = jnp.maximum(ff + 2.0 * factor * along + factor * factor * (tt / (tt + TINY_VALUE)), 0.0)
    new_dt = jnp.where(flagged, 0.5 * dt, jnp.minimum(1.1 * dt, STEP_LIMIT))
    pull = jnp.where(flagged, 0.0, alpha * jnp.sqrt(vv / (band + TINY_VALUE))) + new_dt
    keep = jnp.where(flagged, 0.0, 1.0 - alpha)
    new_alpha = jnp.where(flagged, ALPHA_START, 0.99 * alpha)
    keep = jnp.where(inside, keep, 0.0)
    pull = jnp.where(inside, pull, 0.0)
    return (
        jnp.where(inside, along, 0.0),
        jnp.where(inside, spring, 0.0),
        keep,
        pull,
        pull * factor / root,
        new_dt,
        new_alpha,
    )


def add_kernel(a_ref, b_ref, out_ref):
    out_ref[...] = a_ref[...] + b_ref[...]


def number_kernel(dt_ref, flag_ref, climb_ref, out_ref):
    flags = [flag_ref[0, s].astype(F32) for s in range(flag_ref.shape[1])]
    for i, value in enumerate([dt_ref[0], climb_ref[0].astype(F32)] + flags):
        out_ref[i : i + 1, :] = jnp.full((1, LANES), value, F32)


def second_kernel(images, domains, number_ref, pl_ref, po_ref, pr_ref, own_ref, near_ref, far_ref, *rest):
    count = 2 if domains == 4 else 1
    parts, rest = rest[:count], rest[count:]
    (own_hot, side_hot), weights, (out_ref, record_ref), scr = rest[:2], rest[2:8], rest[8:10], rest[10:]
    packs = [pl_ref, po_ref, pr_ref]
    here = lax.axis_index("img")
    sums = parts[0][...]
    if domains == 4:
        sums = sums + parts[1][...]
    got = [sums[i : i + 1, :] for i in range(6)]
    if domains == 4:
        for one in (near_ref, far_ref):
            for i in range(6):
                got[i] = got[i] + one[6 + i // 4 : 7 + i // 4, (i % 4) * LANES : (i % 4 + 1) * LANES]
    ft, ff, tt, pp, mn, vv = got
    beside = by_parity(near_ref[0:6, :], far_ref[0:6, :])
    shape = (1, LANES)
    along, spring, keep, pull, side, dt, alpha = step_numbers(
        ft,
        ff,
        tt,
        pp,
        mn,
        vv,
        number_ref[0:1, :],
        jnp.full(shape, ALPHA_START, F32),
        number_ref[2:3, :] == 1.0,
        number_ref[1:2, :] == jnp.full(shape, here, jnp.int32).astype(F32),
        jnp.full(shape, jnp.where((here >= 1) & (here <= images - 2), 1, 0), jnp.int32) == 1,
    )
    messages = [beside[0], own_ref[0:6, :], beside[1]]

    def wide(s):
        return jnp.concatenate([s] * SLAB_BLOCKS, axis=1)

    speeds = [
        wide(keep) * p[ROW_V : ROW_V + 3, :] + wide(pull) * m[0:3, :] + wide(side) * m[3:6, :]
        for p, m in zip(packs, messages)
    ]
    moved = [p[ROW_X : ROW_X + 3, :] + wide(dt) * s for p, s in zip(packs, speeds)]
    xs, sst, kept = scr[0], scr[1], scr[2:11]
    fill_region(xs, packs, lambda s: moved[s])
    forward_parts(packs, weights, xs, sst, kept)
    force = force_parts(weights, own_hot, side_hot, kept, *scr[11:])
    for c in range(3):
        for i in range(SLAB_BLOCKS):
            lanes = slice(i * LANES, (i + 1) * LANES)
            row = 4 * c + i
            out_ref[0, row : row + 1, :] = speeds[1][c : c + 1, lanes]
            out_ref[0, 12 + row : 13 + row, :] = force[c : c + 1, lanes]
            out_ref[0, 24 + row : 25 + row, :] = moved[1][c : c + 1, lanes]
    out_ref[0, 36:37, :] = dt
    out_ref[0, 37:38, :] = alpha
    out_ref[0, 38:40, :] = jnp.broadcast_to(number_ref[3:4, :], (2, LANES))
    record_ref[0:1, :] = along
    record_ref[1:2, :] = spring
    record_ref[2:3, :] = number_ref[1:2, :]


PRODUCTS = (
    [("f", "t"), ("f", "f"), ("t", "t"), ("p", "p"), ("d", "d"), ("v", "v")]
    + [("d", "v"), ("d", "f"), ("d", "t"), ("d", "V"), ("d", "F"), ("d", "T"), ("v", "f"), ("v", "t")]
    + [(a, b) for a in "vft" for b in "VFT"]
)


def gram_kernel(images, *refs):
    parts, (before_ref, after_ref), (out_ref, state_ref, messages_ref) = refs[:-5], refs[-5:-3], refs[-3:]
    rows = out_ref.shape[0]
    here = lax.axis_index("img")
    if images == 4:
        places = [here, lax.rem(here + 3, 4), jnp.where(here < 2, 3 - here, here - 2)]
        messages_ref[...] = jnp.zeros(messages_ref.shape, F32)
        for place, beside in [(lax.rem(here + 3, 4), before_ref), (lax.rem(here + 1, 4), after_ref)]:
            for c in range(3):
                for i in range(SLAB_BLOCKS):
                    row = 24 + 4 * c + i
                    messages_ref[place, row : row + 1, :] = beside[c][:, i * LANES : (i + 1) * LANES]
    else:
        places = [lax.rem(here + images - s, images) for s in range(images)]
    for place, part in zip(places, parts):
        messages_ref[place] = part[0]
    blank = [jnp.zeros((rows - images, LANES), F32)] if rows > images else []
    zero = jnp.zeros((1, LANES), F32)

    def gathered(row):
        return jnp.concatenate([messages_ref[i, row : row + 1, :] for i in range(images)] + blank, axis=0)

    def earlier(value):
        return jnp.concatenate([zero, value[0 : rows - 1]], axis=0)

    def later(value):
        return jnp.concatenate([value[1:images], zero] + blank, axis=0)

    number = lax.broadcasted_iota(jnp.int32, (rows, LANES), 0)
    held = number < images
    totals = [jnp.zeros((rows, LANES), F32) for _ in PRODUCTS]
    for row in range(3 * SLAB_BLOCKS):
        v, f, x = gathered(row), gathered(12 + row), gathered(24 + row)
        before = jnp.where(held, earlier(x), 0.0)
        after = later(x)
        t = after - before
        table = {"f": f, "v": v, "t": t, "p": after - x, "d": x - before}
        table["F"], table["V"], table["T"] = earlier(f), earlier(v), earlier(t)
        totals = [old + table[a] * table[b] for old, (a, b) in zip(totals, PRODUCTS)]
        state_ref[row : row + 1, :] = jnp.sum(jnp.where(number == here, t, 0.0), axis=0, keepdims=True)
    lane = lax.broadcasted_iota(jnp.int32, (rows, LANES), 1)
    result = jnp.zeros((rows, LANES), F32)
    for q, one in enumerate(totals):
        one = jnp.broadcast_to(jnp.sum(one, axis=1, keepdims=True), (rows, LANES))
        result = jnp.where(lane == q, one, result)
    out_ref[...] = result
    for i in range(3):
        state_ref[16 + rows * i : 16 + rows * (i + 1), :] = gathered(36 + i)


def final_kernel(images, atoms, own_ref, record_ref, state_ref, *rest):
    parts, (x_ref, v_ref, band_ref, path_ref) = rest[:-4], rest[-4:]
    rows = parts[0].shape[0]
    here = lax.axis_index("img")
    sums = parts[0][...]
    for one in parts[1:]:
        sums = sums + one[...]
    got = {
        pair: jnp.broadcast_to(sums[:, q : q + 1], (rows, LANES)) for q, pair in enumerate(PRODUCTS)
    }
    number = lax.broadcasted_iota(jnp.int32, (rows, LANES), 0)
    inside = (number >= 1) & (number <= images - 2)
    climb = jnp.broadcast_to(record_ref[2:3, :], (rows, LANES))
    dt0, alpha0, flag = (state_ref[16 + rows * i : 16 + rows * (i + 1), :] for i in range(3))
    along, spring, keep, pull, side, dt, _ = step_numbers(
        got["f", "t"],
        got["f", "f"],
        got["t", "t"],
        got["p", "p"],
        got["d", "d"],
        got["v", "v"],
        dt0,
        alpha0,
        flag == 1.0,
        number.astype(F32) == climb,
        inside,
    )

    def shifted(value):
        return jnp.concatenate([jnp.zeros((1, LANES), F32), value[0 : rows - 1]], axis=0)

    now = {"v": dt * keep, "f": dt * pull, "t": dt * side}
    old = {a.upper(): shifted(value) for a, value in now.items()}
    mine = now["v"] * now["v"] * got["v", "v"] + now["f"] * now["f"] * got["f", "f"]
    mine = mine + now["t"] * now["t"] * got["t", "t"]
    cross = now["v"] * now["f"] * got["v", "f"] + now["v"] * now["t"] * got["v", "t"]
    mine = mine + 2.0 * (cross + now["f"] * now["t"] * got["f", "t"])
    both = jnp.zeros((rows, LANES), F32)
    for a in "vft":
        both = both + now[a] * got["d", a]
    for b in "VFT":
        both = both - old[b] * got["d", b]
    for a in "vft":
        for b in "VFT":
            both = both - now[a] * old[b] * got[a, b]
    squared = got["d", "d"] + mine + shifted(mine) + 2.0 * both
    segment = jnp.sqrt(jnp.maximum(squared, 0.0) * (1.0 / (3.0 * atoms)))
    path = jnp.sum(jnp.where(number <= here, segment, 0.0), axis=0, keepdims=True)
    path_ref[...] = path[:, 0:1]
    keep, pull, side, dt, along, spring = (
        jnp.sum(jnp.where(number == here, value, 0.0), axis=0, keepdims=True)
        for value in (keep, pull, side, dt, along, spring)
    )

    for c in range(3):
        speeds, places = [], []
        for i in range(SLAB_BLOCKS):
            row = 4 * c + i
            speed = keep * own_ref[0, row : row + 1, :] + pull * own_ref[0, 12 + row : 13 + row, :]
            speed = speed + side * state_ref[row : row + 1, :]
            speeds.append(speed)
            places.append(own_ref[0, 24 + row : 25 + row, :] + dt * speed)
        v_ref[c] = jnp.concatenate(speeds, axis=1)
        x_ref[c] = jnp.concatenate(places, axis=1)
    band_ref[0] = jnp.concatenate([record_ref[0:1, 0:1], record_ref[1:2, 0:1]], axis=1)
    band_ref[1] = jnp.concatenate([along[:, 0:1], spring[:, 0:1]], axis=1)


VMEM_SPEC = pl.BlockSpec(memory_space=pltpu.VMEM)
SMEM_SPEC = pl.BlockSpec(memory_space=pltpu.SMEM)
HBM_SPEC = pl.BlockSpec(memory_space=pltpu.HBM)


def call(body, outs, scalars, arrays, scratch_shapes=(), flops=0, spec=VMEM_SPEC, vmem=24):
    return pl.pallas_call(
        body,
        out_shape=outs,
        in_specs=[SMEM_SPEC] * len(scalars) + [spec] * len(arrays),
        out_specs=jax.tree.map(lambda _: VMEM_SPEC, outs),
        scratch_shapes=list(scratch_shapes),
        compiler_params=pltpu.CompilerParams(vmem_limit_bytes=vmem * 1024 * 1024),
        cost_estimate=pl.CostEstimate(flops=flops, bytes_accessed=1 << 18, transcendentals=0),
    )(*scalars, *arrays)


def swap(array, axis, partner):
    return lax.ppermute(array, axis, [(i, partner(i)) for i in range(lax.axis_size(axis))])


def exchanged(sums, axis):
    count = lax.axis_size(axis)
    if count == 4:
        return [sums] + [swap(sums, axis, lambda i, by=by: i ^ by) for by in (2, 3, 1)]
    distance = 1
    while distance < count:
        more = swap(sums, axis, lambda i, by=distance: i ^ by)
        sums = call(add_kernel, jax.ShapeDtypeStruct(sums.shape, F32), (), (sums, more))
        distance *= 2
    return [sums]


def collected(state, axis, before, after):
    count = lax.axis_size(axis)
    if count == 4:
        return [state, swap(state, axis, lambda i: (i + 1) % 4), swap(state, axis, lambda i: (2, 3, 1, 0)[i]), before, after]
    return [state] + [swap(state, axis, lambda i, by=by: (i + by) % count) for by in range(1, count)] + [before, after]


def local(
    disp,
    veloc,
    time_step,
    reset_flags,
    climb,
    species,
    neighbours,
    counts,
    lattice,
    embed,
    radial_weight,
    mix_weight,
    update_weight,
    readout,
):
    atoms = disp.shape[2]
    images = lax.axis_size("img")
    domains = lax.axis_size("dom")
    assert disp.shape[0] == 1 and atoms == SLAB_BLOCKS * LANES and domains >= 4
    assert domains & (domains - 1) == 0 and images & (images - 1) == 0
    shape = jax.ShapeDtypeStruct
    x = jnp.transpose(disp, (1, 0, 2))
    v = jnp.transpose(veloc, (1, 0, 2))
    small = (x, v, species, neighbours, counts, embed, readout, radial_weight, mix_weight, update_weight)
    sent, kept_pack = call(
        pack_kernel,
        (shape((PACK_ROWS, atoms), F32), shape((OWN_ROWS, atoms), F32)),
        (),
        (*small, jnp.transpose(lattice, (1, 0, 2))),
        [pltpu.VMEM(a.shape, a.dtype) for a in small] + [pltpu.SemaphoreType.DMA((16,))],
        spec=HBM_SPEC,
        vmem=63,
    )
    sibling = swap(sent, "dom", lambda i: i ^ 1)
    across = swap(sent, "dom", lambda i: (i + 2 * (i % 2) - 1) % domains)
    own_hot, *weights, x_copy, pack = call(
        prepare_kernel,
        (
            shape((SLAB_BLOCKS, 3 * LANES, SLOTS * LANES), BF16),
            shape((CHANNELS, 48), BF16),
            shape((CHANNELS, 192), BF16),
            shape((CHANNELS, 32), BF16),
            shape((CHANNELS, 3 * LANES), BF16),
            shape((16, 192), BF16),
            shape((4, CHANNELS, LANES), F32),
            shape(x.shape, F32),
            shape(sent.shape, F32),
        ),
        (),
        (kept_pack,),
        flops=100000000,
    )
    before = swap(x_copy, "img", lambda i: (i + 1) % images)
    after = swap(x_copy, "img", lambda i: (i - 1) % images)
    force_scratch = forward_scratch() + [pltpu.VMEM(*one) for one in kept_shapes()] + back_scratch()
    force, left, right, side_hot = call(
        first_kernel,
        (
            shape((3, atoms), F32),
            shape(sent.shape, F32),
            shape(sent.shape, F32),
            shape((SIDE_ROWS, SLOTS * LANES), BF16),
        ),
        (),
        (sibling, pack, across, own_hot, *weights),
        force_scratch,
        flops=1000000000,
    )
    message, sums = call(
        functools.partial(blend_kernel, images),
        (shape((8, atoms), F32), shape((8, LANES), F32)),
        (),
        (force, pack, before, after),
    )
    far = swap(message, "dom", lambda i: (i + 2 * (i % 2) - 1) % domains)
    if domains == 4:
        parts = [sums, swap(sums, "dom", lambda i: i ^ 2)]
    else:
        parts = exchanged(sums, "dom")
    near = swap(message, "dom", lambda i: i ^ 1)
    numbers = call(number_kernel, shape((8, LANES), F32), (time_step, jnp.transpose(reset_flags), climb), ())
    state, record = call(
        functools.partial(second_kernel, images, domains),
        (shape((1, 40, LANES), F32), shape((3, LANES), F32)),
        (),
        (numbers, left, pack, right, message, near, far, *parts, own_hot, side_hot, *weights),
        force_scratch,
        flops=1000000000,
    )
    rows = 8 * ((images + 7) // 8)
    sums, extra = call(
        functools.partial(gram_kernel, images),
        (shape((rows, LANES), F32), shape((16 + 3 * rows, LANES), F32)),
        (),
        collected(state, "img", before, after),
        [pltpu.VMEM((images, 40, LANES), F32)],
    )
    new_x, new_v, records, path = call(
        functools.partial(final_kernel, images, atoms * domains),
        (shape(x.shape, F32), shape(x.shape, F32), shape((2, 1, 2), F32), shape((1, 1), F32)),
        (),
        (state, record, extra, *exchanged(sums, "dom")),
    )
    return (
        jnp.transpose(new_x, (1, 0, 2)),
        jnp.transpose(new_v, (1, 0, 2)),
        jnp.transpose(records, (0, 2, 1)),
        path.reshape(1),
    )


def solution(mesh):
    in_specs = (
        P(("group", "img"), None, "dom"),
        P(("group", "img"), None, "dom"),
        P(("group", "img")),
        P(None, ("group", "img")),
        P("group"),
        P(("group", "dom")),
        P(None, ("group", "dom")),
        P(("group", "dom")),
        P(None, None, ("group", "dom")),
        P(),
        P(),
        P(),
        P(),
        P(),
    )
    out_specs = (
        P(("group", "img"), None, "dom"),
        P(("group", "img"), None, "dom"),
        P(None, None, ("group", "img")),
        P(("group", "img")),
    )
    return jax.shard_map(local, mesh=mesh, in_specs=in_specs, out_specs=out_specs, check_vma=False)
```

```python
import functools
import math

import jax
import jax.numpy as jnp
from jax import lax
from jax.experimental import pallas as pl
from jax.experimental.pallas import tpu as pltpu
from jax.sharding import PartitionSpec as P

F32 = jnp.float32
BF16 = jnp.bfloat16
PRECISE = lax.Precision.HIGHEST
SPRING_CONSTANT = 0.5
ALPHA_START = 0.1
STEP_LIMIT = 0.3
TINY_VALUE = 1e-06
SOFTENING = 0.25
LANES = 128
SLOTS = 8
BASIS = 8
CHANNELS = 64
SLAB_BLOCKS = 4
ROW_X = 32
ROW_COUNT = 35
ROW_KIND = 36
ROW_V = 37
PACK_ROWS = 40
OWN_ROWS = PACK_ROWS + CHANNELS + BASIS
NT = (((1,), (1,)), ((), ()))


def split(x):
    high = x.astype(BF16).astype(F32)
    return high, x - high


def left_stack(w):
    high, low = split(w)
    return jnp.concatenate([high, high, low], axis=1)


def right_stack(x):
    high, low = split(x)
    high = high.astype(BF16)
    return jnp.concatenate([high, low.astype(BF16), high], axis=0)


def pair_stack(x):
    high, low = split(x)
    return jnp.concatenate([high.astype(BF16), low.astype(BF16)], axis=0)


def mm(a, b):
    return jnp.dot(a, b, preferred_element_type=F32)


def mm_nt(a, b):
    return lax.dot_general(a, b, NT, preferred_element_type=F32)


def pack_kernel(*refs):
    sources, (out_ref, own_ref), held, sems = refs[:11], refs[11:13], refs[13:23], refs[23]
    lattice = sources[10]
    pairs = list(zip(sources, held))
    for c in range(3):
        rows = pl.ds(8 + 8 * c, 8)
        pairs += [(lattice.at[c], out_ref.at[rows]), (lattice.at[c], own_ref.at[rows])]
    copies = [pltpu.make_async_copy(a, b, sems.at[i]) for i, (a, b) in enumerate(pairs)]
    for one in copies:
        one.start()
    for one in copies:
        one.wait()
    x, v, species, nbr, counts, embed, readout, radial, mix, update = held
    for ref in (out_ref, own_ref):
        ref[0:8, :] = nbr[...].astype(F32)
        for c in range(3):
            ref[ROW_X + c : ROW_X + c + 1, :] = x[c]
            ref[ROW_V + c : ROW_V + c + 1, :] = v[c]
        ref[ROW_COUNT : ROW_COUNT + 1, :] = counts[...].astype(F32).reshape(1, -1)
        ref[ROW_KIND : ROW_KIND + 1, :] = species[...].astype(F32).reshape(1, -1)
    top, low = PACK_ROWS, PACK_ROWS + CHANNELS
    for i, value in enumerate([mix[0], mix[1], update[0], update[1]]):
        own_ref[top:low, i * LANES : i * LANES + CHANNELS] = value
    for i, value in enumerate([radial[0], radial[1], embed[...], readout[...].reshape(1, CHANNELS)]):
        own_ref[low : low + value.shape[0], i * LANES : i * LANES + CHANNELS] = value


def prepare_kernel(po_ref, *rest):
    own_hot, l1_ref, l2_ref, l3_ref, l5_ref, l6_ref, col_ref, copy_ref, pack_ref = rest
    pack_ref[...] = po_ref[0:PACK_ROWS, :]
    for b in range(SLAB_BLOCKS):
        mark(window_index(po_ref, b), [0, 1, 2], own_hot.at[b])
    for c in range(3):
        copy_ref[c] = po_ref[ROW_X + c : ROW_X + c + 1, :]

    def raw(first, count, i):
        return po_ref[first : first + count, i * LANES : i * LANES + CHANNELS]

    low = PACK_ROWS + CHANNELS
    mix_ref = [raw(PACK_ROWS, CHANNELS, i) for i in range(2)]
    update_ref = [raw(PACK_ROWS, CHANNELS, 2 + i) for i in range(2)]
    radial_ref = [raw(low, BASIS, i) for i in range(2)]
    embed_ref, readout = raw(low, 2, 2), raw(low, 1, 3)
    eye = (
        lax.broadcasted_iota(jnp.int32, (CHANNELS, CHANNELS), 0)
        == lax.broadcasted_iota(jnp.int32, (CHANNELS, CHANNELS), 1)
    ).astype(F32)

    def turned(x):
        return lax.dot_general(eye, x, NT, precision=PRECISE, preferred_element_type=F32)

    base0 = embed_ref[0:1, :]
    base1 = embed_ref[1:2, :] - base0
    rows = jnp.concatenate([base0, base1], axis=0)
    sent = jnp.dot(rows, mix_ref[0], precision=PRECISE, preferred_element_type=F32)
    scale = 1.0 / math.sqrt(SLOTS)
    first = jnp.concatenate([radial_ref[0] * sent[0:1], radial_ref[0] * sent[1:2]], axis=0) * scale
    second = radial_ref[1] * scale
    folded = jnp.dot(update_ref[0], mix_ref[1], precision=PRECISE, preferred_element_type=F32)
    mix_t = turned(mix_ref[1])
    l1_ref[...] = left_stack(turned(first)).astype(BF16)
    l2_ref[...] = left_stack(turned(folded)).astype(BF16)
    high, low = split(turned(second))
    l3_ref[...] = jnp.concatenate([high, high, low, jnp.zeros_like(high)], axis=1).astype(BF16)
    high, low = split(folded)
    l5_ref[...] = jnp.concatenate([high, high, high, high, low, low], axis=1).astype(BF16)
    l6_ref[...] = left_stack(first).astype(BF16)
    wide = (CHANNELS, LANES)
    col_ref[0] = jnp.broadcast_to(jnp.sum(mix_t * base0, axis=1, keepdims=True), wide)
    col_ref[1] = jnp.broadcast_to(jnp.sum(mix_t * base1, axis=1, keepdims=True), wide)
    col_ref[2] = jnp.broadcast_to(jnp.sum(update_ref[0] * readout, axis=1, keepdims=True), wide)
    col_ref[3] = jnp.broadcast_to(jnp.sum(update_ref[1] * readout, axis=1, keepdims=True), wide)


def sin_cos(t):
    q = t * t
    s = -1.0 / 39916800.0
    for c in (1.0 / 362880.0, -1.0 / 5040.0, 1.0 / 120.0, -1.0 / 6.0, 1.0):
        s = s * q + c
    k = 1.0 / 479001600.0
    for c in (-1.0 / 3628800.0, 1.0 / 40320.0, -1.0 / 720.0, 1.0 / 24.0, -0.5, 1.0):
        k = k * q + c
    return s * t, k


def wide_row(x, row):
    return jnp.broadcast_to(x[row : row + 1, :], (8, x.shape[1]))


def silu_parts(m):
    sig = 1.0 / (1.0 + jnp.exp(-m))
    return m * sig, sig * (1.0 + m * (1.0 - sig))


def pick(values, lanes):
    return jnp.take_along_axis(values, lanes, axis=1, mode="promise_in_bounds")


def reach(b, first, last):
    return [w for w in range(3) if first <= b - 1 + w <= last]


SIDE_START = {2: 0, 3: LANES, 8: 3 * LANES, 9: 5 * LANES}
SIDE_ROWS = 6 * LANES


def mark(index, ws, target):
    count = len(ws) * LANES
    row_id = (lax.broadcasted_iota(jnp.int32, (count, LANES), 0) + ws[0] * LANES).astype(jnp.int16)
    one, zero = jnp.ones((count, LANES), BF16), jnp.zeros((count, LANES), BF16)
    for k in range(SLOTS):
        wanted = jnp.broadcast_to(index[k : k + 1, :], (16, LANES)).astype(jnp.int16)
        wanted = jnp.concatenate([wanted] * (count // 16), axis=0)
        target[:, k * LANES : (k + 1) * LANES] = jnp.where(row_id == wanted, one, zero)


def window_index(pack, b):
    lanes = slice((b % 4) * LANES, (b % 4 + 1) * LANES)
    return pack[0:8, lanes].astype(jnp.int32) - LANES * (b % 4)


def mark_sides(packs, side):
    for b, start in SIDE_START.items():
        ws = reach(b, 3, 8)
        mark(window_index(packs[b // 4], b), ws, side.at[start : start + len(ws) * LANES])


def forward_parts(packs, weights, xs, sst, kept):
    l1, l2, l3, l5, l6, col = weights
    (widx, kinds, geo, bst, bps, bpr, sent_all, sent_pair, slope) = kept
    centre = 2.0 + 0.5 * lax.broadcasted_iota(jnp.int32, (BASIS, LANES), 0).astype(F32)
    slot = lax.broadcasted_iota(jnp.int32, (SLOTS, LANES), 0)

    def part_rows(value):
        high, low = split(value)
        return jnp.concatenate([high, low], axis=0).astype(BF16)

    def pairs(b):
        pack = packs[b // 4]
        lanes = slice((b % 4) * LANES, (b % 4 + 1) * LANES)
        index = window_index(pack, b)
        widx[b] = index
        inner = index & (LANES - 1)
        part = index >> 7

        def taken(row):
            got = [
                pick(jnp.broadcast_to(xs[b - 1 + w, row : row + 1, :], (SLOTS, LANES)), inner)
                for w in range(3)
            ]
            return jnp.where(part == 0, got[0], jnp.where(part == 1, got[1], got[2]))

        vec = [
            pack[8 + 8 * c : 16 + 8 * c, lanes] + taken(c) - jnp.broadcast_to(xs[b, c : c + 1, :], (SLOTS, LANES))
            for c in range(3)
        ]
        kind = taken(3)
        dist = jnp.sqrt(vec[0] * vec[0] + vec[1] * vec[1] + vec[2] * vec[2] + SOFTENING)
        live = (slot.astype(F32) < jnp.broadcast_to(pack[ROW_COUNT : ROW_COUNT + 1, lanes], (SLOTS, LANES))).astype(F32)
        turns = dist * (1.0 / 12.0)
        turns = turns - jnp.floor(turns + 0.5)
        sine, cosine = sin_cos(turns * math.pi)
        envelope = cosine * cosine * live
        slant = cosine * sine * live * (-math.pi / 6.0)
        if 3 <= b <= 8:
            kinds[b] = kind
            for c in range(3):
                geo[b, c] = vec[c]
            geo[b, 3] = 1.0 / dist
        total = jnp.zeros((BASIS, LANES), F32)
        total_kind = jnp.zeros((BASIS, LANES), F32)
        for k in range(SLOTS):
            away = wide_row(dist, k) - centre
            gauss = jnp.exp(-4.0 * (away * away))
            env_k = wide_row(envelope, k)
            value = gauss * env_k
            total = total + value
            total_kind = total_kind + value * wide_row(kind, k)
            cols = slice(k * LANES, (k + 1) * LANES)
            if 2 <= b <= 9:
                bst[b, :, cols] = part_rows(value)
            if 3 <= b <= 8:
                value = gauss * (wide_row(slant, k) - 8.0 * away * env_k)
                bpr[b, :, cols] = value
                bps[b, :, cols] = part_rows(value)
        high, low = split(jnp.concatenate([total, total_kind], axis=0))
        sst[:, b * LANES : (b + 1) * LANES] = jnp.concatenate([high, low, high], axis=0).astype(BF16)

    for b in range(1, 11):
        pairs(b)

    for b in range(1, 11, 2):
        cols = slice(b * LANES, (b + 2) * LANES)
        value, steep = silu_parts(mm(l1[...], sst[:, cols]))
        sent = mm(l2[...], right_stack(value))
        for i in range(2):
            one = sent[:, i * LANES : (i + 1) * LANES]
            one = one + col[0] + col[1] * jnp.broadcast_to(xs[b + i, 3:4, :], (CHANNELS, LANES))
            sent_all[:, (b + i) * LANES : (b + i + 1) * LANES] = one
            if 3 <= b + i <= 8:
                sent_pair[:, (b + i) * LANES : (b + i + 1) * LANES] = pair_stack(one)
        slope[:, cols] = steep


def force_parts(weights, own_hot, side_hot, kept, dg, pulls, met, acc, held):
    l1, l2, l3, l5, l6, col = weights
    (widx, kinds, geo, bst, bps, bpr, sent_all, sent_pair, slope) = kept
    slot = lax.broadcasted_iota(jnp.int32, (SLOTS, LANES), 0)

    def marks(b, ws):
        if b in SIDE_START:
            start = SIDE_START[b] + (ws[0] - reach(b, 3, 8)[0]) * LANES
            return side_hot.at[start : start + len(ws) * LANES]
        return own_hot.at[b - 4, ws[0] * LANES : (ws[-1] + 1) * LANES]

    def add_rows(sums, first, b, ws, out):
        for i, w in enumerate(ws):
            target = b - 1 + w
            piece = out[i * LANES : (i + 1) * LANES]
            rows = slice((target - first) * LANES, (target - first + 1) * LANES)
            if (first, target) in started:
                sums[rows, :] += piece
            else:
                sums[rows, :] = piece
                started.add((first, target))

    started = set()

    def block_work(b):
        index = widx[b]
        inner, part = index & (LANES - 1), index >> 7
        basis = bst[b]
        radial = mm(l3[...], jnp.concatenate([basis, basis], axis=0))
        if 3 <= b <= 8:
            basis = bps[b]
            steepness = mm(l3[...], jnp.concatenate([basis, basis], axis=0))
        lanes = [jnp.broadcast_to(inner[k : k + 1, :], (16, LANES)) for k in range(SLOTS)]
        parts = [jnp.broadcast_to(part[k : k + 1, :], (16, LANES)) for k in range(SLOTS)]
        own = 4 <= b <= 7
        if own:
            found_all = mm(sent_pair[:, (b - 1) * LANES : (b + 2) * LANES], own_hot[b - 4])
        value = held.at[b % 2]
        total = [jnp.zeros((8, LANES), F32)] * SLOTS
        for u in range(CHANNELS // 16):
            rows = slice(16 * u, 16 * u + 16)
            low_rows = slice(CHANNELS + 16 * u, CHANNELS + 16 * u + 16)
            windows = [sent_all[rows, (b - 1 + w) * LANES : (b + w) * LANES] for w in range(3)]
            got = []
            message = jnp.zeros((16, LANES), F32)
            for k in range(SLOTS):
                cols = slice(k * LANES, (k + 1) * LANES)
                if own:
                    got.append(found_all[rows, cols] + found_all[low_rows, cols])
                else:
                    found = [pick(window, lanes[k]) for window in windows]
                    got.append(jnp.where(parts[k] == 0, found[0], jnp.where(parts[k] == 1, found[1], found[2])))
                message = message + radial[rows, cols] * got[k]
            _, steep = silu_parts(message)
            back = col[3, rows] * steep
            for k in range(SLOTS):
                cols = slice(k * LANES, (k + 1) * LANES)
                high, low = split(radial[rows, cols] * back)
                value[rows, cols] = high.astype(BF16)
                value[low_rows, cols] = low.astype(BF16)
                if 3 <= b <= 8:
                    pull = got[k] * back * steepness[rows, cols]
                    total[k] = total[k] + pull[0:8] + pull[8:16]
            yield
        if 3 <= b <= 8:
            for k in range(SLOTS):
                pulls[b, :, k * LANES : (k + 1) * LANES] = total[k]

    def scatter_work(b):
        ws = reach(b, 3, 8)
        chosen, value = marks(b, ws), held.at[b % 2]
        out = None
        for u in range(4):
            cols = slice(u * 2 * LANES, (u + 1) * 2 * LANES)
            one = mm_nt(chosen[:, cols], value[:, cols])
            out = one if out is None else out + one
            yield
        add_rows(dg, 3, b, ws, out)

    def together(*works):
        works = list(works)
        while works:
            works = [work for work in works if next(work, "end") != "end"]

    together(block_work(2))
    for b in range(3, 10):
        together(scatter_work(b - 1), block_work(b))
    together(scatter_work(9))

    def finish(b, sums):
        kind = kinds[b]
        rows = []
        for k in range(SLOTS):
            cols = slice(k * LANES, (k + 1) * LANES)
            weight = sums[0:8] + wide_row(kind, k) * sums[8:16]
            rows.append(jnp.sum(bpr[b, :, cols] * weight + pulls[b, :, cols], axis=0, keepdims=True))
        pull = jnp.concatenate(rows, axis=0) * geo[b, 3]
        pieces = []
        for c in range(3):
            value = pull * geo[b, c]
            if 4 <= b <= 7:
                acc[b - 4, c] = jnp.sum(value, axis=0, keepdims=True)
            pieces.append(split(value))
        lines = []
        for h in range(2):
            for c in range(3):
                lines.append(jnp.concatenate([jnp.where(slot == k, pieces[c][h], 0.0) for k in range(SLOTS)], axis=1))
        ws = reach(b, 4, 7)
        out = mm_nt(jnp.concatenate(lines, axis=0).astype(BF16), marks(b, ws)[...])
        for c in range(3):
            both = out[8 * c : 8 * c + 8] + out[24 + 8 * c : 32 + 8 * c]
            for i, w in enumerate(ws):
                target = b - 5 + w
                piece = both[:, i * LANES : (i + 1) * LANES]
                if (c, target) in met_blocks:
                    met[target, c] += piece
                else:
                    met[target, c] = piece
                    met_blocks.add((c, target))

    met_blocks = set()

    for b in range(3, 9, 2):
        cols = slice(b * LANES, (b + 2) * LANES)
        high, low = split(dg[(b - 3) * LANES : (b - 1) * LANES, :])
        steep = mm_nt(l5[...], jnp.concatenate([high, low, high], axis=1).astype(BF16))
        steep = steep + jnp.concatenate([col[2], col[2]], axis=1)
        sums = mm(l6[...], right_stack(steep * slope[:, cols]))
        for i in range(2):
            finish(b + i, sums[:, i * LANES : (i + 1) * LANES])

    away = []
    for c in range(3):
        back = [acc[i, c] - jnp.sum(met[i, c], axis=0, keepdims=True) for i in range(SLAB_BLOCKS)]
        away.append(jnp.concatenate(back, axis=1))
    return jnp.concatenate(away, axis=0)


def fill_region(xs, packs, rows_of):
    for b in range(12):
        lanes = slice((b % 4) * LANES, (b % 4 + 1) * LANES)
        pack = packs[b // 4]
        xs[b, 0:3, :] = rows_of(b // 4)[:, lanes]
        xs[b, 3:4, :] = pack[ROW_KIND : ROW_KIND + 1, lanes]


def lane_total(x):
    x = x[:, 0:LANES] + x[:, LANES : 2 * LANES] + x[:, 2 * LANES : 3 * LANES] + x[:, 3 * LANES : 4 * LANES]
    return jnp.sum(x, axis=1, keepdims=True)


def dot3(a, b):
    return jnp.sum(a * b, axis=0, keepdims=True)


def kept_shapes():
    wide = 12 * LANES
    return [
        ((12, 8, LANES), jnp.int32),
        ((12, 8, LANES), F32),
        ((12, 4, 8, LANES), F32),
        ((12, 16, SLOTS * LANES), BF16),
        ((12, 16, SLOTS * LANES), BF16),
        ((12, 8, SLOTS * LANES), F32),
        ((CHANNELS, wide), F32),
        ((2 * CHANNELS, wide), BF16),
        ((CHANNELS, wide), F32),
    ]


def forward_scratch():
    return [pltpu.VMEM((12, 8, LANES), F32), pltpu.VMEM((48, 12 * LANES), BF16)]


def back_scratch():
    return [
        pltpu.VMEM((6 * LANES, 2 * CHANNELS), F32),
        pltpu.VMEM((12, 8, SLOTS * LANES), F32),
        pltpu.VMEM((SLAB_BLOCKS, 3, SLOTS, LANES), F32),
        pltpu.VMEM((SLAB_BLOCKS, 3, 1, LANES), F32),
        pltpu.VMEM((2, 2 * CHANNELS, SLOTS * LANES), BF16),
    ]


def by_parity(sibling, across):
    even = jnp.full(sibling.shape, lax.axis_index("dom") % 2, jnp.int32) == 0
    return jnp.where(even, across, sibling), jnp.where(even, sibling, across)


def first_kernel(sibling_ref, po_ref, across_ref, own_hot, *rest):
    weights, (out_ref, pl_ref, pr_ref, side_hot), scr = rest[:6], rest[6:10], rest[10:]
    xs, sst, kept = scr[0], scr[1], scr[2:11]
    pl_ref[...], pr_ref[...] = by_parity(sibling_ref[...], across_ref[...])
    packs = [pl_ref, po_ref, pr_ref]
    mark_sides(packs, side_hot)
    fill_region(xs, packs, lambda s: packs[s][ROW_X : ROW_X + 3, :])
    forward_parts(packs, weights, xs, sst, kept)
    out_ref[...] = force_parts(weights, own_hot, side_hot, kept, *scr[11:])


def rows_of(ref):
    return jnp.concatenate([ref[c] for c in range(3)], axis=0)


def block_row(*values):
    values = list(values) + [jnp.zeros((1, LANES), F32)] * (SLAB_BLOCKS - len(values))
    return jnp.concatenate(values, axis=1)


def blend_kernel(images, force_ref, po_ref, before_ref, after_ref, out_ref, sums_ref):
    x = po_ref[ROW_X : ROW_X + 3, :]
    v = po_ref[ROW_V : ROW_V + 3, :]
    force = force_ref[...]
    here = lax.axis_index("img")
    before = jnp.where(here > 0, rows_of(before_ref), 0.0)
    after = jnp.where(here < images - 1, rows_of(after_ref), 0.0)
    tangent = after - before
    plus = after - x
    minus = x - before
    sums = jnp.concatenate(
        [
            dot3(force, tangent),
            dot3(force, force),
            dot3(tangent, tangent),
            dot3(plus, plus),
            dot3(minus, minus),
            dot3(v, v),
            jnp.zeros((2, x.shape[1]), F32),
        ],
        axis=0,
    )
    sums = jnp.broadcast_to(lane_total(sums), (8, LANES))
    sums_ref[...] = sums
    out_ref[0:3, :] = force
    out_ref[3:6, :] = tangent
    out_ref[6:7, :] = block_row(*[sums[i : i + 1] for i in range(4)])
    out_ref[7:8, :] = block_row(sums[4:5], sums[5:6])


def step_numbers(ft, ff, tt, pp, mn, vv, dt, alpha, flagged, climbing, inside):
    root = jnp.sqrt(tt + TINY_VALUE)
    along = ft / root
    spring = SPRING_CONSTANT * (jnp.sqrt(pp) - jnp.sqrt(mn))
    factor = jnp.where(climbing, -2.0 * along, spring - along)
    band = jnp.maximum(ff + 2.0 * factor * along + factor * factor * (tt / (tt + TINY_VALUE)), 0.0)
    new_dt = jnp.where(flagged, 0.5 * dt, jnp.minimum(1.1 * dt, STEP_LIMIT))
    pull = jnp.where(flagged, 0.0, alpha * jnp.sqrt(vv / (band + TINY_VALUE))) + new_dt
    keep = jnp.where(flagged, 0.0, 1.0 - alpha)
    new_alpha = jnp.where(flagged, ALPHA_START, 0.99 * alpha)
    keep = jnp.where(inside, keep, 0.0)
    pull = jnp.where(inside, pull, 0.0)
    return (
        jnp.where(inside, along, 0.0),
        jnp.where(inside, spring, 0.0),
        keep,
        pull,
        pull * factor / root,
        new_dt,
        new_alpha,
    )


def add_kernel(a_ref, b_ref, out_ref):
    out_ref[...] = a_ref[...] + b_ref[...]


def number_kernel(dt_ref, flag_ref, climb_ref, out_ref):
    flags = [flag_ref[0, s].astype(F32) for s in range(flag_ref.shape[1])]
    for i, value in enumerate([dt_ref[0], climb_ref[0].astype(F32)] + flags):
        out_ref[i : i + 1, :] = jnp.full((1, LANES), value, F32)


def second_kernel(images, domains, number_ref, pl_ref, po_ref, pr_ref, own_ref, near_ref, far_ref, *rest):
    count = 2 if domains == 4 else 1
    parts, rest = rest[:count], rest[count:]
    (own_hot, side_hot), weights, (out_ref, record_ref), scr = rest[:2], rest[2:8], rest[8:10], rest[10:]
    packs = [pl_ref, po_ref, pr_ref]
    here = lax.axis_index("img")
    sums = parts[0][...]
    if domains == 4:
        sums = sums + parts[1][...]
    got = [sums[i : i + 1, :] for i in range(6)]
    if domains == 4:
        for one in (near_ref, far_ref):
            for i in range(6):
                got[i] = got[i] + one[6 + i // 4 : 7 + i // 4, (i % 4) * LANES : (i % 4 + 1) * LANES]
    ft, ff, tt, pp, mn, vv = got
    beside = by_parity(near_ref[0:6, :], far_ref[0:6, :])
    shape = (1, LANES)
    along, spring, keep, pull, side, dt, alpha = step_numbers(
        ft,
        ff,
        tt,
        pp,
        mn,
        vv,
        number_ref[0:1, :],
        jnp.full(shape, ALPHA_START, F32),
        number_ref[2:3, :] == 1.0,
        number_ref[1:2, :] == jnp.full(shape, here, jnp.int32).astype(F32),
        jnp.full(shape, jnp.where((here >= 1) & (here <= images - 2), 1, 0), jnp.int32) == 1,
    )
    messages = [beside[0], own_ref[0:6, :], beside[1]]

    def wide(s):
        return jnp.concatenate([s] * SLAB_BLOCKS, axis=1)

    speeds = [
        wide(keep) * p[ROW_V : ROW_V + 3, :] + wide(pull) * m[0:3, :] + wide(side) * m[3:6, :]
        for p, m in zip(packs, messages)
    ]
    moved = [p[ROW_X : ROW_X + 3, :] + wide(dt) * s for p, s in zip(packs, speeds)]
    xs, sst, kept = scr[0], scr[1], scr[2:11]
    fill_region(xs, packs, lambda s: moved[s])
    forward_parts(packs, weights, xs, sst, kept)
    force = force_parts(weights, own_hot, side_hot, kept, *scr[11:])
    for c in range(3):
        for i in range(SLAB_BLOCKS):
            lanes = slice(i * LANES, (i + 1) * LANES)
            row = 4 * c + i
            out_ref[0, row : row + 1, :] = speeds[1][c : c + 1, lanes]
            out_ref[0, 12 + row : 13 + row, :] = force[c : c + 1, lanes]
            out_ref[0, 24 + row : 25 + row, :] = moved[1][c : c + 1, lanes]
    out_ref[0, 36:37, :] = dt
    out_ref[0, 37:38, :] = alpha
    out_ref[0, 38:40, :] = jnp.broadcast_to(number_ref[3:4, :], (2, LANES))
    record_ref[0:1, :] = along
    record_ref[1:2, :] = spring
    record_ref[2:3, :] = number_ref[1:2, :]


PRODUCTS = (
    [("f", "t"), ("f", "f"), ("t", "t"), ("p", "p"), ("d", "d"), ("v", "v")]
    + [("d", "v"), ("d", "f"), ("d", "t"), ("d", "V"), ("d", "F"), ("d", "T"), ("v", "f"), ("v", "t")]
    + [(a, b) for a in "vft" for b in "VFT"]
)


def gram_kernel(images, *refs):
    parts, (before_ref, after_ref), (out_ref, state_ref, messages_ref) = refs[:-5], refs[-5:-3], refs[-3:]
    rows = out_ref.shape[0]
    here = lax.axis_index("img")
    if images == 4:
        places = [here, lax.rem(here + 3, 4), jnp.where(here < 2, 3 - here, here - 2)]
        messages_ref[...] = jnp.zeros(messages_ref.shape, F32)
        for place, beside in [(lax.rem(here + 3, 4), before_ref), (lax.rem(here + 1, 4), after_ref)]:
            for c in range(3):
                for i in range(SLAB_BLOCKS):
                    row = 24 + 4 * c + i
                    messages_ref[place, row : row + 1, :] = beside[c][:, i * LANES : (i + 1) * LANES]
    else:
        places = [lax.rem(here + images - s, images) for s in range(images)]
    for place, part in zip(places, parts):
        messages_ref[place] = part[0]
    blank = [jnp.zeros((rows - images, LANES), F32)] if rows > images else []
    zero = jnp.zeros((1, LANES), F32)

    def gathered(row):
        return jnp.concatenate([messages_ref[i, row : row + 1, :] for i in range(images)] + blank, axis=0)

    def earlier(value):
        return jnp.concatenate([zero, value[0 : rows - 1]], axis=0)

    def later(value):
        return jnp.concatenate([value[1:images], zero] + blank, axis=0)

    number = lax.broadcasted_iota(jnp.int32, (rows, LANES), 0)
    held = number < images
    totals = [jnp.zeros((rows, LANES), F32) for _ in PRODUCTS]
    for row in range(3 * SLAB_BLOCKS):
        v, f, x = gathered(row), gathered(12 + row), gathered(24 + row)
        before = jnp.where(held, earlier(x), 0.0)
        after = later(x)
        t = after - before
        table = {"f": f, "v": v, "t": t, "p": after - x, "d": x - before}
        table["F"], table["V"], table["T"] = earlier(f), earlier(v), earlier(t)
        totals = [old + table[a] * table[b] for old, (a, b) in zip(totals, PRODUCTS)]
        state_ref[row : row + 1, :] = jnp.sum(jnp.where(number == here, t, 0.0), axis=0, keepdims=True)
    lane = lax.broadcasted_iota(jnp.int32, (rows, LANES), 1)
    result = jnp.zeros((rows, LANES), F32)
    for q, one in enumerate(totals):
        one = jnp.broadcast_to(jnp.sum(one, axis=1, keepdims=True), (rows, LANES))
        result = jnp.where(lane == q, one, result)
    out_ref[...] = result
    for i in range(3):
        state_ref[16 + rows * i : 16 + rows * (i + 1), :] = gathered(36 + i)


def final_kernel(images, atoms, own_ref, record_ref, state_ref, *rest):
    parts, (x_ref, v_ref, band_ref, path_ref) = rest[:-4], rest[-4:]
    rows = parts[0].shape[0]
    here = lax.axis_index("img")
    sums = parts[0][...]
    for one in parts[1:]:
        sums = sums + one[...]
    got = {
        pair: jnp.broadcast_to(sums[:, q : q + 1], (rows, LANES)) for q, pair in enumerate(PRODUCTS)
    }
    number = lax.broadcasted_iota(jnp.int32, (rows, LANES), 0)
    inside = (number >= 1) & (number <= images - 2)
    climb = jnp.broadcast_to(record_ref[2:3, :], (rows, LANES))
    dt0, alpha0, flag = (state_ref[16 + rows * i : 16 + rows * (i + 1), :] for i in range(3))
    along, spring, keep, pull, side, dt, _ = step_numbers(
        got["f", "t"],
        got["f", "f"],
        got["t", "t"],
        got["p", "p"],
        got["d", "d"],
        got["v", "v"],
        dt0,
        alpha0,
        flag == 1.0,
        number.astype(F32) == climb,
        inside,
    )

    def shifted(value):
        return jnp.concatenate([jnp.zeros((1, LANES), F32), value[0 : rows - 1]], axis=0)

    now = {"v": dt * keep, "f": dt * pull, "t": dt * side}
    old = {a.upper(): shifted(value) for a, value in now.items()}
    mine = now["v"] * now["v"] * got["v", "v"] + now["f"] * now["f"] * got["f", "f"]
    mine = mine + now["t"] * now["t"] * got["t", "t"]
    cross = now["v"] * now["f"] * got["v", "f"] + now["v"] * now["t"] * got["v", "t"]
    mine = mine + 2.0 * (cross + now["f"] * now["t"] * got["f", "t"])
    both = jnp.zeros((rows, LANES), F32)
    for a in "vft":
        both = both + now[a] * got["d", a]
    for b in "VFT":
        both = both - old[b] * got["d", b]
    for a in "vft":
        for b in "VFT":
            both = both - now[a] * old[b] * got[a, b]
    squared = got["d", "d"] + mine + shifted(mine) + 2.0 * both
    segment = jnp.sqrt(jnp.maximum(squared, 0.0) * (1.0 / (3.0 * atoms)))
    path = jnp.sum(jnp.where(number <= here, segment, 0.0), axis=0, keepdims=True)
    path_ref[...] = path[:, 0:1]
    keep, pull, side, dt, along, spring = (
        jnp.sum(jnp.where(number == here, value, 0.0), axis=0, keepdims=True)
        for value in (keep, pull, side, dt, along, spring)
    )

    for c in range(3):
        speeds, places = [], []
        for i in range(SLAB_BLOCKS):
            row = 4 * c + i
            speed = keep * own_ref[0, row : row + 1, :] + pull * own_ref[0, 12 + row : 13 + row, :]
            speed = speed + side * state_ref[row : row + 1, :]
            speeds.append(speed)
            places.append(own_ref[0, 24 + row : 25 + row, :] + dt * speed)
        v_ref[c] = jnp.concatenate(speeds, axis=1)
        x_ref[c] = jnp.concatenate(places, axis=1)
    band_ref[0] = jnp.concatenate([record_ref[0:1, 0:1], record_ref[1:2, 0:1]], axis=1)
    band_ref[1] = jnp.concatenate([along[:, 0:1], spring[:, 0:1]], axis=1)


VMEM_SPEC = pl.BlockSpec(memory_space=pltpu.VMEM)
SMEM_SPEC = pl.BlockSpec(memory_space=pltpu.SMEM)
HBM_SPEC = pl.BlockSpec(memory_space=pltpu.HBM)


def call(body, outs, scalars, arrays, scratch_shapes=(), flops=0, spec=VMEM_SPEC, vmem=24):
    return pl.pallas_call(
        body,
        out_shape=outs,
        in_specs=[SMEM_SPEC] * len(scalars) + [spec] * len(arrays),
        out_specs=jax.tree.map(lambda _: VMEM_SPEC, outs),
        scratch_shapes=list(scratch_shapes),
        compiler_params=pltpu.CompilerParams(vmem_limit_bytes=vmem * 1024 * 1024),
        cost_estimate=pl.CostEstimate(flops=flops, bytes_accessed=1 << 18, transcendentals=0),
    )(*scalars, *arrays)


def swap(array, axis, partner):
    return lax.ppermute(array, axis, [(i, partner(i)) for i in range(lax.axis_size(axis))])


def exchanged(sums, axis):
    count = lax.axis_size(axis)
    if count == 4:
        return [sums] + [swap(sums, axis, lambda i, by=by: i ^ by) for by in (1, 2, 3)]
    distance = 1
    while distance < count:
        more = swap(sums, axis, lambda i, by=distance: i ^ by)
        sums = call(add_kernel, jax.ShapeDtypeStruct(sums.shape, F32), (), (sums, more))
        distance *= 2
    return [sums]


def collected(state, axis, before, after):
    count = lax.axis_size(axis)
    if count == 4:
        return [state, swap(state, axis, lambda i: (i + 1) % 4), swap(state, axis, lambda i: (2, 3, 1, 0)[i]), before, after]
    return [state] + [swap(state, axis, lambda i, by=by: (i + by) % count) for by in range(1, count)] + [before, after]


def local(
    disp,
    veloc,
    time_step,
    reset_flags,
    climb,
    species,
    neighbours,
    counts,
    lattice,
    embed,
    radial_weight,
    mix_weight,
    update_weight,
    readout,
):
    atoms = disp.shape[2]
    images = lax.axis_size("img")
    domains = lax.axis_size("dom")
    assert disp.shape[0] == 1 and atoms == SLAB_BLOCKS * LANES and domains >= 4
    assert domains & (domains - 1) == 0 and images & (images - 1) == 0
    shape = jax.ShapeDtypeStruct
    x = jnp.transpose(disp, (1, 0, 2))
    v = jnp.transpose(veloc, (1, 0, 2))
    small = (x, v, species, neighbours, counts, embed, readout, radial_weight, mix_weight, update_weight)
    sent, kept_pack = call(
        pack_kernel,
        (shape((PACK_ROWS, atoms), F32), shape((OWN_ROWS, atoms), F32)),
        (),
        (*small, jnp.transpose(lattice, (1, 0, 2))),
        [pltpu.VMEM(a.shape, a.dtype) for a in small] + [pltpu.SemaphoreType.DMA((16,))],
        spec=HBM_SPEC,
        vmem=63,
    )
    sibling = swap(sent, "dom", lambda i: i ^ 1)
    across = swap(sent, "dom", lambda i: (i + 2 * (i % 2) - 1) % domains)
    own_hot, *weights, x_copy, pack = call(
        prepare_kernel,
        (
            shape((SLAB_BLOCKS, 3 * LANES, SLOTS * LANES), BF16),
            shape((CHANNELS, 48), BF16),
            shape((CHANNELS, 192), BF16),
            shape((CHANNELS, 32), BF16),
            shape((CHANNELS, 3 * LANES), BF16),
            shape((16, 192), BF16),
            shape((4, CHANNELS, LANES), F32),
            shape(x.shape, F32),
            shape(sent.shape, F32),
        ),
        (),
        (kept_pack,),
        flops=100000000,
    )
    before = swap(x_copy, "img", lambda i: (i + 1) % images)
    after = swap(x_copy, "img", lambda i: (i - 1) % images)
    force_scratch = forward_scratch() + [pltpu.VMEM(*one) for one in kept_shapes()] + back_scratch()
    force, left, right, side_hot = call(
        first_kernel,
        (
            shape((3, atoms), F32),
            shape(sent.shape, F32),
            shape(sent.shape, F32),
            shape((SIDE_ROWS, SLOTS * LANES), BF16),
        ),
        (),
        (sibling, pack, across, own_hot, *weights),
        force_scratch,
        flops=1000000000,
    )
    message, sums = call(
        functools.partial(blend_kernel, images),
        (shape((8, atoms), F32), shape((8, LANES), F32)),
        (),
        (force, pack, before, after),
    )
    far = swap(message, "dom", lambda i: (i + 2 * (i % 2) - 1) % domains)
    if domains == 4:
        parts = [sums, swap(sums, "dom", lambda i: i ^ 2)]
    else:
        parts = exchanged(sums, "dom")
    near = swap(message, "dom", lambda i: i ^ 1)
    numbers = call(number_kernel, shape((8, LANES), F32), (time_step, jnp.transpose(reset_flags), climb), ())
    state, record = call(
        functools.partial(second_kernel, images, domains),
        (shape((1, 40, LANES), F32), shape((3, LANES), F32)),
        (),
        (numbers, left, pack, right, message, near, far, *parts, own_hot, side_hot, *weights),
        force_scratch,
        flops=1000000000,
    )
    rows = 8 * ((images + 7) // 8)
    sums, extra = call(
        functools.partial(gram_kernel, images),
        (shape((rows, LANES), F32), shape((16 + 3 * rows, LANES), F32)),
        (),
        collected(state, "img", before, after),
        [pltpu.VMEM((images, 40, LANES), F32)],
    )
    new_x, new_v, records, path = call(
        functools.partial(final_kernel, images, atoms * domains),
        (shape(x.shape, F32), shape(x.shape, F32), shape((2, 1, 2), F32), shape((1, 1), F32)),
        (),
        (state, record, extra, *exchanged(sums, "dom")),
    )
    return (
        jnp.transpose(new_x, (1, 0, 2)),
        jnp.transpose(new_v, (1, 0, 2)),
        jnp.transpose(records, (0, 2, 1)),
        path.reshape(1),
    )


def solution(mesh):
    in_specs = (
        P(("group", "img"), None, "dom"),
        P(("group", "img"), None, "dom"),
        P(("group", "img")),
        P(None, ("group", "img")),
        P("group"),
        P(("group", "dom")),
        P(None, ("group", "dom")),
        P(("group", "dom")),
        P(None, None, ("group", "dom")),
        P(),
        P(),
        P(),
        P(),
        P(),
    )
    out_specs = (
        P(("group", "img"), None, "dom"),
        P(("group", "img"), None, "dom"),
        P(None, None, ("group", "img")),
        P(("group", "img")),
    )
    return jax.shard_map(local, mesh=mesh, in_specs=in_specs, out_specs=out_specs, check_vma=False)
```

```python
import functools
import math

import jax
import jax.numpy as jnp
from jax import lax
from jax.experimental import pallas as pl
from jax.experimental.pallas import tpu as pltpu
from jax.sharding import PartitionSpec as P

F32 = jnp.float32
BF16 = jnp.bfloat16
PRECISE = lax.Precision.HIGHEST
SPRING_CONSTANT = 0.5
ALPHA_START = 0.1
STEP_LIMIT = 0.3
TINY_VALUE = 1e-06
SOFTENING = 0.25
LANES = 128
SLOTS = 8
BASIS = 8
CHANNELS = 64
SLAB_BLOCKS = 4
ROW_X = 32
ROW_COUNT = 35
ROW_KIND = 36
ROW_V = 37
PACK_ROWS = 40
OWN_ROWS = PACK_ROWS + CHANNELS + BASIS
NT = (((1,), (1,)), ((), ()))


def split(x):
    high = x.astype(BF16).astype(F32)
    return high, x - high


def left_stack(w):
    high, low = split(w)
    return jnp.concatenate([high, high, low], axis=1)


def right_stack(x):
    high, low = split(x)
    high = high.astype(BF16)
    return jnp.concatenate([high, low.astype(BF16), high], axis=0)


def pair_stack(x):
    high, low = split(x)
    return jnp.concatenate([high.astype(BF16), low.astype(BF16)], axis=0)


def mm(a, b):
    return jnp.dot(a, b, preferred_element_type=F32)


def mm_nt(a, b):
    return lax.dot_general(a, b, NT, preferred_element_type=F32)


def pack_kernel(*refs):
    sources, (out_ref, own_ref), held, sems = refs[:11], refs[11:13], refs[13:23], refs[23]
    lattice = sources[10]
    pairs = list(zip(sources, held))
    for c in range(3):
        rows = pl.ds(8 + 8 * c, 8)
        pairs += [(lattice.at[c], out_ref.at[rows]), (lattice.at[c], own_ref.at[rows])]
    copies = [pltpu.make_async_copy(a, b, sems.at[i]) for i, (a, b) in enumerate(pairs)]
    for one in copies:
        one.start()
    for one in copies:
        one.wait()
    x, v, species, nbr, counts, embed, readout, radial, mix, update = held
    for ref in (out_ref, own_ref):
        ref[0:8, :] = nbr[...].astype(F32)
        for c in range(3):
            ref[ROW_X + c : ROW_X + c + 1, :] = x[c]
            ref[ROW_V + c : ROW_V + c + 1, :] = v[c]
        ref[ROW_COUNT : ROW_COUNT + 1, :] = counts[...].astype(F32).reshape(1, -1)
        ref[ROW_KIND : ROW_KIND + 1, :] = species[...].astype(F32).reshape(1, -1)
    top, low = PACK_ROWS, PACK_ROWS + CHANNELS
    for i, value in enumerate([mix[0], mix[1], update[0], update[1]]):
        own_ref[top:low, i * LANES : i * LANES + CHANNELS] = value
    for i, value in enumerate([radial[0], radial[1], embed[...], readout[...].reshape(1, CHANNELS)]):
        own_ref[low : low + value.shape[0], i * LANES : i * LANES + CHANNELS] = value


def prepare_kernel(po_ref, *rest):
    own_hot, l1_ref, l2_ref, l3_ref, l5_ref, l6_ref, col_ref, copy_ref, pack_ref = rest
    pack_ref[...] = po_ref[0:PACK_ROWS, :]
    for b in range(SLAB_BLOCKS):
        mark(window_index(po_ref, b), [0, 1, 2], own_hot.at[b])
    for c in range(3):
        copy_ref[c] = po_ref[ROW_X + c : ROW_X + c + 1, :]

    def raw(first, count, i):
        return po_ref[first : first + count, i * LANES : i * LANES + CHANNELS]

    low = PACK_ROWS + CHANNELS
    mix_ref = [raw(PACK_ROWS, CHANNELS, i) for i in range(2)]
    update_ref = [raw(PACK_ROWS, CHANNELS, 2 + i) for i in range(2)]
    radial_ref = [raw(low, BASIS, i) for i in range(2)]
    embed_ref, readout = raw(low, 2, 2), raw(low, 1, 3)
    eye = (
        lax.broadcasted_iota(jnp.int32, (CHANNELS, CHANNELS), 0)
        == lax.broadcasted_iota(jnp.int32, (CHANNELS, CHANNELS), 1)
    ).astype(F32)

    def turned(x):
        return lax.dot_general(eye, x, NT, precision=PRECISE, preferred_element_type=F32)

    base0 = embed_ref[0:1, :]
    base1 = embed_ref[1:2, :] - base0
    rows = jnp.concatenate([base0, base1], axis=0)
    sent = jnp.dot(rows, mix_ref[0], precision=PRECISE, preferred_element_type=F32)
    scale = 1.0 / math.sqrt(SLOTS)
    first = jnp.concatenate([radial_ref[0] * sent[0:1], radial_ref[0] * sent[1:2]], axis=0) * scale
    second = radial_ref[1] * scale
    folded = jnp.dot(update_ref[0], mix_ref[1], precision=PRECISE, preferred_element_type=F32)
    mix_t = turned(mix_ref[1])
    l1_ref[...] = left_stack(turned(first)).astype(BF16)
    l2_ref[...] = left_stack(turned(folded)).astype(BF16)
    high, low = split(turned(second))
    l3_ref[...] = jnp.concatenate([high, high, low, jnp.zeros_like(high)], axis=1).astype(BF16)
    high, low = split(folded)
    l5_ref[...] = jnp.concatenate([high, high, high, high, low, low], axis=1).astype(BF16)
    l6_ref[...] = left_stack(first).astype(BF16)
    wide = (CHANNELS, LANES)
    col_ref[0] = jnp.broadcast_to(jnp.sum(mix_t * base0, axis=1, keepdims=True), wide)
    col_ref[1] = jnp.broadcast_to(jnp.sum(mix_t * base1, axis=1, keepdims=True), wide)
    col_ref[2] = jnp.broadcast_to(jnp.sum(update_ref[0] * readout, axis=1, keepdims=True), wide)
    col_ref[3] = jnp.broadcast_to(jnp.sum(update_ref[1] * readout, axis=1, keepdims=True), wide)


def sin_cos(t):
    q = t * t
    s = -1.0 / 39916800.0
    for c in (1.0 / 362880.0, -1.0 / 5040.0, 1.0 / 120.0, -1.0 / 6.0, 1.0):
        s = s * q + c
    k = 1.0 / 479001600.0
    for c in (-1.0 / 3628800.0, 1.0 / 40320.0, -1.0 / 720.0, 1.0 / 24.0, -0.5, 1.0):
        k = k * q + c
    return s * t, k


def wide_row(x, row):
    return jnp.broadcast_to(x[row : row + 1, :], (8, x.shape[1]))


def silu_parts(m):
    sig = 1.0 / (1.0 + jnp.exp(-m))
    return m * sig, sig * (1.0 + m * (1.0 - sig))


def pick(values, lanes):
    return jnp.take_along_axis(values, lanes, axis=1, mode="promise_in_bounds")


def reach(b, first, last):
    return [w for w in range(3) if first <= b - 1 + w <= last]


SIDE_START = {2: 0, 3: LANES, 8: 3 * LANES, 9: 5 * LANES}
SIDE_ROWS = 6 * LANES


def mark(index, ws, target):
    count = len(ws) * LANES
    row_id = (lax.broadcasted_iota(jnp.int32, (count, LANES), 0) + ws[0] * LANES).astype(jnp.int16)
    one, zero = jnp.ones((count, LANES), BF16), jnp.zeros((count, LANES), BF16)
    for k in range(SLOTS):
        wanted = jnp.broadcast_to(index[k : k + 1, :], (16, LANES)).astype(jnp.int16)
        wanted = jnp.concatenate([wanted] * (count // 16), axis=0)
        target[:, k * LANES : (k + 1) * LANES] = jnp.where(row_id == wanted, one, zero)


def window_index(pack, b):
    lanes = slice((b % 4) * LANES, (b % 4 + 1) * LANES)
    return pack[0:8, lanes].astype(jnp.int32) - LANES * (b % 4)


def mark_sides(packs, side):
    for b, start in SIDE_START.items():
        ws = reach(b, 3, 8)
        mark(window_index(packs[b // 4], b), ws, side.at[start : start + len(ws) * LANES])


def forward_parts(packs, weights, xs, sst, kept):
    l1, l2, l3, l5, l6, col = weights
    (widx, kinds, geo, bst, bps, bpr, sent_all, sent_pair, slope) = kept
    centre = 2.0 + 0.5 * lax.broadcasted_iota(jnp.int32, (BASIS, LANES), 0).astype(F32)
    slot = lax.broadcasted_iota(jnp.int32, (SLOTS, LANES), 0)

    def part_rows(value):
        high, low = split(value)
        return jnp.concatenate([high, low], axis=0).astype(BF16)

    def pairs(b):
        pack = packs[b // 4]
        lanes = slice((b % 4) * LANES, (b % 4 + 1) * LANES)
        index = window_index(pack, b)
        widx[b] = index
        inner = index & (LANES - 1)
        part = index >> 7

        def taken(row):
            got = [
                pick(jnp.broadcast_to(xs[b - 1 + w, row : row + 1, :], (SLOTS, LANES)), inner)
                for w in range(3)
            ]
            return jnp.where(part == 0, got[0], jnp.where(part == 1, got[1], got[2]))

        vec = [
            pack[8 + 8 * c : 16 + 8 * c, lanes] + taken(c) - jnp.broadcast_to(xs[b, c : c + 1, :], (SLOTS, LANES))
            for c in range(3)
        ]
        kind = taken(3)
        dist = jnp.sqrt(vec[0] * vec[0] + vec[1] * vec[1] + vec[2] * vec[2] + SOFTENING)
        live = (slot.astype(F32) < jnp.broadcast_to(pack[ROW_COUNT : ROW_COUNT + 1, lanes], (SLOTS, LANES))).astype(F32)
        turns = dist * (1.0 / 12.0)
        turns = turns - jnp.floor(turns + 0.5)
        sine, cosine = sin_cos(turns * math.pi)
        envelope = cosine * cosine * live
        slant = cosine * sine * live * (-math.pi / 6.0)
        if 3 <= b <= 8:
            kinds[b] = kind
            for c in range(3):
                geo[b, c] = vec[c]
            geo[b, 3] = 1.0 / dist
        total = jnp.zeros((BASIS, LANES), F32)
        total_kind = jnp.zeros((BASIS, LANES), F32)
        for k in range(SLOTS):
            away = wide_row(dist, k) - centre
            gauss = jnp.exp(-4.0 * (away * away))
            env_k = wide_row(envelope, k)
            value = gauss * env_k
            total = total + value
            total_kind = total_kind + value * wide_row(kind, k)
            cols = slice(k * LANES, (k + 1) * LANES)
            if 2 <= b <= 9:
                bst[b, :, cols] = part_rows(value)
            if 3 <= b <= 8:
                value = gauss * (wide_row(slant, k) - 8.0 * away * env_k)
                bpr[b, :, cols] = value
                bps[b, :, cols] = part_rows(value)
        high, low = split(jnp.concatenate([total, total_kind], axis=0))
        sst[:, b * LANES : (b + 1) * LANES] = jnp.concatenate([high, low, high], axis=0).astype(BF16)

    for b in range(1, 11):
        pairs(b)

    for b in range(1, 11, 2):
        cols = slice(b * LANES, (b + 2) * LANES)
        value, steep = silu_parts(mm(l1[...], sst[:, cols]))
        sent = mm(l2[...], right_stack(value))
        for i in range(2):
            one = sent[:, i * LANES : (i + 1) * LANES]
            one = one + col[0] + col[1] * jnp.broadcast_to(xs[b + i, 3:4, :], (CHANNELS, LANES))
            sent_all[:, (b + i) * LANES : (b + i + 1) * LANES] = one
            if 3 <= b + i <= 8:
                sent_pair[:, (b + i) * LANES : (b + i + 1) * LANES] = pair_stack(one)
        slope[:, cols] = steep


def force_parts(weights, own_hot, side_hot, kept, dg, pulls, met, acc, held):
    l1, l2, l3, l5, l6, col = weights
    (widx, kinds, geo, bst, bps, bpr, sent_all, sent_pair, slope) = kept
    slot = lax.broadcasted_iota(jnp.int32, (SLOTS, LANES), 0)

    def marks(b, ws):
        if b in SIDE_START:
            start = SIDE_START[b] + (ws[0] - reach(b, 3, 8)[0]) * LANES
            return side_hot.at[start : start + len(ws) * LANES]
        return own_hot.at[b - 4, ws[0] * LANES : (ws[-1] + 1) * LANES]

    def add_rows(sums, first, b, ws, out):
        for i, w in enumerate(ws):
            target = b - 1 + w
            piece = out[i * LANES : (i + 1) * LANES]
            rows = slice((target - first) * LANES, (target - first + 1) * LANES)
            if (first, target) in started:
                sums[rows, :] += piece
            else:
                sums[rows, :] = piece
                started.add((first, target))

    started = set()

    def block_work(b):
        index = widx[b]
        inner, part = index & (LANES - 1), index >> 7
        basis = bst[b]
        radial = mm(l3[...], jnp.concatenate([basis, basis], axis=0))
        if 3 <= b <= 8:
            basis = bps[b]
            steepness = mm(l3[...], jnp.concatenate([basis, basis], axis=0))
        lanes = [jnp.broadcast_to(inner[k : k + 1, :], (16, LANES)) for k in range(SLOTS)]
        parts = [jnp.broadcast_to(part[k : k + 1, :], (16, LANES)) for k in range(SLOTS)]
        own = 4 <= b <= 7
        if own:
            found_all = mm(sent_pair[:, (b - 1) * LANES : (b + 2) * LANES], own_hot[b - 4])
        value = held.at[b % 2]
        total = [jnp.zeros((8, LANES), F32)] * SLOTS
        for u in range(CHANNELS // 16):
            rows = slice(16 * u, 16 * u + 16)
            low_rows = slice(CHANNELS + 16 * u, CHANNELS + 16 * u + 16)
            windows = [sent_all[rows, (b - 1 + w) * LANES : (b + w) * LANES] for w in range(3)]
            got = []
            message = jnp.zeros((16, LANES), F32)
            for k in range(SLOTS):
                cols = slice(k * LANES, (k + 1) * LANES)
                if own:
                    got.append(found_all[rows, cols] + found_all[low_rows, cols])
                else:
                    found = [pick(window, lanes[k]) for window in windows]
                    got.append(jnp.where(parts[k] == 0, found[0], jnp.where(parts[k] == 1, found[1], found[2])))
                message = message + radial[rows, cols] * got[k]
            _, steep = silu_parts(message)
            back = col[3, rows] * steep
            for k in range(SLOTS):
                cols = slice(k * LANES, (k + 1) * LANES)
                high, low = split(radial[rows, cols] * back)
                value[rows, cols] = high.astype(BF16)
                value[low_rows, cols] = low.astype(BF16)
                if 3 <= b <= 8:
                    pull = got[k] * back * steepness[rows, cols]
                    total[k] = total[k] + pull[0:8] + pull[8:16]
            yield
        if 3 <= b <= 8:
            for k in range(SLOTS):
                pulls[b, :, k * LANES : (k + 1) * LANES] = total[k]

    def scatter_work(b):
        ws = reach(b, 3, 8)
        chosen, value = marks(b, ws), held.at[b % 2]
        out = None
        for u in range(4):
            cols = slice(u * 2 * LANES, (u + 1) * 2 * LANES)
            one = mm_nt(chosen[:, cols], value[:, cols])
            out = one if out is None else out + one
            yield
        add_rows(dg, 3, b, ws, out)

    def together(*works):
        works = list(works)
        while works:
            works = [work for work in works if next(work, "end") != "end"]

    together(block_work(2))
    for b in range(3, 10):
        together(scatter_work(b - 1), block_work(b))
    together(scatter_work(9))

    def finish(b, sums):
        kind = kinds[b]
        rows = []
        for k in range(SLOTS):
            cols = slice(k * LANES, (k + 1) * LANES)
            weight = sums[0:8] + wide_row(kind, k) * sums[8:16]
            rows.append(jnp.sum(bpr[b, :, cols] * weight + pulls[b, :, cols], axis=0, keepdims=True))
        pull = jnp.concatenate(rows, axis=0) * geo[b, 3]
        pieces = []
        for c in range(3):
            value = pull * geo[b, c]
            if 4 <= b <= 7:
                acc[b - 4, c] = jnp.sum(value, axis=0, keepdims=True)
            pieces.append(split(value))
        lines = []
        for h in range(2):
            for c in range(3):
                lines.append(jnp.concatenate([jnp.where(slot == k, pieces[c][h], 0.0) for k in range(SLOTS)], axis=1))
        ws = reach(b, 4, 7)
        out = mm_nt(jnp.concatenate(lines, axis=0).astype(BF16), marks(b, ws)[...])
        for c in range(3):
            both = out[8 * c : 8 * c + 8] + out[24 + 8 * c : 32 + 8 * c]
            for i, w in enumerate(ws):
                target = b - 5 + w
                piece = both[:, i * LANES : (i + 1) * LANES]
                if (c, target) in met_blocks:
                    met[target, c] += piece
                else:
                    met[target, c] = piece
                    met_blocks.add((c, target))

    met_blocks = set()

    for b in range(3, 9, 2):
        cols = slice(b * LANES, (b + 2) * LANES)
        high, low = split(dg[(b - 3) * LANES : (b - 1) * LANES, :])
        steep = mm_nt(l5[...], jnp.concatenate([high, low, high], axis=1).astype(BF16))
        steep = steep + jnp.concatenate([col[2], col[2]], axis=1)
        sums = mm(l6[...], right_stack(steep * slope[:, cols]))
        for i in range(2):
            finish(b + i, sums[:, i * LANES : (i + 1) * LANES])

    away = []
    for c in range(3):
        back = [acc[i, c] - jnp.sum(met[i, c], axis=0, keepdims=True) for i in range(SLAB_BLOCKS)]
        away.append(jnp.concatenate(back, axis=1))
    return jnp.concatenate(away, axis=0)


def fill_region(xs, packs, rows_of):
    for b in range(12):
        lanes = slice((b % 4) * LANES, (b % 4 + 1) * LANES)
        pack = packs[b // 4]
        xs[b, 0:3, :] = rows_of(b // 4)[:, lanes]
        xs[b, 3:4, :] = pack[ROW_KIND : ROW_KIND + 1, lanes]


def lane_total(x):
    x = x[:, 0:LANES] + x[:, LANES : 2 * LANES] + x[:, 2 * LANES : 3 * LANES] + x[:, 3 * LANES : 4 * LANES]
    return jnp.sum(x, axis=1, keepdims=True)


def dot3(a, b):
    return jnp.sum(a * b, axis=0, keepdims=True)


def kept_shapes():
    wide = 12 * LANES
    return [
        ((12, 8, LANES), jnp.int32),
        ((12, 8, LANES), F32),
        ((12, 4, 8, LANES), F32),
        ((12, 16, SLOTS * LANES), BF16),
        ((12, 16, SLOTS * LANES), BF16),
        ((12, 8, SLOTS * LANES), F32),
        ((CHANNELS, wide), F32),
        ((2 * CHANNELS, wide), BF16),
        ((CHANNELS, wide), F32),
    ]


def forward_scratch():
    return [pltpu.VMEM((12, 8, LANES), F32), pltpu.VMEM((48, 12 * LANES), BF16)]


def back_scratch():
    return [
        pltpu.VMEM((6 * LANES, 2 * CHANNELS), F32),
        pltpu.VMEM((12, 8, SLOTS * LANES), F32),
        pltpu.VMEM((SLAB_BLOCKS, 3, SLOTS, LANES), F32),
        pltpu.VMEM((SLAB_BLOCKS, 3, 1, LANES), F32),
        pltpu.VMEM((2, 2 * CHANNELS, SLOTS * LANES), BF16),
    ]


def by_parity(sibling, across):
    even = jnp.full(sibling.shape, lax.axis_index("dom") % 2, jnp.int32) == 0
    return jnp.where(even, across, sibling), jnp.where(even, sibling, across)


def first_kernel(sibling_ref, po_ref, across_ref, own_hot, *rest):
    weights, (out_ref, pl_ref, pr_ref, side_hot), scr = rest[:6], rest[6:10], rest[10:]
    xs, sst, kept = scr[0], scr[1], scr[2:11]
    pl_ref[...], pr_ref[...] = by_parity(sibling_ref[...], across_ref[...])
    packs = [pl_ref, po_ref, pr_ref]
    mark_sides(packs, side_hot)
    fill_region(xs, packs, lambda s: packs[s][ROW_X : ROW_X + 3, :])
    forward_parts(packs, weights, xs, sst, kept)
    out_ref[...] = force_parts(weights, own_hot, side_hot, kept, *scr[11:])


def rows_of(ref):
    return jnp.concatenate([ref[c] for c in range(3)], axis=0)


def block_row(*values):
    values = list(values) + [jnp.zeros((1, LANES), F32)] * (SLAB_BLOCKS - len(values))
    return jnp.concatenate(values, axis=1)


def blend_kernel(images, force_ref, po_ref, before_ref, after_ref, out_ref, sums_ref):
    x = po_ref[ROW_X : ROW_X + 3, :]
    v = po_ref[ROW_V : ROW_V + 3, :]
    force = force_ref[...]
    here = lax.axis_index("img")
    before = jnp.where(here > 0, rows_of(before_ref), 0.0)
    after = jnp.where(here < images - 1, rows_of(after_ref), 0.0)
    tangent = after - before
    plus = after - x
    minus = x - before
    sums = jnp.concatenate(
        [
            dot3(force, tangent),
            dot3(force, force),
            dot3(tangent, tangent),
            dot3(plus, plus),
            dot3(minus, minus),
            dot3(v, v),
            jnp.zeros((2, x.shape[1]), F32),
        ],
        axis=0,
    )
    sums = jnp.broadcast_to(lane_total(sums), (8, LANES))
    sums_ref[...] = sums
    out_ref[0:3, :] = force
    out_ref[3:6, :] = tangent
    out_ref[6:7, :] = block_row(*[sums[i : i + 1] for i in range(4)])
    out_ref[7:8, :] = block_row(sums[4:5], sums[5:6])


def step_numbers(ft, ff, tt, pp, mn, vv, dt, alpha, flagged, climbing, inside):
    root = jnp.sqrt(tt + TINY_VALUE)
    along = ft / root
    spring = SPRING_CONSTANT * (jnp.sqrt(pp) - jnp.sqrt(mn))
    factor = jnp.where(climbing, -2.0 * along, spring - along)
    band = jnp.maximum(ff + 2.0 * factor * along + factor * factor * (tt / (tt + TINY_VALUE)), 0.0)
    new_dt = jnp.where(flagged, 0.5 * dt, jnp.minimum(1.1 * dt, STEP_LIMIT))
    pull = jnp.where(flagged, 0.0, alpha * jnp.sqrt(vv / (band + TINY_VALUE))) + new_dt
    keep = jnp.where(flagged, 0.0, 1.0 - alpha)
    new_alpha = jnp.where(flagged, ALPHA_START, 0.99 * alpha)
    keep = jnp.where(inside, keep, 0.0)
    pull = jnp.where(inside, pull, 0.0)
    return (
        jnp.where(inside, along, 0.0),
        jnp.where(inside, spring, 0.0),
        keep,
        pull,
        pull * factor / root,
        new_dt,
        new_alpha,
    )


def add_kernel(a_ref, b_ref, out_ref):
    out_ref[...] = a_ref[...] + b_ref[...]


def number_kernel(dt_ref, flag_ref, climb_ref, out_ref):
    flags = [flag_ref[0, s].astype(F32) for s in range(flag_ref.shape[1])]
    for i, value in enumerate([dt_ref[0], climb_ref[0].astype(F32)] + flags):
        out_ref[i : i + 1, :] = jnp.full((1, LANES), value, F32)


def second_kernel(images, domains, number_ref, pl_ref, po_ref, pr_ref, own_ref, near_ref, far_ref, *rest):
    count = 2 if domains == 4 else 1
    parts, rest = rest[:count], rest[count:]
    (own_hot, side_hot), weights, (out_ref, record_ref), scr = rest[:2], rest[2:8], rest[8:10], rest[10:]
    packs = [pl_ref, po_ref, pr_ref]
    here = lax.axis_index("img")
    sums = parts[0][...]
    if domains == 4:
        sums = sums + parts[1][...]
    got = [sums[i : i + 1, :] for i in range(6)]
    if domains == 4:
        for one in (near_ref, far_ref):
            for i in range(6):
                got[i] = got[i] + one[6 + i // 4 : 7 + i // 4, (i % 4) * LANES : (i % 4 + 1) * LANES]
    ft, ff, tt, pp, mn, vv = got
    beside = by_parity(near_ref[0:6, :], far_ref[0:6, :])
    shape = (1, LANES)
    along, spring, keep, pull, side, dt, alpha = step_numbers(
        ft,
        ff,
        tt,
        pp,
        mn,
        vv,
        number_ref[0:1, :],
        jnp.full(shape, ALPHA_START, F32),
        number_ref[2:3, :] == 1.0,
        number_ref[1:2, :] == jnp.full(shape, here, jnp.int32).astype(F32),
        jnp.full(shape, jnp.where((here >= 1) & (here <= images - 2), 1, 0), jnp.int32) == 1,
    )
    messages = [beside[0], own_ref[0:6, :], beside[1]]

    def wide(s):
        return jnp.concatenate([s] * SLAB_BLOCKS, axis=1)

    speeds = [
        wide(keep) * p[ROW_V : ROW_V + 3, :] + wide(pull) * m[0:3, :] + wide(side) * m[3:6, :]
        for p, m in zip(packs, messages)
    ]
    moved = [p[ROW_X : ROW_X + 3, :] + wide(dt) * s for p, s in zip(packs, speeds)]
    xs, sst, kept = scr[0], scr[1], scr[2:11]
    fill_region(xs, packs, lambda s: moved[s])
    forward_parts(packs, weights, xs, sst, kept)
    force = force_parts(weights, own_hot, side_hot, kept, *scr[11:])
    for c in range(3):
        for i in range(SLAB_BLOCKS):
            lanes = slice(i * LANES, (i + 1) * LANES)
            row = 4 * c + i
            out_ref[0, row : row + 1, :] = speeds[1][c : c + 1, lanes]
            out_ref[0, 12 + row : 13 + row, :] = force[c : c + 1, lanes]
            out_ref[0, 24 + row : 25 + row, :] = moved[1][c : c + 1, lanes]
    out_ref[0, 36:37, :] = dt
    out_ref[0, 37:38, :] = alpha
    out_ref[0, 38:40, :] = jnp.broadcast_to(number_ref[3:4, :], (2, LANES))
    record_ref[0:1, :] = along
    record_ref[1:2, :] = spring
    record_ref[2:3, :] = number_ref[1:2, :]


PRODUCTS = (
    [("f", "t"), ("f", "f"), ("t", "t"), ("p", "p"), ("d", "d"), ("v", "v")]
    + [("d", "v"), ("d", "f"), ("d", "t"), ("d", "V"), ("d", "F"), ("d", "T"), ("v", "f"), ("v", "t")]
    + [(a, b) for a in "vft" for b in "VFT"]
)


def gram_kernel(images, *refs):
    parts, (before_ref, after_ref), (out_ref, state_ref, messages_ref) = refs[:-5], refs[-5:-3], refs[-3:]
    rows = out_ref.shape[0]
    here = lax.axis_index("img")
    if images == 4:
        places = [here, lax.rem(here + 3, 4), jnp.where(here < 2, 3 - here, here - 2)]
        messages_ref[...] = jnp.zeros(messages_ref.shape, F32)
        for place, beside in [(lax.rem(here + 3, 4), before_ref), (lax.rem(here + 1, 4), after_ref)]:
            for c in range(3):
                for i in range(SLAB_BLOCKS):
                    row = 24 + 4 * c + i
                    messages_ref[place, row : row + 1, :] = beside[c][:, i * LANES : (i + 1) * LANES]
    else:
        places = [lax.rem(here + images - s, images) for s in range(images)]
    for place, part in zip(places, parts):
        messages_ref[place] = part[0]
    blank = [jnp.zeros((rows - images, LANES), F32)] if rows > images else []
    zero = jnp.zeros((1, LANES), F32)

    def gathered(row):
        return jnp.concatenate([messages_ref[i, row : row + 1, :] for i in range(images)] + blank, axis=0)

    def earlier(value):
        return jnp.concatenate([zero, value[0 : rows - 1]], axis=0)

    def later(value):
        return jnp.concatenate([value[1:images], zero] + blank, axis=0)

    number = lax.broadcasted_iota(jnp.int32, (rows, LANES), 0)
    held = number < images
    totals = [jnp.zeros((rows, LANES), F32) for _ in PRODUCTS]
    for row in range(3 * SLAB_BLOCKS):
        v, f, x = gathered(row), gathered(12 + row), gathered(24 + row)
        before = jnp.where(held, earlier(x), 0.0)
        after = later(x)
        t = after - before
        table = {"f": f, "v": v, "t": t, "p": after - x, "d": x - before}
        table["F"], table["V"], table["T"] = earlier(f), earlier(v), earlier(t)
        totals = [old + table[a] * table[b] for old, (a, b) in zip(totals, PRODUCTS)]
        state_ref[row : row + 1, :] = jnp.sum(jnp.where(number == here, t, 0.0), axis=0, keepdims=True)
    lane = lax.broadcasted_iota(jnp.int32, (rows, LANES), 1)
    result = jnp.zeros((rows, LANES), F32)
    for q, one in enumerate(totals):
        one = jnp.broadcast_to(jnp.sum(one, axis=1, keepdims=True), (rows, LANES))
        result = jnp.where(lane == q, one, result)
    out_ref[...] = result
    for i in range(3):
        state_ref[16 + rows * i : 16 + rows * (i + 1), :] = gathered(36 + i)


def final_kernel(images, atoms, own_ref, record_ref, state_ref, *rest):
    parts, (x_ref, v_ref, band_ref, path_ref) = rest[:-4], rest[-4:]
    rows = parts[0].shape[0]
    here = lax.axis_index("img")
    sums = parts[0][...]
    for one in parts[1:]:
        sums = sums + one[...]
    got = {
        pair: jnp.broadcast_to(sums[:, q : q + 1], (rows, LANES)) for q, pair in enumerate(PRODUCTS)
    }
    number = lax.broadcasted_iota(jnp.int32, (rows, LANES), 0)
    inside = (number >= 1) & (number <= images - 2)
    climb = jnp.broadcast_to(record_ref[2:3, :], (rows, LANES))
    dt0, alpha0, flag = (state_ref[16 + rows * i : 16 + rows * (i + 1), :] for i in range(3))
    along, spring, keep, pull, side, dt, _ = step_numbers(
        got["f", "t"],
        got["f", "f"],
        got["t", "t"],
        got["p", "p"],
        got["d", "d"],
        got["v", "v"],
        dt0,
        alpha0,
        flag == 1.0,
        number.astype(F32) == climb,
        inside,
    )

    def shifted(value):
        return jnp.concatenate([jnp.zeros((1, LANES), F32), value[0 : rows - 1]], axis=0)

    now = {"v": dt * keep, "f": dt * pull, "t": dt * side}
    old = {a.upper(): shifted(value) for a, value in now.items()}
    mine = now["v"] * now["v"] * got["v", "v"] + now["f"] * now["f"] * got["f", "f"]
    mine = mine + now["t"] * now["t"] * got["t", "t"]
    cross = now["v"] * now["f"] * got["v", "f"] + now["v"] * now["t"] * got["v", "t"]
    mine = mine + 2.0 * (cross + now["f"] * now["t"] * got["f", "t"])
    both = jnp.zeros((rows, LANES), F32)
    for a in "vft":
        both = both + now[a] * got["d", a]
    for b in "VFT":
        both = both - old[b] * got["d", b]
    for a in "vft":
        for b in "VFT":
            both = both - now[a] * old[b] * got[a, b]
    squared = got["d", "d"] + mine + shifted(mine) + 2.0 * both
    segment = jnp.sqrt(jnp.maximum(squared, 0.0) * (1.0 / (3.0 * atoms)))
    path = jnp.sum(jnp.where(number <= here, segment, 0.0), axis=0, keepdims=True)
    path_ref[...] = path[:, 0:1]
    keep, pull, side, dt, along, spring = (
        jnp.sum(jnp.where(number == here, value, 0.0), axis=0, keepdims=True)
        for value in (keep, pull, side, dt, along, spring)
    )

    for c in range(3):
        speeds, places = [], []
        for i in range(SLAB_BLOCKS):
            row = 4 * c + i
            speed = keep * own_ref[0, row : row + 1, :] + pull * own_ref[0, 12 + row : 13 + row, :]
            speed = speed + side * state_ref[row : row + 1, :]
            speeds.append(speed)
            places.append(own_ref[0, 24 + row : 25 + row, :] + dt * speed)
        v_ref[c] = jnp.concatenate(speeds, axis=1)
        x_ref[c] = jnp.concatenate(places, axis=1)
    band_ref[0] = jnp.concatenate([record_ref[0:1, 0:1], record_ref[1:2, 0:1]], axis=1)
    band_ref[1] = jnp.concatenate([along[:, 0:1], spring[:, 0:1]], axis=1)


VMEM_SPEC = pl.BlockSpec(memory_space=pltpu.VMEM)
SMEM_SPEC = pl.BlockSpec(memory_space=pltpu.SMEM)
HBM_SPEC = pl.BlockSpec(memory_space=pltpu.HBM)


def call(body, outs, scalars, arrays, scratch_shapes=(), flops=0, spec=VMEM_SPEC, vmem=24):
    return pl.pallas_call(
        body,
        out_shape=outs,
        in_specs=[SMEM_SPEC] * len(scalars) + [spec] * len(arrays),
        out_specs=jax.tree.map(lambda _: VMEM_SPEC, outs),
        scratch_shapes=list(scratch_shapes),
        compiler_params=pltpu.CompilerParams(vmem_limit_bytes=vmem * 1024 * 1024),
        cost_estimate=pl.CostEstimate(flops=flops, bytes_accessed=1 << 18, transcendentals=0),
    )(*scalars, *arrays)


def swap(array, axis, partner):
    return lax.ppermute(array, axis, [(i, partner(i)) for i in range(lax.axis_size(axis))])


def exchanged(sums, axis):
    count = lax.axis_size(axis)
    if count == 4:
        return [sums] + [swap(sums, axis, lambda i, by=by: i ^ by) for by in (2, 1, 3)]
    distance = 1
    while distance < count:
        more = swap(sums, axis, lambda i, by=distance: i ^ by)
        sums = call(add_kernel, jax.ShapeDtypeStruct(sums.shape, F32), (), (sums, more))
        distance *= 2
    return [sums]


def collected(state, axis, before, after):
    count = lax.axis_size(axis)
    if count == 4:
        return [state, swap(state, axis, lambda i: (i + 1) % 4), swap(state, axis, lambda i: (2, 3, 1, 0)[i]), before, after]
    return [state] + [swap(state, axis, lambda i, by=by: (i + by) % count) for by in range(1, count)] + [before, after]


def local(
    disp,
    veloc,
    time_step,
    reset_flags,
    climb,
    species,
    neighbours,
    counts,
    lattice,
    embed,
    radial_weight,
    mix_weight,
    update_weight,
    readout,
):
    atoms = disp.shape[2]
    images = lax.axis_size("img")
    domains = lax.axis_size("dom")
    assert disp.shape[0] == 1 and atoms == SLAB_BLOCKS * LANES and domains >= 4
    assert domains & (domains - 1) == 0 and images & (images - 1) == 0
    shape = jax.ShapeDtypeStruct
    x = jnp.transpose(disp, (1, 0, 2))
    v = jnp.transpose(veloc, (1, 0, 2))
    small = (x, v, species, neighbours, counts, embed, readout, radial_weight, mix_weight, update_weight)
    sent, kept_pack = call(
        pack_kernel,
        (shape((PACK_ROWS, atoms), F32), shape((OWN_ROWS, atoms), F32)),
        (),
        (*small, jnp.transpose(lattice, (1, 0, 2))),
        [pltpu.VMEM(a.shape, a.dtype) for a in small] + [pltpu.SemaphoreType.DMA((16,))],
        spec=HBM_SPEC,
        vmem=63,
    )
    sibling = swap(sent, "dom", lambda i: i ^ 1)
    across = swap(sent, "dom", lambda i: (i + 2 * (i % 2) - 1) % domains)
    own_hot, *weights, x_copy, pack = call(
        prepare_kernel,
        (
            shape((SLAB_BLOCKS, 3 * LANES, SLOTS * LANES), BF16),
            shape((CHANNELS, 48), BF16),
            shape((CHANNELS, 192), BF16),
            shape((CHANNELS, 32), BF16),
            shape((CHANNELS, 3 * LANES), BF16),
            shape((16, 192), BF16),
            shape((4, CHANNELS, LANES), F32),
            shape(x.shape, F32),
            shape(sent.shape, F32),
        ),
        (),
        (kept_pack,),
        flops=100000000,
    )
    before = swap(x_copy, "img", lambda i: (i + 1) % images)
    after = swap(x_copy, "img", lambda i: (i - 1) % images)
    force_scratch = forward_scratch() + [pltpu.VMEM(*one) for one in kept_shapes()] + back_scratch()
    force, left, right, side_hot = call(
        first_kernel,
        (
            shape((3, atoms), F32),
            shape(sent.shape, F32),
            shape(sent.shape, F32),
            shape((SIDE_ROWS, SLOTS * LANES), BF16),
        ),
        (),
        (sibling, pack, across, own_hot, *weights),
        force_scratch,
        flops=1000000000,
    )
    message, sums = call(
        functools.partial(blend_kernel, images),
        (shape((8, atoms), F32), shape((8, LANES), F32)),
        (),
        (force, pack, before, after),
    )
    far = swap(message, "dom", lambda i: (i + 2 * (i % 2) - 1) % domains)
    if domains == 4:
        parts = [sums, swap(sums, "dom", lambda i: i ^ 2)]
    else:
        parts = exchanged(sums, "dom")
    near = swap(message, "dom", lambda i: i ^ 1)
    numbers = call(number_kernel, shape((8, LANES), F32), (time_step, jnp.transpose(reset_flags), climb), ())
    state, record = call(
        functools.partial(second_kernel, images, domains),
        (shape((1, 40, LANES), F32), shape((3, LANES), F32)),
        (),
        (numbers, left, pack, right, message, near, far, *parts, own_hot, side_hot, *weights),
        force_scratch,
        flops=1000000000,
    )
    rows = 8 * ((images + 7) // 8)
    sums, extra = call(
        functools.partial(gram_kernel, images),
        (shape((rows, LANES), F32), shape((16 + 3 * rows, LANES), F32)),
        (),
        collected(state, "img", before, after),
        [pltpu.VMEM((images, 40, LANES), F32)],
    )
    new_x, new_v, records, path = call(
        functools.partial(final_kernel, images, atoms * domains),
        (shape(x.shape, F32), shape(x.shape, F32), shape((2, 1, 2), F32), shape((1, 1), F32)),
        (),
        (state, record, extra, *exchanged(sums, "dom")),
    )
    return (
        jnp.transpose(new_x, (1, 0, 2)),
        jnp.transpose(new_v, (1, 0, 2)),
        jnp.transpose(records, (0, 2, 1)),
        path.reshape(1),
    )


def solution(mesh):
    in_specs = (
        P(("group", "img"), None, "dom"),
        P(("group", "img"), None, "dom"),
        P(("group", "img")),
        P(None, ("group", "img")),
        P("group"),
        P(("group", "dom")),
        P(None, ("group", "dom")),
        P(("group", "dom")),
        P(None, None, ("group", "dom")),
        P(),
        P(),
        P(),
        P(),
        P(),
    )
    out_specs = (
        P(("group", "img"), None, "dom"),
        P(("group", "img"), None, "dom"),
        P(None, None, ("group", "img")),
        P(("group", "img")),
    )
    return jax.shard_map(local, mesh=mesh, in_specs=in_specs, out_specs=out_specs, check_vma=False)
```

```python
import functools
import math

import jax
import jax.numpy as jnp
from jax import lax
from jax.experimental import pallas as pl
from jax.experimental.pallas import tpu as pltpu
from jax.sharding import PartitionSpec as P

F32 = jnp.float32
BF16 = jnp.bfloat16
PRECISE = lax.Precision.HIGHEST
SPRING_CONSTANT = 0.5
ALPHA_START = 0.1
STEP_LIMIT = 0.3
TINY_VALUE = 1e-06
SOFTENING = 0.25
LANES = 128
SLOTS = 8
BASIS = 8
CHANNELS = 64
SLAB_BLOCKS = 4
ROW_X = 32
ROW_COUNT = 35
ROW_KIND = 36
ROW_V = 37
PACK_ROWS = 40
OWN_ROWS = PACK_ROWS + CHANNELS + BASIS
NT = (((1,), (1,)), ((), ()))


def split(x):
    high = x.astype(BF16).astype(F32)
    return high, x - high


def left_stack(w):
    high, low = split(w)
    return jnp.concatenate([high, high, low], axis=1)


def right_stack(x):
    high, low = split(x)
    high = high.astype(BF16)
    return jnp.concatenate([high, low.astype(BF16), high], axis=0)


def pair_stack(x):
    high, low = split(x)
    return jnp.concatenate([high.astype(BF16), low.astype(BF16)], axis=0)


def mm(a, b):
    return jnp.dot(a, b, preferred_element_type=F32)


def mm_nt(a, b):
    return lax.dot_general(a, b, NT, preferred_element_type=F32)


def pack_kernel(*refs):
    sources, (out_ref, own_ref), held, sems = refs[:11], refs[11:13], refs[13:23], refs[23]
    lattice = sources[10]
    pairs = list(zip(sources, held))
    for c in range(3):
        rows = pl.ds(8 + 8 * c, 8)
        pairs += [(lattice.at[c], out_ref.at[rows]), (lattice.at[c], own_ref.at[rows])]
    copies = [pltpu.make_async_copy(a, b, sems.at[i]) for i, (a, b) in enumerate(pairs)]
    for one in copies:
        one.start()
    for one in copies:
        one.wait()
    x, v, species, nbr, counts, embed, readout, radial, mix, update = held
    for ref in (out_ref, own_ref):
        ref[0:8, :] = nbr[...].astype(F32)
        for c in range(3):
            ref[ROW_X + c : ROW_X + c + 1, :] = x[c]
            ref[ROW_V + c : ROW_V + c + 1, :] = v[c]
        ref[ROW_COUNT : ROW_COUNT + 1, :] = counts[...].astype(F32).reshape(1, -1)
        ref[ROW_KIND : ROW_KIND + 1, :] = species[...].astype(F32).reshape(1, -1)
    top, low = PACK_ROWS, PACK_ROWS + CHANNELS
    for i, value in enumerate([mix[0], mix[1], update[0], update[1]]):
        own_ref[top:low, i * LANES : i * LANES + CHANNELS] = value
    for i, value in enumerate([radial[0], radial[1], embed[...], readout[...].reshape(1, CHANNELS)]):
        own_ref[low : low + value.shape[0], i * LANES : i * LANES + CHANNELS] = value


def prepare_kernel(po_ref, *rest):
    own_hot, l1_ref, l2_ref, l3_ref, l5_ref, l6_ref, col_ref, copy_ref, pack_ref = rest
    pack_ref[...] = po_ref[0:PACK_ROWS, :]
    for b in range(SLAB_BLOCKS):
        mark(window_index(po_ref, b), [0, 1, 2], own_hot.at[b])
    for c in range(3):
        copy_ref[c] = po_ref[ROW_X + c : ROW_X + c + 1, :]

    def raw(first, count, i):
        return po_ref[first : first + count, i * LANES : i * LANES + CHANNELS]

    low = PACK_ROWS + CHANNELS
    mix_ref = [raw(PACK_ROWS, CHANNELS, i) for i in range(2)]
    update_ref = [raw(PACK_ROWS, CHANNELS, 2 + i) for i in range(2)]
    radial_ref = [raw(low, BASIS, i) for i in range(2)]
    embed_ref, readout = raw(low, 2, 2), raw(low, 1, 3)
    eye = (
        lax.broadcasted_iota(jnp.int32, (CHANNELS, CHANNELS), 0)
        == lax.broadcasted_iota(jnp.int32, (CHANNELS, CHANNELS), 1)
    ).astype(F32)

    def turned(x):
        return lax.dot_general(eye, x, NT, precision=PRECISE, preferred_element_type=F32)

    base0 = embed_ref[0:1, :]
    base1 = embed_ref[1:2, :] - base0
    rows = jnp.concatenate([base0, base1], axis=0)
    sent = jnp.dot(rows, mix_ref[0], precision=PRECISE, preferred_element_type=F32)
    scale = 1.0 / math.sqrt(SLOTS)
    first = jnp.concatenate([radial_ref[0] * sent[0:1], radial_ref[0] * sent[1:2]], axis=0) * scale
    second = radial_ref[1] * scale
    folded = jnp.dot(update_ref[0], mix_ref[1], precision=PRECISE, preferred_element_type=F32)
    mix_t = turned(mix_ref[1])
    l1_ref[...] = left_stack(turned(first)).astype(BF16)
    l2_ref[...] = left_stack(turned(folded)).astype(BF16)
    high, low = split(turned(second))
    l3_ref[...] = jnp.concatenate([high, high, low, jnp.zeros_like(high)], axis=1).astype(BF16)
    high, low = split(folded)
    l5_ref[...] = jnp.concatenate([high, high, high, high, low, low], axis=1).astype(BF16)
    l6_ref[...] = left_stack(first).astype(BF16)
    wide = (CHANNELS, LANES)
    col_ref[0] = jnp.broadcast_to(jnp.sum(mix_t * base0, axis=1, keepdims=True), wide)
    col_ref[1] = jnp.broadcast_to(jnp.sum(mix_t * base1, axis=1, keepdims=True), wide)
    col_ref[2] = jnp.broadcast_to(jnp.sum(update_ref[0] * readout, axis=1, keepdims=True), wide)
    col_ref[3] = jnp.broadcast_to(jnp.sum(update_ref[1] * readout, axis=1, keepdims=True), wide)


def sin_cos(t):
    q = t * t
    s = -1.0 / 39916800.0
    for c in (1.0 / 362880.0, -1.0 / 5040.0, 1.0 / 120.0, -1.0 / 6.0, 1.0):
        s = s * q + c
    k = 1.0 / 479001600.0
    for c in (-1.0 / 3628800.0, 1.0 / 40320.0, -1.0 / 720.0, 1.0 / 24.0, -0.5, 1.0):
        k = k * q + c
    return s * t, k


def wide_row(x, row):
    return jnp.broadcast_to(x[row : row + 1, :], (8, x.shape[1]))


def silu_parts(m):
    sig = 1.0 / (1.0 + jnp.exp(-m))
    return m * sig, sig * (1.0 + m * (1.0 - sig))


def pick(values, lanes):
    return jnp.take_along_axis(values, lanes, axis=1, mode="promise_in_bounds")


def reach(b, first, last):
    return [w for w in range(3) if first <= b - 1 + w <= last]


SIDE_START = {2: 0, 3: LANES, 8: 3 * LANES, 9: 5 * LANES}
SIDE_ROWS = 6 * LANES


def mark(index, ws, target):
    count = len(ws) * LANES
    row_id = (lax.broadcasted_iota(jnp.int32, (count, LANES), 0) + ws[0] * LANES).astype(jnp.int16)
    one, zero = jnp.ones((count, LANES), BF16), jnp.zeros((count, LANES), BF16)
    for k in range(SLOTS):
        wanted = jnp.broadcast_to(index[k : k + 1, :], (16, LANES)).astype(jnp.int16)
        wanted = jnp.concatenate([wanted] * (count // 16), axis=0)
        target[:, k * LANES : (k + 1) * LANES] = jnp.where(row_id == wanted, one, zero)


def window_index(pack, b):
    lanes = slice((b % 4) * LANES, (b % 4 + 1) * LANES)
    return pack[0:8, lanes].astype(jnp.int32) - LANES * (b % 4)


def mark_sides(packs, side):
    for b, start in SIDE_START.items():
        ws = reach(b, 3, 8)
        mark(window_index(packs[b // 4], b), ws, side.at[start : start + len(ws) * LANES])


def forward_parts(packs, weights, xs, sst, kept):
    l1, l2, l3, l5, l6, col = weights
    (widx, kinds, geo, bst, bps, bpr, sent_all, sent_pair, slope) = kept
    centre = 2.0 + 0.5 * lax.broadcasted_iota(jnp.int32, (BASIS, LANES), 0).astype(F32)
    slot = lax.broadcasted_iota(jnp.int32, (SLOTS, LANES), 0)

    def part_rows(value):
        high, low = split(value)
        return jnp.concatenate([high, low], axis=0).astype(BF16)

    def pairs(b):
        pack = packs[b // 4]
        lanes = slice((b % 4) * LANES, (b % 4 + 1) * LANES)
        index = window_index(pack, b)
        widx[b] = index
        inner = index & (LANES - 1)
        part = index >> 7

        def taken(row):
            got = [
                pick(jnp.broadcast_to(xs[b - 1 + w, row : row + 1, :], (SLOTS, LANES)), inner)
                for w in range(3)
            ]
            return jnp.where(part == 0, got[0], jnp.where(part == 1, got[1], got[2]))

        vec = [
            pack[8 + 8 * c : 16 + 8 * c, lanes] + taken(c) - jnp.broadcast_to(xs[b, c : c + 1, :], (SLOTS, LANES))
            for c in range(3)
        ]
        kind = taken(3)
        dist = jnp.sqrt(vec[0] * vec[0] + vec[1] * vec[1] + vec[2] * vec[2] + SOFTENING)
        live = (slot.astype(F32) < jnp.broadcast_to(pack[ROW_COUNT : ROW_COUNT + 1, lanes], (SLOTS, LANES))).astype(F32)
        turns = dist * (1.0 / 12.0)
        turns = turns - jnp.floor(turns + 0.5)
        sine, cosine = sin_cos(turns * math.pi)
        envelope = cosine * cosine * live
        slant = cosine * sine * live * (-math.pi / 6.0)
        if 3 <= b <= 8:
            kinds[b] = kind
            for c in range(3):
                geo[b, c] = vec[c]
            geo[b, 3] = 1.0 / dist
        total = jnp.zeros((BASIS, LANES), F32)
        total_kind = jnp.zeros((BASIS, LANES), F32)
        for k in range(SLOTS):
            away = wide_row(dist, k) - centre
            gauss = jnp.exp(-4.0 * (away * away))
            env_k = wide_row(envelope, k)
            value = gauss * env_k
            total = total + value
            total_kind = total_kind + value * wide_row(kind, k)
            cols = slice(k * LANES, (k + 1) * LANES)
            if 2 <= b <= 9:
                bst[b, :, cols] = part_rows(value)
            if 3 <= b <= 8:
                value = gauss * (wide_row(slant, k) - 8.0 * away * env_k)
                bpr[b, :, cols] = value
                bps[b, :, cols] = part_rows(value)
        high, low = split(jnp.concatenate([total, total_kind], axis=0))
        sst[:, b * LANES : (b + 1) * LANES] = jnp.concatenate([high, low, high], axis=0).astype(BF16)

    for b in range(1, 11):
        pairs(b)

    for b in range(1, 11, 2):
        cols = slice(b * LANES, (b + 2) * LANES)
        value, steep = silu_parts(mm(l1[...], sst[:, cols]))
        sent = mm(l2[...], right_stack(value))
        for i in range(2):
            one = sent[:, i * LANES : (i + 1) * LANES]
            one = one + col[0] + col[1] * jnp.broadcast_to(xs[b + i, 3:4, :], (CHANNELS, LANES))
            sent_all[:, (b + i) * LANES : (b + i + 1) * LANES] = one
            if 3 <= b + i <= 8:
                sent_pair[:, (b + i) * LANES : (b + i + 1) * LANES] = pair_stack(one)
        slope[:, cols] = steep


def force_parts(weights, own_hot, side_hot, kept, dg, pulls, met, acc, held):
    l1, l2, l3, l5, l6, col = weights
    (widx, kinds, geo, bst, bps, bpr, sent_all, sent_pair, slope) = kept
    slot = lax.broadcasted_iota(jnp.int32, (SLOTS, LANES), 0)

    def marks(b, ws):
        if b in SIDE_START:
            start = SIDE_START[b] + (ws[0] - reach(b, 3, 8)[0]) * LANES
            return side_hot.at[start : start + len(ws) * LANES]
        return own_hot.at[b - 4, ws[0] * LANES : (ws[-1] + 1) * LANES]

    def add_rows(sums, first, b, ws, out):
        for i, w in enumerate(ws):
            target = b - 1 + w
            piece = out[i * LANES : (i + 1) * LANES]
            rows = slice((target - first) * LANES, (target - first + 1) * LANES)
            if (first, target) in started:
                sums[rows, :] += piece
            else:
                sums[rows, :] = piece
                started.add((first, target))

    started = set()

    def block_work(b):
        index = widx[b]
        inner, part = index & (LANES - 1), index >> 7
        basis = bst[b]
        radial = mm(l3[...], jnp.concatenate([basis, basis], axis=0))
        if 3 <= b <= 8:
            basis = bps[b]
            steepness = mm(l3[...], jnp.concatenate([basis, basis], axis=0))
        lanes = [jnp.broadcast_to(inner[k : k + 1, :], (16, LANES)) for k in range(SLOTS)]
        parts = [jnp.broadcast_to(part[k : k + 1, :], (16, LANES)) for k in range(SLOTS)]
        own = 4 <= b <= 7
        if own:
            found_all = mm(sent_pair[:, (b - 1) * LANES : (b + 2) * LANES], own_hot[b - 4])
        value = held.at[b % 2]
        total = [jnp.zeros((8, LANES), F32)] * SLOTS
        for u in range(CHANNELS // 16):
            rows = slice(16 * u, 16 * u + 16)
            low_rows = slice(CHANNELS + 16 * u, CHANNELS + 16 * u + 16)
            windows = [sent_all[rows, (b - 1 + w) * LANES : (b + w) * LANES] for w in range(3)]
            got = []
            message = jnp.zeros((16, LANES), F32)
            for k in range(SLOTS):
                cols = slice(k * LANES, (k + 1) * LANES)
                if own:
                    got.append(found_all[rows, cols] + found_all[low_rows, cols])
                else:
                    found = [pick(window, lanes[k]) for window in windows]
                    got.append(jnp.where(parts[k] == 0, found[0], jnp.where(parts[k] == 1, found[1], found[2])))
                message = message + radial[rows, cols] * got[k]
            _, steep = silu_parts(message)
            back = col[3, rows] * steep
            for k in range(SLOTS):
                cols = slice(k * LANES, (k + 1) * LANES)
                high, low = split(radial[rows, cols] * back)
                value[rows, cols] = high.astype(BF16)
                value[low_rows, cols] = low.astype(BF16)
                if 3 <= b <= 8:
                    pull = got[k] * back * steepness[rows, cols]
                    total[k] = total[k] + pull[0:8] + pull[8:16]
            yield
        if 3 <= b <= 8:
            for k in range(SLOTS):
                pulls[b, :, k * LANES : (k + 1) * LANES] = total[k]

    def scatter_work(b):
        ws = reach(b, 3, 8)
        chosen, value = marks(b, ws), held.at[b % 2]
        out = None
        for u in range(4):
            cols = slice(u * 2 * LANES, (u + 1) * 2 * LANES)
            one = mm_nt(chosen[:, cols], value[:, cols])
            out = one if out is None else out + one
            yield
        add_rows(dg, 3, b, ws, out)

    def together(*works):
        works = list(works)
        while works:
            works = [work for work in works if next(work, "end") != "end"]

    together(block_work(2))
    for b in range(3, 10):
        together(scatter_work(b - 1), block_work(b))
    together(scatter_work(9))

    def finish(b, sums):
        kind = kinds[b]
        rows = []
        for k in range(SLOTS):
            cols = slice(k * LANES, (k + 1) * LANES)
            weight = sums[0:8] + wide_row(kind, k) * sums[8:16]
            rows.append(jnp.sum(bpr[b, :, cols] * weight + pulls[b, :, cols], axis=0, keepdims=True))
        pull = jnp.concatenate(rows, axis=0) * geo[b, 3]
        pieces = []
        for c in range(3):
            value = pull * geo[b, c]
            if 4 <= b <= 7:
                acc[b - 4, c] = jnp.sum(value, axis=0, keepdims=True)
            pieces.append(split(value))
        lines = []
        for h in range(2):
            for c in range(3):
                lines.append(jnp.concatenate([jnp.where(slot == k, pieces[c][h], 0.0) for k in range(SLOTS)], axis=1))
        ws = reach(b, 4, 7)
        out = mm_nt(jnp.concatenate(lines, axis=0).astype(BF16), marks(b, ws)[...])
        for c in range(3):
            both = out[8 * c : 8 * c + 8] + out[24 + 8 * c : 32 + 8 * c]
            for i, w in enumerate(ws):
                target = b - 5 + w
                piece = both[:, i * LANES : (i + 1) * LANES]
                if (c, target) in met_blocks:
                    met[target, c] += piece
                else:
                    met[target, c] = piece
                    met_blocks.add((c, target))

    met_blocks = set()

    for b in range(3, 9, 2):
        cols = slice(b * LANES, (b + 2) * LANES)
        high, low = split(dg[(b - 3) * LANES : (b - 1) * LANES, :])
        steep = mm_nt(l5[...], jnp.concatenate([high, low, high], axis=1).astype(BF16))
        steep = steep + jnp.concatenate([col[2], col[2]], axis=1)
        sums = mm(l6[...], right_stack(steep * slope[:, cols]))
        for i in range(2):
            finish(b + i, sums[:, i * LANES : (i + 1) * LANES])

    away = []
    for c in range(3):
        back = [acc[i, c] - jnp.sum(met[i, c], axis=0, keepdims=True) for i in range(SLAB_BLOCKS)]
        away.append(jnp.concatenate(back, axis=1))
    return jnp.concatenate(away, axis=0)


def fill_region(xs, packs, rows_of):
    for b in range(12):
        lanes = slice((b % 4) * LANES, (b % 4 + 1) * LANES)
        pack = packs[b // 4]
        xs[b, 0:3, :] = rows_of(b // 4)[:, lanes]
        xs[b, 3:4, :] = pack[ROW_KIND : ROW_KIND + 1, lanes]


def lane_total(x):
    x = x[:, 0:LANES] + x[:, LANES : 2 * LANES] + x[:, 2 * LANES : 3 * LANES] + x[:, 3 * LANES : 4 * LANES]
    return jnp.sum(x, axis=1, keepdims=True)


def dot3(a, b):
    return jnp.sum(a * b, axis=0, keepdims=True)


def kept_shapes():
    wide = 12 * LANES
    return [
        ((12, 8, LANES), jnp.int32),
        ((12, 8, LANES), F32),
        ((12, 4, 8, LANES), F32),
        ((12, 16, SLOTS * LANES), BF16),
        ((12, 16, SLOTS * LANES), BF16),
        ((12, 8, SLOTS * LANES), F32),
        ((CHANNELS, wide), F32),
        ((2 * CHANNELS, wide), BF16),
        ((CHANNELS, wide), F32),
    ]


def forward_scratch():
    return [pltpu.VMEM((12, 8, LANES), F32), pltpu.VMEM((48, 12 * LANES), BF16)]


def back_scratch():
    return [
        pltpu.VMEM((6 * LANES, 2 * CHANNELS), F32),
        pltpu.VMEM((12, 8, SLOTS * LANES), F32),
        pltpu.VMEM((SLAB_BLOCKS, 3, SLOTS, LANES), F32),
        pltpu.VMEM((SLAB_BLOCKS, 3, 1, LANES), F32),
        pltpu.VMEM((2, 2 * CHANNELS, SLOTS * LANES), BF16),
    ]


def by_parity(sibling, across):
    even = jnp.full(sibling.shape, lax.axis_index("dom") % 2, jnp.int32) == 0
    return jnp.where(even, across, sibling), jnp.where(even, sibling, across)


def first_kernel(sibling_ref, po_ref, across_ref, own_hot, *rest):
    weights, (out_ref, pl_ref, pr_ref, side_hot), scr = rest[:6], rest[6:10], rest[10:]
    xs, sst, kept = scr[0], scr[1], scr[2:11]
    pl_ref[...], pr_ref[...] = by_parity(sibling_ref[...], across_ref[...])
    packs = [pl_ref, po_ref, pr_ref]
    mark_sides(packs, side_hot)
    fill_region(xs, packs, lambda s: packs[s][ROW_X : ROW_X + 3, :])
    forward_parts(packs, weights, xs, sst, kept)
    out_ref[...] = force_parts(weights, own_hot, side_hot, kept, *scr[11:])


def rows_of(ref):
    return jnp.concatenate([ref[c] for c in range(3)], axis=0)


def block_row(*values):
    values = list(values) + [jnp.zeros((1, LANES), F32)] * (SLAB_BLOCKS - len(values))
    return jnp.concatenate(values, axis=1)


def blend_kernel(images, force_ref, po_ref, before_ref, after_ref, out_ref, sums_ref):
    x = po_ref[ROW_X : ROW_X + 3, :]
    v = po_ref[ROW_V : ROW_V + 3, :]
    force = force_ref[...]
    here = lax.axis_index("img")
    before = jnp.where(here > 0, rows_of(before_ref), 0.0)
    after = jnp.where(here < images - 1, rows_of(after_ref), 0.0)
    tangent = after - before
    plus = after - x
    minus = x - before
    sums = jnp.concatenate(
        [
            dot3(force, tangent),
            dot3(force, force),
            dot3(tangent, tangent),
            dot3(plus, plus),
            dot3(minus, minus),
            dot3(v, v),
            jnp.zeros((2, x.shape[1]), F32),
        ],
        axis=0,
    )
    sums = jnp.broadcast_to(lane_total(sums), (8, LANES))
    sums_ref[...] = sums
    out_ref[0:3, :] = force
    out_ref[3:6, :] = tangent
    out_ref[6:7, :] = block_row(*[sums[i : i + 1] for i in range(4)])
    out_ref[7:8, :] = block_row(sums[4:5], sums[5:6])


def step_numbers(ft, ff, tt, pp, mn, vv, dt, alpha, flagged, climbing, inside):
    root = jnp.sqrt(tt + TINY_VALUE)
    along = ft / root
    spring = SPRING_CONSTANT * (jnp.sqrt(pp) - jnp.sqrt(mn))
    factor = jnp.where(climbing, -2.0 * along, spring - along)
    band = jnp.maximum(ff + 2.0 * factor * along + factor * factor * (tt / (tt + TINY_VALUE)), 0.0)
    new_dt = jnp.where(flagged, 0.5 * dt, jnp.minimum(1.1 * dt, STEP_LIMIT))
    pull = jnp.where(flagged, 0.0, alpha * jnp.sqrt(vv / (band + TINY_VALUE))) + new_dt
    keep = jnp.where(flagged, 0.0, 1.0 - alpha)
    new_alpha = jnp.where(flagged, ALPHA_START, 0.99 * alpha)
    keep = jnp.where(inside, keep, 0.0)
    pull = jnp.where(inside, pull, 0.0)
    return (
        jnp.where(inside, along, 0.0),
        jnp.where(inside, spring, 0.0),
        keep,
        pull,
        pull * factor / root,
        new_dt,
        new_alpha,
    )


def add_kernel(a_ref, b_ref, out_ref):
    out_ref[...] = a_ref[...] + b_ref[...]


def number_kernel(dt_ref, flag_ref, climb_ref, out_ref):
    flags = [flag_ref[0, s].astype(F32) for s in range(flag_ref.shape[1])]
    for i, value in enumerate([dt_ref[0], climb_ref[0].astype(F32)] + flags):
        out_ref[i : i + 1, :] = jnp.full((1, LANES), value, F32)


def second_kernel(images, domains, number_ref, pl_ref, po_ref, pr_ref, own_ref, near_ref, far_ref, *rest):
    count = 2 if domains == 4 else 1
    parts, rest = rest[:count], rest[count:]
    (own_hot, side_hot), weights, (out_ref, record_ref), scr = rest[:2], rest[2:8], rest[8:10], rest[10:]
    packs = [pl_ref, po_ref, pr_ref]
    here = lax.axis_index("img")
    sums = parts[0][...]
    if domains == 4:
        sums = sums + parts[1][...]
    got = [sums[i : i + 1, :] for i in range(6)]
    if domains == 4:
        for one in (near_ref, far_ref):
            for i in range(6):
                got[i] = got[i] + one[6 + i // 4 : 7 + i // 4, (i % 4) * LANES : (i % 4 + 1) * LANES]
    ft, ff, tt, pp, mn, vv = got
    beside = by_parity(near_ref[0:6, :], far_ref[0:6, :])
    shape = (1, LANES)
    along, spring, keep, pull, side, dt, alpha = step_numbers(
        ft,
        ff,
        tt,
        pp,
        mn,
        vv,
        number_ref[0:1, :],
        jnp.full(shape, ALPHA_START, F32),
        number_ref[2:3, :] == 1.0,
        number_ref[1:2, :] == jnp.full(shape, here, jnp.int32).astype(F32),
        jnp.full(shape, jnp.where((here >= 1) & (here <= images - 2), 1, 0), jnp.int32) == 1,
    )
    messages = [beside[0], own_ref[0:6, :], beside[1]]

    def wide(s):
        return jnp.concatenate([s] * SLAB_BLOCKS, axis=1)

    speeds = [
        wide(keep) * p[ROW_V : ROW_V + 3, :] + wide(pull) * m[0:3, :] + wide(side) * m[3:6, :]
        for p, m in zip(packs, messages)
    ]
    moved = [p[ROW_X : ROW_X + 3, :] + wide(dt) * s for p, s in zip(packs, speeds)]
    xs, sst, kept = scr[0], scr[1], scr[2:11]
    fill_region(xs, packs, lambda s: moved[s])
    forward_parts(packs, weights, xs, sst, kept)
    force = force_parts(weights, own_hot, side_hot, kept, *scr[11:])
    for c in range(3):
        for i in range(SLAB_BLOCKS):
            lanes = slice(i * LANES, (i + 1) * LANES)
            row = 4 * c + i
            out_ref[0, row : row + 1, :] = speeds[1][c : c + 1, lanes]
            out_ref[0, 12 + row : 13 + row, :] = force[c : c + 1, lanes]
            out_ref[0, 24 + row : 25 + row, :] = moved[1][c : c + 1, lanes]
    out_ref[0, 36:37, :] = dt
    out_ref[0, 37:38, :] = alpha
    out_ref[0, 38:40, :] = jnp.broadcast_to(number_ref[3:4, :], (2, LANES))
    record_ref[0:1, :] = along
    record_ref[1:2, :] = spring
    record_ref[2:3, :] = number_ref[1:2, :]


PRODUCTS = (
    [("f", "t"), ("f", "f"), ("t", "t"), ("p", "p"), ("d", "d"), ("v", "v")]
    + [("d", "v"), ("d", "f"), ("d", "t"), ("d", "V"), ("d", "F"), ("d", "T"), ("v", "f"), ("v", "t")]
    + [(a, b) for a in "vft" for b in "VFT"]
)


def gram_kernel(images, *refs):
    parts, (before_ref, after_ref), (out_ref, state_ref, messages_ref) = refs[:-5], refs[-5:-3], refs[-3:]
    rows = out_ref.shape[0]
    here = lax.axis_index("img")
    if images == 4:
        places = [here, lax.rem(here + 3, 4), jnp.where(here < 2, 3 - here, here - 2)]
        messages_ref[...] = jnp.zeros(messages_ref.shape, F32)
        for place, beside in [(lax.rem(here + 3, 4), before_ref), (lax.rem(here + 1, 4), after_ref)]:
            for c in range(3):
                for i in range(SLAB_BLOCKS):
                    row = 24 + 4 * c + i
                    messages_ref[place, row : row + 1, :] = beside[c][:, i * LANES : (i + 1) * LANES]
    else:
        places = [lax.rem(here + images - s, images) for s in range(images)]
    for place, part in zip(places, parts):
        messages_ref[place] = part[0]
    blank = [jnp.zeros((rows - images, LANES), F32)] if rows > images else []
    zero = jnp.zeros((1, LANES), F32)

    def gathered(row):
        return jnp.concatenate([messages_ref[i, row : row + 1, :] for i in range(images)] + blank, axis=0)

    def earlier(value):
        return jnp.concatenate([zero, value[0 : rows - 1]], axis=0)

    def later(value):
        return jnp.concatenate([value[1:images], zero] + blank, axis=0)

    number = lax.broadcasted_iota(jnp.int32, (rows, LANES), 0)
    held = number < images
    totals = [jnp.zeros((rows, LANES), F32) for _ in PRODUCTS]
    for row in range(3 * SLAB_BLOCKS):
        v, f, x = gathered(row), gathered(12 + row), gathered(24 + row)
        before = jnp.where(held, earlier(x), 0.0)
        after = later(x)
        t = after - before
        table = {"f": f, "v": v, "t": t, "p": after - x, "d": x - before}
        table["F"], table["V"], table["T"] = earlier(f), earlier(v), earlier(t)
        totals = [old + table[a] * table[b] for old, (a, b) in zip(totals, PRODUCTS)]
        state_ref[row : row + 1, :] = jnp.sum(jnp.where(number == here, t, 0.0), axis=0, keepdims=True)
    lane = lax.broadcasted_iota(jnp.int32, (rows, LANES), 1)
    result = jnp.zeros((rows, LANES), F32)
    for q, one in enumerate(totals):
        one = jnp.broadcast_to(jnp.sum(one, axis=1, keepdims=True), (rows, LANES))
        result = jnp.where(lane == q, one, result)
    out_ref[...] = result
    for i in range(3):
        state_ref[16 + rows * i : 16 + rows * (i + 1), :] = gathered(36 + i)


def final_kernel(images, atoms, own_ref, record_ref, state_ref, *rest):
    parts, (x_ref, v_ref, band_ref, path_ref) = rest[:-4], rest[-4:]
    rows = parts[0].shape[0]
    here = lax.axis_index("img")
    sums = parts[0][...]
    for one in parts[1:]:
        sums = sums + one[...]
    got = {
        pair: jnp.broadcast_to(sums[:, q : q + 1], (rows, LANES)) for q, pair in enumerate(PRODUCTS)
    }
    number = lax.broadcasted_iota(jnp.int32, (rows, LANES), 0)
    inside = (number >= 1) & (number <= images - 2)
    climb = jnp.broadcast_to(record_ref[2:3, :], (rows, LANES))
    dt0, alpha0, flag = (state_ref[16 + rows * i : 16 + rows * (i + 1), :] for i in range(3))
    along, spring, keep, pull, side, dt, _ = step_numbers(
        got["f", "t"],
        got["f", "f"],
        got["t", "t"],
        got["p", "p"],
        got["d", "d"],
        got["v", "v"],
        dt0,
        alpha0,
        flag == 1.0,
        number.astype(F32) == climb,
        inside,
    )

    def shifted(value):
        return jnp.concatenate([jnp.zeros((1, LANES), F32), value[0 : rows - 1]], axis=0)

    now = {"v": dt * keep, "f": dt * pull, "t": dt * side}
    old = {a.upper(): shifted(value) for a, value in now.items()}
    mine = now["v"] * now["v"] * got["v", "v"] + now["f"] * now["f"] * got["f", "f"]
    mine = mine + now["t"] * now["t"] * got["t", "t"]
    cross = now["v"] * now["f"] * got["v", "f"] + now["v"] * now["t"] * got["v", "t"]
    mine = mine + 2.0 * (cross + now["f"] * now["t"] * got["f", "t"])
    both = jnp.zeros((rows, LANES), F32)
    for a in "vft":
        both = both + now[a] * got["d", a]
    for b in "VFT":
        both = both - old[b] * got["d", b]
    for a in "vft":
        for b in "VFT":
            both = both - now[a] * old[b] * got[a, b]
    squared = got["d", "d"] + mine + shifted(mine) + 2.0 * both
    segment = jnp.sqrt(jnp.maximum(squared, 0.0) * (1.0 / (3.0 * atoms)))
    path = jnp.sum(jnp.where(number <= here, segment, 0.0), axis=0, keepdims=True)
    path_ref[...] = path[:, 0:1]
    keep, pull, side, dt, along, spring = (
        jnp.sum(jnp.where(number == here, value, 0.0), axis=0, keepdims=True)
        for value in (keep, pull, side, dt, along, spring)
    )

    for c in range(3):
        speeds, places = [], []
        for i in range(SLAB_BLOCKS):
            row = 4 * c + i
            speed = keep * own_ref[0, row : row + 1, :] + pull * own_ref[0, 12 + row : 13 + row, :]
            speed = speed + side * state_ref[row : row + 1, :]
            speeds.append(speed)
            places.append(own_ref[0, 24 + row : 25 + row, :] + dt * speed)
        v_ref[c] = jnp.concatenate(speeds, axis=1)
        x_ref[c] = jnp.concatenate(places, axis=1)
    band_ref[0] = jnp.concatenate([record_ref[0:1, 0:1], record_ref[1:2, 0:1]], axis=1)
    band_ref[1] = jnp.concatenate([along[:, 0:1], spring[:, 0:1]], axis=1)


VMEM_SPEC = pl.BlockSpec(memory_space=pltpu.VMEM)
SMEM_SPEC = pl.BlockSpec(memory_space=pltpu.SMEM)
HBM_SPEC = pl.BlockSpec(memory_space=pltpu.HBM)


def call(body, outs, scalars, arrays, scratch_shapes=(), flops=0, spec=VMEM_SPEC, vmem=24):
    return pl.pallas_call(
        body,
        out_shape=outs,
        in_specs=[SMEM_SPEC] * len(scalars) + [spec] * len(arrays),
        out_specs=jax.tree.map(lambda _: VMEM_SPEC, outs),
        scratch_shapes=list(scratch_shapes),
        compiler_params=pltpu.CompilerParams(vmem_limit_bytes=vmem * 1024 * 1024),
        cost_estimate=pl.CostEstimate(flops=flops, bytes_accessed=1 << 18, transcendentals=0),
    )(*scalars, *arrays)


def swap(array, axis, partner):
    return lax.ppermute(array, axis, [(i, partner(i)) for i in range(lax.axis_size(axis))])


def exchanged(sums, axis):
    count = lax.axis_size(axis)
    if count == 4:
        return [sums] + [swap(sums, axis, lambda i, by=by: i ^ by) for by in (1, 3, 2)]
    distance = 1
    while distance < count:
        more = swap(sums, axis, lambda i, by=distance: i ^ by)
        sums = call(add_kernel, jax.ShapeDtypeStruct(sums.shape, F32), (), (sums, more))
        distance *= 2
    return [sums]


def collected(state, axis, before, after):
    count = lax.axis_size(axis)
    if count == 4:
        return [state, swap(state, axis, lambda i: (i + 1) % 4), swap(state, axis, lambda i: (2, 3, 1, 0)[i]), before, after]
    return [state] + [swap(state, axis, lambda i, by=by: (i + by) % count) for by in range(1, count)] + [before, after]


def local(
    disp,
    veloc,
    time_step,
    reset_flags,
    climb,
    species,
    neighbours,
    counts,
    lattice,
    embed,
    radial_weight,
    mix_weight,
    update_weight,
    readout,
):
    atoms = disp.shape[2]
    images = lax.axis_size("img")
    domains = lax.axis_size("dom")
    assert disp.shape[0] == 1 and atoms == SLAB_BLOCKS * LANES and domains >= 4
    assert domains & (domains - 1) == 0 and images & (images - 1) == 0
    shape = jax.ShapeDtypeStruct
    x = jnp.transpose(disp, (1, 0, 2))
    v = jnp.transpose(veloc, (1, 0, 2))
    small = (x, v, species, neighbours, counts, embed, readout, radial_weight, mix_weight, update_weight)
    sent, kept_pack = call(
        pack_kernel,
        (shape((PACK_ROWS, atoms), F32), shape((OWN_ROWS, atoms), F32)),
        (),
        (*small, jnp.transpose(lattice, (1, 0, 2))),
        [pltpu.VMEM(a.shape, a.dtype) for a in small] + [pltpu.SemaphoreType.DMA((16,))],
        spec=HBM_SPEC,
        vmem=63,
    )
    sibling = swap(sent, "dom", lambda i: i ^ 1)
    across = swap(sent, "dom", lambda i: (i + 2 * (i % 2) - 1) % domains)
    own_hot, *weights, x_copy, pack = call(
        prepare_kernel,
        (
            shape((SLAB_BLOCKS, 3 * LANES, SLOTS * LANES), BF16),
            shape((CHANNELS, 48), BF16),
            shape((CHANNELS, 192), BF16),
            shape((CHANNELS, 32), BF16),
            shape((CHANNELS, 3 * LANES), BF16),
            shape((16, 192), BF16),
            shape((4, CHANNELS, LANES), F32),
            shape(x.shape, F32),
            shape(sent.shape, F32),
        ),
        (),
        (kept_pack,),
        flops=100000000,
    )
    before = swap(x_copy, "img", lambda i: (i + 1) % images)
    after = swap(x_copy, "img", lambda i: (i - 1) % images)
    force_scratch = forward_scratch() + [pltpu.VMEM(*one) for one in kept_shapes()] + back_scratch()
    force, left, right, side_hot = call(
        first_kernel,
        (
            shape((3, atoms), F32),
            shape(sent.shape, F32),
            shape(sent.shape, F32),
            shape((SIDE_ROWS, SLOTS * LANES), BF16),
        ),
        (),
        (sibling, pack, across, own_hot, *weights),
        force_scratch,
        flops=1000000000,
    )
    message, sums = call(
        functools.partial(blend_kernel, images),
        (shape((8, atoms), F32), shape((8, LANES), F32)),
        (),
        (force, pack, before, after),
    )
    far = swap(message, "dom", lambda i: (i + 2 * (i % 2) - 1) % domains)
    if domains == 4:
        parts = [sums, swap(sums, "dom", lambda i: i ^ 2)]
    else:
        parts = exchanged(sums, "dom")
    near = swap(message, "dom", lambda i: i ^ 1)
    numbers = call(number_kernel, shape((8, LANES), F32), (time_step, jnp.transpose(reset_flags), climb), ())
    state, record = call(
        functools.partial(second_kernel, images, domains),
        (shape((1, 40, LANES), F32), shape((3, LANES), F32)),
        (),
        (numbers, left, pack, right, message, near, far, *parts, own_hot, side_hot, *weights),
        force_scratch,
        flops=1000000000,
    )
    rows = 8 * ((images + 7) // 8)
    sums, extra = call(
        functools.partial(gram_kernel, images),
        (shape((rows, LANES), F32), shape((16 + 3 * rows, LANES), F32)),
        (),
        collected(state, "img", before, after),
        [pltpu.VMEM((images, 40, LANES), F32)],
    )
    new_x, new_v, records, path = call(
        functools.partial(final_kernel, images, atoms * domains),
        (shape(x.shape, F32), shape(x.shape, F32), shape((2, 1, 2), F32), shape((1, 1), F32)),
        (),
        (state, record, extra, *exchanged(sums, "dom")),
    )
    return (
        jnp.transpose(new_x, (1, 0, 2)),
        jnp.transpose(new_v, (1, 0, 2)),
        jnp.transpose(records, (0, 2, 1)),
        path.reshape(1),
    )


def solution(mesh):
    in_specs = (
        P(("group", "img"), None, "dom"),
        P(("group", "img"), None, "dom"),
        P(("group", "img")),
        P(None, ("group", "img")),
        P("group"),
        P(("group", "dom")),
        P(None, ("group", "dom")),
        P(("group", "dom")),
        P(None, None, ("group", "dom")),
        P(),
        P(),
        P(),
        P(),
        P(),
    )
    out_specs = (
        P(("group", "img"), None, "dom"),
        P(("group", "img"), None, "dom"),
        P(None, None, ("group", "img")),
        P(("group", "img")),
    )
    return jax.shard_map(local, mesh=mesh, in_specs=in_specs, out_specs=out_specs, check_vma=False)
```
